32 devices in a mesh: gx: 8 (over z, core), gy: 2 (over y), gz: 2 (over x).
Axes of the slice: x: 2, y: 2, z: 4, core: 2. Of those that a mesh axis runs over, the one named last changes fastest.
Arguments:
- fields: float32 [2, 4, 3, 16, 128, 256], P(None, None, None, 'gz', 'gx', 'gy'), may hold values from -6 to 6
- material: int32 [16, 128, 256], P('gz', 'gx', 'gy'), may hold values from 0 to 3
- pml_width: int32 [6], replicated, may hold values from 2 to 4
- eps_real: float32 [4], replicated, may hold values from 1 to 12
- eps_loss: float32 [4], replicated, may hold values from 0.05 to 1
- coeffs: float32 [2, 4, 4], replicated, may hold values from -3 to 3
- ritz: float32 [2, 4], replicated, may hold values from -4 to 4
Outputs:
- basis_new: float32 [2, 4, 3, 16, 128, 256], P(None, None, None, 'gz', 'gx', 'gy')
- residual: float32 [2, 4, 3, 16, 128, 256], P(None, None, None, 'gz', 'gx', 'gy')
- gram_out: float32 [2, 4, 4], replicated
The draws below stay inside these ranges and needn't reach their ends.
All inputs are finite; a program needn't handle non-finite values.
Results may differ from the reference program's by a relative error of at most 0.000078.
Values sent between devices are 32-bit elements; how exact they have to be, the bound alone decides.
No kernel may reach another device: no remote copies, remote signals or barrier semaphores. Data moves between devices by JAX's collectives and lax.ppermute only.
A program may use at most 64 MiB of HBM per device.

```python
import math
import jax
import jax.numpy as jnp
from jax import lax

NV = 4
NMAT = 4
NX = 128
NY = 256
NZ = 16


def draw_fields(key, part):
    first_key, second_key = jax.random.split(key)
    dimensions = (NV, 3, NZ, NX, NY)
    real_part = jnp.clip(jax.random.normal(first_key, dimensions, jnp.float32), -4.0, 4.0)
    imag_part = jnp.clip(jax.random.normal(second_key, dimensions, jnp.float32), -4.0, 4.0)
    envelope = (0.5 + jnp.arange(NX, dtype=jnp.float32) / NX)[:, None]
    return jnp.stack([real_part * envelope, 0.5 * imag_part * envelope])


def touch_ends(values, own_key, smallest, high):
    place = [jax.random.randint(jax.random.fold_in(own_key, axis), (), 0, length) for axis, length in enumerate(values.shape)]
    widest = values.shape.index(max(values.shape))
    next_to = place[:widest] + [(place[widest] + 1) % values.shape[widest]] + place[widest + 1:]
    return values.at[tuple(place)].set(smallest).at[tuple(next_to)].set(high)


def gaussian(own_key, shape, deviation, limit, kind=jnp.bfloat16):
    return jnp.clip(deviation * jax.random.normal(own_key, shape, jnp.float32), -limit, limit).astype(kind)


def setup_inputs(seed: int = 0) -> dict:
    seeds = jax.random.split(jax.random.key(seed), 8)
    return {
        "fields": draw_fields(jax.random.fold_in(seeds[7], 71), 0),
        "material": touch_ends(jax.random.randint(seeds[1], (NZ, NX, NY), 0, NMAT), jax.random.fold_in(seeds[1], 1), 0, NMAT - 1).astype(jnp.int32),
        "pml_width": touch_ends(jax.random.randint(seeds[2], (6,), 2, 5), jax.random.fold_in(seeds[2], 1), 2, 4).astype(jnp.int32),
        "eps_real": jnp.clip(jnp.exp(jax.random.uniform(seeds[3], (NMAT,), jnp.float32, math.log(1.0), math.log(12.0))), 1.0, 12.0),
        "eps_loss": jnp.clip(jax.random.uniform(seeds[4], (NMAT,), jnp.float32, 0.05, 1.0), 0.05, 1.0),
        "coeffs": gaussian(seeds[5], (2, NV, NV), 0.5, 3.0, jnp.float32),
        "ritz": gaussian(seeds[6], (2, NV), 1.0, 4.0, jnp.float32),
    }


OMEGA_SQ = 0.36
SIGMA_TOP = 3.0


def inverse_stretch(places, length, low_width, high_width):
    low_width = low_width.astype(jnp.float32)
    high_width = high_width.astype(jnp.float32)
    inside_depth = jnp.clip((low_width - places) / low_width, 0.0, 1.0) + jnp.clip((places + 1.0 - length + high_width) / high_width, 0.0, 1.0)
    absorb = SIGMA_TOP * inside_depth * inside_depth
    scaled = 1.0 / (1.0 + absorb * absorb)
    return jnp.stack([scaled, -absorb * scaled])


def complex_mul(factor, values):
    real_part = factor[0] * values[0] - factor[1] * values[1]
    imag_part = factor[0] * values[1] + factor[1] * values[0]
    return jnp.stack([real_part, imag_part])


def spread(factor, direction, rank):
    layout = [2] + [1] * (rank - 1)
    layout[rank - 3 + direction] = factor.shape[1]
    return factor.reshape(layout)


def curl_of(components, derivative):
    return [derivative(components[2], 2) - derivative(components[1], 0),
            derivative(components[0], 0) - derivative(components[2], 1),
            derivative(components[1], 1) - derivative(components[0], 2)]


def step_up(values, direction):
    where_dim = values.ndim - 3 + direction
    following = jnp.concatenate([lax.slice_in_dim(values, 1, values.shape[where_dim], axis=where_dim), jnp.zeros_like(lax.slice_in_dim(values, 0, 1, axis=where_dim))], axis=where_dim)
    return following - values


def step_down(values, direction):
    where_dim = values.ndim - 3 + direction
    previous = jnp.concatenate([jnp.zeros_like(lax.slice_in_dim(values, 0, 1, axis=where_dim)), lax.slice_in_dim(values, 0, values.shape[where_dim] - 1, axis=where_dim)], axis=where_dim)
    return values - previous


def operate(single_field, eps_cell, stretch_e, stretch_h):
    components = [single_field[:, number] for number in range(3)]
    magnetic = curl_of(components, lambda values, direction: complex_mul(spread(stretch_h[direction], direction, 4), step_up(values, direction)))
    electric = curl_of(magnetic, lambda values, direction: complex_mul(spread(stretch_e[direction], direction, 4), step_down(values, direction)))
    images = [electric[number] - OMEGA_SQ * complex_mul(eps_cell, components[number]) for number in range(3)]
    return jnp.stack(images, axis=1)


def product(left, right):
    return jnp.einsum('am,bm->ab', left, right, precision=lax.Precision.HIGHEST)


def bilinear(values, images):
    gram_re = product(values[0], images[0]) - product(values[1], images[1])
    gram_im = product(values[0], images[1]) + product(values[1], images[0])
    return gram_re, gram_im


def matmul_complex(left, right):
    high = lax.Precision.HIGHEST
    real_part = jnp.matmul(left[0], right[0], precision=high) - jnp.matmul(left[1], right[1], precision=high)
    imag_part = jnp.matmul(left[0], right[1], precision=high) + jnp.matmul(left[1], right[0], precision=high)
    return jnp.stack([real_part, imag_part])


def rotate_small(gram_full, coeffs):
    turned = jnp.stack([coeffs[0].T, coeffs[1].T])
    return matmul_complex(turned, matmul_complex(gram_full, coeffs))


def rotate(values, coeffs):
    high = lax.Precision.HIGHEST
    real_part = jnp.einsum('ab,am->bm', coeffs[0], values[0], precision=high) - jnp.einsum('ab,am->bm', coeffs[1], values[1], precision=high)
    imag_part = jnp.einsum('ab,am->bm', coeffs[0], values[1], precision=high) + jnp.einsum('ab,am->bm', coeffs[1], values[0], precision=high)
    return jnp.stack([real_part, imag_part])


def reference(fields, material, pml_width, eps_real, eps_loss, coeffs, ritz):
    lengths = (NZ, NX, NY)
    bounds = ((4, 5), (0, 1), (2, 3))
    stretch_e = []
    stretch_h = []
    for direction in range(3):
        length = lengths[direction]
        places = jnp.arange(length, dtype=jnp.int32).astype(jnp.float32)
        low_slot, high_slot = bounds[direction]
        stretch_e.append(inverse_stretch(places, jnp.float32(length), pml_width[low_slot], pml_width[high_slot]))
        stretch_h.append(inverse_stretch(places + 0.5, jnp.float32(length), pml_width[low_slot], pml_width[high_slot]))
    eps_re = jnp.zeros(material.shape, jnp.float32)
    eps_im = jnp.zeros(material.shape, jnp.float32)
    for number in range(NMAT):
        chosen = (material == number).astype(jnp.float32)
        eps_re = eps_re + eps_real[number] * chosen
        eps_im = eps_im + eps_loss[number] * chosen
    eps_cell = jnp.stack([eps_re, eps_im])
    images = lax.map(lambda single_field: operate(single_field, eps_cell, stretch_e, stretch_h), jnp.moveaxis(fields, 1, 0))
    images = jnp.moveaxis(images, 0, 1)
    values = fields.reshape(2, NV, -1)
    image_flat = images.reshape(2, NV, -1)
    gram_re, gram_im = bilinear(values, image_flat)
    weight_scale = 1.0 / (3.0 * NX * NY * NZ)
    gram_out = rotate_small(jnp.stack([gram_re, gram_im]), coeffs) * weight_scale
    basis_new = rotate(values, coeffs)
    rotated_image = rotate(image_flat, coeffs)
    residual = rotated_image - complex_mul(ritz[:, :, None], basis_new)
    return basis_new.reshape(fields.shape), residual.reshape(fields.shape), gram_out
```

```python
import functools

import jax
import jax.numpy as jnp
from jax import lax
from jax.experimental import pallas as pl
from jax.experimental.pallas import tpu as pltpu
from jax.sharding import PartitionSpec as P

OMEGA_SQ = 0.36
SIGMA_TOP = 3.0
BOUNDS = ((4, 5), (0, 1), (2, 3))
AXES = ("gz", "gx", "gy")

VMEM = pl.BlockSpec(memory_space=pltpu.VMEM)
SMEM = pl.BlockSpec(memory_space=pltpu.SMEM)
HIGH = lax.Precision.HIGHEST


def passed_along(value, axis, steps):
    count = lax.axis_size(axis)
    leading, last = (max(0, -steps), min(count, count - steps))
    return lax.ppermute(value, axis, [(source, source + steps) for source in range(leading, last)])


def inverse_stretch(places, length, low_width, high_width):
    inside_depth = jnp.clip((low_width - places) / low_width, 0.0, 1.0) + jnp.clip(
        (places + 1.0 - length + high_width) / high_width, 0.0, 1.0
    )
    absorb = SIGMA_TOP * inside_depth * inside_depth
    scaled = 1.0 / (1.0 + absorb * absorb)
    return scaled, -absorb * scaled


def cmul(left, right):
    return (left[0] * right[0] - left[1] * right[1], left[0] * right[1] + left[1] * right[0])


def add(left, right):
    return (left[0] + right[0], left[1] + right[1])


def sub(left, right):
    return (left[0] - right[0], left[1] - right[1])


def axis_stretch(pml_ref, direction, count, places):
    total = count * lax.axis_size(AXES[direction])
    low_slot, high_slot = BOUNDS[direction]
    low = jnp.full(places.shape, pml_ref[low_slot], jnp.int32).astype(jnp.float32)
    high = jnp.full(places.shape, pml_ref[high_slot], jnp.int32).astype(jnp.float32)
    return inverse_stretch(places, jnp.float32(total), low, high)


def local_places(direction, count, shape, dim):
    start = lax.axis_index(AXES[direction]) * count
    return (lax.broadcasted_iota(jnp.int32, shape, dim) + start).astype(jnp.float32)


def one_place(direction, count, offset, shape):
    start = lax.axis_index(AXES[direction]) * count + offset
    return jnp.full(shape, start, jnp.int32).astype(jnp.float32)


def packed_lane(slot, part, vector, vectors):
    return (slot * 2 + part) * vectors + vector


def rotate_kernel(coeffs_ref, fields_ref, basis_ref, zf_ref, xf_ref, yf_ref):
    _, vectors, _, nz, nx, ny = fields_ref.shape
    lanes = lax.broadcasted_iota(jnp.int32, (nx, ny), 1)

    @pl.loop(0, nz)
    def _(z):
        packed = jnp.zeros((nx, ny), jnp.float32)
        for comp in range(3):
            old = [(fields_ref[0, a, comp, z], fields_ref[1, a, comp, z]) for a in range(vectors)]
            for b in range(vectors):
                new = None
                for a in range(vectors):
                    term = cmul((coeffs_ref[0, a, b], coeffs_ref[1, a, b]), old[a])
                    new = term if new is None else add(new, term)
                for part in range(2):
                    basis_ref[part, b, comp, z] = new[part]
                    if comp != 1:
                        lane = packed_lane(comp // 2, part, b, vectors)
                        packed = jnp.where(lanes == lane, pltpu.roll(new[part], lane, 1), packed)
                    if comp != 0:
                        xf_ref[part, b, comp - 1, pl.ds(z, 1)] = new[part][0:1]
        yf_ref[z] = packed

    for part in range(2):
        for b in range(vectors):
            for comp in range(2):
                zf_ref[part, b, comp] = basis_ref[part, b, comp, 0]


def image_kernel(
    pml_ref, eps_real_ref, eps_loss_ref, ritz_ref,
    basis_ref, material_ref, zf_ref, xf_ref, yf_ref,
    residual_ref, gram_ref, hzf_ref, hxf_ref, hyf_ref,
    eps_ref, sz_ref, acc_ref, lift_ref,
):
    _, vectors, _, nz, nx, ny = basis_ref.shape
    plane = (nx, ny)
    rows = lax.broadcasted_iota(jnp.int32, plane, 0)
    lanes = lax.broadcasted_iota(jnp.int32, plane, 1)
    shx = axis_stretch(pml_ref, 1, nx, local_places(1, nx, plane, 0) + 0.5)
    sex = axis_stretch(pml_ref, 1, nx, local_places(1, nx, plane, 0))
    shy = axis_stretch(pml_ref, 2, ny, local_places(2, ny, plane, 1) + 0.5)
    sey = axis_stretch(pml_ref, 2, ny, local_places(2, ny, plane, 1))
    table = (nz, ny)
    sez_rows = axis_stretch(pml_ref, 0, nz, local_places(0, nz, table, 0))
    shz_rows = axis_stretch(pml_ref, 0, nz, local_places(0, nz, table, 0) + 0.5)
    for part in range(2):
        sz_ref[part] = sez_rows[part]
        sz_ref[2 + part] = shz_rows[part]
    sz_next = axis_stretch(pml_ref, 0, nz, one_place(0, nz, nz, (1, ny)))
    sx_next = axis_stretch(pml_ref, 1, nx, one_place(1, nx, nx, (1, ny)))
    sy_next = axis_stretch(pml_ref, 2, ny, one_place(2, ny, ny, (1, ny)))

    material = material_ref[...]
    for part, source in enumerate((eps_real_ref, eps_loss_ref)):
        value = jnp.zeros(material.shape, jnp.float32)
        for number in range(source.shape[0]):
            value = jnp.where(material == number, -OMEGA_SQ * source[number], value)
        eps_ref[part] = value

    for a in range(vectors):
        for comp in range(2):
            scaled = cmul(sz_next, (zf_ref[0, a, comp], zf_ref[1, a, comp]))
            for part in range(2):
                lift_ref[part, a, comp] = scaled[part]

    def field(b, comp, z):
        return (basis_ref[0, b, comp, z], basis_ref[1, b, comp, z])

    def ahead_x(value, b, comp, z):
        return tuple(
            jnp.where(rows == nx - 1, xf_ref[part, b, comp - 1, pl.ds(z, 1)], pltpu.roll(value[part], nx - 1, 0))
            for part in range(2)
        )

    def ahead_y(value, b, comp, z):
        out = []
        for part in range(2):
            lane = packed_lane(comp // 2, part, b, vectors)
            edge = pltpu.roll(yf_ref[z], ny - 1 - lane, 1)
            out.append(jnp.where(lanes == ny - 1, edge, pltpu.roll(value[part], ny - 1, 1)))
        return tuple(out)

    def behind(value, axis):
        places = rows if axis == 0 else lanes
        return tuple(jnp.where(places == 0, 0.0, pltpu.roll(value[part], 1, axis)) for part in range(2))

    def fold(value):
        return functools.reduce(jnp.add, [value[row:row + 8] for row in range(0, value.shape[0], 8)])

    @pl.loop(0, nz)
    def _(z):
        hyf_ref[z] = jnp.zeros(plane, jnp.float32)

    for b in range(vectors):
        factor = (ritz_ref[0, b], ritz_ref[1, b])

        def step(z, carry, last, b=b, factor=factor):
            hx_before, hy_before, sums = carry
            sez = (sz_ref[0, pl.ds(z, 1)], sz_ref[1, pl.ds(z, 1)])
            shz = (sz_ref[2, pl.ds(z, 1)], sz_ref[3, pl.ds(z, 1)])
            u = [field(b, comp, z) for comp in range(3)]
            if last:
                up = [(zf_ref[0, b, comp], zf_ref[1, b, comp]) for comp in range(2)]
            else:
                up = [field(b, comp, z + 1) for comp in range(2)]
            dzx, dzy = (cmul(shz, sub(up[comp], u[comp])) for comp in range(2))
            dxy, dxz = (cmul(shx, sub(ahead_x(u[comp], b, comp, z), u[comp])) for comp in (1, 2))
            dyx, dyz = (cmul(shy, sub(ahead_y(u[comp], b, comp, z), u[comp])) for comp in (0, 2))
            hx, hy, hz = sub(dyz, dzy), sub(dzx, dxz), sub(dxy, dyx)
            byz, byx = (cmul(sey, sub(h, behind(h, 1))) for h in (hz, hx))
            bxz, bxy = (cmul(sex, sub(h, behind(h, 0))) for h in (hz, hy))
            bzy = cmul(sez, sub(hy, hy_before))
            bzx = cmul(sez, sub(hx, hx_before))
            eps = (eps_ref[0, z], eps_ref[1, z])
            w = [
                add(curl, cmul(eps, u[comp]))
                for comp, curl in enumerate((sub(byz, bzy), sub(bzx, bxz), sub(bxy, byx)))
            ]
            for comp in range(3):
                left = sub(w[comp], cmul(factor, u[comp]))
                for part in range(2):
                    residual_ref[part, b, comp, z] = left[part]
            for part in range(2):
                hxf_ref[part, b, 0, pl.ds(z, 1)] = hy[part][nx - 1:nx]
                hxf_ref[part, b, 1, pl.ds(z, 1)] = hz[part][nx - 1:nx]
            packed = hyf_ref[z]
            for slot, value in enumerate((hz, hx)):
                for part in range(2):
                    lane = packed_lane(slot, part, b, vectors)
                    packed = jnp.where(lanes == lane, pltpu.roll(value[part], (lane + 1) % ny, 1), packed)
            hyf_ref[z] = packed
            new_sums = []
            for a in range(vectors):
                total = None
                for comp in range(3):
                    term = cmul(field(a, comp, z), w[comp])
                    total = term if total is None else add(total, term)
                if last:
                    total = add(total, cmul((lift_ref[0, a, 0], lift_ref[1, a, 0]), hy))
                    total = sub(total, cmul((lift_ref[0, a, 1], lift_ref[1, a, 1]), hx))
                new_sums.append((sums[a][0] + fold(total[0]), sums[a][1] + fold(total[1])))
            if last:
                for part in range(2):
                    hzf_ref[part, b, 0] = hx[part]
                    hzf_ref[part, b, 1] = hy[part]
            return hx, hy, tuple(new_sums)

        zero = jnp.zeros(plane, jnp.float32)
        none = jnp.zeros((8, ny), jnp.float32)
        carry = ((zero, zero), (zero, zero), tuple((none, none) for _ in range(vectors)))
        carry = lax.fori_loop(0, nz - 1, lambda z, c: step(z, c, False), carry)
        _, _, sums = step(nz - 1, carry, True)
        h_y = (hxf_ref[0, b, 0], hxf_ref[1, b, 0])
        h_z = (hxf_ref[0, b, 1], hxf_ref[1, b, 1])
        for a in range(vectors):
            over = cmul((xf_ref[0, a, 0], xf_ref[1, a, 0]), h_z)
            over = sub(over, cmul((xf_ref[0, a, 1], xf_ref[1, a, 1]), h_y))
            over = cmul(sx_next, over)
            for part in range(2):
                acc_ref[b, part * vectors + a] = sums[a][part] + fold(over[part])

    pairs = lax.dot_general(
        yf_ref[...].reshape(nz * nx, ny), hyf_ref[...].reshape(nz * nx, ny),
        (((0,), (0,)), ((), ())), precision=HIGH, preferred_element_type=jnp.float32,
    )
    both = 2 * vectors
    block = pairs[both:2 * both, both:2 * both] - pairs[0:both, 0:both]
    side = cmul(
        (sy_next[0][:, :vectors], sy_next[1][:, :vectors]),
        (
            block[:vectors, :vectors] - block[vectors:, vectors:],
            block[:vectors, vectors:] + block[vectors:, :vectors],
        ),
    )
    totals = jnp.sum(jnp.sum(acc_ref[...], axis=2), axis=2, keepdims=True)
    columns = lax.broadcasted_iota(jnp.int32, (both, ny), 1)
    body_sum = jnp.zeros((both, ny), jnp.float32)
    for b in range(vectors):
        body_sum = jnp.where(columns == b, totals[b], body_sum)
    cells = 3.0 * nz * nx * ny
    for axis in AXES:
        cells = cells * lax.axis_size(axis)
    for part in range(2):
        whole = body_sum[part * vectors:(part + 1) * vectors, :vectors] + side[part]
        gram_ref[part] = whole * (1.0 / cells)


def rim_kernel(pml_ref, partial_ref, hzf_ref, hxf_ref, hyf_ref, residual_ref):
    _, vectors, _, nz, nx, ny = partial_ref.shape
    plane = (nx, ny)
    rows = lax.broadcasted_iota(jnp.int32, plane, 0)
    lanes = lax.broadcasted_iota(jnp.int32, plane, 1)
    sez = axis_stretch(pml_ref, 0, nz, one_place(0, nz, 0, plane))
    sex = axis_stretch(pml_ref, 1, nx, one_place(1, nx, 0, (1, ny)))
    sey = axis_stretch(pml_ref, 2, ny, one_place(2, ny, 0, plane))
    none = jnp.zeros(plane, jnp.float32)
    sex = tuple(jnp.where(rows == 0, part, none) for part in sex)
    sey = tuple(jnp.where(lanes == 0, part, none) for part in sey)

    def step(z, first):
        packed = hyf_ref[z]
        for b in range(vectors):

            def column(slot, b=b):
                return tuple(
                    pltpu.roll(packed, (ny - packed_lane(slot, part, b, vectors)) % ny, 1) for part in range(2)
                )

            def row(slot, b=b):
                return tuple(hxf_ref[part, b, slot, pl.ds(z, 1)] for part in range(2))

            left = [(partial_ref[0, b, comp, z], partial_ref[1, b, comp, z]) for comp in range(3)]
            left[0] = sub(left[0], cmul(sey, column(0)))
            left[2] = add(left[2], cmul(sey, column(1)))
            left[1] = add(left[1], cmul(sex, row(1)))
            left[2] = sub(left[2], cmul(sex, row(0)))
            if first:
                left[0] = add(left[0], cmul(sez, (hzf_ref[0, b, 1], hzf_ref[1, b, 1])))
                left[1] = sub(left[1], cmul(sez, (hzf_ref[0, b, 0], hzf_ref[1, b, 0])))
            for comp in range(3):
                for part in range(2):
                    residual_ref[part, b, comp, z] = left[comp][part]

    step(0, True)

    @pl.loop(1, nz)
    def _(z):
        step(z, False)


def summed_everywhere(value):
    for axis in ("gz", "gy", "gx"):
        count = lax.axis_size(axis)
        if count & (count - 1):
            value = lax.psum(value, axis)
            continue
        reach = 1
        while reach < count:
            value = value + lax.ppermute(value, axis, [(source, source ^ reach) for source in range(count)])
            reach *= 2
    return value


def body(fields, material, pml_width, eps_real, eps_loss, coeffs, ritz):
    _, vectors, _, nz, nx, ny = fields.shape
    f32 = lambda *shape: jax.ShapeDtypeStruct(shape, jnp.float32)
    params = pltpu.CompilerParams(vmem_limit_bytes=40 * 1024 * 1024)
    zf_shape = (2, vectors, 2, nx, ny)
    xf_shape = (2, vectors, 2, nz, ny)
    yf_shape = (nz, nx, ny)
    basis, zf, xf, yf = pl.pallas_call(
        rotate_kernel,
        out_shape=(f32(*fields.shape), f32(*zf_shape), f32(*xf_shape), f32(*yf_shape)),
        in_specs=[SMEM, VMEM],
        out_specs=(VMEM,) * 4,
        compiler_params=params,
        name="rotate_vectors",
    )(coeffs, fields)
    zf = passed_along(zf, "gz", -1)
    xf = passed_along(xf, "gx", -1)
    yf = passed_along(yf, "gy", -1)
    partial, gram, hzf, hxf, hyf = pl.pallas_call(
        image_kernel,
        out_shape=(
            f32(*fields.shape), f32(2, vectors, vectors), f32(*zf_shape), f32(*xf_shape), f32(*yf_shape),
        ),
        in_specs=[SMEM] * 4 + [VMEM] * 5,
        out_specs=(VMEM,) * 5,
        scratch_shapes=[
            pltpu.VMEM((2, nz, nx, ny), jnp.float32),
            pltpu.VMEM((4, nz, ny), jnp.float32),
            pltpu.VMEM((vectors, 2 * vectors, 8, ny), jnp.float32),
            pltpu.VMEM(zf_shape, jnp.float32),
        ],
        compiler_params=params,
        name="apply_operator",
    )(pml_width, eps_real, eps_loss, ritz, basis, material, zf, xf, yf)
    hzf = passed_along(hzf, "gz", 1)
    hxf = passed_along(hxf, "gx", 1)
    hyf = passed_along(hyf, "gy", 1)
    gram = summed_everywhere(gram)
    residual = pl.pallas_call(
        rim_kernel,
        out_shape=f32(*fields.shape),
        in_specs=[SMEM] + [VMEM] * 4,
        out_specs=VMEM,
        compiler_params=params,
        name="add_rims",
    )(pml_width, partial, hzf, hxf, hyf)
    return basis, residual, gram


def solution(mesh):
    in_specs = (P(None, None, None, "gz", "gx", "gy"), P("gz", "gx", "gy"), P(), P(), P(), P(), P())
    out_specs = (P(None, None, None, "gz", "gx", "gy"), P(None, None, None, "gz", "gx", "gy"), P())
    return jax.shard_map(body, mesh=mesh, in_specs=in_specs, out_specs=out_specs, check_vma=False)
```

```python
import functools

import jax
import jax.numpy as jnp
from jax import lax
from jax.experimental import pallas as pl
from jax.experimental.pallas import tpu as pltpu
from jax.sharding import PartitionSpec as P

OMEGA_SQ = 0.36
SIGMA_TOP = 3.0
BOUNDS = ((4, 5), (0, 1), (2, 3))
AXES = ("gz", "gx", "gy")

VMEM = pl.BlockSpec(memory_space=pltpu.VMEM)
SMEM = pl.BlockSpec(memory_space=pltpu.SMEM)
HBM = pl.BlockSpec(memory_space=pltpu.HBM)
HIGH = lax.Precision.HIGHEST


def passed_round(value, axis, steps):
    count = lax.axis_size(axis)
    return lax.ppermute(value, axis, [(source, (source + steps) % count) for source in range(count)])


def inverse_stretch(places, length, low_width, high_width):
    inside_depth = jnp.clip((low_width - places) / low_width, 0.0, 1.0) + jnp.clip(
        (places + 1.0 - length + high_width) / high_width, 0.0, 1.0
    )
    absorb = SIGMA_TOP * inside_depth * inside_depth
    scaled = 1.0 / (1.0 + absorb * absorb)
    return scaled, -absorb * scaled


def cmul(left, right):
    return (left[0] * right[0] - left[1] * right[1], left[0] * right[1] + left[1] * right[0])


def add(left, right):
    return (left[0] + right[0], left[1] + right[1])


def sub(left, right):
    return (left[0] - right[0], left[1] - right[1])


def axis_stretch(pml_ref, direction, count, places):
    total = count * lax.axis_size(AXES[direction])
    low_slot, high_slot = BOUNDS[direction]
    low = jnp.full(places.shape, pml_ref[low_slot], jnp.int32).astype(jnp.float32)
    high = jnp.full(places.shape, pml_ref[high_slot], jnp.int32).astype(jnp.float32)
    return inverse_stretch(places, jnp.float32(total), low, high)


def local_places(direction, count, shape, dim):
    start = lax.axis_index(AXES[direction]) * count
    return (lax.broadcasted_iota(jnp.int32, shape, dim) + start).astype(jnp.float32)


def one_place(direction, count, offset, shape):
    start = lax.axis_index(AXES[direction]) * count + offset
    return jnp.full(shape, start, jnp.int32).astype(jnp.float32)


def packed_row(slot, part, vector, vectors):
    return (slot * 2 + part) * vectors + vector


def has_neighbour(direction, steps):
    place = lax.axis_index(AXES[direction]) + steps
    inside = (place >= 0) & (place < lax.axis_size(AXES[direction]))
    return jnp.where(inside, 1.0, 0.0).astype(jnp.float32)


def face_kernel(fields_hbm, fields_ref, zf_ref, xf_ref, yf_ref, sems):
    _, vectors, _, nz, nx, ny = fields_ref.shape
    lanes = lax.broadcasted_iota(jnp.int32, (nx, ny), 1)
    copies = [
        pltpu.make_async_copy(fields_hbm.at[part, :, comp], fields_ref.at[part, :, comp], sems.at[part, comp])
        for comp in (0, 2, 1) for part in range(2)
    ]
    for copy in copies:
        copy.start()
    for copy in copies:
        copy.wait()

    packed = [jnp.zeros((nx, ny), jnp.float32)] * nz
    for comp in (0, 2):
        for part in range(2):
            for a in range(vectors):
                row = packed_row(comp // 2, part, a, vectors)
                for z in range(nz):
                    value = fields_ref[part, a, comp, z]
                    packed[z] = jnp.where(lanes == row, pltpu.roll(value, row, 1) if row else value, packed[z])
    turned = jnp.concatenate(packed, axis=0).T
    yf_ref[...] = turned[:yf_ref.shape[0]]
    for part in range(2):
        for a in range(vectors):
            for slot in range(2):
                zf_ref[part, a, slot] = fields_ref[part, a, slot, 0]
                xf_ref[part, a, slot] = fields_ref[part, a, slot + 1, :, 0, :]


def rotated(coeffs_ref, old, b):
    new = None
    for a, value in enumerate(old):
        term = cmul((coeffs_ref[0, a, b], coeffs_ref[1, a, b]), value)
        new = term if new is None else add(new, term)
    return new


def rotate_kernel(coeffs_ref, fields_ref, basis_ref):
    _, vectors, _, nz, nx, ny = fields_ref.shape

    @pl.loop(0, nz)
    def _(z):
        for comp in range(3):
            old = [(fields_ref[0, a, comp, z], fields_ref[1, a, comp, z]) for a in range(vectors)]
            for b in range(vectors):
                new = rotated(coeffs_ref, old, b)
                for part in range(2):
                    basis_ref[part, b, comp, z] = new[part]


def image_kernel(
    pml_ref, eps_real_ref, eps_loss_ref, coeffs_ref,
    basis_ref, material_ref, raw_zf_ref, raw_xf_ref, raw_yf_ref,
    image_ref, gram_ref, hzf_ref, hxf_ref, hyf_ref, basis_hbm,
    eps_ref, sz_ref, acc_ref, lift_ref, zf_ref, xf_ref, yt_ref, yf_ref, packed_ref, sem,
):
    _, vectors, _, nz, nx, ny = basis_ref.shape
    keep = pltpu.make_async_copy(basis_ref, basis_hbm, sem)
    keep.start()
    plane = (nx, ny)
    rows = lax.broadcasted_iota(jnp.int32, plane, 0)
    lanes = lax.broadcasted_iota(jnp.int32, plane, 1)
    shx = axis_stretch(pml_ref, 1, nx, local_places(1, nx, plane, 0) + 0.5)
    sex = axis_stretch(pml_ref, 1, nx, local_places(1, nx, plane, 0))
    shy = axis_stretch(pml_ref, 2, ny, local_places(2, ny, plane, 1) + 0.5)
    sey = axis_stretch(pml_ref, 2, ny, local_places(2, ny, plane, 1))
    table = (nz, ny)
    sez_rows = axis_stretch(pml_ref, 0, nz, local_places(0, nz, table, 0))
    shz_rows = axis_stretch(pml_ref, 0, nz, local_places(0, nz, table, 0) + 0.5)
    for part in range(2):
        sz_ref[part] = sez_rows[part]
        sz_ref[2 + part] = shz_rows[part]
    sz_next = axis_stretch(pml_ref, 0, nz, one_place(0, nz, nz, (1, ny)))
    sx_next = axis_stretch(pml_ref, 1, nx, one_place(1, nx, nx, (1, ny)))
    sy_next = axis_stretch(pml_ref, 2, ny, one_place(2, ny, ny, (1, ny)))

    material = material_ref[...]
    for part, source in enumerate((eps_real_ref, eps_loss_ref)):
        value = jnp.zeros(material.shape, jnp.float32)
        for number in range(source.shape[0]):
            value = jnp.where(material == number, -OMEGA_SQ * source[number], value)
        eps_ref[part] = value

    for direction, raw_ref, face_ref in ((0, raw_zf_ref, zf_ref), (1, raw_xf_ref, xf_ref)):
        inside = has_neighbour(direction, 1)
        for slot in range(2):
            old = [(raw_ref[0, a, slot] * inside, raw_ref[1, a, slot] * inside) for a in range(vectors)]
            for b in range(vectors):
                new = rotated(coeffs_ref, old, b)
                for part in range(2):
                    face_ref[part, b, slot] = new[part]
    inside = has_neighbour(2, 1)
    both = 2 * vectors
    cells = nz * nx
    which = lax.broadcasted_iota(jnp.int32, (both, cells), 0)
    turned = [jnp.zeros((both, cells), jnp.float32)] * 2
    for part in range(2):
        for a in range(vectors):
            column = jnp.zeros((both, cells), jnp.float32)
            for b in range(vectors):
                first, second = coeffs_ref[0, a, b] * inside, coeffs_ref[1, a, b] * inside
                if part:
                    first, second = -second, first
                column = jnp.where(which == b, first, column)
                column = jnp.where(which == vectors + b, second, column)
            for slot in range(2):
                row = packed_row(slot, part, a, vectors)
                turned[slot] = turned[slot] + column * raw_yf_ref[row:row + 1]
    yt_ref[...] = jnp.zeros(yt_ref.shape, jnp.float32)
    for slot in range(2):
        yt_ref[slot * both:(slot + 1) * both] = turned[slot]
    yf_ref[...] = yt_ref[...].T.reshape(nz, nx, ny)

    for a in range(vectors):
        for comp in range(2):
            scaled = cmul(sz_next, (zf_ref[0, a, comp], zf_ref[1, a, comp]))
            for part in range(2):
                lift_ref[part, a, comp] = scaled[part]

    def field(b, comp, z):
        return (basis_ref[0, b, comp, z], basis_ref[1, b, comp, z])

    def ahead_x(value, b, comp, z):
        return tuple(
            jnp.where(rows == nx - 1, xf_ref[part, b, comp - 1, pl.ds(z, 1)], pltpu.roll(value[part], nx - 1, 0))
            for part in range(2)
        )

    def ahead_y(value, b, comp, z):
        out = []
        for part in range(2):
            row = packed_row(comp // 2, part, b, vectors)
            edge = pltpu.roll(yf_ref[z], ny - 1 - row, 1)
            out.append(jnp.where(lanes == ny - 1, edge, pltpu.roll(value[part], ny - 1, 1)))
        return tuple(out)

    def behind(value, axis):
        places = rows if axis == 0 else lanes
        return tuple(jnp.where(places == 0, 0.0, pltpu.roll(value[part], 1, axis)) for part in range(2))

    def fold(value):
        return functools.reduce(jnp.add, [value[row:row + 8] for row in range(0, value.shape[0], 8)])

    @pl.loop(0, nz)
    def _(z):
        packed_ref[z] = jnp.zeros(plane, jnp.float32)

    for b in range(vectors):

        def step(z, carry, last, b=b):
            hx_before, hy_before, sums = carry
            sez = (sz_ref[0, pl.ds(z, 1)], sz_ref[1, pl.ds(z, 1)])
            shz = (sz_ref[2, pl.ds(z, 1)], sz_ref[3, pl.ds(z, 1)])
            u = [field(b, comp, z) for comp in range(3)]
            if last:
                up = [(zf_ref[0, b, comp], zf_ref[1, b, comp]) for comp in range(2)]
            else:
                up = [field(b, comp, z + 1) for comp in range(2)]
            dzx, dzy = (cmul(shz, sub(up[comp], u[comp])) for comp in range(2))
            dxy, dxz = (cmul(shx, sub(ahead_x(u[comp], b, comp, z), u[comp])) for comp in (1, 2))
            dyx, dyz = (cmul(shy, sub(ahead_y(u[comp], b, comp, z), u[comp])) for comp in (0, 2))
            hx, hy, hz = sub(dyz, dzy), sub(dzx, dxz), sub(dxy, dyx)
            byz, byx = (cmul(sey, sub(h, behind(h, 1))) for h in (hz, hx))
            bxz, bxy = (cmul(sex, sub(h, behind(h, 0))) for h in (hz, hy))
            bzy = cmul(sez, sub(hy, hy_before))
            bzx = cmul(sez, sub(hx, hx_before))
            eps = (eps_ref[0, z], eps_ref[1, z])
            w = [
                add(curl, cmul(eps, u[comp]))
                for comp, curl in enumerate((sub(byz, bzy), sub(bzx, bxz), sub(bxy, byx)))
            ]
            for comp in range(3):
                for part in range(2):
                    image_ref[part, b, comp, z] = w[comp][part]
            for part in range(2):
                hxf_ref[part, b, 0, pl.ds(z, 1)] = hy[part][nx - 1:nx]
                hxf_ref[part, b, 1, pl.ds(z, 1)] = hz[part][nx - 1:nx]
            packed = packed_ref[z]
            for slot, value in enumerate((hz, hx)):
                for part in range(2):
                    row = packed_row(slot, part, b, vectors)
                    packed = jnp.where(lanes == row, pltpu.roll(value[part], (row + 1) % ny, 1), packed)
            packed_ref[z] = packed
            new_sums = []
            for a in range(vectors):
                total = None
                for comp in range(3):
                    term = cmul(field(a, comp, z), w[comp])
                    total = term if total is None else add(total, term)
                if last:
                    total = add(total, cmul((lift_ref[0, a, 0], lift_ref[1, a, 0]), hy))
                    total = sub(total, cmul((lift_ref[0, a, 1], lift_ref[1, a, 1]), hx))
                new_sums.append((sums[a][0] + fold(total[0]), sums[a][1] + fold(total[1])))
            if last:
                for part in range(2):
                    hzf_ref[part, b, 0] = hx[part]
                    hzf_ref[part, b, 1] = hy[part]
            return hx, hy, tuple(new_sums)

        zero = jnp.zeros(plane, jnp.float32)
        none = jnp.zeros((8, ny), jnp.float32)
        carry = ((zero, zero), (zero, zero), tuple((none, none) for _ in range(vectors)))
        carry = lax.fori_loop(0, nz - 1, lambda z, c: step(z, c, False), carry)
        _, _, sums = step(nz - 1, carry, True)
        h_y = (hxf_ref[0, b, 0], hxf_ref[1, b, 0])
        h_z = (hxf_ref[0, b, 1], hxf_ref[1, b, 1])
        for a in range(vectors):
            over = cmul((xf_ref[0, a, 0], xf_ref[1, a, 0]), h_z)
            over = sub(over, cmul((xf_ref[0, a, 1], xf_ref[1, a, 1]), h_y))
            over = cmul(sx_next, over)
            for part in range(2):
                acc_ref[b, part * vectors + a] = sums[a][part] + fold(over[part])

    hyf_ref[...] = packed_ref[...].reshape(cells, ny).T[:2 * both]
    pairs = lax.dot_general(
        yt_ref[0:2 * both], hyf_ref[...], (((1,), (1,)), ((), ())),
        precision=HIGH, preferred_element_type=jnp.float32,
    )
    block = pairs[both:2 * both, both:2 * both] - pairs[0:both, 0:both]
    side = cmul(
        (sy_next[0][:, :vectors], sy_next[1][:, :vectors]),
        (
            block[:vectors, :vectors] - block[vectors:, vectors:],
            block[:vectors, vectors:] + block[vectors:, :vectors],
        ),
    )
    totals = jnp.sum(jnp.sum(acc_ref[...], axis=2), axis=2, keepdims=True)
    columns = lax.broadcasted_iota(jnp.int32, (both, ny), 1)
    body_sum = jnp.zeros((both, ny), jnp.float32)
    for b in range(vectors):
        body_sum = jnp.where(columns == b, totals[b], body_sum)
    everywhere = 3.0 * nz * nx * ny
    for axis in AXES:
        everywhere = everywhere * lax.axis_size(axis)
    for part in range(2):
        whole = body_sum[part * vectors:(part + 1) * vectors, :vectors] + side[part]
        gram_ref[part] = whole * (1.0 / everywhere)
    keep.wait()


def rim_kernel(
    pml_ref, ritz_ref, basis_ref, image_ref, hzf_ref, hxf_ref, hyf_ref, residual_ref, yt_ref, packed_ref
):
    _, vectors, _, nz, nx, ny = basis_ref.shape
    plane = (nx, ny)
    rows = lax.broadcasted_iota(jnp.int32, plane, 0)
    lanes = lax.broadcasted_iota(jnp.int32, plane, 1)
    sez = axis_stretch(pml_ref, 0, nz, one_place(0, nz, 0, plane))
    sex = axis_stretch(pml_ref, 1, nx, one_place(1, nx, 0, (1, ny)))
    sey = axis_stretch(pml_ref, 2, ny, one_place(2, ny, 0, plane))
    none = jnp.zeros(plane, jnp.float32)
    sez = tuple(part * has_neighbour(0, -1) for part in sez)
    sex = tuple(jnp.where(rows == 0, part * has_neighbour(1, -1), none) for part in sex)
    sey = tuple(jnp.where(lanes == 0, part * has_neighbour(2, -1), none) for part in sey)
    yt_ref[...] = jnp.zeros(yt_ref.shape, jnp.float32)
    yt_ref[:hyf_ref.shape[0]] = hyf_ref[...]
    packed_ref[...] = yt_ref[...].T.reshape(nz, nx, ny)

    def step(z, first):
        packed = packed_ref[z]
        for b in range(vectors):

            def column(slot, b=b):
                return tuple(
                    pltpu.roll(packed, (ny - packed_row(slot, part, b, vectors)) % ny, 1) for part in range(2)
                )

            def row(slot, b=b):
                return tuple(hxf_ref[part, b, slot, pl.ds(z, 1)] for part in range(2))

            factor = (ritz_ref[0, b], ritz_ref[1, b])
            left = []
            for comp in range(3):
                u = (basis_ref[0, b, comp, z], basis_ref[1, b, comp, z])
                w = (image_ref[0, b, comp, z], image_ref[1, b, comp, z])
                left.append(sub(w, cmul(factor, u)))
            left[0] = sub(left[0], cmul(sey, column(0)))
            left[2] = add(left[2], cmul(sey, column(1)))
            left[1] = add(left[1], cmul(sex, row(1)))
            left[2] = sub(left[2], cmul(sex, row(0)))
            if first:
                left[0] = add(left[0], cmul(sez, (hzf_ref[0, b, 1], hzf_ref[1, b, 1])))
                left[1] = sub(left[1], cmul(sez, (hzf_ref[0, b, 0], hzf_ref[1, b, 0])))
            for comp in range(3):
                for part in range(2):
                    residual_ref[part, b, comp, z] = left[comp][part]

    step(0, True)

    @pl.loop(1, nz)
    def _(z):
        step(z, False)


def sum_steps(axes):
    steps = []
    for axis in axes:
        count = lax.axis_size(axis)
        if count & (count - 1):
            steps.append(lambda value, axis=axis: lax.psum(value, axis) - value)
            continue
        reach = 1
        while reach < count:
            pairs = [(source, source ^ reach) for source in range(count)]
            steps.append(functools.partial(lax.ppermute, axis_name=axis, perm=pairs))
            reach *= 2
    return steps


def body(fields, material, pml_width, eps_real, eps_loss, coeffs, ritz):
    _, vectors, _, nz, nx, ny = fields.shape
    f32 = lambda *shape: jax.ShapeDtypeStruct(shape, jnp.float32)
    scratch = lambda *shape: pltpu.VMEM(shape, jnp.float32)
    params = pltpu.CompilerParams(vmem_limit_bytes=40 * 1024 * 1024)
    whole = f32(*fields.shape)
    zf_shape = (2, vectors, 2, nx, ny)
    xf_shape = (2, vectors, 2, nz, ny)
    yf_shape = (4 * vectors, nz * nx)
    faces = (f32(*zf_shape), f32(*xf_shape), f32(*yf_shape))
    near, zf, xf, yf = pl.pallas_call(
        face_kernel,
        out_shape=(whole,) + faces,
        in_specs=[HBM],
        out_specs=(VMEM,) * 4,
        scratch_shapes=[pltpu.SemaphoreType.DMA((2, 3))],
        compiler_params=params,
        name="take_faces",
    )(pltpu.with_memory_space_constraint(fields, pltpu.HBM))
    zf = passed_round(zf, "gz", -1)
    xf = passed_round(xf, "gx", -1)
    yf = passed_round(yf, "gy", -1)
    cells = fields.size // 6 // vectors
    basis = pl.pallas_call(
        rotate_kernel,
        out_shape=whole,
        in_specs=[SMEM, VMEM],
        out_specs=VMEM,
        compiler_params=params,
        cost_estimate=pl.CostEstimate(flops=400 * cells, bytes_accessed=8 * fields.size, transcendentals=0),
        name="rotate_vectors",
    )(coeffs, near)
    image, gram, hzf, hxf, hyf, basis_new = pl.pallas_call(
        image_kernel,
        out_shape=(whole, f32(2, vectors, vectors)) + faces + (whole,),
        in_specs=[SMEM] * 4 + [VMEM] * 5,
        out_specs=(VMEM,) * 5 + (HBM,),
        scratch_shapes=[
            scratch(2, nz, nx, ny),
            scratch(4, nz, ny),
            scratch(vectors, 2 * vectors, 8, ny),
            scratch(*zf_shape),
            scratch(*zf_shape),
            scratch(*xf_shape),
            scratch(ny, nz * nx),
            scratch(nz, nx, ny),
            scratch(nz, nx, ny),
            pltpu.SemaphoreType.DMA,
        ],
        compiler_params=params,
        cost_estimate=pl.CostEstimate(flops=1200 * cells, bytes_accessed=8 * fields.size, transcendentals=0),
        name="apply_operator",
    )(pml_width, eps_real, eps_loss, coeffs, basis, material, zf, xf, yf)
    hzf = passed_round(hzf, "gz", 1)
    hxf = passed_round(hxf, "gx", 1)
    hyf = passed_round(hyf, "gy", 1)
    steps = sum_steps(("gx", "gy", "gz"))
    for step in steps[:-2]:
        gram = gram + step(gram)
    gram, image = lax.optimization_barrier((gram, image))
    other = steps[-2](gram)
    residual = pl.pallas_call(
        rim_kernel,
        out_shape=whole,
        in_specs=[SMEM] * 2 + [VMEM] * 5,
        out_specs=VMEM,
        scratch_shapes=[scratch(ny, nz * nx), scratch(nz, nx, ny)],
        compiler_params=params,
        cost_estimate=pl.CostEstimate(flops=200 * cells, bytes_accessed=12 * fields.size, transcendentals=0),
        name="add_rims",
    )(pml_width, ritz, basis, image, hzf, hxf, hyf)
    other, residual = lax.optimization_barrier((other, residual))
    gram = gram + other
    return basis_new, residual, gram + steps[-1](gram)


def solution(mesh):
    in_specs = (P(None, None, None, "gz", "gx", "gy"), P("gz", "gx", "gy"), P(), P(), P(), P(), P())
    out_specs = (P(None, None, None, "gz", "gx", "gy"), P(None, None, None, "gz", "gx", "gy"), P())
    return jax.shard_map(body, mesh=mesh, in_specs=in_specs, out_specs=out_specs, check_vma=False)
```

```python
import functools

import jax
import jax.numpy as jnp
from jax import lax
from jax.experimental import pallas as pl
from jax.experimental.pallas import tpu as pltpu
from jax.sharding import PartitionSpec as P

OMEGA_SQ = 0.36
SIGMA_TOP = 3.0
BOUNDS = ((4, 5), (0, 1), (2, 3))
AXES = ("gz", "gx", "gy")

VMEM = pl.BlockSpec(memory_space=pltpu.VMEM)
SMEM = pl.BlockSpec(memory_space=pltpu.SMEM)
HBM = pl.BlockSpec(memory_space=pltpu.HBM)
HIGH = lax.Precision.HIGHEST


def passed_round(value, axis, steps):
    count = lax.axis_size(axis)
    return lax.ppermute(value, axis, [(source, (source + steps) % count) for source in range(count)])


def inverse_stretch(places, length, low_width, high_width):
    inside_depth = jnp.clip((low_width - places) / low_width, 0.0, 1.0) + jnp.clip(
        (places + 1.0 - length + high_width) / high_width, 0.0, 1.0
    )
    absorb = SIGMA_TOP * inside_depth * inside_depth
    scaled = 1.0 / (1.0 + absorb * absorb)
    return scaled, -absorb * scaled


def cmul(left, right):
    return (left[0] * right[0] - left[1] * right[1], left[0] * right[1] + left[1] * right[0])


def add(left, right):
    return (left[0] + right[0], left[1] + right[1])


def sub(left, right):
    return (left[0] - right[0], left[1] - right[1])


def axis_stretch(pml_ref, direction, count, places):
    total = count * lax.axis_size(AXES[direction])
    low_slot, high_slot = BOUNDS[direction]
    low = jnp.full(places.shape, pml_ref[low_slot], jnp.int32).astype(jnp.float32)
    high = jnp.full(places.shape, pml_ref[high_slot], jnp.int32).astype(jnp.float32)
    return inverse_stretch(places, jnp.float32(total), low, high)


def local_places(direction, count, shape, dim):
    start = lax.axis_index(AXES[direction]) * count
    return (lax.broadcasted_iota(jnp.int32, shape, dim) + start).astype(jnp.float32)


def one_place(direction, count, offset, shape):
    start = lax.axis_index(AXES[direction]) * count + offset
    return jnp.full(shape, start, jnp.int32).astype(jnp.float32)


def packed_row(slot, part, vector, vectors):
    return (slot * 2 + part) * vectors + vector


def has_neighbour(direction, steps):
    place = lax.axis_index(AXES[direction]) + steps
    inside = (place >= 0) & (place < lax.axis_size(AXES[direction]))
    return jnp.where(inside, 1.0, 0.0).astype(jnp.float32)


def face_kernel(fields_hbm, fields_ref, zf_ref, xf_ref, yf_ref, sems):
    _, vectors, _, nz, nx, ny = fields_ref.shape
    lanes = lax.broadcasted_iota(jnp.int32, (nx, ny), 1)
    copies = [
        pltpu.make_async_copy(fields_hbm.at[part, :, comp], fields_ref.at[part, :, comp], sems.at[part, comp])
        for comp in (0, 2, 1) for part in range(2)
    ]
    for copy in copies:
        copy.start()
    for copy in copies:
        copy.wait()

    packed = [jnp.zeros((nx, ny), jnp.float32)] * nz
    for comp in (0, 2):
        for part in range(2):
            for a in range(vectors):
                row = packed_row(comp // 2, part, a, vectors)
                for z in range(nz):
                    value = fields_ref[part, a, comp, z]
                    packed[z] = jnp.where(lanes == row, pltpu.roll(value, row, 1) if row else value, packed[z])
    turned = jnp.concatenate(packed, axis=0).T
    yf_ref[...] = turned[:yf_ref.shape[0]]
    for part in range(2):
        for a in range(vectors):
            for slot in range(2):
                zf_ref[part, a, slot] = fields_ref[part, a, slot, 0]
                xf_ref[part, a, slot] = fields_ref[part, a, slot + 1, :, 0, :]


def rotated(coeffs_ref, old, b):
    new = None
    for a, value in enumerate(old):
        term = cmul((coeffs_ref[0, a, b], coeffs_ref[1, a, b]), value)
        new = term if new is None else add(new, term)
    return new


def rotate_kernel(coeffs_ref, fields_ref, basis_ref):
    _, vectors, _, nz, nx, ny = fields_ref.shape

    @pl.loop(0, nz)
    def _(z):
        for comp in range(3):
            old = [(fields_ref[0, a, comp, z], fields_ref[1, a, comp, z]) for a in range(vectors)]
            for b in range(vectors):
                new = rotated(coeffs_ref, old, b)
                for part in range(2):
                    basis_ref[part, b, comp, z] = new[part]


def image_kernel(
    pml_ref, eps_real_ref, eps_loss_ref, coeffs_ref,
    basis_ref, material_ref, raw_zf_ref, raw_xf_ref, raw_yf_ref,
    image_ref, gram_ref, hzf_ref, hxf_ref, hyf_ref, basis_hbm,
    eps_ref, sz_ref, acc_ref, lift_ref, zf_ref, xf_ref, yt_ref, yf_ref, packed_ref, sem,
):
    _, vectors, _, nz, nx, ny = basis_ref.shape
    keep = pltpu.make_async_copy(basis_ref, basis_hbm, sem)
    keep.start()
    plane = (nx, ny)
    rows = lax.broadcasted_iota(jnp.int32, plane, 0)
    lanes = lax.broadcasted_iota(jnp.int32, plane, 1)
    shx = axis_stretch(pml_ref, 1, nx, local_places(1, nx, plane, 0) + 0.5)
    sex = axis_stretch(pml_ref, 1, nx, local_places(1, nx, plane, 0))
    shy = axis_stretch(pml_ref, 2, ny, local_places(2, ny, plane, 1) + 0.5)
    sey = axis_stretch(pml_ref, 2, ny, local_places(2, ny, plane, 1))
    table = (nz, ny)
    sez_rows = axis_stretch(pml_ref, 0, nz, local_places(0, nz, table, 0))
    shz_rows = axis_stretch(pml_ref, 0, nz, local_places(0, nz, table, 0) + 0.5)
    for part in range(2):
        sz_ref[part] = sez_rows[part]
        sz_ref[2 + part] = shz_rows[part]
    sz_next = axis_stretch(pml_ref, 0, nz, one_place(0, nz, nz, (1, ny)))
    sx_next = axis_stretch(pml_ref, 1, nx, one_place(1, nx, nx, (1, ny)))
    sy_next = axis_stretch(pml_ref, 2, ny, one_place(2, ny, ny, (1, ny)))

    material = material_ref[...]
    for part, source in enumerate((eps_real_ref, eps_loss_ref)):
        value = jnp.zeros(material.shape, jnp.float32)
        for number in range(source.shape[0]):
            value = jnp.where(material == number, -OMEGA_SQ * source[number], value)
        eps_ref[part] = value

    for direction, raw_ref, face_ref in ((0, raw_zf_ref, zf_ref), (1, raw_xf_ref, xf_ref)):
        inside = has_neighbour(direction, 1)
        for slot in range(2):
            old = [(raw_ref[0, a, slot] * inside, raw_ref[1, a, slot] * inside) for a in range(vectors)]
            for b in range(vectors):
                new = rotated(coeffs_ref, old, b)
                for part in range(2):
                    face_ref[part, b, slot] = new[part]
    inside = has_neighbour(2, 1)
    both = 2 * vectors
    cells = nz * nx
    which = lax.broadcasted_iota(jnp.int32, (both, cells), 0)
    turned = [jnp.zeros((both, cells), jnp.float32)] * 2
    for part in range(2):
        for a in range(vectors):
            column = jnp.zeros((both, cells), jnp.float32)
            for b in range(vectors):
                first, second = coeffs_ref[0, a, b] * inside, coeffs_ref[1, a, b] * inside
                if part:
                    first, second = -second, first
                column = jnp.where(which == b, first, column)
                column = jnp.where(which == vectors + b, second, column)
            for slot in range(2):
                row = packed_row(slot, part, a, vectors)
                turned[slot] = turned[slot] + column * raw_yf_ref[row:row + 1]
    yt_ref[...] = jnp.zeros(yt_ref.shape, jnp.float32)
    for slot in range(2):
        yt_ref[slot * both:(slot + 1) * both] = turned[slot]
    yf_ref[...] = yt_ref[...].T.reshape(nz, nx, ny)

    for a in range(vectors):
        for comp in range(2):
            scaled = cmul(sz_next, (zf_ref[0, a, comp], zf_ref[1, a, comp]))
            for part in range(2):
                lift_ref[part, a, comp] = scaled[part]

    def field(b, comp, z):
        return (basis_ref[0, b, comp, z], basis_ref[1, b, comp, z])

    def ahead_x(value, b, comp, z):
        return tuple(
            jnp.where(rows == nx - 1, xf_ref[part, b, comp - 1, pl.ds(z, 1)], pltpu.roll(value[part], nx - 1, 0))
            for part in range(2)
        )

    def ahead_y(value, b, comp, z):
        out = []
        for part in range(2):
            row = packed_row(comp // 2, part, b, vectors)
            edge = pltpu.roll(yf_ref[z], ny - 1 - row, 1)
            out.append(jnp.where(lanes == ny - 1, edge, pltpu.roll(value[part], ny - 1, 1)))
        return tuple(out)

    def behind(value, axis):
        places = rows if axis == 0 else lanes
        return tuple(jnp.where(places == 0, 0.0, pltpu.roll(value[part], 1, axis)) for part in range(2))

    def fold(value):
        return functools.reduce(jnp.add, [value[row:row + 8] for row in range(0, value.shape[0], 8)])

    @pl.loop(0, nz)
    def _(z):
        packed_ref[z] = jnp.zeros(plane, jnp.float32)

    for b in range(vectors):

        def step(z, carry, last, b=b):
            hx_before, hy_before, sums = carry
            sez = (sz_ref[0, pl.ds(z, 1)], sz_ref[1, pl.ds(z, 1)])
            shz = (sz_ref[2, pl.ds(z, 1)], sz_ref[3, pl.ds(z, 1)])
            u = [field(b, comp, z) for comp in range(3)]
            if last:
                up = [(zf_ref[0, b, comp], zf_ref[1, b, comp]) for comp in range(2)]
            else:
                up = [field(b, comp, z + 1) for comp in range(2)]
            dzx, dzy = (cmul(shz, sub(up[comp], u[comp])) for comp in range(2))
            dxy, dxz = (cmul(shx, sub(ahead_x(u[comp], b, comp, z), u[comp])) for comp in (1, 2))
            dyx, dyz = (cmul(shy, sub(ahead_y(u[comp], b, comp, z), u[comp])) for comp in (0, 2))
            hx, hy, hz = sub(dyz, dzy), sub(dzx, dxz), sub(dxy, dyx)
            byz, byx = (cmul(sey, sub(h, behind(h, 1))) for h in (hz, hx))
            bxz, bxy = (cmul(sex, sub(h, behind(h, 0))) for h in (hz, hy))
            bzy = cmul(sez, sub(hy, hy_before))
            bzx = cmul(sez, sub(hx, hx_before))
            eps = (eps_ref[0, z], eps_ref[1, z])
            w = [
                add(curl, cmul(eps, u[comp]))
                for comp, curl in enumerate((sub(byz, bzy), sub(bzx, bxz), sub(bxy, byx)))
            ]
            for comp in range(3):
                for part in range(2):
                    image_ref[part, b, comp, z] = w[comp][part]
            for part in range(2):
                hxf_ref[part, b, 0, pl.ds(z, 1)] = hy[part][nx - 1:nx]
                hxf_ref[part, b, 1, pl.ds(z, 1)] = hz[part][nx - 1:nx]
            packed = packed_ref[z]
            for slot, value in enumerate((hz, hx)):
                for part in range(2):
                    row = packed_row(slot, part, b, vectors)
                    packed = jnp.where(lanes == row, pltpu.roll(value[part], (row + 1) % ny, 1), packed)
            packed_ref[z] = packed
            new_sums = []
            for a in range(vectors):
                total = None
                for comp in range(3):
                    term = cmul(field(a, comp, z), w[comp])
                    total = term if total is None else add(total, term)
                if last:
                    total = add(total, cmul((lift_ref[0, a, 0], lift_ref[1, a, 0]), hy))
                    total = sub(total, cmul((lift_ref[0, a, 1], lift_ref[1, a, 1]), hx))
                new_sums.append((sums[a][0] + fold(total[0]), sums[a][1] + fold(total[1])))
            if last:
                for part in range(2):
                    hzf_ref[part, b, 0] = hx[part]
                    hzf_ref[part, b, 1] = hy[part]
            return hx, hy, tuple(new_sums)

        zero = jnp.zeros(plane, jnp.float32)
        none = jnp.zeros((8, ny), jnp.float32)
        carry = ((zero, zero), (zero, zero), tuple((none, none) for _ in range(vectors)))
        carry = lax.fori_loop(0, nz - 1, lambda z, c: step(z, c, False), carry)
        _, _, sums = step(nz - 1, carry, True)
        h_y = (hxf_ref[0, b, 0], hxf_ref[1, b, 0])
        h_z = (hxf_ref[0, b, 1], hxf_ref[1, b, 1])
        for a in range(vectors):
            over = cmul((xf_ref[0, a, 0], xf_ref[1, a, 0]), h_z)
            over = sub(over, cmul((xf_ref[0, a, 1], xf_ref[1, a, 1]), h_y))
            over = cmul(sx_next, over)
            for part in range(2):
                acc_ref[b, part * vectors + a] = sums[a][part] + fold(over[part])

    hyf_ref[...] = packed_ref[...].reshape(cells, ny).T[:2 * both]
    pairs = lax.dot_general(
        yt_ref[0:2 * both], hyf_ref[...], (((1,), (1,)), ((), ())),
        precision=HIGH, preferred_element_type=jnp.float32,
    )
    block = pairs[both:2 * both, both:2 * both] - pairs[0:both, 0:both]
    side = cmul(
        (sy_next[0][:, :vectors], sy_next[1][:, :vectors]),
        (
            block[:vectors, :vectors] - block[vectors:, vectors:],
            block[:vectors, vectors:] + block[vectors:, :vectors],
        ),
    )
    totals = jnp.sum(jnp.sum(acc_ref[...], axis=2), axis=2, keepdims=True)
    columns = lax.broadcasted_iota(jnp.int32, (both, ny), 1)
    body_sum = jnp.zeros((both, ny), jnp.float32)
    for b in range(vectors):
        body_sum = jnp.where(columns == b, totals[b], body_sum)
    everywhere = 3.0 * nz * nx * ny
    for axis in AXES:
        everywhere = everywhere * lax.axis_size(axis)
    for part in range(2):
        whole = body_sum[part * vectors:(part + 1) * vectors, :vectors] + side[part]
        gram_ref[part] = whole * (1.0 / everywhere)
    keep.wait()


def rim_kernel(
    pml_ref, ritz_ref, basis_ref, image_ref, hzf_ref, hxf_ref, hyf_ref, residual_ref, yt_ref, packed_ref
):
    _, vectors, _, nz, nx, ny = basis_ref.shape
    plane = (nx, ny)
    rows = lax.broadcasted_iota(jnp.int32, plane, 0)
    lanes = lax.broadcasted_iota(jnp.int32, plane, 1)
    sez = axis_stretch(pml_ref, 0, nz, one_place(0, nz, 0, plane))
    sex = axis_stretch(pml_ref, 1, nx, one_place(1, nx, 0, (1, ny)))
    sey = axis_stretch(pml_ref, 2, ny, one_place(2, ny, 0, plane))
    none = jnp.zeros(plane, jnp.float32)
    sez = tuple(part * has_neighbour(0, -1) for part in sez)
    sex = tuple(jnp.where(rows == 0, part * has_neighbour(1, -1), none) for part in sex)
    sey = tuple(jnp.where(lanes == 0, part * has_neighbour(2, -1), none) for part in sey)
    yt_ref[...] = jnp.zeros(yt_ref.shape, jnp.float32)
    yt_ref[:hyf_ref.shape[0]] = hyf_ref[...]
    packed_ref[...] = yt_ref[...].T.reshape(nz, nx, ny)

    def step(z, first):
        packed = packed_ref[z]
        for b in range(vectors):

            def column(slot, b=b):
                return tuple(
                    pltpu.roll(packed, (ny - packed_row(slot, part, b, vectors)) % ny, 1) for part in range(2)
                )

            def row(slot, b=b):
                return tuple(hxf_ref[part, b, slot, pl.ds(z, 1)] for part in range(2))

            factor = (ritz_ref[0, b], ritz_ref[1, b])
            left = []
            for comp in range(3):
                u = (basis_ref[0, b, comp, z], basis_ref[1, b, comp, z])
                w = (image_ref[0, b, comp, z], image_ref[1, b, comp, z])
                left.append(sub(w, cmul(factor, u)))
            left[0] = sub(left[0], cmul(sey, column(0)))
            left[2] = add(left[2], cmul(sey, column(1)))
            left[1] = add(left[1], cmul(sex, row(1)))
            left[2] = sub(left[2], cmul(sex, row(0)))
            if first:
                left[0] = add(left[0], cmul(sez, (hzf_ref[0, b, 1], hzf_ref[1, b, 1])))
                left[1] = sub(left[1], cmul(sez, (hzf_ref[0, b, 0], hzf_ref[1, b, 0])))
            for comp in range(3):
                for part in range(2):
                    residual_ref[part, b, comp, z] = left[comp][part]

    step(0, True)

    @pl.loop(1, nz)
    def _(z):
        step(z, False)


def sum_phases():
    sizes = [lax.axis_size(axis) for axis in ("gx", "gy", "gz")]
    if any(size & (size - 1) for size in sizes):
        return None
    across = sizes[1] * sizes[2]
    masks = [1 << bit for bit in range((sizes[0] * across).bit_length() - 1)]
    along = [mask for mask in masks if mask >= across]
    rest = [mask for mask in masks if mask < across]
    phases = [along[place:place + 2] for place in range(1, len(along), 2)] + [along[:1]]
    phases += [rest[place:place + 2] for place in range(0, len(rest), 2)]
    return [phase for phase in phases if phase]


def from_partners(value, phase):
    axes = ("gx", "gy", "gz")
    count = 1
    for axis in axes:
        count *= lax.axis_size(axis)
    first, second = phase[0], phase[-1]
    distances = [first] if len(phase) == 1 else [first, second, first ^ second]
    return [
        lax.ppermute(value, axes, [(source, source ^ distance) for source in range(count)])
        for distance in distances
    ]


def joined(value, others):
    value = value + others[0]
    return value + (others[1] + others[2]) if others[1:] else value


def body(fields, material, pml_width, eps_real, eps_loss, coeffs, ritz):
    _, vectors, _, nz, nx, ny = fields.shape
    f32 = lambda *shape: jax.ShapeDtypeStruct(shape, jnp.float32)
    scratch = lambda *shape: pltpu.VMEM(shape, jnp.float32)
    params = pltpu.CompilerParams(vmem_limit_bytes=40 * 1024 * 1024)
    whole = f32(*fields.shape)
    zf_shape = (2, vectors, 2, nx, ny)
    xf_shape = (2, vectors, 2, nz, ny)
    yf_shape = (4 * vectors, nz * nx)
    faces = (f32(*zf_shape), f32(*xf_shape), f32(*yf_shape))
    near, zf, xf, yf = pl.pallas_call(
        face_kernel,
        out_shape=(whole,) + faces,
        in_specs=[HBM],
        out_specs=(VMEM,) * 4,
        scratch_shapes=[pltpu.SemaphoreType.DMA((2, 3))],
        compiler_params=params,
        name="take_faces",
    )(pltpu.with_memory_space_constraint(fields, pltpu.HBM))
    zf = passed_round(zf, "gz", -1)
    xf = passed_round(xf, "gx", -1)
    yf = passed_round(yf, "gy", -1)
    cells = fields.size // 6 // vectors
    basis = pl.pallas_call(
        rotate_kernel,
        out_shape=whole,
        in_specs=[SMEM, VMEM],
        out_specs=VMEM,
        compiler_params=params,
        cost_estimate=pl.CostEstimate(flops=400 * cells, bytes_accessed=8 * fields.size, transcendentals=0),
        name="rotate_vectors",
    )(coeffs, near)
    image, gram, hzf, hxf, hyf, basis_new = pl.pallas_call(
        image_kernel,
        out_shape=(whole, f32(2, vectors, vectors)) + faces + (whole,),
        in_specs=[SMEM] * 4 + [VMEM] * 5,
        out_specs=(VMEM,) * 5 + (HBM,),
        scratch_shapes=[
            scratch(2, nz, nx, ny),
            scratch(4, nz, ny),
            scratch(vectors, 2 * vectors, 8, ny),
            scratch(*zf_shape),
            scratch(*zf_shape),
            scratch(*xf_shape),
            scratch(ny, nz * nx),
            scratch(nz, nx, ny),
            scratch(nz, nx, ny),
            pltpu.SemaphoreType.DMA,
        ],
        compiler_params=params,
        cost_estimate=pl.CostEstimate(flops=1200 * cells, bytes_accessed=8 * fields.size, transcendentals=0),
        name="apply_operator",
    )(pml_width, eps_real, eps_loss, coeffs, basis, material, zf, xf, yf)
    phases = sum_phases()
    others = from_partners(gram, phases[0])
    hzf = passed_round(hzf, "gz", 1)
    hxf = passed_round(hxf, "gx", 1)
    hyf = passed_round(hyf, "gy", 1)
    for phase in phases[1:]:
        gram = joined(gram, others)
        if phase is phases[-1]:
            gram, image = lax.optimization_barrier((gram, image))
        others = from_partners(gram, phase)
    residual = pl.pallas_call(
        rim_kernel,
        out_shape=whole,
        in_specs=[SMEM] * 2 + [VMEM] * 5,
        out_specs=VMEM,
        scratch_shapes=[scratch(ny, nz * nx), scratch(nz, nx, ny)],
        compiler_params=params,
        cost_estimate=pl.CostEstimate(flops=200 * cells, bytes_accessed=12 * fields.size, transcendentals=0),
        name="add_rims",
    )(pml_width, ritz, basis, image, hzf, hxf, hyf)
    others, residual = lax.optimization_barrier((others, residual))
    return basis_new, residual, joined(gram, others)


def solution(mesh):
    in_specs = (P(None, None, None, "gz", "gx", "gy"), P("gz", "gx", "gy"), P(), P(), P(), P(), P())
    out_specs = (P(None, None, None, "gz", "gx", "gy"), P(None, None, None, "gz", "gx", "gy"), P())
    return jax.shard_map(body, mesh=mesh, in_specs=in_specs, out_specs=out_specs, check_vma=False)
```

```python
import functools

import jax
import jax.numpy as jnp
from jax import lax
from jax.experimental import pallas as pl
from jax.experimental.pallas import tpu as pltpu
from jax.sharding import PartitionSpec as P

OMEGA_SQ = 0.36
SIGMA_TOP = 3.0
BOUNDS = ((4, 5), (0, 1), (2, 3))
AXES = ("gz", "gx", "gy")

VMEM = pl.BlockSpec(memory_space=pltpu.VMEM)
SMEM = pl.BlockSpec(memory_space=pltpu.SMEM)
HBM = pl.BlockSpec(memory_space=pltpu.HBM)
HIGH = lax.Precision.HIGHEST


def passed_round(value, axis, steps):
    count = lax.axis_size(axis)
    return lax.ppermute(value, axis, [(source, (source + steps) % count) for source in range(count)])


def inverse_stretch(places, length, low_width, high_width):
    inside_depth = jnp.clip((low_width - places) / low_width, 0.0, 1.0) + jnp.clip(
        (places + 1.0 - length + high_width) / high_width, 0.0, 1.0
    )
    absorb = SIGMA_TOP * inside_depth * inside_depth
    scaled = 1.0 / (1.0 + absorb * absorb)
    return scaled, -absorb * scaled


def cmul(left, right):
    return (left[0] * right[0] - left[1] * right[1], left[0] * right[1] + left[1] * right[0])


def add(left, right):
    return (left[0] + right[0], left[1] + right[1])


def sub(left, right):
    return (left[0] - right[0], left[1] - right[1])


def axis_stretch(pml_ref, direction, count, places):
    total = count * lax.axis_size(AXES[direction])
    low_slot, high_slot = BOUNDS[direction]
    low = jnp.full(places.shape, pml_ref[low_slot], jnp.int32).astype(jnp.float32)
    high = jnp.full(places.shape, pml_ref[high_slot], jnp.int32).astype(jnp.float32)
    return inverse_stretch(places, jnp.float32(total), low, high)


def local_places(direction, count, shape, dim):
    start = lax.axis_index(AXES[direction]) * count
    return (lax.broadcasted_iota(jnp.int32, shape, dim) + start).astype(jnp.float32)


def one_place(direction, count, offset, shape):
    start = lax.axis_index(AXES[direction]) * count + offset
    return jnp.full(shape, start, jnp.int32).astype(jnp.float32)


def packed_row(slot, part, vector, vectors):
    return (slot * 2 + part) * vectors + vector


def has_neighbour(direction, steps):
    place = lax.axis_index(AXES[direction]) + steps
    inside = (place >= 0) & (place < lax.axis_size(AXES[direction]))
    return jnp.where(inside, 1.0, 0.0).astype(jnp.float32)


def face_kernel(fields_hbm, fields_ref, zf_ref, xf_ref, yf_ref, sems):
    _, vectors, _, nz, nx, ny = fields_ref.shape
    lanes = lax.broadcasted_iota(jnp.int32, (nx, ny), 1)
    copies = [
        pltpu.make_async_copy(fields_hbm.at[part, :, comp], fields_ref.at[part, :, comp], sems.at[part, comp])
        for comp in (0, 2, 1) for part in range(2)
    ]
    for copy in copies:
        copy.start()
    for copy in copies:
        copy.wait()

    packed = [jnp.zeros((nx, ny), jnp.float32)] * nz
    for comp in (0, 2):
        for part in range(2):
            for a in range(vectors):
                row = packed_row(comp // 2, part, a, vectors)
                for z in range(nz):
                    value = fields_ref[part, a, comp, z]
                    packed[z] = jnp.where(lanes == row, pltpu.roll(value, row, 1) if row else value, packed[z])
    turned = jnp.concatenate(packed, axis=0).T
    yf_ref[...] = turned[:yf_ref.shape[0]]
    for part in range(2):
        for a in range(vectors):
            for slot in range(2):
                zf_ref[part, a, slot] = fields_ref[part, a, slot, 0]
                xf_ref[part, a, slot] = fields_ref[part, a, slot + 1, :, 0, :]


def rotated(coeffs_ref, old, b):
    new = None
    for a, value in enumerate(old):
        term = cmul((coeffs_ref[0, a, b], coeffs_ref[1, a, b]), value)
        new = term if new is None else add(new, term)
    return new


def rotate_kernel(coeffs_ref, fields_ref, basis_ref):
    _, vectors, _, nz, nx, ny = fields_ref.shape

    @pl.loop(0, nz)
    def _(z):
        for comp in range(3):
            old = [(fields_ref[0, a, comp, z], fields_ref[1, a, comp, z]) for a in range(vectors)]
            for b in range(vectors):
                new = rotated(coeffs_ref, old, b)
                for part in range(2):
                    basis_ref[part, b, comp, z] = new[part]


def image_kernel(
    pml_ref, eps_real_ref, eps_loss_ref, coeffs_ref,
    basis_ref, material_ref, raw_zf_ref, raw_xf_ref, raw_yf_ref,
    image_ref, gram_ref, hzf_ref, hxf_ref, hyf_ref, basis_hbm,
    eps_ref, sz_ref, acc_ref, lift_ref, zf_ref, xf_ref, yt_ref, yf_ref, packed_ref, sem,
):
    _, vectors, _, nz, nx, ny = basis_ref.shape
    keep = pltpu.make_async_copy(basis_ref, basis_hbm, sem)
    keep.start()
    plane = (nx, ny)
    rows = lax.broadcasted_iota(jnp.int32, plane, 0)
    lanes = lax.broadcasted_iota(jnp.int32, plane, 1)
    shx = axis_stretch(pml_ref, 1, nx, local_places(1, nx, plane, 0) + 0.5)
    sex = axis_stretch(pml_ref, 1, nx, local_places(1, nx, plane, 0))
    shy = axis_stretch(pml_ref, 2, ny, local_places(2, ny, plane, 1) + 0.5)
    sey = axis_stretch(pml_ref, 2, ny, local_places(2, ny, plane, 1))
    table = (nz, ny)
    sez_rows = axis_stretch(pml_ref, 0, nz, local_places(0, nz, table, 0))
    shz_rows = axis_stretch(pml_ref, 0, nz, local_places(0, nz, table, 0) + 0.5)
    for part in range(2):
        sz_ref[part] = sez_rows[part]
        sz_ref[2 + part] = shz_rows[part]
    sz_next = axis_stretch(pml_ref, 0, nz, one_place(0, nz, nz, (1, ny)))
    sx_next = axis_stretch(pml_ref, 1, nx, one_place(1, nx, nx, (1, ny)))
    sy_next = axis_stretch(pml_ref, 2, ny, one_place(2, ny, ny, (1, ny)))

    material = material_ref[...]
    for part, source in enumerate((eps_real_ref, eps_loss_ref)):
        value = jnp.zeros(material.shape, jnp.float32)
        for number in range(source.shape[0]):
            value = jnp.where(material == number, -OMEGA_SQ * source[number], value)
        eps_ref[part] = value

    for direction, raw_ref, face_ref in ((0, raw_zf_ref, zf_ref), (1, raw_xf_ref, xf_ref)):
        inside = has_neighbour(direction, 1)
        for slot in range(2):
            old = [(raw_ref[0, a, slot] * inside, raw_ref[1, a, slot] * inside) for a in range(vectors)]
            for b in range(vectors):
                new = rotated(coeffs_ref, old, b)
                for part in range(2):
                    face_ref[part, b, slot] = new[part]
    inside = has_neighbour(2, 1)
    both = 2 * vectors
    cells = nz * nx
    which = lax.broadcasted_iota(jnp.int32, (both, cells), 0)
    turned = [jnp.zeros((both, cells), jnp.float32)] * 2
    for part in range(2):
        for a in range(vectors):
            column = jnp.zeros((both, cells), jnp.float32)
            for b in range(vectors):
                first, second = coeffs_ref[0, a, b] * inside, coeffs_ref[1, a, b] * inside
                if part:
                    first, second = -second, first
                column = jnp.where(which == b, first, column)
                column = jnp.where(which == vectors + b, second, column)
            for slot in range(2):
                row = packed_row(slot, part, a, vectors)
                turned[slot] = turned[slot] + column * raw_yf_ref[row:row + 1]
    yt_ref[...] = jnp.zeros(yt_ref.shape, jnp.float32)
    for slot in range(2):
        yt_ref[slot * both:(slot + 1) * both] = turned[slot]
    yf_ref[...] = yt_ref[...].T.reshape(nz, nx, ny)

    for a in range(vectors):
        for comp in range(2):
            scaled = cmul(sz_next, (zf_ref[0, a, comp], zf_ref[1, a, comp]))
            for part in range(2):
                lift_ref[part, a, comp] = scaled[part]

    def field(b, comp, z):
        return (basis_ref[0, b, comp, z], basis_ref[1, b, comp, z])

    def ahead_x(value, b, comp, z):
        return tuple(
            jnp.where(rows == nx - 1, xf_ref[part, b, comp - 1, pl.ds(z, 1)], pltpu.roll(value[part], nx - 1, 0))
            for part in range(2)
        )

    def ahead_y(value, b, comp, z):
        out = []
        for part in range(2):
            row = packed_row(comp // 2, part, b, vectors)
            edge = pltpu.roll(yf_ref[z], ny - 1 - row, 1)
            out.append(jnp.where(lanes == ny - 1, edge, pltpu.roll(value[part], ny - 1, 1)))
        return tuple(out)

    def behind(value, axis):
        places = rows if axis == 0 else lanes
        return tuple(jnp.where(places == 0, 0.0, pltpu.roll(value[part], 1, axis)) for part in range(2))

    def fold(value):
        return functools.reduce(jnp.add, [value[row:row + 8] for row in range(0, value.shape[0], 8)])

    @pl.loop(0, nz)
    def _(z):
        packed_ref[z] = jnp.zeros(plane, jnp.float32)

    for b in range(vectors):

        def step(z, carry, last, b=b):
            hx_before, hy_before, sums = carry
            sez = (sz_ref[0, pl.ds(z, 1)], sz_ref[1, pl.ds(z, 1)])
            shz = (sz_ref[2, pl.ds(z, 1)], sz_ref[3, pl.ds(z, 1)])
            u = [field(b, comp, z) for comp in range(3)]
            if last:
                up = [(zf_ref[0, b, comp], zf_ref[1, b, comp]) for comp in range(2)]
            else:
                up = [field(b, comp, z + 1) for comp in range(2)]
            dzx, dzy = (cmul(shz, sub(up[comp], u[comp])) for comp in range(2))
            dxy, dxz = (cmul(shx, sub(ahead_x(u[comp], b, comp, z), u[comp])) for comp in (1, 2))
            dyx, dyz = (cmul(shy, sub(ahead_y(u[comp], b, comp, z), u[comp])) for comp in (0, 2))
            hx, hy, hz = sub(dyz, dzy), sub(dzx, dxz), sub(dxy, dyx)
            byz, byx = (cmul(sey, sub(h, behind(h, 1))) for h in (hz, hx))
            bxz, bxy = (cmul(sex, sub(h, behind(h, 0))) for h in (hz, hy))
            bzy = cmul(sez, sub(hy, hy_before))
            bzx = cmul(sez, sub(hx, hx_before))
            eps = (eps_ref[0, z], eps_ref[1, z])
            w = [
                add(curl, cmul(eps, u[comp]))
                for comp, curl in enumerate((sub(byz, bzy), sub(bzx, bxz), sub(bxy, byx)))
            ]
            for comp in range(3):
                for part in range(2):
                    image_ref[part, b, comp, z] = w[comp][part]
            for part in range(2):
                hxf_ref[part, b, 0, pl.ds(z, 1)] = hy[part][nx - 1:nx]
                hxf_ref[part, b, 1, pl.ds(z, 1)] = hz[part][nx - 1:nx]
            packed = packed_ref[z]
            for slot, value in enumerate((hz, hx)):
                for part in range(2):
                    row = packed_row(slot, part, b, vectors)
                    packed = jnp.where(lanes == row, pltpu.roll(value[part], (row + 1) % ny, 1), packed)
            packed_ref[z] = packed
            new_sums = []
            for a in range(vectors):
                total = None
                for comp in range(3):
                    term = cmul(field(a, comp, z), w[comp])
                    total = term if total is None else add(total, term)
                if last:
                    total = add(total, cmul((lift_ref[0, a, 0], lift_ref[1, a, 0]), hy))
                    total = sub(total, cmul((lift_ref[0, a, 1], lift_ref[1, a, 1]), hx))
                new_sums.append((sums[a][0] + fold(total[0]), sums[a][1] + fold(total[1])))
            if last:
                for part in range(2):
                    hzf_ref[part, b, 0] = hx[part]
                    hzf_ref[part, b, 1] = hy[part]
            return hx, hy, tuple(new_sums)

        zero = jnp.zeros(plane, jnp.float32)
        none = jnp.zeros((8, ny), jnp.float32)
        carry = ((zero, zero), (zero, zero), tuple((none, none) for _ in range(vectors)))
        carry = lax.fori_loop(0, nz - 1, lambda z, c: step(z, c, False), carry)
        _, _, sums = step(nz - 1, carry, True)
        h_y = (hxf_ref[0, b, 0], hxf_ref[1, b, 0])
        h_z = (hxf_ref[0, b, 1], hxf_ref[1, b, 1])
        for a in range(vectors):
            over = cmul((xf_ref[0, a, 0], xf_ref[1, a, 0]), h_z)
            over = sub(over, cmul((xf_ref[0, a, 1], xf_ref[1, a, 1]), h_y))
            over = cmul(sx_next, over)
            for part in range(2):
                acc_ref[b, part * vectors + a] = sums[a][part] + fold(over[part])

    hyf_ref[...] = packed_ref[...].reshape(cells, ny).T[:2 * both]
    pairs = lax.dot_general(
        yt_ref[0:2 * both], hyf_ref[...], (((1,), (1,)), ((), ())),
        precision=HIGH, preferred_element_type=jnp.float32,
    )
    block = pairs[both:2 * both, both:2 * both] - pairs[0:both, 0:both]
    side = cmul(
        (sy_next[0][:, :vectors], sy_next[1][:, :vectors]),
        (
            block[:vectors, :vectors] - block[vectors:, vectors:],
            block[:vectors, vectors:] + block[vectors:, :vectors],
        ),
    )
    totals = jnp.sum(jnp.sum(acc_ref[...], axis=2), axis=2, keepdims=True)
    columns = lax.broadcasted_iota(jnp.int32, (both, ny), 1)
    body_sum = jnp.zeros((both, ny), jnp.float32)
    for b in range(vectors):
        body_sum = jnp.where(columns == b, totals[b], body_sum)
    everywhere = 3.0 * nz * nx * ny
    for axis in AXES:
        everywhere = everywhere * lax.axis_size(axis)
    for part in range(2):
        whole = body_sum[part * vectors:(part + 1) * vectors, :vectors] + side[part]
        gram_ref[part] = whole * (1.0 / everywhere)
    keep.wait()


def rim_kernel(
    pml_ref, ritz_ref, basis_ref, image_ref, hzf_ref, hxf_ref, hyf_ref, residual_ref, yt_ref, packed_ref
):
    _, vectors, _, nz, nx, ny = basis_ref.shape
    plane = (nx, ny)
    rows = lax.broadcasted_iota(jnp.int32, plane, 0)
    lanes = lax.broadcasted_iota(jnp.int32, plane, 1)
    sez = axis_stretch(pml_ref, 0, nz, one_place(0, nz, 0, plane))
    sex = axis_stretch(pml_ref, 1, nx, one_place(1, nx, 0, (1, ny)))
    sey = axis_stretch(pml_ref, 2, ny, one_place(2, ny, 0, plane))
    none = jnp.zeros(plane, jnp.float32)
    sez = tuple(part * has_neighbour(0, -1) for part in sez)
    sex = tuple(jnp.where(rows == 0, part * has_neighbour(1, -1), none) for part in sex)
    sey = tuple(jnp.where(lanes == 0, part * has_neighbour(2, -1), none) for part in sey)
    yt_ref[...] = jnp.zeros(yt_ref.shape, jnp.float32)
    yt_ref[:hyf_ref.shape[0]] = hyf_ref[...]
    packed_ref[...] = yt_ref[...].T.reshape(nz, nx, ny)

    def step(z, first):
        packed = packed_ref[z]
        for b in range(vectors):

            def column(slot, b=b):
                return tuple(
                    pltpu.roll(packed, (ny - packed_row(slot, part, b, vectors)) % ny, 1) for part in range(2)
                )

            def row(slot, b=b):
                return tuple(hxf_ref[part, b, slot, pl.ds(z, 1)] for part in range(2))

            factor = (ritz_ref[0, b], ritz_ref[1, b])
            left = []
            for comp in range(3):
                u = (basis_ref[0, b, comp, z], basis_ref[1, b, comp, z])
                w = (image_ref[0, b, comp, z], image_ref[1, b, comp, z])
                left.append(sub(w, cmul(factor, u)))
            left[0] = sub(left[0], cmul(sey, column(0)))
            left[2] = add(left[2], cmul(sey, column(1)))
            left[1] = add(left[1], cmul(sex, row(1)))
            left[2] = sub(left[2], cmul(sex, row(0)))
            if first:
                left[0] = add(left[0], cmul(sez, (hzf_ref[0, b, 1], hzf_ref[1, b, 1])))
                left[1] = sub(left[1], cmul(sez, (hzf_ref[0, b, 0], hzf_ref[1, b, 0])))
            for comp in range(3):
                for part in range(2):
                    residual_ref[part, b, comp, z] = left[comp][part]

    step(0, True)

    @pl.loop(1, nz)
    def _(z):
        step(z, False)


def body(fields, material, pml_width, eps_real, eps_loss, coeffs, ritz):
    _, vectors, _, nz, nx, ny = fields.shape
    f32 = lambda *shape: jax.ShapeDtypeStruct(shape, jnp.float32)
    scratch = lambda *shape: pltpu.VMEM(shape, jnp.float32)
    params = pltpu.CompilerParams(vmem_limit_bytes=40 * 1024 * 1024)
    whole = f32(*fields.shape)
    zf_shape = (2, vectors, 2, nx, ny)
    xf_shape = (2, vectors, 2, nz, ny)
    yf_shape = (4 * vectors, nz * nx)
    faces = (f32(*zf_shape), f32(*xf_shape), f32(*yf_shape))
    near, zf, xf, yf = pl.pallas_call(
        face_kernel,
        out_shape=(whole,) + faces,
        in_specs=[HBM],
        out_specs=(VMEM,) * 4,
        scratch_shapes=[pltpu.SemaphoreType.DMA((2, 3))],
        compiler_params=params,
        name="take_faces",
    )(pltpu.with_memory_space_constraint(fields, pltpu.HBM))
    zf = passed_round(zf, "gz", -1)
    xf = passed_round(xf, "gx", -1)
    yf = passed_round(yf, "gy", -1)
    cells = fields.size // 6 // vectors
    basis = pl.pallas_call(
        rotate_kernel,
        out_shape=whole,
        in_specs=[SMEM, VMEM],
        out_specs=VMEM,
        compiler_params=params,
        cost_estimate=pl.CostEstimate(flops=400 * cells, bytes_accessed=8 * fields.size, transcendentals=0),
        name="rotate_vectors",
    )(coeffs, near)
    image, gram, hzf, hxf, hyf, basis_new = pl.pallas_call(
        image_kernel,
        out_shape=(whole, f32(2, vectors, vectors)) + faces + (whole,),
        in_specs=[SMEM] * 4 + [VMEM] * 5,
        out_specs=(VMEM,) * 5 + (HBM,),
        scratch_shapes=[
            scratch(2, nz, nx, ny),
            scratch(4, nz, ny),
            scratch(vectors, 2 * vectors, 8, ny),
            scratch(*zf_shape),
            scratch(*zf_shape),
            scratch(*xf_shape),
            scratch(ny, nz * nx),
            scratch(nz, nx, ny),
            scratch(nz, nx, ny),
            pltpu.SemaphoreType.DMA,
        ],
        compiler_params=params,
        cost_estimate=pl.CostEstimate(flops=1200 * cells, bytes_accessed=8 * fields.size, transcendentals=0),
        name="apply_operator",
    )(pml_width, eps_real, eps_loss, coeffs, basis, material, zf, xf, yf)
    grams = lax.all_gather(gram, ("gx", "gy", "gz"))
    hzf = passed_round(hzf, "gz", 1)
    hxf = passed_round(hxf, "gx", 1)
    hyf = passed_round(hyf, "gy", 1)
    residual = pl.pallas_call(
        rim_kernel,
        out_shape=whole,
        in_specs=[SMEM] * 2 + [VMEM] * 5,
        out_specs=VMEM,
        scratch_shapes=[scratch(ny, nz * nx), scratch(nz, nx, ny)],
        compiler_params=params,
        cost_estimate=pl.CostEstimate(flops=200 * cells, bytes_accessed=12 * fields.size, transcendentals=0),
        name="add_rims",
    )(pml_width, ritz, basis, image, hzf, hxf, hyf)
    grams, residual = lax.optimization_barrier((grams, residual))
    return basis_new, residual, jnp.sum(grams, axis=0)


def solution(mesh):
    in_specs = (P(None, None, None, "gz", "gx", "gy"), P("gz", "gx", "gy"), P(), P(), P(), P(), P())
    out_specs = (P(None, None, None, "gz", "gx", "gy"), P(None, None, None, "gz", "gx", "gy"), P())
    return jax.shard_map(body, mesh=mesh, in_specs=in_specs, out_specs=out_specs, check_vma=False)
```

```python
import functools

import jax
import jax.numpy as jnp
from jax import lax
from jax.experimental import pallas as pl
from jax.experimental.pallas import tpu as pltpu
from jax.sharding import PartitionSpec as P

OMEGA_SQ = 0.36
SIGMA_TOP = 3.0
BOUNDS = ((4, 5), (0, 1), (2, 3))
AXES = ("gz", "gx", "gy")

VMEM = pl.BlockSpec(memory_space=pltpu.VMEM)
SMEM = pl.BlockSpec(memory_space=pltpu.SMEM)
HBM = pl.BlockSpec(memory_space=pltpu.HBM)


def passed_round(value, axis, steps):
    count = lax.axis_size(axis)
    return lax.ppermute(value, axis, [(source, (source + steps) % count) for source in range(count)])


def inverse_stretch(places, length, low_width, high_width):
    inside_depth = jnp.clip((low_width - places) / low_width, 0.0, 1.0) + jnp.clip(
        (places + 1.0 - length + high_width) / high_width, 0.0, 1.0
    )
    absorb = SIGMA_TOP * inside_depth * inside_depth
    scaled = 1.0 / (1.0 + absorb * absorb)
    return scaled, -absorb * scaled


def cmul(left, right):
    return (left[0] * right[0] - left[1] * right[1], left[0] * right[1] + left[1] * right[0])


def add(left, right):
    return (left[0] + right[0], left[1] + right[1])


def sub(left, right):
    return (left[0] - right[0], left[1] - right[1])


def axis_stretch(pml_ref, direction, count, places):
    total = count * lax.axis_size(AXES[direction])
    low_slot, high_slot = BOUNDS[direction]
    low = jnp.full(places.shape, pml_ref[low_slot], jnp.int32).astype(jnp.float32)
    high = jnp.full(places.shape, pml_ref[high_slot], jnp.int32).astype(jnp.float32)
    return inverse_stretch(places, jnp.float32(total), low, high)


def local_places(direction, count, shape, dim):
    start = lax.axis_index(AXES[direction]) * count
    return (lax.broadcasted_iota(jnp.int32, shape, dim) + start).astype(jnp.float32)


def one_place(direction, count, offset, shape):
    start = lax.axis_index(AXES[direction]) * count + offset
    return jnp.full(shape, start, jnp.int32).astype(jnp.float32)


def packed_row(slot, part, vector, vectors):
    return (slot * 2 + part) * vectors + vector


def has_neighbour(direction, steps):
    place = lax.axis_index(AXES[direction]) + steps
    inside = (place >= 0) & (place < lax.axis_size(AXES[direction]))
    return jnp.where(inside, 1.0, 0.0).astype(jnp.float32)


def face_kernel(fields_hbm, fields_ref, zf_ref, xf_ref, yf_ref, sems):
    _, vectors, _, nz, nx, ny = fields_ref.shape
    lanes = lax.broadcasted_iota(jnp.int32, (nx, ny), 1)
    copies = [
        pltpu.make_async_copy(fields_hbm.at[part, :, comp], fields_ref.at[part, :, comp], sems.at[part, comp])
        for comp in (0, 2, 1) for part in range(2)
    ]
    for copy in copies:
        copy.start()
    for copy in copies:
        copy.wait()

    packed = [jnp.zeros((nx, ny), jnp.float32)] * nz
    for comp in (0, 2):
        for part in range(2):
            for a in range(vectors):
                row = packed_row(comp // 2, part, a, vectors)
                for z in range(nz):
                    value = fields_ref[part, a, comp, z]
                    packed[z] = jnp.where(lanes == row, pltpu.roll(value, row, 1) if row else value, packed[z])
    turned = jnp.concatenate(packed, axis=0).T
    yf_ref[...] = turned[:yf_ref.shape[0]]
    for part in range(2):
        for a in range(vectors):
            for slot in range(2):
                zf_ref[part, a, slot] = fields_ref[part, a, slot, 0]
                xf_ref[part, a, slot] = fields_ref[part, a, slot + 1, :, 0, :]


def rotated(coeffs_ref, old, b):
    new = None
    for a, value in enumerate(old):
        term = cmul((coeffs_ref[0, a, b], coeffs_ref[1, a, b]), value)
        new = term if new is None else add(new, term)
    return new


SUB = 8
SHX, SEX, SHY, SEY = range(0, 8, 2)


def prepare_kernel(
    pml_ref, eps_real_ref, eps_loss_ref, coeffs_ref, fields_ref, material_ref,
    basis_ref, eps_ref, table_ref, sz_ref,
):
    _, vectors, _, nz, nx, ny = fields_ref.shape
    plane = (nx, ny)
    for slot, direction, half, count, dim in (
        (SHX, 1, 0.5, nx, 0), (SEX, 1, 0.0, nx, 0), (SHY, 2, 0.5, ny, 1), (SEY, 2, 0.0, ny, 1),
    ):
        values = axis_stretch(pml_ref, direction, count, local_places(direction, count, plane, dim) + half)
        for part in range(2):
            table_ref[slot + part] = values[part]
    for slot, half in ((0, 0.0), (2, 0.5)):
        values = axis_stretch(pml_ref, 0, nz, local_places(0, nz, (nz, ny), 0) + half)
        for part in range(2):
            sz_ref[slot + part] = values[part]

    @pl.loop(0, nz)
    def _(z):
        material = material_ref[z]
        for part, source in enumerate((eps_real_ref, eps_loss_ref)):
            value = jnp.zeros(plane, jnp.float32)
            for number in range(source.shape[0]):
                value = jnp.where(material == number, -OMEGA_SQ * source[number], value)
            eps_ref[part, z] = value
        for comp in range(3):
            old = [(fields_ref[0, a, comp, z], fields_ref[1, a, comp, z]) for a in range(vectors)]
            for b in range(vectors):
                new = rotated(coeffs_ref, old, b)
                for part in range(2):
                    basis_ref[part, b, comp, z] = new[part]


def turn_face(coeffs_ref, direction, raw_ref, face_ref):
    inside = has_neighbour(direction, 1)
    vectors = raw_ref.shape[1]
    for slot in range(2):
        old = [(raw_ref[0, a, slot] * inside, raw_ref[1, a, slot] * inside) for a in range(vectors)]
        for b in range(vectors):
            new = rotated(coeffs_ref, old, b)
            for part in range(2):
                face_ref[part, b, slot] = new[part]


def turn_column(coeffs_ref, raw_ref, rows_ref, cells_ref):
    vectors = coeffs_ref.shape[1]
    nz, nx, ny = cells_ref.shape
    inside = has_neighbour(2, 1)
    both = 2 * vectors
    which = lax.broadcasted_iota(jnp.int32, (both, nz * nx), 0)
    turned = [jnp.zeros((both, nz * nx), jnp.float32)] * 2
    for part in range(2):
        for a in range(vectors):
            column = jnp.zeros((both, nz * nx), jnp.float32)
            for b in range(vectors):
                first, second = coeffs_ref[0, a, b] * inside, coeffs_ref[1, a, b] * inside
                if part:
                    first, second = -second, first
                column = jnp.where(which == b, first, column)
                column = jnp.where(which == vectors + b, second, column)
            for slot in range(2):
                row = packed_row(slot, part, a, vectors)
                turned[slot] = turned[slot] + column * raw_ref[row:row + 1]
    for slot in range(2):
        rows_ref[slot * both:(slot + 1) * both] = turned[slot]
    rest = jnp.zeros((ny - 2 * both, nz * nx), jnp.float32)
    cells_ref[...] = jnp.concatenate(turned + [rest], axis=0).T.reshape(nz, nx, ny)


def plane_step(
    b, z, before, sums, up_of, basis_ref, eps_ref, table_ref, sz_ref, xf_ref, yf_ref, image_ref, hxf_ref, packed_ref
):
    _, vectors, _, _, nx, ny = basis_ref.shape
    tile = (SUB, ny)
    rows = lax.broadcasted_iota(jnp.int32, tile, 0)
    lanes = lax.broadcasted_iota(jnp.int32, tile, 1)
    parts = range(2)
    count = nx // SUB
    cut = [slice(SUB * t, SUB * (t + 1)) for t in range(count)]

    def table(slot, t):
        return tuple(table_ref[slot + part, cut[t]] for part in parts)

    sez = tuple(sz_ref[part, pl.ds(z, 1)] for part in parts)
    shz = tuple(sz_ref[2 + part, pl.ds(z, 1)] for part in parts)
    shy, sey = table(SHY, 0), table(SEY, 0)

    def turned_up(comp, t):
        return tuple(pltpu.roll(basis_ref[part, b, comp, z, cut[t]], SUB - 1, 0) for part in parts)

    sums = list(sums)
    after, behind_y, behind_z = [], None, None
    for t in range(count):
        u = [tuple(basis_ref[part, b, comp, z, cut[t]] for part in parts) for comp in range(3)]
        up = [up_of(comp, t) for comp in range(2)]
        dzx, dzy = (cmul(shz, sub(up[comp], u[comp])) for comp in range(2))

        def ahead_x(comp):
            if t + 1 < count:
                edge = turned_up(comp, t + 1)
            else:
                edge = tuple(xf_ref[part, b, comp - 1, pl.ds(z, 1)] for part in parts)
            here = turned_up(comp, t)
            return tuple(jnp.where(rows == SUB - 1, edge[part], here[part]) for part in parts)

        def ahead_y(comp):
            out = []
            for part in parts:
                row = packed_row(comp // 2, part, b, vectors)
                edge = pltpu.roll(yf_ref[z, cut[t]], ny - 1 - row, 1)
                out.append(jnp.where(lanes == ny - 1, edge, pltpu.roll(u[comp][part], ny - 1, 1)))
            return tuple(out)

        shx, sex = table(SHX, t), table(SEX, t)
        dxy, dxz = (cmul(shx, sub(ahead_x(comp), u[comp])) for comp in (1, 2))
        dyx, dyz = (cmul(shy, sub(ahead_y(comp), u[comp])) for comp in (0, 2))
        hx, hy, hz = sub(dyz, dzy), sub(dzx, dxz), sub(dxy, dyx)

        def behind_x(here, past):
            return tuple(
                jnp.where(rows == 0, 0.0 if past is None else past[part], here[part]) for part in parts
            )

        def back_y(value):
            return tuple(jnp.where(lanes == 0, 0.0, pltpu.roll(value[part], 1, 1)) for part in parts)

        down_y = tuple(pltpu.roll(hy[part], 1, 0) for part in parts)
        down_z = tuple(pltpu.roll(hz[part], 1, 0) for part in parts)
        bxy = cmul(sex, sub(hy, behind_x(down_y, behind_y)))
        bxz = cmul(sex, sub(hz, behind_x(down_z, behind_z)))
        behind_y, behind_z = down_y, down_z
        byz, byx = (cmul(sey, sub(h, back_y(h))) for h in (hz, hx))
        bzx, bzy = (cmul(sez, sub(h, past)) for h, past in zip((hx, hy), before[t]))
        eps = tuple(eps_ref[part, z, cut[t]] for part in parts)
        w = [
            add(curl, cmul(eps, u[comp]))
            for comp, curl in enumerate((sub(byz, bzy), sub(bzx, bxz), sub(bxy, byx)))
        ]
        for comp in range(3):
            for part in parts:
                image_ref[part, b, comp, z, cut[t]] = w[comp][part]
        for a in range(vectors):
            total = sums[a]
            for comp in range(3):
                total = add(total, cmul(tuple(basis_ref[part, a, comp, z, cut[t]] for part in parts), w[comp]))
            sums[a] = total
        packed = packed_ref[z, cut[t]]
        for slot, value in enumerate((hz, hx)):
            for part in parts:
                row = packed_row(slot, part, b, vectors)
                packed = jnp.where(lanes == row, pltpu.roll(value[part], (row + 1) % ny, 1), packed)
        packed_ref[z, cut[t]] = packed
        after.append((hx, hy))
    for part in parts:
        hxf_ref[part, b, 0, pl.ds(z, 1)] = hy[part][SUB - 1:]
        hxf_ref[part, b, 1, pl.ds(z, 1)] = hz[part][SUB - 1:]
    return after, sums


def inner_kernel(
    coeffs_ref, basis_ref, eps_ref, table_ref, sz_ref, raw_xf_ref, raw_yf_ref,
    image_ref, acc_ref, before_ref, hxf_ref, packed_ref, xf_ref, yt_ref, yf_ref, basis_hbm, sem,
):
    _, vectors, _, nz, nx, ny = basis_ref.shape
    keep = pltpu.make_async_copy(basis_ref, basis_hbm, sem)
    keep.start()
    turn_face(coeffs_ref, 1, raw_xf_ref, xf_ref)
    turn_column(coeffs_ref, raw_yf_ref, yt_ref, yf_ref)
    packed_ref[...] = jnp.zeros(packed_ref.shape, jnp.float32)
    count = nx // SUB

    for b in range(vectors):

        def step(z, carry, b=b):
            def up_of(comp, t):
                return tuple(basis_ref[part, b, comp, z + 1, SUB * t:SUB * (t + 1)] for part in range(2))

            return plane_step(
                b, z, *carry, up_of, basis_ref, eps_ref, table_ref, sz_ref, xf_ref, yf_ref,
                image_ref, hxf_ref, packed_ref,
            )

        none = (jnp.zeros((SUB, ny), jnp.float32),) * 2
        before, sums = lax.fori_loop(0, nz - 1, step, ([(none, none)] * count, [none] * vectors))
        for part in range(2):
            for a in range(vectors):
                acc_ref[b, part * vectors + a] = sums[a][part]
            for t in range(count):
                for slot in range(2):
                    before_ref[part, b, slot, SUB * t:SUB * (t + 1)] = before[t][slot][part]
    keep.wait()


def outer_kernel(
    pml_ref, coeffs_ref, basis_ref, eps_ref, table_ref, sz_ref, raw_zf_ref, xf_ref, yt_ref, yf_ref,
    image_in, acc_ref, before_ref, hxf_in, packed_in,
    image_ref, hxf_ref, packed_ref, gram_ref, hzf_ref, hyf_ref, zf_ref,
):
    del image_in, hxf_in, packed_in
    _, vectors, _, nz, nx, ny = basis_ref.shape
    count = nx // SUB
    turn_face(coeffs_ref, 0, raw_zf_ref, zf_ref)
    sz_next = axis_stretch(pml_ref, 0, nz, one_place(0, nz, nz, (1, ny)))
    sx_next = axis_stretch(pml_ref, 1, nx, one_place(1, nx, nx, (1, ny)))
    sy_next = axis_stretch(pml_ref, 2, ny, one_place(2, ny, ny, (1, nz * nx)))
    all_sums = []
    for b in range(vectors):

        def tile_of(ref, slot, t, b=b):
            return tuple(ref[part, b, slot, SUB * t:SUB * (t + 1)] for part in range(2))

        before = [tuple(tile_of(before_ref, slot, t) for slot in range(2)) for t in range(count)]
        sums = [(acc_ref[b, a], acc_ref[b, vectors + a]) for a in range(vectors)]
        after, sums = plane_step(
            b, nz - 1, before, sums, functools.partial(tile_of, zf_ref), basis_ref, eps_ref, table_ref, sz_ref,
            xf_ref, yf_ref, image_ref, hxf_ref, packed_ref,
        )
        h_y = tuple(hxf_ref[part, b, 0] for part in range(2))
        h_z = tuple(hxf_ref[part, b, 1] for part in range(2))
        for a in range(vectors):
            over = None
            for t, (hx, hy) in enumerate(after):
                ends = [tuple(zf_ref[part, a, slot, SUB * t:SUB * (t + 1)] for part in range(2)) for slot in range(2)]
                term = sub(cmul(ends[0], hy), cmul(ends[1], hx))
                over = term if over is None else add(over, term)
            total = add(sums[a], cmul(sz_next, over))
            over = cmul(tuple(xf_ref[part, a, 0] for part in range(2)), h_z)
            over = sub(over, cmul(tuple(xf_ref[part, a, 1] for part in range(2)), h_y))
            over = cmul(sx_next, over)
            for row in range(0, nz, SUB):
                total = add(total, tuple(part[row:row + SUB] for part in over))
            sums[a] = total
        all_sums.append(sums)
        for part in range(2):
            for t, pair in enumerate(after):
                for slot in range(2):
                    hzf_ref[part, b, slot, SUB * t:SUB * (t + 1)] = pair[slot][part]

    both = 2 * vectors
    hyf_ref[...] = packed_ref[...].reshape(nz * nx, ny).T[:2 * both]
    ends = [
        cmul(sy_next, (yt_ref[slot * both:slot * both + vectors], yt_ref[slot * both + vectors:(slot + 1) * both]))
        for slot in range(2)
    ]
    columns = lax.broadcasted_iota(jnp.int32, (both, ny), 1)
    gram = jnp.zeros((both, ny), jnp.float32)
    for b in range(vectors):
        flat = jnp.concatenate(
            [jnp.sum(all_sums[b][a][part], axis=0, keepdims=True) for part in range(2) for a in range(vectors)], axis=0
        )
        over = None
        for slot in range(2):
            h = tuple(hyf_ref[packed_row(slot, part, b, vectors)][None] for part in range(2))
            term = cmul(ends[slot], h)
            over = term if over is None else sub(term, over)
        side = jnp.concatenate(over, axis=0)
        total = jnp.sum(flat, axis=1, keepdims=True) + jnp.sum(side, axis=1, keepdims=True)
        gram = jnp.where(columns == b, total, gram)
    everywhere = 3.0 * nz * nx * ny
    for axis in AXES:
        everywhere = everywhere * lax.axis_size(axis)
    gram = gram * (1.0 / everywhere)
    for part in range(2):
        gram_ref[part] = gram[part * vectors:(part + 1) * vectors, :vectors]


def rim_kernel(
    pml_ref, ritz_ref, basis_ref, image_ref, hzf_ref, hxf_ref, hyf_ref, residual_hbm, residual_ref, packed_ref, sems
):
    _, vectors, _, nz, nx, ny = basis_ref.shape
    plane = (nx, ny)
    rows = lax.broadcasted_iota(jnp.int32, plane, 0)
    lanes = lax.broadcasted_iota(jnp.int32, plane, 1)
    sez = axis_stretch(pml_ref, 0, nz, one_place(0, nz, 0, plane))
    sex = axis_stretch(pml_ref, 1, nx, one_place(1, nx, 0, (1, ny)))
    sey = axis_stretch(pml_ref, 2, ny, one_place(2, ny, 0, plane))
    none = jnp.zeros(plane, jnp.float32)
    sez = tuple(part * has_neighbour(0, -1) for part in sez)
    sex = tuple(jnp.where(rows == 0, part * has_neighbour(1, -1), none) for part in sex)
    sey = tuple(jnp.where(lanes == 0, part * has_neighbour(2, -1), none) for part in sey)
    rest = jnp.zeros((ny - hyf_ref.shape[0], nz * nx), jnp.float32)
    packed_ref[...] = jnp.concatenate([hyf_ref[...], rest], axis=0).T.reshape(nz, nx, ny)

    def kept(z):
        return pltpu.make_async_copy(residual_ref.at[:, :, :, z], residual_hbm.at[:, :, :, z], sems.at[z])

    def step(z, first):
        packed = packed_ref[z]
        for b in range(vectors):

            def column(slot, b=b):
                return tuple(
                    pltpu.roll(packed, (ny - packed_row(slot, part, b, vectors)) % ny, 1) for part in range(2)
                )

            def row(slot, b=b):
                return tuple(hxf_ref[part, b, slot, pl.ds(z, 1)] for part in range(2))

            factor = (ritz_ref[0, b], ritz_ref[1, b])
            left = []
            for comp in range(3):
                u = (basis_ref[0, b, comp, z], basis_ref[1, b, comp, z])
                w = (image_ref[0, b, comp, z], image_ref[1, b, comp, z])
                left.append(sub(w, cmul(factor, u)))
            left[0] = sub(left[0], cmul(sey, column(0)))
            left[2] = add(left[2], cmul(sey, column(1)))
            left[1] = add(left[1], cmul(sex, row(1)))
            left[2] = sub(left[2], cmul(sex, row(0)))
            if first:
                left[0] = add(left[0], cmul(sez, (hzf_ref[0, b, 1], hzf_ref[1, b, 1])))
                left[1] = sub(left[1], cmul(sez, (hzf_ref[0, b, 0], hzf_ref[1, b, 0])))
            for comp in range(3):
                for part in range(2):
                    residual_ref[part, b, comp, z] = left[comp][part]
        kept(z).start()

    step(0, True)

    @pl.loop(1, nz)
    def _(z):
        step(z, False)

    @pl.loop(0, nz)
    def _(z):
        kept(z).wait()


def sum_phases():
    sizes = [lax.axis_size(axis) for axis in ("gx", "gy", "gz")]
    if any(size & (size - 1) for size in sizes):
        return None
    across = sizes[1] * sizes[2]
    masks = [1 << bit for bit in range((sizes[0] * across).bit_length() - 1)]
    along = [mask for mask in masks if mask >= across]
    rest = [mask for mask in masks if mask < across]
    phases = [along[place:place + 2] for place in range(1, len(along), 2)] + [along[:1]]
    phases += [rest[place:place + 2] for place in range(0, len(rest), 2)]
    return [phase for phase in phases if phase]


def from_partners(value, phase):
    axes = ("gx", "gy", "gz")
    count = 1
    for axis in axes:
        count *= lax.axis_size(axis)
    first, second = phase[0], phase[-1]
    distances = [first] if len(phase) == 1 else [first, second, first ^ second]
    return [
        lax.ppermute(value, axes, [(source, source ^ distance) for source in range(count)])
        for distance in distances
    ]


def joined(value, others):
    value = value + others[0]
    return value + (others[1] + others[2]) if others[1:] else value


def body(fields, material, pml_width, eps_real, eps_loss, coeffs, ritz):
    _, vectors, _, nz, nx, ny = fields.shape
    f32 = lambda *shape: jax.ShapeDtypeStruct(shape, jnp.float32)
    scratch = lambda *shape: pltpu.VMEM(shape, jnp.float32)
    params = pltpu.CompilerParams(vmem_limit_bytes=40 * 1024 * 1024)
    whole = f32(*fields.shape)
    zf_shape = (2, vectors, 2, nx, ny)
    xf_shape = (2, vectors, 2, nz, ny)
    yf_shape = (4 * vectors, nz * nx)
    faces = (f32(*zf_shape), f32(*xf_shape), f32(*yf_shape))
    near, zf, xf, yf = pl.pallas_call(
        face_kernel,
        out_shape=(whole,) + faces,
        in_specs=[HBM],
        out_specs=(VMEM,) * 4,
        scratch_shapes=[pltpu.SemaphoreType.DMA((2, 3))],
        compiler_params=params,
        name="take_faces",
    )(pltpu.with_memory_space_constraint(fields, pltpu.HBM))
    xf = passed_round(xf, "gx", -1)
    yf = passed_round(yf, "gy", -1)
    zf = passed_round(zf, "gz", -1)
    cells = fields.size // 6 // vectors

    def cost(flops, passes):
        return pl.CostEstimate(flops=flops * cells, bytes_accessed=passes * 4 * fields.size, transcendentals=0)

    planes = f32(nz, nx, ny)
    basis, eps, table, sz = pl.pallas_call(
        prepare_kernel,
        out_shape=(whole, f32(2, nz, nx, ny), f32(8, nx, ny), f32(4, nz, ny)),
        in_specs=[SMEM] * 4 + [VMEM] * 2,
        out_specs=(VMEM,) * 4,
        compiler_params=params,
        cost_estimate=cost(400, 2),
        name="prepare",
    )(pml_width, eps_real, eps_loss, coeffs, near, material)
    image, acc, before, hxf, packed, xf, yt, yf, basis_new = pl.pallas_call(
        inner_kernel,
        out_shape=(
            whole, f32(vectors, 2 * vectors, SUB, ny), f32(*zf_shape), f32(*xf_shape), planes,
            f32(*xf_shape), f32(*yf_shape), planes, whole,
        ),
        in_specs=[SMEM] + [VMEM] * 6,
        out_specs=(VMEM,) * 8 + (HBM,),
        scratch_shapes=[pltpu.SemaphoreType.DMA],
        compiler_params=params,
        cost_estimate=cost(1000, 2),
        name="apply_inner",
    )(coeffs, basis, eps, table, sz, xf, yf)
    image, hxf, packed, gram, hzf, hyf = pl.pallas_call(
        outer_kernel,
        out_shape=(
            whole, f32(*xf_shape), planes, f32(2, vectors, vectors), f32(*zf_shape), f32(*yf_shape),
        ),
        in_specs=[SMEM] * 2 + [VMEM] * 13,
        out_specs=(VMEM,) * 6,
        scratch_shapes=[scratch(*zf_shape)],
        input_output_aliases={10: 0, 13: 1, 14: 2},
        compiler_params=params,
        cost_estimate=cost(200, 1),
        name="apply_outer",
    )(pml_width, coeffs, basis, eps, table, sz, zf, xf, yt, yf, image, acc, before, hxf, packed)
    phases = sum_phases()
    others = from_partners(gram, phases[0])
    hzf = passed_round(hzf, "gz", 1)
    hxf = passed_round(hxf, "gx", 1)
    hyf = passed_round(hyf, "gy", 1)
    for phase in phases[1:]:
        gram = joined(gram, others)
        if phase is phases[-1]:
            gram, image = lax.optimization_barrier((gram, image))
        others = from_partners(gram, phase)
    residual = pl.pallas_call(
        rim_kernel,
        out_shape=whole,
        in_specs=[SMEM] * 2 + [VMEM] * 5,
        out_specs=HBM,
        scratch_shapes=[scratch(*fields.shape), scratch(nz, nx, ny), pltpu.SemaphoreType.DMA((nz,))],
        compiler_params=params,
        cost_estimate=cost(200, 3),
        name="add_rims",
    )(pml_width, ritz, basis, image, hzf, hxf, hyf)
    others, residual = lax.optimization_barrier((others, residual))
    return basis_new, residual, joined(gram, others)


def solution(mesh):
    in_specs = (P(None, None, None, "gz", "gx", "gy"), P("gz", "gx", "gy"), P(), P(), P(), P(), P())
    out_specs = (P(None, None, None, "gz", "gx", "gy"), P(None, None, None, "gz", "gx", "gy"), P())
    return jax.shard_map(body, mesh=mesh, in_specs=in_specs, out_specs=out_specs, check_vma=False)
```

```python
import functools

import jax
import jax.numpy as jnp
from jax import lax
from jax.experimental import pallas as pl
from jax.experimental.pallas import tpu as pltpu
from jax.sharding import PartitionSpec as P

OMEGA_SQ = 0.36
SIGMA_TOP = 3.0
BOUNDS = ((4, 5), (0, 1), (2, 3))
AXES = ("gz", "gx", "gy")

VMEM = pl.BlockSpec(memory_space=pltpu.VMEM)
SMEM = pl.BlockSpec(memory_space=pltpu.SMEM)
HBM = pl.BlockSpec(memory_space=pltpu.HBM)


def passed_round(value, axis, steps):
    count = lax.axis_size(axis)
    return lax.ppermute(value, axis, [(source, (source + steps) % count) for source in range(count)])


def inverse_stretch(places, length, low_width, high_width):
    inside_depth = jnp.clip((low_width - places) / low_width, 0.0, 1.0) + jnp.clip(
        (places + 1.0 - length + high_width) / high_width, 0.0, 1.0
    )
    absorb = SIGMA_TOP * inside_depth * inside_depth
    scaled = 1.0 / (1.0 + absorb * absorb)
    return scaled, -absorb * scaled


def cmul(left, right):
    return (left[0] * right[0] - left[1] * right[1], left[0] * right[1] + left[1] * right[0])


def add(left, right):
    return (left[0] + right[0], left[1] + right[1])


def sub(left, right):
    return (left[0] - right[0], left[1] - right[1])


def axis_stretch(pml_ref, direction, count, places):
    total = count * lax.axis_size(AXES[direction])
    low_slot, high_slot = BOUNDS[direction]
    low = jnp.full(places.shape, pml_ref[low_slot], jnp.int32).astype(jnp.float32)
    high = jnp.full(places.shape, pml_ref[high_slot], jnp.int32).astype(jnp.float32)
    return inverse_stretch(places, jnp.float32(total), low, high)


def local_places(direction, count, shape, dim):
    start = lax.axis_index(AXES[direction]) * count
    return (lax.broadcasted_iota(jnp.int32, shape, dim) + start).astype(jnp.float32)


def one_place(direction, count, offset, shape):
    start = lax.axis_index(AXES[direction]) * count + offset
    return jnp.full(shape, start, jnp.int32).astype(jnp.float32)


def packed_row(slot, part, vector, vectors):
    return (slot * 2 + part) * vectors + vector


def has_neighbour(direction, steps):
    place = lax.axis_index(AXES[direction]) + steps
    inside = (place >= 0) & (place < lax.axis_size(AXES[direction]))
    return jnp.where(inside, 1.0, 0.0).astype(jnp.float32)


def face_kernel(fields_hbm, fields_ref, xf_ref, yf_ref, sems):
    _, vectors, _, nz, nx, ny = fields_ref.shape
    lanes = lax.broadcasted_iota(jnp.int32, (nx, ny), 1)
    copies = [
        pltpu.make_async_copy(fields_hbm.at[part, :, comp], fields_ref.at[part, :, comp], sems.at[part, comp])
        for comp in (0, 2, 1) for part in range(2)
    ]
    for copy in copies:
        copy.start()
    for copy in copies:
        copy.wait()

    packed = [jnp.zeros((nx, ny), jnp.float32)] * nz
    for comp in (0, 2):
        for part in range(2):
            for a in range(vectors):
                row = packed_row(comp // 2, part, a, vectors)
                for z in range(nz):
                    value = fields_ref[part, a, comp, z]
                    packed[z] = jnp.where(lanes == row, pltpu.roll(value, row, 1) if row else value, packed[z])
    turned = jnp.concatenate(packed, axis=0).T
    yf_ref[...] = turned[:yf_ref.shape[0]]
    for part in range(2):
        for a in range(vectors):
            for slot in range(2):
                xf_ref[part, a, slot] = fields_ref[part, a, slot + 1, :, 0, :]


def rotated(coeffs_ref, old, b):
    new = None
    for a, value in enumerate(old):
        term = cmul((coeffs_ref[0, a, b], coeffs_ref[1, a, b]), value)
        new = term if new is None else add(new, term)
    return new


SUB = 8
SHX, SEX, SHY, SEY = range(0, 8, 2)


def prepare_kernel(
    pml_ref, eps_real_ref, eps_loss_ref, coeffs_ref, fields_ref, material_ref,
    basis_ref, eps_ref, table_ref, sz_ref,
):
    _, vectors, _, nz, nx, ny = fields_ref.shape
    plane = (nx, ny)
    for slot, direction, half, count, dim in (
        (SHX, 1, 0.5, nx, 0), (SEX, 1, 0.0, nx, 0), (SHY, 2, 0.5, ny, 1), (SEY, 2, 0.0, ny, 1),
    ):
        values = axis_stretch(pml_ref, direction, count, local_places(direction, count, plane, dim) + half)
        for part in range(2):
            table_ref[slot + part] = values[part]
    for slot, half in ((0, 0.0), (2, 0.5)):
        values = axis_stretch(pml_ref, 0, nz, local_places(0, nz, (nz, ny), 0) + half)
        for part in range(2):
            sz_ref[slot + part] = values[part]

    @pl.loop(0, nz)
    def _(z):
        material = material_ref[z]
        for part, source in enumerate((eps_real_ref, eps_loss_ref)):
            value = jnp.zeros(plane, jnp.float32)
            for number in range(source.shape[0]):
                value = jnp.where(material == number, -OMEGA_SQ * source[number], value)
            eps_ref[part, z] = value
        for comp in range(3):
            old = [(fields_ref[0, a, comp, z], fields_ref[1, a, comp, z]) for a in range(vectors)]
            for b in range(vectors):
                new = rotated(coeffs_ref, old, b)
                for part in range(2):
                    basis_ref[part, b, comp, z] = new[part]


def turn_face(coeffs_ref, direction, raw_ref, face_ref):
    inside = has_neighbour(direction, 1)
    vectors = raw_ref.shape[1]
    for slot in range(2):
        old = [(raw_ref[0, a, slot] * inside, raw_ref[1, a, slot] * inside) for a in range(vectors)]
        for b in range(vectors):
            new = rotated(coeffs_ref, old, b)
            for part in range(2):
                face_ref[part, b, slot] = new[part]


def turn_column(coeffs_ref, raw_ref, rows_ref, cells_ref):
    vectors = coeffs_ref.shape[1]
    nz, nx, ny = cells_ref.shape
    inside = has_neighbour(2, 1)
    both = 2 * vectors
    which = lax.broadcasted_iota(jnp.int32, (both, nz * nx), 0)
    turned = [jnp.zeros((both, nz * nx), jnp.float32)] * 2
    for part in range(2):
        for a in range(vectors):
            column = jnp.zeros((both, nz * nx), jnp.float32)
            for b in range(vectors):
                first, second = coeffs_ref[0, a, b] * inside, coeffs_ref[1, a, b] * inside
                if part:
                    first, second = -second, first
                column = jnp.where(which == b, first, column)
                column = jnp.where(which == vectors + b, second, column)
            for slot in range(2):
                row = packed_row(slot, part, a, vectors)
                turned[slot] = turned[slot] + column * raw_ref[row:row + 1]
    for slot in range(2):
        rows_ref[slot * both:(slot + 1) * both] = turned[slot]
    rest = jnp.zeros((ny - 2 * both, nz * nx), jnp.float32)
    cells_ref[...] = jnp.concatenate(turned + [rest], axis=0).T.reshape(nz, nx, ny)


def slab_kernel(
    coeffs_ref, basis_ref, table_ref, sz_ref, raw_xf_ref, raw_yf_ref, xf_ref, yt_ref, yf_ref, zf_ref
):
    _, vectors, _, nz, nx, ny = basis_ref.shape
    turn_face(coeffs_ref, 1, raw_xf_ref, xf_ref)
    turn_column(coeffs_ref, raw_yf_ref, yt_ref, yf_ref)
    tile = (SUB, ny)
    rows = lax.broadcasted_iota(jnp.int32, tile, 0)
    lanes = lax.broadcasted_iota(jnp.int32, tile, 1)
    parts = range(2)
    last = nz - 1
    lower = jnp.full(tile, lax.axis_index(AXES[0]), jnp.int32) == 0
    shz = tuple(sz_ref[2 + part, last:] for part in parts)
    for b in range(vectors):
        for t in range(nx // SUB):
            cut = slice(SUB * t, SUB * (t + 1))
            ex, ey, ez = (tuple(basis_ref[part, b, comp, last, cut] for part in parts) for comp in range(3))
            ahead_x, ahead_y = [], []
            for part in parts:
                if SUB * (t + 1) < nx:
                    edge = basis_ref[part, b, 2, last, SUB * (t + 1):SUB * (t + 1) + 1]
                else:
                    edge = xf_ref[part, b, 1, last:]
                ahead_x.append(jnp.where(rows == SUB - 1, edge, pltpu.roll(ez[part], SUB - 1, 0)))
                row = packed_row(1, part, b, vectors)
                edge = pltpu.roll(yf_ref[last, cut], ny - 1 - row, 1)
                ahead_y.append(jnp.where(lanes == ny - 1, edge, pltpu.roll(ez[part], ny - 1, 1)))
            shx = tuple(table_ref[SHX + part, cut] for part in parts)
            shy = tuple(table_ref[SHY + part, cut] for part in parts)
            share_x = add(cmul(shy, sub(ahead_y, ez)), cmul(shz, ey))
            share_y = add(cmul(shx, sub(ahead_x, ez)), cmul(shz, ex))
            for part in parts:
                zf_ref[part, b, 0, cut] = jnp.where(lower, share_x[part], basis_ref[part, b, 0, 0, cut])
                zf_ref[part, b, 1, cut] = jnp.where(lower, -share_y[part], basis_ref[part, b, 1, 0, cut])


def plane_step(
    b, z, before, sums, up_of, basis_ref, eps_ref, table_ref, sz_ref, xf_ref, yf_ref, image_ref, hxf_ref, packed_ref
):
    _, vectors, _, _, nx, ny = basis_ref.shape
    tile = (SUB, ny)
    rows = lax.broadcasted_iota(jnp.int32, tile, 0)
    lanes = lax.broadcasted_iota(jnp.int32, tile, 1)
    parts = range(2)
    count = nx // SUB
    cut = [slice(SUB * t, SUB * (t + 1)) for t in range(count)]

    def table(slot, t):
        return tuple(table_ref[slot + part, cut[t]] for part in parts)

    sez = tuple(sz_ref[part, pl.ds(z, 1)] for part in parts)
    shz = tuple(sz_ref[2 + part, pl.ds(z, 1)] for part in parts)
    shy, sey = table(SHY, 0), table(SEY, 0)

    def turned_up(comp, t):
        return tuple(pltpu.roll(basis_ref[part, b, comp, z, cut[t]], SUB - 1, 0) for part in parts)

    sums = list(sums)
    after, behind_y, behind_z = [], None, None
    for t in range(count):
        u = [tuple(basis_ref[part, b, comp, z, cut[t]] for part in parts) for comp in range(3)]
        up = [up_of(comp, t) for comp in range(2)]
        dzx, dzy = (cmul(shz, sub(up[comp], u[comp])) for comp in range(2))

        def ahead_x(comp):
            if t + 1 < count:
                edge = turned_up(comp, t + 1)
            else:
                edge = tuple(xf_ref[part, b, comp - 1, pl.ds(z, 1)] for part in parts)
            here = turned_up(comp, t)
            return tuple(jnp.where(rows == SUB - 1, edge[part], here[part]) for part in parts)

        def ahead_y(comp):
            out = []
            for part in parts:
                row = packed_row(comp // 2, part, b, vectors)
                edge = pltpu.roll(yf_ref[z, cut[t]], ny - 1 - row, 1)
                out.append(jnp.where(lanes == ny - 1, edge, pltpu.roll(u[comp][part], ny - 1, 1)))
            return tuple(out)

        shx, sex = table(SHX, t), table(SEX, t)
        dxy, dxz = (cmul(shx, sub(ahead_x(comp), u[comp])) for comp in (1, 2))
        dyx, dyz = (cmul(shy, sub(ahead_y(comp), u[comp])) for comp in (0, 2))
        hx, hy, hz = sub(dyz, dzy), sub(dzx, dxz), sub(dxy, dyx)

        def behind_x(here, past):
            return tuple(
                jnp.where(rows == 0, 0.0 if past is None else past[part], here[part]) for part in parts
            )

        def back_y(value):
            return tuple(jnp.where(lanes == 0, 0.0, pltpu.roll(value[part], 1, 1)) for part in parts)

        down_y = tuple(pltpu.roll(hy[part], 1, 0) for part in parts)
        down_z = tuple(pltpu.roll(hz[part], 1, 0) for part in parts)
        bxy = cmul(sex, sub(hy, behind_x(down_y, behind_y)))
        bxz = cmul(sex, sub(hz, behind_x(down_z, behind_z)))
        behind_y, behind_z = down_y, down_z
        byz, byx = (cmul(sey, sub(h, back_y(h))) for h in (hz, hx))
        bzx, bzy = (cmul(sez, sub(h, past)) for h, past in zip((hx, hy), before[t]))
        eps = tuple(eps_ref[part, z, cut[t]] for part in parts)
        w = [
            add(curl, cmul(eps, u[comp]))
            for comp, curl in enumerate((sub(byz, bzy), sub(bzx, bxz), sub(bxy, byx)))
        ]
        for comp in range(3):
            for part in parts:
                image_ref[part, b, comp, z, cut[t]] = w[comp][part]
        for a in range(vectors):
            total = sums[a]
            for comp in range(3):
                total = add(total, cmul(tuple(basis_ref[part, a, comp, z, cut[t]] for part in parts), w[comp]))
            sums[a] = total
        packed = packed_ref[z, cut[t]]
        for slot, value in enumerate((hz, hx)):
            for part in parts:
                row = packed_row(slot, part, b, vectors)
                packed = jnp.where(lanes == row, pltpu.roll(value[part], (row + 1) % ny, 1), packed)
        packed_ref[z, cut[t]] = packed
        after.append((hx, hy))
    for part in parts:
        hxf_ref[part, b, 0, pl.ds(z, 1)] = hy[part][SUB - 1:]
        hxf_ref[part, b, 1, pl.ds(z, 1)] = hz[part][SUB - 1:]
    return after, sums


def inner_kernel(
    basis_ref, eps_ref, table_ref, sz_ref, xf_ref, yf_ref,
    image_ref, acc_ref, before_ref, hxf_ref, packed_ref, basis_hbm, sem,
):
    _, vectors, _, nz, nx, ny = basis_ref.shape
    keep = pltpu.make_async_copy(basis_ref, basis_hbm, sem)
    keep.start()
    packed_ref[...] = jnp.zeros(packed_ref.shape, jnp.float32)
    count = nx // SUB

    for b in range(vectors):

        def step(z, carry, b=b):
            def up_of(comp, t):
                return tuple(basis_ref[part, b, comp, z + 1, SUB * t:SUB * (t + 1)] for part in range(2))

            return plane_step(
                b, z, *carry, up_of, basis_ref, eps_ref, table_ref, sz_ref, xf_ref, yf_ref,
                image_ref, hxf_ref, packed_ref,
            )

        none = (jnp.zeros((SUB, ny), jnp.float32),) * 2
        before, sums = lax.fori_loop(0, nz - 1, step, ([(none, none)] * count, [none] * vectors))
        for part in range(2):
            for a in range(vectors):
                acc_ref[b, part * vectors + a] = sums[a][part]
            for t in range(count):
                for slot in range(2):
                    before_ref[part, b, slot, SUB * t:SUB * (t + 1)] = before[t][slot][part]
    keep.wait()


def outer_kernel(
    pml_ref, basis_ref, eps_ref, table_ref, sz_ref, zf_ref, xf_ref, yt_ref, yf_ref,
    image_in, acc_ref, before_ref, hxf_in, packed_in,
    image_ref, hxf_ref, packed_ref, hyf_ref,
):
    del image_in, hxf_in, packed_in
    _, vectors, _, nz, nx, ny = basis_ref.shape
    parts = range(2)
    count = nx // SUB
    above, below = has_neighbour(0, 1), has_neighbour(0, -1)
    under = axis_stretch(pml_ref, 0, nz, one_place(0, nz, -1, (1, ny)) + 0.5)
    sez = tuple(sz_ref[part, 0:1] * below for part in parts)
    sx_next = axis_stretch(pml_ref, 1, nx, one_place(1, nx, nx, (1, ny)))
    sy_next = axis_stretch(pml_ref, 2, ny, one_place(2, ny, ny, (1, nz * nx)))
    all_sums = []
    for b in range(vectors):

        def tile_of(ref, slot, t, b=b):
            return tuple(ref[part, b, slot, SUB * t:SUB * (t + 1)] for part in parts)

        def up_of(slot, t):
            return tuple(value * above for value in tile_of(zf_ref, slot, t))

        before = [tuple(tile_of(before_ref, slot, t) for slot in range(2)) for t in range(count)]
        sums = [(acc_ref[b, a], acc_ref[b, vectors + a]) for a in range(vectors)]
        _, sums = plane_step(
            b, nz - 1, before, sums, up_of, basis_ref, eps_ref, table_ref, sz_ref,
            xf_ref, yf_ref, image_ref, hxf_ref, packed_ref,
        )
        for t in range(count):
            cut = slice(SUB * t, SUB * (t + 1))
            ex, ey = (tuple(basis_ref[part, b, comp, 0, cut] for part in parts) for comp in range(2))
            hx = sub(tile_of(zf_ref, 0, t), cmul(under, ey))
            hy = add(tile_of(zf_ref, 1, t), cmul(under, ex))
            more = (cmul(sez, hy), cmul(sez, hx))
            for part in parts:
                image_ref[part, b, 0, 0, cut] = image_ref[part, b, 0, 0, cut] + more[0][part]
                image_ref[part, b, 1, 0, cut] = image_ref[part, b, 1, 0, cut] - more[1][part]
            for a in range(vectors):
                ex, ey = (tuple(basis_ref[part, a, comp, 0, cut] for part in parts) for comp in range(2))
                sums[a] = add(sums[a], sub(cmul(ex, more[0]), cmul(ey, more[1])))
        h_y = tuple(hxf_ref[part, b, 0] for part in parts)
        h_z = tuple(hxf_ref[part, b, 1] for part in parts)
        for a in range(vectors):
            over = cmul(tuple(xf_ref[part, a, 0] for part in parts), h_z)
            over = sub(over, cmul(tuple(xf_ref[part, a, 1] for part in parts), h_y))
            over = cmul(sx_next, over)
            for row in range(0, nz, SUB):
                sums[a] = add(sums[a], tuple(part[row:row + SUB] for part in over))
        all_sums.append(sums)

    both = 2 * vectors
    hyf_ref[:2 * both] = packed_ref[...].reshape(nz * nx, ny).T[:2 * both]
    ends = [
        cmul(sy_next, (yt_ref[slot * both:slot * both + vectors], yt_ref[slot * both + vectors:(slot + 1) * both]))
        for slot in range(2)
    ]
    columns = lax.broadcasted_iota(jnp.int32, (both, ny), 1)
    gram = jnp.zeros((both, ny), jnp.float32)
    for b in range(vectors):
        flat = jnp.concatenate(
            [jnp.sum(all_sums[b][a][part], axis=0, keepdims=True) for part in range(2) for a in range(vectors)], axis=0
        )
        over = None
        for slot in range(2):
            h = tuple(hyf_ref[packed_row(slot, part, b, vectors)][None] for part in range(2))
            term = cmul(ends[slot], h)
            over = term if over is None else sub(term, over)
        side = jnp.concatenate(over, axis=0)
        total = jnp.sum(flat, axis=1, keepdims=True) + jnp.sum(side, axis=1, keepdims=True)
        gram = jnp.where(columns == b, total, gram)
    everywhere = 3.0 * nz * nx * ny
    for axis in AXES:
        everywhere = everywhere * lax.axis_size(axis)
    hyf_ref[2 * both:] = gram * (1.0 / everywhere)


def rim_kernel(
    pml_ref, ritz_ref, basis_ref, image_ref, hxf_ref, hyf_ref, residual_hbm, residual_ref, packed_ref, sems
):
    _, vectors, _, nz, nx, ny = basis_ref.shape
    plane = (nx, ny)
    rows = lax.broadcasted_iota(jnp.int32, plane, 0)
    lanes = lax.broadcasted_iota(jnp.int32, plane, 1)
    sex = axis_stretch(pml_ref, 1, nx, one_place(1, nx, 0, (1, ny)))
    sey = axis_stretch(pml_ref, 2, ny, one_place(2, ny, 0, plane))
    none = jnp.zeros(plane, jnp.float32)
    sex = tuple(jnp.where(rows == 0, part * has_neighbour(1, -1), none) for part in sex)
    sey = tuple(jnp.where(lanes == 0, part * has_neighbour(2, -1), none) for part in sey)
    used = 4 * vectors
    rest = jnp.zeros((ny - used, nz * nx), jnp.float32)
    packed_ref[...] = jnp.concatenate([hyf_ref[:used], rest], axis=0).T.reshape(nz, nx, ny)

    def kept(z):
        return pltpu.make_async_copy(residual_ref.at[:, :, :, z], residual_hbm.at[:, :, :, z], sems.at[z])

    @pl.loop(0, nz)
    def _(z):
        packed = packed_ref[z]
        for b in range(vectors):

            def column(slot, b=b):
                return tuple(
                    pltpu.roll(packed, (ny - packed_row(slot, part, b, vectors)) % ny, 1) for part in range(2)
                )

            def row(slot, b=b):
                return tuple(hxf_ref[part, b, slot, pl.ds(z, 1)] for part in range(2))

            factor = (ritz_ref[0, b], ritz_ref[1, b])
            left = []
            for comp in range(3):
                u = (basis_ref[0, b, comp, z], basis_ref[1, b, comp, z])
                w = (image_ref[0, b, comp, z], image_ref[1, b, comp, z])
                left.append(sub(w, cmul(factor, u)))
            left[0] = sub(left[0], cmul(sey, column(0)))
            left[2] = add(left[2], cmul(sey, column(1)))
            left[1] = add(left[1], cmul(sex, row(1)))
            left[2] = sub(left[2], cmul(sex, row(0)))
            for comp in range(3):
                for part in range(2):
                    residual_ref[part, b, comp, z] = left[comp][part]
        kept(z).start()

    @pl.loop(0, nz)
    def _(z):
        kept(z).wait()


def from_partner(value, mask):
    axes = ("gx", "gy", "gz")
    count = 1
    for axis in axes:
        count *= lax.axis_size(axis)
    return lax.ppermute(value, axes, [(source, source ^ mask) for source in range(count)])


def body(fields, material, pml_width, eps_real, eps_loss, coeffs, ritz):
    _, vectors, _, nz, nx, ny = fields.shape
    f32 = lambda *shape: jax.ShapeDtypeStruct(shape, jnp.float32)
    scratch = lambda *shape: pltpu.VMEM(shape, jnp.float32)
    params = pltpu.CompilerParams(vmem_limit_bytes=40 * 1024 * 1024)
    whole = f32(*fields.shape)
    zf_shape = (2, vectors, 2, nx, ny)
    xf_shape = (2, vectors, 2, nz, ny)
    yf_shape = (4 * vectors, nz * nx)
    near, xf, yf = pl.pallas_call(
        face_kernel,
        out_shape=(whole, f32(*xf_shape), f32(*yf_shape)),
        in_specs=[HBM],
        out_specs=(VMEM,) * 3,
        scratch_shapes=[pltpu.SemaphoreType.DMA((2, 3))],
        compiler_params=params,
        name="take_faces",
    )(pltpu.with_memory_space_constraint(fields, pltpu.HBM))
    xf = passed_round(xf, "gx", -1)
    yf = passed_round(yf, "gy", -1)
    cells = fields.size // 6 // vectors

    def cost(flops, passes):
        return pl.CostEstimate(flops=flops * cells, bytes_accessed=passes * 4 * fields.size, transcendentals=0)

    planes = f32(nz, nx, ny)
    basis, eps, table, sz = pl.pallas_call(
        prepare_kernel,
        out_shape=(whole, f32(2, nz, nx, ny), f32(8, nx, ny), f32(4, nz, ny)),
        in_specs=[SMEM] * 4 + [VMEM] * 2,
        out_specs=(VMEM,) * 4,
        compiler_params=params,
        cost_estimate=cost(400, 2),
        name="prepare",
    )(pml_width, eps_real, eps_loss, coeffs, near, material)
    xf, yt, yf, zf = pl.pallas_call(
        slab_kernel,
        out_shape=(f32(*xf_shape), f32(*yf_shape), planes, f32(*zf_shape)),
        in_specs=[SMEM] + [VMEM] * 5,
        out_specs=(VMEM,) * 4,
        compiler_params=params,
        name="slab_face",
    )(coeffs, basis, table, sz, xf, yf)
    zf = passed_round(zf, "gz", 1)
    image, acc, before, hxf, packed, basis_new = pl.pallas_call(
        inner_kernel,
        out_shape=(
            whole, f32(vectors, 2 * vectors, SUB, ny), f32(*zf_shape), f32(*xf_shape), planes, whole,
        ),
        in_specs=[VMEM] * 6,
        out_specs=(VMEM,) * 5 + (HBM,),
        scratch_shapes=[pltpu.SemaphoreType.DMA],
        compiler_params=params,
        cost_estimate=cost(1000, 2),
        name="apply_inner",
    )(basis, eps, table, sz, xf, yf)
    image, hxf, packed, hyf = pl.pallas_call(
        outer_kernel,
        out_shape=(whole, f32(*xf_shape), planes, f32(6 * vectors, nz * nx)),
        in_specs=[SMEM] + [VMEM] * 13,
        out_specs=(VMEM,) * 4,
        input_output_aliases={9: 0, 12: 1, 13: 2},
        compiler_params=params,
        cost_estimate=cost(200, 1),
        name="apply_outer",
    )(pml_width, basis, eps, table, sz, zf, xf, yt, yf, image, acc, before, hxf, packed)
    across = lax.axis_size("gy") * lax.axis_size("gz")
    masks = [1 << bit for bit in range((across * lax.axis_size("gx") - 1).bit_length())]
    order = [mask for mask in masks if mask > across] + [across] + [mask for mask in reversed(masks) if mask < across]
    gram = hyf[4 * vectors:]
    hyf = passed_round(hyf, "gy", 1)
    if lax.axis_size("gy") == 2:
        gram = gram + hyf[4 * vectors:]
        order.remove(lax.axis_size("gz"))
    hxf = passed_round(hxf, "gx", 1)
    for mask in order[:-1]:
        gram = gram + from_partner(gram, mask)
    gram, image = lax.optimization_barrier((gram, image))
    other = from_partner(gram, order[-1])
    residual = pl.pallas_call(
        rim_kernel,
        out_shape=whole,
        in_specs=[SMEM] * 2 + [VMEM] * 4,
        out_specs=HBM,
        scratch_shapes=[scratch(*fields.shape), scratch(nz, nx, ny), pltpu.SemaphoreType.DMA((nz,))],
        compiler_params=params,
        cost_estimate=cost(200, 3),
        name="add_rims",
    )(pml_width, ritz, basis, image, hxf, hyf)
    other, residual = lax.optimization_barrier((other, residual))
    gram = (gram + other)[:, :vectors].reshape(2, vectors, vectors)
    return basis_new, residual, gram


def solution(mesh):
    in_specs = (P(None, None, None, "gz", "gx", "gy"), P("gz", "gx", "gy"), P(), P(), P(), P(), P())
    out_specs = (P(None, None, None, "gz", "gx", "gy"), P(None, None, None, "gz", "gx", "gy"), P())
    return jax.shard_map(body, mesh=mesh, in_specs=in_specs, out_specs=out_specs, check_vma=False)
```

```python
import functools

import jax
import jax.numpy as jnp
from jax import lax
from jax.experimental import pallas as pl
from jax.experimental.pallas import tpu as pltpu
from jax.sharding import PartitionSpec as P

OMEGA_SQ = 0.36
SIGMA_TOP = 3.0
BOUNDS = ((4, 5), (0, 1), (2, 3))
AXES = ("gz", "gx", "gy")

VMEM = pl.BlockSpec(memory_space=pltpu.VMEM)
SMEM = pl.BlockSpec(memory_space=pltpu.SMEM)
HBM = pl.BlockSpec(memory_space=pltpu.HBM)


def passed_round(value, axis, steps):
    count = lax.axis_size(axis)
    return lax.ppermute(value, axis, [(source, (source + steps) % count) for source in range(count)])


def inverse_stretch(places, length, low_width, high_width):
    inside_depth = jnp.clip((low_width - places) / low_width, 0.0, 1.0) + jnp.clip(
        (places + 1.0 - length + high_width) / high_width, 0.0, 1.0
    )
    absorb = SIGMA_TOP * inside_depth * inside_depth
    scaled = 1.0 / (1.0 + absorb * absorb)
    return scaled, -absorb * scaled


def cmul(left, right):
    return (left[0] * right[0] - left[1] * right[1], left[0] * right[1] + left[1] * right[0])


def add(left, right):
    return (left[0] + right[0], left[1] + right[1])


def sub(left, right):
    return (left[0] - right[0], left[1] - right[1])


def axis_stretch(pml_ref, direction, count, places):
    total = count * lax.axis_size(AXES[direction])
    low_slot, high_slot = BOUNDS[direction]
    low = jnp.full(places.shape, pml_ref[low_slot], jnp.int32).astype(jnp.float32)
    high = jnp.full(places.shape, pml_ref[high_slot], jnp.int32).astype(jnp.float32)
    return inverse_stretch(places, jnp.float32(total), low, high)


def local_places(direction, count, shape, dim):
    start = lax.axis_index(AXES[direction]) * count
    return (lax.broadcasted_iota(jnp.int32, shape, dim) + start).astype(jnp.float32)


def one_place(direction, count, offset, shape):
    start = lax.axis_index(AXES[direction]) * count + offset
    return jnp.full(shape, start, jnp.int32).astype(jnp.float32)


def packed_row(slot, part, vector, vectors):
    return (slot * 2 + part) * vectors + vector


def has_neighbour(direction, steps):
    place = lax.axis_index(AXES[direction]) + steps
    inside = (place >= 0) & (place < lax.axis_size(AXES[direction]))
    return jnp.where(inside, 1.0, 0.0).astype(jnp.float32)


def face_kernel(fields_hbm, fields_ref, xf_ref, yf_ref, sems):
    _, vectors, _, nz, nx, ny = fields_ref.shape
    lanes = lax.broadcasted_iota(jnp.int32, (nx, ny), 1)
    copies = [
        pltpu.make_async_copy(fields_hbm.at[part, :, comp], fields_ref.at[part, :, comp], sems.at[part, comp])
        for comp in (0, 2, 1) for part in range(2)
    ]
    for copy in copies:
        copy.start()
    for copy in copies:
        copy.wait()

    packed = [jnp.zeros((nx, ny), jnp.float32)] * nz
    for comp in (0, 2):
        for part in range(2):
            for a in range(vectors):
                row = packed_row(comp // 2, part, a, vectors)
                for z in range(nz):
                    value = fields_ref[part, a, comp, z]
                    packed[z] = jnp.where(lanes == row, pltpu.roll(value, row, 1) if row else value, packed[z])
    turned = jnp.concatenate(packed, axis=0).T
    yf_ref[...] = turned[:yf_ref.shape[0]]
    for part in range(2):
        for a in range(vectors):
            for slot in range(2):
                xf_ref[part, a, slot] = fields_ref[part, a, slot + 1, :, 0, :]


def rotated(coeffs_ref, old, b):
    new = None
    for a, value in enumerate(old):
        term = cmul((coeffs_ref[0, a, b], coeffs_ref[1, a, b]), value)
        new = term if new is None else add(new, term)
    return new


SUB = 8
SHX, SEX, SHY, SEY = range(0, 8, 2)


def field_of(ref, b, comp, z, cut):
    return tuple(ref[part, b, comp, z, cut] for part in range(2))


def tiles_of(nx):
    return [slice(SUB * t, SUB * (t + 1)) for t in range(nx // SUB)]


def prepare_kernel(
    pml_ref, eps_real_ref, eps_loss_ref, coeffs_ref, fields_ref, material_ref,
    basis_ref, loss_ref, h_ref, packed_ref, table_ref, sz_ref,
):
    _, vectors, _, nz, nx, ny = fields_ref.shape
    plane = (nx, ny)
    parts = range(2)
    for slot, direction, half, count, dim in (
        (SHX, 1, 0.5, nx, 0), (SEX, 1, 0.0, nx, 0), (SHY, 2, 0.5, ny, 1), (SEY, 2, 0.0, ny, 1),
    ):
        values = axis_stretch(pml_ref, direction, count, local_places(direction, count, plane, dim) + half)
        for part in parts:
            table_ref[slot + part] = values[part]
    for slot, half in ((0, 0.0), (2, 0.5)):
        values = axis_stretch(pml_ref, 0, nz, local_places(0, nz, (nz, ny), 0) + half)
        for part in parts:
            sz_ref[slot + part] = values[part]

    @pl.loop(0, nz)
    def _(z):
        material = material_ref[z]
        eps = []
        for source in (eps_real_ref, eps_loss_ref):
            value = jnp.zeros(plane, jnp.float32)
            for number in range(source.shape[0]):
                value = jnp.where(material == number, -OMEGA_SQ * source[number], value)
            eps.append(value)
        for comp in range(3):
            old = [(fields_ref[0, a, comp, z], fields_ref[1, a, comp, z]) for a in range(vectors)]
            for b in range(vectors):
                new = rotated(coeffs_ref, old, b)
                loss = cmul(eps, new)
                for part in parts:
                    basis_ref[part, b, comp, z] = new[part]
                    loss_ref[part, b, comp, z] = loss[part]
        packed_ref[z] = jnp.zeros(plane, jnp.float32)

    tile = (SUB, ny)
    rows = lax.broadcasted_iota(jnp.int32, tile, 0)
    lanes = lax.broadcasted_iota(jnp.int32, tile, 1)
    cuts = tiles_of(nx)

    def magnetic(b, z, last):
        shz = tuple(sz_ref[2 + part, pl.ds(z, 1)] for part in parts)
        for cut in cuts:
            u = [field_of(basis_ref, b, comp, z, cut) for comp in range(3)]

            def step_z(comp):
                if last:
                    return tuple(-value for value in u[comp])
                return sub(field_of(basis_ref, b, comp, z + 1, cut), u[comp])

            def step_x(comp):
                if cut.stop < nx:
                    ahead = field_of(basis_ref, b, comp, z, slice(cut.start + 1, cut.stop + 1))
                else:
                    ahead = tuple(jnp.where(rows == SUB - 1, 0.0, pltpu.roll(value, SUB - 1, 0)) for value in u[comp])
                return sub(ahead, u[comp])

            def step_y(comp):
                ahead = tuple(jnp.where(lanes == ny - 1, 0.0, pltpu.roll(value, ny - 1, 1)) for value in u[comp])
                return sub(ahead, u[comp])

            shx = tuple(table_ref[SHX + part, cut] for part in parts)
            shy = tuple(table_ref[SHY + part, cut] for part in parts)
            h = (
                sub(cmul(shy, step_y(2)), cmul(shz, step_z(1))),
                sub(cmul(shz, step_z(0)), cmul(shx, step_x(2))),
                sub(cmul(shx, step_x(1)), cmul(shy, step_y(0))),
            )
            for comp in range(3):
                for part in parts:
                    h_ref[part, b, comp, z, cut] = h[comp][part]
            packed = packed_ref[z, cut]
            for slot, value in enumerate((h[2], h[0])):
                for part in parts:
                    row = packed_row(slot, part, b, vectors)
                    packed = jnp.where(lanes == row, pltpu.roll(value[part], (row + 1) % ny, 1), packed)
            packed_ref[z, cut] = packed

    for b in range(vectors):

        @pl.loop(0, nz - 1)
        def _(z, b=b):
            magnetic(b, z, False)

        magnetic(b, nz - 1, True)


def turn_face(coeffs_ref, direction, raw_ref, face_ref):
    inside = has_neighbour(direction, 1)
    vectors = raw_ref.shape[1]
    for slot in range(2):
        old = [(raw_ref[0, a, slot] * inside, raw_ref[1, a, slot] * inside) for a in range(vectors)]
        for b in range(vectors):
            new = rotated(coeffs_ref, old, b)
            for part in range(2):
                face_ref[part, b, slot] = new[part]


def turn_column(coeffs_ref, raw_ref, rows_ref):
    vectors = coeffs_ref.shape[1]
    inside = has_neighbour(2, 1)
    both = 2 * vectors
    shape = (both, raw_ref.shape[1])
    which = lax.broadcasted_iota(jnp.int32, shape, 0)
    turned = [jnp.zeros(shape, jnp.float32)] * 2
    for part in range(2):
        for a in range(vectors):
            column = jnp.zeros(shape, jnp.float32)
            for b in range(vectors):
                first, second = coeffs_ref[0, a, b] * inside, coeffs_ref[1, a, b] * inside
                if part:
                    first, second = -second, first
                column = jnp.where(which == b, first, column)
                column = jnp.where(which == vectors + b, second, column)
            for slot in range(2):
                row = packed_row(slot, part, a, vectors)
                turned[slot] = turned[slot] + column * raw_ref[row:row + 1]
    for slot in range(2):
        rows_ref[slot * both:(slot + 1) * both] = turned[slot]


def lane_to_last(values, slot, part, b, vectors):
    ny = values.shape[-1]
    lanes = lax.broadcasted_iota(jnp.int32, values.shape, 1)
    row = packed_row(slot, part, b, vectors)
    return jnp.where(lanes == ny - 1, pltpu.roll(values, ny - 1 - row, 1), 0.0)


def with_halos(h, b, z, cut, nx, xadd_ref, yadd_ref):
    vectors = xadd_ref.shape[1]
    column = yadd_ref[z, cut]
    hx = tuple(h[0][part] + lane_to_last(column, 1, part, b, vectors) for part in range(2))
    hz = tuple(h[2][part] + lane_to_last(column, 0, part, b, vectors) for part in range(2))
    hy = h[1]
    if cut.stop == nx:
        rows = lax.broadcasted_iota(jnp.int32, column.shape, 0)

        def row_of(slot):
            return tuple(
                jnp.where(rows == SUB - 1, xadd_ref[part, b, slot, pl.ds(z, 1)], 0.0) for part in range(2)
            )

        hy, hz = add(hy, row_of(0)), add(hz, row_of(1))
    return hx, hy, hz


def slab_kernel(
    pml_ref, coeffs_ref, basis_ref, h_in, packed_in, raw_xf_ref, raw_yf_ref,
    h_ref, packed_ref, xf_ref, yt_ref, xadd_ref, yadd_ref, hxf_ref, zf_ref,
):
    del h_in, packed_in
    _, vectors, _, nz, nx, ny = basis_ref.shape
    parts = range(2)
    cells = nz * nx
    both = 2 * vectors
    turn_face(coeffs_ref, 1, raw_xf_ref, xf_ref)
    turn_column(coeffs_ref, raw_yf_ref, yt_ref)
    shx = axis_stretch(pml_ref, 1, nx, one_place(1, nx, nx - 1, (1, ny)) + 0.5)
    shy = axis_stretch(pml_ref, 2, ny, one_place(2, ny, ny - 1, (1, cells)) + 0.5)
    for b in range(vectors):
        for slot in range(2):
            value = cmul(shx, tuple(xf_ref[part, b, 1 - slot] for part in parts))
            for part in parts:
                xadd_ref[part, b, slot] = value[part] if slot else -value[part]
    added = []
    for slot in range(2):
        value = cmul(shy, (yt_ref[slot * both:slot * both + vectors], yt_ref[slot * both + vectors:(slot + 1) * both]))
        added += [part if slot else -part for part in value]
    rest = jnp.zeros((ny - 2 * both, cells), jnp.float32)
    yadd_ref[...] = jnp.concatenate(added + [rest], axis=0).T.reshape(nz, nx, ny)
    packed_ref[...] = packed_ref[...] + yadd_ref[...]
    last = nz - 1
    lower = jnp.full((SUB, ny), lax.axis_index(AXES[0]), jnp.int32) == 0
    lanes = lax.broadcasted_iota(jnp.int32, (nz, ny), 1)
    corner = packed_ref[:, nx - 1, :]
    for b in range(vectors):
        for part in parts:
            row = packed_row(0, part, b, vectors)
            edge = pltpu.roll(xadd_ref[part, b, 1], (row + 1) % ny, 1)
            corner = corner + jnp.where(lanes == row, edge, 0.0)
    packed_ref[:, nx - 1, :] = corner
    for b in range(vectors):
        for part in parts:
            hxf_ref[part, b, 0] = h_ref[part, b, 1, :, nx - 1, :] + xadd_ref[part, b, 0]
            hxf_ref[part, b, 1] = (
                h_ref[part, b, 2, :, nx - 1, :] + xadd_ref[part, b, 1]
                + lane_to_last(yadd_ref[:, nx - 1, :], 0, part, b, vectors)
            )
        for cut in tiles_of(nx):
            h = [field_of(h_ref, b, comp, last, cut) for comp in range(3)]
            h = with_halos(h, b, last, cut, nx, xadd_ref, yadd_ref)
            for part in parts:
                for comp in range(3):
                    h_ref[part, b, comp, last, cut] = h[comp][part]
                for comp in range(2):
                    zf_ref[part, b, comp, cut] = jnp.where(lower, h[comp][part], basis_ref[part, b, comp, 0, cut])


def plane_step(b, z, before, sums, basis_ref, loss_ref, table_ref, sz_ref, h_ref, image_ref, halos=None):
    _, vectors, _, _, nx, ny = basis_ref.shape
    rows = lax.broadcasted_iota(jnp.int32, (SUB, ny), 0)
    lanes = lax.broadcasted_iota(jnp.int32, (SUB, ny), 1)
    parts = range(2)
    cuts = tiles_of(nx)
    sez = tuple(sz_ref[part, pl.ds(z, 1)] for part in parts)
    fields = []
    for cut in cuts:
        h = [field_of(h_ref, b, comp, z, cut) for comp in range(3)]
        if halos is not None:
            h = with_halos(h, b, z, cut, nx, *halos)
            for comp in (1, 2):
                for part in parts:
                    h_ref[part, b, comp, z, cut] = h[comp][part]
        fields.append(h)
    sums = list(sums)
    for t, cut in enumerate(cuts):
        hx, hy, hz = fields[t]

        def back_x(comp):
            here = fields[t][comp]
            if t:
                past = field_of(h_ref, b, comp, z, slice(cut.start - 1, cut.stop - 1))
            else:
                past = tuple(jnp.where(rows == 0, 0.0, pltpu.roll(value, 1, 0)) for value in here)
            return sub(here, past)

        def back_y(value):
            return sub(value, tuple(jnp.where(lanes == 0, 0.0, pltpu.roll(part, 1, 1)) for part in value))

        sex = tuple(table_ref[SEX + part, cut] for part in parts)
        sey = tuple(table_ref[SEY + part, cut] for part in parts)
        bxy, bxz = (cmul(sex, back_x(comp)) for comp in (1, 2))
        byz, byx = (cmul(sey, back_y(value)) for value in (hz, hx))
        bzx, bzy = (cmul(sez, sub(value, past)) for value, past in zip((hx, hy), before[t]))
        curl = (sub(byz, bzy), sub(bzx, bxz), sub(bxy, byx))
        w = [add(curl[comp], field_of(loss_ref, b, comp, z, cut)) for comp in range(3)]
        for comp in range(3):
            for part in parts:
                image_ref[part, b, comp, z, cut] = w[comp][part]
        for a in range(vectors):
            total = sums[a]
            for comp in range(3):
                total = add(total, cmul(field_of(basis_ref, a, comp, z, cut), w[comp]))
            sums[a] = total
    return [(h[0], h[1]) for h in fields], sums


def inner_kernel(
    basis_ref, loss_ref, table_ref, sz_ref, h_in, xadd_ref, yadd_ref,
    h_ref, image_ref, acc_ref, before_ref, basis_hbm, sem,
):
    del h_in
    _, vectors, _, nz, nx, ny = basis_ref.shape
    keep = pltpu.make_async_copy(basis_ref, basis_hbm, sem)
    keep.start()
    count = nx // SUB
    for b in range(vectors):

        def step(z, carry, b=b):
            return plane_step(
                b, z, *carry, basis_ref, loss_ref, table_ref, sz_ref, h_ref, image_ref, (xadd_ref, yadd_ref)
            )

        none = (jnp.zeros((SUB, ny), jnp.float32),) * 2
        before, sums = lax.fori_loop(0, nz - 1, step, ([(none, none)] * count, [none] * vectors))
        for part in range(2):
            for a in range(vectors):
                acc_ref[b, part * vectors + a] = sums[a][part]
            for t, cut in enumerate(tiles_of(nx)):
                for slot in range(2):
                    before_ref[part, b, slot, cut] = before[t][slot][part]
    keep.wait()


def last_plane_kernel(sz_ref, zf_ref, h_in, packed_in, hxf_in, h_ref, packed_ref, hxf_ref):
    del h_in, packed_in, hxf_in
    _, vectors, _, nz, nx, ny = h_ref.shape
    parts = range(2)
    last = nz - 1
    lanes = lax.broadcasted_iota(jnp.int32, (SUB, ny), 1)
    shz = tuple(sz_ref[2 + part, last:] * has_neighbour(0, 1) for part in parts)
    packed = [packed_ref[last, cut] for cut in tiles_of(nx)]
    for b in range(vectors):
        for t, cut in enumerate(tiles_of(nx)):
            ex, ey = (tuple(zf_ref[part, b, slot, cut] for part in parts) for slot in range(2))
            more = (tuple(-value for value in cmul(shz, ey)), cmul(shz, ex))
            for part in parts:
                for comp in range(2):
                    h_ref[part, b, comp, last, cut] = h_ref[part, b, comp, last, cut] + more[comp][part]
                row = packed_row(1, part, b, vectors)
                edge = pltpu.roll(more[0][part], (row + 1) % ny, 1)
                packed[t] = packed[t] + jnp.where(lanes == row, edge, 0.0)
                if cut.stop == nx:
                    hxf_ref[part, b, 0, last:] = hxf_ref[part, b, 0, last:] + more[1][part][SUB - 1:]
    for t, cut in enumerate(tiles_of(nx)):
        packed_ref[last, cut] = packed[t]


def outer_kernel(
    pml_ref, basis_ref, loss_ref, table_ref, sz_ref, h_ref, zf_ref, xf_ref, yt_ref, hxf_ref, packed_ref,
    image_in, acc_ref, before_ref, image_ref, hyf_ref,
):
    del image_in
    _, vectors, _, nz, nx, ny = basis_ref.shape
    parts = range(2)
    cuts = tiles_of(nx)
    under = axis_stretch(pml_ref, 0, nz, one_place(0, nz, -1, (1, ny)) + 0.5)
    sez = tuple(sz_ref[part, 0:1] * has_neighbour(0, -1) for part in parts)
    sx_next = axis_stretch(pml_ref, 1, nx, one_place(1, nx, nx, (1, ny)))
    sy_next = axis_stretch(pml_ref, 2, ny, one_place(2, ny, ny, (1, nz * nx)))
    both = 2 * vectors
    hyf_ref[:2 * both] = packed_ref[...].reshape(nz * nx, ny).T[:2 * both]
    ends = [
        cmul(sy_next, (yt_ref[slot * both:slot * both + vectors], yt_ref[slot * both + vectors:(slot + 1) * both]))
        for slot in range(2)
    ]
    columns = lax.broadcasted_iota(jnp.int32, (both, ny), 1)
    gram = jnp.zeros((both, ny), jnp.float32)
    for b in range(vectors):

        def tile_of(ref, slot, cut, b=b):
            return tuple(ref[part, b, slot, cut] for part in parts)

        before = [tuple(tile_of(before_ref, slot, cut) for slot in range(2)) for cut in cuts]
        sums = [(acc_ref[b, a], acc_ref[b, vectors + a]) for a in range(vectors)]
        _, sums = plane_step(
            b, nz - 1, before, sums, basis_ref, loss_ref, table_ref, sz_ref, h_ref, image_ref
        )
        for cut in cuts:
            ex, ey = (field_of(basis_ref, b, comp, 0, cut) for comp in range(2))
            hx = sub(tile_of(zf_ref, 0, cut), cmul(under, ey))
            hy = add(tile_of(zf_ref, 1, cut), cmul(under, ex))
            more = (cmul(sez, hy), cmul(sez, hx))
            for part in parts:
                image_ref[part, b, 0, 0, cut] = image_ref[part, b, 0, 0, cut] + more[0][part]
                image_ref[part, b, 1, 0, cut] = image_ref[part, b, 1, 0, cut] - more[1][part]
            for a in range(vectors):
                ex, ey = (field_of(basis_ref, a, comp, 0, cut) for comp in range(2))
                sums[a] = add(sums[a], sub(cmul(ex, more[0]), cmul(ey, more[1])))
        h_y = tuple(hxf_ref[part, b, 0] for part in parts)
        h_z = tuple(hxf_ref[part, b, 1] for part in parts)
        for a in range(vectors):
            over = cmul(tuple(xf_ref[part, a, 0] for part in parts), h_z)
            over = sub(over, cmul(tuple(xf_ref[part, a, 1] for part in parts), h_y))
            over = cmul(sx_next, over)
            for row in range(0, nz, SUB):
                sums[a] = add(sums[a], tuple(part[row:row + SUB] for part in over))
        flat = jnp.concatenate(
            [jnp.sum(sums[a][part], axis=0, keepdims=True) for part in parts for a in range(vectors)], axis=0
        )
        over = None
        for slot in range(2):
            h = tuple(hyf_ref[packed_row(slot, part, b, vectors)][None] for part in parts)
            term = cmul(ends[slot], h)
            over = term if over is None else sub(term, over)
        side = jnp.concatenate(over, axis=0)
        total = jnp.sum(flat, axis=1, keepdims=True) + jnp.sum(side, axis=1, keepdims=True)
        gram = jnp.where(columns == b, total, gram)
    everywhere = 3.0 * nz * nx * ny
    for axis in AXES:
        everywhere = everywhere * lax.axis_size(axis)
    hyf_ref[2 * both:] = gram * (1.0 / everywhere)


def rim_kernel(
    pml_ref, ritz_ref, basis_ref, image_ref, hxf_ref, hyf_ref, residual_hbm, residual_ref, packed_ref, sems
):
    _, vectors, _, nz, nx, ny = basis_ref.shape
    plane = (nx, ny)
    rows = lax.broadcasted_iota(jnp.int32, plane, 0)
    lanes = lax.broadcasted_iota(jnp.int32, plane, 1)
    sex = axis_stretch(pml_ref, 1, nx, one_place(1, nx, 0, (1, ny)))
    sey = axis_stretch(pml_ref, 2, ny, one_place(2, ny, 0, plane))
    none = jnp.zeros(plane, jnp.float32)
    sex = tuple(jnp.where(rows == 0, part * has_neighbour(1, -1), none) for part in sex)
    sey = tuple(jnp.where(lanes == 0, part * has_neighbour(2, -1), none) for part in sey)
    used = 4 * vectors
    rest = jnp.zeros((ny - used, nz * nx), jnp.float32)
    packed_ref[...] = jnp.concatenate([hyf_ref[:used], rest], axis=0).T.reshape(nz, nx, ny)

    def kept(z):
        return pltpu.make_async_copy(residual_ref.at[:, :, :, z], residual_hbm.at[:, :, :, z], sems.at[z])

    @pl.loop(0, nz)
    def _(z):
        packed = packed_ref[z]
        for b in range(vectors):

            def column(slot, b=b):
                return tuple(
                    pltpu.roll(packed, (ny - packed_row(slot, part, b, vectors)) % ny, 1) for part in range(2)
                )

            def row(slot, b=b):
                return tuple(hxf_ref[part, b, slot, pl.ds(z, 1)] for part in range(2))

            factor = (ritz_ref[0, b], ritz_ref[1, b])
            left = []
            for comp in range(3):
                u = (basis_ref[0, b, comp, z], basis_ref[1, b, comp, z])
                w = (image_ref[0, b, comp, z], image_ref[1, b, comp, z])
                left.append(sub(w, cmul(factor, u)))
            left[0] = sub(left[0], cmul(sey, column(0)))
            left[2] = add(left[2], cmul(sey, column(1)))
            left[1] = add(left[1], cmul(sex, row(1)))
            left[2] = sub(left[2], cmul(sex, row(0)))
            for comp in range(3):
                for part in range(2):
                    residual_ref[part, b, comp, z] = left[comp][part]
        kept(z).start()

    @pl.loop(0, nz)
    def _(z):
        kept(z).wait()


def from_partner(value, mask):
    axes = ("gx", "gy", "gz")
    count = 1
    for axis in axes:
        count *= lax.axis_size(axis)
    return lax.ppermute(value, axes, [(source, source ^ mask) for source in range(count)])


def body(fields, material, pml_width, eps_real, eps_loss, coeffs, ritz):
    _, vectors, _, nz, nx, ny = fields.shape
    f32 = lambda *shape: jax.ShapeDtypeStruct(shape, jnp.float32)
    scratch = lambda *shape: pltpu.VMEM(shape, jnp.float32)
    params = pltpu.CompilerParams(vmem_limit_bytes=40 * 1024 * 1024)
    whole = f32(*fields.shape)
    zf_shape = (2, vectors, 2, nx, ny)
    xf_shape = (2, vectors, 2, nz, ny)
    yf_shape = (4 * vectors, nz * nx)
    near, xf, yf = pl.pallas_call(
        face_kernel,
        out_shape=(whole, f32(*xf_shape), f32(*yf_shape)),
        in_specs=[HBM],
        out_specs=(VMEM,) * 3,
        scratch_shapes=[pltpu.SemaphoreType.DMA((2, 3))],
        compiler_params=params,
        name="take_faces",
    )(pltpu.with_memory_space_constraint(fields, pltpu.HBM))
    xf = passed_round(xf, "gx", -1)
    yf = passed_round(yf, "gy", -1)
    cells = fields.size // 6 // vectors

    def cost(flops, passes):
        return pl.CostEstimate(flops=flops * cells, bytes_accessed=passes * 4 * fields.size, transcendentals=0)

    planes = f32(nz, nx, ny)
    face = f32(*xf_shape)
    basis, loss, h, packed, table, sz = pl.pallas_call(
        prepare_kernel,
        out_shape=(whole, whole, whole, planes, f32(8, nx, ny), f32(4, nz, ny)),
        in_specs=[SMEM] * 4 + [VMEM] * 2,
        out_specs=(VMEM,) * 6,
        compiler_params=params,
        cost_estimate=cost(800, 4),
        name="prepare",
    )(pml_width, eps_real, eps_loss, coeffs, near, material)
    h, packed, xf, yt, xadd, yadd, hxf, zf = pl.pallas_call(
        slab_kernel,
        out_shape=(whole, planes, face, f32(*yf_shape), face, planes, face, f32(*zf_shape)),
        in_specs=[SMEM] * 2 + [VMEM] * 5,
        out_specs=(VMEM,) * 8,
        input_output_aliases={3: 0, 4: 1},
        compiler_params=params,
        name="slab_face",
    )(pml_width, coeffs, basis, h, packed, xf, yf)
    zf = passed_round(zf, "gz", 1)
    h, image, acc, before, basis_new = pl.pallas_call(
        inner_kernel,
        out_shape=(whole, whole, f32(vectors, 2 * vectors, SUB, ny), f32(*zf_shape), whole),
        in_specs=[VMEM] * 7,
        out_specs=(VMEM,) * 4 + (HBM,),
        scratch_shapes=[pltpu.SemaphoreType.DMA],
        input_output_aliases={4: 0},
        compiler_params=params,
        cost_estimate=cost(800, 2),
        name="apply_inner",
    )(basis, loss, table, sz, h, xadd, yadd)
    h, packed, hxf = pl.pallas_call(
        last_plane_kernel,
        out_shape=(whole, planes, face),
        in_specs=[VMEM] * 5,
        out_specs=(VMEM,) * 3,
        input_output_aliases={2: 0, 3: 1, 4: 2},
        compiler_params=params,
        name="last_plane",
    )(sz, zf, h, packed, hxf)
    from_x = passed_round(hxf, "gx", 1)
    image, hyf = pl.pallas_call(
        outer_kernel,
        out_shape=(whole, f32(6 * vectors, nz * nx)),
        in_specs=[SMEM] + [VMEM] * 13,
        out_specs=(VMEM,) * 2,
        input_output_aliases={11: 0},
        compiler_params=params,
        cost_estimate=cost(300, 1),
        name="apply_outer",
    )(pml_width, basis, loss, table, sz, h, zf, xf, yt, hxf, packed, image, acc, before)
    across = lax.axis_size("gy") * lax.axis_size("gz")
    masks = [1 << bit for bit in range((across * lax.axis_size("gx") - 1).bit_length())]
    order = [mask for mask in masks if mask > across] + [across] + [mask for mask in reversed(masks) if mask < across]
    gram = hyf[4 * vectors:]
    hyf = passed_round(hyf, "gy", 1)
    hyf, from_x = lax.optimization_barrier((hyf, from_x))
    if lax.axis_size("gy") == 2:
        gram = gram + hyf[4 * vectors:]
        order.remove(lax.axis_size("gz"))
    for mask in order[:-1]:
        gram = gram + from_partner(gram, mask)
    gram, image = lax.optimization_barrier((gram, image))
    other = from_partner(gram, order[-1])
    residual = pl.pallas_call(
        rim_kernel,
        out_shape=whole,
        in_specs=[SMEM] * 2 + [VMEM] * 4,
        out_specs=HBM,
        scratch_shapes=[scratch(*fields.shape), scratch(nz, nx, ny), pltpu.SemaphoreType.DMA((nz,))],
        compiler_params=params,
        cost_estimate=cost(200, 3),
        name="add_rims",
    )(pml_width, ritz, basis, image, from_x, hyf)
    other, residual = lax.optimization_barrier((other, residual))
    gram = (gram + other)[:, :vectors].reshape(2, vectors, vectors)
    return basis_new, residual, gram


def solution(mesh):
    in_specs = (P(None, None, None, "gz", "gx", "gy"), P("gz", "gx", "gy"), P(), P(), P(), P(), P())
    out_specs = (P(None, None, None, "gz", "gx", "gy"), P(None, None, None, "gz", "gx", "gy"), P())
    return jax.shard_map(body, mesh=mesh, in_specs=in_specs, out_specs=out_specs, check_vma=False)
```

```python
import functools

import jax
import jax.numpy as jnp
from jax import lax
from jax.experimental import pallas as pl
from jax.experimental.pallas import tpu as pltpu
from jax.sharding import PartitionSpec as P

OMEGA_SQ = 0.36
SIGMA_TOP = 3.0
BOUNDS = ((4, 5), (0, 1), (2, 3))
AXES = ("gz", "gx", "gy")

VMEM = pl.BlockSpec(memory_space=pltpu.VMEM)
SMEM = pl.BlockSpec(memory_space=pltpu.SMEM)
HBM = pl.BlockSpec(memory_space=pltpu.HBM)


def passed_round(value, axis, steps):
    count = lax.axis_size(axis)
    return lax.ppermute(value, axis, [(source, (source + steps) % count) for source in range(count)])


def inverse_stretch(places, length, low_width, high_width):
    inside_depth = jnp.clip((low_width - places) / low_width, 0.0, 1.0) + jnp.clip(
        (places + 1.0 - length + high_width) / high_width, 0.0, 1.0
    )
    absorb = SIGMA_TOP * inside_depth * inside_depth
    scaled = 1.0 / (1.0 + absorb * absorb)
    return scaled, -absorb * scaled


def cmul(left, right):
    return (left[0] * right[0] - left[1] * right[1], left[0] * right[1] + left[1] * right[0])


def add(left, right):
    return (left[0] + right[0], left[1] + right[1])


def sub(left, right):
    return (left[0] - right[0], left[1] - right[1])


def axis_stretch(pml_ref, direction, count, places):
    total = count * lax.axis_size(AXES[direction])
    low_slot, high_slot = BOUNDS[direction]
    low = jnp.full(places.shape, pml_ref[low_slot], jnp.int32).astype(jnp.float32)
    high = jnp.full(places.shape, pml_ref[high_slot], jnp.int32).astype(jnp.float32)
    return inverse_stretch(places, jnp.float32(total), low, high)


def local_places(direction, count, shape, dim):
    start = lax.axis_index(AXES[direction]) * count
    return (lax.broadcasted_iota(jnp.int32, shape, dim) + start).astype(jnp.float32)


def one_place(direction, count, offset, shape):
    start = lax.axis_index(AXES[direction]) * count + offset
    return jnp.full(shape, start, jnp.int32).astype(jnp.float32)


def packed_row(slot, part, vector, vectors):
    return (slot * 2 + part) * vectors + vector


def has_neighbour(direction, steps):
    place = lax.axis_index(AXES[direction]) + steps
    inside = (place >= 0) & (place < lax.axis_size(AXES[direction]))
    return jnp.where(inside, 1.0, 0.0).astype(jnp.float32)


def face_kernel(fields_hbm, fields_ref, xf_ref, yf_ref, sems):
    _, vectors, _, nz, nx, ny = fields_ref.shape
    lanes = lax.broadcasted_iota(jnp.int32, (nx, ny), 1)
    copies = [
        pltpu.make_async_copy(fields_hbm.at[part, :, comp], fields_ref.at[part, :, comp], sems.at[part, comp])
        for comp in (0, 2, 1) for part in range(2)
    ]
    for copy in copies:
        copy.start()
    for copy in copies:
        copy.wait()

    packed = [jnp.zeros((nx, ny), jnp.float32)] * nz
    for comp in (0, 2):
        for part in range(2):
            for a in range(vectors):
                row = packed_row(comp // 2, part, a, vectors)
                for z in range(nz):
                    value = fields_ref[part, a, comp, z]
                    packed[z] = jnp.where(lanes == row, pltpu.roll(value, row, 1) if row else value, packed[z])
    turned = jnp.concatenate(packed, axis=0).T
    yf_ref[...] = turned[:yf_ref.shape[0]]
    for part in range(2):
        for a in range(vectors):
            for slot in range(2):
                xf_ref[part, a, slot] = fields_ref[part, a, slot + 1, :, 0, :]


def rotated(coeffs_ref, old, b):
    new = None
    for a, value in enumerate(old):
        term = cmul((coeffs_ref[0, a, b], coeffs_ref[1, a, b]), value)
        new = term if new is None else add(new, term)
    return new


SUB = 8
SHX, SEX, SHY, SEY = range(0, 8, 2)


def field_of(ref, b, comp, z, cut):
    return tuple(ref[part, b, comp, z, cut] for part in range(2))


def tiles_of(nx):
    return [slice(SUB * t, SUB * (t + 1)) for t in range(nx // SUB)]


def prepare_kernel(
    pml_ref, eps_real_ref, eps_loss_ref, coeffs_ref, fields_ref, material_ref,
    basis_ref, loss_ref, h_ref, packed_ref, table_ref, sz_ref,
):
    _, vectors, _, nz, nx, ny = fields_ref.shape
    plane = (nx, ny)
    parts = range(2)
    for slot, direction, half, count, dim in (
        (SHX, 1, 0.5, nx, 0), (SEX, 1, 0.0, nx, 0), (SHY, 2, 0.5, ny, 1), (SEY, 2, 0.0, ny, 1),
    ):
        values = axis_stretch(pml_ref, direction, count, local_places(direction, count, plane, dim) + half)
        for part in parts:
            table_ref[slot + part] = values[part]
    for slot, half in ((0, 0.0), (2, 0.5)):
        values = axis_stretch(pml_ref, 0, nz, local_places(0, nz, (nz, ny), 0) + half)
        for part in parts:
            sz_ref[slot + part] = values[part]

    @pl.loop(0, nz)
    def _(z):
        material = material_ref[z]
        eps = []
        for source in (eps_real_ref, eps_loss_ref):
            value = jnp.zeros(plane, jnp.float32)
            for number in range(source.shape[0]):
                value = jnp.where(material == number, -OMEGA_SQ * source[number], value)
            eps.append(value)
        for comp in range(3):
            old = [(fields_ref[0, a, comp, z], fields_ref[1, a, comp, z]) for a in range(vectors)]
            for b in range(vectors):
                new = rotated(coeffs_ref, old, b)
                loss = cmul(eps, new)
                for part in parts:
                    basis_ref[part, b, comp, z] = new[part]
                    loss_ref[part, b, comp, z] = loss[part]
        packed_ref[z] = jnp.zeros(plane, jnp.float32)

    tile = (SUB, ny)
    rows = lax.broadcasted_iota(jnp.int32, tile, 0)
    lanes = lax.broadcasted_iota(jnp.int32, tile, 1)
    cuts = tiles_of(nx)

    def magnetic(b, z, last):
        shz = tuple(sz_ref[2 + part, pl.ds(z, 1)] for part in parts)
        for cut in cuts:
            u = [field_of(basis_ref, b, comp, z, cut) for comp in range(3)]

            def step_z(comp):
                if last:
                    return tuple(-value for value in u[comp])
                return sub(field_of(basis_ref, b, comp, z + 1, cut), u[comp])

            def step_x(comp):
                if cut.stop < nx:
                    ahead = field_of(basis_ref, b, comp, z, slice(cut.start + 1, cut.stop + 1))
                else:
                    ahead = tuple(jnp.where(rows == SUB - 1, 0.0, pltpu.roll(value, SUB - 1, 0)) for value in u[comp])
                return sub(ahead, u[comp])

            def step_y(comp):
                ahead = tuple(jnp.where(lanes == ny - 1, 0.0, pltpu.roll(value, ny - 1, 1)) for value in u[comp])
                return sub(ahead, u[comp])

            shx = tuple(table_ref[SHX + part, cut] for part in parts)
            shy = tuple(table_ref[SHY + part, cut] for part in parts)
            h = (
                sub(cmul(shy, step_y(2)), cmul(shz, step_z(1))),
                sub(cmul(shz, step_z(0)), cmul(shx, step_x(2))),
                sub(cmul(shx, step_x(1)), cmul(shy, step_y(0))),
            )
            for comp in range(3):
                for part in parts:
                    h_ref[part, b, comp, z, cut] = h[comp][part]
            packed = packed_ref[z, cut]
            for slot, value in enumerate((h[2], h[0])):
                for part in parts:
                    row = packed_row(slot, part, b, vectors)
                    packed = jnp.where(lanes == row, pltpu.roll(value[part], (row + 1) % ny, 1), packed)
            packed_ref[z, cut] = packed

    @pl.loop(0, nz - 1)
    def _(z):
        for b in range(vectors):
            magnetic(b, z, False)

    for b in range(vectors):
        magnetic(b, nz - 1, True)


def turn_face(coeffs_ref, direction, raw_ref, face_ref):
    inside = has_neighbour(direction, 1)
    vectors = raw_ref.shape[1]
    for slot in range(2):
        old = [(raw_ref[0, a, slot] * inside, raw_ref[1, a, slot] * inside) for a in range(vectors)]
        for b in range(vectors):
            new = rotated(coeffs_ref, old, b)
            for part in range(2):
                face_ref[part, b, slot] = new[part]


def turn_column(coeffs_ref, raw_ref, rows_ref):
    vectors = coeffs_ref.shape[1]
    inside = has_neighbour(2, 1)
    both = 2 * vectors
    shape = (both, raw_ref.shape[1])
    which = lax.broadcasted_iota(jnp.int32, shape, 0)
    turned = [jnp.zeros(shape, jnp.float32)] * 2
    for part in range(2):
        for a in range(vectors):
            column = jnp.zeros(shape, jnp.float32)
            for b in range(vectors):
                first, second = coeffs_ref[0, a, b] * inside, coeffs_ref[1, a, b] * inside
                if part:
                    first, second = -second, first
                column = jnp.where(which == b, first, column)
                column = jnp.where(which == vectors + b, second, column)
            for slot in range(2):
                row = packed_row(slot, part, a, vectors)
                turned[slot] = turned[slot] + column * raw_ref[row:row + 1]
    for slot in range(2):
        rows_ref[slot * both:(slot + 1) * both] = turned[slot]


def lane_to_last(values, slot, part, b, vectors):
    ny = values.shape[-1]
    lanes = lax.broadcasted_iota(jnp.int32, values.shape, 1)
    row = packed_row(slot, part, b, vectors)
    return jnp.where(lanes == ny - 1, pltpu.roll(values, ny - 1 - row, 1), 0.0)


def with_halos(h, b, z, cut, nx, xadd_ref, yadd_ref):
    vectors = xadd_ref.shape[1]
    column = yadd_ref[z, cut]
    hx = tuple(h[0][part] + lane_to_last(column, 1, part, b, vectors) for part in range(2))
    hz = tuple(h[2][part] + lane_to_last(column, 0, part, b, vectors) for part in range(2))
    hy = h[1]
    if cut.stop == nx:
        rows = lax.broadcasted_iota(jnp.int32, column.shape, 0)

        def row_of(slot):
            return tuple(
                jnp.where(rows == SUB - 1, xadd_ref[part, b, slot, pl.ds(z, 1)], 0.0) for part in range(2)
            )

        hy, hz = add(hy, row_of(0)), add(hz, row_of(1))
    return hx, hy, hz


def slab_kernel(
    pml_ref, coeffs_ref, basis_ref, h_in, packed_in, raw_xf_ref, raw_yf_ref,
    h_ref, packed_ref, xf_ref, yt_ref, xadd_ref, yadd_ref, hxf_ref, zf_ref,
):
    del h_in, packed_in
    _, vectors, _, nz, nx, ny = basis_ref.shape
    parts = range(2)
    cells = nz * nx
    both = 2 * vectors
    turn_face(coeffs_ref, 1, raw_xf_ref, xf_ref)
    turn_column(coeffs_ref, raw_yf_ref, yt_ref)
    shx = axis_stretch(pml_ref, 1, nx, one_place(1, nx, nx - 1, (1, ny)) + 0.5)
    shy = axis_stretch(pml_ref, 2, ny, one_place(2, ny, ny - 1, (1, cells)) + 0.5)
    for b in range(vectors):
        for slot in range(2):
            value = cmul(shx, tuple(xf_ref[part, b, 1 - slot] for part in parts))
            for part in parts:
                xadd_ref[part, b, slot] = value[part] if slot else -value[part]
    added = []
    for slot in range(2):
        value = cmul(shy, (yt_ref[slot * both:slot * both + vectors], yt_ref[slot * both + vectors:(slot + 1) * both]))
        added += [part if slot else -part for part in value]
    rest = jnp.zeros((ny - 2 * both, cells), jnp.float32)
    yadd_ref[...] = jnp.concatenate(added + [rest], axis=0).T.reshape(nz, nx, ny)
    packed_ref[...] = packed_ref[...] + yadd_ref[...]
    last = nz - 1
    lower = jnp.full((SUB, ny), lax.axis_index(AXES[0]), jnp.int32) == 0
    lanes = lax.broadcasted_iota(jnp.int32, (nz, ny), 1)
    corner = packed_ref[:, nx - 1, :]
    for b in range(vectors):
        for part in parts:
            row = packed_row(0, part, b, vectors)
            edge = pltpu.roll(xadd_ref[part, b, 1], (row + 1) % ny, 1)
            corner = corner + jnp.where(lanes == row, edge, 0.0)
    packed_ref[:, nx - 1, :] = corner
    for b in range(vectors):
        for part in parts:
            hxf_ref[part, b, 0] = h_ref[part, b, 1, :, nx - 1, :] + xadd_ref[part, b, 0]
            hxf_ref[part, b, 1] = (
                h_ref[part, b, 2, :, nx - 1, :] + xadd_ref[part, b, 1]
                + lane_to_last(yadd_ref[:, nx - 1, :], 0, part, b, vectors)
            )
        for cut in tiles_of(nx):
            h = [field_of(h_ref, b, comp, last, cut) for comp in range(3)]
            h = with_halos(h, b, last, cut, nx, xadd_ref, yadd_ref)
            for part in parts:
                for comp in range(3):
                    h_ref[part, b, comp, last, cut] = h[comp][part]
                for comp in range(2):
                    zf_ref[part, b, comp, cut] = jnp.where(lower, h[comp][part], basis_ref[part, b, comp, 0, cut])


def plane_step(b, z, before, sums, basis_ref, loss_ref, table_ref, sz_ref, h_ref, image_ref, halos=None):
    _, vectors, _, _, nx, ny = basis_ref.shape
    rows = lax.broadcasted_iota(jnp.int32, (SUB, ny), 0)
    lanes = lax.broadcasted_iota(jnp.int32, (SUB, ny), 1)
    parts = range(2)
    cuts = tiles_of(nx)
    sez = tuple(sz_ref[part, pl.ds(z, 1)] for part in parts)
    fields = []
    for cut in cuts:
        h = [field_of(h_ref, b, comp, z, cut) for comp in range(3)]
        if halos is not None:
            h = with_halos(h, b, z, cut, nx, *halos)
            for comp in (1, 2):
                for part in parts:
                    h_ref[part, b, comp, z, cut] = h[comp][part]
        fields.append(h)
    sums = list(sums)
    for t, cut in enumerate(cuts):
        hx, hy, hz = fields[t]

        def back_x(comp):
            here = fields[t][comp]
            if t:
                past = field_of(h_ref, b, comp, z, slice(cut.start - 1, cut.stop - 1))
            else:
                past = tuple(jnp.where(rows == 0, 0.0, pltpu.roll(value, 1, 0)) for value in here)
            return sub(here, past)

        def back_y(value):
            return sub(value, tuple(jnp.where(lanes == 0, 0.0, pltpu.roll(part, 1, 1)) for part in value))

        sex = tuple(table_ref[SEX + part, cut] for part in parts)
        sey = tuple(table_ref[SEY + part, cut] for part in parts)
        bxy, bxz = (cmul(sex, back_x(comp)) for comp in (1, 2))
        byz, byx = (cmul(sey, back_y(value)) for value in (hz, hx))
        bzx, bzy = (cmul(sez, sub(value, past)) for value, past in zip((hx, hy), before[t]))
        curl = (sub(byz, bzy), sub(bzx, bxz), sub(bxy, byx))
        w = [add(curl[comp], field_of(loss_ref, b, comp, z, cut)) for comp in range(3)]
        for comp in range(3):
            for part in parts:
                image_ref[part, b, comp, z, cut] = w[comp][part]
        for a in range(vectors):
            total = sums[a]
            for comp in range(3):
                total = add(total, cmul(field_of(basis_ref, a, comp, z, cut), w[comp]))
            sums[a] = total
    return [(h[0], h[1]) for h in fields], sums


def inner_kernel(
    basis_ref, loss_ref, table_ref, sz_ref, h_in, xadd_ref, yadd_ref,
    h_ref, image_ref, acc_ref, before_ref, basis_hbm, sem,
):
    del h_in
    _, vectors, _, nz, nx, ny = basis_ref.shape
    keep = pltpu.make_async_copy(basis_ref, basis_hbm, sem)
    keep.start()
    cuts = tiles_of(nx)
    acc_ref[...] = jnp.zeros(acc_ref.shape, jnp.float32)
    before_ref[...] = jnp.zeros(before_ref.shape, jnp.float32)

    @pl.loop(0, nz - 1)
    def _(z):
        for b in range(vectors):
            before = [
                tuple(tuple(before_ref[part, b, slot, cut] for part in range(2)) for slot in range(2)) for cut in cuts
            ]
            sums = [(acc_ref[b, a], acc_ref[b, vectors + a]) for a in range(vectors)]
            before, sums = plane_step(
                b, z, before, sums, basis_ref, loss_ref, table_ref, sz_ref, h_ref, image_ref, (xadd_ref, yadd_ref)
            )
            for part in range(2):
                for a in range(vectors):
                    acc_ref[b, part * vectors + a] = sums[a][part]
                for t, cut in enumerate(cuts):
                    for slot in range(2):
                        before_ref[part, b, slot, cut] = before[t][slot][part]

    keep.wait()


def last_plane_kernel(sz_ref, zf_ref, h_in, packed_in, hxf_in, h_ref, packed_ref, hxf_ref):
    del h_in, packed_in, hxf_in
    _, vectors, _, nz, nx, ny = h_ref.shape
    parts = range(2)
    last = nz - 1
    lanes = lax.broadcasted_iota(jnp.int32, (SUB, ny), 1)
    shz = tuple(sz_ref[2 + part, last:] * has_neighbour(0, 1) for part in parts)
    packed = [packed_ref[last, cut] for cut in tiles_of(nx)]
    for b in range(vectors):
        for t, cut in enumerate(tiles_of(nx)):
            ex, ey = (tuple(zf_ref[part, b, slot, cut] for part in parts) for slot in range(2))
            more = (tuple(-value for value in cmul(shz, ey)), cmul(shz, ex))
            for part in parts:
                for comp in range(2):
                    h_ref[part, b, comp, last, cut] = h_ref[part, b, comp, last, cut] + more[comp][part]
                row = packed_row(1, part, b, vectors)
                edge = pltpu.roll(more[0][part], (row + 1) % ny, 1)
                packed[t] = packed[t] + jnp.where(lanes == row, edge, 0.0)
                if cut.stop == nx:
                    hxf_ref[part, b, 0, last:] = hxf_ref[part, b, 0, last:] + more[1][part][SUB - 1:]
    for t, cut in enumerate(tiles_of(nx)):
        packed_ref[last, cut] = packed[t]


def outer_kernel(
    pml_ref, basis_ref, loss_ref, table_ref, sz_ref, h_ref, zf_ref, xf_ref, yt_ref, hxf_ref, packed_ref,
    image_in, acc_ref, before_ref, image_ref, hyf_ref,
):
    del image_in
    _, vectors, _, nz, nx, ny = basis_ref.shape
    parts = range(2)
    cuts = tiles_of(nx)
    under = axis_stretch(pml_ref, 0, nz, one_place(0, nz, -1, (1, ny)) + 0.5)
    sez = tuple(sz_ref[part, 0:1] * has_neighbour(0, -1) for part in parts)
    sx_next = axis_stretch(pml_ref, 1, nx, one_place(1, nx, nx, (1, ny)))
    sy_next = axis_stretch(pml_ref, 2, ny, one_place(2, ny, ny, (1, nz * nx)))
    both = 2 * vectors
    hyf_ref[:2 * both] = packed_ref[...].reshape(nz * nx, ny).T[:2 * both]
    ends = [
        cmul(sy_next, (yt_ref[slot * both:slot * both + vectors], yt_ref[slot * both + vectors:(slot + 1) * both]))
        for slot in range(2)
    ]
    columns = lax.broadcasted_iota(jnp.int32, (both, ny), 1)
    gram = jnp.zeros((both, ny), jnp.float32)
    for b in range(vectors):

        def tile_of(ref, slot, cut, b=b):
            return tuple(ref[part, b, slot, cut] for part in parts)

        before = [tuple(tile_of(before_ref, slot, cut) for slot in range(2)) for cut in cuts]
        sums = [(acc_ref[b, a], acc_ref[b, vectors + a]) for a in range(vectors)]
        _, sums = plane_step(
            b, nz - 1, before, sums, basis_ref, loss_ref, table_ref, sz_ref, h_ref, image_ref
        )
        for cut in cuts:
            ex, ey = (field_of(basis_ref, b, comp, 0, cut) for comp in range(2))
            hx = sub(tile_of(zf_ref, 0, cut), cmul(under, ey))
            hy = add(tile_of(zf_ref, 1, cut), cmul(under, ex))
            more = (cmul(sez, hy), cmul(sez, hx))
            for part in parts:
                image_ref[part, b, 0, 0, cut] = image_ref[part, b, 0, 0, cut] + more[0][part]
                image_ref[part, b, 1, 0, cut] = image_ref[part, b, 1, 0, cut] - more[1][part]
            for a in range(vectors):
                ex, ey = (field_of(basis_ref, a, comp, 0, cut) for comp in range(2))
                sums[a] = add(sums[a], sub(cmul(ex, more[0]), cmul(ey, more[1])))
        h_y = tuple(hxf_ref[part, b, 0] for part in parts)
        h_z = tuple(hxf_ref[part, b, 1] for part in parts)
        for a in range(vectors):
            over = cmul(tuple(xf_ref[part, a, 0] for part in parts), h_z)
            over = sub(over, cmul(tuple(xf_ref[part, a, 1] for part in parts), h_y))
            over = cmul(sx_next, over)
            for row in range(0, nz, SUB):
                sums[a] = add(sums[a], tuple(part[row:row + SUB] for part in over))
        flat = jnp.concatenate(
            [jnp.sum(sums[a][part], axis=0, keepdims=True) for part in parts for a in range(vectors)], axis=0
        )
        over = None
        for slot in range(2):
            h = tuple(hyf_ref[packed_row(slot, part, b, vectors)][None] for part in parts)
            term = cmul(ends[slot], h)
            over = term if over is None else sub(term, over)
        side = jnp.concatenate(over, axis=0)
        total = jnp.sum(flat, axis=1, keepdims=True) + jnp.sum(side, axis=1, keepdims=True)
        gram = jnp.where(columns == b, total, gram)
    everywhere = 3.0 * nz * nx * ny
    for axis in AXES:
        everywhere = everywhere * lax.axis_size(axis)
    hyf_ref[2 * both:] = gram * (1.0 / everywhere)


def rim_kernel(
    pml_ref, ritz_ref, basis_ref, image_ref, hxf_ref, hyf_ref, residual_hbm, residual_ref, packed_ref, sems
):
    _, vectors, _, nz, nx, ny = basis_ref.shape
    plane = (nx, ny)
    rows = lax.broadcasted_iota(jnp.int32, plane, 0)
    lanes = lax.broadcasted_iota(jnp.int32, plane, 1)
    sex = axis_stretch(pml_ref, 1, nx, one_place(1, nx, 0, (1, ny)))
    sey = axis_stretch(pml_ref, 2, ny, one_place(2, ny, 0, plane))
    none = jnp.zeros(plane, jnp.float32)
    sex = tuple(jnp.where(rows == 0, part * has_neighbour(1, -1), none) for part in sex)
    sey = tuple(jnp.where(lanes == 0, part * has_neighbour(2, -1), none) for part in sey)
    used = 4 * vectors
    rest = jnp.zeros((ny - used, nz * nx), jnp.float32)
    packed_ref[...] = jnp.concatenate([hyf_ref[:used], rest], axis=0).T.reshape(nz, nx, ny)

    def kept(z):
        return pltpu.make_async_copy(residual_ref.at[:, :, :, z], residual_hbm.at[:, :, :, z], sems.at[z])

    @pl.loop(0, nz)
    def _(z):
        packed = packed_ref[z]
        for b in range(vectors):

            def column(slot, b=b):
                return tuple(
                    pltpu.roll(packed, (ny - packed_row(slot, part, b, vectors)) % ny, 1) for part in range(2)
                )

            def row(slot, b=b):
                return tuple(hxf_ref[part, b, slot, pl.ds(z, 1)] for part in range(2))

            factor = (ritz_ref[0, b], ritz_ref[1, b])
            left = []
            for comp in range(3):
                u = (basis_ref[0, b, comp, z], basis_ref[1, b, comp, z])
                w = (image_ref[0, b, comp, z], image_ref[1, b, comp, z])
                left.append(sub(w, cmul(factor, u)))
            left[0] = sub(left[0], cmul(sey, column(0)))
            left[2] = add(left[2], cmul(sey, column(1)))
            left[1] = add(left[1], cmul(sex, row(1)))
            left[2] = sub(left[2], cmul(sex, row(0)))
            for comp in range(3):
                for part in range(2):
                    residual_ref[part, b, comp, z] = left[comp][part]
        kept(z).start()

    @pl.loop(0, nz)
    def _(z):
        kept(z).wait()


def from_partner(value, mask):
    axes = ("gx", "gy", "gz")
    count = 1
    for axis in axes:
        count *= lax.axis_size(axis)
    return lax.ppermute(value, axes, [(source, source ^ mask) for source in range(count)])


def body(fields, material, pml_width, eps_real, eps_loss, coeffs, ritz):
    _, vectors, _, nz, nx, ny = fields.shape
    f32 = lambda *shape: jax.ShapeDtypeStruct(shape, jnp.float32)
    scratch = lambda *shape: pltpu.VMEM(shape, jnp.float32)
    params = pltpu.CompilerParams(vmem_limit_bytes=40 * 1024 * 1024)
    whole = f32(*fields.shape)
    zf_shape = (2, vectors, 2, nx, ny)
    xf_shape = (2, vectors, 2, nz, ny)
    yf_shape = (4 * vectors, nz * nx)
    near, xf, yf = pl.pallas_call(
        face_kernel,
        out_shape=(whole, f32(*xf_shape), f32(*yf_shape)),
        in_specs=[HBM],
        out_specs=(VMEM,) * 3,
        scratch_shapes=[pltpu.SemaphoreType.DMA((2, 3))],
        compiler_params=params,
        name="take_faces",
    )(pltpu.with_memory_space_constraint(fields, pltpu.HBM))
    xf = passed_round(xf, "gx", -1)
    yf = passed_round(yf, "gy", -1)
    cells = fields.size // 6 // vectors

    def cost(flops, passes):
        return pl.CostEstimate(flops=flops * cells, bytes_accessed=passes * 4 * fields.size, transcendentals=0)

    planes = f32(nz, nx, ny)
    face = f32(*xf_shape)
    basis, loss, h, packed, table, sz = pl.pallas_call(
        prepare_kernel,
        out_shape=(whole, whole, whole, planes, f32(8, nx, ny), f32(4, nz, ny)),
        in_specs=[SMEM] * 4 + [VMEM] * 2,
        out_specs=(VMEM,) * 6,
        compiler_params=params,
        cost_estimate=cost(800, 4),
        name="prepare",
    )(pml_width, eps_real, eps_loss, coeffs, near, material)
    h, packed, xf, yt, xadd, yadd, hxf, zf = pl.pallas_call(
        slab_kernel,
        out_shape=(whole, planes, face, f32(*yf_shape), face, planes, face, f32(*zf_shape)),
        in_specs=[SMEM] * 2 + [VMEM] * 5,
        out_specs=(VMEM,) * 8,
        input_output_aliases={3: 0, 4: 1},
        compiler_params=params,
        name="slab_face",
    )(pml_width, coeffs, basis, h, packed, xf, yf)
    zf = passed_round(zf, "gz", 1)
    h, image, acc, before, basis_new = pl.pallas_call(
        inner_kernel,
        out_shape=(whole, whole, f32(vectors, 2 * vectors, SUB, ny), f32(*zf_shape), whole),
        in_specs=[VMEM] * 7,
        out_specs=(VMEM,) * 4 + (HBM,),
        scratch_shapes=[pltpu.SemaphoreType.DMA],
        input_output_aliases={4: 0},
        compiler_params=params,
        cost_estimate=cost(800, 2),
        name="apply_inner",
    )(basis, loss, table, sz, h, xadd, yadd)
    h, packed, hxf = pl.pallas_call(
        last_plane_kernel,
        out_shape=(whole, planes, face),
        in_specs=[VMEM] * 5,
        out_specs=(VMEM,) * 3,
        input_output_aliases={2: 0, 3: 1, 4: 2},
        compiler_params=params,
        name="last_plane",
    )(sz, zf, h, packed, hxf)
    from_x = passed_round(hxf, "gx", 1)
    image, hyf = pl.pallas_call(
        outer_kernel,
        out_shape=(whole, f32(6 * vectors, nz * nx)),
        in_specs=[SMEM] + [VMEM] * 13,
        out_specs=(VMEM,) * 2,
        input_output_aliases={11: 0},
        compiler_params=params,
        cost_estimate=cost(300, 1),
        name="apply_outer",
    )(pml_width, basis, loss, table, sz, h, zf, xf, yt, hxf, packed, image, acc, before)
    across = lax.axis_size("gy") * lax.axis_size("gz")
    masks = [1 << bit for bit in range((across * lax.axis_size("gx") - 1).bit_length())]
    order = [mask for mask in masks if mask > across] + [across] + [mask for mask in reversed(masks) if mask < across]
    gram = hyf[4 * vectors:]
    hyf = passed_round(hyf, "gy", 1)
    hyf, from_x = lax.optimization_barrier((hyf, from_x))
    if lax.axis_size("gy") == 2:
        gram = gram + hyf[4 * vectors:]
        order.remove(lax.axis_size("gz"))
    for mask in order[:-1]:
        gram = gram + from_partner(gram, mask)
    gram, image = lax.optimization_barrier((gram, image))
    other = from_partner(gram, order[-1])
    residual = pl.pallas_call(
        rim_kernel,
        out_shape=whole,
        in_specs=[SMEM] * 2 + [VMEM] * 4,
        out_specs=HBM,
        scratch_shapes=[scratch(*fields.shape), scratch(nz, nx, ny), pltpu.SemaphoreType.DMA((nz,))],
        compiler_params=params,
        cost_estimate=cost(200, 3),
        name="add_rims",
    )(pml_width, ritz, basis, image, from_x, hyf)
    other, residual = lax.optimization_barrier((other, residual))
    gram = (gram + other)[:, :vectors].reshape(2, vectors, vectors)
    return basis_new, residual, gram


def solution(mesh):
    in_specs = (P(None, None, None, "gz", "gx", "gy"), P("gz", "gx", "gy"), P(), P(), P(), P(), P())
    out_specs = (P(None, None, None, "gz", "gx", "gy"), P(None, None, None, "gz", "gx", "gy"), P())
    return jax.shard_map(body, mesh=mesh, in_specs=in_specs, out_specs=out_specs, check_vma=False)
```

```python
import functools

import jax
import jax.numpy as jnp
from jax import lax
from jax.experimental import pallas as pl
from jax.experimental.pallas import tpu as pltpu
from jax.sharding import PartitionSpec as P

OMEGA_SQ = 0.36
SIGMA_TOP = 3.0
BOUNDS = ((4, 5), (0, 1), (2, 3))
AXES = ("gz", "gx", "gy")

VMEM = pl.BlockSpec(memory_space=pltpu.VMEM)
SMEM = pl.BlockSpec(memory_space=pltpu.SMEM)
HBM = pl.BlockSpec(memory_space=pltpu.HBM)


def passed_round(value, axis, steps):
    count = lax.axis_size(axis)
    return lax.ppermute(value, axis, [(source, (source + steps) % count) for source in range(count)])


def inverse_stretch(places, length, low_width, high_width):
    inside_depth = jnp.clip((low_width - places) / low_width, 0.0, 1.0) + jnp.clip(
        (places + 1.0 - length + high_width) / high_width, 0.0, 1.0
    )
    absorb = SIGMA_TOP * inside_depth * inside_depth
    scaled = 1.0 / (1.0 + absorb * absorb)
    return scaled, -absorb * scaled


def cmul(left, right):
    return (left[0] * right[0] - left[1] * right[1], left[0] * right[1] + left[1] * right[0])


def add(left, right):
    return (left[0] + right[0], left[1] + right[1])


def sub(left, right):
    return (left[0] - right[0], left[1] - right[1])


def axis_stretch(pml_ref, direction, count, places):
    total = count * lax.axis_size(AXES[direction])
    low_slot, high_slot = BOUNDS[direction]
    low = jnp.full(places.shape, pml_ref[low_slot], jnp.int32).astype(jnp.float32)
    high = jnp.full(places.shape, pml_ref[high_slot], jnp.int32).astype(jnp.float32)
    return inverse_stretch(places, jnp.float32(total), low, high)


def local_places(direction, count, shape, dim):
    start = lax.axis_index(AXES[direction]) * count
    return (lax.broadcasted_iota(jnp.int32, shape, dim) + start).astype(jnp.float32)


def one_place(direction, count, offset, shape):
    start = lax.axis_index(AXES[direction]) * count + offset
    return jnp.full(shape, start, jnp.int32).astype(jnp.float32)


def packed_row(slot, part, vector, vectors):
    return (slot * 2 + part) * vectors + vector


def has_neighbour(direction, steps):
    place = lax.axis_index(AXES[direction]) + steps
    inside = (place >= 0) & (place < lax.axis_size(AXES[direction]))
    return jnp.where(inside, 1.0, 0.0).astype(jnp.float32)


def face_kernel(fields_hbm, fields_ref, xf_ref, yf_ref, sems):
    _, vectors, _, nz, nx, ny = fields_ref.shape
    lanes = lax.broadcasted_iota(jnp.int32, (nx, ny), 1)
    copies = [
        pltpu.make_async_copy(fields_hbm.at[part, :, comp], fields_ref.at[part, :, comp], sems.at[part, comp])
        for comp in (0, 2, 1) for part in range(2)
    ]
    for copy in copies:
        copy.start()
    for copy in copies:
        copy.wait()

    packed = [jnp.zeros((nx, ny), jnp.float32)] * nz
    for comp in (0, 2):
        for part in range(2):
            for a in range(vectors):
                row = packed_row(comp // 2, part, a, vectors)
                for z in range(nz):
                    value = fields_ref[part, a, comp, z]
                    packed[z] = jnp.where(lanes == row, pltpu.roll(value, row, 1) if row else value, packed[z])
    turned = jnp.concatenate(packed, axis=0).T
    yf_ref[...] = turned[:yf_ref.shape[0]]
    for part in range(2):
        for a in range(vectors):
            for slot in range(2):
                xf_ref[part, a, slot] = fields_ref[part, a, slot + 1, :, 0, :]


def rotated(coeffs_ref, old, b):
    new = None
    for a, value in enumerate(old):
        term = cmul((coeffs_ref[0, a, b], coeffs_ref[1, a, b]), value)
        new = term if new is None else add(new, term)
    return new


SUB = 8
SHX, SEX, SHY, SEY = range(0, 8, 2)


def field_of(ref, b, comp, z, cut):
    return tuple(ref[part, b, comp, z, cut] for part in range(2))


def tiles_of(nx):
    return [slice(SUB * t, SUB * (t + 1)) for t in range(nx // SUB)]


def prepare_kernel(
    pml_ref, eps_real_ref, eps_loss_ref, coeffs_ref, fields_ref, material_ref,
    basis_ref, loss_ref, h_ref, packed_ref, table_ref, sz_ref,
):
    _, vectors, _, nz, nx, ny = fields_ref.shape
    plane = (nx, ny)
    parts = range(2)
    for slot, direction, half, count, dim in (
        (SHX, 1, 0.5, nx, 0), (SEX, 1, 0.0, nx, 0), (SHY, 2, 0.5, ny, 1), (SEY, 2, 0.0, ny, 1),
    ):
        values = axis_stretch(pml_ref, direction, count, local_places(direction, count, plane, dim) + half)
        for part in parts:
            table_ref[slot + part] = values[part]
    for slot, half in ((0, 0.0), (2, 0.5)):
        values = axis_stretch(pml_ref, 0, nz, local_places(0, nz, (nz, ny), 0) + half)
        for part in parts:
            sz_ref[slot + part] = values[part]

    @pl.loop(0, nz)
    def _(z):
        material = material_ref[z]
        eps = []
        for source in (eps_real_ref, eps_loss_ref):
            value = jnp.zeros(plane, jnp.float32)
            for number in range(source.shape[0]):
                value = jnp.where(material == number, -OMEGA_SQ * source[number], value)
            eps.append(value)
        for comp in range(3):
            old = [(fields_ref[0, a, comp, z], fields_ref[1, a, comp, z]) for a in range(vectors)]
            for b in range(vectors):
                new = rotated(coeffs_ref, old, b)
                loss = cmul(eps, new)
                for part in parts:
                    basis_ref[part, b, comp, z] = new[part]
                    loss_ref[part, b, comp, z] = loss[part]
        packed_ref[z] = jnp.zeros(plane, jnp.float32)

    tile = (SUB, ny)
    rows = lax.broadcasted_iota(jnp.int32, tile, 0)
    lanes = lax.broadcasted_iota(jnp.int32, tile, 1)
    cuts = tiles_of(nx)

    def magnetic(b, z, last):
        shz = tuple(sz_ref[2 + part, pl.ds(z, 1)] for part in parts)
        for cut in cuts:
            u = [field_of(basis_ref, b, comp, z, cut) for comp in range(3)]

            def step_z(comp):
                if last:
                    return tuple(-value for value in u[comp])
                return sub(field_of(basis_ref, b, comp, z + 1, cut), u[comp])

            def step_x(comp):
                if cut.stop < nx:
                    ahead = field_of(basis_ref, b, comp, z, slice(cut.start + 1, cut.stop + 1))
                else:
                    ahead = tuple(jnp.where(rows == SUB - 1, 0.0, pltpu.roll(value, SUB - 1, 0)) for value in u[comp])
                return sub(ahead, u[comp])

            def step_y(comp):
                ahead = tuple(jnp.where(lanes == ny - 1, 0.0, pltpu.roll(value, ny - 1, 1)) for value in u[comp])
                return sub(ahead, u[comp])

            shx = tuple(table_ref[SHX + part, cut] for part in parts)
            shy = tuple(table_ref[SHY + part, cut] for part in parts)
            h = (
                sub(cmul(shy, step_y(2)), cmul(shz, step_z(1))),
                sub(cmul(shz, step_z(0)), cmul(shx, step_x(2))),
                sub(cmul(shx, step_x(1)), cmul(shy, step_y(0))),
            )
            for comp in range(3):
                for part in parts:
                    h_ref[part, b, comp, z, cut] = h[comp][part]
            packed = packed_ref[z, cut]
            for slot, value in enumerate((h[2], h[0])):
                for part in parts:
                    row = packed_row(slot, part, b, vectors)
                    packed = jnp.where(lanes == row, pltpu.roll(value[part], (row + 1) % ny, 1), packed)
            packed_ref[z, cut] = packed

    @pl.loop(0, nz - 1)
    def _(z):
        for b in range(vectors):
            magnetic(b, z, False)

    for b in range(vectors):
        magnetic(b, nz - 1, True)


def turn_face(coeffs_ref, direction, raw_ref, face_ref):
    inside = has_neighbour(direction, 1)
    vectors = raw_ref.shape[1]
    for slot in range(2):
        old = [(raw_ref[0, a, slot] * inside, raw_ref[1, a, slot] * inside) for a in range(vectors)]
        for b in range(vectors):
            new = rotated(coeffs_ref, old, b)
            for part in range(2):
                face_ref[part, b, slot] = new[part]


def turn_column(coeffs_ref, raw_ref, rows_ref):
    vectors = coeffs_ref.shape[1]
    inside = has_neighbour(2, 1)
    both = 2 * vectors
    shape = (both, raw_ref.shape[1])
    which = lax.broadcasted_iota(jnp.int32, shape, 0)
    turned = [jnp.zeros(shape, jnp.float32)] * 2
    for part in range(2):
        for a in range(vectors):
            column = jnp.zeros(shape, jnp.float32)
            for b in range(vectors):
                first, second = coeffs_ref[0, a, b] * inside, coeffs_ref[1, a, b] * inside
                if part:
                    first, second = -second, first
                column = jnp.where(which == b, first, column)
                column = jnp.where(which == vectors + b, second, column)
            for slot in range(2):
                row = packed_row(slot, part, a, vectors)
                turned[slot] = turned[slot] + column * raw_ref[row:row + 1]
    for slot in range(2):
        rows_ref[slot * both:(slot + 1) * both] = turned[slot]


def lane_to_last(values, slot, part, b, vectors):
    ny = values.shape[-1]
    lanes = lax.broadcasted_iota(jnp.int32, values.shape, 1)
    row = packed_row(slot, part, b, vectors)
    return jnp.where(lanes == ny - 1, pltpu.roll(values, ny - 1 - row, 1), 0.0)


def with_halos(h, b, z, cut, nx, xadd_ref, yadd_ref):
    vectors = xadd_ref.shape[1]
    column = yadd_ref[z, cut]
    hx = tuple(h[0][part] + lane_to_last(column, 1, part, b, vectors) for part in range(2))
    hz = tuple(h[2][part] + lane_to_last(column, 0, part, b, vectors) for part in range(2))
    hy = h[1]
    if cut.stop == nx:
        rows = lax.broadcasted_iota(jnp.int32, column.shape, 0)

        def row_of(slot):
            return tuple(
                jnp.where(rows == SUB - 1, xadd_ref[part, b, slot, pl.ds(z, 1)], 0.0) for part in range(2)
            )

        hy, hz = add(hy, row_of(0)), add(hz, row_of(1))
    return hx, hy, hz


def slab_kernel(
    pml_ref, coeffs_ref, basis_ref, h_in, packed_in, raw_xf_ref, raw_yf_ref,
    h_ref, packed_ref, xf_ref, yt_ref, xadd_ref, yadd_ref, hxf_ref, zf_ref,
):
    del h_in, packed_in
    _, vectors, _, nz, nx, ny = basis_ref.shape
    parts = range(2)
    cells = nz * nx
    both = 2 * vectors
    turn_face(coeffs_ref, 1, raw_xf_ref, xf_ref)
    turn_column(coeffs_ref, raw_yf_ref, yt_ref)
    shx = axis_stretch(pml_ref, 1, nx, one_place(1, nx, nx - 1, (1, ny)) + 0.5)
    shy = axis_stretch(pml_ref, 2, ny, one_place(2, ny, ny - 1, (1, cells)) + 0.5)
    for b in range(vectors):
        for slot in range(2):
            value = cmul(shx, tuple(xf_ref[part, b, 1 - slot] for part in parts))
            for part in parts:
                xadd_ref[part, b, slot] = value[part] if slot else -value[part]
    added = []
    for slot in range(2):
        value = cmul(shy, (yt_ref[slot * both:slot * both + vectors], yt_ref[slot * both + vectors:(slot + 1) * both]))
        added += [part if slot else -part for part in value]
    rest = jnp.zeros((ny - 2 * both, cells), jnp.float32)
    yadd_ref[...] = jnp.concatenate(added + [rest], axis=0).T.reshape(nz, nx, ny)
    packed_ref[...] = packed_ref[...] + yadd_ref[...]
    last = nz - 1
    lower = jnp.full((SUB, ny), lax.axis_index(AXES[0]), jnp.int32) == 0
    lanes = lax.broadcasted_iota(jnp.int32, (nz, ny), 1)
    corner = packed_ref[:, nx - 1, :]
    for b in range(vectors):
        for part in parts:
            row = packed_row(0, part, b, vectors)
            edge = pltpu.roll(xadd_ref[part, b, 1], (row + 1) % ny, 1)
            corner = corner + jnp.where(lanes == row, edge, 0.0)
    packed_ref[:, nx - 1, :] = corner
    for b in range(vectors):
        for part in parts:
            hxf_ref[part, b, 0] = h_ref[part, b, 1, :, nx - 1, :] + xadd_ref[part, b, 0]
            hxf_ref[part, b, 1] = (
                h_ref[part, b, 2, :, nx - 1, :] + xadd_ref[part, b, 1]
                + lane_to_last(yadd_ref[:, nx - 1, :], 0, part, b, vectors)
            )
        for cut in tiles_of(nx):
            h = [field_of(h_ref, b, comp, last, cut) for comp in range(3)]
            h = with_halos(h, b, last, cut, nx, xadd_ref, yadd_ref)
            for part in parts:
                for comp in range(3):
                    h_ref[part, b, comp, last, cut] = h[comp][part]
                for comp in range(2):
                    zf_ref[part, b, comp, cut] = jnp.where(lower, h[comp][part], basis_ref[part, b, comp, 0, cut])


def plane_step(b, z, before, sums, basis_ref, loss_ref, table_ref, sz_ref, h_ref, image_ref, halos=None):
    _, vectors, _, _, nx, ny = basis_ref.shape
    rows = lax.broadcasted_iota(jnp.int32, (SUB, ny), 0)
    lanes = lax.broadcasted_iota(jnp.int32, (SUB, ny), 1)
    parts = range(2)
    cuts = tiles_of(nx)
    sez = tuple(sz_ref[part, pl.ds(z, 1)] for part in parts)
    fields = []
    for cut in cuts:
        h = [field_of(h_ref, b, comp, z, cut) for comp in range(3)]
        if halos is not None:
            h = with_halos(h, b, z, cut, nx, *halos)
            for comp in (1, 2):
                for part in parts:
                    h_ref[part, b, comp, z, cut] = h[comp][part]
        fields.append(h)
    sums = list(sums)
    for t, cut in enumerate(cuts):
        hx, hy, hz = fields[t]

        def back_x(comp):
            here = fields[t][comp]
            if t:
                past = field_of(h_ref, b, comp, z, slice(cut.start - 1, cut.stop - 1))
            else:
                past = tuple(jnp.where(rows == 0, 0.0, pltpu.roll(value, 1, 0)) for value in here)
            return sub(here, past)

        def back_y(value):
            return sub(value, tuple(jnp.where(lanes == 0, 0.0, pltpu.roll(part, 1, 1)) for part in value))

        sex = tuple(table_ref[SEX + part, cut] for part in parts)
        sey = tuple(table_ref[SEY + part, cut] for part in parts)
        bxy, bxz = (cmul(sex, back_x(comp)) for comp in (1, 2))
        byz, byx = (cmul(sey, back_y(value)) for value in (hz, hx))
        bzx, bzy = (cmul(sez, sub(value, past)) for value, past in zip((hx, hy), before[t]))
        curl = (sub(byz, bzy), sub(bzx, bxz), sub(bxy, byx))
        w = [add(curl[comp], field_of(loss_ref, b, comp, z, cut)) for comp in range(3)]
        for comp in range(3):
            for part in parts:
                image_ref[part, b, comp, z, cut] = w[comp][part]
        for a in range(vectors):
            total = sums[a]
            for comp in range(3):
                total = add(total, cmul(field_of(basis_ref, a, comp, z, cut), w[comp]))
            sums[a] = total
    return [(h[0], h[1]) for h in fields], sums


def inner_kernel(
    basis_ref, loss_ref, table_ref, sz_ref, h_in, xadd_ref, yadd_ref,
    h_ref, image_ref, acc_ref, before_ref, basis_hbm, sem,
):
    del h_in
    _, vectors, _, nz, nx, ny = basis_ref.shape
    keep = pltpu.make_async_copy(basis_ref, basis_hbm, sem)
    keep.start()
    cuts = tiles_of(nx)
    acc_ref[...] = jnp.zeros(acc_ref.shape, jnp.float32)
    before_ref[...] = jnp.zeros(before_ref.shape, jnp.float32)

    @pl.loop(0, nz - 1)
    def _(z):
        for b in range(vectors):
            before = [
                tuple(tuple(before_ref[part, b, slot, cut] for part in range(2)) for slot in range(2)) for cut in cuts
            ]
            sums = [(acc_ref[b, a], acc_ref[b, vectors + a]) for a in range(vectors)]
            before, sums = plane_step(
                b, z, before, sums, basis_ref, loss_ref, table_ref, sz_ref, h_ref, image_ref, (xadd_ref, yadd_ref)
            )
            for part in range(2):
                for a in range(vectors):
                    acc_ref[b, part * vectors + a] = sums[a][part]
                for t, cut in enumerate(cuts):
                    for slot in range(2):
                        before_ref[part, b, slot, cut] = before[t][slot][part]

    keep.wait()


def last_plane_kernel(sz_ref, zf_ref, h_in, packed_in, hxf_in, h_ref, hxf_ref, hyf_ref):
    del h_in, hxf_in
    _, vectors, _, nz, nx, ny = h_ref.shape
    parts = range(2)
    last = nz - 1
    lanes = lax.broadcasted_iota(jnp.int32, (SUB, ny), 1)
    shz = tuple(sz_ref[2 + part, last:] * has_neighbour(0, 1) for part in parts)
    packed = [packed_in[last, cut] for cut in tiles_of(nx)]
    for b in range(vectors):
        for t, cut in enumerate(tiles_of(nx)):
            ex, ey = (tuple(zf_ref[part, b, slot, cut] for part in parts) for slot in range(2))
            more = (tuple(-value for value in cmul(shz, ey)), cmul(shz, ex))
            for part in parts:
                for comp in range(2):
                    h_ref[part, b, comp, last, cut] = h_ref[part, b, comp, last, cut] + more[comp][part]
                row = packed_row(1, part, b, vectors)
                edge = pltpu.roll(more[0][part], (row + 1) % ny, 1)
                packed[t] = packed[t] + jnp.where(lanes == row, edge, 0.0)
                if cut.stop == nx:
                    hxf_ref[part, b, 0, last:] = hxf_ref[part, b, 0, last:] + more[1][part][SUB - 1:]
    inner = packed_in[:last].reshape(last * nx, ny)
    hyf_ref[...] = jnp.concatenate([inner] + packed, axis=0).T[:hyf_ref.shape[0]]


def outer_kernel(
    pml_ref, basis_ref, loss_ref, table_ref, sz_ref, h_ref, zf_ref, xf_ref, yt_ref, hxf_ref, hyf_ref,
    image_in, acc_ref, before_ref, image_ref, gram_ref,
):
    del image_in
    _, vectors, _, nz, nx, ny = basis_ref.shape
    parts = range(2)
    cuts = tiles_of(nx)
    under = axis_stretch(pml_ref, 0, nz, one_place(0, nz, -1, (1, ny)) + 0.5)
    sez = tuple(sz_ref[part, 0:1] * has_neighbour(0, -1) for part in parts)
    sx_next = axis_stretch(pml_ref, 1, nx, one_place(1, nx, nx, (1, ny)))
    sy_next = axis_stretch(pml_ref, 2, ny, one_place(2, ny, ny, (1, nz * nx)))
    both = 2 * vectors
    ends = [
        cmul(sy_next, (yt_ref[slot * both:slot * both + vectors], yt_ref[slot * both + vectors:(slot + 1) * both]))
        for slot in range(2)
    ]
    columns = lax.broadcasted_iota(jnp.int32, (both, ny), 1)
    gram = jnp.zeros((both, ny), jnp.float32)
    for b in range(vectors):

        def tile_of(ref, slot, cut, b=b):
            return tuple(ref[part, b, slot, cut] for part in parts)

        before = [tuple(tile_of(before_ref, slot, cut) for slot in range(2)) for cut in cuts]
        sums = [(acc_ref[b, a], acc_ref[b, vectors + a]) for a in range(vectors)]
        _, sums = plane_step(
            b, nz - 1, before, sums, basis_ref, loss_ref, table_ref, sz_ref, h_ref, image_ref
        )
        for cut in cuts:
            ex, ey = (field_of(basis_ref, b, comp, 0, cut) for comp in range(2))
            hx = sub(tile_of(zf_ref, 0, cut), cmul(under, ey))
            hy = add(tile_of(zf_ref, 1, cut), cmul(under, ex))
            more = (cmul(sez, hy), cmul(sez, hx))
            for part in parts:
                image_ref[part, b, 0, 0, cut] = image_ref[part, b, 0, 0, cut] + more[0][part]
                image_ref[part, b, 1, 0, cut] = image_ref[part, b, 1, 0, cut] - more[1][part]
            for a in range(vectors):
                ex, ey = (field_of(basis_ref, a, comp, 0, cut) for comp in range(2))
                sums[a] = add(sums[a], sub(cmul(ex, more[0]), cmul(ey, more[1])))
        h_y = tuple(hxf_ref[part, b, 0] for part in parts)
        h_z = tuple(hxf_ref[part, b, 1] for part in parts)
        for a in range(vectors):
            over = cmul(tuple(xf_ref[part, a, 0] for part in parts), h_z)
            over = sub(over, cmul(tuple(xf_ref[part, a, 1] for part in parts), h_y))
            over = cmul(sx_next, over)
            for row in range(0, nz, SUB):
                sums[a] = add(sums[a], tuple(part[row:row + SUB] for part in over))
        flat = jnp.concatenate(
            [jnp.sum(sums[a][part], axis=0, keepdims=True) for part in parts for a in range(vectors)], axis=0
        )
        over = None
        for slot in range(2):
            h = tuple(hyf_ref[packed_row(slot, part, b, vectors)][None] for part in parts)
            term = cmul(ends[slot], h)
            over = term if over is None else sub(term, over)
        side = jnp.concatenate(over, axis=0)
        total = jnp.sum(flat, axis=1, keepdims=True) + jnp.sum(side, axis=1, keepdims=True)
        gram = jnp.where(columns == b, total, gram)
    everywhere = 3.0 * nz * nx * ny
    for axis in AXES:
        everywhere = everywhere * lax.axis_size(axis)
    gram = gram * (1.0 / everywhere)
    flat = gram[0:1]
    for row in range(1, both):
        flat = flat + pltpu.roll(gram[row:row + 1], row * vectors, 1)
    for device in range(gram_ref.shape[0]):
        gram_ref[device] = flat


def gather_kernel(rows_ref, gram_ref):
    vectors = gram_ref.shape[1]
    total = rows_ref[0]
    for device in range(1, rows_ref.shape[0]):
        total = total + rows_ref[device]
    for part in range(2):
        for a in range(vectors):
            row = (part * vectors + a) * vectors
            turned = pltpu.roll(total, (total.shape[1] - row) % total.shape[1], 1)
            gram_ref[part, a:a + 1] = turned[:, :vectors]


def rim_kernel(
    pml_ref, ritz_ref, basis_ref, image_ref, hxf_ref, hyf_ref, residual_hbm, residual_ref, packed_ref, sems
):
    _, vectors, _, nz, nx, ny = basis_ref.shape
    plane = (nx, ny)
    rows = lax.broadcasted_iota(jnp.int32, plane, 0)
    lanes = lax.broadcasted_iota(jnp.int32, plane, 1)
    sex = axis_stretch(pml_ref, 1, nx, one_place(1, nx, 0, (1, ny)))
    sey = axis_stretch(pml_ref, 2, ny, one_place(2, ny, 0, plane))
    none = jnp.zeros(plane, jnp.float32)
    sex = tuple(jnp.where(rows == 0, part * has_neighbour(1, -1), none) for part in sex)
    sey = tuple(jnp.where(lanes == 0, part * has_neighbour(2, -1), none) for part in sey)
    rest = jnp.zeros((ny - hyf_ref.shape[0], nz * nx), jnp.float32)
    packed_ref[...] = jnp.concatenate([hyf_ref[...], rest], axis=0).T.reshape(nz, nx, ny)

    def kept(z):
        return pltpu.make_async_copy(residual_ref.at[:, :, :, z], residual_hbm.at[:, :, :, z], sems.at[z])

    @pl.loop(0, nz)
    def _(z):
        packed = packed_ref[z]
        for b in range(vectors):

            def column(slot, b=b):
                return tuple(
                    pltpu.roll(packed, (ny - packed_row(slot, part, b, vectors)) % ny, 1) for part in range(2)
                )

            def row(slot, b=b):
                return tuple(hxf_ref[part, b, slot, pl.ds(z, 1)] for part in range(2))

            factor = (ritz_ref[0, b], ritz_ref[1, b])
            left = []
            for comp in range(3):
                u = (basis_ref[0, b, comp, z], basis_ref[1, b, comp, z])
                w = (image_ref[0, b, comp, z], image_ref[1, b, comp, z])
                left.append(sub(w, cmul(factor, u)))
            left[0] = sub(left[0], cmul(sey, column(0)))
            left[2] = add(left[2], cmul(sey, column(1)))
            left[1] = add(left[1], cmul(sex, row(1)))
            left[2] = sub(left[2], cmul(sex, row(0)))
            for comp in range(3):
                for part in range(2):
                    residual_ref[part, b, comp, z] = left[comp][part]
        kept(z).start()

    @pl.loop(0, nz)
    def _(z):
        kept(z).wait()


def body(fields, material, pml_width, eps_real, eps_loss, coeffs, ritz):
    _, vectors, _, nz, nx, ny = fields.shape
    f32 = lambda *shape: jax.ShapeDtypeStruct(shape, jnp.float32)
    scratch = lambda *shape: pltpu.VMEM(shape, jnp.float32)
    params = pltpu.CompilerParams(vmem_limit_bytes=40 * 1024 * 1024)
    whole = f32(*fields.shape)
    zf_shape = (2, vectors, 2, nx, ny)
    xf_shape = (2, vectors, 2, nz, ny)
    yf_shape = (4 * vectors, nz * nx)
    near, xf, yf = pl.pallas_call(
        face_kernel,
        out_shape=(whole, f32(*xf_shape), f32(*yf_shape)),
        in_specs=[HBM],
        out_specs=(VMEM,) * 3,
        scratch_shapes=[pltpu.SemaphoreType.DMA((2, 3))],
        compiler_params=params,
        name="take_faces",
    )(pltpu.with_memory_space_constraint(fields, pltpu.HBM))
    xf = passed_round(xf, "gx", -1)
    yf = passed_round(yf, "gy", -1)
    cells = fields.size // 6 // vectors

    def cost(flops, passes):
        return pl.CostEstimate(flops=flops * cells, bytes_accessed=passes * 4 * fields.size, transcendentals=0)

    planes = f32(nz, nx, ny)
    face = f32(*xf_shape)
    basis, loss, h, packed, table, sz = pl.pallas_call(
        prepare_kernel,
        out_shape=(whole, whole, whole, planes, f32(8, nx, ny), f32(4, nz, ny)),
        in_specs=[SMEM] * 4 + [VMEM] * 2,
        out_specs=(VMEM,) * 6,
        compiler_params=params,
        cost_estimate=cost(800, 4),
        name="prepare",
    )(pml_width, eps_real, eps_loss, coeffs, near, material)
    h, packed, xf, yt, xadd, yadd, hxf, zf = pl.pallas_call(
        slab_kernel,
        out_shape=(whole, planes, face, f32(*yf_shape), face, planes, face, f32(*zf_shape)),
        in_specs=[SMEM] * 2 + [VMEM] * 5,
        out_specs=(VMEM,) * 8,
        input_output_aliases={3: 0, 4: 1},
        compiler_params=params,
        name="slab_face",
    )(pml_width, coeffs, basis, h, packed, xf, yf)
    zf = passed_round(zf, "gz", 1)
    h, image, acc, before, basis_new = pl.pallas_call(
        inner_kernel,
        out_shape=(whole, whole, f32(vectors, 2 * vectors, SUB, ny), f32(*zf_shape), whole),
        in_specs=[VMEM] * 7,
        out_specs=(VMEM,) * 4 + (HBM,),
        scratch_shapes=[pltpu.SemaphoreType.DMA],
        input_output_aliases={4: 0},
        compiler_params=params,
        cost_estimate=cost(800, 2),
        name="apply_inner",
    )(basis, loss, table, sz, h, xadd, yadd)
    h, hxf, hyf = pl.pallas_call(
        last_plane_kernel,
        out_shape=(whole, face, f32(*yf_shape)),
        in_specs=[VMEM] * 5,
        out_specs=(VMEM,) * 3,
        input_output_aliases={2: 0, 4: 1},
        compiler_params=params,
        name="last_plane",
    )(sz, zf, h, packed, hxf)
    from_x = passed_round(hxf, "gx", 1)
    from_y = passed_round(hyf, "gy", 1)
    devices = lax.axis_size("gx") * lax.axis_size("gy") * lax.axis_size("gz")
    image, gram = pl.pallas_call(
        outer_kernel,
        out_shape=(whole, f32(devices, 1, ny)),
        in_specs=[SMEM] + [VMEM] * 13,
        out_specs=(VMEM,) * 2,
        input_output_aliases={11: 0},
        compiler_params=params,
        cost_estimate=cost(300, 1),
        name="apply_outer",
    )(pml_width, basis, loss, table, sz, h, zf, xf, yt, hxf, hyf, image, acc, before)
    rows = lax.all_to_all(gram, ("gx", "gy", "gz"), 0, 0)
    residual = pl.pallas_call(
        rim_kernel,
        out_shape=whole,
        in_specs=[SMEM] * 2 + [VMEM] * 4,
        out_specs=HBM,
        scratch_shapes=[scratch(*fields.shape), scratch(nz, nx, ny), pltpu.SemaphoreType.DMA((nz,))],
        compiler_params=params,
        cost_estimate=cost(200, 3),
        name="add_rims",
    )(pml_width, ritz, basis, image, from_x, from_y)
    rows, residual = lax.optimization_barrier((rows, residual))
    gram = pl.pallas_call(
        gather_kernel,
        out_shape=f32(2, vectors, vectors),
        in_specs=[VMEM],
        out_specs=VMEM,
        compiler_params=params,
        name="sum_rows",
    )(rows)
    return basis_new, residual, gram


def solution(mesh):
    in_specs = (P(None, None, None, "gz", "gx", "gy"), P("gz", "gx", "gy"), P(), P(), P(), P(), P())
    out_specs = (P(None, None, None, "gz", "gx", "gy"), P(None, None, None, "gz", "gx", "gy"), P())
    return jax.shard_map(body, mesh=mesh, in_specs=in_specs, out_specs=out_specs, check_vma=False)
```

```python
import functools

import jax
import jax.numpy as jnp
from jax import lax
from jax.experimental import pallas as pl
from jax.experimental.pallas import tpu as pltpu
from jax.sharding import PartitionSpec as P

OMEGA_SQ = 0.36
SIGMA_TOP = 3.0
BOUNDS = ((4, 5), (0, 1), (2, 3))
AXES = ("gz", "gx", "gy")

VMEM = pl.BlockSpec(memory_space=pltpu.VMEM)
SMEM = pl.BlockSpec(memory_space=pltpu.SMEM)
HBM = pl.BlockSpec(memory_space=pltpu.HBM)


def passed_round(value, axis, steps):
    count = lax.axis_size(axis)
    return lax.ppermute(value, axis, [(source, (source + steps) % count) for source in range(count)])


def inverse_stretch(places, length, low_width, high_width):
    inside_depth = jnp.clip((low_width - places) / low_width, 0.0, 1.0) + jnp.clip(
        (places + 1.0 - length + high_width) / high_width, 0.0, 1.0
    )
    absorb = SIGMA_TOP * inside_depth * inside_depth
    scaled = 1.0 / (1.0 + absorb * absorb)
    return scaled, -absorb * scaled


def cmul(left, right):
    return (left[0] * right[0] - left[1] * right[1], left[0] * right[1] + left[1] * right[0])


def add(left, right):
    return (left[0] + right[0], left[1] + right[1])


def sub(left, right):
    return (left[0] - right[0], left[1] - right[1])


def axis_stretch(pml_ref, direction, count, places):
    total = count * lax.axis_size(AXES[direction])
    low_slot, high_slot = BOUNDS[direction]
    low = jnp.full(places.shape, pml_ref[low_slot], jnp.int32).astype(jnp.float32)
    high = jnp.full(places.shape, pml_ref[high_slot], jnp.int32).astype(jnp.float32)
    return inverse_stretch(places, jnp.float32(total), low, high)


def local_places(direction, count, shape, dim):
    start = lax.axis_index(AXES[direction]) * count
    return (lax.broadcasted_iota(jnp.int32, shape, dim) + start).astype(jnp.float32)


def one_place(direction, count, offset, shape):
    start = lax.axis_index(AXES[direction]) * count + offset
    return jnp.full(shape, start, jnp.int32).astype(jnp.float32)


def packed_row(slot, part, vector, vectors):
    return (slot * 2 + part) * vectors + vector


def has_neighbour(direction, steps):
    place = lax.axis_index(AXES[direction]) + steps
    inside = (place >= 0) & (place < lax.axis_size(AXES[direction]))
    return jnp.where(inside, 1.0, 0.0).astype(jnp.float32)


def face_kernel(fields_hbm, fields_ref, xf_ref, yf_ref, sems):
    _, vectors, _, nz, nx, ny = fields_ref.shape
    lanes = lax.broadcasted_iota(jnp.int32, (nx, ny), 1)
    copies = [
        pltpu.make_async_copy(fields_hbm.at[part, :, comp], fields_ref.at[part, :, comp], sems.at[part, comp])
        for comp in (0, 2, 1) for part in range(2)
    ]
    for copy in copies:
        copy.start()
    packed = [jnp.zeros((nx, ny), jnp.float32)] * nz
    for place, comp in enumerate((0, 2)):
        for part in range(2):
            copies[2 * place + part].wait()
            for a in range(vectors):
                row = packed_row(comp // 2, part, a, vectors)
                for z in range(nz):
                    value = fields_ref[part, a, comp, z]
                    packed[z] = jnp.where(lanes == row, pltpu.roll(value, row, 1) if row else value, packed[z])
    turned = jnp.concatenate(packed, axis=0).T
    yf_ref[...] = turned[:yf_ref.shape[0]]
    for part in range(2):
        for a in range(vectors):
            xf_ref[part, a, 1] = fields_ref[part, a, 2, :, 0, :]
    for part in range(2):
        copies[4 + part].wait()
        for a in range(vectors):
            xf_ref[part, a, 0] = fields_ref[part, a, 1, :, 0, :]


def rotated(coeffs_ref, old, b):
    new = None
    for a, value in enumerate(old):
        term = cmul((coeffs_ref[0, a, b], coeffs_ref[1, a, b]), value)
        new = term if new is None else add(new, term)
    return new


SUB = 8
SHX, SEX, SHY, SEY = range(0, 8, 2)


def field_of(ref, b, comp, z, cut):
    return tuple(ref[part, b, comp, z, cut] for part in range(2))


def tiles_of(nx):
    return [slice(SUB * t, SUB * (t + 1)) for t in range(nx // SUB)]


def prepare_kernel(
    pml_ref, eps_real_ref, eps_loss_ref, coeffs_ref, fields_ref, material_ref,
    basis_ref, loss_ref, h_ref, packed_ref, table_ref, sz_ref,
):
    _, vectors, _, nz, nx, ny = fields_ref.shape
    plane = (nx, ny)
    parts = range(2)
    for slot, direction, half, count, dim in (
        (SHX, 1, 0.5, nx, 0), (SEX, 1, 0.0, nx, 0), (SHY, 2, 0.5, ny, 1), (SEY, 2, 0.0, ny, 1),
    ):
        values = axis_stretch(pml_ref, direction, count, local_places(direction, count, plane, dim) + half)
        for part in parts:
            table_ref[slot + part] = values[part]
    for slot, half in ((0, 0.0), (2, 0.5)):
        values = axis_stretch(pml_ref, 0, nz, local_places(0, nz, (nz, ny), 0) + half)
        for part in parts:
            sz_ref[slot + part] = values[part]

    @pl.loop(0, nz)
    def _(z):
        material = material_ref[z]
        eps = []
        for source in (eps_real_ref, eps_loss_ref):
            value = jnp.zeros(plane, jnp.float32)
            for number in range(source.shape[0]):
                value = jnp.where(material == number, -OMEGA_SQ * source[number], value)
            eps.append(value)
        for comp in range(3):
            old = [(fields_ref[0, a, comp, z], fields_ref[1, a, comp, z]) for a in range(vectors)]
            for b in range(vectors):
                new = rotated(coeffs_ref, old, b)
                loss = cmul(eps, new)
                for part in parts:
                    basis_ref[part, b, comp, z] = new[part]
                    loss_ref[part, b, comp, z] = loss[part]
        packed_ref[z] = jnp.zeros(plane, jnp.float32)

    tile = (SUB, ny)
    rows = lax.broadcasted_iota(jnp.int32, tile, 0)
    lanes = lax.broadcasted_iota(jnp.int32, tile, 1)
    cuts = tiles_of(nx)

    def magnetic(b, z, last):
        shz = tuple(sz_ref[2 + part, pl.ds(z, 1)] for part in parts)
        for cut in cuts:
            u = [field_of(basis_ref, b, comp, z, cut) for comp in range(3)]

            def step_z(comp):
                if last:
                    return tuple(-value for value in u[comp])
                return sub(field_of(basis_ref, b, comp, z + 1, cut), u[comp])

            def step_x(comp):
                if cut.stop < nx:
                    ahead = field_of(basis_ref, b, comp, z, slice(cut.start + 1, cut.stop + 1))
                else:
                    ahead = tuple(jnp.where(rows == SUB - 1, 0.0, pltpu.roll(value, SUB - 1, 0)) for value in u[comp])
                return sub(ahead, u[comp])

            def step_y(comp):
                ahead = tuple(jnp.where(lanes == ny - 1, 0.0, pltpu.roll(value, ny - 1, 1)) for value in u[comp])
                return sub(ahead, u[comp])

            shx = tuple(table_ref[SHX + part, cut] for part in parts)
            shy = tuple(table_ref[SHY + part, cut] for part in parts)
            h = (
                sub(cmul(shy, step_y(2)), cmul(shz, step_z(1))),
                sub(cmul(shz, step_z(0)), cmul(shx, step_x(2))),
                sub(cmul(shx, step_x(1)), cmul(shy, step_y(0))),
            )
            for comp in range(3):
                for part in parts:
                    h_ref[part, b, comp, z, cut] = h[comp][part]
            packed = packed_ref[z, cut]
            for slot, value in enumerate((h[2], h[0])):
                for part in parts:
                    row = packed_row(slot, part, b, vectors)
                    packed = jnp.where(lanes == row, pltpu.roll(value[part], (row + 1) % ny, 1), packed)
            packed_ref[z, cut] = packed

    @pl.loop(0, nz - 1)
    def _(z):
        for b in range(vectors):
            magnetic(b, z, False)

    for b in range(vectors):
        magnetic(b, nz - 1, True)


def turn_face(coeffs_ref, direction, raw_ref, face_ref):
    inside = has_neighbour(direction, 1)
    vectors = raw_ref.shape[1]
    for slot in range(2):
        old = [(raw_ref[0, a, slot] * inside, raw_ref[1, a, slot] * inside) for a in range(vectors)]
        for b in range(vectors):
            new = rotated(coeffs_ref, old, b)
            for part in range(2):
                face_ref[part, b, slot] = new[part]


def turn_column(coeffs_ref, raw_ref, rows_ref):
    vectors = coeffs_ref.shape[1]
    inside = has_neighbour(2, 1)
    both = 2 * vectors
    shape = (both, raw_ref.shape[1])
    which = lax.broadcasted_iota(jnp.int32, shape, 0)
    turned = [jnp.zeros(shape, jnp.float32)] * 2
    for part in range(2):
        for a in range(vectors):
            column = jnp.zeros(shape, jnp.float32)
            for b in range(vectors):
                first, second = coeffs_ref[0, a, b] * inside, coeffs_ref[1, a, b] * inside
                if part:
                    first, second = -second, first
                column = jnp.where(which == b, first, column)
                column = jnp.where(which == vectors + b, second, column)
            for slot in range(2):
                row = packed_row(slot, part, a, vectors)
                turned[slot] = turned[slot] + column * raw_ref[row:row + 1]
    for slot in range(2):
        rows_ref[slot * both:(slot + 1) * both] = turned[slot]


def lane_to_last(values, slot, part, b, vectors):
    ny = values.shape[-1]
    lanes = lax.broadcasted_iota(jnp.int32, values.shape, 1)
    row = packed_row(slot, part, b, vectors)
    return jnp.where(lanes == ny - 1, pltpu.roll(values, ny - 1 - row, 1), 0.0)


def with_halos(h, b, z, cut, nx, xadd_ref, yadd_ref):
    vectors = xadd_ref.shape[1]
    column = yadd_ref[z, cut]
    hx = tuple(h[0][part] + lane_to_last(column, 1, part, b, vectors) for part in range(2))
    hz = tuple(h[2][part] + lane_to_last(column, 0, part, b, vectors) for part in range(2))
    hy = h[1]
    if cut.stop == nx:
        rows = lax.broadcasted_iota(jnp.int32, column.shape, 0)

        def row_of(slot):
            return tuple(
                jnp.where(rows == SUB - 1, xadd_ref[part, b, slot, pl.ds(z, 1)], 0.0) for part in range(2)
            )

        hy, hz = add(hy, row_of(0)), add(hz, row_of(1))
    return hx, hy, hz


def slab_kernel(
    pml_ref, coeffs_ref, basis_ref, h_in, packed_in, raw_xf_ref, raw_yf_ref,
    h_ref, packed_ref, xf_ref, yt_ref, xadd_ref, yadd_ref, hxf_ref, zf_ref,
):
    del h_in, packed_in
    _, vectors, _, nz, nx, ny = basis_ref.shape
    parts = range(2)
    cells = nz * nx
    both = 2 * vectors
    turn_face(coeffs_ref, 1, raw_xf_ref, xf_ref)
    turn_column(coeffs_ref, raw_yf_ref, yt_ref)
    shx = axis_stretch(pml_ref, 1, nx, one_place(1, nx, nx - 1, (1, ny)) + 0.5)
    shy = axis_stretch(pml_ref, 2, ny, one_place(2, ny, ny - 1, (1, cells)) + 0.5)
    for b in range(vectors):
        for slot in range(2):
            value = cmul(shx, tuple(xf_ref[part, b, 1 - slot] for part in parts))
            for part in parts:
                xadd_ref[part, b, slot] = value[part] if slot else -value[part]
    added = []
    for slot in range(2):
        value = cmul(shy, (yt_ref[slot * both:slot * both + vectors], yt_ref[slot * both + vectors:(slot + 1) * both]))
        added += [part if slot else -part for part in value]
    rest = jnp.zeros((ny - 2 * both, cells), jnp.float32)
    yadd_ref[...] = jnp.concatenate(added + [rest], axis=0).T.reshape(nz, nx, ny)
    packed_ref[...] = packed_ref[...] + yadd_ref[...]
    last = nz - 1
    lower = jnp.full((SUB, ny), lax.axis_index(AXES[0]), jnp.int32) == 0
    lanes = lax.broadcasted_iota(jnp.int32, (nz, ny), 1)
    corner = packed_ref[:, nx - 1, :]
    for b in range(vectors):
        for part in parts:
            row = packed_row(0, part, b, vectors)
            edge = pltpu.roll(xadd_ref[part, b, 1], (row + 1) % ny, 1)
            corner = corner + jnp.where(lanes == row, edge, 0.0)
    packed_ref[:, nx - 1, :] = corner
    for b in range(vectors):
        for part in parts:
            hxf_ref[part, b, 0] = h_ref[part, b, 1, :, nx - 1, :] + xadd_ref[part, b, 0]
            hxf_ref[part, b, 1] = (
                h_ref[part, b, 2, :, nx - 1, :] + xadd_ref[part, b, 1]
                + lane_to_last(yadd_ref[:, nx - 1, :], 0, part, b, vectors)
            )
        for cut in tiles_of(nx):
            h = [field_of(h_ref, b, comp, last, cut) for comp in range(3)]
            h = with_halos(h, b, last, cut, nx, xadd_ref, yadd_ref)
            for part in parts:
                for comp in range(3):
                    h_ref[part, b, comp, last, cut] = h[comp][part]
                for comp in range(2):
                    zf_ref[part, b, comp, cut] = jnp.where(lower, h[comp][part], basis_ref[part, b, comp, 0, cut])


def plane_step(b, z, before, sums, basis_ref, loss_ref, table_ref, sz_ref, h_ref, image_ref, halos=None):
    _, vectors, _, _, nx, ny = basis_ref.shape
    rows = lax.broadcasted_iota(jnp.int32, (SUB, ny), 0)
    lanes = lax.broadcasted_iota(jnp.int32, (SUB, ny), 1)
    parts = range(2)
    cuts = tiles_of(nx)
    sez = tuple(sz_ref[part, pl.ds(z, 1)] for part in parts)
    fields = []
    for cut in cuts:
        h = [field_of(h_ref, b, comp, z, cut) for comp in range(3)]
        if halos is not None:
            h = with_halos(h, b, z, cut, nx, *halos)
            for comp in (1, 2):
                for part in parts:
                    h_ref[part, b, comp, z, cut] = h[comp][part]
        fields.append(h)
    sums = list(sums)
    for t, cut in enumerate(cuts):
        hx, hy, hz = fields[t]

        def back_x(comp):
            here = fields[t][comp]
            if t:
                past = field_of(h_ref, b, comp, z, slice(cut.start - 1, cut.stop - 1))
            else:
                past = tuple(jnp.where(rows == 0, 0.0, pltpu.roll(value, 1, 0)) for value in here)
            return sub(here, past)

        def back_y(value):
            return sub(value, tuple(jnp.where(lanes == 0, 0.0, pltpu.roll(part, 1, 1)) for part in value))

        sex = tuple(table_ref[SEX + part, cut] for part in parts)
        sey = tuple(table_ref[SEY + part, cut] for part in parts)
        bxy, bxz = (cmul(sex, back_x(comp)) for comp in (1, 2))
        byz, byx = (cmul(sey, back_y(value)) for value in (hz, hx))
        bzx, bzy = (cmul(sez, sub(value, past)) for value, past in zip((hx, hy), before[t]))
        curl = (sub(byz, bzy), sub(bzx, bxz), sub(bxy, byx))
        w = [add(curl[comp], field_of(loss_ref, b, comp, z, cut)) for comp in range(3)]
        for comp in range(3):
            for part in parts:
                image_ref[part, b, comp, z, cut] = w[comp][part]
        for a in range(vectors):
            total = sums[a]
            for comp in range(3):
                total = add(total, cmul(field_of(basis_ref, a, comp, z, cut), w[comp]))
            sums[a] = total
    return [(h[0], h[1]) for h in fields], sums


def inner_kernel(
    basis_ref, loss_ref, table_ref, sz_ref, h_in, xadd_ref, yadd_ref,
    h_ref, image_ref, acc_ref, before_ref, basis_hbm, sem,
):
    del h_in
    _, vectors, _, nz, nx, ny = basis_ref.shape
    keep = pltpu.make_async_copy(basis_ref, basis_hbm, sem)
    keep.start()
    cuts = tiles_of(nx)
    acc_ref[...] = jnp.zeros(acc_ref.shape, jnp.float32)
    before_ref[...] = jnp.zeros(before_ref.shape, jnp.float32)

    @pl.loop(0, nz - 1)
    def _(z):
        for b in range(vectors):
            before = [
                tuple(tuple(before_ref[part, b, slot, cut] for part in range(2)) for slot in range(2)) for cut in cuts
            ]
            sums = [(acc_ref[b, a], acc_ref[b, vectors + a]) for a in range(vectors)]
            before, sums = plane_step(
                b, z, before, sums, basis_ref, loss_ref, table_ref, sz_ref, h_ref, image_ref, (xadd_ref, yadd_ref)
            )
            for part in range(2):
                for a in range(vectors):
                    acc_ref[b, part * vectors + a] = sums[a][part]
                for t, cut in enumerate(cuts):
                    for slot in range(2):
                        before_ref[part, b, slot, cut] = before[t][slot][part]

    keep.wait()


def last_plane_kernel(sz_ref, zf_ref, h_in, packed_in, hxf_in, h_ref, hxf_ref, hyf_ref):
    del h_in, hxf_in
    _, vectors, _, nz, nx, ny = h_ref.shape
    parts = range(2)
    last = nz - 1
    lanes = lax.broadcasted_iota(jnp.int32, (SUB, ny), 1)
    shz = tuple(sz_ref[2 + part, last:] * has_neighbour(0, 1) for part in parts)
    packed = [packed_in[last, cut] for cut in tiles_of(nx)]
    for b in range(vectors):
        for t, cut in enumerate(tiles_of(nx)):
            ex, ey = (tuple(zf_ref[part, b, slot, cut] for part in parts) for slot in range(2))
            more = (tuple(-value for value in cmul(shz, ey)), cmul(shz, ex))
            for part in parts:
                for comp in range(2):
                    h_ref[part, b, comp, last, cut] = h_ref[part, b, comp, last, cut] + more[comp][part]
                row = packed_row(1, part, b, vectors)
                edge = pltpu.roll(more[0][part], (row + 1) % ny, 1)
                packed[t] = packed[t] + jnp.where(lanes == row, edge, 0.0)
                if cut.stop == nx:
                    hxf_ref[part, b, 0, last:] = hxf_ref[part, b, 0, last:] + more[1][part][SUB - 1:]
    inner = packed_in[:last].reshape(last * nx, ny)
    hyf_ref[...] = jnp.concatenate([inner] + packed, axis=0).T[:hyf_ref.shape[0]]


def outer_kernel(
    pml_ref, basis_ref, loss_ref, table_ref, sz_ref, h_ref, zf_ref, xf_ref, yt_ref, hxf_ref, hyf_ref,
    image_in, acc_ref, before_ref, image_ref, gram_ref,
):
    del image_in
    _, vectors, _, nz, nx, ny = basis_ref.shape
    parts = range(2)
    cuts = tiles_of(nx)
    under = axis_stretch(pml_ref, 0, nz, one_place(0, nz, -1, (1, ny)) + 0.5)
    sez = tuple(sz_ref[part, 0:1] * has_neighbour(0, -1) for part in parts)
    sx_next = axis_stretch(pml_ref, 1, nx, one_place(1, nx, nx, (1, ny)))
    sy_next = axis_stretch(pml_ref, 2, ny, one_place(2, ny, ny, (1, nz * nx)))
    both = 2 * vectors
    ends = [
        cmul(sy_next, (yt_ref[slot * both:slot * both + vectors], yt_ref[slot * both + vectors:(slot + 1) * both]))
        for slot in range(2)
    ]
    totals = {}
    for b in range(vectors):

        def tile_of(ref, slot, cut, b=b):
            return tuple(ref[part, b, slot, cut] for part in parts)

        before = [tuple(tile_of(before_ref, slot, cut) for slot in range(2)) for cut in cuts]
        sums = [(acc_ref[b, a], acc_ref[b, vectors + a]) for a in range(vectors)]
        _, sums = plane_step(
            b, nz - 1, before, sums, basis_ref, loss_ref, table_ref, sz_ref, h_ref, image_ref
        )
        for cut in cuts:
            ex, ey = (field_of(basis_ref, b, comp, 0, cut) for comp in range(2))
            hx = sub(tile_of(zf_ref, 0, cut), cmul(under, ey))
            hy = add(tile_of(zf_ref, 1, cut), cmul(under, ex))
            more = (cmul(sez, hy), cmul(sez, hx))
            for part in parts:
                image_ref[part, b, 0, 0, cut] = image_ref[part, b, 0, 0, cut] + more[0][part]
                image_ref[part, b, 1, 0, cut] = image_ref[part, b, 1, 0, cut] - more[1][part]
            for a in range(vectors):
                ex, ey = (field_of(basis_ref, a, comp, 0, cut) for comp in range(2))
                sums[a] = add(sums[a], sub(cmul(ex, more[0]), cmul(ey, more[1])))
        h_y = tuple(hxf_ref[part, b, 0] for part in parts)
        h_z = tuple(hxf_ref[part, b, 1] for part in parts)
        for a in range(vectors):
            over = cmul(tuple(xf_ref[part, a, 0] for part in parts), h_z)
            over = sub(over, cmul(tuple(xf_ref[part, a, 1] for part in parts), h_y))
            over = cmul(sx_next, over)
            for row in range(0, nz, SUB):
                sums[a] = add(sums[a], tuple(part[row:row + SUB] for part in over))
        over = None
        for slot in range(2):
            h = tuple(hyf_ref[packed_row(slot, part, b, vectors)][None] for part in parts)
            term = cmul(ends[slot], h)
            over = term if over is None else sub(term, over)
        for a in range(vectors):
            for part in parts:
                side = jnp.concatenate([over[part][a:a + 1], jnp.zeros((SUB - 1, ny), jnp.float32)], axis=0)
                totals[part, a, b] = sums[a][part] + side
    everywhere = 3.0 * nz * nx * ny
    for axis in AXES:
        everywhere = everywhere * lax.axis_size(axis)
    for part in parts:
        stack = jnp.concatenate([totals[part, a, b] for a in range(vectors) for b in range(vectors)], axis=0)
        row = jnp.sum(stack.T, axis=0, keepdims=True) * (1.0 / everywhere)
        for device in range(gram_ref.shape[0]):
            gram_ref[device, part:part + 1] = row


def tree_sum(values):
    while len(values) > 1:
        pairs = [values[place] + values[place + 1] for place in range(0, len(values) - 1, 2)]
        values = pairs + ([values[-1]] if len(values) % 2 else [])
    return values[0]


def share_kernel(rows_ref, next_ref):
    total = tree_sum([rows_ref[device] for device in range(rows_ref.shape[0])])
    for device in range(next_ref.shape[0]):
        next_ref[device] = total


def gather_kernel(rows_ref, gram_ref):
    _, vectors, _ = gram_ref.shape
    total = tree_sum([rows_ref[device] for device in range(rows_ref.shape[0])])
    count = total.shape[1]
    reach = 1
    while reach < SUB:
        total = total + pltpu.roll(total, count - reach, 1)
        reach *= 2
    lanes = lax.broadcasted_iota(jnp.int32, total.shape, 1)
    for a in range(vectors):
        matrix_row = total
        for b in range(vectors):
            place = (a * vectors + b) * SUB
            matrix_row = jnp.where(lanes == b, pltpu.roll(total, (count + b - place) % count, 1), matrix_row)
        for part in range(2):
            gram_ref[part, a:a + 1] = matrix_row[part:part + 1, :vectors]


def rim_kernel(
    pml_ref, ritz_ref, basis_ref, image_ref, hxf_ref, hyf_ref, residual_hbm, residual_ref, packed_ref, sems
):
    _, vectors, _, nz, nx, ny = basis_ref.shape
    plane = (nx, ny)
    rows = lax.broadcasted_iota(jnp.int32, plane, 0)
    lanes = lax.broadcasted_iota(jnp.int32, plane, 1)
    sex = axis_stretch(pml_ref, 1, nx, one_place(1, nx, 0, (1, ny)))
    sey = axis_stretch(pml_ref, 2, ny, one_place(2, ny, 0, plane))
    none = jnp.zeros(plane, jnp.float32)
    sex = tuple(jnp.where(rows == 0, part * has_neighbour(1, -1), none) for part in sex)
    sey = tuple(jnp.where(lanes == 0, part * has_neighbour(2, -1), none) for part in sey)
    rest = jnp.zeros((ny - hyf_ref.shape[0], nz * nx), jnp.float32)
    packed_ref[...] = jnp.concatenate([hyf_ref[...], rest], axis=0).T.reshape(nz, nx, ny)

    def kept(z):
        return pltpu.make_async_copy(residual_ref.at[:, :, :, z], residual_hbm.at[:, :, :, z], sems.at[z])

    @pl.loop(0, nz)
    def _(z):
        packed = packed_ref[z]
        for b in range(vectors):

            def column(slot, b=b):
                return tuple(
                    pltpu.roll(packed, (ny - packed_row(slot, part, b, vectors)) % ny, 1) for part in range(2)
                )

            def row(slot, b=b):
                return tuple(hxf_ref[part, b, slot, pl.ds(z, 1)] for part in range(2))

            factor = (ritz_ref[0, b], ritz_ref[1, b])
            left = []
            for comp in range(3):
                u = (basis_ref[0, b, comp, z], basis_ref[1, b, comp, z])
                w = (image_ref[0, b, comp, z], image_ref[1, b, comp, z])
                left.append(sub(w, cmul(factor, u)))
            left[0] = sub(left[0], cmul(sey, column(0)))
            left[2] = add(left[2], cmul(sey, column(1)))
            left[1] = add(left[1], cmul(sex, row(1)))
            left[2] = sub(left[2], cmul(sex, row(0)))
            for comp in range(3):
                for part in range(2):
                    residual_ref[part, b, comp, z] = left[comp][part]
        kept(z).start()

    @pl.loop(0, nz)
    def _(z):
        kept(z).wait()


def body(fields, material, pml_width, eps_real, eps_loss, coeffs, ritz):
    _, vectors, _, nz, nx, ny = fields.shape
    f32 = lambda *shape: jax.ShapeDtypeStruct(shape, jnp.float32)
    scratch = lambda *shape: pltpu.VMEM(shape, jnp.float32)
    params = pltpu.CompilerParams(vmem_limit_bytes=40 * 1024 * 1024)
    whole = f32(*fields.shape)
    zf_shape = (2, vectors, 2, nx, ny)
    xf_shape = (2, vectors, 2, nz, ny)
    yf_shape = (4 * vectors, nz * nx)
    near, xf, yf = pl.pallas_call(
        face_kernel,
        out_shape=(whole, f32(*xf_shape), f32(*yf_shape)),
        in_specs=[HBM],
        out_specs=(VMEM,) * 3,
        scratch_shapes=[pltpu.SemaphoreType.DMA((2, 3))],
        compiler_params=params,
        name="take_faces",
    )(pltpu.with_memory_space_constraint(fields, pltpu.HBM))
    xf = passed_round(xf, "gx", -1)
    yf = passed_round(yf, "gy", -1)
    cells = fields.size // 6 // vectors

    def cost(flops, passes):
        return pl.CostEstimate(flops=flops * cells, bytes_accessed=passes * 4 * fields.size, transcendentals=0)

    planes = f32(nz, nx, ny)
    face = f32(*xf_shape)
    basis, loss, h, packed, table, sz = pl.pallas_call(
        prepare_kernel,
        out_shape=(whole, whole, whole, planes, f32(8, nx, ny), f32(4, nz, ny)),
        in_specs=[SMEM] * 4 + [VMEM] * 2,
        out_specs=(VMEM,) * 6,
        compiler_params=params,
        cost_estimate=cost(800, 4),
        name="prepare",
    )(pml_width, eps_real, eps_loss, coeffs, near, material)
    h, packed, xf, yt, xadd, yadd, hxf, zf = pl.pallas_call(
        slab_kernel,
        out_shape=(whole, planes, face, f32(*yf_shape), face, planes, face, f32(*zf_shape)),
        in_specs=[SMEM] * 2 + [VMEM] * 5,
        out_specs=(VMEM,) * 8,
        input_output_aliases={3: 0, 4: 1},
        compiler_params=params,
        name="slab_face",
    )(pml_width, coeffs, basis, h, packed, xf, yf)
    zf = passed_round(zf, "gz", 1)
    h, image, acc, before, basis_new = pl.pallas_call(
        inner_kernel,
        out_shape=(whole, whole, f32(vectors, 2 * vectors, SUB, ny), f32(*zf_shape), whole),
        in_specs=[VMEM] * 7,
        out_specs=(VMEM,) * 4 + (HBM,),
        scratch_shapes=[pltpu.SemaphoreType.DMA],
        input_output_aliases={4: 0},
        compiler_params=params,
        cost_estimate=cost(800, 2),
        name="apply_inner",
    )(basis, loss, table, sz, h, xadd, yadd)
    h, hxf, hyf = pl.pallas_call(
        last_plane_kernel,
        out_shape=(whole, face, f32(*yf_shape)),
        in_specs=[VMEM] * 5,
        out_specs=(VMEM,) * 3,
        input_output_aliases={2: 0, 4: 1},
        compiler_params=params,
        name="last_plane",
    )(sz, zf, h, packed, hxf)
    first, second = lax.axis_size("gx"), lax.axis_size("gy") * lax.axis_size("gz")
    image, gram = pl.pallas_call(
        outer_kernel,
        out_shape=(whole, f32(first, 2, ny)),
        in_specs=[SMEM] + [VMEM] * 13,
        out_specs=(VMEM,) * 2,
        input_output_aliases={11: 0},
        compiler_params=params,
        cost_estimate=cost(300, 1),
        name="apply_outer",
    )(pml_width, basis, loss, table, sz, h, zf, xf, yt, hxf, hyf, image, acc, before)
    gram, hxf, hyf = lax.optimization_barrier((gram, hxf, hyf))
    rows = lax.all_to_all(gram, "gx", 0, 0)
    from_y = passed_round(hyf, "gy", 1)
    from_x = passed_round(hxf, "gx", 1)
    rows, from_y = lax.optimization_barrier((rows, from_y))
    gram = pl.pallas_call(
        share_kernel,
        out_shape=f32(second, 2, ny),
        in_specs=[VMEM],
        out_specs=VMEM,
        compiler_params=params,
        name="share_rows",
    )(rows)
    rows = lax.all_to_all(gram, ("gy", "gz"), 0, 0)
    residual = pl.pallas_call(
        rim_kernel,
        out_shape=whole,
        in_specs=[SMEM] * 2 + [VMEM] * 4,
        out_specs=HBM,
        scratch_shapes=[scratch(*fields.shape), scratch(nz, nx, ny), pltpu.SemaphoreType.DMA((nz,))],
        compiler_params=params,
        cost_estimate=cost(200, 3),
        name="add_rims",
    )(pml_width, ritz, basis, image, from_x, from_y)
    rows, residual = lax.optimization_barrier((rows, residual))
    gram = pl.pallas_call(
        gather_kernel,
        out_shape=f32(2, vectors, vectors),
        in_specs=[VMEM],
        out_specs=VMEM,
        compiler_params=params,
        name="sum_rows",
    )(rows)
    return basis_new, residual, gram


def solution(mesh):
    in_specs = (P(None, None, None, "gz", "gx", "gy"), P("gz", "gx", "gy"), P(), P(), P(), P(), P())
    out_specs = (P(None, None, None, "gz", "gx", "gy"), P(None, None, None, "gz", "gx", "gy"), P())
    return jax.shard_map(body, mesh=mesh, in_specs=in_specs, out_specs=out_specs, check_vma=False)
```

```python
import functools

import jax
import jax.numpy as jnp
from jax import lax
from jax.experimental import pallas as pl
from jax.experimental.pallas import tpu as pltpu
from jax.sharding import PartitionSpec as P

OMEGA_SQ = 0.36
SIGMA_TOP = 3.0
BOUNDS = ((4, 5), (0, 1), (2, 3))
AXES = ("gz", "gx", "gy")

VMEM = pl.BlockSpec(memory_space=pltpu.VMEM)
SMEM = pl.BlockSpec(memory_space=pltpu.SMEM)
HBM = pl.BlockSpec(memory_space=pltpu.HBM)


def passed_round(value, axis, steps):
    count = lax.axis_size(axis)
    return lax.ppermute(value, axis, [(source, (source + steps) % count) for source in range(count)])


def swapped_with_neighbours(value, axis):
    count = lax.axis_size(axis)
    near = [(source, source ^ 1) for source in range(count)]
    far = [(source, min(max(((source + 1) ^ 1) - 1, 0), count - 1)) for source in range(count)]
    return lax.ppermute(value, axis, near), lax.ppermute(value, axis, far)


def inverse_stretch(places, length, low_width, high_width):
    inside_depth = jnp.clip((low_width - places) / low_width, 0.0, 1.0) + jnp.clip(
        (places + 1.0 - length + high_width) / high_width, 0.0, 1.0
    )
    absorb = SIGMA_TOP * inside_depth * inside_depth
    scaled = 1.0 / (1.0 + absorb * absorb)
    return scaled, -absorb * scaled


def cmul(left, right):
    return (left[0] * right[0] - left[1] * right[1], left[0] * right[1] + left[1] * right[0])


def add(left, right):
    return (left[0] + right[0], left[1] + right[1])


def sub(left, right):
    return (left[0] - right[0], left[1] - right[1])


def axis_stretch(pml_ref, direction, count, places):
    total = count * lax.axis_size(AXES[direction])
    low_slot, high_slot = BOUNDS[direction]
    low = jnp.full(places.shape, pml_ref[low_slot], jnp.int32).astype(jnp.float32)
    high = jnp.full(places.shape, pml_ref[high_slot], jnp.int32).astype(jnp.float32)
    return inverse_stretch(places, jnp.float32(total), low, high)


def local_places(direction, count, shape, dim):
    start = lax.axis_index(AXES[direction]) * count
    return (lax.broadcasted_iota(jnp.int32, shape, dim) + start).astype(jnp.float32)


def one_place(direction, count, offset, shape):
    start = lax.axis_index(AXES[direction]) * count + offset
    return jnp.full(shape, start, jnp.int32).astype(jnp.float32)


def packed_row(slot, part, vector, vectors):
    return (slot * 2 + part) * vectors + vector


def has_neighbour(direction, steps):
    place = lax.axis_index(AXES[direction]) + steps
    inside = (place >= 0) & (place < lax.axis_size(AXES[direction]))
    return jnp.where(inside, 1.0, 0.0).astype(jnp.float32)


def face_kernel(fields_hbm, fields_ref, xf_ref, yf_ref, sems):
    _, vectors, _, nz, nx, ny = fields_ref.shape
    lanes = lax.broadcasted_iota(jnp.int32, (nx, ny), 1)
    copies = [
        pltpu.make_async_copy(fields_hbm.at[part, :, comp], fields_ref.at[part, :, comp], sems.at[part, comp])
        for comp in (0, 2, 1) for part in range(2)
    ]
    for copy in copies:
        copy.start()
    packed = [jnp.zeros((nx, ny), jnp.float32)] * nz
    for place, comp in enumerate((0, 2)):
        for part in range(2):
            copies[2 * place + part].wait()
            for a in range(vectors):
                row = packed_row(comp // 2, part, a, vectors)
                for z in range(nz):
                    value = fields_ref[part, a, comp, z]
                    packed[z] = jnp.where(lanes == row, pltpu.roll(value, row, 1) if row else value, packed[z])
    turned = jnp.concatenate(packed, axis=0).T
    yf_ref[...] = turned[:yf_ref.shape[0]]
    for part in range(2):
        for a in range(vectors):
            xf_ref[part, a, 1] = fields_ref[part, a, 2, :, 0, :]
    for part in range(2):
        copies[4 + part].wait()
        for a in range(vectors):
            xf_ref[part, a, 0] = fields_ref[part, a, 1, :, 0, :]


def rotated(coeffs_ref, old, b):
    new = None
    for a, value in enumerate(old):
        term = cmul((coeffs_ref[0, a, b], coeffs_ref[1, a, b]), value)
        new = term if new is None else add(new, term)
    return new


SUB = 8
SHX, SEX, SHY, SEY = range(0, 8, 2)


def field_of(ref, b, comp, z, cut):
    return tuple(ref[part, b, comp, z, cut] for part in range(2))


def tiles_of(nx):
    return [slice(SUB * t, SUB * (t + 1)) for t in range(nx // SUB)]


def prepare_kernel(
    pml_ref, eps_real_ref, eps_loss_ref, coeffs_ref, fields_ref, material_ref,
    basis_ref, loss_ref, h_ref, packed_ref, table_ref, sz_ref,
):
    _, vectors, _, nz, nx, ny = fields_ref.shape
    plane = (nx, ny)
    parts = range(2)
    for slot, direction, half, count, dim in (
        (SHX, 1, 0.5, nx, 0), (SEX, 1, 0.0, nx, 0), (SHY, 2, 0.5, ny, 1), (SEY, 2, 0.0, ny, 1),
    ):
        values = axis_stretch(pml_ref, direction, count, local_places(direction, count, plane, dim) + half)
        for part in parts:
            table_ref[slot + part] = values[part]
    for slot, half in ((0, 0.0), (2, 0.5)):
        values = axis_stretch(pml_ref, 0, nz, local_places(0, nz, (nz, ny), 0) + half)
        for part in parts:
            sz_ref[slot + part] = values[part]

    @pl.loop(0, nz)
    def _(z):
        material = material_ref[z]
        eps = []
        for source in (eps_real_ref, eps_loss_ref):
            value = jnp.zeros(plane, jnp.float32)
            for number in range(source.shape[0]):
                value = jnp.where(material == number, -OMEGA_SQ * source[number], value)
            eps.append(value)
        for comp in range(3):
            old = [(fields_ref[0, a, comp, z], fields_ref[1, a, comp, z]) for a in range(vectors)]
            for b in range(vectors):
                new = rotated(coeffs_ref, old, b)
                loss = cmul(eps, new)
                for part in parts:
                    basis_ref[part, b, comp, z] = new[part]
                    loss_ref[part, b, comp, z] = loss[part]
        packed_ref[z] = jnp.zeros(plane, jnp.float32)

    tile = (SUB, ny)
    rows = lax.broadcasted_iota(jnp.int32, tile, 0)
    lanes = lax.broadcasted_iota(jnp.int32, tile, 1)
    cuts = tiles_of(nx)

    def magnetic(b, z, last):
        shz = tuple(sz_ref[2 + part, pl.ds(z, 1)] for part in parts)
        for cut in cuts:
            u = [field_of(basis_ref, b, comp, z, cut) for comp in range(3)]

            def step_z(comp):
                if last:
                    return tuple(-value for value in u[comp])
                return sub(field_of(basis_ref, b, comp, z + 1, cut), u[comp])

            def step_x(comp):
                if cut.stop < nx:
                    ahead = field_of(basis_ref, b, comp, z, slice(cut.start + 1, cut.stop + 1))
                else:
                    ahead = tuple(jnp.where(rows == SUB - 1, 0.0, pltpu.roll(value, SUB - 1, 0)) for value in u[comp])
                return sub(ahead, u[comp])

            def step_y(comp):
                ahead = tuple(jnp.where(lanes == ny - 1, 0.0, pltpu.roll(value, ny - 1, 1)) for value in u[comp])
                return sub(ahead, u[comp])

            shx = tuple(table_ref[SHX + part, cut] for part in parts)
            shy = tuple(table_ref[SHY + part, cut] for part in parts)
            h = (
                sub(cmul(shy, step_y(2)), cmul(shz, step_z(1))),
                sub(cmul(shz, step_z(0)), cmul(shx, step_x(2))),
                sub(cmul(shx, step_x(1)), cmul(shy, step_y(0))),
            )
            for comp in range(3):
                for part in parts:
                    h_ref[part, b, comp, z, cut] = h[comp][part]
            packed = packed_ref[z, cut]
            for slot, value in enumerate((h[2], h[0])):
                for part in parts:
                    row = packed_row(slot, part, b, vectors)
                    packed = jnp.where(lanes == row, pltpu.roll(value[part], (row + 1) % ny, 1), packed)
            packed_ref[z, cut] = packed

    @pl.loop(0, nz - 1)
    def _(z):
        for b in range(vectors):
            magnetic(b, z, False)

    for b in range(vectors):
        magnetic(b, nz - 1, True)


def pair_weights(steps):
    place = lax.axis_index(AXES[1])
    even = jnp.where(lax.rem(place, 2) == 0, 1.0, 0.0).astype(jnp.float32)
    inside = has_neighbour(1, steps)
    return (even * inside, (1.0 - even) * inside) if steps > 0 else ((1.0 - even) * inside, even * inside)


def turn_face(coeffs_ref, near_ref, far_ref, face_ref):
    near, far = pair_weights(1)
    vectors = near_ref.shape[1]
    for slot in range(2):
        old = [
            tuple(near_ref[part, a, slot] * near + far_ref[part, a, slot] * far for part in range(2))
            for a in range(vectors)
        ]
        for b in range(vectors):
            new = rotated(coeffs_ref, old, b)
            for part in range(2):
                face_ref[part, b, slot] = new[part]


def turn_column(coeffs_ref, raw_ref, rows_ref):
    vectors = coeffs_ref.shape[1]
    inside = has_neighbour(2, 1)
    both = 2 * vectors
    shape = (both, raw_ref.shape[1])
    which = lax.broadcasted_iota(jnp.int32, shape, 0)
    turned = [jnp.zeros(shape, jnp.float32)] * 2
    for part in range(2):
        for a in range(vectors):
            column = jnp.zeros(shape, jnp.float32)
            for b in range(vectors):
                first, second = coeffs_ref[0, a, b] * inside, coeffs_ref[1, a, b] * inside
                if part:
                    first, second = -second, first
                column = jnp.where(which == b, first, column)
                column = jnp.where(which == vectors + b, second, column)
            for slot in range(2):
                row = packed_row(slot, part, a, vectors)
                turned[slot] = turned[slot] + column * raw_ref[row:row + 1]
    for slot in range(2):
        rows_ref[slot * both:(slot + 1) * both] = turned[slot]


def lane_to_last(values, slot, part, b, vectors):
    ny = values.shape[-1]
    lanes = lax.broadcasted_iota(jnp.int32, values.shape, 1)
    row = packed_row(slot, part, b, vectors)
    return jnp.where(lanes == ny - 1, pltpu.roll(values, ny - 1 - row, 1), 0.0)


def with_halos(h, b, z, cut, nx, xadd_ref, yadd_ref):
    vectors = xadd_ref.shape[1]
    column = yadd_ref[z, cut]
    hx = tuple(h[0][part] + lane_to_last(column, 1, part, b, vectors) for part in range(2))
    hz = tuple(h[2][part] + lane_to_last(column, 0, part, b, vectors) for part in range(2))
    hy = h[1]
    if cut.stop == nx:
        rows = lax.broadcasted_iota(jnp.int32, column.shape, 0)

        def row_of(slot):
            return tuple(
                jnp.where(rows == SUB - 1, xadd_ref[part, b, slot, pl.ds(z, 1)], 0.0) for part in range(2)
            )

        hy, hz = add(hy, row_of(0)), add(hz, row_of(1))
    return hx, hy, hz


def slab_kernel(
    pml_ref, coeffs_ref, basis_ref, h_in, packed_in, near_xf_ref, far_xf_ref, raw_yf_ref,
    h_ref, packed_ref, xf_ref, yt_ref, xadd_ref, yadd_ref, hxf_ref, zf_ref,
):
    del h_in, packed_in
    _, vectors, _, nz, nx, ny = basis_ref.shape
    parts = range(2)
    cells = nz * nx
    both = 2 * vectors
    turn_face(coeffs_ref, near_xf_ref, far_xf_ref, xf_ref)
    turn_column(coeffs_ref, raw_yf_ref, yt_ref)
    shx = axis_stretch(pml_ref, 1, nx, one_place(1, nx, nx - 1, (1, ny)) + 0.5)
    shy = axis_stretch(pml_ref, 2, ny, one_place(2, ny, ny - 1, (1, cells)) + 0.5)
    for b in range(vectors):
        for slot in range(2):
            value = cmul(shx, tuple(xf_ref[part, b, 1 - slot] for part in parts))
            for part in parts:
                xadd_ref[part, b, slot] = value[part] if slot else -value[part]
    added = []
    for slot in range(2):
        value = cmul(shy, (yt_ref[slot * both:slot * both + vectors], yt_ref[slot * both + vectors:(slot + 1) * both]))
        added += [part if slot else -part for part in value]
    rest = jnp.zeros((ny - 2 * both, cells), jnp.float32)
    yadd_ref[...] = jnp.concatenate(added + [rest], axis=0).T.reshape(nz, nx, ny)
    packed_ref[...] = packed_ref[...] + yadd_ref[...]
    last = nz - 1
    lower = jnp.full((SUB, ny), lax.axis_index(AXES[0]), jnp.int32) == 0
    lanes = lax.broadcasted_iota(jnp.int32, (nz, ny), 1)
    corner = packed_ref[:, nx - 1, :]
    for b in range(vectors):
        for part in parts:
            row = packed_row(0, part, b, vectors)
            edge = pltpu.roll(xadd_ref[part, b, 1], (row + 1) % ny, 1)
            corner = corner + jnp.where(lanes == row, edge, 0.0)
    packed_ref[:, nx - 1, :] = corner
    for b in range(vectors):
        for part in parts:
            hxf_ref[part, b, 0] = h_ref[part, b, 1, :, nx - 1, :] + xadd_ref[part, b, 0]
            hxf_ref[part, b, 1] = (
                h_ref[part, b, 2, :, nx - 1, :] + xadd_ref[part, b, 1]
                + lane_to_last(yadd_ref[:, nx - 1, :], 0, part, b, vectors)
            )
        for cut in tiles_of(nx):
            h = [field_of(h_ref, b, comp, last, cut) for comp in range(3)]
            h = with_halos(h, b, last, cut, nx, xadd_ref, yadd_ref)
            for part in parts:
                for comp in range(3):
                    h_ref[part, b, comp, last, cut] = h[comp][part]
                for comp in range(2):
                    zf_ref[part, b, comp, cut] = jnp.where(lower, h[comp][part], basis_ref[part, b, comp, 0, cut])


def plane_step(b, z, before, sums, basis_ref, loss_ref, table_ref, sz_ref, h_ref, image_ref, halos=None):
    _, vectors, _, _, nx, ny = basis_ref.shape
    rows = lax.broadcasted_iota(jnp.int32, (SUB, ny), 0)
    lanes = lax.broadcasted_iota(jnp.int32, (SUB, ny), 1)
    parts = range(2)
    cuts = tiles_of(nx)
    sez = tuple(sz_ref[part, pl.ds(z, 1)] for part in parts)
    fields = []
    for cut in cuts:
        h = [field_of(h_ref, b, comp, z, cut) for comp in range(3)]
        if halos is not None:
            h = with_halos(h, b, z, cut, nx, *halos)
            for comp in (1, 2):
                for part in parts:
                    h_ref[part, b, comp, z, cut] = h[comp][part]
        fields.append(h)
    sums = list(sums)
    for t, cut in enumerate(cuts):
        hx, hy, hz = fields[t]

        def back_x(comp):
            here = fields[t][comp]
            if t:
                past = field_of(h_ref, b, comp, z, slice(cut.start - 1, cut.stop - 1))
            else:
                past = tuple(jnp.where(rows == 0, 0.0, pltpu.roll(value, 1, 0)) for value in here)
            return sub(here, past)

        def back_y(value):
            return sub(value, tuple(jnp.where(lanes == 0, 0.0, pltpu.roll(part, 1, 1)) for part in value))

        sex = tuple(table_ref[SEX + part, cut] for part in parts)
        sey = tuple(table_ref[SEY + part, cut] for part in parts)
        bxy, bxz = (cmul(sex, back_x(comp)) for comp in (1, 2))
        byz, byx = (cmul(sey, back_y(value)) for value in (hz, hx))
        bzx, bzy = (cmul(sez, sub(value, past)) for value, past in zip((hx, hy), before[t]))
        curl = (sub(byz, bzy), sub(bzx, bxz), sub(bxy, byx))
        w = [add(curl[comp], field_of(loss_ref, b, comp, z, cut)) for comp in range(3)]
        for comp in range(3):
            for part in parts:
                image_ref[part, b, comp, z, cut] = w[comp][part]
        for a in range(vectors):
            total = sums[a]
            for comp in range(3):
                total = add(total, cmul(field_of(basis_ref, a, comp, z, cut), w[comp]))
            sums[a] = total
    return [(h[0], h[1]) for h in fields], sums


def inner_kernel(
    basis_ref, loss_ref, table_ref, sz_ref, h_in, xadd_ref, yadd_ref,
    h_ref, image_ref, acc_ref, before_ref, basis_hbm, sem,
):
    del h_in
    _, vectors, _, nz, nx, ny = basis_ref.shape
    keep = pltpu.make_async_copy(basis_ref, basis_hbm, sem)
    keep.start()
    cuts = tiles_of(nx)
    acc_ref[...] = jnp.zeros(acc_ref.shape, jnp.float32)
    before_ref[...] = jnp.zeros(before_ref.shape, jnp.float32)

    @pl.loop(0, nz - 1)
    def _(z):
        for b in range(vectors):
            before = [
                tuple(tuple(before_ref[part, b, slot, cut] for part in range(2)) for slot in range(2)) for cut in cuts
            ]
            sums = [(acc_ref[b, a], acc_ref[b, vectors + a]) for a in range(vectors)]
            before, sums = plane_step(
                b, z, before, sums, basis_ref, loss_ref, table_ref, sz_ref, h_ref, image_ref, (xadd_ref, yadd_ref)
            )
            for part in range(2):
                for a in range(vectors):
                    acc_ref[b, part * vectors + a] = sums[a][part]
                for t, cut in enumerate(cuts):
                    for slot in range(2):
                        before_ref[part, b, slot, cut] = before[t][slot][part]

    keep.wait()


def last_plane_kernel(sz_ref, zf_ref, h_in, packed_in, hxf_in, h_ref, hxf_ref, hyf_ref):
    del h_in, hxf_in
    _, vectors, _, nz, nx, ny = h_ref.shape
    parts = range(2)
    last = nz - 1
    lanes = lax.broadcasted_iota(jnp.int32, (SUB, ny), 1)
    shz = tuple(sz_ref[2 + part, last:] * has_neighbour(0, 1) for part in parts)
    packed = [packed_in[last, cut] for cut in tiles_of(nx)]
    for b in range(vectors):
        for t, cut in enumerate(tiles_of(nx)):
            ex, ey = (tuple(zf_ref[part, b, slot, cut] for part in parts) for slot in range(2))
            more = (tuple(-value for value in cmul(shz, ey)), cmul(shz, ex))
            for part in parts:
                for comp in range(2):
                    h_ref[part, b, comp, last, cut] = h_ref[part, b, comp, last, cut] + more[comp][part]
                row = packed_row(1, part, b, vectors)
                edge = pltpu.roll(more[0][part], (row + 1) % ny, 1)
                packed[t] = packed[t] + jnp.where(lanes == row, edge, 0.0)
                if cut.stop == nx:
                    hxf_ref[part, b, 0, last:] = hxf_ref[part, b, 0, last:] + more[1][part][SUB - 1:]
    inner = packed_in[:last].reshape(last * nx, ny)
    hyf_ref[...] = jnp.concatenate([inner] + packed, axis=0).T[:hyf_ref.shape[0]]


def outer_kernel(
    pml_ref, basis_ref, loss_ref, table_ref, sz_ref, h_ref, zf_ref, xf_ref, yt_ref, hxf_ref, hyf_ref,
    image_in, acc_ref, before_ref, image_ref, gram_ref,
):
    del image_in
    _, vectors, _, nz, nx, ny = basis_ref.shape
    parts = range(2)
    cuts = tiles_of(nx)
    under = axis_stretch(pml_ref, 0, nz, one_place(0, nz, -1, (1, ny)) + 0.5)
    sez = tuple(sz_ref[part, 0:1] * has_neighbour(0, -1) for part in parts)
    sx_next = axis_stretch(pml_ref, 1, nx, one_place(1, nx, nx, (1, ny)))
    sy_next = axis_stretch(pml_ref, 2, ny, one_place(2, ny, ny, (1, nz * nx)))
    both = 2 * vectors
    ends = [
        cmul(sy_next, (yt_ref[slot * both:slot * both + vectors], yt_ref[slot * both + vectors:(slot + 1) * both]))
        for slot in range(2)
    ]
    totals = {}
    for b in range(vectors):

        def tile_of(ref, slot, cut, b=b):
            return tuple(ref[part, b, slot, cut] for part in parts)

        before = [tuple(tile_of(before_ref, slot, cut) for slot in range(2)) for cut in cuts]
        sums = [(acc_ref[b, a], acc_ref[b, vectors + a]) for a in range(vectors)]
        _, sums = plane_step(
            b, nz - 1, before, sums, basis_ref, loss_ref, table_ref, sz_ref, h_ref, image_ref
        )
        for cut in cuts:
            ex, ey = (field_of(basis_ref, b, comp, 0, cut) for comp in range(2))
            hx = sub(tile_of(zf_ref, 0, cut), cmul(under, ey))
            hy = add(tile_of(zf_ref, 1, cut), cmul(under, ex))
            more = (cmul(sez, hy), cmul(sez, hx))
            for part in parts:
                image_ref[part, b, 0, 0, cut] = image_ref[part, b, 0, 0, cut] + more[0][part]
                image_ref[part, b, 1, 0, cut] = image_ref[part, b, 1, 0, cut] - more[1][part]
            for a in range(vectors):
                ex, ey = (field_of(basis_ref, a, comp, 0, cut) for comp in range(2))
                sums[a] = add(sums[a], sub(cmul(ex, more[0]), cmul(ey, more[1])))
        h_y = tuple(hxf_ref[part, b, 0] for part in parts)
        h_z = tuple(hxf_ref[part, b, 1] for part in parts)
        for a in range(vectors):
            over = cmul(tuple(xf_ref[part, a, 0] for part in parts), h_z)
            over = sub(over, cmul(tuple(xf_ref[part, a, 1] for part in parts), h_y))
            over = cmul(sx_next, over)
            for row in range(0, nz, SUB):
                sums[a] = add(sums[a], tuple(part[row:row + SUB] for part in over))
        over = None
        for slot in range(2):
            h = tuple(hyf_ref[packed_row(slot, part, b, vectors)][None] for part in parts)
            term = cmul(ends[slot], h)
            over = term if over is None else sub(term, over)
        for a in range(vectors):
            for part in parts:
                side = jnp.concatenate([over[part][a:a + 1], jnp.zeros((SUB - 1, ny), jnp.float32)], axis=0)
                totals[part, a, b] = sums[a][part] + side
    everywhere = 3.0 * nz * nx * ny
    for axis in AXES:
        everywhere = everywhere * lax.axis_size(axis)
    for part in parts:
        stack = jnp.concatenate([totals[part, a, b] for a in range(vectors) for b in range(vectors)], axis=0)
        row = jnp.sum(stack.T, axis=0, keepdims=True) * (1.0 / everywhere)
        for device in range(gram_ref.shape[0]):
            gram_ref[device, part:part + 1] = row


def tree_sum(values):
    while len(values) > 1:
        pairs = [values[place] + values[place + 1] for place in range(0, len(values) - 1, 2)]
        values = pairs + ([values[-1]] if len(values) % 2 else [])
    return values[0]


def gather_kernel(rows_ref, gram_ref):
    _, vectors, _ = gram_ref.shape
    total = tree_sum([rows_ref[device] for device in range(rows_ref.shape[0])])
    count = total.shape[1]
    reach = 1
    while reach < SUB:
        total = total + pltpu.roll(total, count - reach, 1)
        reach *= 2
    lanes = lax.broadcasted_iota(jnp.int32, total.shape, 1)
    for a in range(vectors):
        matrix_row = total
        for b in range(vectors):
            place = (a * vectors + b) * SUB
            matrix_row = jnp.where(lanes == b, pltpu.roll(total, (count + b - place) % count, 1), matrix_row)
        for part in range(2):
            gram_ref[part, a:a + 1] = matrix_row[part:part + 1, :vectors]


def rim_kernel(
    pml_ref, ritz_ref, basis_ref, image_ref, near_ref, far_ref, hyf_ref, residual_hbm, residual_ref, packed_ref, sems
):
    _, vectors, _, nz, nx, ny = basis_ref.shape
    plane = (nx, ny)
    rows = lax.broadcasted_iota(jnp.int32, plane, 0)
    lanes = lax.broadcasted_iota(jnp.int32, plane, 1)
    sex = axis_stretch(pml_ref, 1, nx, one_place(1, nx, 0, (1, ny)))
    sey = axis_stretch(pml_ref, 2, ny, one_place(2, ny, 0, plane))
    none = jnp.zeros(plane, jnp.float32)
    sex = tuple(jnp.where(rows == 0, part, none) for part in sex)
    near, far = pair_weights(-1)
    sey = tuple(jnp.where(lanes == 0, part * has_neighbour(2, -1), none) for part in sey)
    rest = jnp.zeros((ny - hyf_ref.shape[0], nz * nx), jnp.float32)
    packed_ref[...] = jnp.concatenate([hyf_ref[...], rest], axis=0).T.reshape(nz, nx, ny)

    def kept(z):
        return pltpu.make_async_copy(residual_ref.at[:, :, :, z], residual_hbm.at[:, :, :, z], sems.at[z])

    @pl.loop(0, nz)
    def _(z):
        packed = packed_ref[z]
        for b in range(vectors):

            def column(slot, b=b):
                return tuple(
                    pltpu.roll(packed, (ny - packed_row(slot, part, b, vectors)) % ny, 1) for part in range(2)
                )

            def row(slot, b=b):
                return tuple(
                    near_ref[part, b, slot, pl.ds(z, 1)] * near + far_ref[part, b, slot, pl.ds(z, 1)] * far
                    for part in range(2)
                )

            factor = (ritz_ref[0, b], ritz_ref[1, b])
            left = []
            for comp in range(3):
                u = (basis_ref[0, b, comp, z], basis_ref[1, b, comp, z])
                w = (image_ref[0, b, comp, z], image_ref[1, b, comp, z])
                left.append(sub(w, cmul(factor, u)))
            left[0] = sub(left[0], cmul(sey, column(0)))
            left[2] = add(left[2], cmul(sey, column(1)))
            left[1] = add(left[1], cmul(sex, row(1)))
            left[2] = sub(left[2], cmul(sex, row(0)))
            for comp in range(3):
                for part in range(2):
                    residual_ref[part, b, comp, z] = left[comp][part]
        kept(z).start()

    @pl.loop(0, nz)
    def _(z):
        kept(z).wait()


def body(fields, material, pml_width, eps_real, eps_loss, coeffs, ritz):
    _, vectors, _, nz, nx, ny = fields.shape
    f32 = lambda *shape: jax.ShapeDtypeStruct(shape, jnp.float32)
    scratch = lambda *shape: pltpu.VMEM(shape, jnp.float32)
    params = pltpu.CompilerParams(vmem_limit_bytes=40 * 1024 * 1024)
    whole = f32(*fields.shape)
    zf_shape = (2, vectors, 2, nx, ny)
    xf_shape = (2, vectors, 2, nz, ny)
    yf_shape = (4 * vectors, nz * nx)
    near, xf, yf = pl.pallas_call(
        face_kernel,
        out_shape=(whole, f32(*xf_shape), f32(*yf_shape)),
        in_specs=[HBM],
        out_specs=(VMEM,) * 3,
        scratch_shapes=[pltpu.SemaphoreType.DMA((2, 3))],
        compiler_params=params,
        name="take_faces",
    )(pltpu.with_memory_space_constraint(fields, pltpu.HBM))
    near_xf, far_xf = swapped_with_neighbours(xf, "gx")
    yf = passed_round(yf, "gy", -1)
    cells = fields.size // 6 // vectors

    def cost(flops, passes):
        return pl.CostEstimate(flops=flops * cells, bytes_accessed=passes * 4 * fields.size, transcendentals=0)

    planes = f32(nz, nx, ny)
    face = f32(*xf_shape)
    basis, loss, h, packed, table, sz = pl.pallas_call(
        prepare_kernel,
        out_shape=(whole, whole, whole, planes, f32(8, nx, ny), f32(4, nz, ny)),
        in_specs=[SMEM] * 4 + [VMEM] * 2,
        out_specs=(VMEM,) * 6,
        compiler_params=params,
        cost_estimate=cost(800, 4),
        name="prepare",
    )(pml_width, eps_real, eps_loss, coeffs, near, material)
    h, packed, xf, yt, xadd, yadd, hxf, zf = pl.pallas_call(
        slab_kernel,
        out_shape=(whole, planes, face, f32(*yf_shape), face, planes, face, f32(*zf_shape)),
        in_specs=[SMEM] * 2 + [VMEM] * 6,
        out_specs=(VMEM,) * 8,
        input_output_aliases={3: 0, 4: 1},
        compiler_params=params,
        name="slab_face",
    )(pml_width, coeffs, basis, h, packed, near_xf, far_xf, yf)
    zf = passed_round(zf, "gz", 1)
    h, image, acc, before, basis_new = pl.pallas_call(
        inner_kernel,
        out_shape=(whole, whole, f32(vectors, 2 * vectors, SUB, ny), f32(*zf_shape), whole),
        in_specs=[VMEM] * 7,
        out_specs=(VMEM,) * 4 + (HBM,),
        scratch_shapes=[pltpu.SemaphoreType.DMA],
        input_output_aliases={4: 0},
        compiler_params=params,
        cost_estimate=cost(800, 2),
        name="apply_inner",
    )(basis, loss, table, sz, h, xadd, yadd)
    h, hxf, hyf = pl.pallas_call(
        last_plane_kernel,
        out_shape=(whole, face, f32(*yf_shape)),
        in_specs=[VMEM] * 5,
        out_specs=(VMEM,) * 3,
        input_output_aliases={2: 0, 4: 1},
        compiler_params=params,
        name="last_plane",
    )(sz, zf, h, packed, hxf)
    near_hxf, far_hxf = swapped_with_neighbours(hxf, "gx")
    from_y = passed_round(hyf, "gy", 1)
    devices = lax.axis_size("gx") * lax.axis_size("gy") * lax.axis_size("gz")
    image, gram = pl.pallas_call(
        outer_kernel,
        out_shape=(whole, pltpu.VMEM((devices, 2, ny), jnp.float32)),
        in_specs=[SMEM] + [VMEM] * 13,
        out_specs=(VMEM,) * 2,
        input_output_aliases={11: 0},
        compiler_params=params,
        cost_estimate=cost(300, 1),
        name="apply_outer",
    )(pml_width, basis, loss, table, sz, h, zf, xf, yt, hxf, hyf, image, acc, before)
    rows = lax.all_to_all(gram, ("gx", "gy", "gz"), 0, 0)
    residual = pl.pallas_call(
        rim_kernel,
        out_shape=whole,
        in_specs=[SMEM] * 2 + [VMEM] * 5,
        out_specs=HBM,
        scratch_shapes=[scratch(*fields.shape), scratch(nz, nx, ny), pltpu.SemaphoreType.DMA((nz,))],
        compiler_params=params,
        cost_estimate=cost(200, 3),
        name="add_rims",
    )(pml_width, ritz, basis, image, near_hxf, far_hxf, from_y)
    rows, residual = lax.optimization_barrier((rows, residual))
    gram = pl.pallas_call(
        gather_kernel,
        out_shape=f32(2, vectors, vectors),
        in_specs=[VMEM],
        out_specs=VMEM,
        compiler_params=params,
        name="sum_rows",
    )(rows)
    return basis_new, residual, gram


def solution(mesh):
    in_specs = (P(None, None, None, "gz", "gx", "gy"), P("gz", "gx", "gy"), P(), P(), P(), P(), P())
    out_specs = (P(None, None, None, "gz", "gx", "gy"), P(None, None, None, "gz", "gx", "gy"), P())
    return jax.shard_map(body, mesh=mesh, in_specs=in_specs, out_specs=out_specs, check_vma=False)
```

```python
import functools

import jax
import jax.numpy as jnp
from jax import lax
from jax.experimental import pallas as pl
from jax.experimental.pallas import tpu as pltpu
from jax.sharding import PartitionSpec as P

OMEGA_SQ = 0.36
SIGMA_TOP = 3.0
BOUNDS = ((4, 5), (0, 1), (2, 3))
AXES = ("gz", "gx", "gy")

VMEM = pl.BlockSpec(memory_space=pltpu.VMEM)
SMEM = pl.BlockSpec(memory_space=pltpu.SMEM)
HBM = pl.BlockSpec(memory_space=pltpu.HBM)


def passed_round(value, axis, steps):
    count = lax.axis_size(axis)
    return lax.ppermute(value, axis, [(source, (source + steps) % count) for source in range(count)])


def inverse_stretch(places, length, low_width, high_width):
    inside_depth = jnp.clip((low_width - places) / low_width, 0.0, 1.0) + jnp.clip(
        (places + 1.0 - length + high_width) / high_width, 0.0, 1.0
    )
    absorb = SIGMA_TOP * inside_depth * inside_depth
    scaled = 1.0 / (1.0 + absorb * absorb)
    return scaled, -absorb * scaled


def cmul(left, right):
    return (left[0] * right[0] - left[1] * right[1], left[0] * right[1] + left[1] * right[0])


def add(left, right):
    return (left[0] + right[0], left[1] + right[1])


def sub(left, right):
    return (left[0] - right[0], left[1] - right[1])


def axis_stretch(pml_ref, direction, count, places):
    total = count * lax.axis_size(AXES[direction])
    low_slot, high_slot = BOUNDS[direction]
    low = jnp.full(places.shape, pml_ref[low_slot], jnp.int32).astype(jnp.float32)
    high = jnp.full(places.shape, pml_ref[high_slot], jnp.int32).astype(jnp.float32)
    return inverse_stretch(places, jnp.float32(total), low, high)


def local_places(direction, count, shape, dim):
    start = lax.axis_index(AXES[direction]) * count
    return (lax.broadcasted_iota(jnp.int32, shape, dim) + start).astype(jnp.float32)


def one_place(direction, count, offset, shape):
    start = lax.axis_index(AXES[direction]) * count + offset
    return jnp.full(shape, start, jnp.int32).astype(jnp.float32)


def packed_row(slot, part, vector, vectors):
    return (slot * 2 + part) * vectors + vector


def has_neighbour(direction, steps):
    place = lax.axis_index(AXES[direction]) + steps
    inside = (place >= 0) & (place < lax.axis_size(AXES[direction]))
    return jnp.where(inside, 1.0, 0.0).astype(jnp.float32)


def face_kernel(fields_hbm, fields_ref, xf_ref, yf_ref, sems):
    _, vectors, _, nz, nx, ny = fields_ref.shape
    lanes = lax.broadcasted_iota(jnp.int32, (nx, ny), 1)
    copies = [
        pltpu.make_async_copy(fields_hbm.at[part, :, comp], fields_ref.at[part, :, comp], sems.at[part, comp])
        for comp in (0, 2, 1) for part in range(2)
    ]
    for copy in copies:
        copy.start()
    packed = [jnp.zeros((nx, ny), jnp.float32)] * nz
    for place, comp in enumerate((0, 2)):
        for part in range(2):
            copies[2 * place + part].wait()
            for a in range(vectors):
                row = packed_row(comp // 2, part, a, vectors)
                for z in range(nz):
                    value = fields_ref[part, a, comp, z]
                    packed[z] = jnp.where(lanes == row, pltpu.roll(value, row, 1) if row else value, packed[z])
    turned = jnp.concatenate(packed, axis=0).T
    yf_ref[...] = turned[:yf_ref.shape[0]]
    for part in range(2):
        for a in range(vectors):
            xf_ref[part, a, 1] = fields_ref[part, a, 2, :, 0, :]
    for part in range(2):
        copies[4 + part].wait()
        for a in range(vectors):
            xf_ref[part, a, 0] = fields_ref[part, a, 1, :, 0, :]


def rotated(coeffs_ref, old, b):
    new = None
    for a, value in enumerate(old):
        term = cmul((coeffs_ref[0, a, b], coeffs_ref[1, a, b]), value)
        new = term if new is None else add(new, term)
    return new


SUB = 8
SHX, SEX, SHY, SEY = range(0, 8, 2)


def field_of(ref, b, comp, z, cut):
    return tuple(ref[part, b, comp, z, cut] for part in range(2))


def tiles_of(nx):
    return [slice(SUB * t, SUB * (t + 1)) for t in range(nx // SUB)]


def prepare_kernel(
    pml_ref, eps_real_ref, eps_loss_ref, coeffs_ref, fields_ref, material_ref,
    basis_ref, loss_ref, h_ref, packed_ref, table_ref, sz_ref,
):
    _, vectors, _, nz, nx, ny = fields_ref.shape
    plane = (nx, ny)
    parts = range(2)
    for slot, direction, half, count, dim in (
        (SHX, 1, 0.5, nx, 0), (SEX, 1, 0.0, nx, 0), (SHY, 2, 0.5, ny, 1), (SEY, 2, 0.0, ny, 1),
    ):
        values = axis_stretch(pml_ref, direction, count, local_places(direction, count, plane, dim) + half)
        for part in parts:
            table_ref[slot + part] = values[part]
    for slot, half in ((0, 0.0), (2, 0.5)):
        values = axis_stretch(pml_ref, 0, nz, local_places(0, nz, (nz, ny), 0) + half)
        for part in parts:
            sz_ref[slot + part] = values[part]

    @pl.loop(0, nz)
    def _(z):
        material = material_ref[z]
        eps = []
        for source in (eps_real_ref, eps_loss_ref):
            value = jnp.zeros(plane, jnp.float32)
            for number in range(source.shape[0]):
                value = jnp.where(material == number, -OMEGA_SQ * source[number], value)
            eps.append(value)
        for comp in range(3):
            old = [(fields_ref[0, a, comp, z], fields_ref[1, a, comp, z]) for a in range(vectors)]
            for b in range(vectors):
                new = rotated(coeffs_ref, old, b)
                loss = cmul(eps, new)
                for part in parts:
                    basis_ref[part, b, comp, z] = new[part]
                    loss_ref[part, b, comp, z] = loss[part]
        packed_ref[z] = jnp.zeros(plane, jnp.float32)

    tile = (SUB, ny)
    rows = lax.broadcasted_iota(jnp.int32, tile, 0)
    lanes = lax.broadcasted_iota(jnp.int32, tile, 1)
    cuts = tiles_of(nx)

    def magnetic(b, z, last):
        shz = tuple(sz_ref[2 + part, pl.ds(z, 1)] for part in parts)
        for cut in cuts:
            u = [field_of(basis_ref, b, comp, z, cut) for comp in range(3)]

            def step_z(comp):
                if last:
                    return tuple(-value for value in u[comp])
                return sub(field_of(basis_ref, b, comp, z + 1, cut), u[comp])

            def step_x(comp):
                if cut.stop < nx:
                    ahead = field_of(basis_ref, b, comp, z, slice(cut.start + 1, cut.stop + 1))
                else:
                    ahead = tuple(jnp.where(rows == SUB - 1, 0.0, pltpu.roll(value, SUB - 1, 0)) for value in u[comp])
                return sub(ahead, u[comp])

            def step_y(comp):
                ahead = tuple(jnp.where(lanes == ny - 1, 0.0, pltpu.roll(value, ny - 1, 1)) for value in u[comp])
                return sub(ahead, u[comp])

            shx = tuple(table_ref[SHX + part, cut] for part in parts)
            shy = tuple(table_ref[SHY + part, cut] for part in parts)
            h = (
                sub(cmul(shy, step_y(2)), cmul(shz, step_z(1))),
                sub(cmul(shz, step_z(0)), cmul(shx, step_x(2))),
                sub(cmul(shx, step_x(1)), cmul(shy, step_y(0))),
            )
            for comp in range(3):
                for part in parts:
                    h_ref[part, b, comp, z, cut] = h[comp][part]
            packed = packed_ref[z, cut]
            for slot, value in enumerate((h[2], h[0])):
                for part in parts:
                    row = packed_row(slot, part, b, vectors)
                    packed = jnp.where(lanes == row, pltpu.roll(value[part], (row + 1) % ny, 1), packed)
            packed_ref[z, cut] = packed

    @pl.loop(0, nz - 1)
    def _(z):
        for b in range(vectors):
            magnetic(b, z, False)

    for b in range(vectors):
        magnetic(b, nz - 1, True)


def turn_face(coeffs_ref, direction, raw_ref, face_ref):
    inside = has_neighbour(direction, 1)
    vectors = raw_ref.shape[1]
    for slot in range(2):
        old = [(raw_ref[0, a, slot] * inside, raw_ref[1, a, slot] * inside) for a in range(vectors)]
        for b in range(vectors):
            new = rotated(coeffs_ref, old, b)
            for part in range(2):
                face_ref[part, b, slot] = new[part]


def turn_column(coeffs_ref, raw_ref, rows_ref):
    vectors = coeffs_ref.shape[1]
    inside = has_neighbour(2, 1)
    both = 2 * vectors
    shape = (both, raw_ref.shape[1])
    which = lax.broadcasted_iota(jnp.int32, shape, 0)
    turned = [jnp.zeros(shape, jnp.float32)] * 2
    for part in range(2):
        for a in range(vectors):
            column = jnp.zeros(shape, jnp.float32)
            for b in range(vectors):
                first, second = coeffs_ref[0, a, b] * inside, coeffs_ref[1, a, b] * inside
                if part:
                    first, second = -second, first
                column = jnp.where(which == b, first, column)
                column = jnp.where(which == vectors + b, second, column)
            for slot in range(2):
                row = packed_row(slot, part, a, vectors)
                turned[slot] = turned[slot] + column * raw_ref[row:row + 1]
    for slot in range(2):
        rows_ref[slot * both:(slot + 1) * both] = turned[slot]


def lane_to_last(values, slot, part, b, vectors):
    ny = values.shape[-1]
    lanes = lax.broadcasted_iota(jnp.int32, values.shape, 1)
    row = packed_row(slot, part, b, vectors)
    return jnp.where(lanes == ny - 1, pltpu.roll(values, ny - 1 - row, 1), 0.0)


def with_halos(h, b, z, cut, nx, xadd_ref, yadd_ref):
    vectors = xadd_ref.shape[1]
    column = yadd_ref[z, cut]
    hx = tuple(h[0][part] + lane_to_last(column, 1, part, b, vectors) for part in range(2))
    hz = tuple(h[2][part] + lane_to_last(column, 0, part, b, vectors) for part in range(2))
    hy = h[1]
    if cut.stop == nx:
        rows = lax.broadcasted_iota(jnp.int32, column.shape, 0)

        def row_of(slot):
            return tuple(
                jnp.where(rows == SUB - 1, xadd_ref[part, b, slot, pl.ds(z, 1)], 0.0) for part in range(2)
            )

        hy, hz = add(hy, row_of(0)), add(hz, row_of(1))
    return hx, hy, hz


def slab_kernel(
    pml_ref, coeffs_ref, basis_ref, h_in, packed_in, raw_xf_ref, raw_yf_ref,
    h_ref, packed_ref, xf_ref, yt_ref, xadd_ref, yadd_ref, hxf_ref, zf_ref,
):
    del h_in, packed_in
    _, vectors, _, nz, nx, ny = basis_ref.shape
    parts = range(2)
    cells = nz * nx
    both = 2 * vectors
    turn_face(coeffs_ref, 1, raw_xf_ref, xf_ref)
    turn_column(coeffs_ref, raw_yf_ref, yt_ref)
    shx = axis_stretch(pml_ref, 1, nx, one_place(1, nx, nx - 1, (1, ny)) + 0.5)
    shy = axis_stretch(pml_ref, 2, ny, one_place(2, ny, ny - 1, (1, cells)) + 0.5)
    for b in range(vectors):
        for slot in range(2):
            value = cmul(shx, tuple(xf_ref[part, b, 1 - slot] for part in parts))
            for part in parts:
                xadd_ref[part, b, slot] = value[part] if slot else -value[part]
    added = []
    for slot in range(2):
        value = cmul(shy, (yt_ref[slot * both:slot * both + vectors], yt_ref[slot * both + vectors:(slot + 1) * both]))
        added += [part if slot else -part for part in value]
    rest = jnp.zeros((ny - 2 * both, cells), jnp.float32)
    yadd_ref[...] = jnp.concatenate(added + [rest], axis=0).T.reshape(nz, nx, ny)
    packed_ref[...] = packed_ref[...] + yadd_ref[...]
    last = nz - 1
    lower = jnp.full((SUB, ny), lax.axis_index(AXES[0]), jnp.int32) == 0
    lanes = lax.broadcasted_iota(jnp.int32, (nz, ny), 1)
    corner = packed_ref[:, nx - 1, :]
    for b in range(vectors):
        for part in parts:
            row = packed_row(0, part, b, vectors)
            edge = pltpu.roll(xadd_ref[part, b, 1], (row + 1) % ny, 1)
            corner = corner + jnp.where(lanes == row, edge, 0.0)
    packed_ref[:, nx - 1, :] = corner
    for b in range(vectors):
        for part in parts:
            hxf_ref[part, b, 0] = h_ref[part, b, 1, :, nx - 1, :] + xadd_ref[part, b, 0]
            hxf_ref[part, b, 1] = (
                h_ref[part, b, 2, :, nx - 1, :] + xadd_ref[part, b, 1]
                + lane_to_last(yadd_ref[:, nx - 1, :], 0, part, b, vectors)
            )
        for cut in tiles_of(nx):
            h = [field_of(h_ref, b, comp, last, cut) for comp in range(3)]
            h = with_halos(h, b, last, cut, nx, xadd_ref, yadd_ref)
            for part in parts:
                for comp in range(3):
                    h_ref[part, b, comp, last, cut] = h[comp][part]
                for comp in range(2):
                    zf_ref[part, b, comp, cut] = jnp.where(lower, h[comp][part], basis_ref[part, b, comp, 0, cut])


def plane_step(
    b, z, before, sums, ritz_ref, basis_ref, loss_ref, table_ref, sz_ref, h_ref, left_ref, halos=None
):
    _, vectors, _, _, nx, ny = basis_ref.shape
    rows = lax.broadcasted_iota(jnp.int32, (SUB, ny), 0)
    lanes = lax.broadcasted_iota(jnp.int32, (SUB, ny), 1)
    parts = range(2)
    cuts = tiles_of(nx)
    sez = tuple(sz_ref[part, pl.ds(z, 1)] for part in parts)
    fields = []
    for cut in cuts:
        h = [field_of(h_ref, b, comp, z, cut) for comp in range(3)]
        if halos is not None:
            h = with_halos(h, b, z, cut, nx, *halos)
            for comp in (1, 2):
                for part in parts:
                    h_ref[part, b, comp, z, cut] = h[comp][part]
        fields.append(h)
    sums = list(sums)
    for t, cut in enumerate(cuts):
        hx, hy, hz = fields[t]

        def back_x(comp):
            here = fields[t][comp]
            if t:
                past = field_of(h_ref, b, comp, z, slice(cut.start - 1, cut.stop - 1))
            else:
                past = tuple(jnp.where(rows == 0, 0.0, pltpu.roll(value, 1, 0)) for value in here)
            return sub(here, past)

        def back_y(value):
            return sub(value, tuple(jnp.where(lanes == 0, 0.0, pltpu.roll(part, 1, 1)) for part in value))

        sex = tuple(table_ref[SEX + part, cut] for part in parts)
        sey = tuple(table_ref[SEY + part, cut] for part in parts)
        bxy, bxz = (cmul(sex, back_x(comp)) for comp in (1, 2))
        byz, byx = (cmul(sey, back_y(value)) for value in (hz, hx))
        bzx, bzy = (cmul(sez, sub(value, past)) for value, past in zip((hx, hy), before[t]))
        curl = (sub(byz, bzy), sub(bzx, bxz), sub(bxy, byx))
        w = [add(curl[comp], field_of(loss_ref, b, comp, z, cut)) for comp in range(3)]
        for comp in range(3):
            left = sub(w[comp], cmul((ritz_ref[0, b], ritz_ref[1, b]), field_of(basis_ref, b, comp, z, cut)))
            for part in parts:
                left_ref[part, b, comp, z, cut] = left[part]
        for a in range(vectors):
            total = sums[a]
            for comp in range(3):
                total = add(total, cmul(field_of(basis_ref, a, comp, z, cut), w[comp]))
            sums[a] = total
    return [(h[0], h[1]) for h in fields], sums


def inner_kernel(
    ritz_ref, basis_ref, loss_ref, table_ref, sz_ref, h_in, xadd_ref, yadd_ref,
    h_ref, left_ref, acc_ref, before_ref, basis_hbm, sem,
):
    del h_in
    _, vectors, _, nz, nx, ny = basis_ref.shape
    keep = pltpu.make_async_copy(basis_ref, basis_hbm, sem)
    keep.start()
    cuts = tiles_of(nx)
    acc_ref[...] = jnp.zeros(acc_ref.shape, jnp.float32)
    before_ref[...] = jnp.zeros(before_ref.shape, jnp.float32)

    @pl.loop(0, nz - 1)
    def _(z):
        for b in range(vectors):
            before = [
                tuple(tuple(before_ref[part, b, slot, cut] for part in range(2)) for slot in range(2)) for cut in cuts
            ]
            sums = [(acc_ref[b, a], acc_ref[b, vectors + a]) for a in range(vectors)]
            before, sums = plane_step(
                b, z, before, sums, ritz_ref, basis_ref, loss_ref, table_ref, sz_ref, h_ref, left_ref, (xadd_ref, yadd_ref)
            )
            for part in range(2):
                for a in range(vectors):
                    acc_ref[b, part * vectors + a] = sums[a][part]
                for t, cut in enumerate(cuts):
                    for slot in range(2):
                        before_ref[part, b, slot, cut] = before[t][slot][part]

    keep.wait()


def last_plane_kernel(sz_ref, zf_ref, h_in, packed_in, hxf_in, h_ref, hxf_ref, hyf_ref):
    del h_in, hxf_in
    _, vectors, _, nz, nx, ny = h_ref.shape
    parts = range(2)
    last = nz - 1
    lanes = lax.broadcasted_iota(jnp.int32, (SUB, ny), 1)
    shz = tuple(sz_ref[2 + part, last:] * has_neighbour(0, 1) for part in parts)
    packed = [packed_in[last, cut] for cut in tiles_of(nx)]
    for b in range(vectors):
        for t, cut in enumerate(tiles_of(nx)):
            ex, ey = (tuple(zf_ref[part, b, slot, cut] for part in parts) for slot in range(2))
            more = (tuple(-value for value in cmul(shz, ey)), cmul(shz, ex))
            for part in parts:
                for comp in range(2):
                    h_ref[part, b, comp, last, cut] = h_ref[part, b, comp, last, cut] + more[comp][part]
                row = packed_row(1, part, b, vectors)
                edge = pltpu.roll(more[0][part], (row + 1) % ny, 1)
                packed[t] = packed[t] + jnp.where(lanes == row, edge, 0.0)
                if cut.stop == nx:
                    hxf_ref[part, b, 0, last:] = hxf_ref[part, b, 0, last:] + more[1][part][SUB - 1:]
    inner = packed_in[:last].reshape(last * nx, ny)
    hyf_ref[...] = jnp.concatenate([inner] + packed, axis=0).T[:hyf_ref.shape[0]]


def outer_kernel(
    pml_ref, ritz_ref, basis_ref, loss_ref, table_ref, sz_ref, h_ref, zf_ref, xf_ref, yt_ref, hxf_ref, hyf_ref,
    left_in, acc_ref, before_ref, left_ref, gram_ref,
):
    del left_in
    _, vectors, _, nz, nx, ny = basis_ref.shape
    parts = range(2)
    cuts = tiles_of(nx)
    under = axis_stretch(pml_ref, 0, nz, one_place(0, nz, -1, (1, ny)) + 0.5)
    sez = tuple(sz_ref[part, 0:1] * has_neighbour(0, -1) for part in parts)
    sx_next = axis_stretch(pml_ref, 1, nx, one_place(1, nx, nx, (1, ny)))
    sy_next = axis_stretch(pml_ref, 2, ny, one_place(2, ny, ny, (1, nz * nx)))
    both = 2 * vectors
    ends = [
        cmul(sy_next, (yt_ref[slot * both:slot * both + vectors], yt_ref[slot * both + vectors:(slot + 1) * both]))
        for slot in range(2)
    ]
    totals = {}
    for b in range(vectors):

        def tile_of(ref, slot, cut, b=b):
            return tuple(ref[part, b, slot, cut] for part in parts)

        before = [tuple(tile_of(before_ref, slot, cut) for slot in range(2)) for cut in cuts]
        sums = [(acc_ref[b, a], acc_ref[b, vectors + a]) for a in range(vectors)]
        _, sums = plane_step(
            b, nz - 1, before, sums, ritz_ref, basis_ref, loss_ref, table_ref, sz_ref, h_ref, left_ref
        )
        for cut in cuts:
            ex, ey = (field_of(basis_ref, b, comp, 0, cut) for comp in range(2))
            hx = sub(tile_of(zf_ref, 0, cut), cmul(under, ey))
            hy = add(tile_of(zf_ref, 1, cut), cmul(under, ex))
            more = (cmul(sez, hy), cmul(sez, hx))
            for part in parts:
                left_ref[part, b, 0, 0, cut] = left_ref[part, b, 0, 0, cut] + more[0][part]
                left_ref[part, b, 1, 0, cut] = left_ref[part, b, 1, 0, cut] - more[1][part]
            for a in range(vectors):
                ex, ey = (field_of(basis_ref, a, comp, 0, cut) for comp in range(2))
                sums[a] = add(sums[a], sub(cmul(ex, more[0]), cmul(ey, more[1])))
        h_y = tuple(hxf_ref[part, b, 0] for part in parts)
        h_z = tuple(hxf_ref[part, b, 1] for part in parts)
        for a in range(vectors):
            over = cmul(tuple(xf_ref[part, a, 0] for part in parts), h_z)
            over = sub(over, cmul(tuple(xf_ref[part, a, 1] for part in parts), h_y))
            over = cmul(sx_next, over)
            for row in range(0, nz, SUB):
                sums[a] = add(sums[a], tuple(part[row:row + SUB] for part in over))
        over = None
        for slot in range(2):
            h = tuple(hyf_ref[packed_row(slot, part, b, vectors)][None] for part in parts)
            term = cmul(ends[slot], h)
            over = term if over is None else sub(term, over)
        for a in range(vectors):
            for part in parts:
                side = jnp.concatenate([over[part][a:a + 1], jnp.zeros((SUB - 1, ny), jnp.float32)], axis=0)
                totals[part, a, b] = sums[a][part] + side
    everywhere = 3.0 * nz * nx * ny
    for axis in AXES:
        everywhere = everywhere * lax.axis_size(axis)
    for part in parts:
        stack = jnp.concatenate([totals[part, a, b] for a in range(vectors) for b in range(vectors)], axis=0)
        row = jnp.sum(stack.T, axis=0, keepdims=True) * (1.0 / everywhere)
        for device in range(gram_ref.shape[0]):
            gram_ref[device, part:part + 1] = row


def tree_sum(values):
    while len(values) > 1:
        pairs = [values[place] + values[place + 1] for place in range(0, len(values) - 1, 2)]
        values = pairs + ([values[-1]] if len(values) % 2 else [])
    return values[0]


def gather_kernel(rows_ref, gram_ref):
    _, vectors, _ = gram_ref.shape
    total = tree_sum([rows_ref[device] for device in range(rows_ref.shape[0])])
    count = total.shape[1]
    reach = 1
    while reach < SUB:
        total = total + pltpu.roll(total, count - reach, 1)
        reach *= 2
    lanes = lax.broadcasted_iota(jnp.int32, total.shape, 1)
    for a in range(vectors):
        matrix_row = total
        for b in range(vectors):
            place = (a * vectors + b) * SUB
            matrix_row = jnp.where(lanes == b, pltpu.roll(total, (count + b - place) % count, 1), matrix_row)
        for part in range(2):
            gram_ref[part, a:a + 1] = matrix_row[part:part + 1, :vectors]


def rim_kernel(pml_ref, left_in, hxf_ref, hyf_ref, left_ref, residual_hbm, xadd_ref, yadd_ref, sems):
    del left_in
    _, vectors, _, nz, nx, ny = left_ref.shape
    parts = range(2)
    both = 2 * vectors
    sex = axis_stretch(pml_ref, 1, nx, one_place(1, nx, 0, (nz, ny)))
    sex = tuple(part * has_neighbour(1, -1) for part in sex)
    sey = axis_stretch(pml_ref, 2, ny, one_place(2, ny, 0, (vectors, nz * nx)))
    sey = tuple(part * has_neighbour(2, -1) for part in sey)
    for b in range(vectors):
        for slot in range(2):
            value = cmul(sex, tuple(hxf_ref[part, b, slot] for part in parts))
            for part in parts:
                xadd_ref[part, b, slot] = value[part] if slot else -value[part]
    added = []
    for slot in range(2):
        first = slot * both
        value = cmul(sey, (hyf_ref[first:first + vectors], hyf_ref[first + vectors:first + both]))
        added += [part if slot else -part for part in value]
    rest = jnp.zeros((ny - 2 * both, nz * nx), jnp.float32)
    yadd_ref[...] = jnp.concatenate(added + [rest], axis=0).T.reshape(nz, nx, ny)
    rows = lax.broadcasted_iota(jnp.int32, (SUB, ny), 0)
    lanes = lax.broadcasted_iota(jnp.int32, (SUB, ny), 1)

    def kept(z):
        return pltpu.make_async_copy(left_ref.at[:, :, :, z], residual_hbm.at[:, :, :, z], sems.at[z])

    @pl.loop(0, nz)
    def _(z):
        for cut in tiles_of(nx):
            column = yadd_ref[z, cut]
            for b in range(vectors):
                for part in parts:

                    def turned(slot, b=b, part=part):
                        row = packed_row(slot, part, b, vectors)
                        value = pltpu.roll(column, ny - row, 1) if row else column
                        return jnp.where(lanes == 0, value, 0.0)

                    def row_of(slot, b=b, part=part):
                        return jnp.where(rows == 0, xadd_ref[part, b, slot, pl.ds(z, 1)], 0.0)

                    ex = left_ref[part, b, 0, z, cut] + turned(0)
                    ez = left_ref[part, b, 2, z, cut] + turned(1)
                    if cut.start == 0:
                        left_ref[part, b, 1, z, cut] = left_ref[part, b, 1, z, cut] + row_of(1)
                        ez = ez + row_of(0)
                    left_ref[part, b, 0, z, cut] = ex
                    left_ref[part, b, 2, z, cut] = ez
        kept(z).start()

    @pl.loop(0, nz)
    def _(z):
        kept(z).wait()


def body(fields, material, pml_width, eps_real, eps_loss, coeffs, ritz):
    _, vectors, _, nz, nx, ny = fields.shape
    f32 = lambda *shape: jax.ShapeDtypeStruct(shape, jnp.float32)
    scratch = lambda *shape: pltpu.VMEM(shape, jnp.float32)
    params = pltpu.CompilerParams(vmem_limit_bytes=40 * 1024 * 1024)
    whole = f32(*fields.shape)
    zf_shape = (2, vectors, 2, nx, ny)
    xf_shape = (2, vectors, 2, nz, ny)
    yf_shape = (4 * vectors, nz * nx)
    near, xf, yf = pl.pallas_call(
        face_kernel,
        out_shape=(whole, f32(*xf_shape), f32(*yf_shape)),
        in_specs=[HBM],
        out_specs=(VMEM,) * 3,
        scratch_shapes=[pltpu.SemaphoreType.DMA((2, 3))],
        compiler_params=params,
        name="take_faces",
    )(pltpu.with_memory_space_constraint(fields, pltpu.HBM))
    xf = passed_round(xf, "gx", -1)
    yf = passed_round(yf, "gy", -1)
    cells = fields.size // 6 // vectors

    def cost(flops, passes):
        return pl.CostEstimate(flops=flops * cells, bytes_accessed=passes * 4 * fields.size, transcendentals=0)

    planes = f32(nz, nx, ny)
    face = f32(*xf_shape)
    basis, loss, h, packed, table, sz = pl.pallas_call(
        prepare_kernel,
        out_shape=(whole, whole, whole, planes, f32(8, nx, ny), f32(4, nz, ny)),
        in_specs=[SMEM] * 4 + [VMEM] * 2,
        out_specs=(VMEM,) * 6,
        compiler_params=params,
        cost_estimate=cost(800, 4),
        name="prepare",
    )(pml_width, eps_real, eps_loss, coeffs, near, material)
    h, packed, xf, yt, xadd, yadd, hxf, zf = pl.pallas_call(
        slab_kernel,
        out_shape=(whole, planes, face, f32(*yf_shape), face, planes, face, f32(*zf_shape)),
        in_specs=[SMEM] * 2 + [VMEM] * 5,
        out_specs=(VMEM,) * 8,
        input_output_aliases={3: 0, 4: 1},
        compiler_params=params,
        name="slab_face",
    )(pml_width, coeffs, basis, h, packed, xf, yf)
    zf = passed_round(zf, "gz", 1)
    h, left, acc, before, basis_new = pl.pallas_call(
        inner_kernel,
        out_shape=(whole, whole, f32(vectors, 2 * vectors, SUB, ny), f32(*zf_shape), whole),
        in_specs=[SMEM] + [VMEM] * 7,
        out_specs=(VMEM,) * 4 + (HBM,),
        scratch_shapes=[pltpu.SemaphoreType.DMA],
        input_output_aliases={5: 0},
        compiler_params=params,
        cost_estimate=cost(800, 2),
        name="apply_inner",
    )(ritz, basis, loss, table, sz, h, xadd, yadd)
    h, hxf, hyf = pl.pallas_call(
        last_plane_kernel,
        out_shape=(whole, face, f32(*yf_shape)),
        in_specs=[VMEM] * 5,
        out_specs=(VMEM,) * 3,
        input_output_aliases={2: 0, 4: 1},
        compiler_params=params,
        name="last_plane",
    )(sz, zf, h, packed, hxf)
    devices = lax.axis_size("gx") * lax.axis_size("gy") * lax.axis_size("gz")
    left, gram = pl.pallas_call(
        outer_kernel,
        out_shape=(whole, pltpu.VMEM((devices, 2, ny), jnp.float32)),
        in_specs=[SMEM] * 2 + [VMEM] * 13,
        out_specs=(VMEM,) * 2,
        input_output_aliases={12: 0},
        compiler_params=params,
        cost_estimate=cost(300, 1),
        name="apply_outer",
    )(pml_width, ritz, basis, loss, table, sz, h, zf, xf, yt, hxf, hyf, left, acc, before)
    gram, hxf, hyf = lax.optimization_barrier((gram, hxf, hyf))
    rows = lax.all_to_all(gram, ("gx", "gy", "gz"), 0, 0)
    from_x = passed_round(hxf, "gx", 1)
    from_y = passed_round(hyf, "gy", 1)
    _, residual = pl.pallas_call(
        rim_kernel,
        out_shape=(whole, whole),
        in_specs=[SMEM] + [VMEM] * 3,
        out_specs=(VMEM, HBM),
        scratch_shapes=[scratch(*xf_shape), scratch(nz, nx, ny), pltpu.SemaphoreType.DMA((nz,))],
        input_output_aliases={1: 0},
        compiler_params=params,
        cost_estimate=pl.CostEstimate(flops=0, bytes_accessed=0, transcendentals=0),
        name="add_rims",
    )(pml_width, left, from_x, from_y)
    rows, residual = lax.optimization_barrier((rows, residual))
    gram = pl.pallas_call(
        gather_kernel,
        out_shape=f32(2, vectors, vectors),
        in_specs=[VMEM],
        out_specs=VMEM,
        compiler_params=params,
        name="sum_rows",
    )(rows)
    return basis_new, residual, gram


def solution(mesh):
    in_specs = (P(None, None, None, "gz", "gx", "gy"), P("gz", "gx", "gy"), P(), P(), P(), P(), P())
    out_specs = (P(None, None, None, "gz", "gx", "gy"), P(None, None, None, "gz", "gx", "gy"), P())
    return jax.shard_map(body, mesh=mesh, in_specs=in_specs, out_specs=out_specs, check_vma=False)
```

```python
import functools

import jax
import jax.numpy as jnp
from jax import lax
from jax.experimental import pallas as pl
from jax.experimental.pallas import tpu as pltpu
from jax.sharding import PartitionSpec as P

OMEGA_SQ = 0.36
SIGMA_TOP = 3.0
BOUNDS = ((4, 5), (0, 1), (2, 3))
AXES = ("gz", "gx", "gy")

VMEM = pl.BlockSpec(memory_space=pltpu.VMEM)
SMEM = pl.BlockSpec(memory_space=pltpu.SMEM)
HBM = pl.BlockSpec(memory_space=pltpu.HBM)


def passed_round(value, axis, steps):
    count = lax.axis_size(axis)
    return lax.ppermute(value, axis, [(source, (source + steps) % count) for source in range(count)])


def inverse_stretch(places, length, low_width, high_width):
    inside_depth = jnp.clip((low_width - places) / low_width, 0.0, 1.0) + jnp.clip(
        (places + 1.0 - length + high_width) / high_width, 0.0, 1.0
    )
    absorb = SIGMA_TOP * inside_depth * inside_depth
    scaled = 1.0 / (1.0 + absorb * absorb)
    return scaled, -absorb * scaled


def cmul(left, right):
    return (left[0] * right[0] - left[1] * right[1], left[0] * right[1] + left[1] * right[0])


def add(left, right):
    return (left[0] + right[0], left[1] + right[1])


def sub(left, right):
    return (left[0] - right[0], left[1] - right[1])


def axis_stretch(pml_ref, direction, count, places):
    total = count * lax.axis_size(AXES[direction])
    low_slot, high_slot = BOUNDS[direction]
    low = jnp.full(places.shape, pml_ref[low_slot], jnp.int32).astype(jnp.float32)
    high = jnp.full(places.shape, pml_ref[high_slot], jnp.int32).astype(jnp.float32)
    return inverse_stretch(places, jnp.float32(total), low, high)


def local_places(direction, count, shape, dim):
    start = lax.axis_index(AXES[direction]) * count
    return (lax.broadcasted_iota(jnp.int32, shape, dim) + start).astype(jnp.float32)


def one_place(direction, count, offset, shape):
    start = lax.axis_index(AXES[direction]) * count + offset
    return jnp.full(shape, start, jnp.int32).astype(jnp.float32)


def packed_row(slot, part, vector, vectors):
    return (slot * 2 + part) * vectors + vector


def has_neighbour(direction, steps):
    place = lax.axis_index(AXES[direction]) + steps
    inside = (place >= 0) & (place < lax.axis_size(AXES[direction]))
    return jnp.where(inside, 1.0, 0.0).astype(jnp.float32)


def face_kernel(fields_hbm, fields_ref, xf_ref, yf_ref, sems):
    _, vectors, _, nz, nx, ny = fields_ref.shape
    lanes = lax.broadcasted_iota(jnp.int32, (nx, ny), 1)
    copies = [
        pltpu.make_async_copy(fields_hbm.at[part, :, comp], fields_ref.at[part, :, comp], sems.at[part, comp])
        for comp in (0, 2, 1) for part in range(2)
    ]
    for copy in copies:
        copy.start()
    packed = [jnp.zeros((nx, ny), jnp.float32)] * nz
    for place, comp in enumerate((0, 2)):
        for part in range(2):
            copies[2 * place + part].wait()
            for a in range(vectors):
                row = packed_row(comp // 2, part, a, vectors)
                for z in range(nz):
                    value = fields_ref[part, a, comp, z]
                    packed[z] = jnp.where(lanes == row, pltpu.roll(value, row, 1) if row else value, packed[z])
    turned = jnp.concatenate(packed, axis=0).T
    yf_ref[...] = turned[:yf_ref.shape[0]]
    for part in range(2):
        for a in range(vectors):
            xf_ref[part, a, 1] = fields_ref[part, a, 2, :, 0, :]
    for part in range(2):
        copies[4 + part].wait()
        for a in range(vectors):
            xf_ref[part, a, 0] = fields_ref[part, a, 1, :, 0, :]


def rotated(coeffs_ref, old, b):
    new = None
    for a, value in enumerate(old):
        term = cmul((coeffs_ref[0, a, b], coeffs_ref[1, a, b]), value)
        new = term if new is None else add(new, term)
    return new


SUB = 8
SHX, SEX, SHY, SEY = range(0, 8, 2)


def field_of(ref, b, comp, z, cut):
    return tuple(ref[part, b, comp, z, cut] for part in range(2))


def tiles_of(nx):
    return [slice(SUB * t, SUB * (t + 1)) for t in range(nx // SUB)]


def prepare_kernel(
    pml_ref, eps_real_ref, eps_loss_ref, coeffs_ref, fields_ref, material_ref,
    basis_ref, loss_ref, h_ref, packed_ref, table_ref, sz_ref,
):
    _, vectors, _, nz, nx, ny = fields_ref.shape
    plane = (nx, ny)
    parts = range(2)
    for slot, direction, half, count, dim in (
        (SHX, 1, 0.5, nx, 0), (SEX, 1, 0.0, nx, 0), (SHY, 2, 0.5, ny, 1), (SEY, 2, 0.0, ny, 1),
    ):
        values = axis_stretch(pml_ref, direction, count, local_places(direction, count, plane, dim) + half)
        for part in parts:
            table_ref[slot + part] = values[part]
    for slot, half in ((0, 0.0), (2, 0.5)):
        values = axis_stretch(pml_ref, 0, nz, local_places(0, nz, (nz, ny), 0) + half)
        for part in parts:
            sz_ref[slot + part] = values[part]

    @pl.loop(0, nz)
    def _(z):
        material = material_ref[z]
        eps = []
        for source in (eps_real_ref, eps_loss_ref):
            value = jnp.zeros(plane, jnp.float32)
            for number in range(source.shape[0]):
                value = jnp.where(material == number, -OMEGA_SQ * source[number], value)
            eps.append(value)
        for comp in range(3):
            old = [(fields_ref[0, a, comp, z], fields_ref[1, a, comp, z]) for a in range(vectors)]
            for b in range(vectors):
                new = rotated(coeffs_ref, old, b)
                loss = cmul(eps, new)
                for part in parts:
                    basis_ref[part, b, comp, z] = new[part]
                    loss_ref[part, b, comp, z] = loss[part]
        packed_ref[z] = jnp.zeros(plane, jnp.float32)

    tile = (SUB, ny)
    rows = lax.broadcasted_iota(jnp.int32, tile, 0)
    lanes = lax.broadcasted_iota(jnp.int32, tile, 1)
    cuts = tiles_of(nx)

    def magnetic(b, z, last):
        shz = tuple(sz_ref[2 + part, pl.ds(z, 1)] for part in parts)
        for cut in cuts:
            u = [field_of(basis_ref, b, comp, z, cut) for comp in range(3)]

            def step_z(comp):
                if last:
                    return tuple(-value for value in u[comp])
                return sub(field_of(basis_ref, b, comp, z + 1, cut), u[comp])

            def step_x(comp):
                if cut.stop < nx:
                    ahead = field_of(basis_ref, b, comp, z, slice(cut.start + 1, cut.stop + 1))
                else:
                    ahead = tuple(jnp.where(rows == SUB - 1, 0.0, pltpu.roll(value, SUB - 1, 0)) for value in u[comp])
                return sub(ahead, u[comp])

            def step_y(comp):
                ahead = tuple(jnp.where(lanes == ny - 1, 0.0, pltpu.roll(value, ny - 1, 1)) for value in u[comp])
                return sub(ahead, u[comp])

            shx = tuple(table_ref[SHX + part, cut] for part in parts)
            shy = tuple(table_ref[SHY + part, cut] for part in parts)
            h = (
                sub(cmul(shy, step_y(2)), cmul(shz, step_z(1))),
                sub(cmul(shz, step_z(0)), cmul(shx, step_x(2))),
                sub(cmul(shx, step_x(1)), cmul(shy, step_y(0))),
            )
            for comp in range(3):
                for part in parts:
                    h_ref[part, b, comp, z, cut] = h[comp][part]
            packed = packed_ref[z, cut]
            for slot, value in enumerate((h[2], h[0])):
                for part in parts:
                    row = packed_row(slot, part, b, vectors)
                    packed = jnp.where(lanes == row, pltpu.roll(value[part], (row + 1) % ny, 1), packed)
            packed_ref[z, cut] = packed

    @pl.loop(0, nz - 1)
    def _(z):
        for b in range(vectors):
            magnetic(b, z, False)

    for b in range(vectors):
        magnetic(b, nz - 1, True)


def turn_face(coeffs_ref, direction, raw_ref, face_ref):
    inside = has_neighbour(direction, 1)
    vectors = raw_ref.shape[1]
    for slot in range(2):
        old = [(raw_ref[0, a, slot] * inside, raw_ref[1, a, slot] * inside) for a in range(vectors)]
        for b in range(vectors):
            new = rotated(coeffs_ref, old, b)
            for part in range(2):
                face_ref[part, b, slot] = new[part]


def turn_column(coeffs_ref, raw_ref, rows_ref):
    vectors = coeffs_ref.shape[1]
    inside = has_neighbour(2, 1)
    both = 2 * vectors
    shape = (both, raw_ref.shape[1])
    which = lax.broadcasted_iota(jnp.int32, shape, 0)
    turned = [jnp.zeros(shape, jnp.float32)] * 2
    for part in range(2):
        for a in range(vectors):
            column = jnp.zeros(shape, jnp.float32)
            for b in range(vectors):
                first, second = coeffs_ref[0, a, b] * inside, coeffs_ref[1, a, b] * inside
                if part:
                    first, second = -second, first
                column = jnp.where(which == b, first, column)
                column = jnp.where(which == vectors + b, second, column)
            for slot in range(2):
                row = packed_row(slot, part, a, vectors)
                turned[slot] = turned[slot] + column * raw_ref[row:row + 1]
    for slot in range(2):
        rows_ref[slot * both:(slot + 1) * both] = turned[slot]


def lane_to_last(values, slot, part, b, vectors):
    ny = values.shape[-1]
    lanes = lax.broadcasted_iota(jnp.int32, values.shape, 1)
    row = packed_row(slot, part, b, vectors)
    return jnp.where(lanes == ny - 1, pltpu.roll(values, ny - 1 - row, 1), 0.0)


def with_halos(h, b, z, cut, nx, xadd_ref, yadd_ref):
    vectors = xadd_ref.shape[1]
    column = yadd_ref[z, cut]
    hx = tuple(h[0][part] + lane_to_last(column, 1, part, b, vectors) for part in range(2))
    hz = tuple(h[2][part] + lane_to_last(column, 0, part, b, vectors) for part in range(2))
    hy = h[1]
    if cut.stop == nx:
        rows = lax.broadcasted_iota(jnp.int32, column.shape, 0)

        def row_of(slot):
            return tuple(
                jnp.where(rows == SUB - 1, xadd_ref[part, b, slot, pl.ds(z, 1)], 0.0) for part in range(2)
            )

        hy, hz = add(hy, row_of(0)), add(hz, row_of(1))
    return hx, hy, hz


def slab_kernel(
    pml_ref, coeffs_ref, basis_ref, h_in, raw_xf_ref, raw_yf_ref,
    h_ref, xf_ref, yt_ref, xadd_ref, yadd_ref, zf_ref,
):
    del h_in
    _, vectors, _, nz, nx, ny = basis_ref.shape
    parts = range(2)
    cells = nz * nx
    both = 2 * vectors
    turn_face(coeffs_ref, 1, raw_xf_ref, xf_ref)
    turn_column(coeffs_ref, raw_yf_ref, yt_ref)
    shx = axis_stretch(pml_ref, 1, nx, one_place(1, nx, nx - 1, (1, ny)) + 0.5)
    shy = axis_stretch(pml_ref, 2, ny, one_place(2, ny, ny - 1, (1, cells)) + 0.5)
    for b in range(vectors):
        for slot in range(2):
            value = cmul(shx, tuple(xf_ref[part, b, 1 - slot] for part in parts))
            for part in parts:
                xadd_ref[part, b, slot] = value[part] if slot else -value[part]
    added = []
    for slot in range(2):
        value = cmul(shy, (yt_ref[slot * both:slot * both + vectors], yt_ref[slot * both + vectors:(slot + 1) * both]))
        added += [part if slot else -part for part in value]
    rest = jnp.zeros((ny - 2 * both, cells), jnp.float32)
    yadd_ref[...] = jnp.concatenate(added + [rest], axis=0).T.reshape(nz, nx, ny)
    last = nz - 1
    lower = jnp.full((SUB, ny), lax.axis_index(AXES[0]), jnp.int32) == 0
    for b in range(vectors):
        for cut in tiles_of(nx):
            h = [field_of(h_ref, b, comp, last, cut) for comp in range(3)]
            h = with_halos(h, b, last, cut, nx, xadd_ref, yadd_ref)
            for part in parts:
                for comp in range(3):
                    h_ref[part, b, comp, last, cut] = h[comp][part]
                for comp in range(2):
                    zf_ref[part, b, comp, cut] = jnp.where(lower, h[comp][part], basis_ref[part, b, comp, 0, cut])


def plane_step(
    b, z, before, sums, ritz_ref, basis_ref, loss_ref, table_ref, sz_ref, h_ref, left_ref, halos=None
):
    _, vectors, _, _, nx, ny = basis_ref.shape
    rows = lax.broadcasted_iota(jnp.int32, (SUB, ny), 0)
    lanes = lax.broadcasted_iota(jnp.int32, (SUB, ny), 1)
    parts = range(2)
    cuts = tiles_of(nx)
    sez = tuple(sz_ref[part, pl.ds(z, 1)] for part in parts)
    fields = []
    for cut in cuts:
        h = [field_of(h_ref, b, comp, z, cut) for comp in range(3)]
        if halos is not None:
            h = with_halos(h, b, z, cut, nx, *halos)
            for comp in (1, 2):
                for part in parts:
                    h_ref[part, b, comp, z, cut] = h[comp][part]
        fields.append(h)
    sums = list(sums)
    for t, cut in enumerate(cuts):
        hx, hy, hz = fields[t]

        def back_x(comp):
            here = fields[t][comp]
            if t:
                past = field_of(h_ref, b, comp, z, slice(cut.start - 1, cut.stop - 1))
            else:
                past = tuple(jnp.where(rows == 0, 0.0, pltpu.roll(value, 1, 0)) for value in here)
            return sub(here, past)

        def back_y(value):
            return sub(value, tuple(jnp.where(lanes == 0, 0.0, pltpu.roll(part, 1, 1)) for part in value))

        sex = tuple(table_ref[SEX + part, cut] for part in parts)
        sey = tuple(table_ref[SEY + part, cut] for part in parts)
        bxy, bxz = (cmul(sex, back_x(comp)) for comp in (1, 2))
        byz, byx = (cmul(sey, back_y(value)) for value in (hz, hx))
        bzx, bzy = (cmul(sez, sub(value, past)) for value, past in zip((hx, hy), before[t]))
        curl = (sub(byz, bzy), sub(bzx, bxz), sub(bxy, byx))
        w = [add(curl[comp], field_of(loss_ref, b, comp, z, cut)) for comp in range(3)]
        for comp in range(3):
            left = sub(w[comp], cmul((ritz_ref[0, b], ritz_ref[1, b]), field_of(basis_ref, b, comp, z, cut)))
            for part in parts:
                left_ref[part, b, comp, z, cut] = left[part]
        for a in range(vectors):
            total = sums[a]
            for comp in range(3):
                total = add(total, cmul(field_of(basis_ref, a, comp, z, cut), w[comp]))
            sums[a] = total
    return [(h[0], h[1]) for h in fields], sums


def inner_kernel(
    ritz_ref, basis_ref, loss_ref, table_ref, sz_ref, h_in, packed_in, xadd_ref, yadd_ref,
    h_ref, packed_ref, left_ref, acc_ref, before_ref, hxf_ref, basis_hbm, sem,
):
    del h_in, packed_in
    _, vectors, _, nz, nx, ny = basis_ref.shape
    keep = pltpu.make_async_copy(basis_ref, basis_hbm, sem)
    keep.start()
    cuts = tiles_of(nx)
    lanes = lax.broadcasted_iota(jnp.int32, (nz, ny), 1)
    open_plane = lax.broadcasted_iota(jnp.int32, (nz, ny), 0) < nz - 1
    packed_ref[...] = packed_ref[...] + yadd_ref[...]
    corner = packed_ref[:, nx - 1, :]
    for b in range(vectors):
        for part in range(2):
            row = packed_row(0, part, b, vectors)
            more = xadd_ref[part, b, 1]
            corner = corner + jnp.where(lanes == row, pltpu.roll(more, (row + 1) % ny, 1), 0.0)
            more = more + lane_to_last(yadd_ref[:, nx - 1, :], 0, part, b, vectors)
            hxf_ref[part, b, 0] = h_ref[part, b, 1, :, nx - 1, :] + jnp.where(open_plane, xadd_ref[part, b, 0], 0.0)
            hxf_ref[part, b, 1] = h_ref[part, b, 2, :, nx - 1, :] + jnp.where(open_plane, more, 0.0)
    packed_ref[:, nx - 1, :] = corner
    acc_ref[...] = jnp.zeros(acc_ref.shape, jnp.float32)
    before_ref[...] = jnp.zeros(before_ref.shape, jnp.float32)

    @pl.loop(0, nz - 1)
    def _(z):
        for b in range(vectors):
            before = [
                tuple(tuple(before_ref[part, b, slot, cut] for part in range(2)) for slot in range(2)) for cut in cuts
            ]
            sums = [(acc_ref[b, a], acc_ref[b, vectors + a]) for a in range(vectors)]
            before, sums = plane_step(
                b, z, before, sums, ritz_ref, basis_ref, loss_ref, table_ref, sz_ref, h_ref, left_ref, (xadd_ref, yadd_ref)
            )
            for part in range(2):
                for a in range(vectors):
                    acc_ref[b, part * vectors + a] = sums[a][part]
                for t, cut in enumerate(cuts):
                    for slot in range(2):
                        before_ref[part, b, slot, cut] = before[t][slot][part]

    keep.wait()


def last_plane_kernel(sz_ref, zf_ref, h_in, packed_in, hxf_in, h_ref, hxf_ref, hyf_ref):
    del h_in, hxf_in
    _, vectors, _, nz, nx, ny = h_ref.shape
    parts = range(2)
    last = nz - 1
    lanes = lax.broadcasted_iota(jnp.int32, (SUB, ny), 1)
    shz = tuple(sz_ref[2 + part, last:] * has_neighbour(0, 1) for part in parts)
    packed = [packed_in[last, cut] for cut in tiles_of(nx)]
    for b in range(vectors):
        for t, cut in enumerate(tiles_of(nx)):
            ex, ey = (tuple(zf_ref[part, b, slot, cut] for part in parts) for slot in range(2))
            more = (tuple(-value for value in cmul(shz, ey)), cmul(shz, ex))
            for part in parts:
                for comp in range(2):
                    h_ref[part, b, comp, last, cut] = h_ref[part, b, comp, last, cut] + more[comp][part]
                row = packed_row(1, part, b, vectors)
                edge = pltpu.roll(more[0][part], (row + 1) % ny, 1)
                packed[t] = packed[t] + jnp.where(lanes == row, edge, 0.0)
                if cut.stop == nx:
                    hxf_ref[part, b, 0, last:] = hxf_ref[part, b, 0, last:] + more[1][part][SUB - 1:]
    inner = packed_in[:last].reshape(last * nx, ny)
    hyf_ref[...] = jnp.concatenate([inner] + packed, axis=0).T[:hyf_ref.shape[0]]


def outer_kernel(
    pml_ref, ritz_ref, basis_ref, loss_ref, table_ref, sz_ref, h_ref, zf_ref, xf_ref, yt_ref, hxf_ref, hyf_ref,
    left_in, acc_ref, before_ref, left_ref, gram_ref,
):
    del left_in
    _, vectors, _, nz, nx, ny = basis_ref.shape
    parts = range(2)
    cuts = tiles_of(nx)
    under = axis_stretch(pml_ref, 0, nz, one_place(0, nz, -1, (1, ny)) + 0.5)
    sez = tuple(sz_ref[part, 0:1] * has_neighbour(0, -1) for part in parts)
    sx_next = axis_stretch(pml_ref, 1, nx, one_place(1, nx, nx, (1, ny)))
    sy_next = axis_stretch(pml_ref, 2, ny, one_place(2, ny, ny, (1, nz * nx)))
    both = 2 * vectors
    ends = [
        cmul(sy_next, (yt_ref[slot * both:slot * both + vectors], yt_ref[slot * both + vectors:(slot + 1) * both]))
        for slot in range(2)
    ]
    columns = lax.broadcasted_iota(jnp.int32, (both, ny), 1)
    gram = jnp.zeros((both, ny), jnp.float32)
    for b in range(vectors):

        def tile_of(ref, slot, cut, b=b):
            return tuple(ref[part, b, slot, cut] for part in parts)

        before = [tuple(tile_of(before_ref, slot, cut) for slot in range(2)) for cut in cuts]
        sums = [(acc_ref[b, a], acc_ref[b, vectors + a]) for a in range(vectors)]
        _, sums = plane_step(
            b, nz - 1, before, sums, ritz_ref, basis_ref, loss_ref, table_ref, sz_ref, h_ref, left_ref
        )
        for cut in cuts:
            ex, ey = (field_of(basis_ref, b, comp, 0, cut) for comp in range(2))
            hx = sub(tile_of(zf_ref, 0, cut), cmul(under, ey))
            hy = add(tile_of(zf_ref, 1, cut), cmul(under, ex))
            more = (cmul(sez, hy), cmul(sez, hx))
            for part in parts:
                left_ref[part, b, 0, 0, cut] = left_ref[part, b, 0, 0, cut] + more[0][part]
                left_ref[part, b, 1, 0, cut] = left_ref[part, b, 1, 0, cut] - more[1][part]
            for a in range(vectors):
                ex, ey = (field_of(basis_ref, a, comp, 0, cut) for comp in range(2))
                sums[a] = add(sums[a], sub(cmul(ex, more[0]), cmul(ey, more[1])))
        h_y = tuple(hxf_ref[part, b, 0] for part in parts)
        h_z = tuple(hxf_ref[part, b, 1] for part in parts)
        for a in range(vectors):
            over = cmul(tuple(xf_ref[part, a, 0] for part in parts), h_z)
            over = sub(over, cmul(tuple(xf_ref[part, a, 1] for part in parts), h_y))
            over = cmul(sx_next, over)
            for row in range(0, nz, SUB):
                sums[a] = add(sums[a], tuple(part[row:row + SUB] for part in over))
        flat = jnp.concatenate(
            [jnp.sum(sums[a][part], axis=0, keepdims=True) for part in parts for a in range(vectors)], axis=0
        )
        over = None
        for slot in range(2):
            h = tuple(hyf_ref[packed_row(slot, part, b, vectors)][None] for part in parts)
            term = cmul(ends[slot], h)
            over = term if over is None else sub(term, over)
        side = jnp.concatenate(over, axis=0)
        total = jnp.sum(flat, axis=1, keepdims=True) + jnp.sum(side, axis=1, keepdims=True)
        gram = jnp.where(columns == b, total, gram)
    everywhere = 3.0 * nz * nx * ny
    for axis in AXES:
        everywhere = everywhere * lax.axis_size(axis)
    gram = gram * (1.0 / everywhere)
    row = tree_sum([gram[0:1]] + [pltpu.roll(gram[row:row + 1], row * vectors, 1) for row in range(1, both)])
    for device in range(gram_ref.shape[0]):
        gram_ref[device] = row


def tree_sum(values):
    while len(values) > 1:
        pairs = [values[place] + values[place + 1] for place in range(0, len(values) - 1, 2)]
        values = pairs + ([values[-1]] if len(values) % 2 else [])
    return values[0]


def gather_kernel(rows_ref, gram_ref):
    vectors = gram_ref.shape[1]
    total = tree_sum([rows_ref[device] for device in range(rows_ref.shape[0])])
    count = total.shape[1]
    for part in range(2):
        for a in range(vectors):
            row = (part * vectors + a) * vectors
            turned = pltpu.roll(total, count - row, 1) if row else total
            gram_ref[part, a:a + 1] = turned[:, :vectors]


def rim_kernel(pml_ref, left_in, hxf_ref, hyf_ref, left_ref, residual_hbm, xadd_ref, yadd_ref, sems):
    del left_in
    _, vectors, _, nz, nx, ny = left_ref.shape
    parts = range(2)
    both = 2 * vectors
    sex = axis_stretch(pml_ref, 1, nx, one_place(1, nx, 0, (nz, ny)))
    sex = tuple(part * has_neighbour(1, -1) for part in sex)
    sey = axis_stretch(pml_ref, 2, ny, one_place(2, ny, 0, (vectors, nz * nx)))
    sey = tuple(part * has_neighbour(2, -1) for part in sey)
    for b in range(vectors):
        for slot in range(2):
            value = cmul(sex, tuple(hxf_ref[part, b, slot] for part in parts))
            for part in parts:
                xadd_ref[part, b, slot] = value[part] if slot else -value[part]
    added = []
    for slot in range(2):
        first = slot * both
        value = cmul(sey, (hyf_ref[first:first + vectors], hyf_ref[first + vectors:first + both]))
        added += [part if slot else -part for part in value]
    rest = jnp.zeros((ny - 2 * both, nz * nx), jnp.float32)
    yadd_ref[...] = jnp.concatenate(added + [rest], axis=0).T.reshape(nz, nx, ny)
    rows = lax.broadcasted_iota(jnp.int32, (SUB, ny), 0)
    lanes = lax.broadcasted_iota(jnp.int32, (SUB, ny), 1)

    def kept(z):
        return pltpu.make_async_copy(left_ref.at[:, :, :, z], residual_hbm.at[:, :, :, z], sems.at[z])

    @pl.loop(0, nz)
    def _(z):
        for cut in tiles_of(nx):
            column = yadd_ref[z, cut]
            for b in range(vectors):
                for part in parts:

                    def turned(slot, b=b, part=part):
                        row = packed_row(slot, part, b, vectors)
                        value = pltpu.roll(column, ny - row, 1) if row else column
                        return jnp.where(lanes == 0, value, 0.0)

                    def row_of(slot, b=b, part=part):
                        return jnp.where(rows == 0, xadd_ref[part, b, slot, pl.ds(z, 1)], 0.0)

                    ex = left_ref[part, b, 0, z, cut] + turned(0)
                    ez = left_ref[part, b, 2, z, cut] + turned(1)
                    if cut.start == 0:
                        left_ref[part, b, 1, z, cut] = left_ref[part, b, 1, z, cut] + row_of(1)
                        ez = ez + row_of(0)
                    left_ref[part, b, 0, z, cut] = ex
                    left_ref[part, b, 2, z, cut] = ez
        kept(z).start()

    @pl.loop(0, nz)
    def _(z):
        kept(z).wait()


def body(fields, material, pml_width, eps_real, eps_loss, coeffs, ritz):
    _, vectors, _, nz, nx, ny = fields.shape
    f32 = lambda *shape: jax.ShapeDtypeStruct(shape, jnp.float32)
    scratch = lambda *shape: pltpu.VMEM(shape, jnp.float32)
    params = pltpu.CompilerParams(vmem_limit_bytes=40 * 1024 * 1024)
    whole = f32(*fields.shape)
    zf_shape = (2, vectors, 2, nx, ny)
    xf_shape = (2, vectors, 2, nz, ny)
    yf_shape = (4 * vectors, nz * nx)
    near, xf, yf = pl.pallas_call(
        face_kernel,
        out_shape=(whole, f32(*xf_shape), f32(*yf_shape)),
        in_specs=[HBM],
        out_specs=(VMEM,) * 3,
        scratch_shapes=[pltpu.SemaphoreType.DMA((2, 3))],
        compiler_params=params,
        name="take_faces",
    )(pltpu.with_memory_space_constraint(fields, pltpu.HBM))
    xf = passed_round(xf, "gx", -1)
    yf = passed_round(yf, "gy", -1)
    cells = fields.size // 6 // vectors

    def cost(flops, passes):
        return pl.CostEstimate(flops=flops * cells, bytes_accessed=passes * 4 * fields.size, transcendentals=0)

    planes = f32(nz, nx, ny)
    face = f32(*xf_shape)
    basis, loss, h, packed, table, sz = pl.pallas_call(
        prepare_kernel,
        out_shape=(whole, whole, whole, planes, f32(8, nx, ny), f32(4, nz, ny)),
        in_specs=[SMEM] * 4 + [VMEM] * 2,
        out_specs=(VMEM,) * 6,
        compiler_params=params,
        cost_estimate=cost(800, 4),
        name="prepare",
    )(pml_width, eps_real, eps_loss, coeffs, near, material)
    h, xf, yt, xadd, yadd, zf = pl.pallas_call(
        slab_kernel,
        out_shape=(whole, face, f32(*yf_shape), face, planes, f32(*zf_shape)),
        in_specs=[SMEM] * 2 + [VMEM] * 4,
        out_specs=(VMEM,) * 6,
        input_output_aliases={3: 0},
        compiler_params=params,
        name="slab_face",
    )(pml_width, coeffs, basis, h, xf, yf)
    zf = passed_round(zf, "gz", 1)
    h, packed, left, acc, before, hxf, basis_new = pl.pallas_call(
        inner_kernel,
        out_shape=(whole, planes, whole, f32(vectors, 2 * vectors, SUB, ny), f32(*zf_shape), face, whole),
        in_specs=[SMEM] + [VMEM] * 8,
        out_specs=(VMEM,) * 6 + (HBM,),
        scratch_shapes=[pltpu.SemaphoreType.DMA],
        input_output_aliases={5: 0, 6: 1},
        compiler_params=params,
        cost_estimate=cost(800, 2),
        name="apply_inner",
    )(ritz, basis, loss, table, sz, h, packed, xadd, yadd)
    h, hxf, hyf = pl.pallas_call(
        last_plane_kernel,
        out_shape=(whole, face, f32(*yf_shape)),
        in_specs=[VMEM] * 5,
        out_specs=(VMEM,) * 3,
        input_output_aliases={2: 0, 4: 1},
        compiler_params=params,
        name="last_plane",
    )(sz, zf, h, packed, hxf)
    devices = lax.axis_size("gx") * lax.axis_size("gy") * lax.axis_size("gz")
    left, gram = pl.pallas_call(
        outer_kernel,
        out_shape=(whole, pltpu.VMEM((devices, 1, ny), jnp.float32)),
        in_specs=[SMEM] * 2 + [VMEM] * 13,
        out_specs=(VMEM,) * 2,
        input_output_aliases={12: 0},
        compiler_params=params,
        cost_estimate=cost(300, 1),
        name="apply_outer",
    )(pml_width, ritz, basis, loss, table, sz, h, zf, xf, yt, hxf, hyf, left, acc, before)
    gram, hxf, hyf = lax.optimization_barrier((gram, hxf, hyf))
    rows = lax.all_to_all(gram, ("gx", "gy", "gz"), 0, 0)
    from_x = passed_round(hxf, "gx", 1)
    from_y = passed_round(hyf, "gy", 1)
    _, residual = pl.pallas_call(
        rim_kernel,
        out_shape=(whole, whole),
        in_specs=[SMEM] + [VMEM] * 3,
        out_specs=(VMEM, HBM),
        scratch_shapes=[scratch(*xf_shape), scratch(nz, nx, ny), pltpu.SemaphoreType.DMA((nz,))],
        input_output_aliases={1: 0},
        compiler_params=params,
        cost_estimate=pl.CostEstimate(flops=0, bytes_accessed=0, transcendentals=0),
        name="add_rims",
    )(pml_width, left, from_x, from_y)
    rows, residual = lax.optimization_barrier((rows, residual))
    gram = pl.pallas_call(
        gather_kernel,
        out_shape=f32(2, vectors, vectors),
        in_specs=[VMEM],
        out_specs=VMEM,
        compiler_params=params,
        name="sum_rows",
    )(rows)
    return basis_new, residual, gram


def solution(mesh):
    in_specs = (P(None, None, None, "gz", "gx", "gy"), P("gz", "gx", "gy"), P(), P(), P(), P(), P())
    out_specs = (P(None, None, None, "gz", "gx", "gy"), P(None, None, None, "gz", "gx", "gy"), P())
    return jax.shard_map(body, mesh=mesh, in_specs=in_specs, out_specs=out_specs, check_vma=False)
```

```python
import functools

import jax
import jax.numpy as jnp
from jax import lax
from jax.experimental import pallas as pl
from jax.experimental.pallas import tpu as pltpu
from jax.sharding import PartitionSpec as P

OMEGA_SQ = 0.36
SIGMA_TOP = 3.0
BOUNDS = ((4, 5), (0, 1), (2, 3))
AXES = ("gz", "gx", "gy")

VMEM = pl.BlockSpec(memory_space=pltpu.VMEM)
SMEM = pl.BlockSpec(memory_space=pltpu.SMEM)
HBM = pl.BlockSpec(memory_space=pltpu.HBM)


def passed_round(value, axis, steps):
    count = lax.axis_size(axis)
    return lax.ppermute(value, axis, [(source, (source + steps) % count) for source in range(count)])


def inverse_stretch(places, length, low_width, high_width):
    inside_depth = jnp.clip((low_width - places) / low_width, 0.0, 1.0) + jnp.clip(
        (places + 1.0 - length + high_width) / high_width, 0.0, 1.0
    )
    absorb = SIGMA_TOP * inside_depth * inside_depth
    scaled = 1.0 / (1.0 + absorb * absorb)
    return scaled, -absorb * scaled


def cmul(left, right):
    return (left[0] * right[0] - left[1] * right[1], left[0] * right[1] + left[1] * right[0])


def add(left, right):
    return (left[0] + right[0], left[1] + right[1])


def sub(left, right):
    return (left[0] - right[0], left[1] - right[1])


def axis_stretch(pml_ref, direction, count, places):
    total = count * lax.axis_size(AXES[direction])
    low_slot, high_slot = BOUNDS[direction]
    low = jnp.full(places.shape, pml_ref[low_slot], jnp.int32).astype(jnp.float32)
    high = jnp.full(places.shape, pml_ref[high_slot], jnp.int32).astype(jnp.float32)
    return inverse_stretch(places, jnp.float32(total), low, high)


def local_places(direction, count, shape, dim):
    start = lax.axis_index(AXES[direction]) * count
    return (lax.broadcasted_iota(jnp.int32, shape, dim) + start).astype(jnp.float32)


def one_place(direction, count, offset, shape):
    start = lax.axis_index(AXES[direction]) * count + offset
    return jnp.full(shape, start, jnp.int32).astype(jnp.float32)


def packed_row(slot, part, vector, vectors):
    return (slot * 2 + part) * vectors + vector


def has_neighbour(direction, steps):
    place = lax.axis_index(AXES[direction]) + steps
    inside = (place >= 0) & (place < lax.axis_size(AXES[direction]))
    return jnp.where(inside, 1.0, 0.0).astype(jnp.float32)


def face_kernel(fields_hbm, fields_ref, xf_ref, yf_ref, sems):
    _, vectors, _, nz, nx, ny = fields_ref.shape
    lanes = lax.broadcasted_iota(jnp.int32, (nx, ny), 1)
    copies = [
        pltpu.make_async_copy(fields_hbm.at[part, :, comp], fields_ref.at[part, :, comp], sems.at[part, comp])
        for comp in (0, 2, 1) for part in range(2)
    ]
    for copy in copies:
        copy.start()
    packed = [jnp.zeros((nx, ny), jnp.float32)] * nz
    for place, comp in enumerate((0, 2)):
        for part in range(2):
            copies[2 * place + part].wait()
            for a in range(vectors):
                row = packed_row(comp // 2, part, a, vectors)
                for z in range(nz):
                    value = fields_ref[part, a, comp, z]
                    packed[z] = jnp.where(lanes == row, pltpu.roll(value, row, 1) if row else value, packed[z])
    turned = jnp.concatenate(packed, axis=0).T
    yf_ref[...] = turned[:yf_ref.shape[0]]
    for part in range(2):
        for a in range(vectors):
            xf_ref[part, a, 1] = fields_ref[part, a, 2, :, 0, :]
    for part in range(2):
        copies[4 + part].wait()
        for a in range(vectors):
            xf_ref[part, a, 0] = fields_ref[part, a, 1, :, 0, :]


def rotated(coeffs_ref, old, b):
    new = None
    for a, value in enumerate(old):
        term = cmul((coeffs_ref[0, a, b], coeffs_ref[1, a, b]), value)
        new = term if new is None else add(new, term)
    return new


SUB = 8
SHX, SEX, SHY, SEY = range(0, 8, 2)


def field_of(ref, b, comp, z, cut):
    return tuple(ref[part, b, comp, z, cut] for part in range(2))


def tiles_of(nx):
    return [slice(SUB * t, SUB * (t + 1)) for t in range(nx // SUB)]


def prepare_kernel(
    pml_ref, eps_real_ref, eps_loss_ref, coeffs_ref, fields_ref, material_ref,
    basis_ref, loss_ref, h_ref, packed_ref, table_ref, sz_ref,
):
    _, vectors, _, nz, nx, ny = fields_ref.shape
    plane = (nx, ny)
    parts = range(2)
    for slot, direction, half, count, dim in (
        (SHX, 1, 0.5, nx, 0), (SEX, 1, 0.0, nx, 0), (SHY, 2, 0.5, ny, 1), (SEY, 2, 0.0, ny, 1),
    ):
        values = axis_stretch(pml_ref, direction, count, local_places(direction, count, plane, dim) + half)
        for part in parts:
            table_ref[slot + part] = values[part]
    for slot, half in ((0, 0.0), (2, 0.5)):
        values = axis_stretch(pml_ref, 0, nz, local_places(0, nz, (nz, ny), 0) + half)
        for part in parts:
            sz_ref[slot + part] = values[part]

    @pl.loop(0, nz)
    def _(z):
        material = material_ref[z]
        eps = []
        for source in (eps_real_ref, eps_loss_ref):
            value = jnp.zeros(plane, jnp.float32)
            for number in range(source.shape[0]):
                value = jnp.where(material == number, -OMEGA_SQ * source[number], value)
            eps.append(value)
        for comp in range(3):
            old = [(fields_ref[0, a, comp, z], fields_ref[1, a, comp, z]) for a in range(vectors)]
            for b in range(vectors):
                new = rotated(coeffs_ref, old, b)
                loss = cmul(eps, new)
                for part in parts:
                    basis_ref[part, b, comp, z] = new[part]
                    loss_ref[part, b, comp, z] = loss[part]
        packed_ref[z] = jnp.zeros(plane, jnp.float32)

    tile = (SUB, ny)
    rows = lax.broadcasted_iota(jnp.int32, tile, 0)
    lanes = lax.broadcasted_iota(jnp.int32, tile, 1)
    cuts = tiles_of(nx)

    def magnetic(b, z, last):
        shz = tuple(sz_ref[2 + part, pl.ds(z, 1)] for part in parts)
        for cut in cuts:
            u = [field_of(basis_ref, b, comp, z, cut) for comp in range(3)]

            def step_z(comp):
                if last:
                    return tuple(-value for value in u[comp])
                return sub(field_of(basis_ref, b, comp, z + 1, cut), u[comp])

            def step_x(comp):
                if cut.stop < nx:
                    ahead = field_of(basis_ref, b, comp, z, slice(cut.start + 1, cut.stop + 1))
                else:
                    ahead = tuple(jnp.where(rows == SUB - 1, 0.0, pltpu.roll(value, SUB - 1, 0)) for value in u[comp])
                return sub(ahead, u[comp])

            def step_y(comp):
                ahead = tuple(jnp.where(lanes == ny - 1, 0.0, pltpu.roll(value, ny - 1, 1)) for value in u[comp])
                return sub(ahead, u[comp])

            shx = tuple(table_ref[SHX + part, cut] for part in parts)
            shy = tuple(table_ref[SHY + part, cut] for part in parts)
            h = (
                sub(cmul(shy, step_y(2)), cmul(shz, step_z(1))),
                sub(cmul(shz, step_z(0)), cmul(shx, step_x(2))),
                sub(cmul(shx, step_x(1)), cmul(shy, step_y(0))),
            )
            for comp in range(3):
                for part in parts:
                    h_ref[part, b, comp, z, cut] = h[comp][part]
            packed = packed_ref[z, cut]
            for slot, value in enumerate((h[2], h[0])):
                for part in parts:
                    row = packed_row(slot, part, b, vectors)
                    packed = jnp.where(lanes == row, pltpu.roll(value[part], (row + 1) % ny, 1), packed)
            packed_ref[z, cut] = packed

    @pl.loop(0, nz - 1)
    def _(z):
        for b in range(vectors):
            magnetic(b, z, False)

    for b in range(vectors):
        magnetic(b, nz - 1, True)


def turn_face(coeffs_ref, direction, raw_ref, face_ref):
    inside = has_neighbour(direction, 1)
    vectors = raw_ref.shape[1]
    for slot in range(2):
        old = [(raw_ref[0, a, slot] * inside, raw_ref[1, a, slot] * inside) for a in range(vectors)]
        for b in range(vectors):
            new = rotated(coeffs_ref, old, b)
            for part in range(2):
                face_ref[part, b, slot] = new[part]


def turn_column(coeffs_ref, raw_ref, rows_ref):
    vectors = coeffs_ref.shape[1]
    inside = has_neighbour(2, 1)
    both = 2 * vectors
    shape = (both, raw_ref.shape[1])
    which = lax.broadcasted_iota(jnp.int32, shape, 0)
    turned = [jnp.zeros(shape, jnp.float32)] * 2
    for part in range(2):
        for a in range(vectors):
            column = jnp.zeros(shape, jnp.float32)
            for b in range(vectors):
                first, second = coeffs_ref[0, a, b] * inside, coeffs_ref[1, a, b] * inside
                if part:
                    first, second = -second, first
                column = jnp.where(which == b, first, column)
                column = jnp.where(which == vectors + b, second, column)
            for slot in range(2):
                row = packed_row(slot, part, a, vectors)
                turned[slot] = turned[slot] + column * raw_ref[row:row + 1]
    for slot in range(2):
        rows_ref[slot * both:(slot + 1) * both] = turned[slot]


def lane_to_last(values, slot, part, b, vectors):
    ny = values.shape[-1]
    lanes = lax.broadcasted_iota(jnp.int32, values.shape, 1)
    row = packed_row(slot, part, b, vectors)
    return jnp.where(lanes == ny - 1, pltpu.roll(values, ny - 1 - row, 1), 0.0)


def with_halos(h, b, z, cut, nx, xadd_ref, yadd_ref):
    vectors = xadd_ref.shape[1]
    column = yadd_ref[z, cut]
    hx = tuple(h[0][part] + lane_to_last(column, 1, part, b, vectors) for part in range(2))
    hz = tuple(h[2][part] + lane_to_last(column, 0, part, b, vectors) for part in range(2))
    hy = h[1]
    if cut.stop == nx:
        rows = lax.broadcasted_iota(jnp.int32, column.shape, 0)

        def row_of(slot):
            return tuple(
                jnp.where(rows == SUB - 1, xadd_ref[part, b, slot, pl.ds(z, 1)], 0.0) for part in range(2)
            )

        hy, hz = add(hy, row_of(0)), add(hz, row_of(1))
    return hx, hy, hz


def slab_kernel(
    pml_ref, coeffs_ref, basis_ref, h_in, raw_xf_ref, raw_yf_ref,
    h_ref, xf_ref, yt_ref, xadd_ref, yadd_ref, zf_ref,
):
    del h_in
    _, vectors, _, nz, nx, ny = basis_ref.shape
    parts = range(2)
    cells = nz * nx
    both = 2 * vectors
    turn_face(coeffs_ref, 1, raw_xf_ref, xf_ref)
    turn_column(coeffs_ref, raw_yf_ref, yt_ref)
    shx = axis_stretch(pml_ref, 1, nx, one_place(1, nx, nx - 1, (1, ny)) + 0.5)
    shy = axis_stretch(pml_ref, 2, ny, one_place(2, ny, ny - 1, (1, cells)) + 0.5)
    for b in range(vectors):
        for slot in range(2):
            value = cmul(shx, tuple(xf_ref[part, b, 1 - slot] for part in parts))
            for part in parts:
                xadd_ref[part, b, slot] = value[part] if slot else -value[part]
    added = []
    for slot in range(2):
        value = cmul(shy, (yt_ref[slot * both:slot * both + vectors], yt_ref[slot * both + vectors:(slot + 1) * both]))
        added += [part if slot else -part for part in value]
    rest = jnp.zeros((ny - 2 * both, cells), jnp.float32)
    yadd_ref[...] = jnp.concatenate(added + [rest], axis=0).T.reshape(nz, nx, ny)
    last = nz - 1
    lower = jnp.full((SUB, ny), lax.axis_index(AXES[0]), jnp.int32) == 0
    for b in range(vectors):
        for cut in tiles_of(nx):
            h = [field_of(h_ref, b, comp, last, cut) for comp in range(3)]
            h = with_halos(h, b, last, cut, nx, xadd_ref, yadd_ref)
            for part in parts:
                for comp in range(3):
                    h_ref[part, b, comp, last, cut] = h[comp][part]
                for comp in range(2):
                    zf_ref[part, b, comp, cut] = jnp.where(lower, h[comp][part], basis_ref[part, b, comp, 0, cut])


def plane_step(
    b, z, before, sums, ritz_ref, basis_ref, loss_ref, table_ref, sz_ref, h_ref, left_ref, halos=None
):
    _, vectors, _, _, nx, ny = basis_ref.shape
    rows = lax.broadcasted_iota(jnp.int32, (SUB, ny), 0)
    lanes = lax.broadcasted_iota(jnp.int32, (SUB, ny), 1)
    parts = range(2)
    cuts = tiles_of(nx)
    sez = tuple(sz_ref[part, pl.ds(z, 1)] for part in parts)
    fields = []
    for cut in cuts:
        h = [field_of(h_ref, b, comp, z, cut) for comp in range(3)]
        if halos is not None:
            h = with_halos(h, b, z, cut, nx, *halos)
            for comp in (1, 2):
                for part in parts:
                    h_ref[part, b, comp, z, cut] = h[comp][part]
        fields.append(h)
    sums = list(sums)
    for t, cut in enumerate(cuts):
        hx, hy, hz = fields[t]

        def back_x(comp):
            here = fields[t][comp]
            if t:
                past = field_of(h_ref, b, comp, z, slice(cut.start - 1, cut.stop - 1))
            else:
                past = tuple(jnp.where(rows == 0, 0.0, pltpu.roll(value, 1, 0)) for value in here)
            return sub(here, past)

        def back_y(value):
            return sub(value, tuple(jnp.where(lanes == 0, 0.0, pltpu.roll(part, 1, 1)) for part in value))

        sex = tuple(table_ref[SEX + part, cut] for part in parts)
        sey = tuple(table_ref[SEY + part, cut] for part in parts)
        bxy, bxz = (cmul(sex, back_x(comp)) for comp in (1, 2))
        byz, byx = (cmul(sey, back_y(value)) for value in (hz, hx))
        bzx, bzy = (cmul(sez, sub(value, past)) for value, past in zip((hx, hy), before[t]))
        curl = (sub(byz, bzy), sub(bzx, bxz), sub(bxy, byx))
        w = [add(curl[comp], field_of(loss_ref, b, comp, z, cut)) for comp in range(3)]
        for comp in range(3):
            left = sub(w[comp], cmul((ritz_ref[0, b], ritz_ref[1, b]), field_of(basis_ref, b, comp, z, cut)))
            for part in parts:
                left_ref[part, b, comp, z, cut] = left[part]
        for a in range(vectors):
            total = sums[a]
            for comp in range(3):
                total = add(total, cmul(field_of(basis_ref, a, comp, z, cut), w[comp]))
            sums[a] = total
    return [(h[0], h[1]) for h in fields], sums


def inner_kernel(
    ritz_ref, basis_ref, loss_ref, table_ref, sz_ref, h_in, packed_in, xadd_ref, yadd_ref,
    h_ref, packed_ref, left_ref, acc_ref, before_ref, hxf_ref, basis_hbm, sem,
):
    del h_in, packed_in
    _, vectors, _, nz, nx, ny = basis_ref.shape
    keep = pltpu.make_async_copy(basis_ref, basis_hbm, sem)
    keep.start()
    cuts = tiles_of(nx)
    lanes = lax.broadcasted_iota(jnp.int32, (nz, ny), 1)
    open_plane = lax.broadcasted_iota(jnp.int32, (nz, ny), 0) < nz - 1
    packed_ref[...] = packed_ref[...] + yadd_ref[...]
    corner = packed_ref[:, nx - 1, :]
    for b in range(vectors):
        for part in range(2):
            row = packed_row(0, part, b, vectors)
            more = xadd_ref[part, b, 1]
            corner = corner + jnp.where(lanes == row, pltpu.roll(more, (row + 1) % ny, 1), 0.0)
            more = more + lane_to_last(yadd_ref[:, nx - 1, :], 0, part, b, vectors)
            hxf_ref[part, b, 0] = h_ref[part, b, 1, :, nx - 1, :] + jnp.where(open_plane, xadd_ref[part, b, 0], 0.0)
            hxf_ref[part, b, 1] = h_ref[part, b, 2, :, nx - 1, :] + jnp.where(open_plane, more, 0.0)
    packed_ref[:, nx - 1, :] = corner
    acc_ref[...] = jnp.zeros(acc_ref.shape, jnp.float32)
    before_ref[...] = jnp.zeros(before_ref.shape, jnp.float32)

    @pl.loop(0, nz - 1)
    def _(z):
        for b in range(vectors):
            before = [
                tuple(tuple(before_ref[part, b, slot, cut] for part in range(2)) for slot in range(2)) for cut in cuts
            ]
            sums = [(acc_ref[b, a], acc_ref[b, vectors + a]) for a in range(vectors)]
            before, sums = plane_step(
                b, z, before, sums, ritz_ref, basis_ref, loss_ref, table_ref, sz_ref, h_ref, left_ref, (xadd_ref, yadd_ref)
            )
            for part in range(2):
                for a in range(vectors):
                    acc_ref[b, part * vectors + a] = sums[a][part]
                for t, cut in enumerate(cuts):
                    for slot in range(2):
                        before_ref[part, b, slot, cut] = before[t][slot][part]

    keep.wait()


def last_plane_kernel(sz_ref, zf_ref, h_in, packed_in, hxf_in, h_ref, hxf_ref, hyf_ref):
    del h_in, hxf_in
    _, vectors, _, nz, nx, ny = h_ref.shape
    parts = range(2)
    last = nz - 1
    lanes = lax.broadcasted_iota(jnp.int32, (SUB, ny), 1)
    shz = tuple(sz_ref[2 + part, last:] * has_neighbour(0, 1) for part in parts)
    packed = [packed_in[last, cut] for cut in tiles_of(nx)]
    for b in range(vectors):
        for t, cut in enumerate(tiles_of(nx)):
            ex, ey = (tuple(zf_ref[part, b, slot, cut] for part in parts) for slot in range(2))
            more = (tuple(-value for value in cmul(shz, ey)), cmul(shz, ex))
            for part in parts:
                for comp in range(2):
                    h_ref[part, b, comp, last, cut] = h_ref[part, b, comp, last, cut] + more[comp][part]
                row = packed_row(1, part, b, vectors)
                edge = pltpu.roll(more[0][part], (row + 1) % ny, 1)
                packed[t] = packed[t] + jnp.where(lanes == row, edge, 0.0)
                if cut.stop == nx:
                    hxf_ref[part, b, 0, last:] = hxf_ref[part, b, 0, last:] + more[1][part][SUB - 1:]
    inner = packed_in[:last].reshape(last * nx, ny)
    hyf_ref[...] = jnp.concatenate([inner] + packed, axis=0).T[:hyf_ref.shape[0]]


def outer_kernel(
    pml_ref, ritz_ref, basis_ref, loss_ref, table_ref, sz_ref, h_ref, zf_ref, xf_ref, yt_ref, hxf_ref, hyf_ref,
    left_in, acc_ref, before_ref, left_ref, gram_ref,
):
    del left_in
    _, vectors, _, nz, nx, ny = basis_ref.shape
    parts = range(2)
    cuts = tiles_of(nx)
    under = axis_stretch(pml_ref, 0, nz, one_place(0, nz, -1, (1, ny)) + 0.5)
    sez = tuple(sz_ref[part, 0:1] * has_neighbour(0, -1) for part in parts)
    sx_next = axis_stretch(pml_ref, 1, nx, one_place(1, nx, nx, (1, ny)))
    sy_next = axis_stretch(pml_ref, 2, ny, one_place(2, ny, ny, (1, nz * nx)))
    both = 2 * vectors
    ends = [
        cmul(sy_next, (yt_ref[slot * both:slot * both + vectors], yt_ref[slot * both + vectors:(slot + 1) * both]))
        for slot in range(2)
    ]
    columns = lax.broadcasted_iota(jnp.int32, (both, ny), 1)
    gram = jnp.zeros((both, ny), jnp.float32)
    for b in range(vectors):

        def tile_of(ref, slot, cut, b=b):
            return tuple(ref[part, b, slot, cut] for part in parts)

        before = [tuple(tile_of(before_ref, slot, cut) for slot in range(2)) for cut in cuts]
        sums = [(acc_ref[b, a], acc_ref[b, vectors + a]) for a in range(vectors)]
        _, sums = plane_step(
            b, nz - 1, before, sums, ritz_ref, basis_ref, loss_ref, table_ref, sz_ref, h_ref, left_ref
        )
        for cut in cuts:
            ex, ey = (field_of(basis_ref, b, comp, 0, cut) for comp in range(2))
            hx = sub(tile_of(zf_ref, 0, cut), cmul(under, ey))
            hy = add(tile_of(zf_ref, 1, cut), cmul(under, ex))
            more = (cmul(sez, hy), cmul(sez, hx))
            for part in parts:
                left_ref[part, b, 0, 0, cut] = left_ref[part, b, 0, 0, cut] + more[0][part]
                left_ref[part, b, 1, 0, cut] = left_ref[part, b, 1, 0, cut] - more[1][part]
            for a in range(vectors):
                ex, ey = (field_of(basis_ref, a, comp, 0, cut) for comp in range(2))
                sums[a] = add(sums[a], sub(cmul(ex, more[0]), cmul(ey, more[1])))
        h_y = tuple(hxf_ref[part, b, 0] for part in parts)
        h_z = tuple(hxf_ref[part, b, 1] for part in parts)
        for a in range(vectors):
            over = cmul(tuple(xf_ref[part, a, 0] for part in parts), h_z)
            over = sub(over, cmul(tuple(xf_ref[part, a, 1] for part in parts), h_y))
            over = cmul(sx_next, over)
            for row in range(0, nz, SUB):
                sums[a] = add(sums[a], tuple(part[row:row + SUB] for part in over))
        flat = jnp.concatenate(
            [jnp.sum(sums[a][part], axis=0, keepdims=True) for part in parts for a in range(vectors)], axis=0
        )
        over = None
        for slot in range(2):
            h = tuple(hyf_ref[packed_row(slot, part, b, vectors)][None] for part in parts)
            term = cmul(ends[slot], h)
            over = term if over is None else sub(term, over)
        side = jnp.concatenate(over, axis=0)
        total = jnp.sum(flat, axis=1, keepdims=True) + jnp.sum(side, axis=1, keepdims=True)
        gram = jnp.where(columns == b, total, gram)
    everywhere = 3.0 * nz * nx * ny
    for axis in AXES:
        everywhere = everywhere * lax.axis_size(axis)
    gram = gram * (1.0 / everywhere)
    row = tree_sum([gram[0:1]] + [pltpu.roll(gram[row:row + 1], row * vectors, 1) for row in range(1, both)])
    block = jnp.concatenate([row, jnp.zeros((gram_ref.shape[1] - 1, ny), jnp.float32)], axis=0)
    for device in range(gram_ref.shape[0]):
        gram_ref[device] = block


def tree_sum(values):
    while len(values) > 1:
        pairs = [values[place] + values[place + 1] for place in range(0, len(values) - 1, 2)]
        values = pairs + ([values[-1]] if len(values) % 2 else [])
    return values[0]


def gather_kernel(rows_ref, gram_ref):
    vectors = gram_ref.shape[1]
    total = tree_sum([rows_ref[device] for device in range(rows_ref.shape[0])])[0:1]
    count = total.shape[1]
    for part in range(2):
        for a in range(vectors):
            row = (part * vectors + a) * vectors
            turned = pltpu.roll(total, count - row, 1) if row else total
            gram_ref[part, a:a + 1] = turned[:, :vectors]


def rim_kernel(pml_ref, left_in, hxf_ref, hyf_ref, left_ref, residual_hbm, xadd_ref, yadd_ref, sems):
    del left_in
    _, vectors, _, nz, nx, ny = left_ref.shape
    parts = range(2)
    both = 2 * vectors
    sex = axis_stretch(pml_ref, 1, nx, one_place(1, nx, 0, (nz, ny)))
    sex = tuple(part * has_neighbour(1, -1) for part in sex)
    sey = axis_stretch(pml_ref, 2, ny, one_place(2, ny, 0, (vectors, nz * nx)))
    sey = tuple(part * has_neighbour(2, -1) for part in sey)
    for b in range(vectors):
        for slot in range(2):
            value = cmul(sex, tuple(hxf_ref[part, b, slot] for part in parts))
            for part in parts:
                xadd_ref[part, b, slot] = value[part] if slot else -value[part]
    added = []
    for slot in range(2):
        first = slot * both
        value = cmul(sey, (hyf_ref[first:first + vectors], hyf_ref[first + vectors:first + both]))
        added += [part if slot else -part for part in value]
    rest = jnp.zeros((ny - 2 * both, nz * nx), jnp.float32)
    yadd_ref[...] = jnp.concatenate(added + [rest], axis=0).T.reshape(nz, nx, ny)
    rows = lax.broadcasted_iota(jnp.int32, (SUB, ny), 0)
    lanes = lax.broadcasted_iota(jnp.int32, (SUB, ny), 1)

    def kept(z):
        return pltpu.make_async_copy(left_ref.at[:, :, :, z], residual_hbm.at[:, :, :, z], sems.at[z])

    @pl.loop(0, nz)
    def _(z):
        for cut in tiles_of(nx):
            column = yadd_ref[z, cut]
            for b in range(vectors):
                for part in parts:

                    def turned(slot, b=b, part=part):
                        row = packed_row(slot, part, b, vectors)
                        value = pltpu.roll(column, ny - row, 1) if row else column
                        return jnp.where(lanes == 0, value, 0.0)

                    def row_of(slot, b=b, part=part):
                        return jnp.where(rows == 0, xadd_ref[part, b, slot, pl.ds(z, 1)], 0.0)

                    ex = left_ref[part, b, 0, z, cut] + turned(0)
                    ez = left_ref[part, b, 2, z, cut] + turned(1)
                    if cut.start == 0:
                        left_ref[part, b, 1, z, cut] = left_ref[part, b, 1, z, cut] + row_of(1)
                        ez = ez + row_of(0)
                    left_ref[part, b, 0, z, cut] = ex
                    left_ref[part, b, 2, z, cut] = ez
        kept(z).start()

    @pl.loop(0, nz)
    def _(z):
        kept(z).wait()


def body(fields, material, pml_width, eps_real, eps_loss, coeffs, ritz):
    _, vectors, _, nz, nx, ny = fields.shape
    f32 = lambda *shape: jax.ShapeDtypeStruct(shape, jnp.float32)
    scratch = lambda *shape: pltpu.VMEM(shape, jnp.float32)
    params = pltpu.CompilerParams(vmem_limit_bytes=40 * 1024 * 1024)
    whole = f32(*fields.shape)
    zf_shape = (2, vectors, 2, nx, ny)
    xf_shape = (2, vectors, 2, nz, ny)
    yf_shape = (4 * vectors, nz * nx)
    near, xf, yf = pl.pallas_call(
        face_kernel,
        out_shape=(whole, f32(*xf_shape), f32(*yf_shape)),
        in_specs=[HBM],
        out_specs=(VMEM,) * 3,
        scratch_shapes=[pltpu.SemaphoreType.DMA((2, 3))],
        compiler_params=params,
        name="take_faces",
    )(pltpu.with_memory_space_constraint(fields, pltpu.HBM))
    xf = passed_round(xf, "gx", -1)
    yf = passed_round(yf, "gy", -1)
    cells = fields.size // 6 // vectors

    def cost(flops, passes):
        return pl.CostEstimate(flops=flops * cells, bytes_accessed=passes * 4 * fields.size, transcendentals=0)

    planes = f32(nz, nx, ny)
    face = f32(*xf_shape)
    basis, loss, h, packed, table, sz = pl.pallas_call(
        prepare_kernel,
        out_shape=(whole, whole, whole, planes, f32(8, nx, ny), f32(4, nz, ny)),
        in_specs=[SMEM] * 4 + [VMEM] * 2,
        out_specs=(VMEM,) * 6,
        compiler_params=params,
        cost_estimate=cost(800, 4),
        name="prepare",
    )(pml_width, eps_real, eps_loss, coeffs, near, material)
    h, xf, yt, xadd, yadd, zf = pl.pallas_call(
        slab_kernel,
        out_shape=(whole, face, f32(*yf_shape), face, planes, f32(*zf_shape)),
        in_specs=[SMEM] * 2 + [VMEM] * 4,
        out_specs=(VMEM,) * 6,
        input_output_aliases={3: 0},
        compiler_params=params,
        name="slab_face",
    )(pml_width, coeffs, basis, h, xf, yf)
    zf = passed_round(zf, "gz", 1)
    h, packed, left, acc, before, hxf, basis_new = pl.pallas_call(
        inner_kernel,
        out_shape=(whole, planes, whole, f32(vectors, 2 * vectors, SUB, ny), f32(*zf_shape), face, whole),
        in_specs=[SMEM] + [VMEM] * 8,
        out_specs=(VMEM,) * 6 + (HBM,),
        scratch_shapes=[pltpu.SemaphoreType.DMA],
        input_output_aliases={5: 0, 6: 1},
        compiler_params=params,
        cost_estimate=cost(800, 2),
        name="apply_inner",
    )(ritz, basis, loss, table, sz, h, packed, xadd, yadd)
    h, hxf, hyf = pl.pallas_call(
        last_plane_kernel,
        out_shape=(whole, face, f32(*yf_shape)),
        in_specs=[VMEM] * 5,
        out_specs=(VMEM,) * 3,
        input_output_aliases={2: 0, 4: 1},
        compiler_params=params,
        name="last_plane",
    )(sz, zf, h, packed, hxf)
    devices = lax.axis_size("gx") * lax.axis_size("gy") * lax.axis_size("gz")
    left, gram = pl.pallas_call(
        outer_kernel,
        out_shape=(whole, f32(devices, 4, ny)),
        in_specs=[SMEM] * 2 + [VMEM] * 13,
        out_specs=(VMEM,) * 2,
        input_output_aliases={12: 0},
        compiler_params=params,
        cost_estimate=cost(300, 1),
        name="apply_outer",
    )(pml_width, ritz, basis, loss, table, sz, h, zf, xf, yt, hxf, hyf, left, acc, before)
    gram, hxf, hyf = lax.optimization_barrier((gram, hxf, hyf))
    rows = lax.all_to_all(gram, ("gx", "gy", "gz"), 0, 0)
    from_x = passed_round(hxf, "gx", 1)
    from_y = passed_round(hyf, "gy", 1)
    _, residual = pl.pallas_call(
        rim_kernel,
        out_shape=(whole, whole),
        in_specs=[SMEM] + [VMEM] * 3,
        out_specs=(VMEM, HBM),
        scratch_shapes=[scratch(*xf_shape), scratch(nz, nx, ny), pltpu.SemaphoreType.DMA((nz,))],
        input_output_aliases={1: 0},
        compiler_params=params,
        cost_estimate=pl.CostEstimate(flops=0, bytes_accessed=0, transcendentals=0),
        name="add_rims",
    )(pml_width, left, from_x, from_y)
    rows, residual = lax.optimization_barrier((rows, residual))
    gram = pl.pallas_call(
        gather_kernel,
        out_shape=f32(2, vectors, vectors),
        in_specs=[VMEM],
        out_specs=VMEM,
        compiler_params=params,
        name="sum_rows",
    )(rows)
    return basis_new, residual, gram


def solution(mesh):
    in_specs = (P(None, None, None, "gz", "gx", "gy"), P("gz", "gx", "gy"), P(), P(), P(), P(), P())
    out_specs = (P(None, None, None, "gz", "gx", "gy"), P(None, None, None, "gz", "gx", "gy"), P())
    return jax.shard_map(body, mesh=mesh, in_specs=in_specs, out_specs=out_specs, check_vma=False)
```

```python
import functools

import jax
import jax.numpy as jnp
from jax import lax
from jax.experimental import pallas as pl
from jax.experimental.pallas import tpu as pltpu
from jax.sharding import PartitionSpec as P

OMEGA_SQ = 0.36
SIGMA_TOP = 3.0
BOUNDS = ((4, 5), (0, 1), (2, 3))
AXES = ("gz", "gx", "gy")

VMEM = pl.BlockSpec(memory_space=pltpu.VMEM)
SMEM = pl.BlockSpec(memory_space=pltpu.SMEM)
HBM = pl.BlockSpec(memory_space=pltpu.HBM)


def passed_round(value, axis, steps):
    count = lax.axis_size(axis)
    return lax.ppermute(value, axis, [(source, (source + steps) % count) for source in range(count)])


def passed_along(value, axis, steps):
    count = lax.axis_size(axis)
    leading, last = (max(0, -steps), min(count, count - steps))
    return lax.ppermute(value, axis, [(source, source + steps) for source in range(leading, last)])


def inverse_stretch(places, length, low_width, high_width):
    inside_depth = jnp.clip((low_width - places) / low_width, 0.0, 1.0) + jnp.clip(
        (places + 1.0 - length + high_width) / high_width, 0.0, 1.0
    )
    absorb = SIGMA_TOP * inside_depth * inside_depth
    scaled = 1.0 / (1.0 + absorb * absorb)
    return scaled, -absorb * scaled


def cmul(left, right):
    return (left[0] * right[0] - left[1] * right[1], left[0] * right[1] + left[1] * right[0])


def add(left, right):
    return (left[0] + right[0], left[1] + right[1])


def sub(left, right):
    return (left[0] - right[0], left[1] - right[1])


def axis_stretch(pml_ref, direction, count, places):
    total = count * lax.axis_size(AXES[direction])
    low_slot, high_slot = BOUNDS[direction]
    low = jnp.full(places.shape, pml_ref[low_slot], jnp.int32).astype(jnp.float32)
    high = jnp.full(places.shape, pml_ref[high_slot], jnp.int32).astype(jnp.float32)
    return inverse_stretch(places, jnp.float32(total), low, high)


def local_places(direction, count, shape, dim):
    start = lax.axis_index(AXES[direction]) * count
    return (lax.broadcasted_iota(jnp.int32, shape, dim) + start).astype(jnp.float32)


def one_place(direction, count, offset, shape):
    start = lax.axis_index(AXES[direction]) * count + offset
    return jnp.full(shape, start, jnp.int32).astype(jnp.float32)


def packed_row(slot, part, vector, vectors):
    return (slot * 2 + part) * vectors + vector


def has_neighbour(direction, steps):
    place = lax.axis_index(AXES[direction]) + steps
    inside = (place >= 0) & (place < lax.axis_size(AXES[direction]))
    return jnp.where(inside, 1.0, 0.0).astype(jnp.float32)


def face_kernel(fields_hbm, fields_ref, xf_ref, yf_ref, sems):
    _, vectors, _, nz, nx, ny = fields_ref.shape
    lanes = lax.broadcasted_iota(jnp.int32, (nx, ny), 1)
    copies = [
        pltpu.make_async_copy(fields_hbm.at[part, :, comp], fields_ref.at[part, :, comp], sems.at[part, comp])
        for comp in (0, 2, 1) for part in range(2)
    ]
    for copy in copies:
        copy.start()
    packed = [jnp.zeros((nx, ny), jnp.float32)] * nz
    for place, comp in enumerate((0, 2)):
        for part in range(2):
            copies[2 * place + part].wait()
            for a in range(vectors):
                row = packed_row(comp // 2, part, a, vectors)
                for z in range(nz):
                    value = fields_ref[part, a, comp, z]
                    packed[z] = jnp.where(lanes == row, pltpu.roll(value, row, 1) if row else value, packed[z])
    turned = jnp.concatenate(packed, axis=0).T
    yf_ref[...] = turned[:yf_ref.shape[0]]
    for part in range(2):
        for a in range(vectors):
            xf_ref[part, a, 1] = fields_ref[part, a, 2, :, 0, :]
    for part in range(2):
        copies[4 + part].wait()
        for a in range(vectors):
            xf_ref[part, a, 0] = fields_ref[part, a, 1, :, 0, :]


def rotated(coeffs_ref, old, b):
    new = None
    for a, value in enumerate(old):
        term = cmul((coeffs_ref[0, a, b], coeffs_ref[1, a, b]), value)
        new = term if new is None else add(new, term)
    return new


SUB = 8
SHX, SEX, SHY, SEY = range(0, 8, 2)


def field_of(ref, b, comp, z, cut):
    return tuple(ref[part, b, comp, z, cut] for part in range(2))


def tiles_of(nx):
    return [slice(SUB * t, SUB * (t + 1)) for t in range(nx // SUB)]


def prepare_kernel(
    pml_ref, eps_real_ref, eps_loss_ref, coeffs_ref, fields_ref, material_ref,
    basis_ref, loss_ref, h_ref, packed_ref, table_ref, sz_ref,
):
    _, vectors, _, nz, nx, ny = fields_ref.shape
    plane = (nx, ny)
    parts = range(2)
    for slot, direction, half, count, dim in (
        (SHX, 1, 0.5, nx, 0), (SEX, 1, 0.0, nx, 0), (SHY, 2, 0.5, ny, 1), (SEY, 2, 0.0, ny, 1),
    ):
        values = axis_stretch(pml_ref, direction, count, local_places(direction, count, plane, dim) + half)
        for part in parts:
            table_ref[slot + part] = values[part]
    for slot, half in ((0, 0.0), (2, 0.5)):
        values = axis_stretch(pml_ref, 0, nz, local_places(0, nz, (nz, ny), 0) + half)
        for part in parts:
            sz_ref[slot + part] = values[part]

    @pl.loop(0, nz)
    def _(z):
        material = material_ref[z]
        eps = []
        for source in (eps_real_ref, eps_loss_ref):
            value = jnp.zeros(plane, jnp.float32)
            for number in range(source.shape[0]):
                value = jnp.where(material == number, -OMEGA_SQ * source[number], value)
            eps.append(value)
        for comp in range(3):
            old = [(fields_ref[0, a, comp, z], fields_ref[1, a, comp, z]) for a in range(vectors)]
            for b in range(vectors):
                new = rotated(coeffs_ref, old, b)
                loss = cmul(eps, new)
                for part in parts:
                    basis_ref[part, b, comp, z] = new[part]
                    loss_ref[part, b, comp, z] = loss[part]
        packed_ref[z] = jnp.zeros(plane, jnp.float32)

    tile = (SUB, ny)
    rows = lax.broadcasted_iota(jnp.int32, tile, 0)
    lanes = lax.broadcasted_iota(jnp.int32, tile, 1)
    cuts = tiles_of(nx)

    def magnetic(b, z, last):
        shz = tuple(sz_ref[2 + part, pl.ds(z, 1)] for part in parts)
        for cut in cuts:
            u = [field_of(basis_ref, b, comp, z, cut) for comp in range(3)]

            def step_z(comp):
                if last:
                    return tuple(-value for value in u[comp])
                return sub(field_of(basis_ref, b, comp, z + 1, cut), u[comp])

            def step_x(comp):
                if cut.stop < nx:
                    ahead = field_of(basis_ref, b, comp, z, slice(cut.start + 1, cut.stop + 1))
                else:
                    ahead = tuple(jnp.where(rows == SUB - 1, 0.0, pltpu.roll(value, SUB - 1, 0)) for value in u[comp])
                return sub(ahead, u[comp])

            def step_y(comp):
                ahead = tuple(jnp.where(lanes == ny - 1, 0.0, pltpu.roll(value, ny - 1, 1)) for value in u[comp])
                return sub(ahead, u[comp])

            shx = tuple(table_ref[SHX + part, cut] for part in parts)
            shy = tuple(table_ref[SHY + part, cut] for part in parts)
            h = (
                sub(cmul(shy, step_y(2)), cmul(shz, step_z(1))),
                sub(cmul(shz, step_z(0)), cmul(shx, step_x(2))),
                sub(cmul(shx, step_x(1)), cmul(shy, step_y(0))),
            )
            for comp in range(3):
                for part in parts:
                    h_ref[part, b, comp, z, cut] = h[comp][part]
            packed = packed_ref[z, cut]
            for slot, value in enumerate((h[2], h[0])):
                for part in parts:
                    row = packed_row(slot, part, b, vectors)
                    packed = jnp.where(lanes == row, pltpu.roll(value[part], (row + 1) % ny, 1), packed)
            packed_ref[z, cut] = packed

    @pl.loop(0, nz - 1)
    def _(z):
        for b in range(vectors):
            magnetic(b, z, False)

    for b in range(vectors):
        magnetic(b, nz - 1, True)


def turn_face(coeffs_ref, direction, raw_ref, face_ref):
    inside = has_neighbour(direction, 1)
    vectors = raw_ref.shape[1]
    for slot in range(2):
        old = [(raw_ref[0, a, slot] * inside, raw_ref[1, a, slot] * inside) for a in range(vectors)]
        for b in range(vectors):
            new = rotated(coeffs_ref, old, b)
            for part in range(2):
                face_ref[part, b, slot] = new[part]


def turn_column(coeffs_ref, raw_ref, rows_ref):
    vectors = coeffs_ref.shape[1]
    inside = has_neighbour(2, 1)
    both = 2 * vectors
    shape = (both, raw_ref.shape[1])
    which = lax.broadcasted_iota(jnp.int32, shape, 0)
    turned = [jnp.zeros(shape, jnp.float32)] * 2
    for part in range(2):
        for a in range(vectors):
            column = jnp.zeros(shape, jnp.float32)
            for b in range(vectors):
                first, second = coeffs_ref[0, a, b] * inside, coeffs_ref[1, a, b] * inside
                if part:
                    first, second = -second, first
                column = jnp.where(which == b, first, column)
                column = jnp.where(which == vectors + b, second, column)
            for slot in range(2):
                row = packed_row(slot, part, a, vectors)
                turned[slot] = turned[slot] + column * raw_ref[row:row + 1]
    for slot in range(2):
        rows_ref[slot * both:(slot + 1) * both] = turned[slot]


def lane_to_last(values, slot, part, b, vectors):
    ny = values.shape[-1]
    lanes = lax.broadcasted_iota(jnp.int32, values.shape, 1)
    row = packed_row(slot, part, b, vectors)
    return jnp.where(lanes == ny - 1, pltpu.roll(values, ny - 1 - row, 1), 0.0)


def with_halos(h, b, z, cut, nx, xadd_ref, yadd_ref):
    vectors = xadd_ref.shape[1]
    column = yadd_ref[z, cut]
    hx = tuple(h[0][part] + lane_to_last(column, 1, part, b, vectors) for part in range(2))
    hz = tuple(h[2][part] + lane_to_last(column, 0, part, b, vectors) for part in range(2))
    hy = h[1]
    if cut.stop == nx:
        rows = lax.broadcasted_iota(jnp.int32, column.shape, 0)

        def row_of(slot):
            return tuple(
                jnp.where(rows == SUB - 1, xadd_ref[part, b, slot, pl.ds(z, 1)], 0.0) for part in range(2)
            )

        hy, hz = add(hy, row_of(0)), add(hz, row_of(1))
    return hx, hy, hz


def slab_kernel(
    pml_ref, coeffs_ref, basis_ref, h_in, raw_xf_ref, raw_yf_ref,
    h_ref, xf_ref, yt_ref, xadd_ref, yadd_ref, zf_ref,
):
    del h_in
    _, vectors, _, nz, nx, ny = basis_ref.shape
    parts = range(2)
    cells = nz * nx
    both = 2 * vectors
    turn_face(coeffs_ref, 1, raw_xf_ref, xf_ref)
    turn_column(coeffs_ref, raw_yf_ref, yt_ref)
    shx = axis_stretch(pml_ref, 1, nx, one_place(1, nx, nx - 1, (1, ny)) + 0.5)
    shy = axis_stretch(pml_ref, 2, ny, one_place(2, ny, ny - 1, (1, cells)) + 0.5)
    for b in range(vectors):
        for slot in range(2):
            value = cmul(shx, tuple(xf_ref[part, b, 1 - slot] for part in parts))
            for part in parts:
                xadd_ref[part, b, slot] = value[part] if slot else -value[part]
    added = []
    for slot in range(2):
        value = cmul(shy, (yt_ref[slot * both:slot * both + vectors], yt_ref[slot * both + vectors:(slot + 1) * both]))
        added += [part if slot else -part for part in value]
    rest = jnp.zeros((ny - 2 * both, cells), jnp.float32)
    yadd_ref[...] = jnp.concatenate(added + [rest], axis=0).T.reshape(nz, nx, ny)
    last = nz - 1
    lower = jnp.full((SUB, ny), lax.axis_index(AXES[0]), jnp.int32) == 0
    for b in range(vectors):
        for cut in tiles_of(nx):
            h = [field_of(h_ref, b, comp, last, cut) for comp in range(3)]
            h = with_halos(h, b, last, cut, nx, xadd_ref, yadd_ref)
            for part in parts:
                for comp in range(3):
                    h_ref[part, b, comp, last, cut] = h[comp][part]
                for comp in range(2):
                    zf_ref[part, b, comp, cut] = jnp.where(lower, h[comp][part], basis_ref[part, b, comp, 0, cut])


def plane_step(
    b, z, before, sums, ritz_ref, basis_ref, loss_ref, table_ref, sz_ref, h_ref, left_ref, halos=None
):
    _, vectors, _, _, nx, ny = basis_ref.shape
    rows = lax.broadcasted_iota(jnp.int32, (SUB, ny), 0)
    lanes = lax.broadcasted_iota(jnp.int32, (SUB, ny), 1)
    parts = range(2)
    cuts = tiles_of(nx)
    sez = tuple(sz_ref[part, pl.ds(z, 1)] for part in parts)
    fields = []
    for cut in cuts:
        h = [field_of(h_ref, b, comp, z, cut) for comp in range(3)]
        if halos is not None:
            h = with_halos(h, b, z, cut, nx, *halos)
            for comp in (1, 2):
                for part in parts:
                    h_ref[part, b, comp, z, cut] = h[comp][part]
        fields.append(h)
    sums = list(sums)
    for t, cut in enumerate(cuts):
        hx, hy, hz = fields[t]

        def back_x(comp):
            here = fields[t][comp]
            if t:
                past = field_of(h_ref, b, comp, z, slice(cut.start - 1, cut.stop - 1))
            else:
                past = tuple(jnp.where(rows == 0, 0.0, pltpu.roll(value, 1, 0)) for value in here)
            return sub(here, past)

        def back_y(value):
            return sub(value, tuple(jnp.where(lanes == 0, 0.0, pltpu.roll(part, 1, 1)) for part in value))

        sex = tuple(table_ref[SEX + part, cut] for part in parts)
        sey = tuple(table_ref[SEY + part, cut] for part in parts)
        bxy, bxz = (cmul(sex, back_x(comp)) for comp in (1, 2))
        byz, byx = (cmul(sey, back_y(value)) for value in (hz, hx))
        bzx, bzy = (cmul(sez, sub(value, past)) for value, past in zip((hx, hy), before[t]))
        curl = (sub(byz, bzy), sub(bzx, bxz), sub(bxy, byx))
        w = [add(curl[comp], field_of(loss_ref, b, comp, z, cut)) for comp in range(3)]
        for comp in range(3):
            left = sub(w[comp], cmul((ritz_ref[0, b], ritz_ref[1, b]), field_of(basis_ref, b, comp, z, cut)))
            for part in parts:
                left_ref[part, b, comp, z, cut] = left[part]
        for a in range(vectors):
            total = sums[a]
            for comp in range(3):
                total = add(total, cmul(field_of(basis_ref, a, comp, z, cut), w[comp]))
            sums[a] = total
    return [(h[0], h[1]) for h in fields], sums


def inner_kernel(
    ritz_ref, basis_ref, loss_ref, table_ref, sz_ref, h_in, packed_in, xadd_ref, yadd_ref,
    h_ref, packed_ref, left_ref, acc_ref, before_ref, hxf_ref, basis_hbm, sem,
):
    del h_in, packed_in
    _, vectors, _, nz, nx, ny = basis_ref.shape
    keep = pltpu.make_async_copy(basis_ref, basis_hbm, sem)
    keep.start()
    cuts = tiles_of(nx)
    lanes = lax.broadcasted_iota(jnp.int32, (nz, ny), 1)
    open_plane = lax.broadcasted_iota(jnp.int32, (nz, ny), 0) < nz - 1
    packed_ref[...] = packed_ref[...] + yadd_ref[...]
    corner = packed_ref[:, nx - 1, :]
    for b in range(vectors):
        for part in range(2):
            row = packed_row(0, part, b, vectors)
            more = xadd_ref[part, b, 1]
            corner = corner + jnp.where(lanes == row, pltpu.roll(more, (row + 1) % ny, 1), 0.0)
            more = more + lane_to_last(yadd_ref[:, nx - 1, :], 0, part, b, vectors)
            hxf_ref[part, b, 0] = h_ref[part, b, 1, :, nx - 1, :] + jnp.where(open_plane, xadd_ref[part, b, 0], 0.0)
            hxf_ref[part, b, 1] = h_ref[part, b, 2, :, nx - 1, :] + jnp.where(open_plane, more, 0.0)
    packed_ref[:, nx - 1, :] = corner
    acc_ref[...] = jnp.zeros(acc_ref.shape, jnp.float32)
    before_ref[...] = jnp.zeros(before_ref.shape, jnp.float32)

    @pl.loop(0, nz - 1)
    def _(z):
        for b in range(vectors):
            before = [
                tuple(tuple(before_ref[part, b, slot, cut] for part in range(2)) for slot in range(2)) for cut in cuts
            ]
            sums = [(acc_ref[b, a], acc_ref[b, vectors + a]) for a in range(vectors)]
            before, sums = plane_step(
                b, z, before, sums, ritz_ref, basis_ref, loss_ref, table_ref, sz_ref, h_ref, left_ref, (xadd_ref, yadd_ref)
            )
            for part in range(2):
                for a in range(vectors):
                    acc_ref[b, part * vectors + a] = sums[a][part]
                for t, cut in enumerate(cuts):
                    for slot in range(2):
                        before_ref[part, b, slot, cut] = before[t][slot][part]

    keep.wait()


def last_plane_kernel(sz_ref, zf_ref, h_in, packed_in, hxf_in, h_ref, hxf_ref, hyf_ref):
    del h_in, hxf_in
    _, vectors, _, nz, nx, ny = h_ref.shape
    parts = range(2)
    last = nz - 1
    lanes = lax.broadcasted_iota(jnp.int32, (SUB, ny), 1)
    shz = tuple(sz_ref[2 + part, last:] * has_neighbour(0, 1) for part in parts)
    packed = [packed_in[last, cut] for cut in tiles_of(nx)]
    for b in range(vectors):
        for t, cut in enumerate(tiles_of(nx)):
            ex, ey = (tuple(zf_ref[part, b, slot, cut] for part in parts) for slot in range(2))
            more = (tuple(-value for value in cmul(shz, ey)), cmul(shz, ex))
            for part in parts:
                for comp in range(2):
                    h_ref[part, b, comp, last, cut] = h_ref[part, b, comp, last, cut] + more[comp][part]
                row = packed_row(1, part, b, vectors)
                edge = pltpu.roll(more[0][part], (row + 1) % ny, 1)
                packed[t] = packed[t] + jnp.where(lanes == row, edge, 0.0)
                if cut.stop == nx:
                    hxf_ref[part, b, 0, last:] = hxf_ref[part, b, 0, last:] + more[1][part][SUB - 1:]
    inner = packed_in[:last].reshape(last * nx, ny)
    hyf_ref[...] = jnp.concatenate([inner] + packed, axis=0).T[:hyf_ref.shape[0]]


def outer_kernel(
    pml_ref, ritz_ref, basis_ref, loss_ref, table_ref, sz_ref, h_ref, zf_ref, xf_ref, yt_ref, hxf_ref, hyf_ref,
    left_in, acc_ref, before_ref, left_ref, gram_ref,
):
    del left_in
    _, vectors, _, nz, nx, ny = basis_ref.shape
    parts = range(2)
    cuts = tiles_of(nx)
    under = axis_stretch(pml_ref, 0, nz, one_place(0, nz, -1, (1, ny)) + 0.5)
    sez = tuple(sz_ref[part, 0:1] * has_neighbour(0, -1) for part in parts)
    sx_next = axis_stretch(pml_ref, 1, nx, one_place(1, nx, nx, (1, ny)))
    sy_next = axis_stretch(pml_ref, 2, ny, one_place(2, ny, ny, (1, nz * nx)))
    both = 2 * vectors
    ends = [
        cmul(sy_next, (yt_ref[slot * both:slot * both + vectors], yt_ref[slot * both + vectors:(slot + 1) * both]))
        for slot in range(2)
    ]
    columns = lax.broadcasted_iota(jnp.int32, (both, ny), 1)
    gram = jnp.zeros((both, ny), jnp.float32)
    for b in range(vectors):

        def tile_of(ref, slot, cut, b=b):
            return tuple(ref[part, b, slot, cut] for part in parts)

        before = [tuple(tile_of(before_ref, slot, cut) for slot in range(2)) for cut in cuts]
        sums = [(acc_ref[b, a], acc_ref[b, vectors + a]) for a in range(vectors)]
        _, sums = plane_step(
            b, nz - 1, before, sums, ritz_ref, basis_ref, loss_ref, table_ref, sz_ref, h_ref, left_ref
        )
        for cut in cuts:
            ex, ey = (field_of(basis_ref, b, comp, 0, cut) for comp in range(2))
            hx = sub(tile_of(zf_ref, 0, cut), cmul(under, ey))
            hy = add(tile_of(zf_ref, 1, cut), cmul(under, ex))
            more = (cmul(sez, hy), cmul(sez, hx))
            for part in parts:
                left_ref[part, b, 0, 0, cut] = left_ref[part, b, 0, 0, cut] + more[0][part]
                left_ref[part, b, 1, 0, cut] = left_ref[part, b, 1, 0, cut] - more[1][part]
            for a in range(vectors):
                ex, ey = (field_of(basis_ref, a, comp, 0, cut) for comp in range(2))
                sums[a] = add(sums[a], sub(cmul(ex, more[0]), cmul(ey, more[1])))
        h_y = tuple(hxf_ref[part, b, 0] for part in parts)
        h_z = tuple(hxf_ref[part, b, 1] for part in parts)
        for a in range(vectors):
            over = cmul(tuple(xf_ref[part, a, 0] for part in parts), h_z)
            over = sub(over, cmul(tuple(xf_ref[part, a, 1] for part in parts), h_y))
            over = cmul(sx_next, over)
            for row in range(0, nz, SUB):
                sums[a] = add(sums[a], tuple(part[row:row + SUB] for part in over))
        flat = jnp.concatenate(
            [jnp.sum(sums[a][part], axis=0, keepdims=True) for part in parts for a in range(vectors)], axis=0
        )
        over = None
        for slot in range(2):
            h = tuple(hyf_ref[packed_row(slot, part, b, vectors)][None] for part in parts)
            term = cmul(ends[slot], h)
            over = term if over is None else sub(term, over)
        side = jnp.concatenate(over, axis=0)
        total = jnp.sum(flat, axis=1, keepdims=True) + jnp.sum(side, axis=1, keepdims=True)
        gram = jnp.where(columns == b, total, gram)
    everywhere = 3.0 * nz * nx * ny
    for axis in AXES:
        everywhere = everywhere * lax.axis_size(axis)
    gram = gram * (1.0 / everywhere)
    row = tree_sum([gram[0:1]] + [pltpu.roll(gram[row:row + 1], row * vectors, 1) for row in range(1, both)])
    block = jnp.concatenate([row, jnp.zeros((gram_ref.shape[1] - 1, ny), jnp.float32)], axis=0)
    for device in range(gram_ref.shape[0]):
        gram_ref[device] = block


def tree_sum(values):
    while len(values) > 1:
        pairs = [values[place] + values[place + 1] for place in range(0, len(values) - 1, 2)]
        values = pairs + ([values[-1]] if len(values) % 2 else [])
    return values[0]


def gather_kernel(rows_ref, gram_ref):
    vectors = gram_ref.shape[1]
    total = tree_sum([rows_ref[device] for device in range(rows_ref.shape[0])])[0:1]
    count = total.shape[1]
    for part in range(2):
        for a in range(vectors):
            row = (part * vectors + a) * vectors
            turned = pltpu.roll(total, count - row, 1) if row else total
            gram_ref[part, a:a + 1] = turned[:, :vectors]


def rim_y_kernel(pml_ref, left_in, hyf_ref, left_ref, residual_hbm, yadd_ref, sems):
    del left_in
    _, vectors, _, nz, nx, ny = left_ref.shape
    parts = range(2)
    both = 2 * vectors
    sey = axis_stretch(pml_ref, 2, ny, one_place(2, ny, 0, (vectors, nz * nx)))
    sey = tuple(part * has_neighbour(2, -1) for part in sey)
    added = []
    for slot in range(2):
        first = slot * both
        value = cmul(sey, (hyf_ref[first:first + vectors], hyf_ref[first + vectors:first + both]))
        added += [part if slot else -part for part in value]
    rest = jnp.zeros((ny - 2 * both, nz * nx), jnp.float32)
    yadd_ref[...] = jnp.concatenate(added + [rest], axis=0).T.reshape(nz, nx, ny)
    lanes = lax.broadcasted_iota(jnp.int32, (SUB, ny), 1)

    def kept(z):
        blocks = [(slice(None), slice(None), 0, z)]
        blocks += [(slice(None), slice(None), comp, z, slice(SUB, nx)) for comp in (1, 2)]
        return [
            pltpu.make_async_copy(left_ref.at[block], residual_hbm.at[block], sems.at[place, z])
            for place, block in enumerate(blocks)
        ]

    @pl.loop(0, nz)
    def _(z):
        for cut in tiles_of(nx):
            column = yadd_ref[z, cut]
            for b in range(vectors):
                for part in parts:
                    for slot, comp in enumerate((0, 2)):
                        row = packed_row(slot, part, b, vectors)
                        value = pltpu.roll(column, ny - row, 1) if row else column
                        value = jnp.where(lanes == 0, value, 0.0)
                        left_ref[part, b, comp, z, cut] = left_ref[part, b, comp, z, cut] + value
        for copy in kept(z):
            copy.start()

    @pl.loop(0, nz)
    def _(z):
        for copy in kept(z):
            copy.wait()


def rim_x_kernel(pml_ref, left_in, residual_in, hxf_ref, left_ref, residual_hbm, xadd_ref, sem):
    del left_in, residual_in
    _, vectors, _, nz, nx, ny = left_ref.shape
    parts = range(2)
    sex = axis_stretch(pml_ref, 1, nx, one_place(1, nx, 0, (nz, ny)))
    sex = tuple(part * has_neighbour(1, -1) for part in sex)
    for b in range(vectors):
        for slot in range(2):
            value = cmul(sex, tuple(hxf_ref[part, b, slot] for part in parts))
            for part in parts:
                xadd_ref[part, b, slot] = value[part] if slot else -value[part]
    rows = lax.broadcasted_iota(jnp.int32, (SUB, ny), 0)
    first = slice(0, SUB)
    for z in range(nz):
        for b in range(vectors):
            for part in parts:
                for slot, comp in ((1, 1), (0, 2)):
                    value = jnp.where(rows == 0, xadd_ref[part, b, slot, z:z + 1], 0.0)
                    left_ref[part, b, comp, z, first] = left_ref[part, b, comp, z, first] + value
    block = (slice(None), slice(None), slice(1, 3), slice(None), first)
    copy = pltpu.make_async_copy(left_ref.at[block], residual_hbm.at[block], sem)
    copy.start()
    copy.wait()


def body(fields, material, pml_width, eps_real, eps_loss, coeffs, ritz):
    _, vectors, _, nz, nx, ny = fields.shape
    f32 = lambda *shape: jax.ShapeDtypeStruct(shape, jnp.float32)
    scratch = lambda *shape: pltpu.VMEM(shape, jnp.float32)
    params = pltpu.CompilerParams(vmem_limit_bytes=40 * 1024 * 1024)
    whole = f32(*fields.shape)
    zf_shape = (2, vectors, 2, nx, ny)
    xf_shape = (2, vectors, 2, nz, ny)
    yf_shape = (4 * vectors, nz * nx)
    near, xf, yf = pl.pallas_call(
        face_kernel,
        out_shape=(whole, f32(*xf_shape), f32(*yf_shape)),
        in_specs=[HBM],
        out_specs=(VMEM,) * 3,
        scratch_shapes=[pltpu.SemaphoreType.DMA((2, 3))],
        compiler_params=params,
        name="take_faces",
    )(pltpu.with_memory_space_constraint(fields, pltpu.HBM))
    xf = passed_round(xf, "gx", -1)
    yf = passed_round(yf, "gy", -1)
    cells = fields.size // 6 // vectors

    def cost(flops, passes):
        return pl.CostEstimate(flops=flops * cells, bytes_accessed=passes * 4 * fields.size, transcendentals=0)

    planes = f32(nz, nx, ny)
    face = f32(*xf_shape)
    basis, loss, h, packed, table, sz = pl.pallas_call(
        prepare_kernel,
        out_shape=(whole, whole, whole, planes, f32(8, nx, ny), f32(4, nz, ny)),
        in_specs=[SMEM] * 4 + [VMEM] * 2,
        out_specs=(VMEM,) * 6,
        compiler_params=params,
        cost_estimate=cost(800, 4),
        name="prepare",
    )(pml_width, eps_real, eps_loss, coeffs, near, material)
    h, xf, yt, xadd, yadd, zf = pl.pallas_call(
        slab_kernel,
        out_shape=(whole, face, f32(*yf_shape), face, planes, f32(*zf_shape)),
        in_specs=[SMEM] * 2 + [VMEM] * 4,
        out_specs=(VMEM,) * 6,
        input_output_aliases={3: 0},
        compiler_params=params,
        name="slab_face",
    )(pml_width, coeffs, basis, h, xf, yf)
    zf = passed_round(zf, "gz", 1)
    h, packed, left, acc, before, hxf, basis_new = pl.pallas_call(
        inner_kernel,
        out_shape=(whole, planes, whole, f32(vectors, 2 * vectors, SUB, ny), f32(*zf_shape), face, whole),
        in_specs=[SMEM] + [VMEM] * 8,
        out_specs=(VMEM,) * 6 + (HBM,),
        scratch_shapes=[pltpu.SemaphoreType.DMA],
        input_output_aliases={5: 0, 6: 1},
        compiler_params=params,
        cost_estimate=cost(800, 2),
        name="apply_inner",
    )(ritz, basis, loss, table, sz, h, packed, xadd, yadd)
    h, hxf, hyf = pl.pallas_call(
        last_plane_kernel,
        out_shape=(whole, face, f32(*yf_shape)),
        in_specs=[VMEM] * 5,
        out_specs=(VMEM,) * 3,
        input_output_aliases={2: 0, 4: 1},
        compiler_params=params,
        name="last_plane",
    )(sz, zf, h, packed, hxf)
    devices = lax.axis_size("gx") * lax.axis_size("gy") * lax.axis_size("gz")
    left, gram = pl.pallas_call(
        outer_kernel,
        out_shape=(whole, f32(devices, 4, ny)),
        in_specs=[SMEM] * 2 + [VMEM] * 13,
        out_specs=(VMEM,) * 2,
        input_output_aliases={12: 0},
        compiler_params=params,
        cost_estimate=cost(300, 1),
        name="apply_outer",
    )(pml_width, ritz, basis, loss, table, sz, h, zf, xf, yt, hxf, hyf, left, acc, before)
    gram, hxf, hyf = lax.optimization_barrier((gram, hxf, hyf))
    rows = lax.all_to_all(gram, ("gx", "gy", "gz"), 0, 0)
    from_x = passed_along(hxf, "gx", 1)
    from_y = passed_round(hyf, "gy", 1)
    free = pl.CostEstimate(flops=0, bytes_accessed=0, transcendentals=0)
    left, residual = pl.pallas_call(
        rim_y_kernel,
        out_shape=(whole, whole),
        in_specs=[SMEM] + [VMEM] * 2,
        out_specs=(VMEM, HBM),
        scratch_shapes=[scratch(nz, nx, ny), pltpu.SemaphoreType.DMA((3, nz))],
        input_output_aliases={1: 0},
        compiler_params=params,
        cost_estimate=free,
        name="add_y_rims",
    )(pml_width, left, from_y)
    _, residual = pl.pallas_call(
        rim_x_kernel,
        out_shape=(whole, whole),
        in_specs=[SMEM, VMEM, HBM, VMEM],
        out_specs=(VMEM, HBM),
        scratch_shapes=[scratch(*xf_shape), pltpu.SemaphoreType.DMA],
        input_output_aliases={1: 0, 2: 1},
        compiler_params=params,
        cost_estimate=free,
        name="add_x_rims",
    )(pml_width, left, residual, from_x)
    rows, residual = lax.optimization_barrier((rows, residual))
    gram = pl.pallas_call(
        gather_kernel,
        out_shape=f32(2, vectors, vectors),
        in_specs=[VMEM],
        out_specs=VMEM,
        compiler_params=params,
        name="sum_rows",
    )(rows)
    return basis_new, residual, gram


def solution(mesh):
    in_specs = (P(None, None, None, "gz", "gx", "gy"), P("gz", "gx", "gy"), P(), P(), P(), P(), P())
    out_specs = (P(None, None, None, "gz", "gx", "gy"), P(None, None, None, "gz", "gx", "gy"), P())
    return jax.shard_map(body, mesh=mesh, in_specs=in_specs, out_specs=out_specs, check_vma=False)
```

```python
import functools

import jax
import jax.numpy as jnp
from jax import lax
from jax.experimental import pallas as pl
from jax.experimental.pallas import tpu as pltpu
from jax.sharding import PartitionSpec as P

OMEGA_SQ = 0.36
SIGMA_TOP = 3.0
BOUNDS = ((4, 5), (0, 1), (2, 3))
AXES = ("gz", "gx", "gy")

VMEM = pl.BlockSpec(memory_space=pltpu.VMEM)
SMEM = pl.BlockSpec(memory_space=pltpu.SMEM)
HBM = pl.BlockSpec(memory_space=pltpu.HBM)


def passed_round(value, axis, steps):
    count = lax.axis_size(axis)
    return lax.ppermute(value, axis, [(source, (source + steps) % count) for source in range(count)])


def inverse_stretch(places, length, low_width, high_width):
    inside_depth = jnp.clip((low_width - places) / low_width, 0.0, 1.0) + jnp.clip(
        (places + 1.0 - length + high_width) / high_width, 0.0, 1.0
    )
    absorb = SIGMA_TOP * inside_depth * inside_depth
    scaled = 1.0 / (1.0 + absorb * absorb)
    return scaled, -absorb * scaled


def cmul(left, right):
    return (left[0] * right[0] - left[1] * right[1], left[0] * right[1] + left[1] * right[0])


def add(left, right):
    return (left[0] + right[0], left[1] + right[1])


def sub(left, right):
    return (left[0] - right[0], left[1] - right[1])


def axis_stretch(pml_ref, direction, count, places):
    total = count * lax.axis_size(AXES[direction])
    low_slot, high_slot = BOUNDS[direction]
    low = jnp.full(places.shape, pml_ref[low_slot], jnp.int32).astype(jnp.float32)
    high = jnp.full(places.shape, pml_ref[high_slot], jnp.int32).astype(jnp.float32)
    return inverse_stretch(places, jnp.float32(total), low, high)


def local_places(direction, count, shape, dim):
    start = lax.axis_index(AXES[direction]) * count
    return (lax.broadcasted_iota(jnp.int32, shape, dim) + start).astype(jnp.float32)


def one_place(direction, count, offset, shape):
    start = lax.axis_index(AXES[direction]) * count + offset
    return jnp.full(shape, start, jnp.int32).astype(jnp.float32)


def packed_row(slot, part, vector, vectors):
    return (slot * 2 + part) * vectors + vector


def has_neighbour(direction, steps):
    place = lax.axis_index(AXES[direction]) + steps
    inside = (place >= 0) & (place < lax.axis_size(AXES[direction]))
    return jnp.where(inside, 1.0, 0.0).astype(jnp.float32)


def face_kernel(fields_hbm, fields_ref, xf_ref, yf_ref, sems):
    _, vectors, _, nz, nx, ny = fields_ref.shape
    lanes = lax.broadcasted_iota(jnp.int32, (nx, ny), 1)
    copies = [
        pltpu.make_async_copy(fields_hbm.at[part, :, comp], fields_ref.at[part, :, comp], sems.at[part, comp])
        for comp in (0, 2, 1) for part in range(2)
    ]
    for copy in copies:
        copy.start()
    packed = [jnp.zeros((nx, ny), jnp.float32)] * nz
    for place, comp in enumerate((0, 2)):
        for part in range(2):
            copies[2 * place + part].wait()
            for a in range(vectors):
                row = packed_row(comp // 2, part, a, vectors)
                for z in range(nz):
                    value = fields_ref[part, a, comp, z]
                    packed[z] = jnp.where(lanes == row, pltpu.roll(value, row, 1) if row else value, packed[z])
    turned = jnp.concatenate(packed, axis=0).T
    yf_ref[...] = turned[:yf_ref.shape[0]]
    for part in range(2):
        for a in range(vectors):
            xf_ref[part, a, 1] = fields_ref[part, a, 2, :, 0, :]
    for part in range(2):
        copies[4 + part].wait()
        for a in range(vectors):
            xf_ref[part, a, 0] = fields_ref[part, a, 1, :, 0, :]


def rotated(coeffs_ref, old, b):
    new = None
    for a, value in enumerate(old):
        term = cmul((coeffs_ref[0, a, b], coeffs_ref[1, a, b]), value)
        new = term if new is None else add(new, term)
    return new


SUB = 8
SHX, SEX, SHY, SEY = range(0, 8, 2)


def field_of(ref, b, comp, z, cut):
    return tuple(ref[part, b, comp, z, cut] for part in range(2))


def tiles_of(nx):
    return [slice(SUB * t, SUB * (t + 1)) for t in range(nx // SUB)]


def prepare_kernel(
    pml_ref, eps_real_ref, eps_loss_ref, coeffs_ref, fields_ref, material_ref,
    basis_ref, loss_ref, h_ref, packed_ref, table_ref, sz_ref,
):
    _, vectors, _, nz, nx, ny = fields_ref.shape
    plane = (nx, ny)
    parts = range(2)
    for slot, direction, half, count, dim in (
        (SHX, 1, 0.5, nx, 0), (SEX, 1, 0.0, nx, 0), (SHY, 2, 0.5, ny, 1), (SEY, 2, 0.0, ny, 1),
    ):
        values = axis_stretch(pml_ref, direction, count, local_places(direction, count, plane, dim) + half)
        for part in parts:
            table_ref[slot + part] = values[part]
    for slot, half in ((0, 0.0), (2, 0.5)):
        values = axis_stretch(pml_ref, 0, nz, local_places(0, nz, (nz, ny), 0) + half)
        for part in parts:
            sz_ref[slot + part] = values[part]

    @pl.loop(0, nz)
    def _(z):
        material = material_ref[z]
        eps = []
        for source in (eps_real_ref, eps_loss_ref):
            value = jnp.zeros(plane, jnp.float32)
            for number in range(source.shape[0]):
                value = jnp.where(material == number, -OMEGA_SQ * source[number], value)
            eps.append(value)
        for comp in range(3):
            old = [(fields_ref[0, a, comp, z], fields_ref[1, a, comp, z]) for a in range(vectors)]
            for b in range(vectors):
                new = rotated(coeffs_ref, old, b)
                loss = cmul(eps, new)
                for part in parts:
                    basis_ref[part, b, comp, z] = new[part]
                    loss_ref[part, b, comp, z] = loss[part]
        packed_ref[z] = jnp.zeros(plane, jnp.float32)

    tile = (SUB, ny)
    rows = lax.broadcasted_iota(jnp.int32, tile, 0)
    lanes = lax.broadcasted_iota(jnp.int32, tile, 1)
    cuts = tiles_of(nx)

    def magnetic(b, z, last):
        shz = tuple(sz_ref[2 + part, pl.ds(z, 1)] for part in parts)
        for cut in cuts:
            u = [field_of(basis_ref, b, comp, z, cut) for comp in range(3)]

            def step_z(comp):
                if last:
                    return tuple(-value for value in u[comp])
                return sub(field_of(basis_ref, b, comp, z + 1, cut), u[comp])

            def step_x(comp):
                if cut.stop < nx:
                    ahead = field_of(basis_ref, b, comp, z, slice(cut.start + 1, cut.stop + 1))
                else:
                    ahead = tuple(jnp.where(rows == SUB - 1, 0.0, pltpu.roll(value, SUB - 1, 0)) for value in u[comp])
                return sub(ahead, u[comp])

            def step_y(comp):
                ahead = tuple(jnp.where(lanes == ny - 1, 0.0, pltpu.roll(value, ny - 1, 1)) for value in u[comp])
                return sub(ahead, u[comp])

            shx = tuple(table_ref[SHX + part, cut] for part in parts)
            shy = tuple(table_ref[SHY + part, cut] for part in parts)
            h = (
                sub(cmul(shy, step_y(2)), cmul(shz, step_z(1))),
                sub(cmul(shz, step_z(0)), cmul(shx, step_x(2))),
                sub(cmul(shx, step_x(1)), cmul(shy, step_y(0))),
            )
            for comp in range(3):
                for part in parts:
                    h_ref[part, b, comp, z, cut] = h[comp][part]
            packed = packed_ref[z, cut]
            for slot, value in enumerate((h[2], h[0])):
                for part in parts:
                    row = packed_row(slot, part, b, vectors)
                    packed = jnp.where(lanes == row, pltpu.roll(value[part], (row + 1) % ny, 1), packed)
            packed_ref[z, cut] = packed

    @pl.loop(0, nz - 1)
    def _(z):
        for b in range(vectors):
            magnetic(b, z, False)

    for b in range(vectors):
        magnetic(b, nz - 1, True)


def turn_face(coeffs_ref, direction, raw_ref, face_ref):
    inside = has_neighbour(direction, 1)
    vectors = raw_ref.shape[1]
    for slot in range(2):
        old = [(raw_ref[0, a, slot] * inside, raw_ref[1, a, slot] * inside) for a in range(vectors)]
        for b in range(vectors):
            new = rotated(coeffs_ref, old, b)
            for part in range(2):
                face_ref[part, b, slot] = new[part]


def turn_column(coeffs_ref, raw_ref, rows_ref):
    vectors = coeffs_ref.shape[1]
    inside = has_neighbour(2, 1)
    both = 2 * vectors
    shape = (both, raw_ref.shape[1])
    which = lax.broadcasted_iota(jnp.int32, shape, 0)
    turned = [jnp.zeros(shape, jnp.float32)] * 2
    for part in range(2):
        for a in range(vectors):
            column = jnp.zeros(shape, jnp.float32)
            for b in range(vectors):
                first, second = coeffs_ref[0, a, b] * inside, coeffs_ref[1, a, b] * inside
                if part:
                    first, second = -second, first
                column = jnp.where(which == b, first, column)
                column = jnp.where(which == vectors + b, second, column)
            for slot in range(2):
                row = packed_row(slot, part, a, vectors)
                turned[slot] = turned[slot] + column * raw_ref[row:row + 1]
    for slot in range(2):
        rows_ref[slot * both:(slot + 1) * both] = turned[slot]


def lane_to_last(values, slot, part, b, vectors):
    ny = values.shape[-1]
    lanes = lax.broadcasted_iota(jnp.int32, values.shape, 1)
    row = packed_row(slot, part, b, vectors)
    return jnp.where(lanes == ny - 1, pltpu.roll(values, ny - 1 - row, 1), 0.0)


def with_halos(h, b, z, cut, nx, xadd_ref, yadd_ref):
    vectors = xadd_ref.shape[1]
    column = yadd_ref[z, cut]
    hx = tuple(h[0][part] + lane_to_last(column, 1, part, b, vectors) for part in range(2))
    hz = tuple(h[2][part] + lane_to_last(column, 0, part, b, vectors) for part in range(2))
    hy = h[1]
    if cut.stop == nx:
        rows = lax.broadcasted_iota(jnp.int32, column.shape, 0)

        def row_of(slot):
            return tuple(
                jnp.where(rows == SUB - 1, xadd_ref[part, b, slot, pl.ds(z, 1)], 0.0) for part in range(2)
            )

        hy, hz = add(hy, row_of(0)), add(hz, row_of(1))
    return hx, hy, hz


def slab_kernel(
    pml_ref, coeffs_ref, basis_ref, h_in, raw_xf_ref, raw_yf_ref,
    h_ref, xf_ref, yt_ref, xadd_ref, yadd_ref, zf_ref,
):
    del h_in
    _, vectors, _, nz, nx, ny = basis_ref.shape
    parts = range(2)
    cells = nz * nx
    both = 2 * vectors
    turn_face(coeffs_ref, 1, raw_xf_ref, xf_ref)
    turn_column(coeffs_ref, raw_yf_ref, yt_ref)
    shx = axis_stretch(pml_ref, 1, nx, one_place(1, nx, nx - 1, (1, ny)) + 0.5)
    shy = axis_stretch(pml_ref, 2, ny, one_place(2, ny, ny - 1, (1, cells)) + 0.5)
    for b in range(vectors):
        for slot in range(2):
            value = cmul(shx, tuple(xf_ref[part, b, 1 - slot] for part in parts))
            for part in parts:
                xadd_ref[part, b, slot] = value[part] if slot else -value[part]
    added = []
    for slot in range(2):
        value = cmul(shy, (yt_ref[slot * both:slot * both + vectors], yt_ref[slot * both + vectors:(slot + 1) * both]))
        added += [part if slot else -part for part in value]
    rest = jnp.zeros((ny - 2 * both, cells), jnp.float32)
    yadd_ref[...] = jnp.concatenate(added + [rest], axis=0).T.reshape(nz, nx, ny)
    last = nz - 1
    lower = jnp.full((SUB, ny), lax.axis_index(AXES[0]), jnp.int32) == 0
    for b in range(vectors):
        for cut in tiles_of(nx):
            h = [field_of(h_ref, b, comp, last, cut) for comp in range(3)]
            h = with_halos(h, b, last, cut, nx, xadd_ref, yadd_ref)
            for part in parts:
                for comp in range(3):
                    h_ref[part, b, comp, last, cut] = h[comp][part]
                for comp in range(2):
                    zf_ref[part, b, comp, cut] = jnp.where(lower, h[comp][part], basis_ref[part, b, comp, 0, cut])


def plane_step(
    b, z, before, sums, ritz_ref, basis_ref, loss_ref, table_ref, sz_ref, h_ref, left_ref, halos=None
):
    _, vectors, _, _, nx, ny = basis_ref.shape
    rows = lax.broadcasted_iota(jnp.int32, (SUB, ny), 0)
    lanes = lax.broadcasted_iota(jnp.int32, (SUB, ny), 1)
    parts = range(2)
    cuts = tiles_of(nx)
    sez = tuple(sz_ref[part, pl.ds(z, 1)] for part in parts)
    fields = []
    for cut in cuts:
        h = [field_of(h_ref, b, comp, z, cut) for comp in range(3)]
        if halos is not None:
            h = with_halos(h, b, z, cut, nx, *halos)
            for comp in (1, 2):
                for part in parts:
                    h_ref[part, b, comp, z, cut] = h[comp][part]
        fields.append(h)
    sums = list(sums)
    for t, cut in enumerate(cuts):
        hx, hy, hz = fields[t]

        def back_x(comp):
            here = fields[t][comp]
            if t:
                past = field_of(h_ref, b, comp, z, slice(cut.start - 1, cut.stop - 1))
            else:
                past = tuple(jnp.where(rows == 0, 0.0, pltpu.roll(value, 1, 0)) for value in here)
            return sub(here, past)

        def back_y(value):
            return sub(value, tuple(jnp.where(lanes == 0, 0.0, pltpu.roll(part, 1, 1)) for part in value))

        sex = tuple(table_ref[SEX + part, cut] for part in parts)
        sey = tuple(table_ref[SEY + part, cut] for part in parts)
        bxy, bxz = (cmul(sex, back_x(comp)) for comp in (1, 2))
        byz, byx = (cmul(sey, back_y(value)) for value in (hz, hx))
        bzx, bzy = (cmul(sez, sub(value, past)) for value, past in zip((hx, hy), before[t]))
        curl = (sub(byz, bzy), sub(bzx, bxz), sub(bxy, byx))
        w = [add(curl[comp], field_of(loss_ref, b, comp, z, cut)) for comp in range(3)]
        for comp in range(3):
            left = sub(w[comp], cmul((ritz_ref[0, b], ritz_ref[1, b]), field_of(basis_ref, b, comp, z, cut)))
            for part in parts:
                left_ref[part, b, comp, z, cut] = left[part]
        for a in range(vectors):
            total = sums[a]
            for comp in range(3):
                total = add(total, cmul(field_of(basis_ref, a, comp, z, cut), w[comp]))
            sums[a] = total
    return [(h[0], h[1]) for h in fields], sums


def inner_kernel(
    ritz_ref, basis_ref, loss_ref, table_ref, sz_ref, h_in, packed_in, xadd_ref, yadd_ref,
    h_ref, packed_ref, left_ref, acc_ref, before_ref, hxf_ref, basis_hbm, sem,
):
    del h_in, packed_in
    _, vectors, _, nz, nx, ny = basis_ref.shape
    keep = pltpu.make_async_copy(basis_ref, basis_hbm, sem)
    keep.start()
    cuts = tiles_of(nx)
    lanes = lax.broadcasted_iota(jnp.int32, (nz, ny), 1)
    open_plane = lax.broadcasted_iota(jnp.int32, (nz, ny), 0) < nz - 1
    packed_ref[...] = packed_ref[...] + yadd_ref[...]
    corner = packed_ref[:, nx - 1, :]
    for b in range(vectors):
        for part in range(2):
            row = packed_row(0, part, b, vectors)
            more = xadd_ref[part, b, 1]
            corner = corner + jnp.where(lanes == row, pltpu.roll(more, (row + 1) % ny, 1), 0.0)
            more = more + lane_to_last(yadd_ref[:, nx - 1, :], 0, part, b, vectors)
            hxf_ref[part, b, 0] = h_ref[part, b, 1, :, nx - 1, :] + jnp.where(open_plane, xadd_ref[part, b, 0], 0.0)
            hxf_ref[part, b, 1] = h_ref[part, b, 2, :, nx - 1, :] + jnp.where(open_plane, more, 0.0)
    packed_ref[:, nx - 1, :] = corner
    acc_ref[...] = jnp.zeros(acc_ref.shape, jnp.float32)
    before_ref[...] = jnp.zeros(before_ref.shape, jnp.float32)

    @pl.loop(0, nz - 1)
    def _(z):
        for b in range(vectors):
            before = [
                tuple(tuple(before_ref[part, b, slot, cut] for part in range(2)) for slot in range(2)) for cut in cuts
            ]
            sums = [(acc_ref[b, a], acc_ref[b, vectors + a]) for a in range(vectors)]
            before, sums = plane_step(
                b, z, before, sums, ritz_ref, basis_ref, loss_ref, table_ref, sz_ref, h_ref, left_ref, (xadd_ref, yadd_ref)
            )
            for part in range(2):
                for a in range(vectors):
                    acc_ref[b, part * vectors + a] = sums[a][part]
                for t, cut in enumerate(cuts):
                    for slot in range(2):
                        before_ref[part, b, slot, cut] = before[t][slot][part]

    keep.wait()


def last_plane_kernel(sz_ref, zf_ref, h_in, packed_in, hxf_in, h_ref, hxf_ref, hyf_ref):
    del h_in, hxf_in
    _, vectors, _, nz, nx, ny = h_ref.shape
    parts = range(2)
    last = nz - 1
    lanes = lax.broadcasted_iota(jnp.int32, (SUB, ny), 1)
    shz = tuple(sz_ref[2 + part, last:] * has_neighbour(0, 1) for part in parts)
    packed = [packed_in[last, cut] for cut in tiles_of(nx)]
    for b in range(vectors):
        for t, cut in enumerate(tiles_of(nx)):
            ex, ey = (tuple(zf_ref[part, b, slot, cut] for part in parts) for slot in range(2))
            more = (tuple(-value for value in cmul(shz, ey)), cmul(shz, ex))
            for part in parts:
                for comp in range(2):
                    h_ref[part, b, comp, last, cut] = h_ref[part, b, comp, last, cut] + more[comp][part]
                row = packed_row(1, part, b, vectors)
                edge = pltpu.roll(more[0][part], (row + 1) % ny, 1)
                packed[t] = packed[t] + jnp.where(lanes == row, edge, 0.0)
                if cut.stop == nx:
                    hxf_ref[part, b, 0, last:] = hxf_ref[part, b, 0, last:] + more[1][part][SUB - 1:]
    inner = packed_in[:last].reshape(last * nx, ny)
    hyf_ref[...] = jnp.concatenate([inner] + packed, axis=0).T[:hyf_ref.shape[0]]


def outer_kernel(
    pml_ref, ritz_ref, basis_ref, loss_ref, table_ref, sz_ref, h_ref, zf_ref, xf_ref, yt_ref, hxf_ref, hyf_ref,
    left_in, acc_ref, before_ref, left_ref, gram_ref,
):
    del left_in
    _, vectors, _, nz, nx, ny = basis_ref.shape
    parts = range(2)
    cuts = tiles_of(nx)
    under = axis_stretch(pml_ref, 0, nz, one_place(0, nz, -1, (1, ny)) + 0.5)
    sez = tuple(sz_ref[part, 0:1] * has_neighbour(0, -1) for part in parts)
    sx_next = axis_stretch(pml_ref, 1, nx, one_place(1, nx, nx, (1, ny)))
    sy_next = axis_stretch(pml_ref, 2, ny, one_place(2, ny, ny, (1, nz * nx)))
    both = 2 * vectors
    ends = [
        cmul(sy_next, (yt_ref[slot * both:slot * both + vectors], yt_ref[slot * both + vectors:(slot + 1) * both]))
        for slot in range(2)
    ]
    columns = lax.broadcasted_iota(jnp.int32, (both, ny), 1)
    gram = jnp.zeros((both, ny), jnp.float32)
    for b in range(vectors):

        def tile_of(ref, slot, cut, b=b):
            return tuple(ref[part, b, slot, cut] for part in parts)

        before = [tuple(tile_of(before_ref, slot, cut) for slot in range(2)) for cut in cuts]
        sums = [(acc_ref[b, a], acc_ref[b, vectors + a]) for a in range(vectors)]
        _, sums = plane_step(
            b, nz - 1, before, sums, ritz_ref, basis_ref, loss_ref, table_ref, sz_ref, h_ref, left_ref
        )
        for cut in cuts:
            ex, ey = (field_of(basis_ref, b, comp, 0, cut) for comp in range(2))
            hx = sub(tile_of(zf_ref, 0, cut), cmul(under, ey))
            hy = add(tile_of(zf_ref, 1, cut), cmul(under, ex))
            more = (cmul(sez, hy), cmul(sez, hx))
            for part in parts:
                left_ref[part, b, 0, 0, cut] = left_ref[part, b, 0, 0, cut] + more[0][part]
                left_ref[part, b, 1, 0, cut] = left_ref[part, b, 1, 0, cut] - more[1][part]
            for a in range(vectors):
                ex, ey = (field_of(basis_ref, a, comp, 0, cut) for comp in range(2))
                sums[a] = add(sums[a], sub(cmul(ex, more[0]), cmul(ey, more[1])))
        h_y = tuple(hxf_ref[part, b, 0] for part in parts)
        h_z = tuple(hxf_ref[part, b, 1] for part in parts)
        for a in range(vectors):
            over = cmul(tuple(xf_ref[part, a, 0] for part in parts), h_z)
            over = sub(over, cmul(tuple(xf_ref[part, a, 1] for part in parts), h_y))
            over = cmul(sx_next, over)
            for row in range(0, nz, SUB):
                sums[a] = add(sums[a], tuple(part[row:row + SUB] for part in over))
        flat = jnp.concatenate(
            [jnp.sum(sums[a][part], axis=0, keepdims=True) for part in parts for a in range(vectors)], axis=0
        )
        over = None
        for slot in range(2):
            h = tuple(hyf_ref[packed_row(slot, part, b, vectors)][None] for part in parts)
            term = cmul(ends[slot], h)
            over = term if over is None else sub(term, over)
        side = jnp.concatenate(over, axis=0)
        total = jnp.sum(flat, axis=1, keepdims=True) + jnp.sum(side, axis=1, keepdims=True)
        gram = jnp.where(columns == b, total, gram)
    everywhere = 3.0 * nz * nx * ny
    for axis in AXES:
        everywhere = everywhere * lax.axis_size(axis)
    gram = gram * (1.0 / everywhere)
    row = tree_sum([gram[0:1]] + [pltpu.roll(gram[row:row + 1], row * vectors, 1) for row in range(1, both)])
    block = jnp.concatenate([row, jnp.zeros((gram_ref.shape[1] - 1, ny), jnp.float32)], axis=0)
    for device in range(gram_ref.shape[0]):
        gram_ref[device] = block


def tree_sum(values):
    while len(values) > 1:
        pairs = [values[place] + values[place + 1] for place in range(0, len(values) - 1, 2)]
        values = pairs + ([values[-1]] if len(values) % 2 else [])
    return values[0]


def gather_kernel(rows_ref, gram_ref):
    vectors = gram_ref.shape[1]
    total = tree_sum([rows_ref[device] for device in range(rows_ref.shape[0])])[0:1]
    count = total.shape[1]
    for part in range(2):
        for a in range(vectors):
            row = (part * vectors + a) * vectors
            turned = pltpu.roll(total, count - row, 1) if row else total
            gram_ref[part, a:a + 1] = turned[:, :vectors]


def rim_kernel(pml_ref, left_in, hxf_ref, hyf_ref, left_ref, residual_hbm, xadd_ref, yadd_ref, sems):
    del left_in
    _, vectors, _, nz, nx, ny = left_ref.shape
    parts = range(2)
    both = 2 * vectors
    sex = axis_stretch(pml_ref, 1, nx, one_place(1, nx, 0, (nz, ny)))
    sex = tuple(part * has_neighbour(1, -1) for part in sex)
    sey = axis_stretch(pml_ref, 2, ny, one_place(2, ny, 0, (vectors, nz * nx)))
    sey = tuple(part * has_neighbour(2, -1) for part in sey)
    for b in range(vectors):
        for slot in range(2):
            value = cmul(sex, tuple(hxf_ref[part, b, slot] for part in parts))
            for part in parts:
                xadd_ref[part, b, slot] = value[part] if slot else -value[part]
    added = []
    for slot in range(2):
        first = slot * both
        value = cmul(sey, (hyf_ref[first:first + vectors], hyf_ref[first + vectors:first + both]))
        added += [part if slot else -part for part in value]
    rest = jnp.zeros((ny - 2 * both, nz * nx), jnp.float32)
    yadd_ref[...] = jnp.concatenate(added + [rest], axis=0).T.reshape(nz, nx, ny)
    rows = lax.broadcasted_iota(jnp.int32, (SUB, ny), 0)
    lanes = lax.broadcasted_iota(jnp.int32, (SUB, ny), 1)

    def kept(z):
        return pltpu.make_async_copy(left_ref.at[:, :, :, z], residual_hbm.at[:, :, :, z], sems.at[z])

    @pl.loop(0, nz)
    def _(z):
        for cut in tiles_of(nx):
            column = yadd_ref[z, cut]
            for b in range(vectors):
                for part in parts:

                    def turned(slot, b=b, part=part):
                        row = packed_row(slot, part, b, vectors)
                        value = pltpu.roll(column, ny - row, 1) if row else column
                        return jnp.where(lanes == 0, value, 0.0)

                    def row_of(slot, b=b, part=part):
                        return jnp.where(rows == 0, xadd_ref[part, b, slot, pl.ds(z, 1)], 0.0)

                    ex = left_ref[part, b, 0, z, cut] + turned(0)
                    ez = left_ref[part, b, 2, z, cut] + turned(1)
                    if cut.start == 0:
                        left_ref[part, b, 1, z, cut] = left_ref[part, b, 1, z, cut] + row_of(1)
                        ez = ez + row_of(0)
                    left_ref[part, b, 0, z, cut] = ex
                    left_ref[part, b, 2, z, cut] = ez
        kept(z).start()

    @pl.loop(0, nz)
    def _(z):
        kept(z).wait()


def body(fields, material, pml_width, eps_real, eps_loss, coeffs, ritz):
    _, vectors, _, nz, nx, ny = fields.shape
    f32 = lambda *shape: jax.ShapeDtypeStruct(shape, jnp.float32)
    scratch = lambda *shape: pltpu.VMEM(shape, jnp.float32)
    params = pltpu.CompilerParams(vmem_limit_bytes=40 * 1024 * 1024)
    whole = f32(*fields.shape)
    zf_shape = (2, vectors, 2, nx, ny)
    xf_shape = (2, vectors, 2, nz, ny)
    yf_shape = (4 * vectors, nz * nx)
    near, xf, yf = pl.pallas_call(
        face_kernel,
        out_shape=(whole, f32(*xf_shape), f32(*yf_shape)),
        in_specs=[HBM],
        out_specs=(VMEM,) * 3,
        scratch_shapes=[pltpu.SemaphoreType.DMA((2, 3))],
        compiler_params=params,
        name="take_faces",
    )(pltpu.with_memory_space_constraint(fields, pltpu.HBM))
    yf = passed_round(yf, "gy", -1)
    xf = passed_round(xf, "gx", -1)
    cells = fields.size // 6 // vectors

    def cost(flops, passes):
        return pl.CostEstimate(flops=flops * cells, bytes_accessed=passes * 4 * fields.size, transcendentals=0)

    planes = f32(nz, nx, ny)
    face = f32(*xf_shape)
    basis, loss, h, packed, table, sz = pl.pallas_call(
        prepare_kernel,
        out_shape=(whole, whole, whole, planes, f32(8, nx, ny), f32(4, nz, ny)),
        in_specs=[SMEM] * 4 + [VMEM] * 2,
        out_specs=(VMEM,) * 6,
        compiler_params=params,
        cost_estimate=cost(80000, 400),
        name="prepare",
    )(pml_width, eps_real, eps_loss, coeffs, near, material)
    h, xf, yt, xadd, yadd, zf = pl.pallas_call(
        slab_kernel,
        out_shape=(whole, face, f32(*yf_shape), face, planes, f32(*zf_shape)),
        in_specs=[SMEM] * 2 + [VMEM] * 4,
        out_specs=(VMEM,) * 6,
        input_output_aliases={3: 0},
        compiler_params=params,
        name="slab_face",
    )(pml_width, coeffs, basis, h, xf, yf)
    zf = passed_round(zf, "gz", 1)
    h, packed, left, acc, before, hxf, basis_new = pl.pallas_call(
        inner_kernel,
        out_shape=(whole, planes, whole, f32(vectors, 2 * vectors, SUB, ny), f32(*zf_shape), face, whole),
        in_specs=[SMEM] + [VMEM] * 8,
        out_specs=(VMEM,) * 6 + (HBM,),
        scratch_shapes=[pltpu.SemaphoreType.DMA],
        input_output_aliases={5: 0, 6: 1},
        compiler_params=params,
        cost_estimate=cost(800, 2),
        name="apply_inner",
    )(ritz, basis, loss, table, sz, h, packed, xadd, yadd)
    h, hxf, hyf = pl.pallas_call(
        last_plane_kernel,
        out_shape=(whole, face, f32(*yf_shape)),
        in_specs=[VMEM] * 5,
        out_specs=(VMEM,) * 3,
        input_output_aliases={2: 0, 4: 1},
        compiler_params=params,
        name="last_plane",
    )(sz, zf, h, packed, hxf)
    devices = lax.axis_size("gx") * lax.axis_size("gy") * lax.axis_size("gz")
    left, gram = pl.pallas_call(
        outer_kernel,
        out_shape=(whole, f32(devices, 4, ny)),
        in_specs=[SMEM] * 2 + [VMEM] * 13,
        out_specs=(VMEM,) * 2,
        input_output_aliases={12: 0},
        compiler_params=params,
        cost_estimate=cost(300, 1),
        name="apply_outer",
    )(pml_width, ritz, basis, loss, table, sz, h, zf, xf, yt, hxf, hyf, left, acc, before)
    gram, hxf, hyf = lax.optimization_barrier((gram, hxf, hyf))
    rows = lax.all_to_all(gram, ("gx", "gy", "gz"), 0, 0)
    from_x = passed_round(hxf, "gx", 1)
    from_y = passed_round(hyf, "gy", 1)
    _, residual = pl.pallas_call(
        rim_kernel,
        out_shape=(whole, whole),
        in_specs=[SMEM] + [VMEM] * 3,
        out_specs=(VMEM, HBM),
        scratch_shapes=[scratch(*xf_shape), scratch(nz, nx, ny), pltpu.SemaphoreType.DMA((nz,))],
        input_output_aliases={1: 0},
        compiler_params=params,
        cost_estimate=pl.CostEstimate(flops=0, bytes_accessed=0, transcendentals=0),
        name="add_rims",
    )(pml_width, left, from_x, from_y)
    rows, residual = lax.optimization_barrier((rows, residual))
    gram = pl.pallas_call(
        gather_kernel,
        out_shape=f32(2, vectors, vectors),
        in_specs=[VMEM],
        out_specs=VMEM,
        compiler_params=params,
        name="sum_rows",
    )(rows)
    return basis_new, residual, gram


def solution(mesh):
    in_specs = (P(None, None, None, "gz", "gx", "gy"), P("gz", "gx", "gy"), P(), P(), P(), P(), P())
    out_specs = (P(None, None, None, "gz", "gx", "gy"), P(None, None, None, "gz", "gx", "gy"), P())
    return jax.shard_map(body, mesh=mesh, in_specs=in_specs, out_specs=out_specs, check_vma=False)
```

```python
import functools

import jax
import jax.numpy as jnp
from jax import lax
from jax.experimental import pallas as pl
from jax.experimental.pallas import tpu as pltpu
from jax.sharding import PartitionSpec as P

OMEGA_SQ = 0.36
SIGMA_TOP = 3.0
BOUNDS = ((4, 5), (0, 1), (2, 3))
AXES = ("gz", "gx", "gy")

VMEM = pl.BlockSpec(memory_space=pltpu.VMEM)
SMEM = pl.BlockSpec(memory_space=pltpu.SMEM)
HBM = pl.BlockSpec(memory_space=pltpu.HBM)


def passed_round(value, axis, steps):
    count = lax.axis_size(axis)
    return lax.ppermute(value, axis, [(source, (source + steps) % count) for source in range(count)])


def passed_along(value, axis, steps):
    count = lax.axis_size(axis)
    leading, last = (max(0, -steps), min(count, count - steps))
    return lax.ppermute(value, axis, [(source, source + steps) for source in range(leading, last)])


def inverse_stretch(places, length, low_width, high_width):
    inside_depth = jnp.clip((low_width - places) / low_width, 0.0, 1.0) + jnp.clip(
        (places + 1.0 - length + high_width) / high_width, 0.0, 1.0
    )
    absorb = SIGMA_TOP * inside_depth * inside_depth
    scaled = 1.0 / (1.0 + absorb * absorb)
    return scaled, -absorb * scaled


def cmul(left, right):
    return (left[0] * right[0] - left[1] * right[1], left[0] * right[1] + left[1] * right[0])


def add(left, right):
    return (left[0] + right[0], left[1] + right[1])


def sub(left, right):
    return (left[0] - right[0], left[1] - right[1])


def axis_stretch(pml_ref, direction, count, places):
    total = count * lax.axis_size(AXES[direction])
    low_slot, high_slot = BOUNDS[direction]
    low = jnp.full(places.shape, pml_ref[low_slot], jnp.int32).astype(jnp.float32)
    high = jnp.full(places.shape, pml_ref[high_slot], jnp.int32).astype(jnp.float32)
    return inverse_stretch(places, jnp.float32(total), low, high)


def local_places(direction, count, shape, dim):
    start = lax.axis_index(AXES[direction]) * count
    return (lax.broadcasted_iota(jnp.int32, shape, dim) + start).astype(jnp.float32)


def one_place(direction, count, offset, shape):
    start = lax.axis_index(AXES[direction]) * count + offset
    return jnp.full(shape, start, jnp.int32).astype(jnp.float32)


def packed_row(slot, part, vector, vectors):
    return (slot * 2 + part) * vectors + vector


def has_neighbour(direction, steps):
    place = lax.axis_index(AXES[direction]) + steps
    inside = (place >= 0) & (place < lax.axis_size(AXES[direction]))
    return jnp.where(inside, 1.0, 0.0).astype(jnp.float32)


def face_kernel(fields_hbm, fields_ref, xf_ref, yf_ref, sems):
    _, vectors, _, nz, nx, ny = fields_ref.shape
    lanes = lax.broadcasted_iota(jnp.int32, (nx, ny), 1)
    copies = [
        pltpu.make_async_copy(fields_hbm.at[part, :, comp], fields_ref.at[part, :, comp], sems.at[part, comp])
        for comp in (0, 2, 1) for part in range(2)
    ]
    for copy in copies:
        copy.start()
    packed = [jnp.zeros((nx, ny), jnp.float32)] * nz
    for place, comp in enumerate((0, 2)):
        for part in range(2):
            copies[2 * place + part].wait()
            for a in range(vectors):
                row = packed_row(comp // 2, part, a, vectors)
                for z in range(nz):
                    value = fields_ref[part, a, comp, z]
                    packed[z] = jnp.where(lanes == row, pltpu.roll(value, row, 1) if row else value, packed[z])
    turned = jnp.concatenate(packed, axis=0).T
    yf_ref[...] = turned[:yf_ref.shape[0]]
    for part in range(2):
        for a in range(vectors):
            xf_ref[part, a, 1] = fields_ref[part, a, 2, :, 0, :]
    for part in range(2):
        copies[4 + part].wait()
        for a in range(vectors):
            xf_ref[part, a, 0] = fields_ref[part, a, 1, :, 0, :]


def rotated(coeffs_ref, old, b):
    new = None
    for a, value in enumerate(old):
        term = cmul((coeffs_ref[0, a, b], coeffs_ref[1, a, b]), value)
        new = term if new is None else add(new, term)
    return new


SUB = 8
SHX, SEX, SHY, SEY = range(0, 8, 2)


def field_of(ref, b, comp, z, cut):
    return tuple(ref[part, b, comp, z, cut] for part in range(2))


def tiles_of(nx):
    return [slice(SUB * t, SUB * (t + 1)) for t in range(nx // SUB)]


def prepare_kernel(
    pml_ref, eps_real_ref, eps_loss_ref, coeffs_ref, fields_ref, material_ref,
    basis_ref, loss_ref, h_ref, packed_ref, table_ref, sz_ref,
):
    _, vectors, _, nz, nx, ny = fields_ref.shape
    plane = (nx, ny)
    parts = range(2)
    for slot, direction, half, count, dim in (
        (SHX, 1, 0.5, nx, 0), (SEX, 1, 0.0, nx, 0), (SHY, 2, 0.5, ny, 1), (SEY, 2, 0.0, ny, 1),
    ):
        values = axis_stretch(pml_ref, direction, count, local_places(direction, count, plane, dim) + half)
        for part in parts:
            table_ref[slot + part] = values[part]
    for slot, half in ((0, 0.0), (2, 0.5)):
        values = axis_stretch(pml_ref, 0, nz, local_places(0, nz, (nz, ny), 0) + half)
        for part in parts:
            sz_ref[slot + part] = values[part]

    @pl.loop(0, nz)
    def _(z):
        material = material_ref[z]
        eps = []
        for source in (eps_real_ref, eps_loss_ref):
            value = jnp.zeros(plane, jnp.float32)
            for number in range(source.shape[0]):
                value = jnp.where(material == number, -OMEGA_SQ * source[number], value)
            eps.append(value)
        for comp in range(3):
            old = [(fields_ref[0, a, comp, z], fields_ref[1, a, comp, z]) for a in range(vectors)]
            for b in range(vectors):
                new = rotated(coeffs_ref, old, b)
                loss = cmul(eps, new)
                for part in parts:
                    basis_ref[part, b, comp, z] = new[part]
                    loss_ref[part, b, comp, z] = loss[part]
        packed_ref[z] = jnp.zeros(plane, jnp.float32)

    tile = (SUB, ny)
    rows = lax.broadcasted_iota(jnp.int32, tile, 0)
    lanes = lax.broadcasted_iota(jnp.int32, tile, 1)
    cuts = tiles_of(nx)

    def magnetic(b, z, last):
        shz = tuple(sz_ref[2 + part, pl.ds(z, 1)] for part in parts)
        for cut in cuts:
            u = [field_of(basis_ref, b, comp, z, cut) for comp in range(3)]

            def step_z(comp):
                if last:
                    return tuple(-value for value in u[comp])
                return sub(field_of(basis_ref, b, comp, z + 1, cut), u[comp])

            def step_x(comp):
                if cut.stop < nx:
                    ahead = field_of(basis_ref, b, comp, z, slice(cut.start + 1, cut.stop + 1))
                else:
                    ahead = tuple(jnp.where(rows == SUB - 1, 0.0, pltpu.roll(value, SUB - 1, 0)) for value in u[comp])
                return sub(ahead, u[comp])

            def step_y(comp):
                ahead = tuple(jnp.where(lanes == ny - 1, 0.0, pltpu.roll(value, ny - 1, 1)) for value in u[comp])
                return sub(ahead, u[comp])

            shx = tuple(table_ref[SHX + part, cut] for part in parts)
            shy = tuple(table_ref[SHY + part, cut] for part in parts)
            h = (
                sub(cmul(shy, step_y(2)), cmul(shz, step_z(1))),
                sub(cmul(shz, step_z(0)), cmul(shx, step_x(2))),
                sub(cmul(shx, step_x(1)), cmul(shy, step_y(0))),
            )
            for comp in range(3):
                for part in parts:
                    h_ref[part, b, comp, z, cut] = h[comp][part]
            packed = packed_ref[z, cut]
            for slot, value in enumerate((h[2], h[0])):
                for part in parts:
                    row = packed_row(slot, part, b, vectors)
                    packed = jnp.where(lanes == row, pltpu.roll(value[part], (row + 1) % ny, 1), packed)
            packed_ref[z, cut] = packed

    @pl.loop(0, nz - 1)
    def _(z):
        for b in range(vectors):
            magnetic(b, z, False)

    for b in range(vectors):
        magnetic(b, nz - 1, True)


def turn_face(coeffs_ref, direction, raw_ref, face_ref):
    inside = has_neighbour(direction, 1)
    vectors = raw_ref.shape[1]
    for slot in range(2):
        old = [(raw_ref[0, a, slot] * inside, raw_ref[1, a, slot] * inside) for a in range(vectors)]
        for b in range(vectors):
            new = rotated(coeffs_ref, old, b)
            for part in range(2):
                face_ref[part, b, slot] = new[part]


def turn_column(coeffs_ref, raw_ref, rows_ref):
    vectors = coeffs_ref.shape[1]
    inside = has_neighbour(2, 1)
    both = 2 * vectors
    shape = (both, raw_ref.shape[1])
    which = lax.broadcasted_iota(jnp.int32, shape, 0)
    turned = [jnp.zeros(shape, jnp.float32)] * 2
    for part in range(2):
        for a in range(vectors):
            column = jnp.zeros(shape, jnp.float32)
            for b in range(vectors):
                first, second = coeffs_ref[0, a, b] * inside, coeffs_ref[1, a, b] * inside
                if part:
                    first, second = -second, first
                column = jnp.where(which == b, first, column)
                column = jnp.where(which == vectors + b, second, column)
            for slot in range(2):
                row = packed_row(slot, part, a, vectors)
                turned[slot] = turned[slot] + column * raw_ref[row:row + 1]
    for slot in range(2):
        rows_ref[slot * both:(slot + 1) * both] = turned[slot]


def lane_to_last(values, slot, part, b, vectors):
    ny = values.shape[-1]
    lanes = lax.broadcasted_iota(jnp.int32, values.shape, 1)
    row = packed_row(slot, part, b, vectors)
    return jnp.where(lanes == ny - 1, pltpu.roll(values, ny - 1 - row, 1), 0.0)


def with_halos(h, b, z, cut, nx, xadd_ref, yadd_ref):
    vectors = xadd_ref.shape[1]
    column = yadd_ref[z, cut]
    hx = tuple(h[0][part] + lane_to_last(column, 1, part, b, vectors) for part in range(2))
    hz = tuple(h[2][part] + lane_to_last(column, 0, part, b, vectors) for part in range(2))
    hy = h[1]
    if cut.stop == nx:
        rows = lax.broadcasted_iota(jnp.int32, column.shape, 0)

        def row_of(slot):
            return tuple(
                jnp.where(rows == SUB - 1, xadd_ref[part, b, slot, pl.ds(z, 1)], 0.0) for part in range(2)
            )

        hy, hz = add(hy, row_of(0)), add(hz, row_of(1))
    return hx, hy, hz


def slab_kernel(
    pml_ref, coeffs_ref, basis_ref, h_in, raw_xf_ref, raw_yf_ref,
    h_ref, xf_ref, yt_ref, xadd_ref, yadd_ref, zf_ref,
):
    del h_in
    _, vectors, _, nz, nx, ny = basis_ref.shape
    parts = range(2)
    cells = nz * nx
    both = 2 * vectors
    turn_face(coeffs_ref, 1, raw_xf_ref, xf_ref)
    turn_column(coeffs_ref, raw_yf_ref, yt_ref)
    shx = axis_stretch(pml_ref, 1, nx, one_place(1, nx, nx - 1, (1, ny)) + 0.5)
    shy = axis_stretch(pml_ref, 2, ny, one_place(2, ny, ny - 1, (1, cells)) + 0.5)
    for b in range(vectors):
        for slot in range(2):
            value = cmul(shx, tuple(xf_ref[part, b, 1 - slot] for part in parts))
            for part in parts:
                xadd_ref[part, b, slot] = value[part] if slot else -value[part]
    added = []
    for slot in range(2):
        value = cmul(shy, (yt_ref[slot * both:slot * both + vectors], yt_ref[slot * both + vectors:(slot + 1) * both]))
        added += [part if slot else -part for part in value]
    rest = jnp.zeros((ny - 2 * both, cells), jnp.float32)
    yadd_ref[...] = jnp.concatenate(added + [rest], axis=0).T.reshape(nz, nx, ny)
    last = nz - 1
    lower = jnp.full((SUB, ny), lax.axis_index(AXES[0]), jnp.int32) == 0
    for b in range(vectors):
        for cut in tiles_of(nx):
            h = [field_of(h_ref, b, comp, last, cut) for comp in range(3)]
            h = with_halos(h, b, last, cut, nx, xadd_ref, yadd_ref)
            for part in parts:
                for comp in range(3):
                    h_ref[part, b, comp, last, cut] = h[comp][part]
                for comp in range(2):
                    zf_ref[part, b, comp, cut] = jnp.where(lower, h[comp][part], basis_ref[part, b, comp, 0, cut])


def plane_step(
    b, z, before, sums, ritz_ref, basis_ref, loss_ref, table_ref, sz_ref, h_ref, left_ref, halos=None
):
    _, vectors, _, _, nx, ny = basis_ref.shape
    rows = lax.broadcasted_iota(jnp.int32, (SUB, ny), 0)
    lanes = lax.broadcasted_iota(jnp.int32, (SUB, ny), 1)
    parts = range(2)
    cuts = tiles_of(nx)
    sez = tuple(sz_ref[part, pl.ds(z, 1)] for part in parts)
    fields = []
    for cut in cuts:
        h = [field_of(h_ref, b, comp, z, cut) for comp in range(3)]
        if halos is not None:
            h = with_halos(h, b, z, cut, nx, *halos)
            for comp in (1, 2):
                for part in parts:
                    h_ref[part, b, comp, z, cut] = h[comp][part]
        fields.append(h)
    sums = list(sums)
    for t, cut in enumerate(cuts):
        hx, hy, hz = fields[t]

        def back_x(comp):
            here = fields[t][comp]
            if t:
                past = field_of(h_ref, b, comp, z, slice(cut.start - 1, cut.stop - 1))
            else:
                past = tuple(jnp.where(rows == 0, 0.0, pltpu.roll(value, 1, 0)) for value in here)
            return sub(here, past)

        def back_y(value):
            return sub(value, tuple(jnp.where(lanes == 0, 0.0, pltpu.roll(part, 1, 1)) for part in value))

        sex = tuple(table_ref[SEX + part, cut] for part in parts)
        sey = tuple(table_ref[SEY + part, cut] for part in parts)
        bxy, bxz = (cmul(sex, back_x(comp)) for comp in (1, 2))
        byz, byx = (cmul(sey, back_y(value)) for value in (hz, hx))
        bzx, bzy = (cmul(sez, sub(value, past)) for value, past in zip((hx, hy), before[t]))
        curl = (sub(byz, bzy), sub(bzx, bxz), sub(bxy, byx))
        w = [add(curl[comp], field_of(loss_ref, b, comp, z, cut)) for comp in range(3)]
        for comp in range(3):
            left = sub(w[comp], cmul((ritz_ref[0, b], ritz_ref[1, b]), field_of(basis_ref, b, comp, z, cut)))
            for part in parts:
                left_ref[part, b, comp, z, cut] = left[part]
        for a in range(vectors):
            total = sums[a]
            for comp in range(3):
                total = add(total, cmul(field_of(basis_ref, a, comp, z, cut), w[comp]))
            sums[a] = total
    return [(h[0], h[1]) for h in fields], sums


def inner_kernel(
    ritz_ref, basis_ref, loss_ref, table_ref, sz_ref, h_in, packed_in, xadd_ref, yadd_ref,
    h_ref, packed_ref, left_ref, acc_ref, before_ref, hxf_ref, basis_hbm, sem,
):
    del h_in, packed_in
    _, vectors, _, nz, nx, ny = basis_ref.shape
    keep = pltpu.make_async_copy(basis_ref, basis_hbm, sem)
    keep.start()
    cuts = tiles_of(nx)
    lanes = lax.broadcasted_iota(jnp.int32, (nz, ny), 1)
    open_plane = lax.broadcasted_iota(jnp.int32, (nz, ny), 0) < nz - 1
    packed_ref[...] = packed_ref[...] + yadd_ref[...]
    corner = packed_ref[:, nx - 1, :]
    for b in range(vectors):
        for part in range(2):
            row = packed_row(0, part, b, vectors)
            more = xadd_ref[part, b, 1]
            corner = corner + jnp.where(lanes == row, pltpu.roll(more, (row + 1) % ny, 1), 0.0)
            more = more + lane_to_last(yadd_ref[:, nx - 1, :], 0, part, b, vectors)
            hxf_ref[part, b, 0] = h_ref[part, b, 1, :, nx - 1, :] + jnp.where(open_plane, xadd_ref[part, b, 0], 0.0)
            hxf_ref[part, b, 1] = h_ref[part, b, 2, :, nx - 1, :] + jnp.where(open_plane, more, 0.0)
    packed_ref[:, nx - 1, :] = corner
    acc_ref[...] = jnp.zeros(acc_ref.shape, jnp.float32)
    before_ref[...] = jnp.zeros(before_ref.shape, jnp.float32)

    @pl.loop(0, nz - 1)
    def _(z):
        for b in range(vectors):
            before = [
                tuple(tuple(before_ref[part, b, slot, cut] for part in range(2)) for slot in range(2)) for cut in cuts
            ]
            sums = [(acc_ref[b, a], acc_ref[b, vectors + a]) for a in range(vectors)]
            before, sums = plane_step(
                b, z, before, sums, ritz_ref, basis_ref, loss_ref, table_ref, sz_ref, h_ref, left_ref, (xadd_ref, yadd_ref)
            )
            for part in range(2):
                for a in range(vectors):
                    acc_ref[b, part * vectors + a] = sums[a][part]
                for t, cut in enumerate(cuts):
                    for slot in range(2):
                        before_ref[part, b, slot, cut] = before[t][slot][part]

    keep.wait()


def last_plane_kernel(sz_ref, zf_ref, h_in, packed_in, hxf_in, h_ref, hxf_ref, hyf_ref):
    del h_in, hxf_in
    _, vectors, _, nz, nx, ny = h_ref.shape
    parts = range(2)
    last = nz - 1
    lanes = lax.broadcasted_iota(jnp.int32, (SUB, ny), 1)
    shz = tuple(sz_ref[2 + part, last:] * has_neighbour(0, 1) for part in parts)
    packed = [packed_in[last, cut] for cut in tiles_of(nx)]
    for b in range(vectors):
        for t, cut in enumerate(tiles_of(nx)):
            ex, ey = (tuple(zf_ref[part, b, slot, cut] for part in parts) for slot in range(2))
            more = (tuple(-value for value in cmul(shz, ey)), cmul(shz, ex))
            for part in parts:
                for comp in range(2):
                    h_ref[part, b, comp, last, cut] = h_ref[part, b, comp, last, cut] + more[comp][part]
                row = packed_row(1, part, b, vectors)
                edge = pltpu.roll(more[0][part], (row + 1) % ny, 1)
                packed[t] = packed[t] + jnp.where(lanes == row, edge, 0.0)
                if cut.stop == nx:
                    hxf_ref[part, b, 0, last:] = hxf_ref[part, b, 0, last:] + more[1][part][SUB - 1:]
    inner = packed_in[:last].reshape(last * nx, ny)
    hyf_ref[...] = jnp.concatenate([inner] + packed, axis=0).T[:hyf_ref.shape[0]]


def outer_kernel(
    pml_ref, ritz_ref, basis_ref, loss_ref, table_ref, sz_ref, h_ref, zf_ref, xf_ref, yt_ref, hxf_ref, hyf_ref,
    left_in, acc_ref, before_ref, left_ref, gram_ref,
):
    del left_in
    _, vectors, _, nz, nx, ny = basis_ref.shape
    parts = range(2)
    cuts = tiles_of(nx)
    under = axis_stretch(pml_ref, 0, nz, one_place(0, nz, -1, (1, ny)) + 0.5)
    sez = tuple(sz_ref[part, 0:1] * has_neighbour(0, -1) for part in parts)
    sx_next = axis_stretch(pml_ref, 1, nx, one_place(1, nx, nx, (1, ny)))
    sy_next = axis_stretch(pml_ref, 2, ny, one_place(2, ny, ny, (1, nz * nx)))
    both = 2 * vectors
    ends = [
        cmul(sy_next, (yt_ref[slot * both:slot * both + vectors], yt_ref[slot * both + vectors:(slot + 1) * both]))
        for slot in range(2)
    ]
    columns = lax.broadcasted_iota(jnp.int32, (both, ny), 1)
    gram = jnp.zeros((both, ny), jnp.float32)
    for b in range(vectors):

        def tile_of(ref, slot, cut, b=b):
            return tuple(ref[part, b, slot, cut] for part in parts)

        before = [tuple(tile_of(before_ref, slot, cut) for slot in range(2)) for cut in cuts]
        sums = [(acc_ref[b, a], acc_ref[b, vectors + a]) for a in range(vectors)]
        _, sums = plane_step(
            b, nz - 1, before, sums, ritz_ref, basis_ref, loss_ref, table_ref, sz_ref, h_ref, left_ref
        )
        for cut in cuts:
            ex, ey = (field_of(basis_ref, b, comp, 0, cut) for comp in range(2))
            hx = sub(tile_of(zf_ref, 0, cut), cmul(under, ey))
            hy = add(tile_of(zf_ref, 1, cut), cmul(under, ex))
            more = (cmul(sez, hy), cmul(sez, hx))
            for part in parts:
                left_ref[part, b, 0, 0, cut] = left_ref[part, b, 0, 0, cut] + more[0][part]
                left_ref[part, b, 1, 0, cut] = left_ref[part, b, 1, 0, cut] - more[1][part]
            for a in range(vectors):
                ex, ey = (field_of(basis_ref, a, comp, 0, cut) for comp in range(2))
                sums[a] = add(sums[a], sub(cmul(ex, more[0]), cmul(ey, more[1])))
        h_y = tuple(hxf_ref[part, b, 0] for part in parts)
        h_z = tuple(hxf_ref[part, b, 1] for part in parts)
        for a in range(vectors):
            over = cmul(tuple(xf_ref[part, a, 0] for part in parts), h_z)
            over = sub(over, cmul(tuple(xf_ref[part, a, 1] for part in parts), h_y))
            over = cmul(sx_next, over)
            for row in range(0, nz, SUB):
                sums[a] = add(sums[a], tuple(part[row:row + SUB] for part in over))
        flat = jnp.concatenate(
            [jnp.sum(sums[a][part], axis=0, keepdims=True) for part in parts for a in range(vectors)], axis=0
        )
        over = None
        for slot in range(2):
            h = tuple(hyf_ref[packed_row(slot, part, b, vectors)][None] for part in parts)
            term = cmul(ends[slot], h)
            over = term if over is None else sub(term, over)
        side = jnp.concatenate(over, axis=0)
        total = jnp.sum(flat, axis=1, keepdims=True) + jnp.sum(side, axis=1, keepdims=True)
        gram = jnp.where(columns == b, total, gram)
    everywhere = 3.0 * nz * nx * ny
    for axis in AXES:
        everywhere = everywhere * lax.axis_size(axis)
    gram = gram * (1.0 / everywhere)
    row = tree_sum([gram[0:1]] + [pltpu.roll(gram[row:row + 1], row * vectors, 1) for row in range(1, both)])
    for device in range(gram_ref.shape[0]):
        gram_ref[device] = row


def tree_sum(values):
    while len(values) > 1:
        pairs = [values[place] + values[place + 1] for place in range(0, len(values) - 1, 2)]
        values = pairs + ([values[-1]] if len(values) % 2 else [])
    return values[0]


def gather_kernel(rows_ref, gram_ref):
    vectors = gram_ref.shape[1]
    total = tree_sum([rows_ref[device] for device in range(rows_ref.shape[0])])
    count = total.shape[1]
    for part in range(2):
        for a in range(vectors):
            row = (part * vectors + a) * vectors
            turned = pltpu.roll(total, count - row, 1) if row else total
            gram_ref[part, a:a + 1] = turned[:, :vectors]


def rim_kernel(pml_ref, left_in, hxf_ref, hyf_ref, left_ref, residual_hbm, xadd_ref, yadd_ref, sems):
    del left_in
    _, vectors, _, nz, nx, ny = left_ref.shape
    parts = range(2)
    both = 2 * vectors
    sex = axis_stretch(pml_ref, 1, nx, one_place(1, nx, 0, (nz, ny)))
    sex = tuple(part * has_neighbour(1, -1) for part in sex)
    sey = axis_stretch(pml_ref, 2, ny, one_place(2, ny, 0, (vectors, nz * nx)))
    sey = tuple(part * has_neighbour(2, -1) for part in sey)
    for b in range(vectors):
        for slot in range(2):
            value = cmul(sex, tuple(hxf_ref[part, b, slot] for part in parts))
            for part in parts:
                xadd_ref[part, b, slot] = value[part] if slot else -value[part]
    added = []
    for slot in range(2):
        first = slot * both
        value = cmul(sey, (hyf_ref[first:first + vectors], hyf_ref[first + vectors:first + both]))
        added += [part if slot else -part for part in value]
    rest = jnp.zeros((ny - 2 * both, nz * nx), jnp.float32)
    yadd_ref[...] = jnp.concatenate(added + [rest], axis=0).T.reshape(nz, nx, ny)
    rows = lax.broadcasted_iota(jnp.int32, (SUB, ny), 0)
    lanes = lax.broadcasted_iota(jnp.int32, (SUB, ny), 1)

    def kept(z):
        return pltpu.make_async_copy(left_ref.at[:, :, :, z], residual_hbm.at[:, :, :, z], sems.at[z])

    @pl.loop(0, nz)
    def _(z):
        for cut in tiles_of(nx):
            column = yadd_ref[z, cut]
            for b in range(vectors):
                for part in parts:

                    def turned(slot, b=b, part=part):
                        row = packed_row(slot, part, b, vectors)
                        value = pltpu.roll(column, ny - row, 1) if row else column
                        return jnp.where(lanes == 0, value, 0.0)

                    def row_of(slot, b=b, part=part):
                        return jnp.where(rows == 0, xadd_ref[part, b, slot, pl.ds(z, 1)], 0.0)

                    ex = left_ref[part, b, 0, z, cut] + turned(0)
                    ez = left_ref[part, b, 2, z, cut] + turned(1)
                    if cut.start == 0:
                        left_ref[part, b, 1, z, cut] = left_ref[part, b, 1, z, cut] + row_of(1)
                        ez = ez + row_of(0)
                    left_ref[part, b, 0, z, cut] = ex
                    left_ref[part, b, 2, z, cut] = ez
        kept(z).start()

    @pl.loop(0, nz)
    def _(z):
        kept(z).wait()


def body(fields, material, pml_width, eps_real, eps_loss, coeffs, ritz):
    _, vectors, _, nz, nx, ny = fields.shape
    f32 = lambda *shape: jax.ShapeDtypeStruct(shape, jnp.float32)
    scratch = lambda *shape: pltpu.VMEM(shape, jnp.float32)
    params = pltpu.CompilerParams(vmem_limit_bytes=40 * 1024 * 1024)
    whole = f32(*fields.shape)
    zf_shape = (2, vectors, 2, nx, ny)
    xf_shape = (2, vectors, 2, nz, ny)
    yf_shape = (4 * vectors, nz * nx)
    near, xf, yf = pl.pallas_call(
        face_kernel,
        out_shape=(whole, f32(*xf_shape), f32(*yf_shape)),
        in_specs=[HBM],
        out_specs=(VMEM,) * 3,
        scratch_shapes=[pltpu.SemaphoreType.DMA((2, 3))],
        compiler_params=params,
        name="take_faces",
    )(pltpu.with_memory_space_constraint(fields, pltpu.HBM))
    yf = passed_round(yf, "gy", -1)
    xf = passed_round(xf, "gx", -1)
    cells = fields.size // 6 // vectors

    def cost(flops, passes):
        return pl.CostEstimate(flops=flops * cells, bytes_accessed=passes * 4 * fields.size, transcendentals=0)

    planes = f32(nz, nx, ny)
    face = f32(*xf_shape)
    basis, loss, h, packed, table, sz = pl.pallas_call(
        prepare_kernel,
        out_shape=(whole, whole, whole, planes, f32(8, nx, ny), f32(4, nz, ny)),
        in_specs=[SMEM] * 4 + [VMEM] * 2,
        out_specs=(VMEM,) * 6,
        compiler_params=params,
        cost_estimate=cost(80000, 400),
        name="prepare",
    )(pml_width, eps_real, eps_loss, coeffs, near, material)
    h, xf, yt, xadd, yadd, zf = pl.pallas_call(
        slab_kernel,
        out_shape=(whole, face, f32(*yf_shape), face, planes, f32(*zf_shape)),
        in_specs=[SMEM] * 2 + [VMEM] * 4,
        out_specs=(VMEM,) * 6,
        input_output_aliases={3: 0},
        compiler_params=params,
        name="slab_face",
    )(pml_width, coeffs, basis, h, xf, yf)
    zf = passed_round(zf, "gz", 1)
    h, packed, left, acc, before, hxf, basis_new = pl.pallas_call(
        inner_kernel,
        out_shape=(whole, planes, whole, f32(vectors, 2 * vectors, SUB, ny), f32(*zf_shape), face, whole),
        in_specs=[SMEM] + [VMEM] * 8,
        out_specs=(VMEM,) * 6 + (HBM,),
        scratch_shapes=[pltpu.SemaphoreType.DMA],
        input_output_aliases={5: 0, 6: 1},
        compiler_params=params,
        cost_estimate=cost(800, 2),
        name="apply_inner",
    )(ritz, basis, loss, table, sz, h, packed, xadd, yadd)
    h, hxf, hyf = pl.pallas_call(
        last_plane_kernel,
        out_shape=(whole, face, f32(*yf_shape)),
        in_specs=[VMEM] * 5,
        out_specs=(VMEM,) * 3,
        input_output_aliases={2: 0, 4: 1},
        compiler_params=params,
        name="last_plane",
    )(sz, zf, h, packed, hxf)
    devices = lax.axis_size("gx") * lax.axis_size("gy") * lax.axis_size("gz")
    left, gram = pl.pallas_call(
        outer_kernel,
        out_shape=(whole, f32(devices, 1, ny)),
        in_specs=[SMEM] * 2 + [VMEM] * 13,
        out_specs=(VMEM,) * 2,
        input_output_aliases={12: 0},
        compiler_params=params,
        cost_estimate=cost(300, 1),
        name="apply_outer",
    )(pml_width, ritz, basis, loss, table, sz, h, zf, xf, yt, hxf, hyf, left, acc, before)
    gram, hxf, hyf = lax.optimization_barrier((gram, hxf, hyf))
    rows = lax.all_to_all(gram, ("gx", "gy", "gz"), 0, 0)
    from_y = passed_round(hyf, "gy", 1)
    from_x = passed_along(hxf, "gx", 1)
    _, residual = pl.pallas_call(
        rim_kernel,
        out_shape=(whole, whole),
        in_specs=[SMEM] + [VMEM] * 3,
        out_specs=(VMEM, HBM),
        scratch_shapes=[scratch(*xf_shape), scratch(nz, nx, ny), pltpu.SemaphoreType.DMA((nz,))],
        input_output_aliases={1: 0},
        compiler_params=params,
        cost_estimate=cost(80000, 400),
        name="add_rims",
    )(pml_width, left, from_x, from_y)
    rows, residual = lax.optimization_barrier((rows, residual))
    gram = pl.pallas_call(
        gather_kernel,
        out_shape=f32(2, vectors, vectors),
        in_specs=[VMEM],
        out_specs=VMEM,
        compiler_params=params,
        name="sum_rows",
    )(rows)
    return basis_new, residual, gram


def solution(mesh):
    in_specs = (P(None, None, None, "gz", "gx", "gy"), P("gz", "gx", "gy"), P(), P(), P(), P(), P())
    out_specs = (P(None, None, None, "gz", "gx", "gy"), P(None, None, None, "gz", "gx", "gy"), P())
    return jax.shard_map(body, mesh=mesh, in_specs=in_specs, out_specs=out_specs, check_vma=False)
```

```python
import functools

import jax
import jax.numpy as jnp
from jax import lax
from jax.experimental import pallas as pl
from jax.experimental.pallas import tpu as pltpu
from jax.sharding import PartitionSpec as P

OMEGA_SQ = 0.36
SIGMA_TOP = 3.0
BOUNDS = ((4, 5), (0, 1), (2, 3))
AXES = ("gz", "gx", "gy")

VMEM = pl.BlockSpec(memory_space=pltpu.VMEM)
SMEM = pl.BlockSpec(memory_space=pltpu.SMEM)
HBM = pl.BlockSpec(memory_space=pltpu.HBM)


def passed_round(value, axis, steps):
    count = lax.axis_size(axis)
    return lax.ppermute(value, axis, [(source, (source + steps) % count) for source in range(count)])


def passed_along(value, axis, steps):
    count = lax.axis_size(axis)
    leading, last = (max(0, -steps), min(count, count - steps))
    return lax.ppermute(value, axis, [(source, source + steps) for source in range(leading, last)])


def inverse_stretch(places, length, low_width, high_width):
    inside_depth = jnp.clip((low_width - places) / low_width, 0.0, 1.0) + jnp.clip(
        (places + 1.0 - length + high_width) / high_width, 0.0, 1.0
    )
    absorb = SIGMA_TOP * inside_depth * inside_depth
    scaled = 1.0 / (1.0 + absorb * absorb)
    return scaled, -absorb * scaled


def cmul(left, right):
    return (left[0] * right[0] - left[1] * right[1], left[0] * right[1] + left[1] * right[0])


def add(left, right):
    return (left[0] + right[0], left[1] + right[1])


def sub(left, right):
    return (left[0] - right[0], left[1] - right[1])


def axis_stretch(pml_ref, direction, count, places):
    total = count * lax.axis_size(AXES[direction])
    low_slot, high_slot = BOUNDS[direction]
    low = jnp.full(places.shape, pml_ref[low_slot], jnp.int32).astype(jnp.float32)
    high = jnp.full(places.shape, pml_ref[high_slot], jnp.int32).astype(jnp.float32)
    return inverse_stretch(places, jnp.float32(total), low, high)


def local_places(direction, count, shape, dim):
    start = lax.axis_index(AXES[direction]) * count
    return (lax.broadcasted_iota(jnp.int32, shape, dim) + start).astype(jnp.float32)


def one_place(direction, count, offset, shape):
    start = lax.axis_index(AXES[direction]) * count + offset
    return jnp.full(shape, start, jnp.int32).astype(jnp.float32)


def packed_row(slot, part, vector, vectors):
    return (slot * 2 + part) * vectors + vector


def has_neighbour(direction, steps):
    place = lax.axis_index(AXES[direction]) + steps
    inside = (place >= 0) & (place < lax.axis_size(AXES[direction]))
    return jnp.where(inside, 1.0, 0.0).astype(jnp.float32)


def face_kernel(fields_hbm, fields_ref, xf_ref, yf_ref, sems):
    _, vectors, _, nz, nx, ny = fields_ref.shape
    lanes = lax.broadcasted_iota(jnp.int32, (nx, ny), 1)
    copies = [
        pltpu.make_async_copy(fields_hbm.at[part, :, comp], fields_ref.at[part, :, comp], sems.at[part, comp])
        for comp in (0, 2, 1) for part in range(2)
    ]
    for copy in copies:
        copy.start()
    packed = [jnp.zeros((nx, ny), jnp.float32)] * nz
    for place, comp in enumerate((0, 2)):
        for part in range(2):
            copies[2 * place + part].wait()
            for a in range(vectors):
                row = packed_row(comp // 2, part, a, vectors)
                for z in range(nz):
                    value = fields_ref[part, a, comp, z]
                    packed[z] = jnp.where(lanes == row, pltpu.roll(value, row, 1) if row else value, packed[z])
    turned = jnp.concatenate(packed, axis=0).T
    yf_ref[...] = turned[:yf_ref.shape[0]]
    for part in range(2):
        for a in range(vectors):
            xf_ref[part, a, 1] = fields_ref[part, a, 2, :, 0, :]
    for part in range(2):
        copies[4 + part].wait()
        for a in range(vectors):
            xf_ref[part, a, 0] = fields_ref[part, a, 1, :, 0, :]


def rotated(coeffs_ref, old, b):
    new = None
    for a, value in enumerate(old):
        term = cmul((coeffs_ref[0, a, b], coeffs_ref[1, a, b]), value)
        new = term if new is None else add(new, term)
    return new


SUB = 8
SHX, SEX, SHY, SEY = range(0, 8, 2)


def field_of(ref, b, comp, z, cut):
    return tuple(ref[part, b, comp, z, cut] for part in range(2))


def tiles_of(nx):
    return [slice(SUB * t, SUB * (t + 1)) for t in range(nx // SUB)]


def prepare_kernel(
    pml_ref, eps_real_ref, eps_loss_ref, coeffs_ref, fields_ref, material_ref,
    basis_ref, loss_ref, h_ref, packed_ref, table_ref, sz_ref,
):
    _, vectors, _, nz, nx, ny = fields_ref.shape
    plane = (nx, ny)
    parts = range(2)
    for slot, direction, half, count, dim in (
        (SHX, 1, 0.5, nx, 0), (SEX, 1, 0.0, nx, 0), (SHY, 2, 0.5, ny, 1), (SEY, 2, 0.0, ny, 1),
    ):
        values = axis_stretch(pml_ref, direction, count, local_places(direction, count, plane, dim) + half)
        for part in parts:
            table_ref[slot + part] = values[part]
    for slot, half in ((0, 0.0), (2, 0.5)):
        values = axis_stretch(pml_ref, 0, nz, local_places(0, nz, (nz, ny), 0) + half)
        for part in parts:
            sz_ref[slot + part] = values[part]

    @pl.loop(0, nz)
    def _(z):
        material = material_ref[z]
        eps = []
        for source in (eps_real_ref, eps_loss_ref):
            value = jnp.zeros(plane, jnp.float32)
            for number in range(source.shape[0]):
                value = jnp.where(material == number, -OMEGA_SQ * source[number], value)
            eps.append(value)
        for comp in range(3):
            old = [(fields_ref[0, a, comp, z], fields_ref[1, a, comp, z]) for a in range(vectors)]
            for b in range(vectors):
                new = rotated(coeffs_ref, old, b)
                loss = cmul(eps, new)
                for part in parts:
                    basis_ref[part, b, comp, z] = new[part]
                    loss_ref[part, b, comp, z] = loss[part]
        packed_ref[z] = jnp.zeros(plane, jnp.float32)

    tile = (SUB, ny)
    rows = lax.broadcasted_iota(jnp.int32, tile, 0)
    lanes = lax.broadcasted_iota(jnp.int32, tile, 1)
    cuts = tiles_of(nx)

    def magnetic(b, z, last):
        shz = tuple(sz_ref[2 + part, pl.ds(z, 1)] for part in parts)
        for cut in cuts:
            u = [field_of(basis_ref, b, comp, z, cut) for comp in range(3)]

            def step_z(comp):
                if last:
                    return tuple(-value for value in u[comp])
                return sub(field_of(basis_ref, b, comp, z + 1, cut), u[comp])

            def step_x(comp):
                if cut.stop < nx:
                    ahead = field_of(basis_ref, b, comp, z, slice(cut.start + 1, cut.stop + 1))
                else:
                    ahead = tuple(jnp.where(rows == SUB - 1, 0.0, pltpu.roll(value, SUB - 1, 0)) for value in u[comp])
                return sub(ahead, u[comp])

            def step_y(comp):
                ahead = tuple(jnp.where(lanes == ny - 1, 0.0, pltpu.roll(value, ny - 1, 1)) for value in u[comp])
                return sub(ahead, u[comp])

            shx = tuple(table_ref[SHX + part, cut] for part in parts)
            shy = tuple(table_ref[SHY + part, cut] for part in parts)
            h = (
                sub(cmul(shy, step_y(2)), cmul(shz, step_z(1))),
                sub(cmul(shz, step_z(0)), cmul(shx, step_x(2))),
                sub(cmul(shx, step_x(1)), cmul(shy, step_y(0))),
            )
            for comp in range(3):
                for part in parts:
                    h_ref[part, b, comp, z, cut] = h[comp][part]
            packed = packed_ref[z, cut]
            for slot, value in enumerate((h[2], h[0])):
                for part in parts:
                    row = packed_row(slot, part, b, vectors)
                    packed = jnp.where(lanes == row, pltpu.roll(value[part], (row + 1) % ny, 1), packed)
            packed_ref[z, cut] = packed

    @pl.loop(0, nz - 1)
    def _(z):
        for b in range(vectors):
            magnetic(b, z, False)

    for b in range(vectors):
        magnetic(b, nz - 1, True)


def turn_face(coeffs_ref, direction, raw_ref, face_ref):
    inside = has_neighbour(direction, 1)
    vectors = raw_ref.shape[1]
    for slot in range(2):
        old = [(raw_ref[0, a, slot] * inside, raw_ref[1, a, slot] * inside) for a in range(vectors)]
        for b in range(vectors):
            new = rotated(coeffs_ref, old, b)
            for part in range(2):
                face_ref[part, b, slot] = new[part]


def turn_column(coeffs_ref, raw_ref, rows_ref):
    vectors = coeffs_ref.shape[1]
    inside = has_neighbour(2, 1)
    both = 2 * vectors
    shape = (both, raw_ref.shape[1])
    which = lax.broadcasted_iota(jnp.int32, shape, 0)
    turned = [jnp.zeros(shape, jnp.float32)] * 2
    for part in range(2):
        for a in range(vectors):
            column = jnp.zeros(shape, jnp.float32)
            for b in range(vectors):
                first, second = coeffs_ref[0, a, b] * inside, coeffs_ref[1, a, b] * inside
                if part:
                    first, second = -second, first
                column = jnp.where(which == b, first, column)
                column = jnp.where(which == vectors + b, second, column)
            for slot in range(2):
                row = packed_row(slot, part, a, vectors)
                turned[slot] = turned[slot] + column * raw_ref[row:row + 1]
    for slot in range(2):
        rows_ref[slot * both:(slot + 1) * both] = turned[slot]


def lane_to_last(values, slot, part, b, vectors):
    ny = values.shape[-1]
    lanes = lax.broadcasted_iota(jnp.int32, values.shape, 1)
    row = packed_row(slot, part, b, vectors)
    return jnp.where(lanes == ny - 1, pltpu.roll(values, ny - 1 - row, 1), 0.0)


def with_halos(h, b, z, cut, nx, xadd_ref, yadd_ref):
    vectors = xadd_ref.shape[1]
    column = yadd_ref[z, cut]
    hx = tuple(h[0][part] + lane_to_last(column, 1, part, b, vectors) for part in range(2))
    hz = tuple(h[2][part] + lane_to_last(column, 0, part, b, vectors) for part in range(2))
    hy = h[1]
    if cut.stop == nx:
        rows = lax.broadcasted_iota(jnp.int32, column.shape, 0)

        def row_of(slot):
            return tuple(
                jnp.where(rows == SUB - 1, xadd_ref[part, b, slot, pl.ds(z, 1)], 0.0) for part in range(2)
            )

        hy, hz = add(hy, row_of(0)), add(hz, row_of(1))
    return hx, hy, hz


def slab_kernel(
    pml_ref, coeffs_ref, basis_ref, h_in, raw_xf_ref, raw_yf_ref,
    h_ref, xf_ref, yt_ref, xadd_ref, yadd_ref, zf_ref,
):
    del h_in
    _, vectors, _, nz, nx, ny = basis_ref.shape
    parts = range(2)
    cells = nz * nx
    both = 2 * vectors
    turn_face(coeffs_ref, 1, raw_xf_ref, xf_ref)
    turn_column(coeffs_ref, raw_yf_ref, yt_ref)
    shx = axis_stretch(pml_ref, 1, nx, one_place(1, nx, nx - 1, (1, ny)) + 0.5)
    shy = axis_stretch(pml_ref, 2, ny, one_place(2, ny, ny - 1, (1, cells)) + 0.5)
    for b in range(vectors):
        for slot in range(2):
            value = cmul(shx, tuple(xf_ref[part, b, 1 - slot] for part in parts))
            for part in parts:
                xadd_ref[part, b, slot] = value[part] if slot else -value[part]
    added = []
    for slot in range(2):
        value = cmul(shy, (yt_ref[slot * both:slot * both + vectors], yt_ref[slot * both + vectors:(slot + 1) * both]))
        added += [part if slot else -part for part in value]
    rest = jnp.zeros((ny - 2 * both, cells), jnp.float32)
    yadd_ref[...] = jnp.concatenate(added + [rest], axis=0).T.reshape(nz, nx, ny)
    last = nz - 1
    lower = jnp.full((SUB, ny), lax.axis_index(AXES[0]), jnp.int32) == 0
    for b in range(vectors):
        for cut in tiles_of(nx):
            h = [field_of(h_ref, b, comp, last, cut) for comp in range(3)]
            h = with_halos(h, b, last, cut, nx, xadd_ref, yadd_ref)
            for part in parts:
                for comp in range(3):
                    h_ref[part, b, comp, last, cut] = h[comp][part]
                for comp in range(2):
                    zf_ref[part, b, comp, cut] = jnp.where(lower, h[comp][part], basis_ref[part, b, comp, 0, cut])


def plane_step(
    b, z, before, sums, ritz_ref, basis_ref, loss_ref, table_ref, sz_ref, h_ref, left_ref, halos=None
):
    _, vectors, _, _, nx, ny = basis_ref.shape
    rows = lax.broadcasted_iota(jnp.int32, (SUB, ny), 0)
    lanes = lax.broadcasted_iota(jnp.int32, (SUB, ny), 1)
    parts = range(2)
    cuts = tiles_of(nx)
    sez = tuple(sz_ref[part, pl.ds(z, 1)] for part in parts)
    fields = []
    for cut in cuts:
        h = [field_of(h_ref, b, comp, z, cut) for comp in range(3)]
        if halos is not None:
            h = with_halos(h, b, z, cut, nx, *halos)
            for comp in (1, 2):
                for part in parts:
                    h_ref[part, b, comp, z, cut] = h[comp][part]
        fields.append(h)
    sums = list(sums)
    for t, cut in enumerate(cuts):
        hx, hy, hz = fields[t]

        def back_x(comp):
            here = fields[t][comp]
            if t:
                past = field_of(h_ref, b, comp, z, slice(cut.start - 1, cut.stop - 1))
            else:
                past = tuple(jnp.where(rows == 0, 0.0, pltpu.roll(value, 1, 0)) for value in here)
            return sub(here, past)

        def back_y(value):
            return sub(value, tuple(jnp.where(lanes == 0, 0.0, pltpu.roll(part, 1, 1)) for part in value))

        sex = tuple(table_ref[SEX + part, cut] for part in parts)
        sey = tuple(table_ref[SEY + part, cut] for part in parts)
        bxy, bxz = (cmul(sex, back_x(comp)) for comp in (1, 2))
        byz, byx = (cmul(sey, back_y(value)) for value in (hz, hx))
        bzx, bzy = (cmul(sez, sub(value, past)) for value, past in zip((hx, hy), before[t]))
        curl = (sub(byz, bzy), sub(bzx, bxz), sub(bxy, byx))
        w = [add(curl[comp], field_of(loss_ref, b, comp, z, cut)) for comp in range(3)]
        for comp in range(3):
            left = sub(w[comp], cmul((ritz_ref[0, b], ritz_ref[1, b]), field_of(basis_ref, b, comp, z, cut)))
            for part in parts:
                left_ref[part, b, comp, z, cut] = left[part]
        for a in range(vectors):
            total = sums[a]
            for comp in range(3):
                total = add(total, cmul(field_of(basis_ref, a, comp, z, cut), w[comp]))
            sums[a] = total
    return [(h[0], h[1]) for h in fields], sums


def inner_kernel(
    ritz_ref, basis_ref, loss_ref, table_ref, sz_ref, h_in, packed_in, xadd_ref, yadd_ref,
    h_ref, packed_ref, left_ref, acc_ref, before_ref, hxf_ref, basis_hbm, sem,
):
    del h_in, packed_in
    _, vectors, _, nz, nx, ny = basis_ref.shape
    keep = pltpu.make_async_copy(basis_ref, basis_hbm, sem)
    keep.start()
    cuts = tiles_of(nx)
    lanes = lax.broadcasted_iota(jnp.int32, (nz, ny), 1)
    open_plane = lax.broadcasted_iota(jnp.int32, (nz, ny), 0) < nz - 1
    packed_ref[...] = packed_ref[...] + yadd_ref[...]
    corner = packed_ref[:, nx - 1, :]
    for b in range(vectors):
        for part in range(2):
            row = packed_row(0, part, b, vectors)
            more = xadd_ref[part, b, 1]
            corner = corner + jnp.where(lanes == row, pltpu.roll(more, (row + 1) % ny, 1), 0.0)
            more = more + lane_to_last(yadd_ref[:, nx - 1, :], 0, part, b, vectors)
            hxf_ref[part, b, 0] = h_ref[part, b, 1, :, nx - 1, :] + jnp.where(open_plane, xadd_ref[part, b, 0], 0.0)
            hxf_ref[part, b, 1] = h_ref[part, b, 2, :, nx - 1, :] + jnp.where(open_plane, more, 0.0)
    packed_ref[:, nx - 1, :] = corner
    acc_ref[...] = jnp.zeros(acc_ref.shape, jnp.float32)
    before_ref[...] = jnp.zeros(before_ref.shape, jnp.float32)

    @pl.loop(0, nz - 1)
    def _(z):
        for b in range(vectors):
            before = [
                tuple(tuple(before_ref[part, b, slot, cut] for part in range(2)) for slot in range(2)) for cut in cuts
            ]
            sums = [(acc_ref[b, a], acc_ref[b, vectors + a]) for a in range(vectors)]
            before, sums = plane_step(
                b, z, before, sums, ritz_ref, basis_ref, loss_ref, table_ref, sz_ref, h_ref, left_ref, (xadd_ref, yadd_ref)
            )
            for part in range(2):
                for a in range(vectors):
                    acc_ref[b, part * vectors + a] = sums[a][part]
                for t, cut in enumerate(cuts):
                    for slot in range(2):
                        before_ref[part, b, slot, cut] = before[t][slot][part]

    keep.wait()


def last_plane_kernel(sz_ref, zf_ref, h_in, packed_in, hxf_in, h_ref, hxf_ref, hyf_ref):
    del h_in, hxf_in
    _, vectors, _, nz, nx, ny = h_ref.shape
    parts = range(2)
    last = nz - 1
    lanes = lax.broadcasted_iota(jnp.int32, (SUB, ny), 1)
    shz = tuple(sz_ref[2 + part, last:] * has_neighbour(0, 1) for part in parts)
    packed = [packed_in[last, cut] for cut in tiles_of(nx)]
    for b in range(vectors):
        for t, cut in enumerate(tiles_of(nx)):
            ex, ey = (tuple(zf_ref[part, b, slot, cut] for part in parts) for slot in range(2))
            more = (tuple(-value for value in cmul(shz, ey)), cmul(shz, ex))
            for part in parts:
                for comp in range(2):
                    h_ref[part, b, comp, last, cut] = h_ref[part, b, comp, last, cut] + more[comp][part]
                row = packed_row(1, part, b, vectors)
                edge = pltpu.roll(more[0][part], (row + 1) % ny, 1)
                packed[t] = packed[t] + jnp.where(lanes == row, edge, 0.0)
                if cut.stop == nx:
                    hxf_ref[part, b, 0, last:] = hxf_ref[part, b, 0, last:] + more[1][part][SUB - 1:]
    inner = packed_in[:last].reshape(last * nx, ny)
    hyf_ref[...] = jnp.concatenate([inner] + packed, axis=0).T[:hyf_ref.shape[0]]


def outer_kernel(
    pml_ref, ritz_ref, basis_ref, loss_ref, table_ref, sz_ref, h_ref, zf_ref, xf_ref, yt_ref, hxf_ref, hyf_ref,
    left_in, acc_ref, before_ref, left_ref, gram_ref,
):
    del left_in
    _, vectors, _, nz, nx, ny = basis_ref.shape
    parts = range(2)
    cuts = tiles_of(nx)
    under = axis_stretch(pml_ref, 0, nz, one_place(0, nz, -1, (1, ny)) + 0.5)
    sez = tuple(sz_ref[part, 0:1] * has_neighbour(0, -1) for part in parts)
    sx_next = axis_stretch(pml_ref, 1, nx, one_place(1, nx, nx, (1, ny)))
    sy_next = axis_stretch(pml_ref, 2, ny, one_place(2, ny, ny, (1, nz * nx)))
    both = 2 * vectors
    ends = [
        cmul(sy_next, (yt_ref[slot * both:slot * both + vectors], yt_ref[slot * both + vectors:(slot + 1) * both]))
        for slot in range(2)
    ]
    columns = lax.broadcasted_iota(jnp.int32, (both, ny), 1)
    gram = jnp.zeros((both, ny), jnp.float32)
    for b in range(vectors):

        def tile_of(ref, slot, cut, b=b):
            return tuple(ref[part, b, slot, cut] for part in parts)

        before = [tuple(tile_of(before_ref, slot, cut) for slot in range(2)) for cut in cuts]
        sums = [(acc_ref[b, a], acc_ref[b, vectors + a]) for a in range(vectors)]
        _, sums = plane_step(
            b, nz - 1, before, sums, ritz_ref, basis_ref, loss_ref, table_ref, sz_ref, h_ref, left_ref
        )
        for cut in cuts:
            ex, ey = (field_of(basis_ref, b, comp, 0, cut) for comp in range(2))
            hx = sub(tile_of(zf_ref, 0, cut), cmul(under, ey))
            hy = add(tile_of(zf_ref, 1, cut), cmul(under, ex))
            more = (cmul(sez, hy), cmul(sez, hx))
            for part in parts:
                left_ref[part, b, 0, 0, cut] = left_ref[part, b, 0, 0, cut] + more[0][part]
                left_ref[part, b, 1, 0, cut] = left_ref[part, b, 1, 0, cut] - more[1][part]
            for a in range(vectors):
                ex, ey = (field_of(basis_ref, a, comp, 0, cut) for comp in range(2))
                sums[a] = add(sums[a], sub(cmul(ex, more[0]), cmul(ey, more[1])))
        h_y = tuple(hxf_ref[part, b, 0] for part in parts)
        h_z = tuple(hxf_ref[part, b, 1] for part in parts)
        for a in range(vectors):
            over = cmul(tuple(xf_ref[part, a, 0] for part in parts), h_z)
            over = sub(over, cmul(tuple(xf_ref[part, a, 1] for part in parts), h_y))
            over = cmul(sx_next, over)
            for row in range(0, nz, SUB):
                sums[a] = add(sums[a], tuple(part[row:row + SUB] for part in over))
        flat = jnp.concatenate(
            [jnp.sum(sums[a][part], axis=0, keepdims=True) for part in parts for a in range(vectors)], axis=0
        )
        over = None
        for slot in range(2):
            h = tuple(hyf_ref[packed_row(slot, part, b, vectors)][None] for part in parts)
            term = cmul(ends[slot], h)
            over = term if over is None else sub(term, over)
        side = jnp.concatenate(over, axis=0)
        total = jnp.sum(flat, axis=1, keepdims=True) + jnp.sum(side, axis=1, keepdims=True)
        gram = jnp.where(columns == b, total, gram)
    everywhere = 3.0 * nz * nx * ny
    for axis in AXES:
        everywhere = everywhere * lax.axis_size(axis)
    gram = gram * (1.0 / everywhere)
    row = tree_sum([gram[0:1]] + [pltpu.roll(gram[row:row + 1], row * vectors, 1) for row in range(1, both)])
    block = jnp.concatenate([row, jnp.zeros((gram_ref.shape[1] - 1, ny), jnp.float32)], axis=0)
    for device in range(gram_ref.shape[0]):
        gram_ref[device] = block


def tree_sum(values):
    while len(values) > 1:
        pairs = [values[place] + values[place + 1] for place in range(0, len(values) - 1, 2)]
        values = pairs + ([values[-1]] if len(values) % 2 else [])
    return values[0]


def put_gram(rows_ref, gram_ref):
    vectors = gram_ref.shape[1]
    total = tree_sum([rows_ref[device] for device in range(rows_ref.shape[0])])[0:1]
    count = total.shape[1]
    for part in range(2):
        for a in range(vectors):
            row = (part * vectors + a) * vectors
            turned = pltpu.roll(total, count - row, 1) if row else total
            gram_ref[part, a:a + 1] = turned[:, :vectors]


def rim_kernel(
    pml_ref, left_in, hxf_ref, hyf_ref, rows_ref,
    left_ref, residual_hbm, gram_hbm, xadd_ref, yadd_ref, gram_ref, sems, gram_sem,
):
    del left_in
    put_gram(rows_ref, gram_ref)
    gram_copy = pltpu.make_async_copy(gram_ref, gram_hbm, gram_sem)
    gram_copy.start()
    _, vectors, _, nz, nx, ny = left_ref.shape
    parts = range(2)
    both = 2 * vectors
    sex = axis_stretch(pml_ref, 1, nx, one_place(1, nx, 0, (nz, ny)))
    sex = tuple(part * has_neighbour(1, -1) for part in sex)
    sey = axis_stretch(pml_ref, 2, ny, one_place(2, ny, 0, (vectors, nz * nx)))
    sey = tuple(part * has_neighbour(2, -1) for part in sey)
    for b in range(vectors):
        for slot in range(2):
            value = cmul(sex, tuple(hxf_ref[part, b, slot] for part in parts))
            for part in parts:
                xadd_ref[part, b, slot] = value[part] if slot else -value[part]
    added = []
    for slot in range(2):
        first = slot * both
        value = cmul(sey, (hyf_ref[first:first + vectors], hyf_ref[first + vectors:first + both]))
        added += [part if slot else -part for part in value]
    rest = jnp.zeros((ny - 2 * both, nz * nx), jnp.float32)
    yadd_ref[...] = jnp.concatenate(added + [rest], axis=0).T.reshape(nz, nx, ny)
    rows = lax.broadcasted_iota(jnp.int32, (SUB, ny), 0)
    lanes = lax.broadcasted_iota(jnp.int32, (SUB, ny), 1)

    def kept(z):
        return pltpu.make_async_copy(left_ref.at[:, :, :, z], residual_hbm.at[:, :, :, z], sems.at[z])

    @pl.loop(0, nz)
    def _(z):
        for cut in tiles_of(nx):
            column = yadd_ref[z, cut]
            for b in range(vectors):
                for part in parts:

                    def turned(slot, b=b, part=part):
                        row = packed_row(slot, part, b, vectors)
                        value = pltpu.roll(column, ny - row, 1) if row else column
                        return jnp.where(lanes == 0, value, 0.0)

                    def row_of(slot, b=b, part=part):
                        return jnp.where(rows == 0, xadd_ref[part, b, slot, pl.ds(z, 1)], 0.0)

                    ex = left_ref[part, b, 0, z, cut] + turned(0)
                    ez = left_ref[part, b, 2, z, cut] + turned(1)
                    if cut.start == 0:
                        left_ref[part, b, 1, z, cut] = left_ref[part, b, 1, z, cut] + row_of(1)
                        ez = ez + row_of(0)
                    left_ref[part, b, 0, z, cut] = ex
                    left_ref[part, b, 2, z, cut] = ez
        kept(z).start()

    @pl.loop(0, nz)
    def _(z):
        kept(z).wait()

    gram_copy.wait()


def body(fields, material, pml_width, eps_real, eps_loss, coeffs, ritz):
    _, vectors, _, nz, nx, ny = fields.shape
    f32 = lambda *shape: jax.ShapeDtypeStruct(shape, jnp.float32)
    scratch = lambda *shape: pltpu.VMEM(shape, jnp.float32)
    params = pltpu.CompilerParams(vmem_limit_bytes=40 * 1024 * 1024)
    whole = f32(*fields.shape)
    zf_shape = (2, vectors, 2, nx, ny)
    xf_shape = (2, vectors, 2, nz, ny)
    yf_shape = (4 * vectors, nz * nx)
    near, xf, yf = pl.pallas_call(
        face_kernel,
        out_shape=(whole, f32(*xf_shape), f32(*yf_shape)),
        in_specs=[HBM],
        out_specs=(VMEM,) * 3,
        scratch_shapes=[pltpu.SemaphoreType.DMA((2, 3))],
        compiler_params=params,
        name="take_faces",
    )(pltpu.with_memory_space_constraint(fields, pltpu.HBM))
    yf = passed_round(yf, "gy", -1)
    xf = passed_round(xf, "gx", -1)
    cells = fields.size // 6 // vectors

    def cost(flops, passes):
        return pl.CostEstimate(flops=flops * cells, bytes_accessed=passes * 4 * fields.size, transcendentals=0)

    planes = f32(nz, nx, ny)
    face = f32(*xf_shape)
    basis, loss, h, packed, table, sz = pl.pallas_call(
        prepare_kernel,
        out_shape=(whole, whole, whole, planes, f32(8, nx, ny), f32(4, nz, ny)),
        in_specs=[SMEM] * 4 + [VMEM] * 2,
        out_specs=(VMEM,) * 6,
        compiler_params=params,
        cost_estimate=cost(80000, 400),
        name="prepare",
    )(pml_width, eps_real, eps_loss, coeffs, near, material)
    h, xf, yt, xadd, yadd, zf = pl.pallas_call(
        slab_kernel,
        out_shape=(whole, face, f32(*yf_shape), face, planes, f32(*zf_shape)),
        in_specs=[SMEM] * 2 + [VMEM] * 4,
        out_specs=(VMEM,) * 6,
        input_output_aliases={3: 0},
        compiler_params=params,
        name="slab_face",
    )(pml_width, coeffs, basis, h, xf, yf)
    zf = passed_round(zf, "gz", 1)
    h, packed, left, acc, before, hxf, basis_new = pl.pallas_call(
        inner_kernel,
        out_shape=(whole, planes, whole, f32(vectors, 2 * vectors, SUB, ny), f32(*zf_shape), face, whole),
        in_specs=[SMEM] + [VMEM] * 8,
        out_specs=(VMEM,) * 6 + (HBM,),
        scratch_shapes=[pltpu.SemaphoreType.DMA],
        input_output_aliases={5: 0, 6: 1},
        compiler_params=params,
        cost_estimate=cost(800, 2),
        name="apply_inner",
    )(ritz, basis, loss, table, sz, h, packed, xadd, yadd)
    h, hxf, hyf = pl.pallas_call(
        last_plane_kernel,
        out_shape=(whole, face, f32(*yf_shape)),
        in_specs=[VMEM] * 5,
        out_specs=(VMEM,) * 3,
        input_output_aliases={2: 0, 4: 1},
        compiler_params=params,
        name="last_plane",
    )(sz, zf, h, packed, hxf)
    devices = lax.axis_size("gx") * lax.axis_size("gy") * lax.axis_size("gz")
    left, gram = pl.pallas_call(
        outer_kernel,
        out_shape=(whole, f32(devices, 4, ny)),
        in_specs=[SMEM] * 2 + [VMEM] * 13,
        out_specs=(VMEM,) * 2,
        input_output_aliases={12: 0},
        compiler_params=params,
        cost_estimate=cost(300, 1),
        name="apply_outer",
    )(pml_width, ritz, basis, loss, table, sz, h, zf, xf, yt, hxf, hyf, left, acc, before)
    gram, hxf, hyf = lax.optimization_barrier((gram, hxf, hyf))
    rows = lax.all_to_all(gram, ("gx", "gy", "gz"), 0, 0, axis_index_groups=[list(range(devices))[::-1]])
    from_x = passed_along(hxf, "gx", 1)
    from_y = passed_round(hyf, "gy", 1)
    _, residual, gram = pl.pallas_call(
        rim_kernel,
        out_shape=(whole, whole, f32(2, vectors, vectors)),
        in_specs=[SMEM] + [VMEM] * 4,
        out_specs=(VMEM, HBM, HBM),
        scratch_shapes=[
            scratch(*xf_shape), scratch(nz, nx, ny), scratch(2, vectors, vectors),
            pltpu.SemaphoreType.DMA((nz,)), pltpu.SemaphoreType.DMA,
        ],
        input_output_aliases={1: 0},
        compiler_params=params,
        cost_estimate=pl.CostEstimate(flops=0, bytes_accessed=0, transcendentals=0),
        name="add_rims",
    )(pml_width, left, from_x, from_y, rows)
    return basis_new, residual, gram


def solution(mesh):
    in_specs = (P(None, None, None, "gz", "gx", "gy"), P("gz", "gx", "gy"), P(), P(), P(), P(), P())
    out_specs = (P(None, None, None, "gz", "gx", "gy"), P(None, None, None, "gz", "gx", "gy"), P())
    return jax.shard_map(body, mesh=mesh, in_specs=in_specs, out_specs=out_specs, check_vma=False)
```

```python
import functools

import jax
import jax.numpy as jnp
from jax import lax
from jax.experimental import pallas as pl
from jax.experimental.pallas import tpu as pltpu
from jax.sharding import PartitionSpec as P

OMEGA_SQ = 0.36
SIGMA_TOP = 3.0
BOUNDS = ((4, 5), (0, 1), (2, 3))
AXES = ("gz", "gx", "gy")

VMEM = pl.BlockSpec(memory_space=pltpu.VMEM)
SMEM = pl.BlockSpec(memory_space=pltpu.SMEM)
HBM = pl.BlockSpec(memory_space=pltpu.HBM)


def passed_round(value, axis, steps):
    count = lax.axis_size(axis)
    return lax.ppermute(value, axis, [(source, (source + steps) % count) for source in range(count)])


def passed_along(value, axis, steps):
    count = lax.axis_size(axis)
    leading, last = (max(0, -steps), min(count, count - steps))
    return lax.ppermute(value, axis, [(source, source + steps) for source in range(leading, last)])


def inverse_stretch(places, length, low_width, high_width):
    inside_depth = jnp.clip((low_width - places) / low_width, 0.0, 1.0) + jnp.clip(
        (places + 1.0 - length + high_width) / high_width, 0.0, 1.0
    )
    absorb = SIGMA_TOP * inside_depth * inside_depth
    scaled = 1.0 / (1.0 + absorb * absorb)
    return scaled, -absorb * scaled


def cmul(left, right):
    return (left[0] * right[0] - left[1] * right[1], left[0] * right[1] + left[1] * right[0])


def add(left, right):
    return (left[0] + right[0], left[1] + right[1])


def sub(left, right):
    return (left[0] - right[0], left[1] - right[1])


def axis_stretch(pml_ref, direction, count, places):
    total = count * lax.axis_size(AXES[direction])
    low_slot, high_slot = BOUNDS[direction]
    low = jnp.full(places.shape, pml_ref[low_slot], jnp.int32).astype(jnp.float32)
    high = jnp.full(places.shape, pml_ref[high_slot], jnp.int32).astype(jnp.float32)
    return inverse_stretch(places, jnp.float32(total), low, high)


def local_places(direction, count, shape, dim):
    start = lax.axis_index(AXES[direction]) * count
    return (lax.broadcasted_iota(jnp.int32, shape, dim) + start).astype(jnp.float32)


def one_place(direction, count, offset, shape):
    start = lax.axis_index(AXES[direction]) * count + offset
    return jnp.full(shape, start, jnp.int32).astype(jnp.float32)


def packed_row(slot, part, vector, vectors):
    return (slot * 2 + part) * vectors + vector


def has_neighbour(direction, steps):
    place = lax.axis_index(AXES[direction]) + steps
    inside = (place >= 0) & (place < lax.axis_size(AXES[direction]))
    return jnp.where(inside, 1.0, 0.0).astype(jnp.float32)


def face_kernel(fields_hbm, fields_ref, xf_ref, yf_ref, sems):
    _, vectors, _, nz, nx, ny = fields_ref.shape
    lanes = lax.broadcasted_iota(jnp.int32, (nx, ny), 1)
    copies = [
        pltpu.make_async_copy(fields_hbm.at[part, :, comp], fields_ref.at[part, :, comp], sems.at[part, comp])
        for comp in (0, 2, 1) for part in range(2)
    ]
    for copy in copies:
        copy.start()
    packed = [jnp.zeros((nx, ny), jnp.float32)] * nz
    for place, comp in enumerate((0, 2)):
        for part in range(2):
            copies[2 * place + part].wait()
            for a in range(vectors):
                row = packed_row(comp // 2, part, a, vectors)
                for z in range(nz):
                    value = fields_ref[part, a, comp, z]
                    packed[z] = jnp.where(lanes == row, pltpu.roll(value, row, 1) if row else value, packed[z])
    turned = jnp.concatenate(packed, axis=0).T
    yf_ref[...] = turned[:yf_ref.shape[0]]
    for part in range(2):
        for a in range(vectors):
            xf_ref[part, a, 1] = fields_ref[part, a, 2, :, 0, :]
    for part in range(2):
        copies[4 + part].wait()
        for a in range(vectors):
            xf_ref[part, a, 0] = fields_ref[part, a, 1, :, 0, :]


def rotated(coeffs_ref, old, b):
    new = None
    for a, value in enumerate(old):
        term = cmul((coeffs_ref[0, a, b], coeffs_ref[1, a, b]), value)
        new = term if new is None else add(new, term)
    return new


SUB = 8
SHX, SEX, SHY, SEY = range(0, 8, 2)


def field_of(ref, b, comp, z, cut):
    return tuple(ref[part, b, comp, z, cut] for part in range(2))


def tiles_of(nx):
    return [slice(SUB * t, SUB * (t + 1)) for t in range(nx // SUB)]


def prepare_kernel(
    pml_ref, eps_real_ref, eps_loss_ref, coeffs_ref, fields_ref, material_ref,
    basis_ref, loss_ref, h_ref, packed_ref, table_ref, sz_ref,
):
    _, vectors, _, nz, nx, ny = fields_ref.shape
    plane = (nx, ny)
    parts = range(2)
    for slot, direction, half, count, dim in (
        (SHX, 1, 0.5, nx, 0), (SEX, 1, 0.0, nx, 0), (SHY, 2, 0.5, ny, 1), (SEY, 2, 0.0, ny, 1),
    ):
        values = axis_stretch(pml_ref, direction, count, local_places(direction, count, plane, dim) + half)
        for part in parts:
            table_ref[slot + part] = values[part]
    for slot, half in ((0, 0.0), (2, 0.5)):
        values = axis_stretch(pml_ref, 0, nz, local_places(0, nz, (nz, ny), 0) + half)
        for part in parts:
            sz_ref[slot + part] = values[part]

    @pl.loop(0, nz)
    def _(z):
        material = material_ref[z]
        eps = []
        for source in (eps_real_ref, eps_loss_ref):
            value = jnp.zeros(plane, jnp.float32)
            for number in range(source.shape[0]):
                value = jnp.where(material == number, -OMEGA_SQ * source[number], value)
            eps.append(value)
        for comp in range(3):
            old = [(fields_ref[0, a, comp, z], fields_ref[1, a, comp, z]) for a in range(vectors)]
            for b in range(vectors):
                new = rotated(coeffs_ref, old, b)
                loss = cmul(eps, new)
                for part in parts:
                    basis_ref[part, b, comp, z] = new[part]
                    loss_ref[part, b, comp, z] = loss[part]
        packed_ref[z] = jnp.zeros(plane, jnp.float32)

    tile = (SUB, ny)
    rows = lax.broadcasted_iota(jnp.int32, tile, 0)
    lanes = lax.broadcasted_iota(jnp.int32, tile, 1)
    cuts = tiles_of(nx)

    def magnetic(b, z, last):
        shz = tuple(sz_ref[2 + part, pl.ds(z, 1)] for part in parts)
        for cut in cuts:
            u = [field_of(basis_ref, b, comp, z, cut) for comp in range(3)]

            def step_z(comp):
                if last:
                    return tuple(-value for value in u[comp])
                return sub(field_of(basis_ref, b, comp, z + 1, cut), u[comp])

            def step_x(comp):
                if cut.stop < nx:
                    ahead = field_of(basis_ref, b, comp, z, slice(cut.start + 1, cut.stop + 1))
                else:
                    ahead = tuple(jnp.where(rows == SUB - 1, 0.0, pltpu.roll(value, SUB - 1, 0)) for value in u[comp])
                return sub(ahead, u[comp])

            def step_y(comp):
                ahead = tuple(jnp.where(lanes == ny - 1, 0.0, pltpu.roll(value, ny - 1, 1)) for value in u[comp])
                return sub(ahead, u[comp])

            shx = tuple(table_ref[SHX + part, cut] for part in parts)
            shy = tuple(table_ref[SHY + part, cut] for part in parts)
            h = (
                sub(cmul(shy, step_y(2)), cmul(shz, step_z(1))),
                sub(cmul(shz, step_z(0)), cmul(shx, step_x(2))),
                sub(cmul(shx, step_x(1)), cmul(shy, step_y(0))),
            )
            for comp in range(3):
                for part in parts:
                    h_ref[part, b, comp, z, cut] = h[comp][part]
            packed = packed_ref[z, cut]
            for slot, value in enumerate((h[2], h[0])):
                for part in parts:
                    row = packed_row(slot, part, b, vectors)
                    packed = jnp.where(lanes == row, pltpu.roll(value[part], (row + 1) % ny, 1), packed)
            packed_ref[z, cut] = packed

    @pl.loop(0, nz - 1)
    def _(z):
        for b in range(vectors):
            magnetic(b, z, False)

    for b in range(vectors):
        magnetic(b, nz - 1, True)


def turn_face(coeffs_ref, direction, raw_ref, face_ref):
    inside = has_neighbour(direction, 1)
    vectors = raw_ref.shape[1]
    for slot in range(2):
        old = [(raw_ref[0, a, slot] * inside, raw_ref[1, a, slot] * inside) for a in range(vectors)]
        for b in range(vectors):
            new = rotated(coeffs_ref, old, b)
            for part in range(2):
                face_ref[part, b, slot] = new[part]


def turn_column(coeffs_ref, raw_ref, rows_ref):
    vectors = coeffs_ref.shape[1]
    inside = has_neighbour(2, 1)
    both = 2 * vectors
    shape = (both, raw_ref.shape[1])
    which = lax.broadcasted_iota(jnp.int32, shape, 0)
    turned = [jnp.zeros(shape, jnp.float32)] * 2
    for part in range(2):
        for a in range(vectors):
            column = jnp.zeros(shape, jnp.float32)
            for b in range(vectors):
                first, second = coeffs_ref[0, a, b] * inside, coeffs_ref[1, a, b] * inside
                if part:
                    first, second = -second, first
                column = jnp.where(which == b, first, column)
                column = jnp.where(which == vectors + b, second, column)
            for slot in range(2):
                row = packed_row(slot, part, a, vectors)
                turned[slot] = turned[slot] + column * raw_ref[row:row + 1]
    for slot in range(2):
        rows_ref[slot * both:(slot + 1) * both] = turned[slot]


def lane_to_last(values, slot, part, b, vectors):
    ny = values.shape[-1]
    lanes = lax.broadcasted_iota(jnp.int32, values.shape, 1)
    row = packed_row(slot, part, b, vectors)
    return jnp.where(lanes == ny - 1, pltpu.roll(values, ny - 1 - row, 1), 0.0)


def with_halos(h, b, z, cut, nx, xadd_ref, yadd_ref):
    vectors = xadd_ref.shape[1]
    column = yadd_ref[z, cut]
    hx = tuple(h[0][part] + lane_to_last(column, 1, part, b, vectors) for part in range(2))
    hz = tuple(h[2][part] + lane_to_last(column, 0, part, b, vectors) for part in range(2))
    hy = h[1]
    if cut.stop == nx:
        rows = lax.broadcasted_iota(jnp.int32, column.shape, 0)

        def row_of(slot):
            return tuple(
                jnp.where(rows == SUB - 1, xadd_ref[part, b, slot, pl.ds(z, 1)], 0.0) for part in range(2)
            )

        hy, hz = add(hy, row_of(0)), add(hz, row_of(1))
    return hx, hy, hz


def slab_kernel(
    pml_ref, coeffs_ref, basis_ref, h_in, raw_xf_ref, raw_yf_ref,
    h_ref, xf_ref, yt_ref, xadd_ref, yadd_ref, zf_ref,
):
    del h_in
    _, vectors, _, nz, nx, ny = basis_ref.shape
    parts = range(2)
    cells = nz * nx
    both = 2 * vectors
    turn_face(coeffs_ref, 1, raw_xf_ref, xf_ref)
    turn_column(coeffs_ref, raw_yf_ref, yt_ref)
    shx = axis_stretch(pml_ref, 1, nx, one_place(1, nx, nx - 1, (1, ny)) + 0.5)
    shy = axis_stretch(pml_ref, 2, ny, one_place(2, ny, ny - 1, (1, cells)) + 0.5)
    for b in range(vectors):
        for slot in range(2):
            value = cmul(shx, tuple(xf_ref[part, b, 1 - slot] for part in parts))
            for part in parts:
                xadd_ref[part, b, slot] = value[part] if slot else -value[part]
    added = []
    for slot in range(2):
        value = cmul(shy, (yt_ref[slot * both:slot * both + vectors], yt_ref[slot * both + vectors:(slot + 1) * both]))
        added += [part if slot else -part for part in value]
    rest = jnp.zeros((ny - 2 * both, cells), jnp.float32)
    yadd_ref[...] = jnp.concatenate(added + [rest], axis=0).T.reshape(nz, nx, ny)
    last = nz - 1
    lower = jnp.full((SUB, ny), lax.axis_index(AXES[0]), jnp.int32) == 0
    for b in range(vectors):
        for cut in tiles_of(nx):
            h = [field_of(h_ref, b, comp, last, cut) for comp in range(3)]
            h = with_halos(h, b, last, cut, nx, xadd_ref, yadd_ref)
            for part in parts:
                for comp in range(3):
                    h_ref[part, b, comp, last, cut] = h[comp][part]
                for comp in range(2):
                    zf_ref[part, b, comp, cut] = jnp.where(lower, h[comp][part], basis_ref[part, b, comp, 0, cut])


def plane_step(
    b, z, before, sums, ritz_ref, basis_ref, loss_ref, table_ref, sz_ref, h_ref, left_ref, halos=None
):
    _, vectors, _, _, nx, ny = basis_ref.shape
    rows = lax.broadcasted_iota(jnp.int32, (SUB, ny), 0)
    lanes = lax.broadcasted_iota(jnp.int32, (SUB, ny), 1)
    parts = range(2)
    cuts = tiles_of(nx)
    sez = tuple(sz_ref[part, pl.ds(z, 1)] for part in parts)
    fields = []
    for cut in cuts:
        h = [field_of(h_ref, b, comp, z, cut) for comp in range(3)]
        if halos is not None:
            h = with_halos(h, b, z, cut, nx, *halos)
            for comp in (1, 2):
                for part in parts:
                    h_ref[part, b, comp, z, cut] = h[comp][part]
        fields.append(h)
    sums = list(sums)
    for t, cut in enumerate(cuts):
        hx, hy, hz = fields[t]

        def back_x(comp):
            here = fields[t][comp]
            if t:
                past = field_of(h_ref, b, comp, z, slice(cut.start - 1, cut.stop - 1))
            else:
                past = tuple(jnp.where(rows == 0, 0.0, pltpu.roll(value, 1, 0)) for value in here)
            return sub(here, past)

        def back_y(value):
            return sub(value, tuple(jnp.where(lanes == 0, 0.0, pltpu.roll(part, 1, 1)) for part in value))

        sex = tuple(table_ref[SEX + part, cut] for part in parts)
        sey = tuple(table_ref[SEY + part, cut] for part in parts)
        bxy, bxz = (cmul(sex, back_x(comp)) for comp in (1, 2))
        byz, byx = (cmul(sey, back_y(value)) for value in (hz, hx))
        bzx, bzy = (cmul(sez, sub(value, past)) for value, past in zip((hx, hy), before[t]))
        curl = (sub(byz, bzy), sub(bzx, bxz), sub(bxy, byx))
        w = [add(curl[comp], field_of(loss_ref, b, comp, z, cut)) for comp in range(3)]
        for comp in range(3):
            left = sub(w[comp], cmul((ritz_ref[0, b], ritz_ref[1, b]), field_of(basis_ref, b, comp, z, cut)))
            for part in parts:
                left_ref[part, b, comp, z, cut] = left[part]
        for a in range(vectors):
            total = sums[a]
            for comp in range(3):
                total = add(total, cmul(field_of(basis_ref, a, comp, z, cut), w[comp]))
            sums[a] = total
    return [(h[0], h[1]) for h in fields], sums


def inner_kernel(
    ritz_ref, basis_ref, loss_ref, table_ref, sz_ref, h_in, packed_in, xadd_ref, yadd_ref,
    h_ref, packed_ref, left_ref, acc_ref, before_ref, hxf_ref, basis_hbm, sem,
):
    del h_in, packed_in
    _, vectors, _, nz, nx, ny = basis_ref.shape
    keep = pltpu.make_async_copy(basis_ref, basis_hbm, sem)
    keep.start()
    cuts = tiles_of(nx)
    lanes = lax.broadcasted_iota(jnp.int32, (nz, ny), 1)
    open_plane = lax.broadcasted_iota(jnp.int32, (nz, ny), 0) < nz - 1
    packed_ref[...] = packed_ref[...] + yadd_ref[...]
    corner = packed_ref[:, nx - 1, :]
    for b in range(vectors):
        for part in range(2):
            row = packed_row(0, part, b, vectors)
            more = xadd_ref[part, b, 1]
            corner = corner + jnp.where(lanes == row, pltpu.roll(more, (row + 1) % ny, 1), 0.0)
            more = more + lane_to_last(yadd_ref[:, nx - 1, :], 0, part, b, vectors)
            hxf_ref[part, b, 0] = h_ref[part, b, 1, :, nx - 1, :] + jnp.where(open_plane, xadd_ref[part, b, 0], 0.0)
            hxf_ref[part, b, 1] = h_ref[part, b, 2, :, nx - 1, :] + jnp.where(open_plane, more, 0.0)
    packed_ref[:, nx - 1, :] = corner
    acc_ref[...] = jnp.zeros(acc_ref.shape, jnp.float32)
    before_ref[...] = jnp.zeros(before_ref.shape, jnp.float32)

    @pl.loop(0, nz - 1)
    def _(z):
        for b in range(vectors):
            before = [
                tuple(tuple(before_ref[part, b, slot, cut] for part in range(2)) for slot in range(2)) for cut in cuts
            ]
            sums = [(acc_ref[b, a], acc_ref[b, vectors + a]) for a in range(vectors)]
            before, sums = plane_step(
                b, z, before, sums, ritz_ref, basis_ref, loss_ref, table_ref, sz_ref, h_ref, left_ref, (xadd_ref, yadd_ref)
            )
            for part in range(2):
                for a in range(vectors):
                    acc_ref[b, part * vectors + a] = sums[a][part]
                for t, cut in enumerate(cuts):
                    for slot in range(2):
                        before_ref[part, b, slot, cut] = before[t][slot][part]

    keep.wait()


def last_plane_kernel(sz_ref, zf_ref, h_in, packed_in, hxf_in, h_ref, hxf_ref, hyf_ref):
    del h_in, hxf_in
    _, vectors, _, nz, nx, ny = h_ref.shape
    parts = range(2)
    last = nz - 1
    lanes = lax.broadcasted_iota(jnp.int32, (SUB, ny), 1)
    shz = tuple(sz_ref[2 + part, last:] * has_neighbour(0, 1) for part in parts)
    packed = [packed_in[last, cut] for cut in tiles_of(nx)]
    for b in range(vectors):
        for t, cut in enumerate(tiles_of(nx)):
            ex, ey = (tuple(zf_ref[part, b, slot, cut] for part in parts) for slot in range(2))
            more = (tuple(-value for value in cmul(shz, ey)), cmul(shz, ex))
            for part in parts:
                for comp in range(2):
                    h_ref[part, b, comp, last, cut] = h_ref[part, b, comp, last, cut] + more[comp][part]
                row = packed_row(1, part, b, vectors)
                edge = pltpu.roll(more[0][part], (row + 1) % ny, 1)
                packed[t] = packed[t] + jnp.where(lanes == row, edge, 0.0)
                if cut.stop == nx:
                    hxf_ref[part, b, 0, last:] = hxf_ref[part, b, 0, last:] + more[1][part][SUB - 1:]
    inner = packed_in[:last].reshape(last * nx, ny)
    hyf_ref[...] = jnp.concatenate([inner] + packed, axis=0).T


def outer_kernel(
    pml_ref, ritz_ref, basis_ref, loss_ref, table_ref, sz_ref, h_ref, zf_ref, xf_ref, yt_ref, hxf_ref, hyf_ref,
    left_in, acc_ref, before_ref, left_ref, gram_ref,
):
    del left_in
    _, vectors, _, nz, nx, ny = basis_ref.shape
    parts = range(2)
    cuts = tiles_of(nx)
    under = axis_stretch(pml_ref, 0, nz, one_place(0, nz, -1, (1, ny)) + 0.5)
    sez = tuple(sz_ref[part, 0:1] * has_neighbour(0, -1) for part in parts)
    sx_next = axis_stretch(pml_ref, 1, nx, one_place(1, nx, nx, (1, ny)))
    sy_next = axis_stretch(pml_ref, 2, ny, one_place(2, ny, ny, (1, nz * nx)))
    both = 2 * vectors
    ends = [
        cmul(sy_next, (yt_ref[slot * both:slot * both + vectors], yt_ref[slot * both + vectors:(slot + 1) * both]))
        for slot in range(2)
    ]
    columns = lax.broadcasted_iota(jnp.int32, (both, ny), 1)
    gram = jnp.zeros((both, ny), jnp.float32)
    for b in range(vectors):

        def tile_of(ref, slot, cut, b=b):
            return tuple(ref[part, b, slot, cut] for part in parts)

        before = [tuple(tile_of(before_ref, slot, cut) for slot in range(2)) for cut in cuts]
        sums = [(acc_ref[b, a], acc_ref[b, vectors + a]) for a in range(vectors)]
        _, sums = plane_step(
            b, nz - 1, before, sums, ritz_ref, basis_ref, loss_ref, table_ref, sz_ref, h_ref, left_ref
        )
        for cut in cuts:
            ex, ey = (field_of(basis_ref, b, comp, 0, cut) for comp in range(2))
            hx = sub(tile_of(zf_ref, 0, cut), cmul(under, ey))
            hy = add(tile_of(zf_ref, 1, cut), cmul(under, ex))
            more = (cmul(sez, hy), cmul(sez, hx))
            for part in parts:
                left_ref[part, b, 0, 0, cut] = left_ref[part, b, 0, 0, cut] + more[0][part]
                left_ref[part, b, 1, 0, cut] = left_ref[part, b, 1, 0, cut] - more[1][part]
            for a in range(vectors):
                ex, ey = (field_of(basis_ref, a, comp, 0, cut) for comp in range(2))
                sums[a] = add(sums[a], sub(cmul(ex, more[0]), cmul(ey, more[1])))
        h_y = tuple(hxf_ref[part, b, 0] for part in parts)
        h_z = tuple(hxf_ref[part, b, 1] for part in parts)
        for a in range(vectors):
            over = cmul(tuple(xf_ref[part, a, 0] for part in parts), h_z)
            over = sub(over, cmul(tuple(xf_ref[part, a, 1] for part in parts), h_y))
            over = cmul(sx_next, over)
            for row in range(0, nz, SUB):
                sums[a] = add(sums[a], tuple(part[row:row + SUB] for part in over))
        flat = jnp.concatenate(
            [jnp.sum(sums[a][part], axis=0, keepdims=True) for part in parts for a in range(vectors)], axis=0
        )
        over = None
        for slot in range(2):
            h = tuple(hyf_ref[packed_row(slot, part, b, vectors)][None] for part in parts)
            term = cmul(ends[slot], h)
            over = term if over is None else sub(term, over)
        side = jnp.concatenate(over, axis=0)
        total = jnp.sum(flat, axis=1, keepdims=True) + jnp.sum(side, axis=1, keepdims=True)
        gram = jnp.where(columns == b, total, gram)
    everywhere = 3.0 * nz * nx * ny
    for axis in AXES:
        everywhere = everywhere * lax.axis_size(axis)
    gram = gram * (1.0 / everywhere)
    row = tree_sum([gram[0:1]] + [pltpu.roll(gram[row:row + 1], row * vectors, 1) for row in range(1, both)])
    block = jnp.concatenate([row, jnp.zeros((gram_ref.shape[1] - 1, ny), jnp.float32)], axis=0)
    for device in range(gram_ref.shape[0]):
        gram_ref[device] = block


def tree_sum(values):
    while len(values) > 1:
        pairs = [values[place] + values[place + 1] for place in range(0, len(values) - 1, 2)]
        values = pairs + ([values[-1]] if len(values) % 2 else [])
    return values[0]


def gather_kernel(rows_ref, gram_ref):
    vectors = gram_ref.shape[1]
    total = tree_sum([rows_ref[device] for device in range(rows_ref.shape[0])])[0:1]
    count = total.shape[1]
    for part in range(2):
        for a in range(vectors):
            row = (part * vectors + a) * vectors
            turned = pltpu.roll(total, count - row, 1) if row else total
            gram_ref[part, a:a + 1] = turned[:, :vectors]


def rim_kernel(pml_ref, left_in, hxf_ref, hyf_ref, left_ref, residual_hbm, xadd_ref, yadd_ref, sems):
    del left_in
    _, vectors, _, nz, nx, ny = left_ref.shape
    parts = range(2)
    both = 2 * vectors
    sex = axis_stretch(pml_ref, 1, nx, one_place(1, nx, 0, (nz, ny)))
    sex = tuple(part * has_neighbour(1, -1) for part in sex)
    sey = axis_stretch(pml_ref, 2, ny, one_place(2, ny, 0, (vectors, nz * nx)))
    sey = tuple(part * has_neighbour(2, -1) for part in sey)
    for b in range(vectors):
        for slot in range(2):
            value = cmul(sex, tuple(hxf_ref[part, b, slot] for part in parts))
            for part in parts:
                xadd_ref[part, b, slot] = value[part] if slot else -value[part]
    added = []
    for slot in range(2):
        first = slot * both
        value = cmul(sey, (hyf_ref[first:first + vectors], hyf_ref[first + vectors:first + both]))
        added += [part if slot else -part for part in value]
    rest = jnp.zeros((ny - 2 * both, nz * nx), jnp.float32)
    yadd_ref[...] = jnp.concatenate(added + [rest], axis=0).T.reshape(nz, nx, ny)
    rows = lax.broadcasted_iota(jnp.int32, (SUB, ny), 0)
    lanes = lax.broadcasted_iota(jnp.int32, (SUB, ny), 1)

    def kept(z):
        return pltpu.make_async_copy(left_ref.at[:, :, :, z], residual_hbm.at[:, :, :, z], sems.at[z])

    @pl.loop(0, nz)
    def _(z):
        for cut in tiles_of(nx):
            column = yadd_ref[z, cut]
            for b in range(vectors):
                for part in parts:

                    def turned(slot, b=b, part=part):
                        row = packed_row(slot, part, b, vectors)
                        value = pltpu.roll(column, ny - row, 1) if row else column
                        return jnp.where(lanes == 0, value, 0.0)

                    def row_of(slot, b=b, part=part):
                        return jnp.where(rows == 0, xadd_ref[part, b, slot, pl.ds(z, 1)], 0.0)

                    ex = left_ref[part, b, 0, z, cut] + turned(0)
                    ez = left_ref[part, b, 2, z, cut] + turned(1)
                    if cut.start == 0:
                        left_ref[part, b, 1, z, cut] = left_ref[part, b, 1, z, cut] + row_of(1)
                        ez = ez + row_of(0)
                    left_ref[part, b, 0, z, cut] = ex
                    left_ref[part, b, 2, z, cut] = ez
        kept(z).start()

    @pl.loop(0, nz)
    def _(z):
        kept(z).wait()


def body(fields, material, pml_width, eps_real, eps_loss, coeffs, ritz):
    _, vectors, _, nz, nx, ny = fields.shape
    f32 = lambda *shape: jax.ShapeDtypeStruct(shape, jnp.float32)
    scratch = lambda *shape: pltpu.VMEM(shape, jnp.float32)
    params = pltpu.CompilerParams(vmem_limit_bytes=40 * 1024 * 1024)
    whole = f32(*fields.shape)
    zf_shape = (2, vectors, 2, nx, ny)
    xf_shape = (2, vectors, 2, nz, ny)
    yf_shape = (4 * vectors, nz * nx)
    near, xf, yf = pl.pallas_call(
        face_kernel,
        out_shape=(whole, f32(*xf_shape), f32(*yf_shape)),
        in_specs=[HBM],
        out_specs=(VMEM,) * 3,
        scratch_shapes=[pltpu.SemaphoreType.DMA((2, 3))],
        compiler_params=params,
        name="take_faces",
    )(pltpu.with_memory_space_constraint(fields, pltpu.HBM))
    yf = passed_round(yf, "gy", -1)
    xf = passed_round(xf, "gx", -1)
    cells = fields.size // 6 // vectors

    def cost(flops, passes):
        return pl.CostEstimate(flops=flops * cells, bytes_accessed=passes * 4 * fields.size, transcendentals=0)

    planes = f32(nz, nx, ny)
    face = f32(*xf_shape)
    basis, loss, h, packed, table, sz = pl.pallas_call(
        prepare_kernel,
        out_shape=(whole, whole, whole, planes, f32(8, nx, ny), f32(4, nz, ny)),
        in_specs=[SMEM] * 4 + [VMEM] * 2,
        out_specs=(VMEM,) * 6,
        compiler_params=params,
        cost_estimate=cost(80000, 400),
        name="prepare",
    )(pml_width, eps_real, eps_loss, coeffs, near, material)
    h, xf, yt, xadd, yadd, zf = pl.pallas_call(
        slab_kernel,
        out_shape=(whole, face, f32(*yf_shape), face, planes, f32(*zf_shape)),
        in_specs=[SMEM] * 2 + [VMEM] * 4,
        out_specs=(VMEM,) * 6,
        input_output_aliases={3: 0},
        compiler_params=params,
        name="slab_face",
    )(pml_width, coeffs, basis, h, xf, yf)
    zf = passed_round(zf, "gz", 1)
    h, packed, left, acc, before, hxf, basis_new = pl.pallas_call(
        inner_kernel,
        out_shape=(whole, planes, whole, f32(vectors, 2 * vectors, SUB, ny), f32(*zf_shape), face, whole),
        in_specs=[SMEM] + [VMEM] * 8,
        out_specs=(VMEM,) * 6 + (HBM,),
        scratch_shapes=[pltpu.SemaphoreType.DMA],
        input_output_aliases={5: 0, 6: 1},
        compiler_params=params,
        cost_estimate=cost(800, 2),
        name="apply_inner",
    )(ritz, basis, loss, table, sz, h, packed, xadd, yadd)
    h, hxf, hyf = pl.pallas_call(
        last_plane_kernel,
        out_shape=(whole, face, f32(ny, nz * nx)),
        in_specs=[VMEM] * 5,
        out_specs=(VMEM,) * 3,
        input_output_aliases={2: 0, 4: 1},
        compiler_params=params,
        name="last_plane",
    )(sz, zf, h, packed, hxf)
    devices = lax.axis_size("gx") * lax.axis_size("gy") * lax.axis_size("gz")
    left, gram = pl.pallas_call(
        outer_kernel,
        out_shape=(whole, f32(devices, 4, ny)),
        in_specs=[SMEM] * 2 + [VMEM] * 13,
        out_specs=(VMEM,) * 2,
        input_output_aliases={12: 0},
        compiler_params=params,
        cost_estimate=cost(300, 1),
        name="apply_outer",
    )(pml_width, ritz, basis, loss, table, sz, h, zf, xf, yt, hxf, hyf, left, acc, before)
    gram, hxf, hyf = lax.optimization_barrier((gram, hxf, hyf))
    rows = lax.all_to_all(gram, ("gx", "gy", "gz"), 0, 0)
    from_y = passed_round(hyf, "gy", 1)
    from_x = passed_along(hxf, "gx", 1)
    _, residual = pl.pallas_call(
        rim_kernel,
        out_shape=(whole, whole),
        in_specs=[SMEM] + [VMEM] * 3,
        out_specs=(VMEM, HBM),
        scratch_shapes=[scratch(*xf_shape), scratch(nz, nx, ny), pltpu.SemaphoreType.DMA((nz,))],
        input_output_aliases={1: 0},
        compiler_params=params,
        cost_estimate=pl.CostEstimate(flops=0, bytes_accessed=0, transcendentals=0),
        name="add_rims",
    )(pml_width, left, from_x, from_y)
    rows, residual = lax.optimization_barrier((rows, residual))
    gram = pl.pallas_call(
        gather_kernel,
        out_shape=f32(2, vectors, vectors),
        in_specs=[VMEM],
        out_specs=VMEM,
        compiler_params=params,
        name="sum_rows",
    )(rows)
    return basis_new, residual, gram


def solution(mesh):
    in_specs = (P(None, None, None, "gz", "gx", "gy"), P("gz", "gx", "gy"), P(), P(), P(), P(), P())
    out_specs = (P(None, None, None, "gz", "gx", "gy"), P(None, None, None, "gz", "gx", "gy"), P())
    return jax.shard_map(body, mesh=mesh, in_specs=in_specs, out_specs=out_specs, check_vma=False)
```

```python
import functools

import jax
import jax.numpy as jnp
from jax import lax
from jax.experimental import pallas as pl
from jax.experimental.pallas import tpu as pltpu
from jax.sharding import PartitionSpec as P

OMEGA_SQ = 0.36
SIGMA_TOP = 3.0
BOUNDS = ((4, 5), (0, 1), (2, 3))
AXES = ("gz", "gx", "gy")

VMEM = pl.BlockSpec(memory_space=pltpu.VMEM)
SMEM = pl.BlockSpec(memory_space=pltpu.SMEM)
HBM = pl.BlockSpec(memory_space=pltpu.HBM)


def passed_round(value, axis, steps):
    count = lax.axis_size(axis)
    return lax.ppermute(value, axis, [(source, (source + steps) % count) for source in range(count)])


def passed_along(value, axis, steps):
    count = lax.axis_size(axis)
    leading, last = (max(0, -steps), min(count, count - steps))
    return lax.ppermute(value, axis, [(source, source + steps) for source in range(leading, last)])


def inverse_stretch(places, length, low_width, high_width):
    inside_depth = jnp.clip((low_width - places) / low_width, 0.0, 1.0) + jnp.clip(
        (places + 1.0 - length + high_width) / high_width, 0.0, 1.0
    )
    absorb = SIGMA_TOP * inside_depth * inside_depth
    scaled = 1.0 / (1.0 + absorb * absorb)
    return scaled, -absorb * scaled


def cmul(left, right):
    return (left[0] * right[0] - left[1] * right[1], left[0] * right[1] + left[1] * right[0])


def add(left, right):
    return (left[0] + right[0], left[1] + right[1])


def sub(left, right):
    return (left[0] - right[0], left[1] - right[1])


def axis_stretch(pml_ref, direction, count, places):
    total = count * lax.axis_size(AXES[direction])
    low_slot, high_slot = BOUNDS[direction]
    low = jnp.full(places.shape, pml_ref[low_slot], jnp.int32).astype(jnp.float32)
    high = jnp.full(places.shape, pml_ref[high_slot], jnp.int32).astype(jnp.float32)
    return inverse_stretch(places, jnp.float32(total), low, high)


def local_places(direction, count, shape, dim):
    start = lax.axis_index(AXES[direction]) * count
    return (lax.broadcasted_iota(jnp.int32, shape, dim) + start).astype(jnp.float32)


def one_place(direction, count, offset, shape):
    start = lax.axis_index(AXES[direction]) * count + offset
    return jnp.full(shape, start, jnp.int32).astype(jnp.float32)


def packed_row(slot, part, vector, vectors):
    return (slot * 2 + part) * vectors + vector


def has_neighbour(direction, steps):
    place = lax.axis_index(AXES[direction]) + steps
    inside = (place >= 0) & (place < lax.axis_size(AXES[direction]))
    return jnp.where(inside, 1.0, 0.0).astype(jnp.float32)


def face_kernel(fields_hbm, fields_ref, xf_ref, yf_ref, sems):
    _, vectors, _, nz, nx, ny = fields_ref.shape
    lanes = lax.broadcasted_iota(jnp.int32, (nx, ny), 1)
    copies = [
        pltpu.make_async_copy(fields_hbm.at[part, :, comp], fields_ref.at[part, :, comp], sems.at[part, comp])
        for comp in (0, 2, 1) for part in range(2)
    ]
    for copy in copies:
        copy.start()
    packed = [jnp.zeros((nx, ny), jnp.float32)] * nz
    for place, comp in enumerate((0, 2)):
        for part in range(2):
            copies[2 * place + part].wait()
            for a in range(vectors):
                row = packed_row(comp // 2, part, a, vectors)
                for z in range(nz):
                    value = fields_ref[part, a, comp, z]
                    packed[z] = jnp.where(lanes == row, pltpu.roll(value, row, 1) if row else value, packed[z])
    turned = jnp.concatenate(packed, axis=0).T
    yf_ref[...] = turned[:yf_ref.shape[0]]
    for part in range(2):
        for a in range(vectors):
            xf_ref[part, a, 1] = fields_ref[part, a, 2, :, 0, :]
    for part in range(2):
        copies[4 + part].wait()
        for a in range(vectors):
            xf_ref[part, a, 0] = fields_ref[part, a, 1, :, 0, :]


def rotated(coeffs_ref, old, b):
    new = None
    for a, value in enumerate(old):
        term = cmul((coeffs_ref[0, a, b], coeffs_ref[1, a, b]), value)
        new = term if new is None else add(new, term)
    return new


SUB = 8
SHX, SEX, SHY, SEY = range(0, 8, 2)


def field_of(ref, b, comp, z, cut):
    return tuple(ref[part, b, comp, z, cut] for part in range(2))


def tiles_of(nx):
    return [slice(SUB * t, SUB * (t + 1)) for t in range(nx // SUB)]


def prepare_kernel(
    pml_ref, eps_real_ref, eps_loss_ref, coeffs_ref, fields_ref, material_ref,
    basis_ref, loss_ref, h_ref, packed_ref, table_ref, sz_ref,
):
    _, vectors, _, nz, nx, ny = fields_ref.shape
    plane = (nx, ny)
    parts = range(2)
    for slot, direction, half, count, dim in (
        (SHX, 1, 0.5, nx, 0), (SEX, 1, 0.0, nx, 0), (SHY, 2, 0.5, ny, 1), (SEY, 2, 0.0, ny, 1),
    ):
        values = axis_stretch(pml_ref, direction, count, local_places(direction, count, plane, dim) + half)
        for part in parts:
            table_ref[slot + part] = values[part]
    for slot, half in ((0, 0.0), (2, 0.5)):
        values = axis_stretch(pml_ref, 0, nz, local_places(0, nz, (nz, ny), 0) + half)
        for part in parts:
            sz_ref[slot + part] = values[part]

    @pl.loop(0, nz)
    def _(z):
        material = material_ref[z]
        eps = []
        for source in (eps_real_ref, eps_loss_ref):
            value = jnp.zeros(plane, jnp.float32)
            for number in range(source.shape[0]):
                value = jnp.where(material == number, -OMEGA_SQ * source[number], value)
            eps.append(value)
        for comp in range(3):
            old = [(fields_ref[0, a, comp, z], fields_ref[1, a, comp, z]) for a in range(vectors)]
            for b in range(vectors):
                new = rotated(coeffs_ref, old, b)
                loss = cmul(eps, new)
                for part in parts:
                    basis_ref[part, b, comp, z] = new[part]
                    loss_ref[part, b, comp, z] = loss[part]
        packed_ref[z] = jnp.zeros(plane, jnp.float32)

    tile = (SUB, ny)
    rows = lax.broadcasted_iota(jnp.int32, tile, 0)
    lanes = lax.broadcasted_iota(jnp.int32, tile, 1)
    cuts = tiles_of(nx)

    def magnetic(b, z, last):
        shz = tuple(sz_ref[2 + part, pl.ds(z, 1)] for part in parts)
        for cut in cuts:
            u = [field_of(basis_ref, b, comp, z, cut) for comp in range(3)]

            def step_z(comp):
                if last:
                    return tuple(-value for value in u[comp])
                return sub(field_of(basis_ref, b, comp, z + 1, cut), u[comp])

            def step_x(comp):
                if cut.stop < nx:
                    ahead = field_of(basis_ref, b, comp, z, slice(cut.start + 1, cut.stop + 1))
                else:
                    ahead = tuple(jnp.where(rows == SUB - 1, 0.0, pltpu.roll(value, SUB - 1, 0)) for value in u[comp])
                return sub(ahead, u[comp])

            def step_y(comp):
                ahead = tuple(jnp.where(lanes == ny - 1, 0.0, pltpu.roll(value, ny - 1, 1)) for value in u[comp])
                return sub(ahead, u[comp])

            shx = tuple(table_ref[SHX + part, cut] for part in parts)
            shy = tuple(table_ref[SHY + part, cut] for part in parts)
            h = (
                sub(cmul(shy, step_y(2)), cmul(shz, step_z(1))),
                sub(cmul(shz, step_z(0)), cmul(shx, step_x(2))),
                sub(cmul(shx, step_x(1)), cmul(shy, step_y(0))),
            )
            for comp in range(3):
                for part in parts:
                    h_ref[part, b, comp, z, cut] = h[comp][part]
            packed = packed_ref[z, cut]
            for slot, value in enumerate((h[2], h[0])):
                for part in parts:
                    row = packed_row(slot, part, b, vectors)
                    packed = jnp.where(lanes == row, pltpu.roll(value[part], (row + 1) % ny, 1), packed)
            packed_ref[z, cut] = packed

    @pl.loop(0, nz - 1)
    def _(z):
        for b in range(vectors):
            magnetic(b, z, False)

    for b in range(vectors):
        magnetic(b, nz - 1, True)


def turn_face(coeffs_ref, direction, raw_ref, face_ref):
    inside = has_neighbour(direction, 1)
    vectors = raw_ref.shape[1]
    for slot in range(2):
        old = [(raw_ref[0, a, slot] * inside, raw_ref[1, a, slot] * inside) for a in range(vectors)]
        for b in range(vectors):
            new = rotated(coeffs_ref, old, b)
            for part in range(2):
                face_ref[part, b, slot] = new[part]


def turn_column(coeffs_ref, raw_ref, rows_ref):
    vectors = coeffs_ref.shape[1]
    inside = has_neighbour(2, 1)
    both = 2 * vectors
    shape = (both, raw_ref.shape[1])
    which = lax.broadcasted_iota(jnp.int32, shape, 0)
    turned = [jnp.zeros(shape, jnp.float32)] * 2
    for part in range(2):
        for a in range(vectors):
            column = jnp.zeros(shape, jnp.float32)
            for b in range(vectors):
                first, second = coeffs_ref[0, a, b] * inside, coeffs_ref[1, a, b] * inside
                if part:
                    first, second = -second, first
                column = jnp.where(which == b, first, column)
                column = jnp.where(which == vectors + b, second, column)
            for slot in range(2):
                row = packed_row(slot, part, a, vectors)
                turned[slot] = turned[slot] + column * raw_ref[row:row + 1]
    for slot in range(2):
        rows_ref[slot * both:(slot + 1) * both] = turned[slot]


def lane_to_last(values, slot, part, b, vectors):
    ny = values.shape[-1]
    lanes = lax.broadcasted_iota(jnp.int32, values.shape, 1)
    row = packed_row(slot, part, b, vectors)
    return jnp.where(lanes == ny - 1, pltpu.roll(values, ny - 1 - row, 1), 0.0)


def with_halos(h, b, z, cut, nx, xadd_ref, yadd_ref):
    vectors = xadd_ref.shape[1]
    column = yadd_ref[z, cut]
    hx = tuple(h[0][part] + lane_to_last(column, 1, part, b, vectors) for part in range(2))
    hz = tuple(h[2][part] + lane_to_last(column, 0, part, b, vectors) for part in range(2))
    hy = h[1]
    if cut.stop == nx:
        rows = lax.broadcasted_iota(jnp.int32, column.shape, 0)

        def row_of(slot):
            return tuple(
                jnp.where(rows == SUB - 1, xadd_ref[part, b, slot, pl.ds(z, 1)], 0.0) for part in range(2)
            )

        hy, hz = add(hy, row_of(0)), add(hz, row_of(1))
    return hx, hy, hz


def slab_kernel(
    pml_ref, coeffs_ref, basis_ref, h_in, raw_xf_ref, raw_yf_ref,
    h_ref, xf_ref, yt_ref, xadd_ref, yadd_ref, zf_ref,
):
    del h_in
    _, vectors, _, nz, nx, ny = basis_ref.shape
    parts = range(2)
    cells = nz * nx
    both = 2 * vectors
    turn_face(coeffs_ref, 1, raw_xf_ref, xf_ref)
    turn_column(coeffs_ref, raw_yf_ref, yt_ref)
    shx = axis_stretch(pml_ref, 1, nx, one_place(1, nx, nx - 1, (1, ny)) + 0.5)
    shy = axis_stretch(pml_ref, 2, ny, one_place(2, ny, ny - 1, (1, cells)) + 0.5)
    for b in range(vectors):
        for slot in range(2):
            value = cmul(shx, tuple(xf_ref[part, b, 1 - slot] for part in parts))
            for part in parts:
                xadd_ref[part, b, slot] = value[part] if slot else -value[part]
    added = []
    for slot in range(2):
        value = cmul(shy, (yt_ref[slot * both:slot * both + vectors], yt_ref[slot * both + vectors:(slot + 1) * both]))
        added += [part if slot else -part for part in value]
    rest = jnp.zeros((ny - 2 * both, cells), jnp.float32)
    yadd_ref[...] = jnp.concatenate(added + [rest], axis=0).T.reshape(nz, nx, ny)
    last = nz - 1
    lower = jnp.full((SUB, ny), lax.axis_index(AXES[0]), jnp.int32) == 0
    for b in range(vectors):
        for cut in tiles_of(nx):
            h = [field_of(h_ref, b, comp, last, cut) for comp in range(3)]
            h = with_halos(h, b, last, cut, nx, xadd_ref, yadd_ref)
            for part in parts:
                for comp in range(3):
                    h_ref[part, b, comp, last, cut] = h[comp][part]
                for comp in range(2):
                    zf_ref[part, b, comp, cut] = jnp.where(lower, h[comp][part], basis_ref[part, b, comp, 0, cut])


def plane_step(
    b, z, before, sums, ritz_ref, basis_ref, loss_ref, table_ref, sz_ref, h_ref, left_ref, halos=None
):
    _, vectors, _, _, nx, ny = basis_ref.shape
    rows = lax.broadcasted_iota(jnp.int32, (SUB, ny), 0)
    lanes = lax.broadcasted_iota(jnp.int32, (SUB, ny), 1)
    parts = range(2)
    cuts = tiles_of(nx)
    sez = tuple(sz_ref[part, pl.ds(z, 1)] for part in parts)
    fields = []
    for cut in cuts:
        h = [field_of(h_ref, b, comp, z, cut) for comp in range(3)]
        if halos is not None:
            h = with_halos(h, b, z, cut, nx, *halos)
            for comp in (1, 2):
                for part in parts:
                    h_ref[part, b, comp, z, cut] = h[comp][part]
        fields.append(h)
    sums = list(sums)
    for t, cut in enumerate(cuts):
        hx, hy, hz = fields[t]

        def back_x(comp):
            here = fields[t][comp]
            if t:
                past = field_of(h_ref, b, comp, z, slice(cut.start - 1, cut.stop - 1))
            else:
                past = tuple(jnp.where(rows == 0, 0.0, pltpu.roll(value, 1, 0)) for value in here)
            return sub(here, past)

        def back_y(value):
            return sub(value, tuple(jnp.where(lanes == 0, 0.0, pltpu.roll(part, 1, 1)) for part in value))

        sex = tuple(table_ref[SEX + part, cut] for part in parts)
        sey = tuple(table_ref[SEY + part, cut] for part in parts)
        bxy, bxz = (cmul(sex, back_x(comp)) for comp in (1, 2))
        byz, byx = (cmul(sey, back_y(value)) for value in (hz, hx))
        bzx, bzy = (cmul(sez, sub(value, past)) for value, past in zip((hx, hy), before[t]))
        curl = (sub(byz, bzy), sub(bzx, bxz), sub(bxy, byx))
        w = [add(curl[comp], field_of(loss_ref, b, comp, z, cut)) for comp in range(3)]
        for comp in range(3):
            left = sub(w[comp], cmul((ritz_ref[0, b], ritz_ref[1, b]), field_of(basis_ref, b, comp, z, cut)))
            for part in parts:
                left_ref[part, b, comp, z, cut] = left[part]
        for a in range(vectors):
            total = sums[a]
            for comp in range(3):
                total = add(total, cmul(field_of(basis_ref, a, comp, z, cut), w[comp]))
            sums[a] = total
    return [(h[0], h[1]) for h in fields], sums


def inner_kernel(
    ritz_ref, basis_ref, loss_ref, table_ref, sz_ref, h_in, packed_in, xadd_ref, yadd_ref,
    h_ref, packed_ref, left_ref, acc_ref, before_ref, hxf_ref, basis_hbm, sem,
):
    del h_in, packed_in
    _, vectors, _, nz, nx, ny = basis_ref.shape
    keep = pltpu.make_async_copy(basis_ref, basis_hbm, sem)
    keep.start()
    cuts = tiles_of(nx)
    lanes = lax.broadcasted_iota(jnp.int32, (nz, ny), 1)
    open_plane = lax.broadcasted_iota(jnp.int32, (nz, ny), 0) < nz - 1
    packed_ref[...] = packed_ref[...] + yadd_ref[...]
    corner = packed_ref[:, nx - 1, :]
    for b in range(vectors):
        for part in range(2):
            row = packed_row(0, part, b, vectors)
            more = xadd_ref[part, b, 1]
            corner = corner + jnp.where(lanes == row, pltpu.roll(more, (row + 1) % ny, 1), 0.0)
            more = more + lane_to_last(yadd_ref[:, nx - 1, :], 0, part, b, vectors)
            hxf_ref[part, b, 0] = h_ref[part, b, 1, :, nx - 1, :] + jnp.where(open_plane, xadd_ref[part, b, 0], 0.0)
            hxf_ref[part, b, 1] = h_ref[part, b, 2, :, nx - 1, :] + jnp.where(open_plane, more, 0.0)
    packed_ref[:, nx - 1, :] = corner
    acc_ref[...] = jnp.zeros(acc_ref.shape, jnp.float32)
    before_ref[...] = jnp.zeros(before_ref.shape, jnp.float32)

    @pl.loop(0, nz - 1)
    def _(z):
        for b in range(vectors):
            before = [
                tuple(tuple(before_ref[part, b, slot, cut] for part in range(2)) for slot in range(2)) for cut in cuts
            ]
            sums = [(acc_ref[b, a], acc_ref[b, vectors + a]) for a in range(vectors)]
            before, sums = plane_step(
                b, z, before, sums, ritz_ref, basis_ref, loss_ref, table_ref, sz_ref, h_ref, left_ref, (xadd_ref, yadd_ref)
            )
            for part in range(2):
                for a in range(vectors):
                    acc_ref[b, part * vectors + a] = sums[a][part]
                for t, cut in enumerate(cuts):
                    for slot in range(2):
                        before_ref[part, b, slot, cut] = before[t][slot][part]

    keep.wait()


def last_plane_kernel(sz_ref, zf_ref, h_in, packed_in, hxf_in, h_ref, hxf_ref, hyf_ref):
    del h_in, hxf_in
    _, vectors, _, nz, nx, ny = h_ref.shape
    parts = range(2)
    last = nz - 1
    lanes = lax.broadcasted_iota(jnp.int32, (SUB, ny), 1)
    shz = tuple(sz_ref[2 + part, last:] * has_neighbour(0, 1) for part in parts)
    packed = [packed_in[last, cut] for cut in tiles_of(nx)]
    for b in range(vectors):
        for t, cut in enumerate(tiles_of(nx)):
            ex, ey = (tuple(zf_ref[part, b, slot, cut] for part in parts) for slot in range(2))
            more = (tuple(-value for value in cmul(shz, ey)), cmul(shz, ex))
            for part in parts:
                for comp in range(2):
                    h_ref[part, b, comp, last, cut] = h_ref[part, b, comp, last, cut] + more[comp][part]
                row = packed_row(1, part, b, vectors)
                edge = pltpu.roll(more[0][part], (row + 1) % ny, 1)
                packed[t] = packed[t] + jnp.where(lanes == row, edge, 0.0)
                if cut.stop == nx:
                    hxf_ref[part, b, 0, last:] = hxf_ref[part, b, 0, last:] + more[1][part][SUB - 1:]
    inner = packed_in[:last].reshape(last * nx, ny)
    hyf_ref[:ny] = jnp.concatenate([inner] + packed, axis=0).T
    hyf_ref[ny:] = jnp.zeros((hyf_ref.shape[0] - ny, nz * nx), jnp.float32)


def outer_kernel(
    pml_ref, ritz_ref, basis_ref, loss_ref, table_ref, sz_ref, h_ref, zf_ref, xf_ref, yt_ref, hxf_ref, hyf_ref,
    left_in, acc_ref, before_ref, left_ref, gram_ref,
):
    del left_in
    _, vectors, _, nz, nx, ny = basis_ref.shape
    parts = range(2)
    cuts = tiles_of(nx)
    under = axis_stretch(pml_ref, 0, nz, one_place(0, nz, -1, (1, ny)) + 0.5)
    sez = tuple(sz_ref[part, 0:1] * has_neighbour(0, -1) for part in parts)
    sx_next = axis_stretch(pml_ref, 1, nx, one_place(1, nx, nx, (1, ny)))
    sy_next = axis_stretch(pml_ref, 2, ny, one_place(2, ny, ny, (1, nz * nx)))
    both = 2 * vectors
    ends = [
        cmul(sy_next, (yt_ref[slot * both:slot * both + vectors], yt_ref[slot * both + vectors:(slot + 1) * both]))
        for slot in range(2)
    ]
    columns = lax.broadcasted_iota(jnp.int32, (both, ny), 1)
    gram = jnp.zeros((both, ny), jnp.float32)
    for b in range(vectors):

        def tile_of(ref, slot, cut, b=b):
            return tuple(ref[part, b, slot, cut] for part in parts)

        before = [tuple(tile_of(before_ref, slot, cut) for slot in range(2)) for cut in cuts]
        sums = [(acc_ref[b, a], acc_ref[b, vectors + a]) for a in range(vectors)]
        _, sums = plane_step(
            b, nz - 1, before, sums, ritz_ref, basis_ref, loss_ref, table_ref, sz_ref, h_ref, left_ref
        )
        for cut in cuts:
            ex, ey = (field_of(basis_ref, b, comp, 0, cut) for comp in range(2))
            hx = sub(tile_of(zf_ref, 0, cut), cmul(under, ey))
            hy = add(tile_of(zf_ref, 1, cut), cmul(under, ex))
            more = (cmul(sez, hy), cmul(sez, hx))
            for part in parts:
                left_ref[part, b, 0, 0, cut] = left_ref[part, b, 0, 0, cut] + more[0][part]
                left_ref[part, b, 1, 0, cut] = left_ref[part, b, 1, 0, cut] - more[1][part]
            for a in range(vectors):
                ex, ey = (field_of(basis_ref, a, comp, 0, cut) for comp in range(2))
                sums[a] = add(sums[a], sub(cmul(ex, more[0]), cmul(ey, more[1])))
        h_y = tuple(hxf_ref[part, b, 0] for part in parts)
        h_z = tuple(hxf_ref[part, b, 1] for part in parts)
        for a in range(vectors):
            over = cmul(tuple(xf_ref[part, a, 0] for part in parts), h_z)
            over = sub(over, cmul(tuple(xf_ref[part, a, 1] for part in parts), h_y))
            over = cmul(sx_next, over)
            for row in range(0, nz, SUB):
                sums[a] = add(sums[a], tuple(part[row:row + SUB] for part in over))
        flat = jnp.concatenate(
            [jnp.sum(sums[a][part], axis=0, keepdims=True) for part in parts for a in range(vectors)], axis=0
        )
        over = None
        for slot in range(2):
            h = tuple(hyf_ref[packed_row(slot, part, b, vectors)][None] for part in parts)
            term = cmul(ends[slot], h)
            over = term if over is None else sub(term, over)
        side = jnp.concatenate(over, axis=0)
        total = jnp.sum(flat, axis=1, keepdims=True) + jnp.sum(side, axis=1, keepdims=True)
        gram = jnp.where(columns == b, total, gram)
    everywhere = 3.0 * nz * nx * ny
    for axis in AXES:
        everywhere = everywhere * lax.axis_size(axis)
    gram = gram * (1.0 / everywhere)
    row = tree_sum([gram[0:1]] + [pltpu.roll(gram[row:row + 1], row * vectors, 1) for row in range(1, both)])
    block = jnp.concatenate([row, jnp.zeros((gram_ref.shape[1] - 1, ny), jnp.float32)], axis=0)
    for device in range(gram_ref.shape[0]):
        gram_ref[device] = block


def tree_sum(values):
    while len(values) > 1:
        pairs = [values[place] + values[place + 1] for place in range(0, len(values) - 1, 2)]
        values = pairs + ([values[-1]] if len(values) % 2 else [])
    return values[0]


def gather_kernel(rows_ref, gram_ref):
    vectors = gram_ref.shape[1]
    total = tree_sum([rows_ref[device] for device in range(rows_ref.shape[0])])[0:1]
    count = total.shape[1]
    for part in range(2):
        for a in range(vectors):
            row = (part * vectors + a) * vectors
            turned = pltpu.roll(total, count - row, 1) if row else total
            gram_ref[part, a:a + 1] = turned[:, :vectors]


def rim_kernel(pml_ref, left_in, hxf_ref, hyf_ref, left_ref, residual_hbm, xadd_ref, yadd_ref, sems):
    del left_in
    _, vectors, _, nz, nx, ny = left_ref.shape
    parts = range(2)
    both = 2 * vectors
    sex = axis_stretch(pml_ref, 1, nx, one_place(1, nx, 0, (nz, ny)))
    sex = tuple(part * has_neighbour(1, -1) for part in sex)
    sey = axis_stretch(pml_ref, 2, ny, one_place(2, ny, 0, (vectors, nz * nx)))
    sey = tuple(part * has_neighbour(2, -1) for part in sey)
    for b in range(vectors):
        for slot in range(2):
            value = cmul(sex, tuple(hxf_ref[part, b, slot] for part in parts))
            for part in parts:
                xadd_ref[part, b, slot] = value[part] if slot else -value[part]
    added = []
    for slot in range(2):
        first = slot * both
        value = cmul(sey, (hyf_ref[first:first + vectors], hyf_ref[first + vectors:first + both]))
        added += [part if slot else -part for part in value]
    rest = jnp.zeros((ny - 2 * both, nz * nx), jnp.float32)
    yadd_ref[...] = jnp.concatenate(added + [rest], axis=0).T.reshape(nz, nx, ny)
    rows = lax.broadcasted_iota(jnp.int32, (SUB, ny), 0)
    lanes = lax.broadcasted_iota(jnp.int32, (SUB, ny), 1)

    def kept(z):
        return pltpu.make_async_copy(left_ref.at[:, :, :, z], residual_hbm.at[:, :, :, z], sems.at[z])

    @pl.loop(0, nz)
    def _(z):
        for cut in tiles_of(nx):
            column = yadd_ref[z, cut]
            for b in range(vectors):
                for part in parts:

                    def turned(slot, b=b, part=part):
                        row = packed_row(slot, part, b, vectors)
                        value = pltpu.roll(column, ny - row, 1) if row else column
                        return jnp.where(lanes == 0, value, 0.0)

                    def row_of(slot, b=b, part=part):
                        return jnp.where(rows == 0, xadd_ref[part, b, slot, pl.ds(z, 1)], 0.0)

                    ex = left_ref[part, b, 0, z, cut] + turned(0)
                    ez = left_ref[part, b, 2, z, cut] + turned(1)
                    if cut.start == 0:
                        left_ref[part, b, 1, z, cut] = left_ref[part, b, 1, z, cut] + row_of(1)
                        ez = ez + row_of(0)
                    left_ref[part, b, 0, z, cut] = ex
                    left_ref[part, b, 2, z, cut] = ez
        kept(z).start()

    @pl.loop(0, nz)
    def _(z):
        kept(z).wait()


def body(fields, material, pml_width, eps_real, eps_loss, coeffs, ritz):
    _, vectors, _, nz, nx, ny = fields.shape
    f32 = lambda *shape: jax.ShapeDtypeStruct(shape, jnp.float32)
    scratch = lambda *shape: pltpu.VMEM(shape, jnp.float32)
    params = pltpu.CompilerParams(vmem_limit_bytes=40 * 1024 * 1024)
    whole = f32(*fields.shape)
    zf_shape = (2, vectors, 2, nx, ny)
    xf_shape = (2, vectors, 2, nz, ny)
    yf_shape = (4 * vectors, nz * nx)
    near, xf, yf = pl.pallas_call(
        face_kernel,
        out_shape=(whole, f32(*xf_shape), f32(*yf_shape)),
        in_specs=[HBM],
        out_specs=(VMEM,) * 3,
        scratch_shapes=[pltpu.SemaphoreType.DMA((2, 3))],
        compiler_params=params,
        name="take_faces",
    )(pltpu.with_memory_space_constraint(fields, pltpu.HBM))
    yf = passed_round(yf, "gy", -1)
    xf = passed_round(xf, "gx", -1)
    cells = fields.size // 6 // vectors

    def cost(flops, passes):
        return pl.CostEstimate(flops=flops * cells, bytes_accessed=passes * 4 * fields.size, transcendentals=0)

    planes = f32(nz, nx, ny)
    face = f32(*xf_shape)
    basis, loss, h, packed, table, sz = pl.pallas_call(
        prepare_kernel,
        out_shape=(whole, whole, whole, planes, f32(8, nx, ny), f32(4, nz, ny)),
        in_specs=[SMEM] * 4 + [VMEM] * 2,
        out_specs=(VMEM,) * 6,
        compiler_params=params,
        cost_estimate=cost(80000, 400),
        name="prepare",
    )(pml_width, eps_real, eps_loss, coeffs, near, material)
    h, xf, yt, xadd, yadd, zf = pl.pallas_call(
        slab_kernel,
        out_shape=(whole, face, f32(*yf_shape), face, planes, f32(*zf_shape)),
        in_specs=[SMEM] * 2 + [VMEM] * 4,
        out_specs=(VMEM,) * 6,
        input_output_aliases={3: 0},
        compiler_params=params,
        name="slab_face",
    )(pml_width, coeffs, basis, h, xf, yf)
    zf = passed_round(zf, "gz", 1)
    h, packed, left, acc, before, hxf, basis_new = pl.pallas_call(
        inner_kernel,
        out_shape=(whole, planes, whole, f32(vectors, 2 * vectors, SUB, ny), f32(*zf_shape), face, whole),
        in_specs=[SMEM] + [VMEM] * 8,
        out_specs=(VMEM,) * 6 + (HBM,),
        scratch_shapes=[pltpu.SemaphoreType.DMA],
        input_output_aliases={5: 0, 6: 1},
        compiler_params=params,
        cost_estimate=cost(800, 2),
        name="apply_inner",
    )(ritz, basis, loss, table, sz, h, packed, xadd, yadd)
    h, hxf, hyf = pl.pallas_call(
        last_plane_kernel,
        out_shape=(whole, face, f32(ny + SUB, nz * nx)),
        in_specs=[VMEM] * 5,
        out_specs=(VMEM,) * 3,
        input_output_aliases={2: 0, 4: 1},
        compiler_params=params,
        name="last_plane",
    )(sz, zf, h, packed, hxf)
    devices = lax.axis_size("gx") * lax.axis_size("gy") * lax.axis_size("gz")
    left, gram = pl.pallas_call(
        outer_kernel,
        out_shape=(whole, f32(devices, 5, ny)),
        in_specs=[SMEM] * 2 + [VMEM] * 13,
        out_specs=(VMEM,) * 2,
        input_output_aliases={12: 0},
        compiler_params=params,
        cost_estimate=cost(300, 1),
        name="apply_outer",
    )(pml_width, ritz, basis, loss, table, sz, h, zf, xf, yt, hxf, hyf, left, acc, before)
    gram, hxf, hyf = lax.optimization_barrier((gram, hxf, hyf))
    rows = lax.all_to_all(gram, ("gx", "gy", "gz"), 0, 0)
    from_y = passed_round(hyf, "gy", 1)
    from_x = passed_along(hxf, "gx", 1)
    _, residual = pl.pallas_call(
        rim_kernel,
        out_shape=(whole, whole),
        in_specs=[SMEM] + [VMEM] * 3,
        out_specs=(VMEM, HBM),
        scratch_shapes=[scratch(*xf_shape), scratch(nz, nx, ny), pltpu.SemaphoreType.DMA((nz,))],
        input_output_aliases={1: 0},
        compiler_params=params,
        cost_estimate=pl.CostEstimate(flops=0, bytes_accessed=0, transcendentals=0),
        name="add_rims",
    )(pml_width, left, from_x, from_y)
    rows, residual = lax.optimization_barrier((rows, residual))
    gram = pl.pallas_call(
        gather_kernel,
        out_shape=f32(2, vectors, vectors),
        in_specs=[VMEM],
        out_specs=VMEM,
        compiler_params=params,
        name="sum_rows",
    )(rows)
    return basis_new, residual, gram


def solution(mesh):
    in_specs = (P(None, None, None, "gz", "gx", "gy"), P("gz", "gx", "gy"), P(), P(), P(), P(), P())
    out_specs = (P(None, None, None, "gz", "gx", "gy"), P(None, None, None, "gz", "gx", "gy"), P())
    return jax.shard_map(body, mesh=mesh, in_specs=in_specs, out_specs=out_specs, check_vma=False)
```

```python
import functools

import jax
import jax.numpy as jnp
from jax import lax
from jax.experimental import pallas as pl
from jax.experimental.pallas import tpu as pltpu
from jax.sharding import PartitionSpec as P

OMEGA_SQ = 0.36
SIGMA_TOP = 3.0
BOUNDS = ((4, 5), (0, 1), (2, 3))
AXES = ("gz", "gx", "gy")

VMEM = pl.BlockSpec(memory_space=pltpu.VMEM)
SMEM = pl.BlockSpec(memory_space=pltpu.SMEM)
HBM = pl.BlockSpec(memory_space=pltpu.HBM)


def passed_round(value, axis, steps):
    count = lax.axis_size(axis)
    return lax.ppermute(value, axis, [(source, (source + steps) % count) for source in range(count)])


def passed_along(value, axis, steps):
    count = lax.axis_size(axis)
    leading, last = (max(0, -steps), min(count, count - steps))
    return lax.ppermute(value, axis, [(source, source + steps) for source in range(leading, last)])


def inverse_stretch(places, length, low_width, high_width):
    inside_depth = jnp.clip((low_width - places) / low_width, 0.0, 1.0) + jnp.clip(
        (places + 1.0 - length + high_width) / high_width, 0.0, 1.0
    )
    absorb = SIGMA_TOP * inside_depth * inside_depth
    scaled = 1.0 / (1.0 + absorb * absorb)
    return scaled, -absorb * scaled


def tree_sum(values):
    while len(values) > 1:
        pairs = [values[place] + values[place + 1] for place in range(0, len(values) - 1, 2)]
        values = pairs + ([values[-1]] if len(values) % 2 else [])
    return values[0]


def cmul(left, right):
    return (left[0] * right[0] - left[1] * right[1], left[0] * right[1] + left[1] * right[0])


def add(left, right):
    return (left[0] + right[0], left[1] + right[1])


def sub(left, right):
    return (left[0] - right[0], left[1] - right[1])


def axis_stretch(pml_ref, direction, count, places):
    total = count * lax.axis_size(AXES[direction])
    low_slot, high_slot = BOUNDS[direction]
    low = jnp.full(places.shape, pml_ref[low_slot], jnp.int32).astype(jnp.float32)
    high = jnp.full(places.shape, pml_ref[high_slot], jnp.int32).astype(jnp.float32)
    return inverse_stretch(places, jnp.float32(total), low, high)


def local_places(direction, count, shape, dim):
    start = lax.axis_index(AXES[direction]) * count
    return (lax.broadcasted_iota(jnp.int32, shape, dim) + start).astype(jnp.float32)


def one_place(direction, count, offset, shape):
    start = lax.axis_index(AXES[direction]) * count + offset
    return jnp.full(shape, start, jnp.int32).astype(jnp.float32)


def packed_row(slot, part, vector, vectors):
    return (slot * 2 + part) * vectors + vector


def has_neighbour(direction, steps):
    place = lax.axis_index(AXES[direction]) + steps
    inside = (place >= 0) & (place < lax.axis_size(AXES[direction]))
    return jnp.where(inside, 1.0, 0.0).astype(jnp.float32)


def face_kernel(fields_hbm, fields_ref, xf_ref, yf_ref, sems):
    _, vectors, _, nz, nx, ny = fields_ref.shape
    lanes = lax.broadcasted_iota(jnp.int32, (nx, ny), 1)
    copies = [
        pltpu.make_async_copy(fields_hbm.at[part, :, comp], fields_ref.at[part, :, comp], sems.at[part, comp])
        for comp in (0, 2, 1) for part in range(2)
    ]
    for copy in copies:
        copy.start()
    packed = [jnp.zeros((nx, ny), jnp.float32)] * nz
    for place, comp in enumerate((0, 2)):
        for part in range(2):
            copies[2 * place + part].wait()
            for a in range(vectors):
                row = packed_row(comp // 2, part, a, vectors)
                for z in range(nz):
                    value = fields_ref[part, a, comp, z]
                    packed[z] = jnp.where(lanes == row, pltpu.roll(value, row, 1) if row else value, packed[z])
    turned = jnp.concatenate(packed, axis=0).T
    yf_ref[...] = turned[:yf_ref.shape[0]]
    for part in range(2):
        for a in range(vectors):
            xf_ref[part, a, 1] = fields_ref[part, a, 2, :, 0, :]
    for part in range(2):
        copies[4 + part].wait()
        for a in range(vectors):
            xf_ref[part, a, 0] = fields_ref[part, a, 1, :, 0, :]


def rotated(coeffs_ref, old, b):
    new = None
    for a, value in enumerate(old):
        term = cmul((coeffs_ref[0, a, b], coeffs_ref[1, a, b]), value)
        new = term if new is None else add(new, term)
    return new


SUB = 8
SHX, SEX, SHY, SEY = range(0, 8, 2)


def field_of(ref, b, comp, z, cut):
    return tuple(ref[part, b, comp, z, cut] for part in range(2))


def tiles_of(nx):
    return [slice(SUB * t, SUB * (t + 1)) for t in range(nx // SUB)]


def prepare_kernel(
    pml_ref, eps_real_ref, eps_loss_ref, coeffs_ref, fields_ref, material_ref,
    basis_ref, eps_ref, h_ref, packed_ref, table_ref, sz_ref,
):
    _, vectors, _, nz, nx, ny = fields_ref.shape
    plane = (nx, ny)
    parts = range(2)
    for slot, direction, half, count, dim in (
        (SHX, 1, 0.5, nx, 0), (SEX, 1, 0.0, nx, 0), (SHY, 2, 0.5, ny, 1), (SEY, 2, 0.0, ny, 1),
    ):
        values = axis_stretch(pml_ref, direction, count, local_places(direction, count, plane, dim) + half)
        for part in parts:
            table_ref[slot + part] = values[part]
    for slot, half in ((0, 0.0), (2, 0.5)):
        values = axis_stretch(pml_ref, 0, nz, local_places(0, nz, (nz, ny), 0) + half)
        for part in parts:
            sz_ref[slot + part] = values[part]

    @pl.loop(0, nz)
    def _(z):
        material = material_ref[z]
        for part, source in enumerate((eps_real_ref, eps_loss_ref)):
            value = jnp.zeros(plane, jnp.float32)
            for number in range(source.shape[0]):
                value = jnp.where(material == number, -OMEGA_SQ * source[number], value)
            eps_ref[part, z] = value
        for comp in range(3):
            real = [fields_ref[0, a, comp, z] for a in range(vectors)]
            imag = [fields_ref[1, a, comp, z] for a in range(vectors)]
            both = [first + second for first, second in zip(real, imag)]
            for b in range(vectors):
                turns = [(coeffs_ref[0, a, b], coeffs_ref[1, a, b]) for a in range(vectors)]
                shared = tree_sum([turn[0] * value for turn, value in zip(turns, both)])
                less = tree_sum([(turn[0] + turn[1]) * value for turn, value in zip(turns, imag)])
                more = tree_sum([(turn[1] - turn[0]) * value for turn, value in zip(turns, real)])
                basis_ref[0, b, comp, z] = shared - less
                basis_ref[1, b, comp, z] = shared + more
        packed_ref[z] = jnp.zeros(plane, jnp.float32)

    tile = (SUB, ny)
    rows = lax.broadcasted_iota(jnp.int32, tile, 0)
    lanes = lax.broadcasted_iota(jnp.int32, tile, 1)
    cuts = tiles_of(nx)

    def magnetic(b, z, last):
        shz = tuple(sz_ref[2 + part, pl.ds(z, 1)] for part in parts)
        for cut in cuts:
            u = [field_of(basis_ref, b, comp, z, cut) for comp in range(3)]

            def step_z(comp):
                if last:
                    return tuple(-value for value in u[comp])
                return sub(field_of(basis_ref, b, comp, z + 1, cut), u[comp])

            def step_x(comp):
                if cut.stop < nx:
                    ahead = field_of(basis_ref, b, comp, z, slice(cut.start + 1, cut.stop + 1))
                else:
                    ahead = tuple(jnp.where(rows == SUB - 1, 0.0, pltpu.roll(value, SUB - 1, 0)) for value in u[comp])
                return sub(ahead, u[comp])

            def step_y(comp):
                ahead = tuple(jnp.where(lanes == ny - 1, 0.0, pltpu.roll(value, ny - 1, 1)) for value in u[comp])
                return sub(ahead, u[comp])

            shx = tuple(table_ref[SHX + part, cut] for part in parts)
            shy = tuple(table_ref[SHY + part, cut] for part in parts)
            h = (
                sub(cmul(shy, step_y(2)), cmul(shz, step_z(1))),
                sub(cmul(shz, step_z(0)), cmul(shx, step_x(2))),
                sub(cmul(shx, step_x(1)), cmul(shy, step_y(0))),
            )
            for comp in range(3):
                for part in parts:
                    h_ref[part, b, comp, z, cut] = h[comp][part]
            packed = packed_ref[z, cut]
            for slot, value in enumerate((h[2], h[0])):
                for part in parts:
                    row = packed_row(slot, part, b, vectors)
                    packed = jnp.where(lanes == row, pltpu.roll(value[part], (row + 1) % ny, 1), packed)
            packed_ref[z, cut] = packed

    @pl.loop(0, nz - 1)
    def _(z):
        for b in range(vectors):
            magnetic(b, z, False)

    for b in range(vectors):
        magnetic(b, nz - 1, True)


def turn_face(coeffs_ref, direction, raw_ref, face_ref):
    inside = has_neighbour(direction, 1)
    vectors = raw_ref.shape[1]
    for slot in range(2):
        old = [(raw_ref[0, a, slot] * inside, raw_ref[1, a, slot] * inside) for a in range(vectors)]
        for b in range(vectors):
            new = rotated(coeffs_ref, old, b)
            for part in range(2):
                face_ref[part, b, slot] = new[part]


def turn_column(coeffs_ref, raw_ref, rows_ref):
    vectors = coeffs_ref.shape[1]
    inside = has_neighbour(2, 1)
    both = 2 * vectors
    shape = (both, raw_ref.shape[1])
    which = lax.broadcasted_iota(jnp.int32, shape, 0)
    turned = [jnp.zeros(shape, jnp.float32)] * 2
    for part in range(2):
        for a in range(vectors):
            column = jnp.zeros(shape, jnp.float32)
            for b in range(vectors):
                first, second = coeffs_ref[0, a, b] * inside, coeffs_ref[1, a, b] * inside
                if part:
                    first, second = -second, first
                column = jnp.where(which == b, first, column)
                column = jnp.where(which == vectors + b, second, column)
            for slot in range(2):
                row = packed_row(slot, part, a, vectors)
                turned[slot] = turned[slot] + column * raw_ref[row:row + 1]
    for slot in range(2):
        rows_ref[slot * both:(slot + 1) * both] = turned[slot]


def lane_to_last(values, slot, part, b, vectors):
    ny = values.shape[-1]
    lanes = lax.broadcasted_iota(jnp.int32, values.shape, 1)
    row = packed_row(slot, part, b, vectors)
    return jnp.where(lanes == ny - 1, pltpu.roll(values, ny - 1 - row, 1), 0.0)


def with_halos(h, b, z, cut, nx, xadd_ref, yadd_ref):
    vectors = xadd_ref.shape[1]
    column = yadd_ref[z, cut]
    hx = tuple(h[0][part] + lane_to_last(column, 1, part, b, vectors) for part in range(2))
    hz = tuple(h[2][part] + lane_to_last(column, 0, part, b, vectors) for part in range(2))
    hy = h[1]
    if cut.stop == nx:
        rows = lax.broadcasted_iota(jnp.int32, column.shape, 0)

        def row_of(slot):
            return tuple(
                jnp.where(rows == SUB - 1, xadd_ref[part, b, slot, pl.ds(z, 1)], 0.0) for part in range(2)
            )

        hy, hz = add(hy, row_of(0)), add(hz, row_of(1))
    return hx, hy, hz


def slab_kernel(
    pml_ref, coeffs_ref, basis_ref, h_in, raw_xf_ref, raw_yf_ref,
    h_ref, xf_ref, yt_ref, xadd_ref, yadd_ref, zf_ref,
):
    del h_in
    _, vectors, _, nz, nx, ny = basis_ref.shape
    parts = range(2)
    cells = nz * nx
    both = 2 * vectors
    turn_face(coeffs_ref, 1, raw_xf_ref, xf_ref)
    turn_column(coeffs_ref, raw_yf_ref, yt_ref)
    shx = axis_stretch(pml_ref, 1, nx, one_place(1, nx, nx - 1, (1, ny)) + 0.5)
    shy = axis_stretch(pml_ref, 2, ny, one_place(2, ny, ny - 1, (1, cells)) + 0.5)
    for b in range(vectors):
        for slot in range(2):
            value = cmul(shx, tuple(xf_ref[part, b, 1 - slot] for part in parts))
            for part in parts:
                xadd_ref[part, b, slot] = value[part] if slot else -value[part]
    added = []
    for slot in range(2):
        value = cmul(shy, (yt_ref[slot * both:slot * both + vectors], yt_ref[slot * both + vectors:(slot + 1) * both]))
        added += [part if slot else -part for part in value]
    rest = jnp.zeros((ny - 2 * both, cells), jnp.float32)
    yadd_ref[...] = jnp.concatenate(added + [rest], axis=0).T.reshape(nz, nx, ny)
    last = nz - 1
    lower = jnp.full((SUB, ny), lax.axis_index(AXES[0]), jnp.int32) == 0
    for b in range(vectors):
        for cut in tiles_of(nx):
            h = [field_of(h_ref, b, comp, last, cut) for comp in range(3)]
            h = with_halos(h, b, last, cut, nx, xadd_ref, yadd_ref)
            for part in parts:
                for comp in range(3):
                    h_ref[part, b, comp, last, cut] = h[comp][part]
                for comp in range(2):
                    zf_ref[part, b, comp, cut] = jnp.where(lower, h[comp][part], basis_ref[part, b, comp, 0, cut])


def plane_step(
    b, z, before, sums, ritz_ref, basis_ref, eps_ref, table_ref, sz_ref, h_ref, left_ref, halos=None
):
    _, vectors, _, _, nx, ny = basis_ref.shape
    rows = lax.broadcasted_iota(jnp.int32, (SUB, ny), 0)
    lanes = lax.broadcasted_iota(jnp.int32, (SUB, ny), 1)
    parts = range(2)
    cuts = tiles_of(nx)
    sez = tuple(sz_ref[part, pl.ds(z, 1)] for part in parts)
    fields = []
    for cut in cuts:
        h = [field_of(h_ref, b, comp, z, cut) for comp in range(3)]
        if halos is not None:
            h = with_halos(h, b, z, cut, nx, *halos)
            for comp in (1, 2):
                for part in parts:
                    h_ref[part, b, comp, z, cut] = h[comp][part]
        fields.append(h)
    sums = list(sums)
    for t, cut in enumerate(cuts):
        hx, hy, hz = fields[t]

        def back_x(comp):
            here = fields[t][comp]
            if t:
                past = field_of(h_ref, b, comp, z, slice(cut.start - 1, cut.stop - 1))
            else:
                past = tuple(jnp.where(rows == 0, 0.0, pltpu.roll(value, 1, 0)) for value in here)
            return sub(here, past)

        def back_y(value):
            return sub(value, tuple(jnp.where(lanes == 0, 0.0, pltpu.roll(part, 1, 1)) for part in value))

        sex = tuple(table_ref[SEX + part, cut] for part in parts)
        sey = tuple(table_ref[SEY + part, cut] for part in parts)
        bxy, bxz = (cmul(sex, back_x(comp)) for comp in (1, 2))
        byz, byx = (cmul(sey, back_y(value)) for value in (hz, hx))
        bzx, bzy = (cmul(sez, sub(value, past)) for value, past in zip((hx, hy), before[t]))
        curl = (sub(byz, bzy), sub(bzx, bxz), sub(bxy, byx))
        u = [field_of(basis_ref, b, comp, z, cut) for comp in range(3)]
        eps = tuple(eps_ref[part, z, cut] for part in parts)
        w = [add(curl[comp], cmul(eps, u[comp])) for comp in range(3)]
        for comp in range(3):
            left = sub(w[comp], cmul((ritz_ref[0, b], ritz_ref[1, b]), u[comp]))
            for part in parts:
                left_ref[part, b, comp, z, cut] = left[part]
        for a in range(vectors):
            total = sums[a]
            for comp in range(3):
                total = add(total, cmul(field_of(basis_ref, a, comp, z, cut), w[comp]))
            sums[a] = total
    return [(h[0], h[1]) for h in fields], sums


def inner_kernel(
    ritz_ref, basis_ref, eps_ref, table_ref, sz_ref, h_in, packed_in, xadd_ref, yadd_ref,
    h_ref, packed_ref, left_ref, acc_ref, before_ref, hxf_ref, basis_hbm, sem,
):
    del h_in, packed_in
    _, vectors, _, nz, nx, ny = basis_ref.shape
    keep = pltpu.make_async_copy(basis_ref, basis_hbm, sem)
    keep.start()
    cuts = tiles_of(nx)
    lanes = lax.broadcasted_iota(jnp.int32, (nz, ny), 1)
    open_plane = lax.broadcasted_iota(jnp.int32, (nz, ny), 0) < nz - 1
    packed_ref[...] = packed_ref[...] + yadd_ref[...]
    corner = packed_ref[:, nx - 1, :]
    for b in range(vectors):
        for part in range(2):
            row = packed_row(0, part, b, vectors)
            more = xadd_ref[part, b, 1]
            corner = corner + jnp.where(lanes == row, pltpu.roll(more, (row + 1) % ny, 1), 0.0)
            more = more + lane_to_last(yadd_ref[:, nx - 1, :], 0, part, b, vectors)
            hxf_ref[part, b, 0] = h_ref[part, b, 1, :, nx - 1, :] + jnp.where(open_plane, xadd_ref[part, b, 0], 0.0)
            hxf_ref[part, b, 1] = h_ref[part, b, 2, :, nx - 1, :] + jnp.where(open_plane, more, 0.0)
    packed_ref[:, nx - 1, :] = corner
    acc_ref[...] = jnp.zeros(acc_ref.shape, jnp.float32)
    before_ref[...] = jnp.zeros(before_ref.shape, jnp.float32)

    @pl.loop(0, nz - 1)
    def _(z):
        for b in range(vectors):
            before = [
                tuple(tuple(before_ref[part, b, slot, cut] for part in range(2)) for slot in range(2)) for cut in cuts
            ]
            sums = [(acc_ref[b, a], acc_ref[b, vectors + a]) for a in range(vectors)]
            before, sums = plane_step(
                b, z, before, sums, ritz_ref, basis_ref, eps_ref, table_ref, sz_ref, h_ref, left_ref, (xadd_ref, yadd_ref)
            )
            for part in range(2):
                for a in range(vectors):
                    acc_ref[b, part * vectors + a] = sums[a][part]
                for t, cut in enumerate(cuts):
                    for slot in range(2):
                        before_ref[part, b, slot, cut] = before[t][slot][part]

    keep.wait()


def close_last_plane(sz_ref, zf_ref, packed_in, h_ref, hxf_ref, hyf_ref):
    _, vectors, _, nz, nx, ny = h_ref.shape
    parts = range(2)
    last = nz - 1
    lanes = lax.broadcasted_iota(jnp.int32, (SUB, ny), 1)
    shz = tuple(sz_ref[2 + part, last:] * has_neighbour(0, 1) for part in parts)
    packed = [packed_in[last, cut] for cut in tiles_of(nx)]
    for b in range(vectors):
        for t, cut in enumerate(tiles_of(nx)):
            ex, ey = (tuple(zf_ref[part, b, slot, cut] for part in parts) for slot in range(2))
            more = (tuple(-value for value in cmul(shz, ey)), cmul(shz, ex))
            for part in parts:
                for comp in range(2):
                    h_ref[part, b, comp, last, cut] = h_ref[part, b, comp, last, cut] + more[comp][part]
                row = packed_row(1, part, b, vectors)
                edge = pltpu.roll(more[0][part], (row + 1) % ny, 1)
                packed[t] = packed[t] + jnp.where(lanes == row, edge, 0.0)
                if cut.stop == nx:
                    hxf_ref[part, b, 0, last:] = hxf_ref[part, b, 0, last:] + more[1][part][SUB - 1:]
    inner = packed_in[:last].reshape(last * nx, ny)
    hyf_ref[...] = jnp.concatenate([inner] + packed, axis=0).T[:hyf_ref.shape[0]]


def outer_kernel(
    pml_ref, ritz_ref, basis_ref, eps_ref, table_ref, sz_ref, h_in, zf_ref, xf_ref, yt_ref, hxf_in, packed_in,
    left_in, acc_ref, before_ref, left_ref, gram_ref, h_ref, hxf_ref, hyf_ref,
):
    del left_in, h_in, hxf_in
    close_last_plane(sz_ref, zf_ref, packed_in, h_ref, hxf_ref, hyf_ref)
    _, vectors, _, nz, nx, ny = basis_ref.shape
    parts = range(2)
    cuts = tiles_of(nx)
    under = axis_stretch(pml_ref, 0, nz, one_place(0, nz, -1, (1, ny)) + 0.5)
    sez = tuple(sz_ref[part, 0:1] * has_neighbour(0, -1) for part in parts)
    sx_next = axis_stretch(pml_ref, 1, nx, one_place(1, nx, nx, (1, ny)))
    sy_next = axis_stretch(pml_ref, 2, ny, one_place(2, ny, ny, (1, nz * nx)))
    both = 2 * vectors
    ends = [
        cmul(sy_next, (yt_ref[slot * both:slot * both + vectors], yt_ref[slot * both + vectors:(slot + 1) * both]))
        for slot in range(2)
    ]
    columns = lax.broadcasted_iota(jnp.int32, (both, ny), 1)
    gram = jnp.zeros((both, ny), jnp.float32)
    for b in range(vectors):

        def tile_of(ref, slot, cut, b=b):
            return tuple(ref[part, b, slot, cut] for part in parts)

        before = [tuple(tile_of(before_ref, slot, cut) for slot in range(2)) for cut in cuts]
        sums = [(acc_ref[b, a], acc_ref[b, vectors + a]) for a in range(vectors)]
        _, sums = plane_step(
            b, nz - 1, before, sums, ritz_ref, basis_ref, eps_ref, table_ref, sz_ref, h_ref, left_ref
        )
        for cut in cuts:
            ex, ey = (field_of(basis_ref, b, comp, 0, cut) for comp in range(2))
            hx = sub(tile_of(zf_ref, 0, cut), cmul(under, ey))
            hy = add(tile_of(zf_ref, 1, cut), cmul(under, ex))
            more = (cmul(sez, hy), cmul(sez, hx))
            for part in parts:
                left_ref[part, b, 0, 0, cut] = left_ref[part, b, 0, 0, cut] + more[0][part]
                left_ref[part, b, 1, 0, cut] = left_ref[part, b, 1, 0, cut] - more[1][part]
            for a in range(vectors):
                ex, ey = (field_of(basis_ref, a, comp, 0, cut) for comp in range(2))
                sums[a] = add(sums[a], sub(cmul(ex, more[0]), cmul(ey, more[1])))
        h_y = tuple(hxf_ref[part, b, 0] for part in parts)
        h_z = tuple(hxf_ref[part, b, 1] for part in parts)
        for a in range(vectors):
            over = cmul(tuple(xf_ref[part, a, 0] for part in parts), h_z)
            over = sub(over, cmul(tuple(xf_ref[part, a, 1] for part in parts), h_y))
            over = cmul(sx_next, over)
            for row in range(0, nz, SUB):
                sums[a] = add(sums[a], tuple(part[row:row + SUB] for part in over))
        flat = jnp.concatenate(
            [jnp.sum(sums[a][part], axis=0, keepdims=True) for part in parts for a in range(vectors)], axis=0
        )
        over = None
        for slot in range(2):
            h = tuple(hyf_ref[packed_row(slot, part, b, vectors)][None] for part in parts)
            term = cmul(ends[slot], h)
            over = term if over is None else sub(term, over)
        side = jnp.concatenate(over, axis=0)
        total = jnp.sum(flat, axis=1, keepdims=True) + jnp.sum(side, axis=1, keepdims=True)
        gram = jnp.where(columns == b, total, gram)
    everywhere = 3.0 * nz * nx * ny
    for axis in AXES:
        everywhere = everywhere * lax.axis_size(axis)
    gram = gram * (1.0 / everywhere)
    row = tree_sum([gram[0:1]] + [pltpu.roll(gram[row:row + 1], row * vectors, 1) for row in range(1, both)])
    block = jnp.concatenate([row, jnp.zeros((gram_ref.shape[1] - 1, ny), jnp.float32)], axis=0)
    for device in range(gram_ref.shape[0]):
        gram_ref[device] = block


def gather_kernel(rows_ref, gram_ref):
    vectors = gram_ref.shape[1]
    total = tree_sum([rows_ref[device] for device in range(rows_ref.shape[0])])[0:1]
    count = total.shape[1]
    for part in range(2):
        for a in range(vectors):
            row = (part * vectors + a) * vectors
            turned = pltpu.roll(total, count - row, 1) if row else total
            gram_ref[part, a:a + 1] = turned[:, :vectors]


def rim_kernel(pml_ref, left_in, hxf_ref, hyf_ref, left_ref, residual_hbm, xadd_ref, yadd_ref, sems):
    del left_in
    _, vectors, _, nz, nx, ny = left_ref.shape
    parts = range(2)
    both = 2 * vectors
    sex = axis_stretch(pml_ref, 1, nx, one_place(1, nx, 0, (nz, ny)))
    sex = tuple(part * has_neighbour(1, -1) for part in sex)
    sey = axis_stretch(pml_ref, 2, ny, one_place(2, ny, 0, (vectors, nz * nx)))
    sey = tuple(part * has_neighbour(2, -1) for part in sey)
    for b in range(vectors):
        for slot in range(2):
            value = cmul(sex, tuple(hxf_ref[part, b, slot] for part in parts))
            for part in parts:
                xadd_ref[part, b, slot] = value[part] if slot else -value[part]
    added = []
    for slot in range(2):
        first = slot * both
        value = cmul(sey, (hyf_ref[first:first + vectors], hyf_ref[first + vectors:first + both]))
        added += [part if slot else -part for part in value]
    rest = jnp.zeros((ny - 2 * both, nz * nx), jnp.float32)
    yadd_ref[...] = jnp.concatenate(added + [rest], axis=0).T.reshape(nz, nx, ny)
    rows = lax.broadcasted_iota(jnp.int32, (SUB, ny), 0)
    lanes = lax.broadcasted_iota(jnp.int32, (SUB, ny), 1)

    def kept(z):
        return pltpu.make_async_copy(left_ref.at[:, :, :, z], residual_hbm.at[:, :, :, z], sems.at[z])

    @pl.loop(0, nz)
    def _(z):
        for cut in tiles_of(nx):
            column = yadd_ref[z, cut]
            for b in range(vectors):
                for part in parts:

                    def turned(slot, b=b, part=part):
                        row = packed_row(slot, part, b, vectors)
                        value = pltpu.roll(column, ny - row, 1) if row else column
                        return jnp.where(lanes == 0, value, 0.0)

                    def row_of(slot, b=b, part=part):
                        return jnp.where(rows == 0, xadd_ref[part, b, slot, pl.ds(z, 1)], 0.0)

                    ex = left_ref[part, b, 0, z, cut] + turned(0)
                    ez = left_ref[part, b, 2, z, cut] + turned(1)
                    if cut.start == 0:
                        left_ref[part, b, 1, z, cut] = left_ref[part, b, 1, z, cut] + row_of(1)
                        ez = ez + row_of(0)
                    left_ref[part, b, 0, z, cut] = ex
                    left_ref[part, b, 2, z, cut] = ez
        kept(z).start()

    @pl.loop(0, nz)
    def _(z):
        kept(z).wait()


def body(fields, material, pml_width, eps_real, eps_loss, coeffs, ritz):
    _, vectors, _, nz, nx, ny = fields.shape
    f32 = lambda *shape: jax.ShapeDtypeStruct(shape, jnp.float32)
    scratch = lambda *shape: pltpu.VMEM(shape, jnp.float32)
    params = pltpu.CompilerParams(vmem_limit_bytes=40 * 1024 * 1024)
    whole = f32(*fields.shape)
    zf_shape = (2, vectors, 2, nx, ny)
    xf_shape = (2, vectors, 2, nz, ny)
    yf_shape = (4 * vectors, nz * nx)
    near, xf, yf = pl.pallas_call(
        face_kernel,
        out_shape=(whole, f32(*xf_shape), f32(*yf_shape)),
        in_specs=[HBM],
        out_specs=(VMEM,) * 3,
        scratch_shapes=[pltpu.SemaphoreType.DMA((2, 3))],
        compiler_params=params,
        name="take_faces",
    )(pltpu.with_memory_space_constraint(fields, pltpu.HBM))
    xf = passed_round(xf, "gx", -1)
    yf = passed_round(yf, "gy", -1)
    cells = fields.size // 6 // vectors

    def cost(flops, passes):
        return pl.CostEstimate(flops=flops * cells, bytes_accessed=passes * 4 * fields.size, transcendentals=0)

    planes = f32(nz, nx, ny)
    face = f32(*xf_shape)
    basis, eps, h, packed, table, sz = pl.pallas_call(
        prepare_kernel,
        out_shape=(whole, f32(2, nz, nx, ny), whole, planes, f32(8, nx, ny), f32(4, nz, ny)),
        in_specs=[SMEM] * 4 + [VMEM] * 2,
        out_specs=(VMEM,) * 6,
        compiler_params=params,
        cost_estimate=cost(800, 4),
        name="prepare",
    )(pml_width, eps_real, eps_loss, coeffs, near, material)
    h, xf, yt, xadd, yadd, zf = pl.pallas_call(
        slab_kernel,
        out_shape=(whole, face, f32(*yf_shape), face, planes, f32(*zf_shape)),
        in_specs=[SMEM] * 2 + [VMEM] * 4,
        out_specs=(VMEM,) * 6,
        input_output_aliases={3: 0},
        compiler_params=params,
        name="slab_face",
    )(pml_width, coeffs, basis, h, xf, yf)
    zf = passed_round(zf, "gz", 1)
    h, packed, left, acc, before, hxf, basis_new = pl.pallas_call(
        inner_kernel,
        out_shape=(whole, planes, whole, f32(vectors, 2 * vectors, SUB, ny), f32(*zf_shape), face, whole),
        in_specs=[SMEM] + [VMEM] * 8,
        out_specs=(VMEM,) * 6 + (HBM,),
        scratch_shapes=[pltpu.SemaphoreType.DMA],
        input_output_aliases={5: 0, 6: 1},
        compiler_params=params,
        cost_estimate=cost(800, 2),
        name="apply_inner",
    )(ritz, basis, eps, table, sz, h, packed, xadd, yadd)
    devices = lax.axis_size("gx") * lax.axis_size("gy") * lax.axis_size("gz")
    left, gram, _, hxf, hyf = pl.pallas_call(
        outer_kernel,
        out_shape=(whole, f32(devices, 4, ny), whole, face, f32(*yf_shape)),
        in_specs=[SMEM] * 2 + [VMEM] * 13,
        out_specs=(VMEM,) * 5,
        input_output_aliases={12: 0, 6: 2, 10: 3},
        compiler_params=params,
        cost_estimate=cost(300, 1),
        name="apply_outer",
    )(pml_width, ritz, basis, eps, table, sz, h, zf, xf, yt, hxf, packed, left, acc, before)
    gram, hxf, hyf = lax.optimization_barrier((gram, hxf, hyf))
    rows = lax.all_to_all(gram, ("gx", "gy", "gz"), 0, 0)
    from_x = passed_along(hxf, "gx", 1)
    from_y = passed_round(hyf, "gy", 1)
    _, residual = pl.pallas_call(
        rim_kernel,
        out_shape=(whole, whole),
        in_specs=[SMEM] + [VMEM] * 3,
        out_specs=(VMEM, HBM),
        scratch_shapes=[scratch(*xf_shape), scratch(nz, nx, ny), pltpu.SemaphoreType.DMA((nz,))],
        input_output_aliases={1: 0},
        compiler_params=params,
        cost_estimate=pl.CostEstimate(flops=0, bytes_accessed=0, transcendentals=0),
        name="add_rims",
    )(pml_width, left, from_x, from_y)
    rows, residual = lax.optimization_barrier((rows, residual))
    gram = pl.pallas_call(
        gather_kernel,
        out_shape=f32(2, vectors, vectors),
        in_specs=[VMEM],
        out_specs=VMEM,
        compiler_params=params,
        name="sum_rows",
    )(rows)
    return basis_new, residual, gram


def solution(mesh):
    in_specs = (P(None, None, None, "gz", "gx", "gy"), P("gz", "gx", "gy"), P(), P(), P(), P(), P())
    out_specs = (P(None, None, None, "gz", "gx", "gy"), P(None, None, None, "gz", "gx", "gy"), P())
    return jax.shard_map(body, mesh=mesh, in_specs=in_specs, out_specs=out_specs, check_vma=False)
```

```python
import functools

import jax
import jax.numpy as jnp
from jax import lax
from jax.experimental import pallas as pl
from jax.experimental.pallas import tpu as pltpu
from jax.sharding import PartitionSpec as P

OMEGA_SQ = 0.36
SIGMA_TOP = 3.0
BOUNDS = ((4, 5), (0, 1), (2, 3))
AXES = ("gz", "gx", "gy")

VMEM = pl.BlockSpec(memory_space=pltpu.VMEM)
SMEM = pl.BlockSpec(memory_space=pltpu.SMEM)
HBM = pl.BlockSpec(memory_space=pltpu.HBM)


def passed_round(value, axis, steps):
    count = lax.axis_size(axis)
    return lax.ppermute(value, axis, [(source, (source + steps) % count) for source in range(count)])


def passed_along(value, axis, steps):
    count = lax.axis_size(axis)
    leading, last = (max(0, -steps), min(count, count - steps))
    return lax.ppermute(value, axis, [(source, source + steps) for source in range(leading, last)])


def inverse_stretch(places, length, low_width, high_width):
    inside_depth = jnp.clip((low_width - places) / low_width, 0.0, 1.0) + jnp.clip(
        (places + 1.0 - length + high_width) / high_width, 0.0, 1.0
    )
    absorb = SIGMA_TOP * inside_depth * inside_depth
    scaled = 1.0 / (1.0 + absorb * absorb)
    return scaled, -absorb * scaled


def tree_sum(values):
    while len(values) > 1:
        pairs = [values[place] + values[place + 1] for place in range(0, len(values) - 1, 2)]
        values = pairs + ([values[-1]] if len(values) % 2 else [])
    return values[0]


def cmul(left, right):
    return (left[0] * right[0] - left[1] * right[1], left[0] * right[1] + left[1] * right[0])


def add(left, right):
    return (left[0] + right[0], left[1] + right[1])


def sub(left, right):
    return (left[0] - right[0], left[1] - right[1])


def axis_stretch(pml_ref, direction, count, places):
    total = count * lax.axis_size(AXES[direction])
    low_slot, high_slot = BOUNDS[direction]
    low = jnp.full(places.shape, pml_ref[low_slot], jnp.int32).astype(jnp.float32)
    high = jnp.full(places.shape, pml_ref[high_slot], jnp.int32).astype(jnp.float32)
    return inverse_stretch(places, jnp.float32(total), low, high)


def local_places(direction, count, shape, dim):
    start = lax.axis_index(AXES[direction]) * count
    return (lax.broadcasted_iota(jnp.int32, shape, dim) + start).astype(jnp.float32)


def one_place(direction, count, offset, shape):
    start = lax.axis_index(AXES[direction]) * count + offset
    return jnp.full(shape, start, jnp.int32).astype(jnp.float32)


def packed_row(slot, part, vector, vectors):
    return (slot * 2 + part) * vectors + vector


def has_neighbour(direction, steps):
    place = lax.axis_index(AXES[direction]) + steps
    inside = (place >= 0) & (place < lax.axis_size(AXES[direction]))
    return jnp.where(inside, 1.0, 0.0).astype(jnp.float32)


def face_kernel(fields_hbm, fields_ref, xf_ref, yf_ref, sems):
    _, vectors, _, nz, nx, ny = fields_ref.shape
    lanes = lax.broadcasted_iota(jnp.int32, (nx, ny), 1)
    copies = [
        pltpu.make_async_copy(fields_hbm.at[part, :, comp], fields_ref.at[part, :, comp], sems.at[part, comp])
        for comp in (0, 2, 1) for part in range(2)
    ]
    for copy in copies:
        copy.start()
    packed = [jnp.zeros((nx, ny), jnp.float32)] * nz
    for place, comp in enumerate((0, 2)):
        for part in range(2):
            copies[2 * place + part].wait()
            for a in range(vectors):
                row = packed_row(comp // 2, part, a, vectors)
                for z in range(nz):
                    value = fields_ref[part, a, comp, z]
                    packed[z] = jnp.where(lanes == row, pltpu.roll(value, row, 1) if row else value, packed[z])
    turned = jnp.concatenate(packed, axis=0).T
    yf_ref[...] = turned[:yf_ref.shape[0]]
    for part in range(2):
        for a in range(vectors):
            xf_ref[part, a, 1] = fields_ref[part, a, 2, :, 0, :]
    for part in range(2):
        copies[4 + part].wait()
        for a in range(vectors):
            xf_ref[part, a, 0] = fields_ref[part, a, 1, :, 0, :]


def rotated(coeffs_ref, old, b):
    new = None
    for a, value in enumerate(old):
        term = cmul((coeffs_ref[0, a, b], coeffs_ref[1, a, b]), value)
        new = term if new is None else add(new, term)
    return new


SUB = 8
SHX, SEX, SHY, SEY = range(0, 8, 2)


def field_of(ref, b, comp, z, cut):
    return tuple(ref[part, b, comp, z, cut] for part in range(2))


def tiles_of(nx):
    return [slice(SUB * t, SUB * (t + 1)) for t in range(nx // SUB)]


def prepare_kernel(
    pml_ref, eps_real_ref, eps_loss_ref, coeffs_ref, fields_ref, material_ref,
    basis_ref, eps_ref, h_ref, packed_ref, table_ref, sz_ref,
):
    _, vectors, _, nz, nx, ny = fields_ref.shape
    plane = (nx, ny)
    parts = range(2)
    for slot, direction, half, count, dim in (
        (SHX, 1, 0.5, nx, 0), (SEX, 1, 0.0, nx, 0), (SHY, 2, 0.5, ny, 1), (SEY, 2, 0.0, ny, 1),
    ):
        values = axis_stretch(pml_ref, direction, count, local_places(direction, count, plane, dim) + half)
        for part in parts:
            table_ref[slot + part] = values[part]
    for slot, half in ((0, 0.0), (2, 0.5)):
        values = axis_stretch(pml_ref, 0, nz, local_places(0, nz, (nz, ny), 0) + half)
        for part in parts:
            sz_ref[slot + part] = values[part]

    @pl.loop(0, nz)
    def _(z):
        material = material_ref[z]
        for part, source in enumerate((eps_real_ref, eps_loss_ref)):
            value = jnp.zeros(plane, jnp.float32)
            for number in range(source.shape[0]):
                value = jnp.where(material == number, -OMEGA_SQ * source[number], value)
            eps_ref[part, z] = value
        for comp in range(3):
            real = [fields_ref[0, a, comp, z] for a in range(vectors)]
            imag = [fields_ref[1, a, comp, z] for a in range(vectors)]
            both = [first + second for first, second in zip(real, imag)]
            for b in range(vectors):
                turns = [(coeffs_ref[0, a, b], coeffs_ref[1, a, b]) for a in range(vectors)]
                shared = tree_sum([turn[0] * value for turn, value in zip(turns, both)])
                less = tree_sum([(turn[0] + turn[1]) * value for turn, value in zip(turns, imag)])
                more = tree_sum([(turn[1] - turn[0]) * value for turn, value in zip(turns, real)])
                basis_ref[0, b, comp, z] = shared - less
                basis_ref[1, b, comp, z] = shared + more
        packed_ref[z] = jnp.zeros(plane, jnp.float32)

    tile = (SUB, ny)
    rows = lax.broadcasted_iota(jnp.int32, tile, 0)
    lanes = lax.broadcasted_iota(jnp.int32, tile, 1)
    cuts = tiles_of(nx)

    def magnetic(b, z, last):
        shz = tuple(sz_ref[2 + part, pl.ds(z, 1)] for part in parts)
        for cut in cuts:
            u = [field_of(basis_ref, b, comp, z, cut) for comp in range(3)]

            def step_z(comp):
                if last:
                    return tuple(-value for value in u[comp])
                return sub(field_of(basis_ref, b, comp, z + 1, cut), u[comp])

            def step_x(comp):
                if cut.stop < nx:
                    ahead = field_of(basis_ref, b, comp, z, slice(cut.start + 1, cut.stop + 1))
                else:
                    ahead = tuple(jnp.where(rows == SUB - 1, 0.0, pltpu.roll(value, SUB - 1, 0)) for value in u[comp])
                return sub(ahead, u[comp])

            def step_y(comp):
                ahead = tuple(jnp.where(lanes == ny - 1, 0.0, pltpu.roll(value, ny - 1, 1)) for value in u[comp])
                return sub(ahead, u[comp])

            shx = tuple(table_ref[SHX + part, cut] for part in parts)
            shy = tuple(table_ref[SHY + part, cut] for part in parts)
            h = (
                sub(cmul(shy, step_y(2)), cmul(shz, step_z(1))),
                sub(cmul(shz, step_z(0)), cmul(shx, step_x(2))),
                sub(cmul(shx, step_x(1)), cmul(shy, step_y(0))),
            )
            for comp in range(3):
                for part in parts:
                    h_ref[part, b, comp, z, cut] = h[comp][part]
            packed = packed_ref[z, cut]
            for slot, value in enumerate((h[2], h[0])):
                for part in parts:
                    row = packed_row(slot, part, b, vectors)
                    packed = jnp.where(lanes == row, pltpu.roll(value[part], (row + 1) % ny, 1), packed)
            packed_ref[z, cut] = packed

    @pl.loop(0, nz - 1)
    def _(z):
        for b in range(vectors):
            magnetic(b, z, False)

    for b in range(vectors):
        magnetic(b, nz - 1, True)


def turn_face(coeffs_ref, direction, raw_ref, face_ref):
    inside = has_neighbour(direction, 1)
    vectors = raw_ref.shape[1]
    for slot in range(2):
        old = [(raw_ref[0, a, slot] * inside, raw_ref[1, a, slot] * inside) for a in range(vectors)]
        for b in range(vectors):
            new = rotated(coeffs_ref, old, b)
            for part in range(2):
                face_ref[part, b, slot] = new[part]


def turn_column(coeffs_ref, raw_ref, rows_ref):
    vectors = coeffs_ref.shape[1]
    inside = has_neighbour(2, 1)
    both = 2 * vectors
    shape = (both, raw_ref.shape[1])
    which = lax.broadcasted_iota(jnp.int32, shape, 0)
    turned = [jnp.zeros(shape, jnp.float32)] * 2
    for part in range(2):
        for a in range(vectors):
            column = jnp.zeros(shape, jnp.float32)
            for b in range(vectors):
                first, second = coeffs_ref[0, a, b] * inside, coeffs_ref[1, a, b] * inside
                if part:
                    first, second = -second, first
                column = jnp.where(which == b, first, column)
                column = jnp.where(which == vectors + b, second, column)
            for slot in range(2):
                row = packed_row(slot, part, a, vectors)
                turned[slot] = turned[slot] + column * raw_ref[row:row + 1]
    for slot in range(2):
        rows_ref[slot * both:(slot + 1) * both] = turned[slot]


def lane_to_last(values, slot, part, b, vectors):
    ny = values.shape[-1]
    lanes = lax.broadcasted_iota(jnp.int32, values.shape, 1)
    row = packed_row(slot, part, b, vectors)
    return jnp.where(lanes == ny - 1, pltpu.roll(values, ny - 1 - row, 1), 0.0)


def with_halos(h, b, z, cut, nx, xadd_ref, yadd_ref):
    vectors = xadd_ref.shape[1]
    column = yadd_ref[z, cut]
    hx = tuple(h[0][part] + lane_to_last(column, 1, part, b, vectors) for part in range(2))
    hz = tuple(h[2][part] + lane_to_last(column, 0, part, b, vectors) for part in range(2))
    hy = h[1]
    if cut.stop == nx:
        rows = lax.broadcasted_iota(jnp.int32, column.shape, 0)

        def row_of(slot):
            return tuple(
                jnp.where(rows == SUB - 1, xadd_ref[part, b, slot, pl.ds(z, 1)], 0.0) for part in range(2)
            )

        hy, hz = add(hy, row_of(0)), add(hz, row_of(1))
    return hx, hy, hz


def slab_kernel(
    pml_ref, coeffs_ref, basis_ref, h_in, raw_xf_ref, raw_yf_ref,
    h_ref, xf_ref, yt_ref, xadd_ref, yadd_ref, zf_ref,
):
    del h_in
    _, vectors, _, nz, nx, ny = basis_ref.shape
    parts = range(2)
    cells = nz * nx
    both = 2 * vectors
    turn_face(coeffs_ref, 1, raw_xf_ref, xf_ref)
    turn_column(coeffs_ref, raw_yf_ref, yt_ref)
    shx = axis_stretch(pml_ref, 1, nx, one_place(1, nx, nx - 1, (1, ny)) + 0.5)
    shy = axis_stretch(pml_ref, 2, ny, one_place(2, ny, ny - 1, (1, cells)) + 0.5)
    for b in range(vectors):
        for slot in range(2):
            value = cmul(shx, tuple(xf_ref[part, b, 1 - slot] for part in parts))
            for part in parts:
                xadd_ref[part, b, slot] = value[part] if slot else -value[part]
    added = []
    for slot in range(2):
        value = cmul(shy, (yt_ref[slot * both:slot * both + vectors], yt_ref[slot * both + vectors:(slot + 1) * both]))
        added += [part if slot else -part for part in value]
    rest = jnp.zeros((ny - 2 * both, cells), jnp.float32)
    yadd_ref[...] = jnp.concatenate(added + [rest], axis=0).T.reshape(nz, nx, ny)
    last = nz - 1
    lower = jnp.full((SUB, ny), lax.axis_index(AXES[0]), jnp.int32) == 0
    for b in range(vectors):
        for cut in tiles_of(nx):
            h = [field_of(h_ref, b, comp, last, cut) for comp in range(3)]
            h = with_halos(h, b, last, cut, nx, xadd_ref, yadd_ref)
            for part in parts:
                for comp in range(3):
                    h_ref[part, b, comp, last, cut] = h[comp][part]
                for comp in range(2):
                    zf_ref[part, b, comp, cut] = jnp.where(lower, h[comp][part], basis_ref[part, b, comp, 0, cut])


def plane_step(
    b, z, before, sums, ritz_ref, basis_ref, eps_ref, table_ref, sz_ref, h_ref, left_ref, halos=None
):
    _, vectors, _, _, nx, ny = basis_ref.shape
    rows = lax.broadcasted_iota(jnp.int32, (SUB, ny), 0)
    lanes = lax.broadcasted_iota(jnp.int32, (SUB, ny), 1)
    parts = range(2)
    cuts = tiles_of(nx)
    sez = tuple(sz_ref[part, pl.ds(z, 1)] for part in parts)
    fields = []
    for cut in cuts:
        h = [field_of(h_ref, b, comp, z, cut) for comp in range(3)]
        if halos is not None:
            h = with_halos(h, b, z, cut, nx, *halos)
            for comp in (1, 2):
                for part in parts:
                    h_ref[part, b, comp, z, cut] = h[comp][part]
        fields.append(h)
    sums = list(sums)
    for t, cut in enumerate(cuts):
        hx, hy, hz = fields[t]

        def back_x(comp):
            here = fields[t][comp]
            if t:
                past = field_of(h_ref, b, comp, z, slice(cut.start - 1, cut.stop - 1))
            else:
                past = tuple(jnp.where(rows == 0, 0.0, pltpu.roll(value, 1, 0)) for value in here)
            return sub(here, past)

        def back_y(value):
            return sub(value, tuple(jnp.where(lanes == 0, 0.0, pltpu.roll(part, 1, 1)) for part in value))

        sex = tuple(table_ref[SEX + part, cut] for part in parts)
        sey = tuple(table_ref[SEY + part, cut] for part in parts)
        bxy, bxz = (cmul(sex, back_x(comp)) for comp in (1, 2))
        byz, byx = (cmul(sey, back_y(value)) for value in (hz, hx))
        bzx, bzy = (cmul(sez, sub(value, past)) for value, past in zip((hx, hy), before[t]))
        curl = (sub(byz, bzy), sub(bzx, bxz), sub(bxy, byx))
        u = [field_of(basis_ref, b, comp, z, cut) for comp in range(3)]
        eps = tuple(eps_ref[part, z, cut] for part in parts)
        w = [add(curl[comp], cmul(eps, u[comp])) for comp in range(3)]
        for comp in range(3):
            left = sub(w[comp], cmul((ritz_ref[0, b], ritz_ref[1, b]), u[comp]))
            for part in parts:
                left_ref[part, b, comp, z, cut] = left[part]
        for a in range(vectors):
            total = sums[a]
            for comp in range(3):
                total = add(total, cmul(field_of(basis_ref, a, comp, z, cut), w[comp]))
            sums[a] = total
    return [(h[0], h[1]) for h in fields], sums


def inner_kernel(
    ritz_ref, basis_ref, eps_ref, table_ref, sz_ref, h_in, packed_in, xadd_ref, yadd_ref,
    h_ref, packed_ref, left_ref, acc_ref, before_ref, hxf_ref, basis_hbm, sem,
):
    del h_in, packed_in
    _, vectors, _, nz, nx, ny = basis_ref.shape
    keep = pltpu.make_async_copy(basis_ref, basis_hbm, sem)
    keep.start()
    cuts = tiles_of(nx)
    lanes = lax.broadcasted_iota(jnp.int32, (nz, ny), 1)
    open_plane = lax.broadcasted_iota(jnp.int32, (nz, ny), 0) < nz - 1
    packed_ref[...] = packed_ref[...] + yadd_ref[...]
    corner = packed_ref[:, nx - 1, :]
    for b in range(vectors):
        for part in range(2):
            row = packed_row(0, part, b, vectors)
            more = xadd_ref[part, b, 1]
            corner = corner + jnp.where(lanes == row, pltpu.roll(more, (row + 1) % ny, 1), 0.0)
            more = more + lane_to_last(yadd_ref[:, nx - 1, :], 0, part, b, vectors)
            hxf_ref[part, b, 0] = h_ref[part, b, 1, :, nx - 1, :] + jnp.where(open_plane, xadd_ref[part, b, 0], 0.0)
            hxf_ref[part, b, 1] = h_ref[part, b, 2, :, nx - 1, :] + jnp.where(open_plane, more, 0.0)
    packed_ref[:, nx - 1, :] = corner
    acc_ref[...] = jnp.zeros(acc_ref.shape, jnp.float32)
    before_ref[...] = jnp.zeros(before_ref.shape, jnp.float32)

    @pl.loop(0, nz - 1)
    def _(z):
        for b in range(vectors):
            before = [
                tuple(tuple(before_ref[part, b, slot, cut] for part in range(2)) for slot in range(2)) for cut in cuts
            ]
            sums = [(acc_ref[b, a], acc_ref[b, vectors + a]) for a in range(vectors)]
            before, sums = plane_step(
                b, z, before, sums, ritz_ref, basis_ref, eps_ref, table_ref, sz_ref, h_ref, left_ref, (xadd_ref, yadd_ref)
            )
            for part in range(2):
                for a in range(vectors):
                    acc_ref[b, part * vectors + a] = sums[a][part]
                for t, cut in enumerate(cuts):
                    for slot in range(2):
                        before_ref[part, b, slot, cut] = before[t][slot][part]

    keep.wait()


def close_last_plane(sz_ref, zf_ref, packed_in, h_ref, hxf_ref, hyf_ref):
    _, vectors, _, nz, nx, ny = h_ref.shape
    parts = range(2)
    last = nz - 1
    lanes = lax.broadcasted_iota(jnp.int32, (SUB, ny), 1)
    shz = tuple(sz_ref[2 + part, last:] * has_neighbour(0, 1) for part in parts)
    packed = [packed_in[last, cut] for cut in tiles_of(nx)]
    for b in range(vectors):
        for t, cut in enumerate(tiles_of(nx)):
            ex, ey = (tuple(zf_ref[part, b, slot, cut] for part in parts) for slot in range(2))
            more = (tuple(-value for value in cmul(shz, ey)), cmul(shz, ex))
            for part in parts:
                for comp in range(2):
                    h_ref[part, b, comp, last, cut] = h_ref[part, b, comp, last, cut] + more[comp][part]
                row = packed_row(1, part, b, vectors)
                edge = pltpu.roll(more[0][part], (row + 1) % ny, 1)
                packed[t] = packed[t] + jnp.where(lanes == row, edge, 0.0)
                if cut.stop == nx:
                    hxf_ref[part, b, 0, last:] = hxf_ref[part, b, 0, last:] + more[1][part][SUB - 1:]
    inner = packed_in[:last].reshape(last * nx, ny)
    hyf_ref[...] = jnp.concatenate([inner] + packed, axis=0).T[:hyf_ref.shape[0]]


def outer_kernel(
    pml_ref, ritz_ref, basis_ref, eps_ref, table_ref, sz_ref, h_in, zf_ref, xf_ref, yt_ref, hxf_in, packed_in,
    left_in, acc_ref, before_ref, left_ref, gram_ref, h_ref, hxf_ref, hyf_ref,
):
    del left_in, h_in, hxf_in
    close_last_plane(sz_ref, zf_ref, packed_in, h_ref, hxf_ref, hyf_ref)
    _, vectors, _, nz, nx, ny = basis_ref.shape
    parts = range(2)
    cuts = tiles_of(nx)
    under = axis_stretch(pml_ref, 0, nz, one_place(0, nz, -1, (1, ny)) + 0.5)
    sez = tuple(sz_ref[part, 0:1] * has_neighbour(0, -1) for part in parts)
    sx_next = axis_stretch(pml_ref, 1, nx, one_place(1, nx, nx, (1, ny)))
    sy_next = axis_stretch(pml_ref, 2, ny, one_place(2, ny, ny, (1, nz * nx)))
    both = 2 * vectors
    ends = [
        cmul(sy_next, (yt_ref[slot * both:slot * both + vectors], yt_ref[slot * both + vectors:(slot + 1) * both]))
        for slot in range(2)
    ]
    columns = lax.broadcasted_iota(jnp.int32, (both, ny), 1)
    gram = jnp.zeros((both, ny), jnp.float32)
    for b in range(vectors):

        def tile_of(ref, slot, cut, b=b):
            return tuple(ref[part, b, slot, cut] for part in parts)

        before = [tuple(tile_of(before_ref, slot, cut) for slot in range(2)) for cut in cuts]
        sums = [(acc_ref[b, a], acc_ref[b, vectors + a]) for a in range(vectors)]
        _, sums = plane_step(
            b, nz - 1, before, sums, ritz_ref, basis_ref, eps_ref, table_ref, sz_ref, h_ref, left_ref
        )
        for cut in cuts:
            ex, ey = (field_of(basis_ref, b, comp, 0, cut) for comp in range(2))
            hx = sub(tile_of(zf_ref, 0, cut), cmul(under, ey))
            hy = add(tile_of(zf_ref, 1, cut), cmul(under, ex))
            more = (cmul(sez, hy), cmul(sez, hx))
            for part in parts:
                left_ref[part, b, 0, 0, cut] = left_ref[part, b, 0, 0, cut] + more[0][part]
                left_ref[part, b, 1, 0, cut] = left_ref[part, b, 1, 0, cut] - more[1][part]
            for a in range(vectors):
                ex, ey = (field_of(basis_ref, a, comp, 0, cut) for comp in range(2))
                sums[a] = add(sums[a], sub(cmul(ex, more[0]), cmul(ey, more[1])))
        h_y = tuple(hxf_ref[part, b, 0] for part in parts)
        h_z = tuple(hxf_ref[part, b, 1] for part in parts)
        for a in range(vectors):
            over = cmul(tuple(xf_ref[part, a, 0] for part in parts), h_z)
            over = sub(over, cmul(tuple(xf_ref[part, a, 1] for part in parts), h_y))
            over = cmul(sx_next, over)
            for row in range(0, nz, SUB):
                sums[a] = add(sums[a], tuple(part[row:row + SUB] for part in over))
        flat = jnp.concatenate(
            [jnp.sum(sums[a][part], axis=0, keepdims=True) for part in parts for a in range(vectors)], axis=0
        )
        over = None
        for slot in range(2):
            h = tuple(hyf_ref[packed_row(slot, part, b, vectors)][None] for part in parts)
            term = cmul(ends[slot], h)
            over = term if over is None else sub(term, over)
        side = jnp.concatenate(over, axis=0)
        total = jnp.sum(flat, axis=1, keepdims=True) + jnp.sum(side, axis=1, keepdims=True)
        gram = jnp.where(columns == b, total, gram)
    everywhere = 3.0 * nz * nx * ny
    for axis in AXES:
        everywhere = everywhere * lax.axis_size(axis)
    gram = gram * (1.0 / everywhere)
    row = tree_sum([gram[0:1]] + [pltpu.roll(gram[row:row + 1], row * vectors, 1) for row in range(1, both)])
    block = jnp.concatenate([row, jnp.zeros((gram_ref.shape[1] - 1, ny), jnp.float32)], axis=0)
    for device in range(gram_ref.shape[0]):
        gram_ref[device] = block


def gather_kernel(rows_ref, gram_ref):
    vectors = gram_ref.shape[1]
    total = tree_sum([rows_ref[device] for device in range(rows_ref.shape[0])])[0:1]
    count = total.shape[1]
    for part in range(2):
        for a in range(vectors):
            row = (part * vectors + a) * vectors
            turned = pltpu.roll(total, count - row, 1) if row else total
            gram_ref[part, a:a + 1] = turned[:, :vectors]


def rim_kernel(pml_ref, left_in, hxf_ref, hyf_ref, left_ref, residual_hbm, xadd_ref, yadd_ref, sems):
    del left_in
    _, vectors, _, nz, nx, ny = left_ref.shape
    parts = range(2)
    both = 2 * vectors
    sex = axis_stretch(pml_ref, 1, nx, one_place(1, nx, 0, (nz, ny)))
    sex = tuple(part * has_neighbour(1, -1) for part in sex)
    sey = axis_stretch(pml_ref, 2, ny, one_place(2, ny, 0, (vectors, nz * nx)))
    sey = tuple(part * has_neighbour(2, -1) for part in sey)
    for b in range(vectors):
        for slot in range(2):
            value = cmul(sex, tuple(hxf_ref[part, b, slot] for part in parts))
            for part in parts:
                xadd_ref[part, b, slot] = value[part] if slot else -value[part]
    added = []
    for slot in range(2):
        first = slot * both
        value = cmul(sey, (hyf_ref[first:first + vectors], hyf_ref[first + vectors:first + both]))
        added += [part if slot else -part for part in value]
    rest = jnp.zeros((ny - 2 * both, nz * nx), jnp.float32)
    yadd_ref[...] = jnp.concatenate(added + [rest], axis=0).T.reshape(nz, nx, ny)
    rows = lax.broadcasted_iota(jnp.int32, (SUB, ny), 0)
    lanes = lax.broadcasted_iota(jnp.int32, (SUB, ny), 1)

    def kept(z):
        return pltpu.make_async_copy(left_ref.at[:, :, :, z], residual_hbm.at[:, :, :, z], sems.at[z])

    @pl.loop(0, nz)
    def _(z):
        for cut in tiles_of(nx):
            column = yadd_ref[z, cut]
            for b in range(vectors):
                for part in parts:

                    def turned(slot, b=b, part=part):
                        row = packed_row(slot, part, b, vectors)
                        value = pltpu.roll(column, ny - row, 1) if row else column
                        return jnp.where(lanes == 0, value, 0.0)

                    def row_of(slot, b=b, part=part):
                        return jnp.where(rows == 0, xadd_ref[part, b, slot, pl.ds(z, 1)], 0.0)

                    ex = left_ref[part, b, 0, z, cut] + turned(0)
                    ez = left_ref[part, b, 2, z, cut] + turned(1)
                    if cut.start == 0:
                        left_ref[part, b, 1, z, cut] = left_ref[part, b, 1, z, cut] + row_of(1)
                        ez = ez + row_of(0)
                    left_ref[part, b, 0, z, cut] = ex
                    left_ref[part, b, 2, z, cut] = ez
        kept(z).start()

    @pl.loop(0, nz)
    def _(z):
        kept(z).wait()


def body(fields, material, pml_width, eps_real, eps_loss, coeffs, ritz):
    _, vectors, _, nz, nx, ny = fields.shape
    f32 = lambda *shape: jax.ShapeDtypeStruct(shape, jnp.float32)
    scratch = lambda *shape: pltpu.VMEM(shape, jnp.float32)
    params = pltpu.CompilerParams(vmem_limit_bytes=40 * 1024 * 1024)
    whole = f32(*fields.shape)
    zf_shape = (2, vectors, 2, nx, ny)
    xf_shape = (2, vectors, 2, nz, ny)
    yf_shape = (4 * vectors, nz * nx)
    near, xf, yf = pl.pallas_call(
        face_kernel,
        out_shape=(whole, f32(*xf_shape), f32(*yf_shape)),
        in_specs=[HBM],
        out_specs=(VMEM,) * 3,
        scratch_shapes=[pltpu.SemaphoreType.DMA((2, 3))],
        compiler_params=params,
        name="take_faces",
    )(pltpu.with_memory_space_constraint(fields, pltpu.HBM))
    xf = passed_along(xf, "gx", -1)
    yf = passed_round(yf, "gy", -1)
    cells = fields.size // 6 // vectors

    def cost(flops, passes):
        return pl.CostEstimate(flops=flops * cells, bytes_accessed=passes * 4 * fields.size, transcendentals=0)

    planes = f32(nz, nx, ny)
    face = f32(*xf_shape)
    basis, eps, h, packed, table, sz = pl.pallas_call(
        prepare_kernel,
        out_shape=(whole, f32(2, nz, nx, ny), whole, planes, f32(8, nx, ny), f32(4, nz, ny)),
        in_specs=[SMEM] * 4 + [VMEM] * 2,
        out_specs=(VMEM,) * 6,
        compiler_params=params,
        cost_estimate=cost(800, 4),
        name="prepare",
    )(pml_width, eps_real, eps_loss, coeffs, near, material)
    h, xf, yt, xadd, yadd, zf = pl.pallas_call(
        slab_kernel,
        out_shape=(whole, face, f32(*yf_shape), face, planes, f32(*zf_shape)),
        in_specs=[SMEM] * 2 + [VMEM] * 4,
        out_specs=(VMEM,) * 6,
        input_output_aliases={3: 0},
        compiler_params=params,
        name="slab_face",
    )(pml_width, coeffs, basis, h, xf, yf)
    zf = passed_round(zf, "gz", 1)
    h, packed, left, acc, before, hxf, basis_new = pl.pallas_call(
        inner_kernel,
        out_shape=(whole, planes, whole, f32(vectors, 2 * vectors, SUB, ny), f32(*zf_shape), face, whole),
        in_specs=[SMEM] + [VMEM] * 8,
        out_specs=(VMEM,) * 6 + (HBM,),
        scratch_shapes=[pltpu.SemaphoreType.DMA],
        input_output_aliases={5: 0, 6: 1},
        compiler_params=params,
        cost_estimate=cost(800, 2),
        name="apply_inner",
    )(ritz, basis, eps, table, sz, h, packed, xadd, yadd)
    devices = lax.axis_size("gx") * lax.axis_size("gy") * lax.axis_size("gz")
    left, gram, _, hxf, hyf = pl.pallas_call(
        outer_kernel,
        out_shape=(whole, f32(devices, 4, ny), whole, face, f32(*yf_shape)),
        in_specs=[SMEM] * 2 + [VMEM] * 13,
        out_specs=(VMEM,) * 5,
        input_output_aliases={12: 0, 6: 2, 10: 3},
        compiler_params=params,
        cost_estimate=cost(300, 1),
        name="apply_outer",
    )(pml_width, ritz, basis, eps, table, sz, h, zf, xf, yt, hxf, packed, left, acc, before)
    gram, hxf, hyf = lax.optimization_barrier((gram, hxf, hyf))
    rows = lax.all_to_all(gram, ("gx", "gy", "gz"), 0, 0)
    from_x = passed_along(hxf, "gx", 1)
    from_y = passed_round(hyf, "gy", 1)
    _, residual = pl.pallas_call(
        rim_kernel,
        out_shape=(whole, whole),
        in_specs=[SMEM] + [VMEM] * 3,
        out_specs=(VMEM, HBM),
        scratch_shapes=[scratch(*xf_shape), scratch(nz, nx, ny), pltpu.SemaphoreType.DMA((nz,))],
        input_output_aliases={1: 0},
        compiler_params=params,
        cost_estimate=pl.CostEstimate(flops=0, bytes_accessed=0, transcendentals=0),
        name="add_rims",
    )(pml_width, left, from_x, from_y)
    rows, residual = lax.optimization_barrier((rows, residual))
    gram = pl.pallas_call(
        gather_kernel,
        out_shape=f32(2, vectors, vectors),
        in_specs=[VMEM],
        out_specs=VMEM,
        compiler_params=params,
        name="sum_rows",
    )(rows)
    return basis_new, residual, gram


def solution(mesh):
    in_specs = (P(None, None, None, "gz", "gx", "gy"), P("gz", "gx", "gy"), P(), P(), P(), P(), P())
    out_specs = (P(None, None, None, "gz", "gx", "gy"), P(None, None, None, "gz", "gx", "gy"), P())
    return jax.shard_map(body, mesh=mesh, in_specs=in_specs, out_specs=out_specs, check_vma=False)
```

```python
import functools

import jax
import jax.numpy as jnp
from jax import lax
from jax.experimental import pallas as pl
from jax.experimental.pallas import tpu as pltpu
from jax.sharding import PartitionSpec as P

OMEGA_SQ = 0.36
SIGMA_TOP = 3.0
BOUNDS = ((4, 5), (0, 1), (2, 3))
AXES = ("gz", "gx", "gy")

VMEM = pl.BlockSpec(memory_space=pltpu.VMEM)
SMEM = pl.BlockSpec(memory_space=pltpu.SMEM)
HBM = pl.BlockSpec(memory_space=pltpu.HBM)


def passed_round(value, axis, steps):
    count = lax.axis_size(axis)
    return lax.ppermute(value, axis, [(source, (source + steps) % count) for source in range(count)])


def passed_over(value, axis, across, steps):
    count, rows = lax.axis_size(axis), lax.axis_size(across)
    pairs = []
    for place in range(count):
        for row in range(rows):
            turns, target = divmod(place + steps, count)
            pairs.append((place * rows + row, target * rows + (row + turns) % rows))
    return lax.ppermute(value, (axis, across), pairs)


def passed_along(value, axis, steps):
    count = lax.axis_size(axis)
    leading, last = (max(0, -steps), min(count, count - steps))
    return lax.ppermute(value, axis, [(source, source + steps) for source in range(leading, last)])


def inverse_stretch(places, length, low_width, high_width):
    inside_depth = jnp.clip((low_width - places) / low_width, 0.0, 1.0) + jnp.clip(
        (places + 1.0 - length + high_width) / high_width, 0.0, 1.0
    )
    absorb = SIGMA_TOP * inside_depth * inside_depth
    scaled = 1.0 / (1.0 + absorb * absorb)
    return scaled, -absorb * scaled


def tree_sum(values):
    while len(values) > 1:
        pairs = [values[place] + values[place + 1] for place in range(0, len(values) - 1, 2)]
        values = pairs + ([values[-1]] if len(values) % 2 else [])
    return values[0]


def cmul(left, right):
    return (left[0] * right[0] - left[1] * right[1], left[0] * right[1] + left[1] * right[0])


def add(left, right):
    return (left[0] + right[0], left[1] + right[1])


def sub(left, right):
    return (left[0] - right[0], left[1] - right[1])


def axis_stretch(pml_ref, direction, count, places):
    total = count * lax.axis_size(AXES[direction])
    low_slot, high_slot = BOUNDS[direction]
    low = jnp.full(places.shape, pml_ref[low_slot], jnp.int32).astype(jnp.float32)
    high = jnp.full(places.shape, pml_ref[high_slot], jnp.int32).astype(jnp.float32)
    return inverse_stretch(places, jnp.float32(total), low, high)


def local_places(direction, count, shape, dim):
    start = lax.axis_index(AXES[direction]) * count
    return (lax.broadcasted_iota(jnp.int32, shape, dim) + start).astype(jnp.float32)


def one_place(direction, count, offset, shape):
    start = lax.axis_index(AXES[direction]) * count + offset
    return jnp.full(shape, start, jnp.int32).astype(jnp.float32)


def packed_row(slot, part, vector, vectors):
    return (slot * 2 + part) * vectors + vector


def has_neighbour(direction, steps):
    place = lax.axis_index(AXES[direction]) + steps
    inside = (place >= 0) & (place < lax.axis_size(AXES[direction]))
    return jnp.where(inside, 1.0, 0.0).astype(jnp.float32)


def face_kernel(fields_hbm, fields_ref, xf_ref, yf_ref, sems):
    _, vectors, _, nz, nx, ny = fields_ref.shape
    lanes = lax.broadcasted_iota(jnp.int32, (nx, ny), 1)
    copies = [
        pltpu.make_async_copy(fields_hbm.at[part, :, comp], fields_ref.at[part, :, comp], sems.at[part, comp])
        for comp in (0, 2, 1) for part in range(2)
    ]
    for copy in copies:
        copy.start()
    packed = [jnp.zeros((nx, ny), jnp.float32)] * nz
    for place, comp in enumerate((0, 2)):
        for part in range(2):
            copies[2 * place + part].wait()
            for a in range(vectors):
                row = packed_row(comp // 2, part, a, vectors)
                for z in range(nz):
                    value = fields_ref[part, a, comp, z]
                    packed[z] = jnp.where(lanes == row, pltpu.roll(value, row, 1) if row else value, packed[z])
    turned = jnp.concatenate(packed, axis=0).T
    yf_ref[...] = turned[:yf_ref.shape[0]]
    for part in range(2):
        for a in range(vectors):
            xf_ref[part, a, 1] = fields_ref[part, a, 2, :, 0, :]
    for part in range(2):
        copies[4 + part].wait()
        for a in range(vectors):
            xf_ref[part, a, 0] = fields_ref[part, a, 1, :, 0, :]


def rotated(coeffs_ref, old, b):
    new = None
    for a, value in enumerate(old):
        term = cmul((coeffs_ref[0, a, b], coeffs_ref[1, a, b]), value)
        new = term if new is None else add(new, term)
    return new


SUB = 8
SHX, SEX, SHY, SEY = range(0, 8, 2)


def field_of(ref, b, comp, z, cut):
    return tuple(ref[part, b, comp, z, cut] for part in range(2))


def tiles_of(nx):
    return [slice(SUB * t, SUB * (t + 1)) for t in range(nx // SUB)]


def prepare_kernel(
    pml_ref, eps_real_ref, eps_loss_ref, coeffs_ref, fields_ref, material_ref,
    basis_ref, eps_ref, h_ref, packed_ref, table_ref, sz_ref,
):
    _, vectors, _, nz, nx, ny = fields_ref.shape
    plane = (nx, ny)
    parts = range(2)
    for slot, direction, half, count, dim in (
        (SHX, 1, 0.5, nx, 0), (SEX, 1, 0.0, nx, 0), (SHY, 2, 0.5, ny, 1), (SEY, 2, 0.0, ny, 1),
    ):
        values = axis_stretch(pml_ref, direction, count, local_places(direction, count, plane, dim) + half)
        for part in parts:
            table_ref[slot + part] = values[part]
    for slot, half in ((0, 0.0), (2, 0.5)):
        values = axis_stretch(pml_ref, 0, nz, local_places(0, nz, (nz, ny), 0) + half)
        for part in parts:
            sz_ref[slot + part] = values[part]

    @pl.loop(0, nz)
    def _(z):
        material = material_ref[z]
        for part, source in enumerate((eps_real_ref, eps_loss_ref)):
            value = jnp.zeros(plane, jnp.float32)
            for number in range(source.shape[0]):
                value = jnp.where(material == number, -OMEGA_SQ * source[number], value)
            eps_ref[part, z] = value
        for comp in range(3):
            real = [fields_ref[0, a, comp, z] for a in range(vectors)]
            imag = [fields_ref[1, a, comp, z] for a in range(vectors)]
            both = [first + second for first, second in zip(real, imag)]
            for b in range(vectors):
                turns = [(coeffs_ref[0, a, b], coeffs_ref[1, a, b]) for a in range(vectors)]
                shared = tree_sum([turn[0] * value for turn, value in zip(turns, both)])
                less = tree_sum([(turn[0] + turn[1]) * value for turn, value in zip(turns, imag)])
                more = tree_sum([(turn[1] - turn[0]) * value for turn, value in zip(turns, real)])
                basis_ref[0, b, comp, z] = shared - less
                basis_ref[1, b, comp, z] = shared + more
        packed_ref[z] = jnp.zeros(plane, jnp.float32)

    tile = (SUB, ny)
    rows = lax.broadcasted_iota(jnp.int32, tile, 0)
    lanes = lax.broadcasted_iota(jnp.int32, tile, 1)
    cuts = tiles_of(nx)

    def magnetic(b, z, last):
        shz = tuple(sz_ref[2 + part, pl.ds(z, 1)] for part in parts)
        for cut in cuts:
            u = [field_of(basis_ref, b, comp, z, cut) for comp in range(3)]

            def step_z(comp):
                if last:
                    return tuple(-value for value in u[comp])
                return sub(field_of(basis_ref, b, comp, z + 1, cut), u[comp])

            def step_x(comp):
                if cut.stop < nx:
                    ahead = field_of(basis_ref, b, comp, z, slice(cut.start + 1, cut.stop + 1))
                else:
                    ahead = tuple(jnp.where(rows == SUB - 1, 0.0, pltpu.roll(value, SUB - 1, 0)) for value in u[comp])
                return sub(ahead, u[comp])

            def step_y(comp):
                ahead = tuple(jnp.where(lanes == ny - 1, 0.0, pltpu.roll(value, ny - 1, 1)) for value in u[comp])
                return sub(ahead, u[comp])

            shx = tuple(table_ref[SHX + part, cut] for part in parts)
            shy = tuple(table_ref[SHY + part, cut] for part in parts)
            h = (
                sub(cmul(shy, step_y(2)), cmul(shz, step_z(1))),
                sub(cmul(shz, step_z(0)), cmul(shx, step_x(2))),
                sub(cmul(shx, step_x(1)), cmul(shy, step_y(0))),
            )
            for comp in range(3):
                for part in parts:
                    h_ref[part, b, comp, z, cut] = h[comp][part]
            packed = packed_ref[z, cut]
            for slot, value in enumerate((h[2], h[0])):
                for part in parts:
                    row = packed_row(slot, part, b, vectors)
                    packed = jnp.where(lanes == row, pltpu.roll(value[part], (row + 1) % ny, 1), packed)
            packed_ref[z, cut] = packed

    @pl.loop(0, nz - 1)
    def _(z):
        for b in range(vectors):
            magnetic(b, z, False)

    for b in range(vectors):
        magnetic(b, nz - 1, True)


def turn_face(coeffs_ref, direction, raw_ref, face_ref):
    inside = has_neighbour(direction, 1)
    vectors = raw_ref.shape[1]
    for slot in range(2):
        old = [(raw_ref[0, a, slot] * inside, raw_ref[1, a, slot] * inside) for a in range(vectors)]
        for b in range(vectors):
            new = rotated(coeffs_ref, old, b)
            for part in range(2):
                face_ref[part, b, slot] = new[part]


def turn_column(coeffs_ref, raw_ref, rows_ref):
    vectors = coeffs_ref.shape[1]
    inside = has_neighbour(2, 1)
    both = 2 * vectors
    shape = (both, raw_ref.shape[1])
    which = lax.broadcasted_iota(jnp.int32, shape, 0)
    turned = [jnp.zeros(shape, jnp.float32)] * 2
    for part in range(2):
        for a in range(vectors):
            column = jnp.zeros(shape, jnp.float32)
            for b in range(vectors):
                first, second = coeffs_ref[0, a, b] * inside, coeffs_ref[1, a, b] * inside
                if part:
                    first, second = -second, first
                column = jnp.where(which == b, first, column)
                column = jnp.where(which == vectors + b, second, column)
            for slot in range(2):
                row = packed_row(slot, part, a, vectors)
                turned[slot] = turned[slot] + column * raw_ref[row:row + 1]
    for slot in range(2):
        rows_ref[slot * both:(slot + 1) * both] = turned[slot]


def lane_to_last(values, slot, part, b, vectors):
    ny = values.shape[-1]
    lanes = lax.broadcasted_iota(jnp.int32, values.shape, 1)
    row = packed_row(slot, part, b, vectors)
    return jnp.where(lanes == ny - 1, pltpu.roll(values, ny - 1 - row, 1), 0.0)


def with_halos(h, b, z, cut, nx, xadd_ref, yadd_ref):
    vectors = xadd_ref.shape[1]
    column = yadd_ref[z, cut]
    hx = tuple(h[0][part] + lane_to_last(column, 1, part, b, vectors) for part in range(2))
    hz = tuple(h[2][part] + lane_to_last(column, 0, part, b, vectors) for part in range(2))
    hy = h[1]
    if cut.stop == nx:
        rows = lax.broadcasted_iota(jnp.int32, column.shape, 0)

        def row_of(slot):
            return tuple(
                jnp.where(rows == SUB - 1, xadd_ref[part, b, slot, pl.ds(z, 1)], 0.0) for part in range(2)
            )

        hy, hz = add(hy, row_of(0)), add(hz, row_of(1))
    return hx, hy, hz


def slab_kernel(
    pml_ref, coeffs_ref, basis_ref, h_in, raw_xf_ref, raw_yf_ref,
    h_ref, xf_ref, yt_ref, xadd_ref, yadd_ref, zf_ref,
):
    del h_in
    _, vectors, _, nz, nx, ny = basis_ref.shape
    parts = range(2)
    cells = nz * nx
    both = 2 * vectors
    turn_face(coeffs_ref, 1, raw_xf_ref, xf_ref)
    turn_column(coeffs_ref, raw_yf_ref, yt_ref)
    shx = axis_stretch(pml_ref, 1, nx, one_place(1, nx, nx - 1, (1, ny)) + 0.5)
    shy = axis_stretch(pml_ref, 2, ny, one_place(2, ny, ny - 1, (1, cells)) + 0.5)
    for b in range(vectors):
        for slot in range(2):
            value = cmul(shx, tuple(xf_ref[part, b, 1 - slot] for part in parts))
            for part in parts:
                xadd_ref[part, b, slot] = value[part] if slot else -value[part]
    added = []
    for slot in range(2):
        value = cmul(shy, (yt_ref[slot * both:slot * both + vectors], yt_ref[slot * both + vectors:(slot + 1) * both]))
        added += [part if slot else -part for part in value]
    rest = jnp.zeros((ny - 2 * both, cells), jnp.float32)
    yadd_ref[...] = jnp.concatenate(added + [rest], axis=0).T.reshape(nz, nx, ny)
    last = nz - 1
    lower = jnp.full((SUB, ny), lax.axis_index(AXES[0]), jnp.int32) == 0
    for b in range(vectors):
        for cut in tiles_of(nx):
            h = [field_of(h_ref, b, comp, last, cut) for comp in range(3)]
            h = with_halos(h, b, last, cut, nx, xadd_ref, yadd_ref)
            for part in parts:
                for comp in range(3):
                    h_ref[part, b, comp, last, cut] = h[comp][part]
                for comp in range(2):
                    zf_ref[part, b, comp, cut] = jnp.where(lower, h[comp][part], basis_ref[part, b, comp, 0, cut])


def plane_step(
    b, z, before, sums, ritz_ref, basis_ref, eps_ref, table_ref, sz_ref, h_ref, left_ref, halos=None
):
    _, vectors, _, _, nx, ny = basis_ref.shape
    rows = lax.broadcasted_iota(jnp.int32, (SUB, ny), 0)
    lanes = lax.broadcasted_iota(jnp.int32, (SUB, ny), 1)
    parts = range(2)
    cuts = tiles_of(nx)
    sez = tuple(sz_ref[part, pl.ds(z, 1)] for part in parts)
    fields = []
    for cut in cuts:
        h = [field_of(h_ref, b, comp, z, cut) for comp in range(3)]
        if halos is not None:
            h = with_halos(h, b, z, cut, nx, *halos)
            for comp in (1, 2):
                for part in parts:
                    h_ref[part, b, comp, z, cut] = h[comp][part]
        fields.append(h)
    sums = list(sums)
    for t, cut in enumerate(cuts):
        hx, hy, hz = fields[t]

        def back_x(comp):
            here = fields[t][comp]
            if t:
                past = field_of(h_ref, b, comp, z, slice(cut.start - 1, cut.stop - 1))
            else:
                past = tuple(jnp.where(rows == 0, 0.0, pltpu.roll(value, 1, 0)) for value in here)
            return sub(here, past)

        def back_y(value):
            return sub(value, tuple(jnp.where(lanes == 0, 0.0, pltpu.roll(part, 1, 1)) for part in value))

        sex = tuple(table_ref[SEX + part, cut] for part in parts)
        sey = tuple(table_ref[SEY + part, cut] for part in parts)
        bxy, bxz = (cmul(sex, back_x(comp)) for comp in (1, 2))
        byz, byx = (cmul(sey, back_y(value)) for value in (hz, hx))
        bzx, bzy = (cmul(sez, sub(value, past)) for value, past in zip((hx, hy), before[t]))
        curl = (sub(byz, bzy), sub(bzx, bxz), sub(bxy, byx))
        u = [field_of(basis_ref, b, comp, z, cut) for comp in range(3)]
        eps = tuple(eps_ref[part, z, cut] for part in parts)
        w = [add(curl[comp], cmul(eps, u[comp])) for comp in range(3)]
        for comp in range(3):
            left = sub(w[comp], cmul((ritz_ref[0, b], ritz_ref[1, b]), u[comp]))
            for part in parts:
                left_ref[part, b, comp, z, cut] = left[part]
        for a in range(vectors):
            total = sums[a]
            for comp in range(3):
                total = add(total, cmul(field_of(basis_ref, a, comp, z, cut), w[comp]))
            sums[a] = total
    return [(h[0], h[1]) for h in fields], sums


def inner_kernel(
    ritz_ref, basis_ref, eps_ref, table_ref, sz_ref, h_in, packed_in, xadd_ref, yadd_ref,
    h_ref, packed_ref, left_ref, acc_ref, before_ref, hxf_ref, basis_hbm, sem,
):
    del h_in, packed_in
    _, vectors, _, nz, nx, ny = basis_ref.shape
    keep = pltpu.make_async_copy(basis_ref, basis_hbm, sem)
    keep.start()
    cuts = tiles_of(nx)
    lanes = lax.broadcasted_iota(jnp.int32, (nz, ny), 1)
    open_plane = lax.broadcasted_iota(jnp.int32, (nz, ny), 0) < nz - 1
    packed_ref[...] = packed_ref[...] + yadd_ref[...]
    corner = packed_ref[:, nx - 1, :]
    for b in range(vectors):
        for part in range(2):
            row = packed_row(0, part, b, vectors)
            more = xadd_ref[part, b, 1]
            corner = corner + jnp.where(lanes == row, pltpu.roll(more, (row + 1) % ny, 1), 0.0)
            more = more + lane_to_last(yadd_ref[:, nx - 1, :], 0, part, b, vectors)
            hxf_ref[part, b, 0] = h_ref[part, b, 1, :, nx - 1, :] + jnp.where(open_plane, xadd_ref[part, b, 0], 0.0)
            hxf_ref[part, b, 1] = h_ref[part, b, 2, :, nx - 1, :] + jnp.where(open_plane, more, 0.0)
    packed_ref[:, nx - 1, :] = corner
    acc_ref[...] = jnp.zeros(acc_ref.shape, jnp.float32)
    before_ref[...] = jnp.zeros(before_ref.shape, jnp.float32)

    @pl.loop(0, nz - 1)
    def _(z):
        for b in range(vectors):
            before = [
                tuple(tuple(before_ref[part, b, slot, cut] for part in range(2)) for slot in range(2)) for cut in cuts
            ]
            sums = [(acc_ref[b, a], acc_ref[b, vectors + a]) for a in range(vectors)]
            before, sums = plane_step(
                b, z, before, sums, ritz_ref, basis_ref, eps_ref, table_ref, sz_ref, h_ref, left_ref, (xadd_ref, yadd_ref)
            )
            for part in range(2):
                for a in range(vectors):
                    acc_ref[b, part * vectors + a] = sums[a][part]
                for t, cut in enumerate(cuts):
                    for slot in range(2):
                        before_ref[part, b, slot, cut] = before[t][slot][part]

    keep.wait()


def close_last_plane(sz_ref, zf_ref, packed_in, h_ref, hxf_ref, hyf_ref):
    _, vectors, _, nz, nx, ny = h_ref.shape
    parts = range(2)
    last = nz - 1
    lanes = lax.broadcasted_iota(jnp.int32, (SUB, ny), 1)
    shz = tuple(sz_ref[2 + part, last:] * has_neighbour(0, 1) for part in parts)
    packed = [packed_in[last, cut] for cut in tiles_of(nx)]
    for b in range(vectors):
        for t, cut in enumerate(tiles_of(nx)):
            ex, ey = (tuple(zf_ref[part, b, slot, cut] for part in parts) for slot in range(2))
            more = (tuple(-value for value in cmul(shz, ey)), cmul(shz, ex))
            for part in parts:
                for comp in range(2):
                    h_ref[part, b, comp, last, cut] = h_ref[part, b, comp, last, cut] + more[comp][part]
                row = packed_row(1, part, b, vectors)
                edge = pltpu.roll(more[0][part], (row + 1) % ny, 1)
                packed[t] = packed[t] + jnp.where(lanes == row, edge, 0.0)
                if cut.stop == nx:
                    hxf_ref[part, b, 0, last:] = hxf_ref[part, b, 0, last:] + more[1][part][SUB - 1:]
    inner = packed_in[:last].reshape(last * nx, ny)
    hyf_ref[...] = jnp.concatenate([inner] + packed, axis=0).T[:hyf_ref.shape[0]]


def outer_kernel(
    pml_ref, ritz_ref, basis_ref, eps_ref, table_ref, sz_ref, h_in, zf_ref, xf_ref, yt_ref, hxf_in, packed_in,
    left_in, acc_ref, before_ref, left_ref, gram_ref, h_ref, hxf_ref, hyf_ref,
):
    del left_in, h_in, hxf_in
    close_last_plane(sz_ref, zf_ref, packed_in, h_ref, hxf_ref, hyf_ref)
    _, vectors, _, nz, nx, ny = basis_ref.shape
    parts = range(2)
    cuts = tiles_of(nx)
    under = axis_stretch(pml_ref, 0, nz, one_place(0, nz, -1, (1, ny)) + 0.5)
    sez = tuple(sz_ref[part, 0:1] * has_neighbour(0, -1) for part in parts)
    sx_next = axis_stretch(pml_ref, 1, nx, one_place(1, nx, nx, (1, ny)))
    sy_next = axis_stretch(pml_ref, 2, ny, one_place(2, ny, ny, (1, nz * nx)))
    both = 2 * vectors
    ends = [
        cmul(sy_next, (yt_ref[slot * both:slot * both + vectors], yt_ref[slot * both + vectors:(slot + 1) * both]))
        for slot in range(2)
    ]
    columns = lax.broadcasted_iota(jnp.int32, (both, ny), 1)
    gram = jnp.zeros((both, ny), jnp.float32)
    for b in range(vectors):

        def tile_of(ref, slot, cut, b=b):
            return tuple(ref[part, b, slot, cut] for part in parts)

        before = [tuple(tile_of(before_ref, slot, cut) for slot in range(2)) for cut in cuts]
        sums = [(acc_ref[b, a], acc_ref[b, vectors + a]) for a in range(vectors)]
        _, sums = plane_step(
            b, nz - 1, before, sums, ritz_ref, basis_ref, eps_ref, table_ref, sz_ref, h_ref, left_ref
        )
        for cut in cuts:
            ex, ey = (field_of(basis_ref, b, comp, 0, cut) for comp in range(2))
            hx = sub(tile_of(zf_ref, 0, cut), cmul(under, ey))
            hy = add(tile_of(zf_ref, 1, cut), cmul(under, ex))
            more = (cmul(sez, hy), cmul(sez, hx))
            for part in parts:
                left_ref[part, b, 0, 0, cut] = left_ref[part, b, 0, 0, cut] + more[0][part]
                left_ref[part, b, 1, 0, cut] = left_ref[part, b, 1, 0, cut] - more[1][part]
            for a in range(vectors):
                ex, ey = (field_of(basis_ref, a, comp, 0, cut) for comp in range(2))
                sums[a] = add(sums[a], sub(cmul(ex, more[0]), cmul(ey, more[1])))
        h_y = tuple(hxf_ref[part, b, 0] for part in parts)
        h_z = tuple(hxf_ref[part, b, 1] for part in parts)
        for a in range(vectors):
            over = cmul(tuple(xf_ref[part, a, 0] for part in parts), h_z)
            over = sub(over, cmul(tuple(xf_ref[part, a, 1] for part in parts), h_y))
            over = cmul(sx_next, over)
            for row in range(0, nz, SUB):
                sums[a] = add(sums[a], tuple(part[row:row + SUB] for part in over))
        flat = jnp.concatenate(
            [jnp.sum(sums[a][part], axis=0, keepdims=True) for part in parts for a in range(vectors)], axis=0
        )
        over = None
        for slot in range(2):
            h = tuple(hyf_ref[packed_row(slot, part, b, vectors)][None] for part in parts)
            term = cmul(ends[slot], h)
            over = term if over is None else sub(term, over)
        side = jnp.concatenate(over, axis=0)
        total = jnp.sum(flat, axis=1, keepdims=True) + jnp.sum(side, axis=1, keepdims=True)
        gram = jnp.where(columns == b, total, gram)
    everywhere = 3.0 * nz * nx * ny
    for axis in AXES:
        everywhere = everywhere * lax.axis_size(axis)
    gram = gram * (1.0 / everywhere)
    row = tree_sum([gram[0:1]] + [pltpu.roll(gram[row:row + 1], row * vectors, 1) for row in range(1, both)])
    block = jnp.concatenate([row, jnp.zeros((gram_ref.shape[1] - 1, ny), jnp.float32)], axis=0)
    for device in range(gram_ref.shape[0]):
        gram_ref[device] = block


def gather_kernel(rows_ref, gram_ref):
    vectors = gram_ref.shape[1]
    total = tree_sum([rows_ref[device] for device in range(rows_ref.shape[0])])[0:1]
    count = total.shape[1]
    for part in range(2):
        for a in range(vectors):
            row = (part * vectors + a) * vectors
            turned = pltpu.roll(total, count - row, 1) if row else total
            gram_ref[part, a:a + 1] = turned[:, :vectors]


def rim_kernel(pml_ref, left_in, hxf_ref, hyf_ref, left_ref, residual_hbm, xadd_ref, yadd_ref, sems):
    del left_in
    _, vectors, _, nz, nx, ny = left_ref.shape
    parts = range(2)
    both = 2 * vectors
    sex = axis_stretch(pml_ref, 1, nx, one_place(1, nx, 0, (nz, ny)))
    sex = tuple(part * has_neighbour(1, -1) for part in sex)
    sey = axis_stretch(pml_ref, 2, ny, one_place(2, ny, 0, (vectors, nz * nx)))
    sey = tuple(part * has_neighbour(2, -1) for part in sey)
    for b in range(vectors):
        for slot in range(2):
            value = cmul(sex, tuple(hxf_ref[part, b, slot] for part in parts))
            for part in parts:
                xadd_ref[part, b, slot] = value[part] if slot else -value[part]
    added = []
    for slot in range(2):
        first = slot * both
        value = cmul(sey, (hyf_ref[first:first + vectors], hyf_ref[first + vectors:first + both]))
        added += [part if slot else -part for part in value]
    rest = jnp.zeros((ny - 2 * both, nz * nx), jnp.float32)
    yadd_ref[...] = jnp.concatenate(added + [rest], axis=0).T.reshape(nz, nx, ny)
    rows = lax.broadcasted_iota(jnp.int32, (SUB, ny), 0)
    lanes = lax.broadcasted_iota(jnp.int32, (SUB, ny), 1)

    def kept(z):
        return pltpu.make_async_copy(left_ref.at[:, :, :, z], residual_hbm.at[:, :, :, z], sems.at[z])

    @pl.loop(0, nz)
    def _(z):
        for cut in tiles_of(nx):
            column = yadd_ref[z, cut]
            for b in range(vectors):
                for part in parts:

                    def turned(slot, b=b, part=part):
                        row = packed_row(slot, part, b, vectors)
                        value = pltpu.roll(column, ny - row, 1) if row else column
                        return jnp.where(lanes == 0, value, 0.0)

                    def row_of(slot, b=b, part=part):
                        return jnp.where(rows == 0, xadd_ref[part, b, slot, pl.ds(z, 1)], 0.0)

                    ex = left_ref[part, b, 0, z, cut] + turned(0)
                    ez = left_ref[part, b, 2, z, cut] + turned(1)
                    if cut.start == 0:
                        left_ref[part, b, 1, z, cut] = left_ref[part, b, 1, z, cut] + row_of(1)
                        ez = ez + row_of(0)
                    left_ref[part, b, 0, z, cut] = ex
                    left_ref[part, b, 2, z, cut] = ez
        kept(z).start()

    @pl.loop(0, nz)
    def _(z):
        kept(z).wait()


def body(fields, material, pml_width, eps_real, eps_loss, coeffs, ritz):
    _, vectors, _, nz, nx, ny = fields.shape
    f32 = lambda *shape: jax.ShapeDtypeStruct(shape, jnp.float32)
    scratch = lambda *shape: pltpu.VMEM(shape, jnp.float32)
    params = pltpu.CompilerParams(vmem_limit_bytes=40 * 1024 * 1024)
    whole = f32(*fields.shape)
    zf_shape = (2, vectors, 2, nx, ny)
    xf_shape = (2, vectors, 2, nz, ny)
    yf_shape = (4 * vectors, nz * nx)
    near, xf, yf = pl.pallas_call(
        face_kernel,
        out_shape=(whole, f32(*xf_shape), f32(*yf_shape)),
        in_specs=[HBM],
        out_specs=(VMEM,) * 3,
        scratch_shapes=[pltpu.SemaphoreType.DMA((2, 3))],
        compiler_params=params,
        name="take_faces",
    )(pltpu.with_memory_space_constraint(fields, pltpu.HBM))
    xf = passed_over(xf, "gx", "gz", -1)
    yf = passed_round(yf, "gy", -1)
    cells = fields.size // 6 // vectors

    def cost(flops, passes):
        return pl.CostEstimate(flops=flops * cells, bytes_accessed=passes * 4 * fields.size, transcendentals=0)

    planes = f32(nz, nx, ny)
    face = f32(*xf_shape)
    basis, eps, h, packed, table, sz = pl.pallas_call(
        prepare_kernel,
        out_shape=(whole, f32(2, nz, nx, ny), whole, planes, f32(8, nx, ny), f32(4, nz, ny)),
        in_specs=[SMEM] * 4 + [VMEM] * 2,
        out_specs=(VMEM,) * 6,
        compiler_params=params,
        cost_estimate=cost(800, 4),
        name="prepare",
    )(pml_width, eps_real, eps_loss, coeffs, near, material)
    h, xf, yt, xadd, yadd, zf = pl.pallas_call(
        slab_kernel,
        out_shape=(whole, face, f32(*yf_shape), face, planes, f32(*zf_shape)),
        in_specs=[SMEM] * 2 + [VMEM] * 4,
        out_specs=(VMEM,) * 6,
        input_output_aliases={3: 0},
        compiler_params=params,
        name="slab_face",
    )(pml_width, coeffs, basis, h, xf, yf)
    zf = passed_round(zf, "gz", 1)
    h, packed, left, acc, before, hxf, basis_new = pl.pallas_call(
        inner_kernel,
        out_shape=(whole, planes, whole, f32(vectors, 2 * vectors, SUB, ny), f32(*zf_shape), face, whole),
        in_specs=[SMEM] + [VMEM] * 8,
        out_specs=(VMEM,) * 6 + (HBM,),
        scratch_shapes=[pltpu.SemaphoreType.DMA],
        input_output_aliases={5: 0, 6: 1},
        compiler_params=params,
        cost_estimate=cost(800, 2),
        name="apply_inner",
    )(ritz, basis, eps, table, sz, h, packed, xadd, yadd)
    devices = lax.axis_size("gx") * lax.axis_size("gy") * lax.axis_size("gz")
    left, gram, _, hxf, hyf = pl.pallas_call(
        outer_kernel,
        out_shape=(whole, f32(devices, 4, ny), whole, face, f32(*yf_shape)),
        in_specs=[SMEM] * 2 + [VMEM] * 13,
        out_specs=(VMEM,) * 5,
        input_output_aliases={12: 0, 6: 2, 10: 3},
        compiler_params=params,
        cost_estimate=cost(300, 1),
        name="apply_outer",
    )(pml_width, ritz, basis, eps, table, sz, h, zf, xf, yt, hxf, packed, left, acc, before)
    gram, hxf, hyf = lax.optimization_barrier((gram, hxf, hyf))
    rows = lax.all_to_all(gram, ("gx", "gy", "gz"), 0, 0)
    from_x = passed_along(hxf, "gx", 1)
    from_y = passed_round(hyf, "gy", 1)
    _, residual = pl.pallas_call(
        rim_kernel,
        out_shape=(whole, whole),
        in_specs=[SMEM] + [VMEM] * 3,
        out_specs=(VMEM, HBM),
        scratch_shapes=[scratch(*xf_shape), scratch(nz, nx, ny), pltpu.SemaphoreType.DMA((nz,))],
        input_output_aliases={1: 0},
        compiler_params=params,
        cost_estimate=pl.CostEstimate(flops=0, bytes_accessed=0, transcendentals=0),
        name="add_rims",
    )(pml_width, left, from_x, from_y)
    rows, residual = lax.optimization_barrier((rows, residual))
    gram = pl.pallas_call(
        gather_kernel,
        out_shape=f32(2, vectors, vectors),
        in_specs=[VMEM],
        out_specs=VMEM,
        compiler_params=params,
        name="sum_rows",
    )(rows)
    return basis_new, residual, gram


def solution(mesh):
    in_specs = (P(None, None, None, "gz", "gx", "gy"), P("gz", "gx", "gy"), P(), P(), P(), P(), P())
    out_specs = (P(None, None, None, "gz", "gx", "gy"), P(None, None, None, "gz", "gx", "gy"), P())
    return jax.shard_map(body, mesh=mesh, in_specs=in_specs, out_specs=out_specs, check_vma=False)
```

```python
import functools

import jax
import jax.numpy as jnp
from jax import lax
from jax.experimental import pallas as pl
from jax.experimental.pallas import tpu as pltpu
from jax.sharding import PartitionSpec as P

OMEGA_SQ = 0.36
SIGMA_TOP = 3.0
BOUNDS = ((4, 5), (0, 1), (2, 3))
AXES = ("gz", "gx", "gy")

VMEM = pl.BlockSpec(memory_space=pltpu.VMEM)
SMEM = pl.BlockSpec(memory_space=pltpu.SMEM)
HBM = pl.BlockSpec(memory_space=pltpu.HBM)


def passed_round(value, axis, steps):
    count = lax.axis_size(axis)
    return lax.ppermute(value, axis, [(source, (source + steps) % count) for source in range(count)])


def inverse_stretch(places, length, low_width, high_width):
    inside_depth = jnp.clip((low_width - places) / low_width, 0.0, 1.0) + jnp.clip(
        (places + 1.0 - length + high_width) / high_width, 0.0, 1.0
    )
    absorb = SIGMA_TOP * inside_depth * inside_depth
    scaled = 1.0 / (1.0 + absorb * absorb)
    return scaled, -absorb * scaled


def tree_sum(values):
    while len(values) > 1:
        pairs = [values[place] + values[place + 1] for place in range(0, len(values) - 1, 2)]
        values = pairs + ([values[-1]] if len(values) % 2 else [])
    return values[0]


def cmul(left, right):
    return (left[0] * right[0] - left[1] * right[1], left[0] * right[1] + left[1] * right[0])


def add(left, right):
    return (left[0] + right[0], left[1] + right[1])


def sub(left, right):
    return (left[0] - right[0], left[1] - right[1])


def axis_stretch(pml_ref, direction, count, places):
    total = count * lax.axis_size(AXES[direction])
    low_slot, high_slot = BOUNDS[direction]
    low = jnp.full(places.shape, pml_ref[low_slot], jnp.int32).astype(jnp.float32)
    high = jnp.full(places.shape, pml_ref[high_slot], jnp.int32).astype(jnp.float32)
    return inverse_stretch(places, jnp.float32(total), low, high)


def local_places(direction, count, shape, dim):
    start = lax.axis_index(AXES[direction]) * count
    return (lax.broadcasted_iota(jnp.int32, shape, dim) + start).astype(jnp.float32)


def one_place(direction, count, offset, shape):
    start = lax.axis_index(AXES[direction]) * count + offset
    return jnp.full(shape, start, jnp.int32).astype(jnp.float32)


def packed_row(slot, part, vector, vectors):
    return (slot * 2 + part) * vectors + vector


def has_neighbour(direction, steps):
    place = lax.axis_index(AXES[direction]) + steps
    inside = (place >= 0) & (place < lax.axis_size(AXES[direction]))
    return jnp.where(inside, 1.0, 0.0).astype(jnp.float32)


def face_kernel(fields_hbm, fields_ref, xf_ref, yf_ref, sems):
    _, vectors, _, nz, nx, ny = fields_ref.shape
    lanes = lax.broadcasted_iota(jnp.int32, (nx, ny), 1)
    copies = [
        pltpu.make_async_copy(fields_hbm.at[part, :, comp], fields_ref.at[part, :, comp], sems.at[part, comp])
        for comp in (0, 2, 1) for part in range(2)
    ]
    for copy in copies:
        copy.start()
    packed = [jnp.zeros((nx, ny), jnp.float32)] * nz
    for place, comp in enumerate((0, 2)):
        for part in range(2):
            copies[2 * place + part].wait()
            for a in range(vectors):
                row = packed_row(comp // 2, part, a, vectors)
                for z in range(nz):
                    value = fields_ref[part, a, comp, z]
                    packed[z] = jnp.where(lanes == row, pltpu.roll(value, row, 1) if row else value, packed[z])
    turned = jnp.concatenate(packed, axis=0).T
    yf_ref[...] = turned[:yf_ref.shape[0]]
    for part in range(2):
        for a in range(vectors):
            xf_ref[part, a, 1] = fields_ref[part, a, 2, :, 0, :]
    for part in range(2):
        copies[4 + part].wait()
        for a in range(vectors):
            xf_ref[part, a, 0] = fields_ref[part, a, 1, :, 0, :]


def rotated(coeffs_ref, old, b):
    new = None
    for a, value in enumerate(old):
        term = cmul((coeffs_ref[0, a, b], coeffs_ref[1, a, b]), value)
        new = term if new is None else add(new, term)
    return new


SUB = 8
SHX, SEX, SHY, SEY = range(0, 8, 2)


def field_of(ref, b, comp, z, cut):
    return tuple(ref[part, b, comp, z, cut] for part in range(2))


def tiles_of(nx):
    return [slice(SUB * t, SUB * (t + 1)) for t in range(nx // SUB)]


def prepare_kernel(
    pml_ref, eps_real_ref, eps_loss_ref, coeffs_ref, fields_ref, material_ref,
    basis_ref, eps_ref, h_ref, packed_ref, table_ref, sz_ref,
):
    _, vectors, _, nz, nx, ny = fields_ref.shape
    plane = (nx, ny)
    parts = range(2)
    for slot, direction, half, count, dim in (
        (SHX, 1, 0.5, nx, 0), (SEX, 1, 0.0, nx, 0), (SHY, 2, 0.5, ny, 1), (SEY, 2, 0.0, ny, 1),
    ):
        values = axis_stretch(pml_ref, direction, count, local_places(direction, count, plane, dim) + half)
        for part in parts:
            table_ref[slot + part] = values[part]
    for slot, half in ((0, 0.0), (2, 0.5)):
        values = axis_stretch(pml_ref, 0, nz, local_places(0, nz, (nz, ny), 0) + half)
        for part in parts:
            sz_ref[slot + part] = values[part]

    @pl.loop(0, nz)
    def _(z):
        material = material_ref[z]
        for part, source in enumerate((eps_real_ref, eps_loss_ref)):
            value = jnp.zeros(plane, jnp.float32)
            for number in range(source.shape[0]):
                value = jnp.where(material == number, -OMEGA_SQ * source[number], value)
            eps_ref[part, z] = value
        for comp in range(3):
            real = [fields_ref[0, a, comp, z] for a in range(vectors)]
            imag = [fields_ref[1, a, comp, z] for a in range(vectors)]
            both = [first + second for first, second in zip(real, imag)]
            for b in range(vectors):
                turns = [(coeffs_ref[0, a, b], coeffs_ref[1, a, b]) for a in range(vectors)]
                shared = tree_sum([turn[0] * value for turn, value in zip(turns, both)])
                less = tree_sum([(turn[0] + turn[1]) * value for turn, value in zip(turns, imag)])
                more = tree_sum([(turn[1] - turn[0]) * value for turn, value in zip(turns, real)])
                basis_ref[0, b, comp, z] = shared - less
                basis_ref[1, b, comp, z] = shared + more
        packed_ref[z] = jnp.zeros(plane, jnp.float32)

    tile = (SUB, ny)
    rows = lax.broadcasted_iota(jnp.int32, tile, 0)
    lanes = lax.broadcasted_iota(jnp.int32, tile, 1)
    cuts = tiles_of(nx)

    def magnetic(b, z, last):
        shz = tuple(sz_ref[2 + part, pl.ds(z, 1)] for part in parts)
        for cut in cuts:
            u = [field_of(basis_ref, b, comp, z, cut) for comp in range(3)]

            def step_z(comp):
                if last:
                    return tuple(-value for value in u[comp])
                return sub(field_of(basis_ref, b, comp, z + 1, cut), u[comp])

            def step_x(comp):
                if cut.stop < nx:
                    ahead = field_of(basis_ref, b, comp, z, slice(cut.start + 1, cut.stop + 1))
                else:
                    ahead = tuple(jnp.where(rows == SUB - 1, 0.0, pltpu.roll(value, SUB - 1, 0)) for value in u[comp])
                return sub(ahead, u[comp])

            def step_y(comp):
                ahead = tuple(jnp.where(lanes == ny - 1, 0.0, pltpu.roll(value, ny - 1, 1)) for value in u[comp])
                return sub(ahead, u[comp])

            shx = tuple(table_ref[SHX + part, cut] for part in parts)
            shy = tuple(table_ref[SHY + part, cut] for part in parts)
            h = (
                sub(cmul(shy, step_y(2)), cmul(shz, step_z(1))),
                sub(cmul(shz, step_z(0)), cmul(shx, step_x(2))),
                sub(cmul(shx, step_x(1)), cmul(shy, step_y(0))),
            )
            for comp in range(3):
                for part in parts:
                    h_ref[part, b, comp, z, cut] = h[comp][part]
            packed = packed_ref[z, cut]
            for slot, value in enumerate((h[2], h[0])):
                for part in parts:
                    row = packed_row(slot, part, b, vectors)
                    packed = jnp.where(lanes == row, pltpu.roll(value[part], (row + 1) % ny, 1), packed)
            packed_ref[z, cut] = packed

    @pl.loop(0, nz - 1)
    def _(z):
        for b in range(vectors):
            magnetic(b, z, False)

    for b in range(vectors):
        magnetic(b, nz - 1, True)


def turn_face(coeffs_ref, direction, raw_ref, face_ref):
    inside = has_neighbour(direction, 1)
    vectors = raw_ref.shape[1]
    for slot in range(2):
        old = [(raw_ref[0, a, slot] * inside, raw_ref[1, a, slot] * inside) for a in range(vectors)]
        for b in range(vectors):
            new = rotated(coeffs_ref, old, b)
            for part in range(2):
                face_ref[part, b, slot] = new[part]


def turn_column(coeffs_ref, raw_ref, rows_ref):
    vectors = coeffs_ref.shape[1]
    inside = has_neighbour(2, 1)
    both = 2 * vectors
    shape = (both, raw_ref.shape[1])
    which = lax.broadcasted_iota(jnp.int32, shape, 0)
    turned = [jnp.zeros(shape, jnp.float32)] * 2
    for part in range(2):
        for a in range(vectors):
            column = jnp.zeros(shape, jnp.float32)
            for b in range(vectors):
                first, second = coeffs_ref[0, a, b] * inside, coeffs_ref[1, a, b] * inside
                if part:
                    first, second = -second, first
                column = jnp.where(which == b, first, column)
                column = jnp.where(which == vectors + b, second, column)
            for slot in range(2):
                row = packed_row(slot, part, a, vectors)
                turned[slot] = turned[slot] + column * raw_ref[row:row + 1]
    for slot in range(2):
        rows_ref[slot * both:(slot + 1) * both] = turned[slot]


def lane_to_last(values, slot, part, b, vectors):
    ny = values.shape[-1]
    lanes = lax.broadcasted_iota(jnp.int32, values.shape, 1)
    row = packed_row(slot, part, b, vectors)
    return jnp.where(lanes == ny - 1, pltpu.roll(values, ny - 1 - row, 1), 0.0)


def with_halos(h, b, z, cut, nx, xadd_ref, yadd_ref):
    vectors = xadd_ref.shape[1]
    column = yadd_ref[z, cut]
    hx = tuple(h[0][part] + lane_to_last(column, 1, part, b, vectors) for part in range(2))
    hz = tuple(h[2][part] + lane_to_last(column, 0, part, b, vectors) for part in range(2))
    hy = h[1]
    if cut.stop == nx:
        rows = lax.broadcasted_iota(jnp.int32, column.shape, 0)

        def row_of(slot):
            return tuple(
                jnp.where(rows == SUB - 1, xadd_ref[part, b, slot, pl.ds(z, 1)], 0.0) for part in range(2)
            )

        hy, hz = add(hy, row_of(0)), add(hz, row_of(1))
    return hx, hy, hz


def slab_kernel(
    pml_ref, coeffs_ref, basis_ref, h_in, raw_xf_ref, raw_yf_ref,
    h_ref, xf_ref, yt_ref, xadd_ref, yadd_ref, zf_ref,
):
    del h_in
    _, vectors, _, nz, nx, ny = basis_ref.shape
    parts = range(2)
    cells = nz * nx
    both = 2 * vectors
    turn_face(coeffs_ref, 1, raw_xf_ref, xf_ref)
    turn_column(coeffs_ref, raw_yf_ref, yt_ref)
    shx = axis_stretch(pml_ref, 1, nx, one_place(1, nx, nx - 1, (1, ny)) + 0.5)
    shy = axis_stretch(pml_ref, 2, ny, one_place(2, ny, ny - 1, (1, cells)) + 0.5)
    for b in range(vectors):
        for slot in range(2):
            value = cmul(shx, tuple(xf_ref[part, b, 1 - slot] for part in parts))
            for part in parts:
                xadd_ref[part, b, slot] = value[part] if slot else -value[part]
    added = []
    for slot in range(2):
        value = cmul(shy, (yt_ref[slot * both:slot * both + vectors], yt_ref[slot * both + vectors:(slot + 1) * both]))
        added += [part if slot else -part for part in value]
    rest = jnp.zeros((ny - 2 * both, cells), jnp.float32)
    yadd_ref[...] = jnp.concatenate(added + [rest], axis=0).T.reshape(nz, nx, ny)
    last = nz - 1
    lower = jnp.full((SUB, ny), lax.axis_index(AXES[0]), jnp.int32) == 0
    for b in range(vectors):
        for cut in tiles_of(nx):
            h = [field_of(h_ref, b, comp, last, cut) for comp in range(3)]
            h = with_halos(h, b, last, cut, nx, xadd_ref, yadd_ref)
            for part in parts:
                for comp in range(3):
                    h_ref[part, b, comp, last, cut] = h[comp][part]
                for comp in range(2):
                    zf_ref[part, b, comp, cut] = jnp.where(lower, h[comp][part], basis_ref[part, b, comp, 0, cut])


def plane_step(
    b, z, before, sums, ritz_ref, basis_ref, eps_ref, table_ref, sz_ref, h_ref, left_ref, halos=None
):
    _, vectors, _, _, nx, ny = basis_ref.shape
    rows = lax.broadcasted_iota(jnp.int32, (SUB, ny), 0)
    lanes = lax.broadcasted_iota(jnp.int32, (SUB, ny), 1)
    parts = range(2)
    cuts = tiles_of(nx)
    sez = tuple(sz_ref[part, pl.ds(z, 1)] for part in parts)
    fields = []
    for cut in cuts:
        h = [field_of(h_ref, b, comp, z, cut) for comp in range(3)]
        if halos is not None:
            h = with_halos(h, b, z, cut, nx, *halos)
            for comp in (1, 2):
                for part in parts:
                    h_ref[part, b, comp, z, cut] = h[comp][part]
        fields.append(h)
    sums = list(sums)
    for t, cut in enumerate(cuts):
        hx, hy, hz = fields[t]

        def back_x(comp):
            here = fields[t][comp]
            if t:
                past = field_of(h_ref, b, comp, z, slice(cut.start - 1, cut.stop - 1))
            else:
                past = tuple(jnp.where(rows == 0, 0.0, pltpu.roll(value, 1, 0)) for value in here)
            return sub(here, past)

        def back_y(value):
            return sub(value, tuple(jnp.where(lanes == 0, 0.0, pltpu.roll(part, 1, 1)) for part in value))

        sex = tuple(table_ref[SEX + part, cut] for part in parts)
        sey = tuple(table_ref[SEY + part, cut] for part in parts)
        bxy, bxz = (cmul(sex, back_x(comp)) for comp in (1, 2))
        byz, byx = (cmul(sey, back_y(value)) for value in (hz, hx))
        bzx, bzy = (cmul(sez, sub(value, past)) for value, past in zip((hx, hy), before[t]))
        curl = (sub(byz, bzy), sub(bzx, bxz), sub(bxy, byx))
        u = [field_of(basis_ref, b, comp, z, cut) for comp in range(3)]
        eps = tuple(eps_ref[part, z, cut] for part in parts)
        w = [add(curl[comp], cmul(eps, u[comp])) for comp in range(3)]
        for comp in range(3):
            left = sub(w[comp], cmul((ritz_ref[0, b], ritz_ref[1, b]), u[comp]))
            for part in parts:
                left_ref[part, b, comp, z, cut] = left[part]
        for a in range(vectors):
            total = sums[a]
            for comp in range(3):
                total = add(total, cmul(field_of(basis_ref, a, comp, z, cut), w[comp]))
            sums[a] = total
    return [(h[0], h[1]) for h in fields], sums


def inner_kernel(
    ritz_ref, basis_ref, eps_ref, table_ref, sz_ref, h_in, packed_in, xadd_ref, yadd_ref,
    h_ref, packed_ref, left_ref, acc_ref, before_ref, hxf_ref, basis_hbm, sem,
):
    del h_in, packed_in
    _, vectors, _, nz, nx, ny = basis_ref.shape
    keep = pltpu.make_async_copy(basis_ref, basis_hbm, sem)
    keep.start()
    cuts = tiles_of(nx)
    lanes = lax.broadcasted_iota(jnp.int32, (nz, ny), 1)
    open_plane = lax.broadcasted_iota(jnp.int32, (nz, ny), 0) < nz - 1
    packed_ref[...] = packed_ref[...] + yadd_ref[...]
    corner = packed_ref[:, nx - 1, :]
    for b in range(vectors):
        for part in range(2):
            row = packed_row(0, part, b, vectors)
            more = xadd_ref[part, b, 1]
            corner = corner + jnp.where(lanes == row, pltpu.roll(more, (row + 1) % ny, 1), 0.0)
            more = more + lane_to_last(yadd_ref[:, nx - 1, :], 0, part, b, vectors)
            hxf_ref[part, b, 0] = h_ref[part, b, 1, :, nx - 1, :] + jnp.where(open_plane, xadd_ref[part, b, 0], 0.0)
            hxf_ref[part, b, 1] = h_ref[part, b, 2, :, nx - 1, :] + jnp.where(open_plane, more, 0.0)
    packed_ref[:, nx - 1, :] = corner
    acc_ref[...] = jnp.zeros(acc_ref.shape, jnp.float32)
    before_ref[...] = jnp.zeros(before_ref.shape, jnp.float32)

    @pl.loop(0, nz - 1)
    def _(z):
        for b in range(vectors):
            before = [
                tuple(tuple(before_ref[part, b, slot, cut] for part in range(2)) for slot in range(2)) for cut in cuts
            ]
            sums = [(acc_ref[b, a], acc_ref[b, vectors + a]) for a in range(vectors)]
            before, sums = plane_step(
                b, z, before, sums, ritz_ref, basis_ref, eps_ref, table_ref, sz_ref, h_ref, left_ref, (xadd_ref, yadd_ref)
            )
            for part in range(2):
                for a in range(vectors):
                    acc_ref[b, part * vectors + a] = sums[a][part]
                for t, cut in enumerate(cuts):
                    for slot in range(2):
                        before_ref[part, b, slot, cut] = before[t][slot][part]

    keep.wait()


def close_last_plane(sz_ref, zf_ref, packed_in, h_ref, hxf_ref, hyf_ref):
    _, vectors, _, nz, nx, ny = h_ref.shape
    parts = range(2)
    last = nz - 1
    lanes = lax.broadcasted_iota(jnp.int32, (SUB, ny), 1)
    shz = tuple(sz_ref[2 + part, last:] * has_neighbour(0, 1) for part in parts)
    packed = [packed_in[last, cut] for cut in tiles_of(nx)]
    for b in range(vectors):
        for t, cut in enumerate(tiles_of(nx)):
            ex, ey = (tuple(zf_ref[part, b, slot, cut] for part in parts) for slot in range(2))
            more = (tuple(-value for value in cmul(shz, ey)), cmul(shz, ex))
            for part in parts:
                for comp in range(2):
                    h_ref[part, b, comp, last, cut] = h_ref[part, b, comp, last, cut] + more[comp][part]
                row = packed_row(1, part, b, vectors)
                edge = pltpu.roll(more[0][part], (row + 1) % ny, 1)
                packed[t] = packed[t] + jnp.where(lanes == row, edge, 0.0)
                if cut.stop == nx:
                    hxf_ref[part, b, 0, last:] = hxf_ref[part, b, 0, last:] + more[1][part][SUB - 1:]
    inner = packed_in[:last].reshape(last * nx, ny)
    hyf_ref[...] = jnp.concatenate([inner] + packed, axis=0).T[:hyf_ref.shape[0]]


def outer_kernel(
    pml_ref, ritz_ref, basis_ref, eps_ref, table_ref, sz_ref, h_in, zf_ref, xf_ref, yt_ref, hxf_in, packed_in,
    left_in, acc_ref, before_ref, left_ref, gram_ref, h_ref, hxf_ref, hyf_ref,
):
    del left_in, h_in, hxf_in
    close_last_plane(sz_ref, zf_ref, packed_in, h_ref, hxf_ref, hyf_ref)
    _, vectors, _, nz, nx, ny = basis_ref.shape
    parts = range(2)
    cuts = tiles_of(nx)
    under = axis_stretch(pml_ref, 0, nz, one_place(0, nz, -1, (1, ny)) + 0.5)
    sez = tuple(sz_ref[part, 0:1] * has_neighbour(0, -1) for part in parts)
    sx_next = axis_stretch(pml_ref, 1, nx, one_place(1, nx, nx, (1, ny)))
    sy_next = axis_stretch(pml_ref, 2, ny, one_place(2, ny, ny, (1, nz * nx)))
    both = 2 * vectors
    ends = [
        cmul(sy_next, (yt_ref[slot * both:slot * both + vectors], yt_ref[slot * both + vectors:(slot + 1) * both]))
        for slot in range(2)
    ]
    columns = lax.broadcasted_iota(jnp.int32, (both, ny), 1)
    gram = jnp.zeros((both, ny), jnp.float32)
    for b in range(vectors):

        def tile_of(ref, slot, cut, b=b):
            return tuple(ref[part, b, slot, cut] for part in parts)

        before = [tuple(tile_of(before_ref, slot, cut) for slot in range(2)) for cut in cuts]
        sums = [(acc_ref[b, a], acc_ref[b, vectors + a]) for a in range(vectors)]
        _, sums = plane_step(
            b, nz - 1, before, sums, ritz_ref, basis_ref, eps_ref, table_ref, sz_ref, h_ref, left_ref
        )
        for cut in cuts:
            ex, ey = (field_of(basis_ref, b, comp, 0, cut) for comp in range(2))
            hx = sub(tile_of(zf_ref, 0, cut), cmul(under, ey))
            hy = add(tile_of(zf_ref, 1, cut), cmul(under, ex))
            more = (cmul(sez, hy), cmul(sez, hx))
            for part in parts:
                left_ref[part, b, 0, 0, cut] = left_ref[part, b, 0, 0, cut] + more[0][part]
                left_ref[part, b, 1, 0, cut] = left_ref[part, b, 1, 0, cut] - more[1][part]
            for a in range(vectors):
                ex, ey = (field_of(basis_ref, a, comp, 0, cut) for comp in range(2))
                sums[a] = add(sums[a], sub(cmul(ex, more[0]), cmul(ey, more[1])))
        h_y = tuple(hxf_ref[part, b, 0] for part in parts)
        h_z = tuple(hxf_ref[part, b, 1] for part in parts)
        for a in range(vectors):
            over = cmul(tuple(xf_ref[part, a, 0] for part in parts), h_z)
            over = sub(over, cmul(tuple(xf_ref[part, a, 1] for part in parts), h_y))
            over = cmul(sx_next, over)
            for row in range(0, nz, SUB):
                sums[a] = add(sums[a], tuple(part[row:row + SUB] for part in over))
        flat = jnp.concatenate(
            [jnp.sum(sums[a][part], axis=0, keepdims=True) for part in parts for a in range(vectors)], axis=0
        )
        over = None
        for slot in range(2):
            h = tuple(hyf_ref[packed_row(slot, part, b, vectors)][None] for part in parts)
            term = cmul(ends[slot], h)
            over = term if over is None else sub(term, over)
        side = jnp.concatenate(over, axis=0)
        total = jnp.sum(flat, axis=1, keepdims=True) + jnp.sum(side, axis=1, keepdims=True)
        gram = jnp.where(columns == b, total, gram)
    everywhere = 3.0 * nz * nx * ny
    for axis in AXES:
        everywhere = everywhere * lax.axis_size(axis)
    gram = gram * (1.0 / everywhere)
    row = tree_sum([gram[0:1]] + [pltpu.roll(gram[row:row + 1], row * vectors, 1) for row in range(1, both)])
    block = jnp.concatenate([row, jnp.zeros((gram_ref.shape[1] - 1, ny), jnp.float32)], axis=0)
    for device in range(gram_ref.shape[0]):
        gram_ref[device] = block


def gather_kernel(rows_ref, gram_ref):
    vectors = gram_ref.shape[1]
    total = tree_sum([rows_ref[device] for device in range(rows_ref.shape[0])])[0:1]
    count = total.shape[1]
    for part in range(2):
        for a in range(vectors):
            row = (part * vectors + a) * vectors
            turned = pltpu.roll(total, count - row, 1) if row else total
            gram_ref[part, a:a + 1] = turned[:, :vectors]


def rim_y_kernel(pml_ref, left_in, hyf_ref, left_ref, residual_hbm, yadd_ref, sems):
    del left_in
    _, vectors, _, nz, nx, ny = left_ref.shape
    parts = range(2)
    both = 2 * vectors
    sey = axis_stretch(pml_ref, 2, ny, one_place(2, ny, 0, (vectors, nz * nx)))
    sey = tuple(part * has_neighbour(2, -1) for part in sey)
    added = []
    for slot in range(2):
        first = slot * both
        value = cmul(sey, (hyf_ref[first:first + vectors], hyf_ref[first + vectors:first + both]))
        added += [part if slot else -part for part in value]
    rest = jnp.zeros((ny - 2 * both, nz * nx), jnp.float32)
    yadd_ref[...] = jnp.concatenate(added + [rest], axis=0).T.reshape(nz, nx, ny)
    lanes = lax.broadcasted_iota(jnp.int32, (SUB, ny), 1)

    def kept(z):
        blocks = [(slice(None), slice(None), 0, z)]
        blocks += [(slice(None), slice(None), comp, z, slice(SUB, nx)) for comp in (1, 2)]
        return [
            pltpu.make_async_copy(left_ref.at[block], residual_hbm.at[block], sems.at[place, z])
            for place, block in enumerate(blocks)
        ]

    @pl.loop(0, nz)
    def _(z):
        for cut in tiles_of(nx):
            column = yadd_ref[z, cut]
            for b in range(vectors):
                for part in parts:
                    for slot, comp in enumerate((0, 2)):
                        row = packed_row(slot, part, b, vectors)
                        value = pltpu.roll(column, ny - row, 1) if row else column
                        value = jnp.where(lanes == 0, value, 0.0)
                        left_ref[part, b, comp, z, cut] = left_ref[part, b, comp, z, cut] + value
        for copy in kept(z):
            copy.start()

    @pl.loop(0, nz)
    def _(z):
        for copy in kept(z):
            copy.wait()


def rim_x_kernel(pml_ref, left_in, residual_in, hxf_ref, left_ref, residual_hbm, xadd_ref, sems):
    del left_in, residual_in
    _, vectors, _, nz, nx, ny = left_ref.shape
    parts = range(2)
    sex = axis_stretch(pml_ref, 1, nx, one_place(1, nx, 0, (nz, ny)))
    sex = tuple(part * has_neighbour(1, -1) for part in sex)
    for b in range(vectors):
        for slot in range(2):
            value = cmul(sex, tuple(hxf_ref[part, b, slot] for part in parts))
            for part in parts:
                xadd_ref[part, b, slot] = value[part] if slot else -value[part]
    rows = lax.broadcasted_iota(jnp.int32, (SUB, ny), 0)
    first = slice(0, SUB)
    copies = []
    for z in range(nz):
        for b in range(vectors):
            for part in parts:
                for slot, comp in ((1, 1), (0, 2)):
                    value = jnp.where(rows == 0, xadd_ref[part, b, slot, z:z + 1], 0.0)
                    left_ref[part, b, comp, z, first] = left_ref[part, b, comp, z, first] + value
        block = (slice(None), slice(None), slice(1, 3), z, first)
        copies.append(pltpu.make_async_copy(left_ref.at[block], residual_hbm.at[block], sems.at[z]))
        copies[-1].start()
    for copy in copies:
        copy.wait()


def body(fields, material, pml_width, eps_real, eps_loss, coeffs, ritz):
    _, vectors, _, nz, nx, ny = fields.shape
    f32 = lambda *shape: jax.ShapeDtypeStruct(shape, jnp.float32)
    scratch = lambda *shape: pltpu.VMEM(shape, jnp.float32)
    params = pltpu.CompilerParams(vmem_limit_bytes=40 * 1024 * 1024)
    whole = f32(*fields.shape)
    zf_shape = (2, vectors, 2, nx, ny)
    xf_shape = (2, vectors, 2, nz, ny)
    yf_shape = (4 * vectors, nz * nx)
    near, xf, yf = pl.pallas_call(
        face_kernel,
        out_shape=(whole, f32(*xf_shape), f32(*yf_shape)),
        in_specs=[HBM],
        out_specs=(VMEM,) * 3,
        scratch_shapes=[pltpu.SemaphoreType.DMA((2, 3))],
        compiler_params=params,
        name="take_faces",
    )(pltpu.with_memory_space_constraint(fields, pltpu.HBM))
    xf = passed_round(xf, "gx", -1)
    yf = passed_round(yf, "gy", -1)
    cells = fields.size // 6 // vectors

    def cost(flops, passes):
        return pl.CostEstimate(flops=flops * cells, bytes_accessed=passes * 4 * fields.size, transcendentals=0)

    planes = f32(nz, nx, ny)
    face = f32(*xf_shape)
    basis, eps, h, packed, table, sz = pl.pallas_call(
        prepare_kernel,
        out_shape=(whole, f32(2, nz, nx, ny), whole, planes, f32(8, nx, ny), f32(4, nz, ny)),
        in_specs=[SMEM] * 4 + [VMEM] * 2,
        out_specs=(VMEM,) * 6,
        compiler_params=params,
        cost_estimate=cost(800, 4),
        name="prepare",
    )(pml_width, eps_real, eps_loss, coeffs, near, material)
    h, xf, yt, xadd, yadd, zf = pl.pallas_call(
        slab_kernel,
        out_shape=(whole, face, f32(*yf_shape), face, planes, f32(*zf_shape)),
        in_specs=[SMEM] * 2 + [VMEM] * 4,
        out_specs=(VMEM,) * 6,
        input_output_aliases={3: 0},
        compiler_params=params,
        name="slab_face",
    )(pml_width, coeffs, basis, h, xf, yf)
    zf = passed_round(zf, "gz", 1)
    h, packed, left, acc, before, hxf, basis_new = pl.pallas_call(
        inner_kernel,
        out_shape=(whole, planes, whole, f32(vectors, 2 * vectors, SUB, ny), f32(*zf_shape), face, whole),
        in_specs=[SMEM] + [VMEM] * 8,
        out_specs=(VMEM,) * 6 + (HBM,),
        scratch_shapes=[pltpu.SemaphoreType.DMA],
        input_output_aliases={5: 0, 6: 1},
        compiler_params=params,
        cost_estimate=cost(800, 2),
        name="apply_inner",
    )(ritz, basis, eps, table, sz, h, packed, xadd, yadd)
    devices = lax.axis_size("gx") * lax.axis_size("gy") * lax.axis_size("gz")
    left, gram, _, hxf, hyf = pl.pallas_call(
        outer_kernel,
        out_shape=(whole, f32(devices, 4, ny), whole, face, f32(*yf_shape)),
        in_specs=[SMEM] * 2 + [VMEM] * 13,
        out_specs=(VMEM,) * 5,
        input_output_aliases={12: 0, 6: 2, 10: 3},
        compiler_params=params,
        cost_estimate=cost(300, 1),
        name="apply_outer",
    )(pml_width, ritz, basis, eps, table, sz, h, zf, xf, yt, hxf, packed, left, acc, before)
    gram, hxf, hyf = lax.optimization_barrier((gram, hxf, hyf))
    rows = lax.all_to_all(gram, ("gx", "gy", "gz"), 0, 0)
    from_x = passed_round(hxf, "gx", 1)
    from_y = passed_round(hyf, "gy", 1)
    free = pl.CostEstimate(flops=0, bytes_accessed=0, transcendentals=0)
    left, residual = pl.pallas_call(
        rim_y_kernel,
        out_shape=(whole, whole),
        in_specs=[SMEM] + [VMEM] * 2,
        out_specs=(VMEM, HBM),
        scratch_shapes=[scratch(nz, nx, ny), pltpu.SemaphoreType.DMA((3, nz))],
        input_output_aliases={1: 0},
        compiler_params=params,
        cost_estimate=free,
        name="add_y_rims",
    )(pml_width, left, from_y)
    _, residual = pl.pallas_call(
        rim_x_kernel,
        out_shape=(whole, whole),
        in_specs=[SMEM, VMEM, HBM, VMEM],
        out_specs=(VMEM, HBM),
        scratch_shapes=[scratch(*xf_shape), pltpu.SemaphoreType.DMA((nz,))],
        input_output_aliases={1: 0, 2: 1},
        compiler_params=params,
        cost_estimate=free,
        name="add_x_rims",
    )(pml_width, left, residual, from_x)
    rows, residual = lax.optimization_barrier((rows, residual))
    gram = pl.pallas_call(
        gather_kernel,
        out_shape=f32(2, vectors, vectors),
        in_specs=[VMEM],
        out_specs=VMEM,
        compiler_params=params,
        name="sum_rows",
    )(rows)
    return basis_new, residual, gram


def solution(mesh):
    in_specs = (P(None, None, None, "gz", "gx", "gy"), P("gz", "gx", "gy"), P(), P(), P(), P(), P())
    out_specs = (P(None, None, None, "gz", "gx", "gy"), P(None, None, None, "gz", "gx", "gy"), P())
    return jax.shard_map(body, mesh=mesh, in_specs=in_specs, out_specs=out_specs, check_vma=False)
```

```python
import functools

import jax
import jax.numpy as jnp
from jax import lax
from jax.experimental import pallas as pl
from jax.experimental.pallas import tpu as pltpu
from jax.sharding import PartitionSpec as P

OMEGA_SQ = 0.36
SIGMA_TOP = 3.0
BOUNDS = ((4, 5), (0, 1), (2, 3))
AXES = ("gz", "gx", "gy")

VMEM = pl.BlockSpec(memory_space=pltpu.VMEM)
SMEM = pl.BlockSpec(memory_space=pltpu.SMEM)
HBM = pl.BlockSpec(memory_space=pltpu.HBM)


def passed_round(value, axis, steps):
    count = lax.axis_size(axis)
    return lax.ppermute(value, axis, [(source, (source + steps) % count) for source in range(count)])


def inverse_stretch(places, length, low_width, high_width):
    inside_depth = jnp.clip((low_width - places) / low_width, 0.0, 1.0) + jnp.clip(
        (places + 1.0 - length + high_width) / high_width, 0.0, 1.0
    )
    absorb = SIGMA_TOP * inside_depth * inside_depth
    scaled = 1.0 / (1.0 + absorb * absorb)
    return scaled, -absorb * scaled


def tree_sum(values):
    while len(values) > 1:
        pairs = [values[place] + values[place + 1] for place in range(0, len(values) - 1, 2)]
        values = pairs + ([values[-1]] if len(values) % 2 else [])
    return values[0]


def cmul(left, right):
    return (left[0] * right[0] - left[1] * right[1], left[0] * right[1] + left[1] * right[0])


def add(left, right):
    return (left[0] + right[0], left[1] + right[1])


def sub(left, right):
    return (left[0] - right[0], left[1] - right[1])


def axis_stretch(pml_ref, direction, count, places):
    total = count * lax.axis_size(AXES[direction])
    low_slot, high_slot = BOUNDS[direction]
    low = jnp.full(places.shape, pml_ref[low_slot], jnp.int32).astype(jnp.float32)
    high = jnp.full(places.shape, pml_ref[high_slot], jnp.int32).astype(jnp.float32)
    return inverse_stretch(places, jnp.float32(total), low, high)


def local_places(direction, count, shape, dim):
    start = lax.axis_index(AXES[direction]) * count
    return (lax.broadcasted_iota(jnp.int32, shape, dim) + start).astype(jnp.float32)


def one_place(direction, count, offset, shape):
    start = lax.axis_index(AXES[direction]) * count + offset
    return jnp.full(shape, start, jnp.int32).astype(jnp.float32)


def packed_row(slot, part, vector, vectors):
    return (slot * 2 + part) * vectors + vector


def has_neighbour(direction, steps):
    place = lax.axis_index(AXES[direction]) + steps
    inside = (place >= 0) & (place < lax.axis_size(AXES[direction]))
    return jnp.where(inside, 1.0, 0.0).astype(jnp.float32)


def face_kernel(fields_hbm, fields_ref, xf_ref, yf_ref, sems):
    _, vectors, _, nz, nx, ny = fields_ref.shape
    lanes = lax.broadcasted_iota(jnp.int32, (nx, ny), 1)
    copies = [
        pltpu.make_async_copy(fields_hbm.at[part, :, comp], fields_ref.at[part, :, comp], sems.at[part, comp])
        for comp in (0, 2, 1) for part in range(2)
    ]
    for copy in copies:
        copy.start()
    packed = [jnp.zeros((nx, ny), jnp.float32)] * nz
    for place, comp in enumerate((0, 2)):
        for part in range(2):
            copies[2 * place + part].wait()
            for a in range(vectors):
                row = packed_row(comp // 2, part, a, vectors)
                for z in range(nz):
                    value = fields_ref[part, a, comp, z]
                    packed[z] = jnp.where(lanes == row, pltpu.roll(value, row, 1) if row else value, packed[z])
    turned = jnp.concatenate(packed, axis=0).T
    yf_ref[...] = turned[:yf_ref.shape[0]]
    for part in range(2):
        for a in range(vectors):
            xf_ref[part, a, 1] = fields_ref[part, a, 2, :, 0, :]
    for part in range(2):
        copies[4 + part].wait()
        for a in range(vectors):
            xf_ref[part, a, 0] = fields_ref[part, a, 1, :, 0, :]


def rotated(coeffs_ref, old, b):
    new = None
    for a, value in enumerate(old):
        term = cmul((coeffs_ref[0, a, b], coeffs_ref[1, a, b]), value)
        new = term if new is None else add(new, term)
    return new


SUB = 8
SHX, SEX, SHY, SEY = range(0, 8, 2)


class Splats:
    def __init__(self, ref, first, shape):
        self.ref, self.first, self.shape = ref, first, shape

    def __getitem__(self, place):
        row = 0
        for index, size in zip(place, self.shape):
            row = row * size + index
        return self.ref[self.first + row:self.first + row + 1]


ENDS = ("under", "next_x", "next_y", "first_x", "first_y", "last_x", "last_y")


def end_value(splat_ref, name, width=None):
    row = 2 * ENDS.index(name)
    return tuple(splat_ref[row + part:row + part + 1, :width] for part in range(2))


def ritz_rows(splat_ref, vectors):
    return Splats(splat_ref, 2 * len(ENDS), (2, vectors))


def coeff_rows(splat_ref, vectors):
    return Splats(splat_ref, 2 * len(ENDS) + 2 * vectors, (2, vectors, vectors))


def splat_count(vectors):
    return -(-(2 * len(ENDS) + 2 * vectors * (vectors + 1)) // SUB) * SUB


def field_of(ref, b, comp, z, cut):
    return tuple(ref[part, b, comp, z, cut] for part in range(2))


def tiles_of(nx):
    return [slice(SUB * t, SUB * (t + 1)) for t in range(nx // SUB)]


def prepare_kernel(
    pml_ref, eps_real_ref, eps_loss_ref, coeffs_ref, ritz_ref, fields_ref, material_ref,
    basis_ref, eps_ref, h_ref, packed_ref, table_ref, sz_ref, splat_ref,
):
    _, vectors, _, nz, nx, ny = fields_ref.shape
    plane = (nx, ny)
    parts = range(2)
    for slot, direction, half, count, dim in (
        (SHX, 1, 0.5, nx, 0), (SEX, 1, 0.0, nx, 0), (SHY, 2, 0.5, ny, 1), (SEY, 2, 0.0, ny, 1),
    ):
        values = axis_stretch(pml_ref, direction, count, local_places(direction, count, plane, dim) + half)
        for part in parts:
            table_ref[slot + part] = values[part]
    line = (1, ny)
    ends = {
        "under": (0, nz, -1, 0.5, 1.0),
        "next_x": (1, nx, nx, 0.0, 1.0),
        "next_y": (2, ny, ny, 0.0, 1.0),
        "first_x": (1, nx, 0, 0.0, has_neighbour(1, -1)),
        "first_y": (2, ny, 0, 0.0, has_neighbour(2, -1)),
        "last_x": (1, nx, nx - 1, 0.5, 1.0),
        "last_y": (2, ny, ny - 1, 0.5, 1.0),
    }
    lines = []
    for name in ENDS:
        direction, count, offset, half, factor = ends[name]
        values = axis_stretch(pml_ref, direction, count, one_place(direction, count, offset, line) + half)
        lines += [value * factor for value in values]
    lines += [jnp.full(line, ritz_ref[part, b], jnp.float32) for part in parts for b in range(vectors)]
    lines += [
        jnp.full(line, coeffs_ref[part, a, b], jnp.float32)
        for part in parts for a in range(vectors) for b in range(vectors)
    ]
    for row, value in enumerate(lines):
        splat_ref[row:row + 1] = value
    splat_ref[len(lines):] = jnp.zeros((splat_ref.shape[0] - len(lines), ny), jnp.float32)
    for slot, half in ((0, 0.0), (2, 0.5)):
        values = axis_stretch(pml_ref, 0, nz, local_places(0, nz, (nz, ny), 0) + half)
        for part in parts:
            sz_ref[slot + part] = values[part]

    @pl.loop(0, nz)
    def _(z):
        material = material_ref[z]
        for part, source in enumerate((eps_real_ref, eps_loss_ref)):
            value = jnp.zeros(plane, jnp.float32)
            for number in range(source.shape[0]):
                value = jnp.where(material == number, -OMEGA_SQ * source[number], value)
            eps_ref[part, z] = value
        for comp in range(3):
            real = [fields_ref[0, a, comp, z] for a in range(vectors)]
            imag = [fields_ref[1, a, comp, z] for a in range(vectors)]
            both = [first + second for first, second in zip(real, imag)]
            for b in range(vectors):
                turns = [(coeffs_ref[0, a, b], coeffs_ref[1, a, b]) for a in range(vectors)]
                shared = tree_sum([turn[0] * value for turn, value in zip(turns, both)])
                less = tree_sum([(turn[0] + turn[1]) * value for turn, value in zip(turns, imag)])
                more = tree_sum([(turn[1] - turn[0]) * value for turn, value in zip(turns, real)])
                basis_ref[0, b, comp, z] = shared - less
                basis_ref[1, b, comp, z] = shared + more
        packed_ref[z] = jnp.zeros(plane, jnp.float32)

    tile = (SUB, ny)
    rows = lax.broadcasted_iota(jnp.int32, tile, 0)
    lanes = lax.broadcasted_iota(jnp.int32, tile, 1)
    cuts = tiles_of(nx)

    def magnetic(b, z, last):
        shz = tuple(sz_ref[2 + part, pl.ds(z, 1)] for part in parts)
        for cut in cuts:
            u = [field_of(basis_ref, b, comp, z, cut) for comp in range(3)]

            def step_z(comp):
                if last:
                    return tuple(-value for value in u[comp])
                return sub(field_of(basis_ref, b, comp, z + 1, cut), u[comp])

            def step_x(comp):
                if cut.stop < nx:
                    ahead = field_of(basis_ref, b, comp, z, slice(cut.start + 1, cut.stop + 1))
                else:
                    ahead = tuple(jnp.where(rows == SUB - 1, 0.0, pltpu.roll(value, SUB - 1, 0)) for value in u[comp])
                return sub(ahead, u[comp])

            def step_y(comp):
                ahead = tuple(jnp.where(lanes == ny - 1, 0.0, pltpu.roll(value, ny - 1, 1)) for value in u[comp])
                return sub(ahead, u[comp])

            shx = tuple(table_ref[SHX + part, cut] for part in parts)
            shy = tuple(table_ref[SHY + part, cut] for part in parts)
            h = (
                sub(cmul(shy, step_y(2)), cmul(shz, step_z(1))),
                sub(cmul(shz, step_z(0)), cmul(shx, step_x(2))),
                sub(cmul(shx, step_x(1)), cmul(shy, step_y(0))),
            )
            for comp in range(3):
                for part in parts:
                    h_ref[part, b, comp, z, cut] = h[comp][part]
            packed = packed_ref[z, cut]
            for slot, value in enumerate((h[2], h[0])):
                for part in parts:
                    row = packed_row(slot, part, b, vectors)
                    packed = jnp.where(lanes == row, pltpu.roll(value[part], (row + 1) % ny, 1), packed)
            packed_ref[z, cut] = packed

    @pl.loop(0, nz - 1)
    def _(z):
        for b in range(vectors):
            magnetic(b, z, False)

    for b in range(vectors):
        magnetic(b, nz - 1, True)


def turn_face(coeffs_ref, direction, raw_ref, face_ref):
    inside = has_neighbour(direction, 1)
    vectors = raw_ref.shape[1]
    for slot in range(2):
        old = [(raw_ref[0, a, slot] * inside, raw_ref[1, a, slot] * inside) for a in range(vectors)]
        for b in range(vectors):
            new = rotated(coeffs_ref, old, b)
            for part in range(2):
                face_ref[part, b, slot] = new[part]


def turn_column(coeffs_ref, raw_ref, rows_ref):
    vectors = coeffs_ref.shape[1]
    inside = has_neighbour(2, 1)
    both = 2 * vectors
    shape = (both, raw_ref.shape[1])
    which = lax.broadcasted_iota(jnp.int32, shape, 0)
    turned = [jnp.zeros(shape, jnp.float32)] * 2
    for part in range(2):
        for a in range(vectors):
            column = jnp.zeros(shape, jnp.float32)
            for b in range(vectors):
                first, second = (coeffs_ref[0, a, b] * inside)[:, :shape[1]], (coeffs_ref[1, a, b] * inside)[:, :shape[1]]
                if part:
                    first, second = -second, first
                column = jnp.where(which == b, first, column)
                column = jnp.where(which == vectors + b, second, column)
            for slot in range(2):
                row = packed_row(slot, part, a, vectors)
                turned[slot] = turned[slot] + column * raw_ref[row:row + 1]
    for slot in range(2):
        rows_ref[slot * both:(slot + 1) * both] = turned[slot]


def lane_to_last(values, slot, part, b, vectors):
    ny = values.shape[-1]
    lanes = lax.broadcasted_iota(jnp.int32, values.shape, 1)
    row = packed_row(slot, part, b, vectors)
    return jnp.where(lanes == ny - 1, pltpu.roll(values, ny - 1 - row, 1), 0.0)


def with_halos(h, b, z, cut, nx, xadd_ref, yadd_ref):
    vectors = xadd_ref.shape[1]
    column = yadd_ref[z, cut]
    hx = tuple(h[0][part] + lane_to_last(column, 1, part, b, vectors) for part in range(2))
    hz = tuple(h[2][part] + lane_to_last(column, 0, part, b, vectors) for part in range(2))
    hy = h[1]
    if cut.stop == nx:
        rows = lax.broadcasted_iota(jnp.int32, column.shape, 0)

        def row_of(slot):
            return tuple(
                jnp.where(rows == SUB - 1, xadd_ref[part, b, slot, pl.ds(z, 1)], 0.0) for part in range(2)
            )

        hy, hz = add(hy, row_of(0)), add(hz, row_of(1))
    return hx, hy, hz


def slab_kernel(
    splat_ref, basis_ref, h_in, raw_xf_ref, raw_yf_ref,
    h_ref, xf_ref, yt_ref, xadd_ref, yadd_ref, zf_ref,
):
    del h_in
    _, vectors, _, nz, nx, ny = basis_ref.shape
    parts = range(2)
    cells = nz * nx
    both = 2 * vectors
    coeffs = coeff_rows(splat_ref, vectors)
    turn_face(coeffs, 1, raw_xf_ref, xf_ref)
    turn_column(coeffs, raw_yf_ref, yt_ref)
    shx = end_value(splat_ref, "last_x")
    shy = end_value(splat_ref, "last_y", cells)
    for b in range(vectors):
        for slot in range(2):
            value = cmul(shx, tuple(xf_ref[part, b, 1 - slot] for part in parts))
            for part in parts:
                xadd_ref[part, b, slot] = value[part] if slot else -value[part]
    added = []
    for slot in range(2):
        value = cmul(shy, (yt_ref[slot * both:slot * both + vectors], yt_ref[slot * both + vectors:(slot + 1) * both]))
        added += [part if slot else -part for part in value]
    rest = jnp.zeros((ny - 2 * both, cells), jnp.float32)
    yadd_ref[...] = jnp.concatenate(added + [rest], axis=0).T.reshape(nz, nx, ny)
    last = nz - 1
    lower = jnp.full((SUB, ny), lax.axis_index(AXES[0]), jnp.int32) == 0
    for b in range(vectors):
        for cut in tiles_of(nx):
            h = [field_of(h_ref, b, comp, last, cut) for comp in range(3)]
            h = with_halos(h, b, last, cut, nx, xadd_ref, yadd_ref)
            for part in parts:
                for comp in range(3):
                    h_ref[part, b, comp, last, cut] = h[comp][part]
                for comp in range(2):
                    zf_ref[part, b, comp, cut] = jnp.where(lower, h[comp][part], basis_ref[part, b, comp, 0, cut])


def plane_step(
    b, z, before, sums, ritz_ref, basis_ref, eps_ref, table_ref, sz_ref, h_ref, left_ref, halos=None
):
    _, vectors, _, _, nx, ny = basis_ref.shape
    rows = lax.broadcasted_iota(jnp.int32, (SUB, ny), 0)
    lanes = lax.broadcasted_iota(jnp.int32, (SUB, ny), 1)
    parts = range(2)
    cuts = tiles_of(nx)
    sez = tuple(sz_ref[part, pl.ds(z, 1)] for part in parts)
    fields = []
    for cut in cuts:
        h = [field_of(h_ref, b, comp, z, cut) for comp in range(3)]
        if halos is not None:
            h = with_halos(h, b, z, cut, nx, *halos)
            for comp in (1, 2):
                for part in parts:
                    h_ref[part, b, comp, z, cut] = h[comp][part]
        fields.append(h)
    sums = list(sums)
    for t, cut in enumerate(cuts):
        hx, hy, hz = fields[t]

        def back_x(comp):
            here = fields[t][comp]
            if t:
                past = field_of(h_ref, b, comp, z, slice(cut.start - 1, cut.stop - 1))
            else:
                past = tuple(jnp.where(rows == 0, 0.0, pltpu.roll(value, 1, 0)) for value in here)
            return sub(here, past)

        def back_y(value):
            return sub(value, tuple(jnp.where(lanes == 0, 0.0, pltpu.roll(part, 1, 1)) for part in value))

        sex = tuple(table_ref[SEX + part, cut] for part in parts)
        sey = tuple(table_ref[SEY + part, cut] for part in parts)
        bxy, bxz = (cmul(sex, back_x(comp)) for comp in (1, 2))
        byz, byx = (cmul(sey, back_y(value)) for value in (hz, hx))
        bzx, bzy = (cmul(sez, sub(value, past)) for value, past in zip((hx, hy), before[t]))
        curl = (sub(byz, bzy), sub(bzx, bxz), sub(bxy, byx))
        u = [field_of(basis_ref, b, comp, z, cut) for comp in range(3)]
        eps = tuple(eps_ref[part, z, cut] for part in parts)
        w = [add(curl[comp], cmul(eps, u[comp])) for comp in range(3)]
        for comp in range(3):
            left = sub(w[comp], cmul((ritz_ref[0, b], ritz_ref[1, b]), u[comp]))
            for part in parts:
                left_ref[part, b, comp, z, cut] = left[part]
        for a in range(vectors):
            total = sums[a]
            for comp in range(3):
                total = add(total, cmul(field_of(basis_ref, a, comp, z, cut), w[comp]))
            sums[a] = total
    return [(h[0], h[1]) for h in fields], sums


def inner_kernel(
    splat_ref, basis_ref, eps_ref, table_ref, sz_ref, h_in, packed_in, xadd_ref, yadd_ref,
    h_ref, packed_ref, left_ref, acc_ref, before_ref, hxf_ref, basis_hbm, sem,
):
    del h_in, packed_in
    _, vectors, _, nz, nx, ny = basis_ref.shape
    keep = pltpu.make_async_copy(basis_ref, basis_hbm, sem)
    keep.start()
    cuts = tiles_of(nx)
    lanes = lax.broadcasted_iota(jnp.int32, (nz, ny), 1)
    open_plane = lax.broadcasted_iota(jnp.int32, (nz, ny), 0) < nz - 1
    packed_ref[...] = packed_ref[...] + yadd_ref[...]
    corner = packed_ref[:, nx - 1, :]
    for b in range(vectors):
        for part in range(2):
            row = packed_row(0, part, b, vectors)
            more = xadd_ref[part, b, 1]
            corner = corner + jnp.where(lanes == row, pltpu.roll(more, (row + 1) % ny, 1), 0.0)
            more = more + lane_to_last(yadd_ref[:, nx - 1, :], 0, part, b, vectors)
            hxf_ref[part, b, 0] = h_ref[part, b, 1, :, nx - 1, :] + jnp.where(open_plane, xadd_ref[part, b, 0], 0.0)
            hxf_ref[part, b, 1] = h_ref[part, b, 2, :, nx - 1, :] + jnp.where(open_plane, more, 0.0)
    packed_ref[:, nx - 1, :] = corner
    acc_ref[...] = jnp.zeros(acc_ref.shape, jnp.float32)
    before_ref[...] = jnp.zeros(before_ref.shape, jnp.float32)

    @pl.loop(0, nz - 1)
    def _(z):
        for b in range(vectors):
            before = [
                tuple(tuple(before_ref[part, b, slot, cut] for part in range(2)) for slot in range(2)) for cut in cuts
            ]
            sums = [(acc_ref[b, a], acc_ref[b, vectors + a]) for a in range(vectors)]
            before, sums = plane_step(
                b, z, before, sums, ritz_rows(splat_ref, vectors), basis_ref, eps_ref, table_ref, sz_ref, h_ref, left_ref, (xadd_ref, yadd_ref)
            )
            for part in range(2):
                for a in range(vectors):
                    acc_ref[b, part * vectors + a] = sums[a][part]
                for t, cut in enumerate(cuts):
                    for slot in range(2):
                        before_ref[part, b, slot, cut] = before[t][slot][part]

    keep.wait()


def close_last_plane(sz_ref, zf_ref, packed_in, h_ref, hxf_ref, hyf_ref):
    _, vectors, _, nz, nx, ny = h_ref.shape
    parts = range(2)
    last = nz - 1
    lanes = lax.broadcasted_iota(jnp.int32, (SUB, ny), 1)
    shz = tuple(sz_ref[2 + part, last:] * has_neighbour(0, 1) for part in parts)
    packed = [packed_in[last, cut] for cut in tiles_of(nx)]
    for b in range(vectors):
        for t, cut in enumerate(tiles_of(nx)):
            ex, ey = (tuple(zf_ref[part, b, slot, cut] for part in parts) for slot in range(2))
            more = (tuple(-value for value in cmul(shz, ey)), cmul(shz, ex))
            for part in parts:
                for comp in range(2):
                    h_ref[part, b, comp, last, cut] = h_ref[part, b, comp, last, cut] + more[comp][part]
                row = packed_row(1, part, b, vectors)
                edge = pltpu.roll(more[0][part], (row + 1) % ny, 1)
                packed[t] = packed[t] + jnp.where(lanes == row, edge, 0.0)
                if cut.stop == nx:
                    hxf_ref[part, b, 0, last:] = hxf_ref[part, b, 0, last:] + more[1][part][SUB - 1:]
    inner = packed_in[:last].reshape(last * nx, ny)
    hyf_ref[...] = jnp.concatenate([inner] + packed, axis=0).T[:hyf_ref.shape[0]]


def outer_kernel(
    splat_ref, basis_ref, eps_ref, table_ref, sz_ref, h_in, zf_ref, xf_ref, yt_ref, hxf_in, packed_in,
    left_in, acc_ref, before_ref, left_ref, gram_ref, h_ref, hxf_ref, hyf_ref,
):
    del left_in, h_in, hxf_in
    close_last_plane(sz_ref, zf_ref, packed_in, h_ref, hxf_ref, hyf_ref)
    _, vectors, _, nz, nx, ny = basis_ref.shape
    parts = range(2)
    cuts = tiles_of(nx)
    under = end_value(splat_ref, "under")
    sez = tuple(sz_ref[part, 0:1] * has_neighbour(0, -1) for part in parts)
    sx_next = end_value(splat_ref, "next_x")
    sy_next = end_value(splat_ref, "next_y", nz * nx)
    both = 2 * vectors
    ends = [
        cmul(sy_next, (yt_ref[slot * both:slot * both + vectors], yt_ref[slot * both + vectors:(slot + 1) * both]))
        for slot in range(2)
    ]
    columns = lax.broadcasted_iota(jnp.int32, (both, ny), 1)
    gram = jnp.zeros((both, ny), jnp.float32)
    for b in range(vectors):

        def tile_of(ref, slot, cut, b=b):
            return tuple(ref[part, b, slot, cut] for part in parts)

        before = [tuple(tile_of(before_ref, slot, cut) for slot in range(2)) for cut in cuts]
        sums = [(acc_ref[b, a], acc_ref[b, vectors + a]) for a in range(vectors)]
        _, sums = plane_step(
            b, nz - 1, before, sums, ritz_rows(splat_ref, vectors), basis_ref, eps_ref, table_ref, sz_ref, h_ref, left_ref
        )
        for cut in cuts:
            ex, ey = (field_of(basis_ref, b, comp, 0, cut) for comp in range(2))
            hx = sub(tile_of(zf_ref, 0, cut), cmul(under, ey))
            hy = add(tile_of(zf_ref, 1, cut), cmul(under, ex))
            more = (cmul(sez, hy), cmul(sez, hx))
            for part in parts:
                left_ref[part, b, 0, 0, cut] = left_ref[part, b, 0, 0, cut] + more[0][part]
                left_ref[part, b, 1, 0, cut] = left_ref[part, b, 1, 0, cut] - more[1][part]
            for a in range(vectors):
                ex, ey = (field_of(basis_ref, a, comp, 0, cut) for comp in range(2))
                sums[a] = add(sums[a], sub(cmul(ex, more[0]), cmul(ey, more[1])))
        h_y = tuple(hxf_ref[part, b, 0] for part in parts)
        h_z = tuple(hxf_ref[part, b, 1] for part in parts)
        for a in range(vectors):
            over = cmul(tuple(xf_ref[part, a, 0] for part in parts), h_z)
            over = sub(over, cmul(tuple(xf_ref[part, a, 1] for part in parts), h_y))
            over = cmul(sx_next, over)
            for row in range(0, nz, SUB):
                sums[a] = add(sums[a], tuple(part[row:row + SUB] for part in over))
        flat = jnp.concatenate(
            [jnp.sum(sums[a][part], axis=0, keepdims=True) for part in parts for a in range(vectors)], axis=0
        )
        over = None
        for slot in range(2):
            h = tuple(hyf_ref[packed_row(slot, part, b, vectors)][None] for part in parts)
            term = cmul(ends[slot], h)
            over = term if over is None else sub(term, over)
        side = jnp.concatenate(over, axis=0)
        total = jnp.sum(flat, axis=1, keepdims=True) + jnp.sum(side, axis=1, keepdims=True)
        gram = jnp.where(columns == b, total, gram)
    everywhere = 3.0 * nz * nx * ny
    for axis in AXES:
        everywhere = everywhere * lax.axis_size(axis)
    gram = gram * (1.0 / everywhere)
    row = tree_sum([gram[0:1]] + [pltpu.roll(gram[row:row + 1], row * vectors, 1) for row in range(1, both)])
    block = jnp.concatenate([row, jnp.zeros((gram_ref.shape[1] - 1, ny), jnp.float32)], axis=0)
    for device in range(gram_ref.shape[0]):
        gram_ref[device] = block


def gather_kernel(rows_ref, gram_ref):
    vectors = gram_ref.shape[1]
    total = tree_sum([rows_ref[device] for device in range(rows_ref.shape[0])])[0:1]
    count = total.shape[1]
    for part in range(2):
        for a in range(vectors):
            row = (part * vectors + a) * vectors
            turned = pltpu.roll(total, count - row, 1) if row else total
            gram_ref[part, a:a + 1] = turned[:, :vectors]


def rim_y_kernel(splat_ref, left_in, hyf_ref, left_ref, residual_hbm, yadd_ref, sems):
    del left_in
    _, vectors, _, nz, nx, ny = left_ref.shape
    parts = range(2)
    both = 2 * vectors
    sey = end_value(splat_ref, "first_y", nz * nx)
    added = []
    for slot in range(2):
        first = slot * both
        value = cmul(sey, (hyf_ref[first:first + vectors], hyf_ref[first + vectors:first + both]))
        added += [part if slot else -part for part in value]
    rest = jnp.zeros((ny - 2 * both, nz * nx), jnp.float32)
    yadd_ref[...] = jnp.concatenate(added + [rest], axis=0).T.reshape(nz, nx, ny)
    lanes = lax.broadcasted_iota(jnp.int32, (SUB, ny), 1)

    def kept(z):
        blocks = [(slice(None), slice(None), 0, z)]
        blocks += [(slice(None), slice(None), comp, z, slice(SUB, nx)) for comp in (1, 2)]
        return [
            pltpu.make_async_copy(left_ref.at[block], residual_hbm.at[block], sems.at[place, z])
            for place, block in enumerate(blocks)
        ]

    @pl.loop(0, nz)
    def _(z):
        for cut in tiles_of(nx):
            column = yadd_ref[z, cut]
            for b in range(vectors):
                for part in parts:
                    for slot, comp in enumerate((0, 2)):
                        row = packed_row(slot, part, b, vectors)
                        value = pltpu.roll(column, ny - row, 1) if row else column
                        value = jnp.where(lanes == 0, value, 0.0)
                        left_ref[part, b, comp, z, cut] = left_ref[part, b, comp, z, cut] + value
        for copy in kept(z):
            copy.start()

    @pl.loop(0, nz)
    def _(z):
        for copy in kept(z):
            copy.wait()


def rim_x_kernel(splat_ref, left_in, residual_in, hxf_ref, left_ref, residual_hbm, xadd_ref, sems):
    del left_in, residual_in
    _, vectors, _, nz, nx, ny = left_ref.shape
    parts = range(2)
    sex = end_value(splat_ref, "first_x")
    for b in range(vectors):
        for slot in range(2):
            value = cmul(sex, tuple(hxf_ref[part, b, slot] for part in parts))
            for part in parts:
                xadd_ref[part, b, slot] = value[part] if slot else -value[part]
    rows = lax.broadcasted_iota(jnp.int32, (SUB, ny), 0)
    first = slice(0, SUB)
    copies = []
    for z in range(nz):
        for b in range(vectors):
            for part in parts:
                for slot, comp in ((1, 1), (0, 2)):
                    value = jnp.where(rows == 0, xadd_ref[part, b, slot, z:z + 1], 0.0)
                    left_ref[part, b, comp, z, first] = left_ref[part, b, comp, z, first] + value
        block = (slice(None), slice(None), slice(1, 3), z, first)
        copies.append(pltpu.make_async_copy(left_ref.at[block], residual_hbm.at[block], sems.at[z]))
        copies[-1].start()
    for copy in copies:
        copy.wait()


def body(fields, material, pml_width, eps_real, eps_loss, coeffs, ritz):
    _, vectors, _, nz, nx, ny = fields.shape
    f32 = lambda *shape: jax.ShapeDtypeStruct(shape, jnp.float32)
    scratch = lambda *shape: pltpu.VMEM(shape, jnp.float32)
    params = pltpu.CompilerParams(vmem_limit_bytes=40 * 1024 * 1024)
    whole = f32(*fields.shape)
    zf_shape = (2, vectors, 2, nx, ny)
    xf_shape = (2, vectors, 2, nz, ny)
    yf_shape = (4 * vectors, nz * nx)
    near, xf, yf = pl.pallas_call(
        face_kernel,
        out_shape=(whole, f32(*xf_shape), f32(*yf_shape)),
        in_specs=[HBM],
        out_specs=(VMEM,) * 3,
        scratch_shapes=[pltpu.SemaphoreType.DMA((2, 3))],
        compiler_params=params,
        name="take_faces",
    )(pltpu.with_memory_space_constraint(fields, pltpu.HBM))
    xf = passed_round(xf, "gx", -1)
    yf = passed_round(yf, "gy", -1)
    cells = fields.size // 6 // vectors

    def cost(flops, passes):
        return pl.CostEstimate(flops=flops * cells, bytes_accessed=passes * 4 * fields.size, transcendentals=0)

    planes = f32(nz, nx, ny)
    face = f32(*xf_shape)
    basis, eps, h, packed, table, sz, splats = pl.pallas_call(
        prepare_kernel,
        out_shape=(whole, f32(2, nz, nx, ny), whole, planes, f32(8, nx, ny), f32(4, nz, ny), f32(splat_count(vectors), ny)),
        in_specs=[SMEM] * 5 + [VMEM] * 2,
        out_specs=(VMEM,) * 7,
        compiler_params=params,
        cost_estimate=cost(800, 4),
        name="prepare",
    )(pml_width, eps_real, eps_loss, coeffs, ritz, near, material)
    h, xf, yt, xadd, yadd, zf = pl.pallas_call(
        slab_kernel,
        out_shape=(whole, face, f32(*yf_shape), face, planes, f32(*zf_shape)),
        in_specs=[VMEM] * 5,
        out_specs=(VMEM,) * 6,
        input_output_aliases={2: 0},
        compiler_params=params,
        name="slab_face",
    )(splats, basis, h, xf, yf)
    zf = passed_round(zf, "gz", 1)
    h, packed, left, acc, before, hxf, basis_new = pl.pallas_call(
        inner_kernel,
        out_shape=(whole, planes, whole, f32(vectors, 2 * vectors, SUB, ny), f32(*zf_shape), face, whole),
        in_specs=[VMEM] * 9,
        out_specs=(VMEM,) * 6 + (HBM,),
        scratch_shapes=[pltpu.SemaphoreType.DMA],
        input_output_aliases={5: 0, 6: 1},
        compiler_params=params,
        cost_estimate=cost(800, 2),
        name="apply_inner",
    )(splats, basis, eps, table, sz, h, packed, xadd, yadd)
    devices = lax.axis_size("gx") * lax.axis_size("gy") * lax.axis_size("gz")
    left, gram, _, hxf, hyf = pl.pallas_call(
        outer_kernel,
        out_shape=(whole, f32(devices, 4, ny), whole, face, f32(*yf_shape)),
        in_specs=[VMEM] * 14,
        out_specs=(VMEM,) * 5,
        input_output_aliases={11: 0, 5: 2, 9: 3},
        compiler_params=params,
        cost_estimate=cost(300, 1),
        name="apply_outer",
    )(splats, basis, eps, table, sz, h, zf, xf, yt, hxf, packed, left, acc, before)
    gram, hxf, hyf = lax.optimization_barrier((gram, hxf, hyf))
    rows = lax.all_to_all(gram, ("gx", "gy", "gz"), 0, 0)
    from_x = passed_round(hxf, "gx", 1)
    from_y = passed_round(hyf, "gy", 1)
    free = pl.CostEstimate(flops=0, bytes_accessed=0, transcendentals=0)
    left, residual = pl.pallas_call(
        rim_y_kernel,
        out_shape=(whole, whole),
        in_specs=[VMEM] * 3,
        out_specs=(VMEM, HBM),
        scratch_shapes=[scratch(nz, nx, ny), pltpu.SemaphoreType.DMA((3, nz))],
        input_output_aliases={1: 0},
        compiler_params=params,
        cost_estimate=free,
        name="add_y_rims",
    )(splats, left, from_y)
    _, residual = pl.pallas_call(
        rim_x_kernel,
        out_shape=(whole, whole),
        in_specs=[VMEM, VMEM, HBM, VMEM],
        out_specs=(VMEM, HBM),
        scratch_shapes=[scratch(*xf_shape), pltpu.SemaphoreType.DMA((nz,))],
        input_output_aliases={1: 0, 2: 1},
        compiler_params=params,
        cost_estimate=free,
        name="add_x_rims",
    )(splats, left, residual, from_x)
    rows, residual = lax.optimization_barrier((rows, residual))
    gram = pl.pallas_call(
        gather_kernel,
        out_shape=f32(2, vectors, vectors),
        in_specs=[VMEM],
        out_specs=VMEM,
        compiler_params=params,
        name="sum_rows",
    )(rows)
    return basis_new, residual, gram


def solution(mesh):
    in_specs = (P(None, None, None, "gz", "gx", "gy"), P("gz", "gx", "gy"), P(), P(), P(), P(), P())
    out_specs = (P(None, None, None, "gz", "gx", "gy"), P(None, None, None, "gz", "gx", "gy"), P())
    return jax.shard_map(body, mesh=mesh, in_specs=in_specs, out_specs=out_specs, check_vma=False)
```

```python
import functools

import jax
import jax.numpy as jnp
from jax import lax
from jax.experimental import pallas as pl
from jax.experimental.pallas import tpu as pltpu
from jax.sharding import PartitionSpec as P

OMEGA_SQ = 0.36
SIGMA_TOP = 3.0
BOUNDS = ((4, 5), (0, 1), (2, 3))
AXES = ("gz", "gx", "gy")

VMEM = pl.BlockSpec(memory_space=pltpu.VMEM)
HBM = pl.BlockSpec(memory_space=pltpu.HBM)


def passed_round(value, axis, steps):
    count = lax.axis_size(axis)
    return lax.ppermute(value, axis, [(source, (source + steps) % count) for source in range(count)])


def inverse_stretch(places, length, low_width, high_width):
    inside_depth = jnp.clip((low_width - places) / low_width, 0.0, 1.0) + jnp.clip(
        (places + 1.0 - length + high_width) / high_width, 0.0, 1.0
    )
    absorb = SIGMA_TOP * inside_depth * inside_depth
    scaled = 1.0 / (1.0 + absorb * absorb)
    return scaled, -absorb * scaled


def tree_sum(values):
    while len(values) > 1:
        pairs = [values[place] + values[place + 1] for place in range(0, len(values) - 1, 2)]
        values = pairs + ([values[-1]] if len(values) % 2 else [])
    return values[0]


def cmul(left, right):
    return (left[0] * right[0] - left[1] * right[1], left[0] * right[1] + left[1] * right[0])


def add(left, right):
    return (left[0] + right[0], left[1] + right[1])


def sub(left, right):
    return (left[0] - right[0], left[1] - right[1])


def axis_stretch(pml_ref, direction, count, places):
    total = count * lax.axis_size(AXES[direction])
    low_slot, high_slot = BOUNDS[direction]
    low, high = (
        jnp.broadcast_to(pml_ref[0:1, slot:slot + 1].astype(jnp.float32), places.shape) for slot in (low_slot, high_slot)
    )
    return inverse_stretch(places, jnp.float32(total), low, high)


def local_places(direction, count, shape, dim):
    start = lax.axis_index(AXES[direction]) * count
    return (lax.broadcasted_iota(jnp.int32, shape, dim) + start).astype(jnp.float32)


def one_place(direction, count, offset, shape):
    start = lax.axis_index(AXES[direction]) * count + offset
    return jnp.full(shape, start, jnp.int32).astype(jnp.float32)


def packed_row(slot, part, vector, vectors):
    return (slot * 2 + part) * vectors + vector


def has_neighbour(direction, steps):
    place = lax.axis_index(AXES[direction]) + steps
    inside = (place >= 0) & (place < lax.axis_size(AXES[direction]))
    return jnp.where(inside, 1.0, 0.0).astype(jnp.float32)


def face_kernel(fields_hbm, fields_ref, xf_ref, yf_ref, sems):
    _, vectors, _, nz, nx, ny = fields_ref.shape
    lanes = lax.broadcasted_iota(jnp.int32, (nx, ny), 1)
    copies = [
        pltpu.make_async_copy(fields_hbm.at[part, :, comp], fields_ref.at[part, :, comp], sems.at[part, comp])
        for comp in (0, 2, 1) for part in range(2)
    ]
    for copy in copies:
        copy.start()
    packed = [jnp.zeros((nx, ny), jnp.float32)] * nz
    for place, comp in enumerate((0, 2)):
        for part in range(2):
            copies[2 * place + part].wait()
            for a in range(vectors):
                row = packed_row(comp // 2, part, a, vectors)
                for z in range(nz):
                    value = fields_ref[part, a, comp, z]
                    packed[z] = jnp.where(lanes == row, pltpu.roll(value, row, 1) if row else value, packed[z])
    turned = jnp.concatenate(packed, axis=0).T
    yf_ref[...] = turned[:yf_ref.shape[0]]
    for part in range(2):
        for a in range(vectors):
            xf_ref[part, a, 1] = fields_ref[part, a, 2, :, 0, :]
    for part in range(2):
        copies[4 + part].wait()
        for a in range(vectors):
            xf_ref[part, a, 0] = fields_ref[part, a, 1, :, 0, :]


def rotated(coeffs_ref, old, b):
    new = None
    for a, value in enumerate(old):
        term = cmul((coeffs_ref[0, a, b], coeffs_ref[1, a, b]), value)
        new = term if new is None else add(new, term)
    return new


SUB = 8
SHX, SEX, SHY, SEY = range(0, 8, 2)


class Splats:
    def __init__(self, ref, first, shape):
        self.ref, self.first, self.shape = ref, first, shape

    def __getitem__(self, place):
        row = 0
        for index, size in zip(place, self.shape):
            row = row * size + index
        return self.ref[self.first + row:self.first + row + 1]


ENDS = ("under", "next_x", "next_y", "first_x", "first_y", "last_x", "last_y")


def end_value(splat_ref, name, width=None):
    row = 2 * ENDS.index(name)
    return tuple(splat_ref[row + part:row + part + 1, :width] for part in range(2))


def ritz_rows(splat_ref, vectors):
    return Splats(splat_ref, 2 * len(ENDS), (2, vectors))


def coeff_rows(splat_ref, vectors):
    return Splats(splat_ref, 2 * len(ENDS) + 2 * vectors, (2, vectors, vectors))


def mixed_rows(splat_ref, vectors):
    return Splats(splat_ref, 2 * len(ENDS) + 2 * vectors * (vectors + 1), (2, vectors, vectors))


def splat_count(vectors):
    return -(-(2 * len(ENDS) + 2 * vectors * (2 * vectors + 1)) // SUB) * SUB


def field_of(ref, b, comp, z, cut):
    return tuple(ref[part, b, comp, z, cut] for part in range(2))


def tiles_of(nx):
    return [slice(SUB * t, SUB * (t + 1)) for t in range(nx // SUB)]


def prepare_kernel(
    pml_ref, eps_real_ref, eps_loss_ref, coeffs_ref, ritz_ref, fields_ref, material_ref,
    basis_ref, eps_ref, h_ref, packed_ref, table_ref, sz_ref, splat_ref,
):
    _, vectors, _, nz, nx, ny = fields_ref.shape
    plane = (nx, ny)
    parts = range(2)
    for slot, direction, half, count, dim in (
        (SHX, 1, 0.5, nx, 0), (SEX, 1, 0.0, nx, 0), (SHY, 2, 0.5, ny, 1), (SEY, 2, 0.0, ny, 1),
    ):
        values = axis_stretch(pml_ref, direction, count, local_places(direction, count, plane, dim) + half)
        for part in parts:
            table_ref[slot + part] = values[part]
    line = (1, ny)
    ends = {
        "under": (0, nz, -1, 0.5, 1.0),
        "next_x": (1, nx, nx, 0.0, 1.0),
        "next_y": (2, ny, ny, 0.0, 1.0),
        "first_x": (1, nx, 0, 0.0, has_neighbour(1, -1)),
        "first_y": (2, ny, 0, 0.0, has_neighbour(2, -1)),
        "last_x": (1, nx, nx - 1, 0.5, 1.0),
        "last_y": (2, ny, ny - 1, 0.5, 1.0),
    }
    lines = []
    for name in ENDS:
        direction, count, offset, half, factor = ends[name]
        values = axis_stretch(pml_ref, direction, count, one_place(direction, count, offset, line) + half)
        lines += [value * factor for value in values]
    lines += [
        jnp.broadcast_to(ritz_ref[part:part + 1, b:b + 1], line) for part in parts for b in range(vectors)
    ]
    real, imag = (
        [
            jnp.broadcast_to(coeffs_ref[part, a:a + 1, b:b + 1], line)
            for a in range(vectors) for b in range(vectors)
        ]
        for part in parts
    )
    lines += real + imag
    lines += [second + first for first, second in zip(real, imag)] + [second - first for first, second in zip(real, imag)]
    for row, value in enumerate(lines):
        splat_ref[row:row + 1] = value
    splat_ref[len(lines):] = jnp.zeros((splat_ref.shape[0] - len(lines), ny), jnp.float32)
    for slot, half in ((0, 0.0), (2, 0.5)):
        values = axis_stretch(pml_ref, 0, nz, local_places(0, nz, (nz, ny), 0) + half)
        for part in parts:
            sz_ref[slot + part] = values[part]

    coeffs, mixed = coeff_rows(splat_ref, vectors), mixed_rows(splat_ref, vectors)
    choices = [
        [jnp.broadcast_to(-OMEGA_SQ * source[0:1, number:number + 1], plane) for number in range(source.shape[1])]
        for source in (eps_real_ref, eps_loss_ref)
    ]

    @pl.loop(0, nz)
    def _(z):
        material = material_ref[z]
        for part in parts:
            value = jnp.zeros(plane, jnp.float32)
            for number, choice in enumerate(choices[part]):
                value = jnp.where(material == number, choice, value)
            eps_ref[part, z] = value
        for comp in range(3):
            real = [fields_ref[0, a, comp, z] for a in range(vectors)]
            imag = [fields_ref[1, a, comp, z] for a in range(vectors)]
            both = [first + second for first, second in zip(real, imag)]
            for b in range(vectors):
                shared = tree_sum([coeffs[0, a, b] * both[a] for a in range(vectors)])
                less = tree_sum([mixed[0, a, b] * imag[a] for a in range(vectors)])
                more = tree_sum([mixed[1, a, b] * real[a] for a in range(vectors)])
                basis_ref[0, b, comp, z] = shared - less
                basis_ref[1, b, comp, z] = shared + more
        packed_ref[z] = jnp.zeros(plane, jnp.float32)

    tile = (SUB, ny)
    rows = lax.broadcasted_iota(jnp.int32, tile, 0)
    lanes = lax.broadcasted_iota(jnp.int32, tile, 1)
    cuts = tiles_of(nx)

    def magnetic(b, z, last):
        shz = tuple(sz_ref[2 + part, pl.ds(z, 1)] for part in parts)
        for cut in cuts:
            u = [field_of(basis_ref, b, comp, z, cut) for comp in range(3)]

            def step_z(comp):
                if last:
                    return tuple(-value for value in u[comp])
                return sub(field_of(basis_ref, b, comp, z + 1, cut), u[comp])

            def step_x(comp):
                if cut.stop < nx:
                    ahead = field_of(basis_ref, b, comp, z, slice(cut.start + 1, cut.stop + 1))
                else:
                    ahead = tuple(jnp.where(rows == SUB - 1, 0.0, pltpu.roll(value, SUB - 1, 0)) for value in u[comp])
                return sub(ahead, u[comp])

            def step_y(comp):
                ahead = tuple(jnp.where(lanes == ny - 1, 0.0, pltpu.roll(value, ny - 1, 1)) for value in u[comp])
                return sub(ahead, u[comp])

            shx = tuple(table_ref[SHX + part, cut] for part in parts)
            shy = tuple(table_ref[SHY + part, cut] for part in parts)
            h = (
                sub(cmul(shy, step_y(2)), cmul(shz, step_z(1))),
                sub(cmul(shz, step_z(0)), cmul(shx, step_x(2))),
                sub(cmul(shx, step_x(1)), cmul(shy, step_y(0))),
            )
            for comp in range(3):
                for part in parts:
                    h_ref[part, b, comp, z, cut] = h[comp][part]
            packed = packed_ref[z, cut]
            for slot, value in enumerate((h[2], h[0])):
                for part in parts:
                    row = packed_row(slot, part, b, vectors)
                    packed = jnp.where(lanes == row, pltpu.roll(value[part], (row + 1) % ny, 1), packed)
            packed_ref[z, cut] = packed

    @pl.loop(0, nz - 1)
    def _(z):
        for b in range(vectors):
            magnetic(b, z, False)

    for b in range(vectors):
        magnetic(b, nz - 1, True)


def turn_face(coeffs_ref, direction, raw_ref, face_ref):
    inside = has_neighbour(direction, 1)
    vectors = raw_ref.shape[1]
    for slot in range(2):
        old = [(raw_ref[0, a, slot] * inside, raw_ref[1, a, slot] * inside) for a in range(vectors)]
        for b in range(vectors):
            new = rotated(coeffs_ref, old, b)
            for part in range(2):
                face_ref[part, b, slot] = new[part]


def turn_column(coeffs_ref, raw_ref, rows_ref):
    vectors = coeffs_ref.shape[1]
    inside = has_neighbour(2, 1)
    both = 2 * vectors
    shape = (both, raw_ref.shape[1])
    which = lax.broadcasted_iota(jnp.int32, shape, 0)
    turned = [jnp.zeros(shape, jnp.float32)] * 2
    for part in range(2):
        for a in range(vectors):
            column = jnp.zeros(shape, jnp.float32)
            for b in range(vectors):
                first, second = (coeffs_ref[0, a, b] * inside)[:, :shape[1]], (coeffs_ref[1, a, b] * inside)[:, :shape[1]]
                if part:
                    first, second = -second, first
                column = jnp.where(which == b, first, column)
                column = jnp.where(which == vectors + b, second, column)
            for slot in range(2):
                row = packed_row(slot, part, a, vectors)
                turned[slot] = turned[slot] + column * raw_ref[row:row + 1]
    for slot in range(2):
        rows_ref[slot * both:(slot + 1) * both] = turned[slot]


def lane_to_last(values, slot, part, b, vectors):
    ny = values.shape[-1]
    lanes = lax.broadcasted_iota(jnp.int32, values.shape, 1)
    row = packed_row(slot, part, b, vectors)
    return jnp.where(lanes == ny - 1, pltpu.roll(values, ny - 1 - row, 1), 0.0)


def with_halos(h, b, z, cut, nx, xadd_ref, yadd_ref):
    vectors = xadd_ref.shape[1]
    column = yadd_ref[z, cut]
    hx = tuple(h[0][part] + lane_to_last(column, 1, part, b, vectors) for part in range(2))
    hz = tuple(h[2][part] + lane_to_last(column, 0, part, b, vectors) for part in range(2))
    hy = h[1]
    if cut.stop == nx:
        rows = lax.broadcasted_iota(jnp.int32, column.shape, 0)

        def row_of(slot):
            return tuple(
                jnp.where(rows == SUB - 1, xadd_ref[part, b, slot, pl.ds(z, 1)], 0.0) for part in range(2)
            )

        hy, hz = add(hy, row_of(0)), add(hz, row_of(1))
    return hx, hy, hz


def slab_kernel(
    splat_ref, basis_ref, h_in, raw_xf_ref, raw_yf_ref,
    h_ref, xf_ref, yt_ref, xadd_ref, yadd_ref, zf_ref,
):
    del h_in
    _, vectors, _, nz, nx, ny = basis_ref.shape
    parts = range(2)
    cells = nz * nx
    both = 2 * vectors
    coeffs = coeff_rows(splat_ref, vectors)
    turn_face(coeffs, 1, raw_xf_ref, xf_ref)
    turn_column(coeffs, raw_yf_ref, yt_ref)
    shx = end_value(splat_ref, "last_x")
    shy = end_value(splat_ref, "last_y", cells)
    for b in range(vectors):
        for slot in range(2):
            value = cmul(shx, tuple(xf_ref[part, b, 1 - slot] for part in parts))
            for part in parts:
                xadd_ref[part, b, slot] = value[part] if slot else -value[part]
    added = []
    for slot in range(2):
        value = cmul(shy, (yt_ref[slot * both:slot * both + vectors], yt_ref[slot * both + vectors:(slot + 1) * both]))
        added += [part if slot else -part for part in value]
    rest = jnp.zeros((ny - 2 * both, cells), jnp.float32)
    yadd_ref[...] = jnp.concatenate(added + [rest], axis=0).T.reshape(nz, nx, ny)
    last = nz - 1
    lower = jnp.full((SUB, ny), lax.axis_index(AXES[0]), jnp.int32) == 0
    for b in range(vectors):
        for cut in tiles_of(nx):
            h = [field_of(h_ref, b, comp, last, cut) for comp in range(3)]
            h = with_halos(h, b, last, cut, nx, xadd_ref, yadd_ref)
            for part in parts:
                for comp in range(3):
                    h_ref[part, b, comp, last, cut] = h[comp][part]
                for comp in range(2):
                    zf_ref[part, b, comp, cut] = jnp.where(lower, h[comp][part], basis_ref[part, b, comp, 0, cut])


def plane_step(
    b, z, before, sums, ritz_ref, basis_ref, eps_ref, table_ref, sz_ref, h_ref, left_ref, halos=None
):
    _, vectors, _, _, nx, ny = basis_ref.shape
    rows = lax.broadcasted_iota(jnp.int32, (SUB, ny), 0)
    lanes = lax.broadcasted_iota(jnp.int32, (SUB, ny), 1)
    parts = range(2)
    cuts = tiles_of(nx)
    sez = tuple(sz_ref[part, pl.ds(z, 1)] for part in parts)
    fields = []
    for cut in cuts:
        h = [field_of(h_ref, b, comp, z, cut) for comp in range(3)]
        if halos is not None:
            h = with_halos(h, b, z, cut, nx, *halos)
            for comp in (1, 2):
                for part in parts:
                    h_ref[part, b, comp, z, cut] = h[comp][part]
        fields.append(h)
    sums = list(sums)
    for t, cut in enumerate(cuts):
        hx, hy, hz = fields[t]

        def back_x(comp):
            here = fields[t][comp]
            if t:
                past = field_of(h_ref, b, comp, z, slice(cut.start - 1, cut.stop - 1))
            else:
                past = tuple(jnp.where(rows == 0, 0.0, pltpu.roll(value, 1, 0)) for value in here)
            return sub(here, past)

        def back_y(value):
            return sub(value, tuple(jnp.where(lanes == 0, 0.0, pltpu.roll(part, 1, 1)) for part in value))

        sex = tuple(table_ref[SEX + part, cut] for part in parts)
        sey = tuple(table_ref[SEY + part, cut] for part in parts)
        bxy, bxz = (cmul(sex, back_x(comp)) for comp in (1, 2))
        byz, byx = (cmul(sey, back_y(value)) for value in (hz, hx))
        bzx, bzy = (cmul(sez, sub(value, past)) for value, past in zip((hx, hy), before[t]))
        curl = (sub(byz, bzy), sub(bzx, bxz), sub(bxy, byx))
        u = [field_of(basis_ref, b, comp, z, cut) for comp in range(3)]
        eps = tuple(eps_ref[part, z, cut] for part in parts)
        w = [add(curl[comp], cmul(eps, u[comp])) for comp in range(3)]
        for comp in range(3):
            left = sub(w[comp], cmul((ritz_ref[0, b], ritz_ref[1, b]), u[comp]))
            for part in parts:
                left_ref[part, b, comp, z, cut] = left[part]
        for a in range(vectors):
            total = sums[a]
            for comp in range(3):
                total = add(total, cmul(field_of(basis_ref, a, comp, z, cut), w[comp]))
            sums[a] = total
    return [(h[0], h[1]) for h in fields], sums


def inner_kernel(
    splat_ref, basis_ref, eps_ref, table_ref, sz_ref, h_in, packed_in, xadd_ref, yadd_ref,
    h_ref, packed_ref, left_ref, acc_ref, before_ref, hxf_ref, basis_hbm, sem,
):
    del h_in, packed_in
    _, vectors, _, nz, nx, ny = basis_ref.shape
    keep = pltpu.make_async_copy(basis_ref, basis_hbm, sem)
    keep.start()
    cuts = tiles_of(nx)
    lanes = lax.broadcasted_iota(jnp.int32, (nz, ny), 1)
    open_plane = lax.broadcasted_iota(jnp.int32, (nz, ny), 0) < nz - 1
    packed_ref[...] = packed_ref[...] + yadd_ref[...]
    corner = packed_ref[:, nx - 1, :]
    for b in range(vectors):
        for part in range(2):
            row = packed_row(0, part, b, vectors)
            more = xadd_ref[part, b, 1]
            corner = corner + jnp.where(lanes == row, pltpu.roll(more, (row + 1) % ny, 1), 0.0)
            more = more + lane_to_last(yadd_ref[:, nx - 1, :], 0, part, b, vectors)
            hxf_ref[part, b, 0] = h_ref[part, b, 1, :, nx - 1, :] + jnp.where(open_plane, xadd_ref[part, b, 0], 0.0)
            hxf_ref[part, b, 1] = h_ref[part, b, 2, :, nx - 1, :] + jnp.where(open_plane, more, 0.0)
    packed_ref[:, nx - 1, :] = corner
    acc_ref[...] = jnp.zeros(acc_ref.shape, jnp.float32)
    before_ref[...] = jnp.zeros(before_ref.shape, jnp.float32)

    @pl.loop(0, nz - 1)
    def _(z):
        for b in range(vectors):
            before = [
                tuple(tuple(before_ref[part, b, slot, cut] for part in range(2)) for slot in range(2)) for cut in cuts
            ]
            sums = [(acc_ref[b, a], acc_ref[b, vectors + a]) for a in range(vectors)]
            before, sums = plane_step(
                b, z, before, sums, ritz_rows(splat_ref, vectors), basis_ref, eps_ref, table_ref, sz_ref, h_ref, left_ref, (xadd_ref, yadd_ref)
            )
            for part in range(2):
                for a in range(vectors):
                    acc_ref[b, part * vectors + a] = sums[a][part]
                for t, cut in enumerate(cuts):
                    for slot in range(2):
                        before_ref[part, b, slot, cut] = before[t][slot][part]

    keep.wait()


def close_last_plane(sz_ref, zf_ref, packed_in, h_ref, hxf_ref, hyf_ref):
    _, vectors, _, nz, nx, ny = h_ref.shape
    parts = range(2)
    last = nz - 1
    lanes = lax.broadcasted_iota(jnp.int32, (SUB, ny), 1)
    shz = tuple(sz_ref[2 + part, last:] * has_neighbour(0, 1) for part in parts)
    packed = [packed_in[last, cut] for cut in tiles_of(nx)]
    for b in range(vectors):
        for t, cut in enumerate(tiles_of(nx)):
            ex, ey = (tuple(zf_ref[part, b, slot, cut] for part in parts) for slot in range(2))
            more = (tuple(-value for value in cmul(shz, ey)), cmul(shz, ex))
            for part in parts:
                for comp in range(2):
                    h_ref[part, b, comp, last, cut] = h_ref[part, b, comp, last, cut] + more[comp][part]
                row = packed_row(1, part, b, vectors)
                edge = pltpu.roll(more[0][part], (row + 1) % ny, 1)
                packed[t] = packed[t] + jnp.where(lanes == row, edge, 0.0)
                if cut.stop == nx:
                    hxf_ref[part, b, 0, last:] = hxf_ref[part, b, 0, last:] + more[1][part][SUB - 1:]
    inner = packed_in[:last].reshape(last * nx, ny)
    hyf_ref[...] = jnp.concatenate([inner] + packed, axis=0).T[:hyf_ref.shape[0]]


def outer_kernel(
    splat_ref, basis_ref, eps_ref, table_ref, sz_ref, h_in, zf_ref, xf_ref, yt_ref, hxf_in, packed_in,
    left_in, acc_ref, before_ref, left_ref, gram_ref, h_ref, hxf_ref, hyf_ref,
):
    del left_in, h_in, hxf_in
    close_last_plane(sz_ref, zf_ref, packed_in, h_ref, hxf_ref, hyf_ref)
    _, vectors, _, nz, nx, ny = basis_ref.shape
    parts = range(2)
    cuts = tiles_of(nx)
    under = end_value(splat_ref, "under")
    sez = tuple(sz_ref[part, 0:1] * has_neighbour(0, -1) for part in parts)
    sx_next = end_value(splat_ref, "next_x")
    sy_next = end_value(splat_ref, "next_y", nz * nx)
    both = 2 * vectors
    ends = [
        cmul(sy_next, (yt_ref[slot * both:slot * both + vectors], yt_ref[slot * both + vectors:(slot + 1) * both]))
        for slot in range(2)
    ]
    columns = lax.broadcasted_iota(jnp.int32, (both, ny), 1)
    gram = jnp.zeros((both, ny), jnp.float32)
    for b in range(vectors):

        def tile_of(ref, slot, cut, b=b):
            return tuple(ref[part, b, slot, cut] for part in parts)

        before = [tuple(tile_of(before_ref, slot, cut) for slot in range(2)) for cut in cuts]
        sums = [(acc_ref[b, a], acc_ref[b, vectors + a]) for a in range(vectors)]
        _, sums = plane_step(
            b, nz - 1, before, sums, ritz_rows(splat_ref, vectors), basis_ref, eps_ref, table_ref, sz_ref, h_ref, left_ref
        )
        for cut in cuts:
            ex, ey = (field_of(basis_ref, b, comp, 0, cut) for comp in range(2))
            hx = sub(tile_of(zf_ref, 0, cut), cmul(under, ey))
            hy = add(tile_of(zf_ref, 1, cut), cmul(under, ex))
            more = (cmul(sez, hy), cmul(sez, hx))
            for part in parts:
                left_ref[part, b, 0, 0, cut] = left_ref[part, b, 0, 0, cut] + more[0][part]
                left_ref[part, b, 1, 0, cut] = left_ref[part, b, 1, 0, cut] - more[1][part]
            for a in range(vectors):
                ex, ey = (field_of(basis_ref, a, comp, 0, cut) for comp in range(2))
                sums[a] = add(sums[a], sub(cmul(ex, more[0]), cmul(ey, more[1])))
        h_y = tuple(hxf_ref[part, b, 0] for part in parts)
        h_z = tuple(hxf_ref[part, b, 1] for part in parts)
        for a in range(vectors):
            over = cmul(tuple(xf_ref[part, a, 0] for part in parts), h_z)
            over = sub(over, cmul(tuple(xf_ref[part, a, 1] for part in parts), h_y))
            over = cmul(sx_next, over)
            for row in range(0, nz, SUB):
                sums[a] = add(sums[a], tuple(part[row:row + SUB] for part in over))
        flat = jnp.concatenate(
            [jnp.sum(sums[a][part], axis=0, keepdims=True) for part in parts for a in range(vectors)], axis=0
        )
        over = None
        for slot in range(2):
            h = tuple(hyf_ref[packed_row(slot, part, b, vectors)][None] for part in parts)
            term = cmul(ends[slot], h)
            over = term if over is None else sub(term, over)
        side = jnp.concatenate(over, axis=0)
        total = jnp.sum(flat, axis=1, keepdims=True) + jnp.sum(side, axis=1, keepdims=True)
        gram = jnp.where(columns == b, total, gram)
    everywhere = 3.0 * nz * nx * ny
    for axis in AXES:
        everywhere = everywhere * lax.axis_size(axis)
    gram = gram * (1.0 / everywhere)
    row = tree_sum([gram[0:1]] + [pltpu.roll(gram[row:row + 1], row * vectors, 1) for row in range(1, both)])
    block = jnp.concatenate([row, jnp.zeros((gram_ref.shape[1] - 1, ny), jnp.float32)], axis=0)
    for device in range(gram_ref.shape[0]):
        gram_ref[device] = block


def gather_kernel(rows_ref, gram_ref):
    vectors = gram_ref.shape[1]
    total = tree_sum([rows_ref[device] for device in range(rows_ref.shape[0])])[0:1]
    count = total.shape[1]
    for part in range(2):
        for a in range(vectors):
            row = (part * vectors + a) * vectors
            turned = pltpu.roll(total, count - row, 1) if row else total
            gram_ref[part, a:a + 1] = turned[:, :vectors]


def rim_y_kernel(splat_ref, left_in, hyf_ref, left_ref, residual_hbm, yadd_ref, sems):
    del left_in
    _, vectors, _, nz, nx, ny = left_ref.shape
    parts = range(2)
    both = 2 * vectors
    sey = end_value(splat_ref, "first_y", nz * nx)
    added = []
    for slot in range(2):
        first = slot * both
        value = cmul(sey, (hyf_ref[first:first + vectors], hyf_ref[first + vectors:first + both]))
        added += [part if slot else -part for part in value]
    rest = jnp.zeros((ny - 2 * both, nz * nx), jnp.float32)
    yadd_ref[...] = jnp.concatenate(added + [rest], axis=0).T.reshape(nz, nx, ny)
    lanes = lax.broadcasted_iota(jnp.int32, (SUB, ny), 1)

    def kept(z):
        blocks = [(slice(None), slice(None), 0, z)]
        blocks += [(slice(None), slice(None), comp, z, slice(SUB, nx)) for comp in (1, 2)]
        return [
            pltpu.make_async_copy(left_ref.at[block], residual_hbm.at[block], sems.at[place, z])
            for place, block in enumerate(blocks)
        ]

    @pl.loop(0, nz)
    def _(z):
        for cut in tiles_of(nx):
            column = yadd_ref[z, cut]
            for b in range(vectors):
                for part in parts:
                    for slot, comp in enumerate((0, 2)):
                        row = packed_row(slot, part, b, vectors)
                        value = pltpu.roll(column, ny - row, 1) if row else column
                        value = jnp.where(lanes == 0, value, 0.0)
                        left_ref[part, b, comp, z, cut] = left_ref[part, b, comp, z, cut] + value
        for copy in kept(z):
            copy.start()

    @pl.loop(0, nz)
    def _(z):
        for copy in kept(z):
            copy.wait()


def rim_x_kernel(splat_ref, left_in, residual_in, hxf_ref, left_ref, residual_hbm, xadd_ref, sems):
    del left_in, residual_in
    _, vectors, _, nz, nx, ny = left_ref.shape
    parts = range(2)
    sex = end_value(splat_ref, "first_x")
    for b in range(vectors):
        for slot in range(2):
            value = cmul(sex, tuple(hxf_ref[part, b, slot] for part in parts))
            for part in parts:
                xadd_ref[part, b, slot] = value[part] if slot else -value[part]
    rows = lax.broadcasted_iota(jnp.int32, (SUB, ny), 0)
    first = slice(0, SUB)
    copies = []
    for z in range(nz):
        for b in range(vectors):
            for part in parts:
                for slot, comp in ((1, 1), (0, 2)):
                    value = jnp.where(rows == 0, xadd_ref[part, b, slot, z:z + 1], 0.0)
                    left_ref[part, b, comp, z, first] = left_ref[part, b, comp, z, first] + value
        block = (slice(None), slice(None), slice(1, 3), z, first)
        copies.append(pltpu.make_async_copy(left_ref.at[block], residual_hbm.at[block], sems.at[z]))
        copies[-1].start()
    for copy in copies:
        copy.wait()


def body(fields, material, pml_width, eps_real, eps_loss, coeffs, ritz):
    _, vectors, _, nz, nx, ny = fields.shape
    f32 = lambda *shape: jax.ShapeDtypeStruct(shape, jnp.float32)
    scratch = lambda *shape: pltpu.VMEM(shape, jnp.float32)
    params = pltpu.CompilerParams(vmem_limit_bytes=40 * 1024 * 1024)
    whole = f32(*fields.shape)
    zf_shape = (2, vectors, 2, nx, ny)
    xf_shape = (2, vectors, 2, nz, ny)
    yf_shape = (4 * vectors, nz * nx)
    near, xf, yf = pl.pallas_call(
        face_kernel,
        out_shape=(whole, f32(*xf_shape), f32(*yf_shape)),
        in_specs=[HBM],
        out_specs=(VMEM,) * 3,
        scratch_shapes=[pltpu.SemaphoreType.DMA((2, 3))],
        compiler_params=params,
        name="take_faces",
    )(pltpu.with_memory_space_constraint(fields, pltpu.HBM))
    xf = passed_round(xf, "gx", -1)
    yf = passed_round(yf, "gy", -1)
    cells = fields.size // 6 // vectors

    def cost(flops, passes):
        return pl.CostEstimate(flops=flops * cells, bytes_accessed=passes * 4 * fields.size, transcendentals=0)

    planes = f32(nz, nx, ny)
    face = f32(*xf_shape)
    basis, eps, h, packed, table, sz, splats = pl.pallas_call(
        prepare_kernel,
        out_shape=(whole, f32(2, nz, nx, ny), whole, planes, f32(8, nx, ny), f32(4, nz, ny), f32(splat_count(vectors), ny)),
        in_specs=[VMEM] * 7,
        out_specs=(VMEM,) * 7,
        compiler_params=params,
        cost_estimate=cost(800, 4),
        name="prepare",
    )(pml_width[None], eps_real[None], eps_loss[None], coeffs, ritz, near, material)
    h, xf, yt, xadd, yadd, zf = pl.pallas_call(
        slab_kernel,
        out_shape=(whole, face, f32(*yf_shape), face, planes, f32(*zf_shape)),
        in_specs=[VMEM] * 5,
        out_specs=(VMEM,) * 6,
        input_output_aliases={2: 0},
        compiler_params=params,
        name="slab_face",
    )(splats, basis, h, xf, yf)
    zf = passed_round(zf, "gz", 1)
    h, packed, left, acc, before, hxf, basis_new = pl.pallas_call(
        inner_kernel,
        out_shape=(whole, planes, whole, f32(vectors, 2 * vectors, SUB, ny), f32(*zf_shape), face, whole),
        in_specs=[VMEM] * 9,
        out_specs=(VMEM,) * 6 + (HBM,),
        scratch_shapes=[pltpu.SemaphoreType.DMA],
        input_output_aliases={5: 0, 6: 1},
        compiler_params=params,
        cost_estimate=cost(800, 2),
        name="apply_inner",
    )(splats, basis, eps, table, sz, h, packed, xadd, yadd)
    devices = lax.axis_size("gx") * lax.axis_size("gy") * lax.axis_size("gz")
    left, gram, _, hxf, hyf = pl.pallas_call(
        outer_kernel,
        out_shape=(whole, f32(devices, 4, ny), whole, face, f32(*yf_shape)),
        in_specs=[VMEM] * 14,
        out_specs=(VMEM,) * 5,
        input_output_aliases={11: 0, 5: 2, 9: 3},
        compiler_params=params,
        cost_estimate=cost(300, 1),
        name="apply_outer",
    )(splats, basis, eps, table, sz, h, zf, xf, yt, hxf, packed, left, acc, before)
    gram, hxf, hyf = lax.optimization_barrier((gram, hxf, hyf))
    rows = lax.all_to_all(gram, ("gx", "gy", "gz"), 0, 0)
    from_x = passed_round(hxf, "gx", 1)
    from_y = passed_round(hyf, "gy", 1)
    free = pl.CostEstimate(flops=0, bytes_accessed=0, transcendentals=0)
    left, residual = pl.pallas_call(
        rim_y_kernel,
        out_shape=(whole, whole),
        in_specs=[VMEM] * 3,
        out_specs=(VMEM, HBM),
        scratch_shapes=[scratch(nz, nx, ny), pltpu.SemaphoreType.DMA((3, nz))],
        input_output_aliases={1: 0},
        compiler_params=params,
        cost_estimate=free,
        name="add_y_rims",
    )(splats, left, from_y)
    _, residual = pl.pallas_call(
        rim_x_kernel,
        out_shape=(whole, whole),
        in_specs=[VMEM, VMEM, HBM, VMEM],
        out_specs=(VMEM, HBM),
        scratch_shapes=[scratch(*xf_shape), pltpu.SemaphoreType.DMA((nz,))],
        input_output_aliases={1: 0, 2: 1},
        compiler_params=params,
        cost_estimate=free,
        name="add_x_rims",
    )(splats, left, residual, from_x)
    rows, residual = lax.optimization_barrier((rows, residual))
    gram = pl.pallas_call(
        gather_kernel,
        out_shape=f32(2, vectors, vectors),
        in_specs=[VMEM],
        out_specs=VMEM,
        compiler_params=params,
        name="sum_rows",
    )(rows)
    return basis_new, residual, gram


def solution(mesh):
    in_specs = (P(None, None, None, "gz", "gx", "gy"), P("gz", "gx", "gy"), P(), P(), P(), P(), P())
    out_specs = (P(None, None, None, "gz", "gx", "gy"), P(None, None, None, "gz", "gx", "gy"), P())
    return jax.shard_map(body, mesh=mesh, in_specs=in_specs, out_specs=out_specs, check_vma=False)
```

```python
import functools

import jax
import jax.numpy as jnp
from jax import lax
from jax.experimental import pallas as pl
from jax.experimental.pallas import tpu as pltpu
from jax.sharding import PartitionSpec as P

OMEGA_SQ = 0.36
SIGMA_TOP = 3.0
BOUNDS = ((4, 5), (0, 1), (2, 3))
AXES = ("gz", "gx", "gy")

VMEM = pl.BlockSpec(memory_space=pltpu.VMEM)
HBM = pl.BlockSpec(memory_space=pltpu.HBM)


def passed_round(value, axis, steps):
    count = lax.axis_size(axis)
    return lax.ppermute(value, axis, [(source, (source + steps) % count) for source in range(count)])


def inverse_stretch(places, length, low_width, high_width):
    inside_depth = jnp.clip((low_width - places) / low_width, 0.0, 1.0) + jnp.clip(
        (places + 1.0 - length + high_width) / high_width, 0.0, 1.0
    )
    absorb = SIGMA_TOP * inside_depth * inside_depth
    scaled = 1.0 / (1.0 + absorb * absorb)
    return scaled, -absorb * scaled


def tree_sum(values):
    while len(values) > 1:
        pairs = [values[place] + values[place + 1] for place in range(0, len(values) - 1, 2)]
        values = pairs + ([values[-1]] if len(values) % 2 else [])
    return values[0]


def cmul(left, right):
    return (left[0] * right[0] - left[1] * right[1], left[0] * right[1] + left[1] * right[0])


def add(left, right):
    return (left[0] + right[0], left[1] + right[1])


def sub(left, right):
    return (left[0] - right[0], left[1] - right[1])


def axis_stretch(pml_ref, direction, count, places):
    total = count * lax.axis_size(AXES[direction])
    low_slot, high_slot = BOUNDS[direction]
    low, high = (
        jnp.broadcast_to(pml_ref[0:1, slot:slot + 1].astype(jnp.float32), places.shape) for slot in (low_slot, high_slot)
    )
    return inverse_stretch(places, jnp.float32(total), low, high)


def local_places(direction, count, shape, dim):
    start = lax.axis_index(AXES[direction]) * count
    return (lax.broadcasted_iota(jnp.int32, shape, dim) + start).astype(jnp.float32)


def one_place(direction, count, offset, shape):
    start = lax.axis_index(AXES[direction]) * count + offset
    return jnp.full(shape, start, jnp.int32).astype(jnp.float32)


def packed_row(slot, part, vector, vectors):
    return (slot * 2 + part) * vectors + vector


def has_neighbour(direction, steps):
    place = lax.axis_index(AXES[direction]) + steps
    inside = (place >= 0) & (place < lax.axis_size(AXES[direction]))
    return jnp.where(inside, 1.0, 0.0).astype(jnp.float32)


def face_kernel(fields_hbm, fields_ref, xf_ref, yf_ref, sems):
    _, vectors, _, nz, nx, ny = fields_ref.shape
    lanes = lax.broadcasted_iota(jnp.int32, (nx, ny), 1)
    copies = [
        pltpu.make_async_copy(fields_hbm.at[part, :, comp], fields_ref.at[part, :, comp], sems.at[part, comp])
        for comp in (0, 2, 1) for part in range(2)
    ]
    for copy in copies:
        copy.start()
    packed = [jnp.zeros((nx, ny), jnp.float32)] * nz
    for place, comp in enumerate((0, 2)):
        for part in range(2):
            copies[2 * place + part].wait()
            for a in range(vectors):
                row = packed_row(comp // 2, part, a, vectors)
                for z in range(nz):
                    value = fields_ref[part, a, comp, z]
                    packed[z] = jnp.where(lanes == row, pltpu.roll(value, row, 1) if row else value, packed[z])
    turned = jnp.concatenate(packed, axis=0).T
    yf_ref[...] = turned[:yf_ref.shape[0]]
    for part in range(2):
        for a in range(vectors):
            xf_ref[part, a, 1] = fields_ref[part, a, 2, :, 0, :]
    for part in range(2):
        copies[4 + part].wait()
        for a in range(vectors):
            xf_ref[part, a, 0] = fields_ref[part, a, 1, :, 0, :]


def rotated(coeffs_ref, old, b):
    new = None
    for a, value in enumerate(old):
        term = cmul((coeffs_ref[0, a, b], coeffs_ref[1, a, b]), value)
        new = term if new is None else add(new, term)
    return new


SUB = 8
SHX, SEX, SHY, SEY = range(0, 8, 2)


class Splats:
    def __init__(self, ref, first, shape):
        self.ref, self.first, self.shape = ref, first, shape

    def __getitem__(self, place):
        row = 0
        for index, size in zip(place, self.shape):
            row = row * size + index
        return self.ref[self.first + row:self.first + row + 1]


ENDS = ("under", "next_x", "next_y", "first_x", "first_y", "last_x", "last_y")


def end_value(splat_ref, name, width=None):
    row = 2 * ENDS.index(name)
    return tuple(splat_ref[row + part:row + part + 1, :width] for part in range(2))


def ritz_rows(splat_ref, vectors):
    return Splats(splat_ref, 2 * len(ENDS), (2, vectors))


def coeff_rows(splat_ref, vectors):
    return Splats(splat_ref, 2 * len(ENDS) + 2 * vectors, (2, vectors, vectors))


def mixed_rows(splat_ref, vectors):
    return Splats(splat_ref, 2 * len(ENDS) + 2 * vectors * (vectors + 1), (2, vectors, vectors))


def splat_count(vectors):
    return -(-(2 * len(ENDS) + 2 * vectors * (2 * vectors + 1)) // SUB) * SUB


def field_of(ref, b, comp, z, cut):
    return tuple(ref[part, b, comp, z, cut] for part in range(2))


def tiles_of(nx):
    return [slice(SUB * t, SUB * (t + 1)) for t in range(nx // SUB)]


def open_magnetic(basis_ref, table_ref, sz_ref, h_ref, packed_ref):
    _, vectors, _, nz, nx, ny = basis_ref.shape
    parts = range(2)
    tile = (SUB, ny)
    rows = lax.broadcasted_iota(jnp.int32, tile, 0)
    lanes = lax.broadcasted_iota(jnp.int32, tile, 1)
    cuts = tiles_of(nx)

    def magnetic(b, z, last):
        shz = tuple(sz_ref[2 + part, pl.ds(z, 1)] for part in parts)
        for cut in cuts:
            u = [field_of(basis_ref, b, comp, z, cut) for comp in range(3)]

            def step_z(comp):
                if last:
                    return tuple(-value for value in u[comp])
                return sub(field_of(basis_ref, b, comp, z + 1, cut), u[comp])

            def step_x(comp):
                if cut.stop < nx:
                    ahead = field_of(basis_ref, b, comp, z, slice(cut.start + 1, cut.stop + 1))
                else:
                    ahead = tuple(jnp.where(rows == SUB - 1, 0.0, pltpu.roll(value, SUB - 1, 0)) for value in u[comp])
                return sub(ahead, u[comp])

            def step_y(comp):
                ahead = tuple(jnp.where(lanes == ny - 1, 0.0, pltpu.roll(value, ny - 1, 1)) for value in u[comp])
                return sub(ahead, u[comp])

            shx = tuple(table_ref[SHX + part, cut] for part in parts)
            shy = tuple(table_ref[SHY + part, cut] for part in parts)
            h = (
                sub(cmul(shy, step_y(2)), cmul(shz, step_z(1))),
                sub(cmul(shz, step_z(0)), cmul(shx, step_x(2))),
                sub(cmul(shx, step_x(1)), cmul(shy, step_y(0))),
            )
            for comp in range(3):
                for part in parts:
                    h_ref[part, b, comp, z, cut] = h[comp][part]
            packed = packed_ref[z, cut]
            for slot, value in enumerate((h[2], h[0])):
                for part in parts:
                    row = packed_row(slot, part, b, vectors)
                    packed = jnp.where(lanes == row, pltpu.roll(value[part], (row + 1) % ny, 1), packed)
            packed_ref[z, cut] = packed

    return magnetic


def prepare_kernel(
    pml_ref, eps_real_ref, eps_loss_ref, coeffs_ref, ritz_ref, fields_ref, material_ref,
    basis_ref, eps_ref, h_ref, packed_ref, table_ref, sz_ref, splat_ref,
):
    _, vectors, _, nz, nx, ny = fields_ref.shape
    plane = (nx, ny)
    parts = range(2)
    for slot, direction, half, count, dim in (
        (SHX, 1, 0.5, nx, 0), (SEX, 1, 0.0, nx, 0), (SHY, 2, 0.5, ny, 1), (SEY, 2, 0.0, ny, 1),
    ):
        values = axis_stretch(pml_ref, direction, count, local_places(direction, count, plane, dim) + half)
        for part in parts:
            table_ref[slot + part] = values[part]
    line = (1, ny)
    ends = {
        "under": (0, nz, -1, 0.5, 1.0),
        "next_x": (1, nx, nx, 0.0, 1.0),
        "next_y": (2, ny, ny, 0.0, 1.0),
        "first_x": (1, nx, 0, 0.0, has_neighbour(1, -1)),
        "first_y": (2, ny, 0, 0.0, has_neighbour(2, -1)),
        "last_x": (1, nx, nx - 1, 0.5, 1.0),
        "last_y": (2, ny, ny - 1, 0.5, 1.0),
    }
    lines = []
    for name in ENDS:
        direction, count, offset, half, factor = ends[name]
        values = axis_stretch(pml_ref, direction, count, one_place(direction, count, offset, line) + half)
        lines += [value * factor for value in values]
    lines += [
        jnp.broadcast_to(ritz_ref[part:part + 1, b:b + 1], line) for part in parts for b in range(vectors)
    ]
    real, imag = (
        [
            jnp.broadcast_to(coeffs_ref[part, a:a + 1, b:b + 1], line)
            for a in range(vectors) for b in range(vectors)
        ]
        for part in parts
    )
    lines += real + imag
    lines += [second + first for first, second in zip(real, imag)] + [second - first for first, second in zip(real, imag)]
    for row, value in enumerate(lines):
        splat_ref[row:row + 1] = value
    splat_ref[len(lines):] = jnp.zeros((splat_ref.shape[0] - len(lines), ny), jnp.float32)
    for slot, half in ((0, 0.0), (2, 0.5)):
        values = axis_stretch(pml_ref, 0, nz, local_places(0, nz, (nz, ny), 0) + half)
        for part in parts:
            sz_ref[slot + part] = values[part]

    coeffs, mixed = coeff_rows(splat_ref, vectors), mixed_rows(splat_ref, vectors)
    choices = [
        [jnp.broadcast_to(-OMEGA_SQ * source[0:1, number:number + 1], plane) for number in range(source.shape[1])]
        for source in (eps_real_ref, eps_loss_ref)
    ]

    @pl.loop(0, nz)
    def _(z):
        material = material_ref[z]
        for part in parts:
            value = jnp.zeros(plane, jnp.float32)
            for number, choice in enumerate(choices[part]):
                value = jnp.where(material == number, choice, value)
            eps_ref[part, z] = value
        for comp in range(3):
            real = [fields_ref[0, a, comp, z] for a in range(vectors)]
            imag = [fields_ref[1, a, comp, z] for a in range(vectors)]
            both = [first + second for first, second in zip(real, imag)]
            for b in range(vectors):
                shared = tree_sum([coeffs[0, a, b] * both[a] for a in range(vectors)])
                less = tree_sum([mixed[0, a, b] * imag[a] for a in range(vectors)])
                more = tree_sum([mixed[1, a, b] * real[a] for a in range(vectors)])
                basis_ref[0, b, comp, z] = shared - less
                basis_ref[1, b, comp, z] = shared + more
        packed_ref[z] = jnp.zeros(plane, jnp.float32)

    magnetic = open_magnetic(basis_ref, table_ref, sz_ref, h_ref, packed_ref)
    for b in range(vectors):
        magnetic(b, nz - 1, True)


def turn_face(coeffs_ref, direction, raw_ref, face_ref):
    inside = has_neighbour(direction, 1)
    vectors = raw_ref.shape[1]
    for slot in range(2):
        old = [(raw_ref[0, a, slot] * inside, raw_ref[1, a, slot] * inside) for a in range(vectors)]
        for b in range(vectors):
            new = rotated(coeffs_ref, old, b)
            for part in range(2):
                face_ref[part, b, slot] = new[part]


def turn_column(coeffs_ref, raw_ref, rows_ref):
    vectors = coeffs_ref.shape[1]
    inside = has_neighbour(2, 1)
    both = 2 * vectors
    shape = (both, raw_ref.shape[1])
    which = lax.broadcasted_iota(jnp.int32, shape, 0)
    turned = [jnp.zeros(shape, jnp.float32)] * 2
    for part in range(2):
        for a in range(vectors):
            column = jnp.zeros(shape, jnp.float32)
            for b in range(vectors):
                first, second = (coeffs_ref[0, a, b] * inside)[:, :shape[1]], (coeffs_ref[1, a, b] * inside)[:, :shape[1]]
                if part:
                    first, second = -second, first
                column = jnp.where(which == b, first, column)
                column = jnp.where(which == vectors + b, second, column)
            for slot in range(2):
                row = packed_row(slot, part, a, vectors)
                turned[slot] = turned[slot] + column * raw_ref[row:row + 1]
    for slot in range(2):
        rows_ref[slot * both:(slot + 1) * both] = turned[slot]


def lane_to_last(values, slot, part, b, vectors):
    ny = values.shape[-1]
    lanes = lax.broadcasted_iota(jnp.int32, values.shape, 1)
    row = packed_row(slot, part, b, vectors)
    return jnp.where(lanes == ny - 1, pltpu.roll(values, ny - 1 - row, 1), 0.0)


def with_halos(h, b, z, cut, nx, xadd_ref, yadd_ref):
    vectors = xadd_ref.shape[1]
    column = yadd_ref[z, cut]
    hx = tuple(h[0][part] + lane_to_last(column, 1, part, b, vectors) for part in range(2))
    hz = tuple(h[2][part] + lane_to_last(column, 0, part, b, vectors) for part in range(2))
    hy = h[1]
    if cut.stop == nx:
        rows = lax.broadcasted_iota(jnp.int32, column.shape, 0)

        def row_of(slot):
            return tuple(
                jnp.where(rows == SUB - 1, xadd_ref[part, b, slot, pl.ds(z, 1)], 0.0) for part in range(2)
            )

        hy, hz = add(hy, row_of(0)), add(hz, row_of(1))
    return hx, hy, hz


def slab_kernel(
    splat_ref, basis_ref, h_in, raw_xf_ref, raw_yf_ref,
    h_ref, xf_ref, yt_ref, xadd_ref, yadd_ref, zf_ref,
):
    del h_in
    _, vectors, _, nz, nx, ny = basis_ref.shape
    parts = range(2)
    cells = nz * nx
    both = 2 * vectors
    coeffs = coeff_rows(splat_ref, vectors)
    turn_face(coeffs, 1, raw_xf_ref, xf_ref)
    turn_column(coeffs, raw_yf_ref, yt_ref)
    shx = end_value(splat_ref, "last_x")
    shy = end_value(splat_ref, "last_y", cells)
    for b in range(vectors):
        for slot in range(2):
            value = cmul(shx, tuple(xf_ref[part, b, 1 - slot] for part in parts))
            for part in parts:
                xadd_ref[part, b, slot] = value[part] if slot else -value[part]
    added = []
    for slot in range(2):
        value = cmul(shy, (yt_ref[slot * both:slot * both + vectors], yt_ref[slot * both + vectors:(slot + 1) * both]))
        added += [part if slot else -part for part in value]
    rest = jnp.zeros((ny - 2 * both, cells), jnp.float32)
    yadd_ref[...] = jnp.concatenate(added + [rest], axis=0).T.reshape(nz, nx, ny)
    last = nz - 1
    lower = jnp.full((SUB, ny), lax.axis_index(AXES[0]), jnp.int32) == 0
    for b in range(vectors):
        for cut in tiles_of(nx):
            h = [field_of(h_ref, b, comp, last, cut) for comp in range(3)]
            h = with_halos(h, b, last, cut, nx, xadd_ref, yadd_ref)
            for part in parts:
                for comp in range(3):
                    h_ref[part, b, comp, last, cut] = h[comp][part]
                for comp in range(2):
                    zf_ref[part, b, comp, cut] = jnp.where(lower, h[comp][part], basis_ref[part, b, comp, 0, cut])


def plane_step(
    b, z, before, sums, ritz_ref, basis_ref, eps_ref, table_ref, sz_ref, h_ref, left_ref, halos=None
):
    _, vectors, _, _, nx, ny = basis_ref.shape
    rows = lax.broadcasted_iota(jnp.int32, (SUB, ny), 0)
    lanes = lax.broadcasted_iota(jnp.int32, (SUB, ny), 1)
    parts = range(2)
    cuts = tiles_of(nx)
    sez = tuple(sz_ref[part, pl.ds(z, 1)] for part in parts)
    fields = []
    for cut in cuts:
        h = [field_of(h_ref, b, comp, z, cut) for comp in range(3)]
        if halos is not None:
            h = with_halos(h, b, z, cut, nx, *halos)
            for comp in (1, 2):
                for part in parts:
                    h_ref[part, b, comp, z, cut] = h[comp][part]
        fields.append(h)
    sums = list(sums)
    for t, cut in enumerate(cuts):
        hx, hy, hz = fields[t]

        def back_x(comp):
            here = fields[t][comp]
            if t:
                past = field_of(h_ref, b, comp, z, slice(cut.start - 1, cut.stop - 1))
            else:
                past = tuple(jnp.where(rows == 0, 0.0, pltpu.roll(value, 1, 0)) for value in here)
            return sub(here, past)

        def back_y(value):
            return sub(value, tuple(jnp.where(lanes == 0, 0.0, pltpu.roll(part, 1, 1)) for part in value))

        sex = tuple(table_ref[SEX + part, cut] for part in parts)
        sey = tuple(table_ref[SEY + part, cut] for part in parts)
        bxy, bxz = (cmul(sex, back_x(comp)) for comp in (1, 2))
        byz, byx = (cmul(sey, back_y(value)) for value in (hz, hx))
        bzx, bzy = (cmul(sez, sub(value, past)) for value, past in zip((hx, hy), before[t]))
        curl = (sub(byz, bzy), sub(bzx, bxz), sub(bxy, byx))
        u = [field_of(basis_ref, b, comp, z, cut) for comp in range(3)]
        eps = tuple(eps_ref[part, z, cut] for part in parts)
        w = [add(curl[comp], cmul(eps, u[comp])) for comp in range(3)]
        for comp in range(3):
            left = sub(w[comp], cmul((ritz_ref[0, b], ritz_ref[1, b]), u[comp]))
            for part in parts:
                left_ref[part, b, comp, z, cut] = left[part]
        for a in range(vectors):
            total = sums[a]
            for comp in range(3):
                total = add(total, cmul(field_of(basis_ref, a, comp, z, cut), w[comp]))
            sums[a] = total
    return [(h[0], h[1]) for h in fields], sums


def inner_kernel(
    splat_ref, basis_ref, eps_ref, table_ref, sz_ref, h_in, packed_in, xadd_ref, yadd_ref,
    h_ref, packed_ref, left_ref, acc_ref, before_ref, hxf_ref, basis_hbm, sem,
):
    del h_in, packed_in
    _, vectors, _, nz, nx, ny = basis_ref.shape
    keep = pltpu.make_async_copy(basis_ref, basis_hbm, sem)
    keep.start()
    cuts = tiles_of(nx)
    magnetic = open_magnetic(basis_ref, table_ref, sz_ref, h_ref, packed_ref)

    @pl.loop(0, nz - 1)
    def _(z):
        for b in range(vectors):
            magnetic(b, z, False)

    lanes = lax.broadcasted_iota(jnp.int32, (nz, ny), 1)
    open_plane = lax.broadcasted_iota(jnp.int32, (nz, ny), 0) < nz - 1
    packed_ref[...] = packed_ref[...] + yadd_ref[...]
    corner = packed_ref[:, nx - 1, :]
    for b in range(vectors):
        for part in range(2):
            row = packed_row(0, part, b, vectors)
            more = xadd_ref[part, b, 1]
            corner = corner + jnp.where(lanes == row, pltpu.roll(more, (row + 1) % ny, 1), 0.0)
            more = more + lane_to_last(yadd_ref[:, nx - 1, :], 0, part, b, vectors)
            hxf_ref[part, b, 0] = h_ref[part, b, 1, :, nx - 1, :] + jnp.where(open_plane, xadd_ref[part, b, 0], 0.0)
            hxf_ref[part, b, 1] = h_ref[part, b, 2, :, nx - 1, :] + jnp.where(open_plane, more, 0.0)
    packed_ref[:, nx - 1, :] = corner
    acc_ref[...] = jnp.zeros(acc_ref.shape, jnp.float32)
    before_ref[...] = jnp.zeros(before_ref.shape, jnp.float32)

    @pl.loop(0, nz - 1)
    def _(z):
        for b in range(vectors):
            before = [
                tuple(tuple(before_ref[part, b, slot, cut] for part in range(2)) for slot in range(2)) for cut in cuts
            ]
            sums = [(acc_ref[b, a], acc_ref[b, vectors + a]) for a in range(vectors)]
            before, sums = plane_step(
                b, z, before, sums, ritz_rows(splat_ref, vectors), basis_ref, eps_ref, table_ref, sz_ref, h_ref, left_ref, (xadd_ref, yadd_ref)
            )
            for part in range(2):
                for a in range(vectors):
                    acc_ref[b, part * vectors + a] = sums[a][part]
                for t, cut in enumerate(cuts):
                    for slot in range(2):
                        before_ref[part, b, slot, cut] = before[t][slot][part]

    keep.wait()


def close_last_plane(sz_ref, zf_ref, packed_in, h_ref, hxf_ref, hyf_ref):
    _, vectors, _, nz, nx, ny = h_ref.shape
    parts = range(2)
    last = nz - 1
    lanes = lax.broadcasted_iota(jnp.int32, (SUB, ny), 1)
    shz = tuple(sz_ref[2 + part, last:] * has_neighbour(0, 1) for part in parts)
    packed = [packed_in[last, cut] for cut in tiles_of(nx)]
    for b in range(vectors):
        for t, cut in enumerate(tiles_of(nx)):
            ex, ey = (tuple(zf_ref[part, b, slot, cut] for part in parts) for slot in range(2))
            more = (tuple(-value for value in cmul(shz, ey)), cmul(shz, ex))
            for part in parts:
                for comp in range(2):
                    h_ref[part, b, comp, last, cut] = h_ref[part, b, comp, last, cut] + more[comp][part]
                row = packed_row(1, part, b, vectors)
                edge = pltpu.roll(more[0][part], (row + 1) % ny, 1)
                packed[t] = packed[t] + jnp.where(lanes == row, edge, 0.0)
                if cut.stop == nx:
                    hxf_ref[part, b, 0, last:] = hxf_ref[part, b, 0, last:] + more[1][part][SUB - 1:]
    inner = packed_in[:last].reshape(last * nx, ny)
    hyf_ref[...] = jnp.concatenate([inner] + packed, axis=0).T[:hyf_ref.shape[0]]


def outer_kernel(
    splat_ref, basis_ref, eps_ref, table_ref, sz_ref, h_in, zf_ref, xf_ref, yt_ref, hxf_in, packed_in,
    left_in, acc_ref, before_ref, left_ref, gram_ref, h_ref, hxf_ref, hyf_ref,
):
    del left_in, h_in, hxf_in
    close_last_plane(sz_ref, zf_ref, packed_in, h_ref, hxf_ref, hyf_ref)
    _, vectors, _, nz, nx, ny = basis_ref.shape
    parts = range(2)
    cuts = tiles_of(nx)
    under = end_value(splat_ref, "under")
    sez = tuple(sz_ref[part, 0:1] * has_neighbour(0, -1) for part in parts)
    sx_next = end_value(splat_ref, "next_x")
    sy_next = end_value(splat_ref, "next_y", nz * nx)
    both = 2 * vectors
    ends = [
        cmul(sy_next, (yt_ref[slot * both:slot * both + vectors], yt_ref[slot * both + vectors:(slot + 1) * both]))
        for slot in range(2)
    ]
    columns = lax.broadcasted_iota(jnp.int32, (both, ny), 1)
    gram = jnp.zeros((both, ny), jnp.float32)
    for b in range(vectors):

        def tile_of(ref, slot, cut, b=b):
            return tuple(ref[part, b, slot, cut] for part in parts)

        before = [tuple(tile_of(before_ref, slot, cut) for slot in range(2)) for cut in cuts]
        sums = [(acc_ref[b, a], acc_ref[b, vectors + a]) for a in range(vectors)]
        _, sums = plane_step(
            b, nz - 1, before, sums, ritz_rows(splat_ref, vectors), basis_ref, eps_ref, table_ref, sz_ref, h_ref, left_ref
        )
        for cut in cuts:
            ex, ey = (field_of(basis_ref, b, comp, 0, cut) for comp in range(2))
            hx = sub(tile_of(zf_ref, 0, cut), cmul(under, ey))
            hy = add(tile_of(zf_ref, 1, cut), cmul(under, ex))
            more = (cmul(sez, hy), cmul(sez, hx))
            for part in parts:
                left_ref[part, b, 0, 0, cut] = left_ref[part, b, 0, 0, cut] + more[0][part]
                left_ref[part, b, 1, 0, cut] = left_ref[part, b, 1, 0, cut] - more[1][part]
            for a in range(vectors):
                ex, ey = (field_of(basis_ref, a, comp, 0, cut) for comp in range(2))
                sums[a] = add(sums[a], sub(cmul(ex, more[0]), cmul(ey, more[1])))
        h_y = tuple(hxf_ref[part, b, 0] for part in parts)
        h_z = tuple(hxf_ref[part, b, 1] for part in parts)
        for a in range(vectors):
            over = cmul(tuple(xf_ref[part, a, 0] for part in parts), h_z)
            over = sub(over, cmul(tuple(xf_ref[part, a, 1] for part in parts), h_y))
            over = cmul(sx_next, over)
            for row in range(0, nz, SUB):
                sums[a] = add(sums[a], tuple(part[row:row + SUB] for part in over))
        flat = jnp.concatenate(
            [jnp.sum(sums[a][part], axis=0, keepdims=True) for part in parts for a in range(vectors)], axis=0
        )
        over = None
        for slot in range(2):
            h = tuple(hyf_ref[packed_row(slot, part, b, vectors)][None] for part in parts)
            term = cmul(ends[slot], h)
            over = term if over is None else sub(term, over)
        side = jnp.concatenate(over, axis=0)
        total = jnp.sum(flat, axis=1, keepdims=True) + jnp.sum(side, axis=1, keepdims=True)
        gram = jnp.where(columns == b, total, gram)
    everywhere = 3.0 * nz * nx * ny
    for axis in AXES:
        everywhere = everywhere * lax.axis_size(axis)
    gram = gram * (1.0 / everywhere)
    row = tree_sum([gram[0:1]] + [pltpu.roll(gram[row:row + 1], row * vectors, 1) for row in range(1, both)])
    block = jnp.concatenate([row, jnp.zeros((gram_ref.shape[1] - 1, ny), jnp.float32)], axis=0)
    for device in range(gram_ref.shape[0]):
        gram_ref[device] = block


def gather_kernel(rows_ref, gram_ref):
    vectors = gram_ref.shape[1]
    total = tree_sum([rows_ref[device] for device in range(rows_ref.shape[0])])[0:1]
    count = total.shape[1]
    for part in range(2):
        for a in range(vectors):
            row = (part * vectors + a) * vectors
            turned = pltpu.roll(total, count - row, 1) if row else total
            gram_ref[part, a:a + 1] = turned[:, :vectors]


def rim_y_kernel(splat_ref, left_in, hyf_ref, left_ref, residual_hbm, yadd_ref, sems):
    del left_in
    _, vectors, _, nz, nx, ny = left_ref.shape
    parts = range(2)
    both = 2 * vectors
    sey = end_value(splat_ref, "first_y", nz * nx)
    added = []
    for slot in range(2):
        first = slot * both
        value = cmul(sey, (hyf_ref[first:first + vectors], hyf_ref[first + vectors:first + both]))
        added += [part if slot else -part for part in value]
    rest = jnp.zeros((ny - 2 * both, nz * nx), jnp.float32)
    yadd_ref[...] = jnp.concatenate(added + [rest], axis=0).T.reshape(nz, nx, ny)
    lanes = lax.broadcasted_iota(jnp.int32, (SUB, ny), 1)

    def kept(z):
        blocks = [(slice(None), slice(None), 0, z)]
        blocks += [(slice(None), slice(None), comp, z, slice(SUB, nx)) for comp in (1, 2)]
        return [
            pltpu.make_async_copy(left_ref.at[block], residual_hbm.at[block], sems.at[place, z])
            for place, block in enumerate(blocks)
        ]

    @pl.loop(0, nz)
    def _(z):
        for cut in tiles_of(nx):
            column = yadd_ref[z, cut]
            for b in range(vectors):
                for part in parts:
                    for slot, comp in enumerate((0, 2)):
                        row = packed_row(slot, part, b, vectors)
                        value = pltpu.roll(column, ny - row, 1) if row else column
                        value = jnp.where(lanes == 0, value, 0.0)
                        left_ref[part, b, comp, z, cut] = left_ref[part, b, comp, z, cut] + value
        for copy in kept(z):
            copy.start()

    @pl.loop(0, nz)
    def _(z):
        for copy in kept(z):
            copy.wait()


def rim_x_kernel(splat_ref, left_in, residual_in, hxf_ref, left_ref, residual_hbm, xadd_ref, sems):
    del left_in, residual_in
    _, vectors, _, nz, nx, ny = left_ref.shape
    parts = range(2)
    sex = end_value(splat_ref, "first_x")
    for b in range(vectors):
        for slot in range(2):
            value = cmul(sex, tuple(hxf_ref[part, b, slot] for part in parts))
            for part in parts:
                xadd_ref[part, b, slot] = value[part] if slot else -value[part]
    rows = lax.broadcasted_iota(jnp.int32, (SUB, ny), 0)
    first = slice(0, SUB)
    copies = []
    for z in range(nz):
        for b in range(vectors):
            for part in parts:
                for slot, comp in ((1, 1), (0, 2)):
                    value = jnp.where(rows == 0, xadd_ref[part, b, slot, z:z + 1], 0.0)
                    left_ref[part, b, comp, z, first] = left_ref[part, b, comp, z, first] + value
        block = (slice(None), slice(None), slice(1, 3), z, first)
        copies.append(pltpu.make_async_copy(left_ref.at[block], residual_hbm.at[block], sems.at[z]))
        copies[-1].start()
    for copy in copies:
        copy.wait()


def body(fields, material, pml_width, eps_real, eps_loss, coeffs, ritz):
    _, vectors, _, nz, nx, ny = fields.shape
    f32 = lambda *shape: jax.ShapeDtypeStruct(shape, jnp.float32)
    scratch = lambda *shape: pltpu.VMEM(shape, jnp.float32)
    params = pltpu.CompilerParams(vmem_limit_bytes=40 * 1024 * 1024)
    whole = f32(*fields.shape)
    zf_shape = (2, vectors, 2, nx, ny)
    xf_shape = (2, vectors, 2, nz, ny)
    yf_shape = (4 * vectors, nz * nx)
    near, xf, yf = pl.pallas_call(
        face_kernel,
        out_shape=(whole, f32(*xf_shape), f32(*yf_shape)),
        in_specs=[HBM],
        out_specs=(VMEM,) * 3,
        scratch_shapes=[pltpu.SemaphoreType.DMA((2, 3))],
        compiler_params=params,
        name="take_faces",
    )(pltpu.with_memory_space_constraint(fields, pltpu.HBM))
    xf = passed_round(xf, "gx", -1)
    yf = passed_round(yf, "gy", -1)
    cells = fields.size // 6 // vectors

    def cost(flops, passes):
        return pl.CostEstimate(flops=flops * cells, bytes_accessed=passes * 4 * fields.size, transcendentals=0)

    planes = f32(nz, nx, ny)
    face = f32(*xf_shape)
    basis, eps, h, packed, table, sz, splats = pl.pallas_call(
        prepare_kernel,
        out_shape=(whole, f32(2, nz, nx, ny), whole, planes, f32(8, nx, ny), f32(4, nz, ny), f32(splat_count(vectors), ny)),
        in_specs=[VMEM] * 7,
        out_specs=(VMEM,) * 7,
        compiler_params=params,
        cost_estimate=cost(800, 4),
        name="prepare",
    )(pml_width[None], eps_real[None], eps_loss[None], coeffs, ritz, near, material)
    h, xf, yt, xadd, yadd, zf = pl.pallas_call(
        slab_kernel,
        out_shape=(whole, face, f32(*yf_shape), face, planes, f32(*zf_shape)),
        in_specs=[VMEM] * 5,
        out_specs=(VMEM,) * 6,
        input_output_aliases={2: 0},
        compiler_params=params,
        name="slab_face",
    )(splats, basis, h, xf, yf)
    zf = passed_round(zf, "gz", 1)
    h, packed, left, acc, before, hxf, basis_new = pl.pallas_call(
        inner_kernel,
        out_shape=(whole, planes, whole, f32(vectors, 2 * vectors, SUB, ny), f32(*zf_shape), face, whole),
        in_specs=[VMEM] * 9,
        out_specs=(VMEM,) * 6 + (HBM,),
        scratch_shapes=[pltpu.SemaphoreType.DMA],
        input_output_aliases={5: 0, 6: 1},
        compiler_params=params,
        cost_estimate=cost(800, 2),
        name="apply_inner",
    )(splats, basis, eps, table, sz, h, packed, xadd, yadd)
    devices = lax.axis_size("gx") * lax.axis_size("gy") * lax.axis_size("gz")
    left, gram, _, hxf, hyf = pl.pallas_call(
        outer_kernel,
        out_shape=(whole, f32(devices, 4, ny), whole, face, f32(*yf_shape)),
        in_specs=[VMEM] * 14,
        out_specs=(VMEM,) * 5,
        input_output_aliases={11: 0, 5: 2, 9: 3},
        compiler_params=params,
        cost_estimate=cost(300, 1),
        name="apply_outer",
    )(splats, basis, eps, table, sz, h, zf, xf, yt, hxf, packed, left, acc, before)
    gram, hxf, hyf = lax.optimization_barrier((gram, hxf, hyf))
    rows = lax.all_to_all(gram, ("gx", "gy", "gz"), 0, 0)
    from_x = passed_round(hxf, "gx", 1)
    from_y = passed_round(hyf, "gy", 1)
    free = pl.CostEstimate(flops=0, bytes_accessed=0, transcendentals=0)
    left, residual = pl.pallas_call(
        rim_y_kernel,
        out_shape=(whole, whole),
        in_specs=[VMEM] * 3,
        out_specs=(VMEM, HBM),
        scratch_shapes=[scratch(nz, nx, ny), pltpu.SemaphoreType.DMA((3, nz))],
        input_output_aliases={1: 0},
        compiler_params=params,
        cost_estimate=free,
        name="add_y_rims",
    )(splats, left, from_y)
    _, residual = pl.pallas_call(
        rim_x_kernel,
        out_shape=(whole, whole),
        in_specs=[VMEM, VMEM, HBM, VMEM],
        out_specs=(VMEM, HBM),
        scratch_shapes=[scratch(*xf_shape), pltpu.SemaphoreType.DMA((nz,))],
        input_output_aliases={1: 0, 2: 1},
        compiler_params=params,
        cost_estimate=free,
        name="add_x_rims",
    )(splats, left, residual, from_x)
    rows, residual = lax.optimization_barrier((rows, residual))
    gram = pl.pallas_call(
        gather_kernel,
        out_shape=f32(2, vectors, vectors),
        in_specs=[VMEM],
        out_specs=VMEM,
        compiler_params=params,
        name="sum_rows",
    )(rows)
    return basis_new, residual, gram


def solution(mesh):
    in_specs = (P(None, None, None, "gz", "gx", "gy"), P("gz", "gx", "gy"), P(), P(), P(), P(), P())
    out_specs = (P(None, None, None, "gz", "gx", "gy"), P(None, None, None, "gz", "gx", "gy"), P())
    return jax.shard_map(body, mesh=mesh, in_specs=in_specs, out_specs=out_specs, check_vma=False)
```

```python
import functools

import jax
import jax.numpy as jnp
from jax import lax
from jax.experimental import pallas as pl
from jax.experimental.pallas import tpu as pltpu
from jax.sharding import PartitionSpec as P

OMEGA_SQ = 0.36
SIGMA_TOP = 3.0
BOUNDS = ((4, 5), (0, 1), (2, 3))
AXES = ("gz", "gx", "gy")

VMEM = pl.BlockSpec(memory_space=pltpu.VMEM)
HBM = pl.BlockSpec(memory_space=pltpu.HBM)


def passed_round(value, axis, steps):
    count = lax.axis_size(axis)
    return lax.ppermute(value, axis, [(source, (source + steps) % count) for source in range(count)])


def inverse_stretch(places, length, low_width, high_width):
    inside_depth = jnp.clip((low_width - places) / low_width, 0.0, 1.0) + jnp.clip(
        (places + 1.0 - length + high_width) / high_width, 0.0, 1.0
    )
    absorb = SIGMA_TOP * inside_depth * inside_depth
    scaled = 1.0 / (1.0 + absorb * absorb)
    return scaled, -absorb * scaled


def tree_sum(values):
    while len(values) > 1:
        pairs = [values[place] + values[place + 1] for place in range(0, len(values) - 1, 2)]
        values = pairs + ([values[-1]] if len(values) % 2 else [])
    return values[0]


def cmul(left, right):
    return (left[0] * right[0] - left[1] * right[1], left[0] * right[1] + left[1] * right[0])


def add(left, right):
    return (left[0] + right[0], left[1] + right[1])


def sub(left, right):
    return (left[0] - right[0], left[1] - right[1])


def axis_stretch(pml_ref, direction, count, places):
    total = count * lax.axis_size(AXES[direction])
    low_slot, high_slot = BOUNDS[direction]
    low, high = (
        jnp.broadcast_to(pml_ref[0:1, slot:slot + 1].astype(jnp.float32), places.shape) for slot in (low_slot, high_slot)
    )
    return inverse_stretch(places, jnp.float32(total), low, high)


def local_places(direction, count, shape, dim):
    start = lax.axis_index(AXES[direction]) * count
    return (lax.broadcasted_iota(jnp.int32, shape, dim) + start).astype(jnp.float32)


def one_place(direction, count, offset, shape):
    start = lax.axis_index(AXES[direction]) * count + offset
    return jnp.full(shape, start, jnp.int32).astype(jnp.float32)


def packed_row(slot, part, vector, vectors):
    return (slot * 2 + part) * vectors + vector


def has_neighbour(direction, steps):
    place = lax.axis_index(AXES[direction]) + steps
    inside = (place >= 0) & (place < lax.axis_size(AXES[direction]))
    return jnp.where(inside, 1.0, 0.0).astype(jnp.float32)


def face_kernel(fields_hbm, fields_ref, xf_ref, yf_ref, sems):
    _, vectors, _, nz, nx, ny = fields_ref.shape
    lanes = lax.broadcasted_iota(jnp.int32, (nx, ny), 1)
    copies = [
        pltpu.make_async_copy(fields_hbm.at[part, :, comp], fields_ref.at[part, :, comp], sems.at[part, comp])
        for comp in (0, 2, 1) for part in range(2)
    ]
    for copy in copies:
        copy.start()
    packed = [jnp.zeros((nx, ny), jnp.float32)] * nz
    for place, comp in enumerate((0, 2)):
        for part in range(2):
            copies[2 * place + part].wait()
            for a in range(vectors):
                row = packed_row(comp // 2, part, a, vectors)
                for z in range(nz):
                    value = fields_ref[part, a, comp, z]
                    packed[z] = jnp.where(lanes == row, pltpu.roll(value, row, 1) if row else value, packed[z])
    turned = jnp.concatenate(packed, axis=0).T
    yf_ref[...] = turned[:yf_ref.shape[0]]
    for part in range(2):
        for a in range(vectors):
            xf_ref[part, a, 1] = fields_ref[part, a, 2, :, 0, :]
    for part in range(2):
        copies[4 + part].wait()
        for a in range(vectors):
            xf_ref[part, a, 0] = fields_ref[part, a, 1, :, 0, :]


def rotated(coeffs_ref, old, b):
    new = None
    for a, value in enumerate(old):
        term = cmul((coeffs_ref[0, a, b], coeffs_ref[1, a, b]), value)
        new = term if new is None else add(new, term)
    return new


SUB = 8
SHX, SEX, SHY, SEY = range(0, 8, 2)


class Splats:
    def __init__(self, ref, first, shape):
        self.ref, self.first, self.shape = ref, first, shape

    def __getitem__(self, place):
        row = 0
        for index, size in zip(place, self.shape):
            row = row * size + index
        return self.ref[self.first + row:self.first + row + 1]


ENDS = ("under", "next_x", "next_y", "first_x", "first_y", "last_x", "last_y")


def end_value(splat_ref, name, width=None):
    row = 2 * ENDS.index(name)
    return tuple(splat_ref[row + part:row + part + 1, :width] for part in range(2))


def ritz_rows(splat_ref, vectors):
    return Splats(splat_ref, 2 * len(ENDS), (2, vectors))


def coeff_rows(splat_ref, vectors):
    return Splats(splat_ref, 2 * len(ENDS) + 2 * vectors, (2, vectors, vectors))


def mixed_rows(splat_ref, vectors):
    return Splats(splat_ref, 2 * len(ENDS) + 2 * vectors * (vectors + 1), (2, vectors, vectors))


def splat_count(vectors):
    return -(-(2 * len(ENDS) + 2 * vectors * (2 * vectors + 1)) // SUB) * SUB


def field_of(ref, b, comp, z, cut):
    return tuple(ref[part, b, comp, z, cut] for part in range(2))


def tiles_of(nx):
    return [slice(SUB * t, SUB * (t + 1)) for t in range(nx // SUB)]


def early_planes(nz):
    return (nz - 1) // 2


def open_magnetic(basis_ref, table_ref, sz_ref, h_ref, packed_ref):
    _, vectors, _, nz, nx, ny = basis_ref.shape
    parts = range(2)
    tile = (SUB, ny)
    rows = lax.broadcasted_iota(jnp.int32, tile, 0)
    lanes = lax.broadcasted_iota(jnp.int32, tile, 1)
    cuts = tiles_of(nx)

    def magnetic(b, z, last):
        shz = tuple(sz_ref[2 + part, pl.ds(z, 1)] for part in parts)
        for cut in cuts:
            u = [field_of(basis_ref, b, comp, z, cut) for comp in range(3)]

            def step_z(comp):
                if last:
                    return tuple(-value for value in u[comp])
                return sub(field_of(basis_ref, b, comp, z + 1, cut), u[comp])

            def step_x(comp):
                if cut.stop < nx:
                    ahead = field_of(basis_ref, b, comp, z, slice(cut.start + 1, cut.stop + 1))
                else:
                    ahead = tuple(jnp.where(rows == SUB - 1, 0.0, pltpu.roll(value, SUB - 1, 0)) for value in u[comp])
                return sub(ahead, u[comp])

            def step_y(comp):
                ahead = tuple(jnp.where(lanes == ny - 1, 0.0, pltpu.roll(value, ny - 1, 1)) for value in u[comp])
                return sub(ahead, u[comp])

            shx = tuple(table_ref[SHX + part, cut] for part in parts)
            shy = tuple(table_ref[SHY + part, cut] for part in parts)
            h = (
                sub(cmul(shy, step_y(2)), cmul(shz, step_z(1))),
                sub(cmul(shz, step_z(0)), cmul(shx, step_x(2))),
                sub(cmul(shx, step_x(1)), cmul(shy, step_y(0))),
            )
            for comp in range(3):
                for part in parts:
                    h_ref[part, b, comp, z, cut] = h[comp][part]
            packed = packed_ref[z, cut]
            for slot, value in enumerate((h[2], h[0])):
                for part in parts:
                    row = packed_row(slot, part, b, vectors)
                    packed = jnp.where(lanes == row, pltpu.roll(value[part], (row + 1) % ny, 1), packed)
            packed_ref[z, cut] = packed

    return magnetic


def prepare_kernel(
    pml_ref, eps_real_ref, eps_loss_ref, coeffs_ref, ritz_ref, fields_ref, material_ref,
    basis_ref, eps_ref, h_ref, packed_ref, table_ref, sz_ref, splat_ref,
):
    _, vectors, _, nz, nx, ny = fields_ref.shape
    plane = (nx, ny)
    parts = range(2)
    for slot, direction, half, count, dim in (
        (SHX, 1, 0.5, nx, 0), (SEX, 1, 0.0, nx, 0), (SHY, 2, 0.5, ny, 1), (SEY, 2, 0.0, ny, 1),
    ):
        values = axis_stretch(pml_ref, direction, count, local_places(direction, count, plane, dim) + half)
        for part in parts:
            table_ref[slot + part] = values[part]
    line = (1, ny)
    ends = {
        "under": (0, nz, -1, 0.5, 1.0),
        "next_x": (1, nx, nx, 0.0, 1.0),
        "next_y": (2, ny, ny, 0.0, 1.0),
        "first_x": (1, nx, 0, 0.0, has_neighbour(1, -1)),
        "first_y": (2, ny, 0, 0.0, has_neighbour(2, -1)),
        "last_x": (1, nx, nx - 1, 0.5, 1.0),
        "last_y": (2, ny, ny - 1, 0.5, 1.0),
    }
    lines = []
    for name in ENDS:
        direction, count, offset, half, factor = ends[name]
        values = axis_stretch(pml_ref, direction, count, one_place(direction, count, offset, line) + half)
        lines += [value * factor for value in values]
    lines += [
        jnp.broadcast_to(ritz_ref[part:part + 1, b:b + 1], line) for part in parts for b in range(vectors)
    ]
    real, imag = (
        [
            jnp.broadcast_to(coeffs_ref[part, a:a + 1, b:b + 1], line)
            for a in range(vectors) for b in range(vectors)
        ]
        for part in parts
    )
    lines += real + imag
    lines += [second + first for first, second in zip(real, imag)] + [second - first for first, second in zip(real, imag)]
    for row, value in enumerate(lines):
        splat_ref[row:row + 1] = value
    splat_ref[len(lines):] = jnp.zeros((splat_ref.shape[0] - len(lines), ny), jnp.float32)
    for slot, half in ((0, 0.0), (2, 0.5)):
        values = axis_stretch(pml_ref, 0, nz, local_places(0, nz, (nz, ny), 0) + half)
        for part in parts:
            sz_ref[slot + part] = values[part]

    coeffs, mixed = coeff_rows(splat_ref, vectors), mixed_rows(splat_ref, vectors)
    choices = [
        [jnp.broadcast_to(-OMEGA_SQ * source[0:1, number:number + 1], plane) for number in range(source.shape[1])]
        for source in (eps_real_ref, eps_loss_ref)
    ]

    @pl.loop(0, nz)
    def _(z):
        material = material_ref[z]
        for part in parts:
            value = jnp.zeros(plane, jnp.float32)
            for number, choice in enumerate(choices[part]):
                value = jnp.where(material == number, choice, value)
            eps_ref[part, z] = value
        for comp in range(3):
            real = [fields_ref[0, a, comp, z] for a in range(vectors)]
            imag = [fields_ref[1, a, comp, z] for a in range(vectors)]
            both = [first + second for first, second in zip(real, imag)]
            for b in range(vectors):
                shared = tree_sum([coeffs[0, a, b] * both[a] for a in range(vectors)])
                less = tree_sum([mixed[0, a, b] * imag[a] for a in range(vectors)])
                more = tree_sum([mixed[1, a, b] * real[a] for a in range(vectors)])
                basis_ref[0, b, comp, z] = shared - less
                basis_ref[1, b, comp, z] = shared + more
        packed_ref[z] = jnp.zeros(plane, jnp.float32)

    magnetic = open_magnetic(basis_ref, table_ref, sz_ref, h_ref, packed_ref)

    @pl.loop(0, early_planes(nz))
    def _(z):
        for b in range(vectors):
            magnetic(b, z, False)

    for b in range(vectors):
        magnetic(b, nz - 1, True)


def turn_face(coeffs_ref, direction, raw_ref, face_ref):
    inside = has_neighbour(direction, 1)
    vectors = raw_ref.shape[1]
    for slot in range(2):
        old = [(raw_ref[0, a, slot] * inside, raw_ref[1, a, slot] * inside) for a in range(vectors)]
        for b in range(vectors):
            new = rotated(coeffs_ref, old, b)
            for part in range(2):
                face_ref[part, b, slot] = new[part]


def turn_column(coeffs_ref, raw_ref, rows_ref):
    vectors = coeffs_ref.shape[1]
    inside = has_neighbour(2, 1)
    both = 2 * vectors
    shape = (both, raw_ref.shape[1])
    which = lax.broadcasted_iota(jnp.int32, shape, 0)
    turned = [jnp.zeros(shape, jnp.float32)] * 2
    for part in range(2):
        for a in range(vectors):
            column = jnp.zeros(shape, jnp.float32)
            for b in range(vectors):
                first, second = (coeffs_ref[0, a, b] * inside)[:, :shape[1]], (coeffs_ref[1, a, b] * inside)[:, :shape[1]]
                if part:
                    first, second = -second, first
                column = jnp.where(which == b, first, column)
                column = jnp.where(which == vectors + b, second, column)
            for slot in range(2):
                row = packed_row(slot, part, a, vectors)
                turned[slot] = turned[slot] + column * raw_ref[row:row + 1]
    for slot in range(2):
        rows_ref[slot * both:(slot + 1) * both] = turned[slot]


def lane_to_last(values, slot, part, b, vectors):
    ny = values.shape[-1]
    lanes = lax.broadcasted_iota(jnp.int32, values.shape, 1)
    row = packed_row(slot, part, b, vectors)
    return jnp.where(lanes == ny - 1, pltpu.roll(values, ny - 1 - row, 1), 0.0)


def with_halos(h, b, z, cut, nx, xadd_ref, yadd_ref):
    vectors = xadd_ref.shape[1]
    column = yadd_ref[z, cut]
    hx = tuple(h[0][part] + lane_to_last(column, 1, part, b, vectors) for part in range(2))
    hz = tuple(h[2][part] + lane_to_last(column, 0, part, b, vectors) for part in range(2))
    hy = h[1]
    if cut.stop == nx:
        rows = lax.broadcasted_iota(jnp.int32, column.shape, 0)

        def row_of(slot):
            return tuple(
                jnp.where(rows == SUB - 1, xadd_ref[part, b, slot, pl.ds(z, 1)], 0.0) for part in range(2)
            )

        hy, hz = add(hy, row_of(0)), add(hz, row_of(1))
    return hx, hy, hz


def slab_kernel(
    splat_ref, basis_ref, h_in, raw_xf_ref, raw_yf_ref,
    h_ref, xf_ref, yt_ref, xadd_ref, yadd_ref, zf_ref,
):
    del h_in
    _, vectors, _, nz, nx, ny = basis_ref.shape
    parts = range(2)
    cells = nz * nx
    both = 2 * vectors
    coeffs = coeff_rows(splat_ref, vectors)
    turn_face(coeffs, 1, raw_xf_ref, xf_ref)
    turn_column(coeffs, raw_yf_ref, yt_ref)
    shx = end_value(splat_ref, "last_x")
    shy = end_value(splat_ref, "last_y", cells)
    for b in range(vectors):
        for slot in range(2):
            value = cmul(shx, tuple(xf_ref[part, b, 1 - slot] for part in parts))
            for part in parts:
                xadd_ref[part, b, slot] = value[part] if slot else -value[part]
    added = []
    for slot in range(2):
        value = cmul(shy, (yt_ref[slot * both:slot * both + vectors], yt_ref[slot * both + vectors:(slot + 1) * both]))
        added += [part if slot else -part for part in value]
    rest = jnp.zeros((ny - 2 * both, cells), jnp.float32)
    yadd_ref[...] = jnp.concatenate(added + [rest], axis=0).T.reshape(nz, nx, ny)
    last = nz - 1
    lower = jnp.full((SUB, ny), lax.axis_index(AXES[0]), jnp.int32) == 0
    for b in range(vectors):
        for cut in tiles_of(nx):
            h = [field_of(h_ref, b, comp, last, cut) for comp in range(3)]
            h = with_halos(h, b, last, cut, nx, xadd_ref, yadd_ref)
            for part in parts:
                for comp in range(3):
                    h_ref[part, b, comp, last, cut] = h[comp][part]
                for comp in range(2):
                    zf_ref[part, b, comp, cut] = jnp.where(lower, h[comp][part], basis_ref[part, b, comp, 0, cut])


def plane_step(
    b, z, before, sums, ritz_ref, basis_ref, eps_ref, table_ref, sz_ref, h_ref, left_ref, halos=None
):
    _, vectors, _, _, nx, ny = basis_ref.shape
    rows = lax.broadcasted_iota(jnp.int32, (SUB, ny), 0)
    lanes = lax.broadcasted_iota(jnp.int32, (SUB, ny), 1)
    parts = range(2)
    cuts = tiles_of(nx)
    sez = tuple(sz_ref[part, pl.ds(z, 1)] for part in parts)
    fields = []
    for cut in cuts:
        h = [field_of(h_ref, b, comp, z, cut) for comp in range(3)]
        if halos is not None:
            h = with_halos(h, b, z, cut, nx, *halos)
            for comp in (1, 2):
                for part in parts:
                    h_ref[part, b, comp, z, cut] = h[comp][part]
        fields.append(h)
    sums = list(sums)
    for t, cut in enumerate(cuts):
        hx, hy, hz = fields[t]

        def back_x(comp):
            here = fields[t][comp]
            if t:
                past = field_of(h_ref, b, comp, z, slice(cut.start - 1, cut.stop - 1))
            else:
                past = tuple(jnp.where(rows == 0, 0.0, pltpu.roll(value, 1, 0)) for value in here)
            return sub(here, past)

        def back_y(value):
            return sub(value, tuple(jnp.where(lanes == 0, 0.0, pltpu.roll(part, 1, 1)) for part in value))

        sex = tuple(table_ref[SEX + part, cut] for part in parts)
        sey = tuple(table_ref[SEY + part, cut] for part in parts)
        bxy, bxz = (cmul(sex, back_x(comp)) for comp in (1, 2))
        byz, byx = (cmul(sey, back_y(value)) for value in (hz, hx))
        bzx, bzy = (cmul(sez, sub(value, past)) for value, past in zip((hx, hy), before[t]))
        curl = (sub(byz, bzy), sub(bzx, bxz), sub(bxy, byx))
        u = [field_of(basis_ref, b, comp, z, cut) for comp in range(3)]
        eps = tuple(eps_ref[part, z, cut] for part in parts)
        w = [add(curl[comp], cmul(eps, u[comp])) for comp in range(3)]
        for comp in range(3):
            left = sub(w[comp], cmul((ritz_ref[0, b], ritz_ref[1, b]), u[comp]))
            for part in parts:
                left_ref[part, b, comp, z, cut] = left[part]
        for a in range(vectors):
            total = sums[a]
            for comp in range(3):
                total = add(total, cmul(field_of(basis_ref, a, comp, z, cut), w[comp]))
            sums[a] = total
    return [(h[0], h[1]) for h in fields], sums


def inner_kernel(
    splat_ref, basis_ref, eps_ref, table_ref, sz_ref, h_in, packed_in, xadd_ref, yadd_ref,
    h_ref, packed_ref, left_ref, acc_ref, before_ref, hxf_ref, basis_hbm, sem,
):
    del h_in, packed_in
    _, vectors, _, nz, nx, ny = basis_ref.shape
    keep = pltpu.make_async_copy(basis_ref, basis_hbm, sem)
    keep.start()
    cuts = tiles_of(nx)
    magnetic = open_magnetic(basis_ref, table_ref, sz_ref, h_ref, packed_ref)

    @pl.loop(early_planes(nz), nz - 1)
    def _(z):
        for b in range(vectors):
            magnetic(b, z, False)

    lanes = lax.broadcasted_iota(jnp.int32, (nz, ny), 1)
    open_plane = lax.broadcasted_iota(jnp.int32, (nz, ny), 0) < nz - 1
    packed_ref[...] = packed_ref[...] + yadd_ref[...]
    corner = packed_ref[:, nx - 1, :]
    for b in range(vectors):
        for part in range(2):
            row = packed_row(0, part, b, vectors)
            more = xadd_ref[part, b, 1]
            corner = corner + jnp.where(lanes == row, pltpu.roll(more, (row + 1) % ny, 1), 0.0)
            more = more + lane_to_last(yadd_ref[:, nx - 1, :], 0, part, b, vectors)
            hxf_ref[part, b, 0] = h_ref[part, b, 1, :, nx - 1, :] + jnp.where(open_plane, xadd_ref[part, b, 0], 0.0)
            hxf_ref[part, b, 1] = h_ref[part, b, 2, :, nx - 1, :] + jnp.where(open_plane, more, 0.0)
    packed_ref[:, nx - 1, :] = corner
    acc_ref[...] = jnp.zeros(acc_ref.shape, jnp.float32)
    before_ref[...] = jnp.zeros(before_ref.shape, jnp.float32)

    @pl.loop(0, nz - 1)
    def _(z):
        for b in range(vectors):
            before = [
                tuple(tuple(before_ref[part, b, slot, cut] for part in range(2)) for slot in range(2)) for cut in cuts
            ]
            sums = [(acc_ref[b, a], acc_ref[b, vectors + a]) for a in range(vectors)]
            before, sums = plane_step(
                b, z, before, sums, ritz_rows(splat_ref, vectors), basis_ref, eps_ref, table_ref, sz_ref, h_ref, left_ref, (xadd_ref, yadd_ref)
            )
            for part in range(2):
                for a in range(vectors):
                    acc_ref[b, part * vectors + a] = sums[a][part]
                for t, cut in enumerate(cuts):
                    for slot in range(2):
                        before_ref[part, b, slot, cut] = before[t][slot][part]

    keep.wait()


def close_last_plane(sz_ref, zf_ref, packed_in, h_ref, hxf_ref, hyf_ref):
    _, vectors, _, nz, nx, ny = h_ref.shape
    parts = range(2)
    last = nz - 1
    lanes = lax.broadcasted_iota(jnp.int32, (SUB, ny), 1)
    shz = tuple(sz_ref[2 + part, last:] * has_neighbour(0, 1) for part in parts)
    packed = [packed_in[last, cut] for cut in tiles_of(nx)]
    for b in range(vectors):
        for t, cut in enumerate(tiles_of(nx)):
            ex, ey = (tuple(zf_ref[part, b, slot, cut] for part in parts) for slot in range(2))
            more = (tuple(-value for value in cmul(shz, ey)), cmul(shz, ex))
            for part in parts:
                for comp in range(2):
                    h_ref[part, b, comp, last, cut] = h_ref[part, b, comp, last, cut] + more[comp][part]
                row = packed_row(1, part, b, vectors)
                edge = pltpu.roll(more[0][part], (row + 1) % ny, 1)
                packed[t] = packed[t] + jnp.where(lanes == row, edge, 0.0)
                if cut.stop == nx:
                    hxf_ref[part, b, 0, last:] = hxf_ref[part, b, 0, last:] + more[1][part][SUB - 1:]
    inner = packed_in[:last].reshape(last * nx, ny)
    hyf_ref[...] = jnp.concatenate([inner] + packed, axis=0).T[:hyf_ref.shape[0]]


def outer_kernel(
    splat_ref, basis_ref, eps_ref, table_ref, sz_ref, h_in, zf_ref, xf_ref, yt_ref, hxf_in, packed_in,
    left_in, acc_ref, before_ref, left_ref, gram_ref, h_ref, hxf_ref, hyf_ref,
):
    del left_in, h_in, hxf_in
    close_last_plane(sz_ref, zf_ref, packed_in, h_ref, hxf_ref, hyf_ref)
    _, vectors, _, nz, nx, ny = basis_ref.shape
    parts = range(2)
    cuts = tiles_of(nx)
    under = end_value(splat_ref, "under")
    sez = tuple(sz_ref[part, 0:1] * has_neighbour(0, -1) for part in parts)
    sx_next = end_value(splat_ref, "next_x")
    sy_next = end_value(splat_ref, "next_y", nz * nx)
    both = 2 * vectors
    ends = [
        cmul(sy_next, (yt_ref[slot * both:slot * both + vectors], yt_ref[slot * both + vectors:(slot + 1) * both]))
        for slot in range(2)
    ]
    columns = lax.broadcasted_iota(jnp.int32, (both, ny), 1)
    gram = jnp.zeros((both, ny), jnp.float32)
    for b in range(vectors):

        def tile_of(ref, slot, cut, b=b):
            return tuple(ref[part, b, slot, cut] for part in parts)

        before = [tuple(tile_of(before_ref, slot, cut) for slot in range(2)) for cut in cuts]
        sums = [(acc_ref[b, a], acc_ref[b, vectors + a]) for a in range(vectors)]
        _, sums = plane_step(
            b, nz - 1, before, sums, ritz_rows(splat_ref, vectors), basis_ref, eps_ref, table_ref, sz_ref, h_ref, left_ref
        )
        for cut in cuts:
            ex, ey = (field_of(basis_ref, b, comp, 0, cut) for comp in range(2))
            hx = sub(tile_of(zf_ref, 0, cut), cmul(under, ey))
            hy = add(tile_of(zf_ref, 1, cut), cmul(under, ex))
            more = (cmul(sez, hy), cmul(sez, hx))
            for part in parts:
                left_ref[part, b, 0, 0, cut] = left_ref[part, b, 0, 0, cut] + more[0][part]
                left_ref[part, b, 1, 0, cut] = left_ref[part, b, 1, 0, cut] - more[1][part]
            for a in range(vectors):
                ex, ey = (field_of(basis_ref, a, comp, 0, cut) for comp in range(2))
                sums[a] = add(sums[a], sub(cmul(ex, more[0]), cmul(ey, more[1])))
        h_y = tuple(hxf_ref[part, b, 0] for part in parts)
        h_z = tuple(hxf_ref[part, b, 1] for part in parts)
        for a in range(vectors):
            over = cmul(tuple(xf_ref[part, a, 0] for part in parts), h_z)
            over = sub(over, cmul(tuple(xf_ref[part, a, 1] for part in parts), h_y))
            over = cmul(sx_next, over)
            for row in range(0, nz, SUB):
                sums[a] = add(sums[a], tuple(part[row:row + SUB] for part in over))
        flat = jnp.concatenate(
            [jnp.sum(sums[a][part], axis=0, keepdims=True) for part in parts for a in range(vectors)], axis=0
        )
        over = None
        for slot in range(2):
            h = tuple(hyf_ref[packed_row(slot, part, b, vectors)][None] for part in parts)
            term = cmul(ends[slot], h)
            over = term if over is None else sub(term, over)
        side = jnp.concatenate(over, axis=0)
        total = jnp.sum(flat, axis=1, keepdims=True) + jnp.sum(side, axis=1, keepdims=True)
        gram = jnp.where(columns == b, total, gram)
    everywhere = 3.0 * nz * nx * ny
    for axis in AXES:
        everywhere = everywhere * lax.axis_size(axis)
    gram = gram * (1.0 / everywhere)
    row = tree_sum([gram[0:1]] + [pltpu.roll(gram[row:row + 1], row * vectors, 1) for row in range(1, both)])
    block = jnp.concatenate([row, jnp.zeros((gram_ref.shape[1] - 1, ny), jnp.float32)], axis=0)
    for device in range(gram_ref.shape[0]):
        gram_ref[device] = block


def gather_kernel(rows_ref, gram_ref):
    vectors = gram_ref.shape[1]
    total = tree_sum([rows_ref[device] for device in range(rows_ref.shape[0])])[0:1]
    count = total.shape[1]
    for part in range(2):
        for a in range(vectors):
            row = (part * vectors + a) * vectors
            turned = pltpu.roll(total, count - row, 1) if row else total
            gram_ref[part, a:a + 1] = turned[:, :vectors]


def rim_y_kernel(splat_ref, left_in, hyf_ref, left_ref, residual_hbm, yadd_ref, sems):
    del left_in
    _, vectors, _, nz, nx, ny = left_ref.shape
    parts = range(2)
    both = 2 * vectors
    sey = end_value(splat_ref, "first_y", nz * nx)
    added = []
    for slot in range(2):
        first = slot * both
        value = cmul(sey, (hyf_ref[first:first + vectors], hyf_ref[first + vectors:first + both]))
        added += [part if slot else -part for part in value]
    rest = jnp.zeros((ny - 2 * both, nz * nx), jnp.float32)
    yadd_ref[...] = jnp.concatenate(added + [rest], axis=0).T.reshape(nz, nx, ny)
    lanes = lax.broadcasted_iota(jnp.int32, (SUB, ny), 1)

    def kept(z):
        blocks = [(slice(None), slice(None), 0, z)]
        blocks += [(slice(None), slice(None), comp, z, slice(SUB, nx)) for comp in (1, 2)]
        return [
            pltpu.make_async_copy(left_ref.at[block], residual_hbm.at[block], sems.at[place, z])
            for place, block in enumerate(blocks)
        ]

    @pl.loop(0, nz)
    def _(z):
        for cut in tiles_of(nx):
            column = yadd_ref[z, cut]
            for b in range(vectors):
                for part in parts:
                    for slot, comp in enumerate((0, 2)):
                        row = packed_row(slot, part, b, vectors)
                        value = pltpu.roll(column, ny - row, 1) if row else column
                        value = jnp.where(lanes == 0, value, 0.0)
                        left_ref[part, b, comp, z, cut] = left_ref[part, b, comp, z, cut] + value
        for copy in kept(z):
            copy.start()

    @pl.loop(0, nz)
    def _(z):
        for copy in kept(z):
            copy.wait()


def rim_x_kernel(splat_ref, left_in, residual_in, hxf_ref, left_ref, residual_hbm, xadd_ref, sems):
    del left_in, residual_in
    _, vectors, _, nz, nx, ny = left_ref.shape
    parts = range(2)
    sex = end_value(splat_ref, "first_x")
    for b in range(vectors):
        for slot in range(2):
            value = cmul(sex, tuple(hxf_ref[part, b, slot] for part in parts))
            for part in parts:
                xadd_ref[part, b, slot] = value[part] if slot else -value[part]
    rows = lax.broadcasted_iota(jnp.int32, (SUB, ny), 0)
    first = slice(0, SUB)
    copies = []
    for z in range(nz):
        for b in range(vectors):
            for part in parts:
                for slot, comp in ((1, 1), (0, 2)):
                    value = jnp.where(rows == 0, xadd_ref[part, b, slot, z:z + 1], 0.0)
                    left_ref[part, b, comp, z, first] = left_ref[part, b, comp, z, first] + value
        block = (slice(None), slice(None), slice(1, 3), z, first)
        copies.append(pltpu.make_async_copy(left_ref.at[block], residual_hbm.at[block], sems.at[z]))
        copies[-1].start()
    for copy in copies:
        copy.wait()


def body(fields, material, pml_width, eps_real, eps_loss, coeffs, ritz):
    _, vectors, _, nz, nx, ny = fields.shape
    f32 = lambda *shape: jax.ShapeDtypeStruct(shape, jnp.float32)
    scratch = lambda *shape: pltpu.VMEM(shape, jnp.float32)
    params = pltpu.CompilerParams(vmem_limit_bytes=40 * 1024 * 1024)
    whole = f32(*fields.shape)
    zf_shape = (2, vectors, 2, nx, ny)
    xf_shape = (2, vectors, 2, nz, ny)
    yf_shape = (4 * vectors, nz * nx)
    near, xf, yf = pl.pallas_call(
        face_kernel,
        out_shape=(whole, f32(*xf_shape), f32(*yf_shape)),
        in_specs=[HBM],
        out_specs=(VMEM,) * 3,
        scratch_shapes=[pltpu.SemaphoreType.DMA((2, 3))],
        compiler_params=params,
        name="take_faces",
    )(pltpu.with_memory_space_constraint(fields, pltpu.HBM))
    xf = passed_round(xf, "gx", -1)
    yf = passed_round(yf, "gy", -1)
    cells = fields.size // 6 // vectors

    def cost(flops, passes):
        return pl.CostEstimate(flops=flops * cells, bytes_accessed=passes * 4 * fields.size, transcendentals=0)

    planes = f32(nz, nx, ny)
    face = f32(*xf_shape)
    basis, eps, h, packed, table, sz, splats = pl.pallas_call(
        prepare_kernel,
        out_shape=(whole, f32(2, nz, nx, ny), whole, planes, f32(8, nx, ny), f32(4, nz, ny), f32(splat_count(vectors), ny)),
        in_specs=[VMEM] * 7,
        out_specs=(VMEM,) * 7,
        compiler_params=params,
        cost_estimate=cost(800, 4),
        name="prepare",
    )(pml_width[None], eps_real[None], eps_loss[None], coeffs, ritz, near, material)
    h, xf, yt, xadd, yadd, zf = pl.pallas_call(
        slab_kernel,
        out_shape=(whole, face, f32(*yf_shape), face, planes, f32(*zf_shape)),
        in_specs=[VMEM] * 5,
        out_specs=(VMEM,) * 6,
        input_output_aliases={2: 0},
        compiler_params=params,
        name="slab_face",
    )(splats, basis, h, xf, yf)
    zf = passed_round(zf, "gz", 1)
    h, packed, left, acc, before, hxf, basis_new = pl.pallas_call(
        inner_kernel,
        out_shape=(whole, planes, whole, f32(vectors, 2 * vectors, SUB, ny), f32(*zf_shape), face, whole),
        in_specs=[VMEM] * 9,
        out_specs=(VMEM,) * 6 + (HBM,),
        scratch_shapes=[pltpu.SemaphoreType.DMA],
        input_output_aliases={5: 0, 6: 1},
        compiler_params=params,
        cost_estimate=cost(800, 2),
        name="apply_inner",
    )(splats, basis, eps, table, sz, h, packed, xadd, yadd)
    devices = lax.axis_size("gx") * lax.axis_size("gy") * lax.axis_size("gz")
    left, gram, _, hxf, hyf = pl.pallas_call(
        outer_kernel,
        out_shape=(whole, f32(devices, 4, ny), whole, face, f32(*yf_shape)),
        in_specs=[VMEM] * 14,
        out_specs=(VMEM,) * 5,
        input_output_aliases={11: 0, 5: 2, 9: 3},
        compiler_params=params,
        cost_estimate=cost(300, 1),
        name="apply_outer",
    )(splats, basis, eps, table, sz, h, zf, xf, yt, hxf, packed, left, acc, before)
    gram, hxf, hyf = lax.optimization_barrier((gram, hxf, hyf))
    rows = lax.all_to_all(gram, ("gx", "gy", "gz"), 0, 0)
    from_x = passed_round(hxf, "gx", 1)
    from_y = passed_round(hyf, "gy", 1)
    free = pl.CostEstimate(flops=0, bytes_accessed=0, transcendentals=0)
    left, residual = pl.pallas_call(
        rim_y_kernel,
        out_shape=(whole, whole),
        in_specs=[VMEM] * 3,
        out_specs=(VMEM, HBM),
        scratch_shapes=[scratch(nz, nx, ny), pltpu.SemaphoreType.DMA((3, nz))],
        input_output_aliases={1: 0},
        compiler_params=params,
        cost_estimate=free,
        name="add_y_rims",
    )(splats, left, from_y)
    _, residual = pl.pallas_call(
        rim_x_kernel,
        out_shape=(whole, whole),
        in_specs=[VMEM, VMEM, HBM, VMEM],
        out_specs=(VMEM, HBM),
        scratch_shapes=[scratch(*xf_shape), pltpu.SemaphoreType.DMA((nz,))],
        input_output_aliases={1: 0, 2: 1},
        compiler_params=params,
        cost_estimate=free,
        name="add_x_rims",
    )(splats, left, residual, from_x)
    rows, residual = lax.optimization_barrier((rows, residual))
    gram = pl.pallas_call(
        gather_kernel,
        out_shape=f32(2, vectors, vectors),
        in_specs=[VMEM],
        out_specs=VMEM,
        compiler_params=params,
        name="sum_rows",
    )(rows)
    return basis_new, residual, gram


def solution(mesh):
    in_specs = (P(None, None, None, "gz", "gx", "gy"), P("gz", "gx", "gy"), P(), P(), P(), P(), P())
    out_specs = (P(None, None, None, "gz", "gx", "gy"), P(None, None, None, "gz", "gx", "gy"), P())
    return jax.shard_map(body, mesh=mesh, in_specs=in_specs, out_specs=out_specs, check_vma=False)
```

```python
import functools

import jax
import jax.numpy as jnp
from jax import lax
from jax.experimental import pallas as pl
from jax.experimental.pallas import tpu as pltpu
from jax.sharding import PartitionSpec as P

OMEGA_SQ = 0.36
SIGMA_TOP = 3.0
BOUNDS = ((4, 5), (0, 1), (2, 3))
AXES = ("gz", "gx", "gy")

VMEM = pl.BlockSpec(memory_space=pltpu.VMEM)
HBM = pl.BlockSpec(memory_space=pltpu.HBM)


def passed_round(value, axis, steps):
    count = lax.axis_size(axis)
    return lax.ppermute(value, axis, [(source, (source + steps) % count) for source in range(count)])


def inverse_stretch(places, length, low_width, high_width):
    inside_depth = jnp.clip((low_width - places) / low_width, 0.0, 1.0) + jnp.clip(
        (places + 1.0 - length + high_width) / high_width, 0.0, 1.0
    )
    absorb = SIGMA_TOP * inside_depth * inside_depth
    scaled = 1.0 / (1.0 + absorb * absorb)
    return scaled, -absorb * scaled


def tree_sum(values):
    while len(values) > 1:
        pairs = [values[place] + values[place + 1] for place in range(0, len(values) - 1, 2)]
        values = pairs + ([values[-1]] if len(values) % 2 else [])
    return values[0]


def cmul(left, right):
    return (left[0] * right[0] - left[1] * right[1], left[0] * right[1] + left[1] * right[0])


def add(left, right):
    return (left[0] + right[0], left[1] + right[1])


def sub(left, right):
    return (left[0] - right[0], left[1] - right[1])


def axis_stretch(pml_ref, direction, count, places):
    total = count * lax.axis_size(AXES[direction])
    low_slot, high_slot = BOUNDS[direction]
    low, high = (
        jnp.broadcast_to(pml_ref[0:1, slot:slot + 1].astype(jnp.float32), places.shape) for slot in (low_slot, high_slot)
    )
    return inverse_stretch(places, jnp.float32(total), low, high)


def local_places(direction, count, shape, dim):
    start = lax.axis_index(AXES[direction]) * count
    return (lax.broadcasted_iota(jnp.int32, shape, dim) + start).astype(jnp.float32)


def one_place(direction, count, offset, shape):
    start = lax.axis_index(AXES[direction]) * count + offset
    return jnp.full(shape, start, jnp.int32).astype(jnp.float32)


def packed_row(slot, part, vector, vectors):
    return (slot * 2 + part) * vectors + vector


def has_neighbour(direction, steps):
    place = lax.axis_index(AXES[direction]) + steps
    inside = (place >= 0) & (place < lax.axis_size(AXES[direction]))
    return jnp.where(inside, 1.0, 0.0).astype(jnp.float32)


def face_kernel(fields_hbm, fields_ref, xf_ref, yf_ref, sems):
    _, vectors, _, nz, nx, ny = fields_ref.shape
    lanes = lax.broadcasted_iota(jnp.int32, (nx, ny), 1)
    copies = {}
    for comp in (0, 2, 1):
        for part in range(2):
            for a in range(vectors):
                copy = pltpu.make_async_copy(
                    fields_hbm.at[part, a, comp], fields_ref.at[part, a, comp], sems.at[part, comp, a]
                )
                copy.start()
                copies[comp, part, a] = copy
    packed = [jnp.zeros((nx, ny), jnp.float32)] * nz
    for comp in (0, 2):
        for part in range(2):
            for a in range(vectors):
                copies[comp, part, a].wait()
                row = packed_row(comp // 2, part, a, vectors)
                for z in range(nz):
                    value = fields_ref[part, a, comp, z]
                    packed[z] = jnp.where(lanes == row, pltpu.roll(value, row, 1) if row else value, packed[z])
    turned = jnp.concatenate(packed, axis=0).T
    yf_ref[...] = turned[:yf_ref.shape[0]]
    for part in range(2):
        for a in range(vectors):
            xf_ref[part, a, 1] = fields_ref[part, a, 2, :, 0, :]
    for part in range(2):
        for a in range(vectors):
            copies[1, part, a].wait()
            xf_ref[part, a, 0] = fields_ref[part, a, 1, :, 0, :]


def rotated(coeffs_ref, old, b):
    new = None
    for a, value in enumerate(old):
        term = cmul((coeffs_ref[0, a, b], coeffs_ref[1, a, b]), value)
        new = term if new is None else add(new, term)
    return new


SUB = 8
SHX, SEX, SHY, SEY = range(0, 8, 2)


class Splats:
    def __init__(self, ref, first, shape):
        self.ref, self.first, self.shape = ref, first, shape

    def __getitem__(self, place):
        row = 0
        for index, size in zip(place, self.shape):
            row = row * size + index
        return self.ref[self.first + row:self.first + row + 1]


ENDS = ("under", "next_x", "next_y", "first_x", "first_y", "last_x", "last_y")


def end_value(splat_ref, name, width=None):
    row = 2 * ENDS.index(name)
    return tuple(splat_ref[row + part:row + part + 1, :width] for part in range(2))


def ritz_rows(splat_ref, vectors):
    return Splats(splat_ref, 2 * len(ENDS), (2, vectors))


def coeff_rows(splat_ref, vectors):
    return Splats(splat_ref, 2 * len(ENDS) + 2 * vectors, (2, vectors, vectors))


def mixed_rows(splat_ref, vectors):
    return Splats(splat_ref, 2 * len(ENDS) + 2 * vectors * (vectors + 1), (2, vectors, vectors))


def splat_count(vectors):
    return -(-(2 * len(ENDS) + 2 * vectors * (2 * vectors + 1)) // SUB) * SUB


def field_of(ref, b, comp, z, cut):
    return tuple(ref[part, b, comp, z, cut] for part in range(2))


def tiles_of(nx):
    return [slice(SUB * t, SUB * (t + 1)) for t in range(nx // SUB)]


def early_planes(nz):
    return (nz - 1) // 2


def open_magnetic(basis_ref, table_ref, sz_ref, h_ref, packed_ref):
    _, vectors, _, nz, nx, ny = basis_ref.shape
    parts = range(2)
    tile = (SUB, ny)
    rows = lax.broadcasted_iota(jnp.int32, tile, 0)
    lanes = lax.broadcasted_iota(jnp.int32, tile, 1)
    cuts = tiles_of(nx)

    def magnetic(b, z, last):
        shz = tuple(sz_ref[2 + part, pl.ds(z, 1)] for part in parts)
        for cut in cuts:
            u = [field_of(basis_ref, b, comp, z, cut) for comp in range(3)]

            def step_z(comp):
                if last:
                    return tuple(-value for value in u[comp])
                return sub(field_of(basis_ref, b, comp, z + 1, cut), u[comp])

            def step_x(comp):
                if cut.stop < nx:
                    ahead = field_of(basis_ref, b, comp, z, slice(cut.start + 1, cut.stop + 1))
                else:
                    ahead = tuple(jnp.where(rows == SUB - 1, 0.0, pltpu.roll(value, SUB - 1, 0)) for value in u[comp])
                return sub(ahead, u[comp])

            def step_y(comp):
                ahead = tuple(jnp.where(lanes == ny - 1, 0.0, pltpu.roll(value, ny - 1, 1)) for value in u[comp])
                return sub(ahead, u[comp])

            shx = tuple(table_ref[SHX + part, cut] for part in parts)
            shy = tuple(table_ref[SHY + part, cut] for part in parts)
            h = (
                sub(cmul(shy, step_y(2)), cmul(shz, step_z(1))),
                sub(cmul(shz, step_z(0)), cmul(shx, step_x(2))),
                sub(cmul(shx, step_x(1)), cmul(shy, step_y(0))),
            )
            for comp in range(3):
                for part in parts:
                    h_ref[part, b, comp, z, cut] = h[comp][part]
            packed = packed_ref[z, cut]
            for slot, value in enumerate((h[2], h[0])):
                for part in parts:
                    row = packed_row(slot, part, b, vectors)
                    packed = jnp.where(lanes == row, pltpu.roll(value[part], (row + 1) % ny, 1), packed)
            packed_ref[z, cut] = packed

    return magnetic


def prepare_kernel(
    pml_ref, eps_real_ref, eps_loss_ref, coeffs_ref, ritz_ref, fields_ref, material_ref,
    basis_ref, eps_ref, h_ref, packed_ref, table_ref, sz_ref, splat_ref,
):
    _, vectors, _, nz, nx, ny = fields_ref.shape
    plane = (nx, ny)
    parts = range(2)
    for slot, direction, half, count, dim in (
        (SHX, 1, 0.5, nx, 0), (SEX, 1, 0.0, nx, 0), (SHY, 2, 0.5, ny, 1), (SEY, 2, 0.0, ny, 1),
    ):
        values = axis_stretch(pml_ref, direction, count, local_places(direction, count, plane, dim) + half)
        for part in parts:
            table_ref[slot + part] = values[part]
    line = (1, ny)
    ends = {
        "under": (0, nz, -1, 0.5, 1.0),
        "next_x": (1, nx, nx, 0.0, 1.0),
        "next_y": (2, ny, ny, 0.0, 1.0),
        "first_x": (1, nx, 0, 0.0, has_neighbour(1, -1)),
        "first_y": (2, ny, 0, 0.0, has_neighbour(2, -1)),
        "last_x": (1, nx, nx - 1, 0.5, 1.0),
        "last_y": (2, ny, ny - 1, 0.5, 1.0),
    }
    lines = []
    for name in ENDS:
        direction, count, offset, half, factor = ends[name]
        values = axis_stretch(pml_ref, direction, count, one_place(direction, count, offset, line) + half)
        lines += [value * factor for value in values]
    lines += [
        jnp.broadcast_to(ritz_ref[part:part + 1, b:b + 1], line) for part in parts for b in range(vectors)
    ]
    real, imag = (
        [
            jnp.broadcast_to(coeffs_ref[part, a:a + 1, b:b + 1], line)
            for a in range(vectors) for b in range(vectors)
        ]
        for part in parts
    )
    lines += real + imag
    lines += [second + first for first, second in zip(real, imag)] + [second - first for first, second in zip(real, imag)]
    for row, value in enumerate(lines):
        splat_ref[row:row + 1] = value
    splat_ref[len(lines):] = jnp.zeros((splat_ref.shape[0] - len(lines), ny), jnp.float32)
    for slot, half in ((0, 0.0), (2, 0.5)):
        values = axis_stretch(pml_ref, 0, nz, local_places(0, nz, (nz, ny), 0) + half)
        for part in parts:
            sz_ref[slot + part] = values[part]

    coeffs, mixed = coeff_rows(splat_ref, vectors), mixed_rows(splat_ref, vectors)
    choices = [
        [jnp.broadcast_to(-OMEGA_SQ * source[0:1, number:number + 1], plane) for number in range(source.shape[1])]
        for source in (eps_real_ref, eps_loss_ref)
    ]

    @pl.loop(0, nz)
    def _(z):
        material = material_ref[z]
        for part in parts:
            value = jnp.zeros(plane, jnp.float32)
            for number, choice in enumerate(choices[part]):
                value = jnp.where(material == number, choice, value)
            eps_ref[part, z] = value
        for comp in range(3):
            real = [fields_ref[0, a, comp, z] for a in range(vectors)]
            imag = [fields_ref[1, a, comp, z] for a in range(vectors)]
            both = [first + second for first, second in zip(real, imag)]
            for b in range(vectors):
                shared = tree_sum([coeffs[0, a, b] * both[a] for a in range(vectors)])
                less = tree_sum([mixed[0, a, b] * imag[a] for a in range(vectors)])
                more = tree_sum([mixed[1, a, b] * real[a] for a in range(vectors)])
                basis_ref[0, b, comp, z] = shared - less
                basis_ref[1, b, comp, z] = shared + more
        packed_ref[z] = jnp.zeros(plane, jnp.float32)

    magnetic = open_magnetic(basis_ref, table_ref, sz_ref, h_ref, packed_ref)

    @pl.loop(0, early_planes(nz))
    def _(z):
        for b in range(vectors):
            magnetic(b, z, False)

    for b in range(vectors):
        magnetic(b, nz - 1, True)


def turn_face(coeffs_ref, direction, raw_ref, face_ref):
    inside = has_neighbour(direction, 1)
    vectors = raw_ref.shape[1]
    for slot in range(2):
        old = [(raw_ref[0, a, slot] * inside, raw_ref[1, a, slot] * inside) for a in range(vectors)]
        for b in range(vectors):
            new = rotated(coeffs_ref, old, b)
            for part in range(2):
                face_ref[part, b, slot] = new[part]


def turn_column(coeffs_ref, raw_ref, rows_ref):
    vectors = coeffs_ref.shape[1]
    inside = has_neighbour(2, 1)
    both = 2 * vectors
    shape = (both, raw_ref.shape[1])
    which = lax.broadcasted_iota(jnp.int32, shape, 0)
    turned = [jnp.zeros(shape, jnp.float32)] * 2
    for part in range(2):
        for a in range(vectors):
            column = jnp.zeros(shape, jnp.float32)
            for b in range(vectors):
                first, second = (coeffs_ref[0, a, b] * inside)[:, :shape[1]], (coeffs_ref[1, a, b] * inside)[:, :shape[1]]
                if part:
                    first, second = -second, first
                column = jnp.where(which == b, first, column)
                column = jnp.where(which == vectors + b, second, column)
            for slot in range(2):
                row = packed_row(slot, part, a, vectors)
                turned[slot] = turned[slot] + column * raw_ref[row:row + 1]
    for slot in range(2):
        rows_ref[slot * both:(slot + 1) * both] = turned[slot]


def lane_to_last(values, slot, part, b, vectors):
    ny = values.shape[-1]
    lanes = lax.broadcasted_iota(jnp.int32, values.shape, 1)
    row = packed_row(slot, part, b, vectors)
    return jnp.where(lanes == ny - 1, pltpu.roll(values, ny - 1 - row, 1), 0.0)


def with_halos(h, b, z, cut, nx, xadd_ref, yadd_ref):
    vectors = xadd_ref.shape[1]
    column = yadd_ref[z, cut]
    hx = tuple(h[0][part] + lane_to_last(column, 1, part, b, vectors) for part in range(2))
    hz = tuple(h[2][part] + lane_to_last(column, 0, part, b, vectors) for part in range(2))
    hy = h[1]
    if cut.stop == nx:
        rows = lax.broadcasted_iota(jnp.int32, column.shape, 0)

        def row_of(slot):
            return tuple(
                jnp.where(rows == SUB - 1, xadd_ref[part, b, slot, pl.ds(z, 1)], 0.0) for part in range(2)
            )

        hy, hz = add(hy, row_of(0)), add(hz, row_of(1))
    return hx, hy, hz


def slab_kernel(
    splat_ref, basis_ref, h_in, raw_xf_ref, raw_yf_ref,
    h_ref, xf_ref, yt_ref, xadd_ref, yadd_ref, zf_ref,
):
    del h_in
    _, vectors, _, nz, nx, ny = basis_ref.shape
    parts = range(2)
    cells = nz * nx
    both = 2 * vectors
    coeffs = coeff_rows(splat_ref, vectors)
    turn_face(coeffs, 1, raw_xf_ref, xf_ref)
    turn_column(coeffs, raw_yf_ref, yt_ref)
    shx = end_value(splat_ref, "last_x")
    shy = end_value(splat_ref, "last_y", cells)
    for b in range(vectors):
        for slot in range(2):
            value = cmul(shx, tuple(xf_ref[part, b, 1 - slot] for part in parts))
            for part in parts:
                xadd_ref[part, b, slot] = value[part] if slot else -value[part]
    added = []
    for slot in range(2):
        value = cmul(shy, (yt_ref[slot * both:slot * both + vectors], yt_ref[slot * both + vectors:(slot + 1) * both]))
        added += [part if slot else -part for part in value]
    rest = jnp.zeros((ny - 2 * both, cells), jnp.float32)
    yadd_ref[...] = jnp.concatenate(added + [rest], axis=0).T.reshape(nz, nx, ny)
    last = nz - 1
    lower = jnp.full((SUB, ny), lax.axis_index(AXES[0]), jnp.int32) == 0
    for b in range(vectors):
        for cut in tiles_of(nx):
            h = [field_of(h_ref, b, comp, last, cut) for comp in range(3)]
            h = with_halos(h, b, last, cut, nx, xadd_ref, yadd_ref)
            for part in parts:
                for comp in range(3):
                    h_ref[part, b, comp, last, cut] = h[comp][part]
                for comp in range(2):
                    zf_ref[part, b, comp, cut] = jnp.where(lower, h[comp][part], basis_ref[part, b, comp, 0, cut])


def plane_step(
    b, z, before, sums, ritz_ref, basis_ref, eps_ref, table_ref, sz_ref, h_ref, left_ref, halos=None
):
    _, vectors, _, _, nx, ny = basis_ref.shape
    rows = lax.broadcasted_iota(jnp.int32, (SUB, ny), 0)
    lanes = lax.broadcasted_iota(jnp.int32, (SUB, ny), 1)
    parts = range(2)
    cuts = tiles_of(nx)
    sez = tuple(sz_ref[part, pl.ds(z, 1)] for part in parts)
    fields = []
    for cut in cuts:
        h = [field_of(h_ref, b, comp, z, cut) for comp in range(3)]
        if halos is not None:
            h = with_halos(h, b, z, cut, nx, *halos)
            for comp in (1, 2):
                for part in parts:
                    h_ref[part, b, comp, z, cut] = h[comp][part]
        fields.append(h)
    sums = list(sums)
    for t, cut in enumerate(cuts):
        hx, hy, hz = fields[t]

        def back_x(comp):
            here = fields[t][comp]
            if t:
                past = field_of(h_ref, b, comp, z, slice(cut.start - 1, cut.stop - 1))
            else:
                past = tuple(jnp.where(rows == 0, 0.0, pltpu.roll(value, 1, 0)) for value in here)
            return sub(here, past)

        def back_y(value):
            return sub(value, tuple(jnp.where(lanes == 0, 0.0, pltpu.roll(part, 1, 1)) for part in value))

        sex = tuple(table_ref[SEX + part, cut] for part in parts)
        sey = tuple(table_ref[SEY + part, cut] for part in parts)
        bxy, bxz = (cmul(sex, back_x(comp)) for comp in (1, 2))
        byz, byx = (cmul(sey, back_y(value)) for value in (hz, hx))
        bzx, bzy = (cmul(sez, sub(value, past)) for value, past in zip((hx, hy), before[t]))
        curl = (sub(byz, bzy), sub(bzx, bxz), sub(bxy, byx))
        u = [field_of(basis_ref, b, comp, z, cut) for comp in range(3)]
        eps = tuple(eps_ref[part, z, cut] for part in parts)
        w = [add(curl[comp], cmul(eps, u[comp])) for comp in range(3)]
        for comp in range(3):
            left = sub(w[comp], cmul((ritz_ref[0, b], ritz_ref[1, b]), u[comp]))
            for part in parts:
                left_ref[part, b, comp, z, cut] = left[part]
        for a in range(vectors):
            total = sums[a]
            for comp in range(3):
                total = add(total, cmul(field_of(basis_ref, a, comp, z, cut), w[comp]))
            sums[a] = total
    return [(h[0], h[1]) for h in fields], sums


def inner_kernel(
    splat_ref, basis_ref, eps_ref, table_ref, sz_ref, h_in, packed_in, xadd_ref, yadd_ref,
    h_ref, packed_ref, left_ref, acc_ref, before_ref, hxf_ref, basis_hbm, sem,
):
    del h_in, packed_in
    _, vectors, _, nz, nx, ny = basis_ref.shape
    keep = pltpu.make_async_copy(basis_ref, basis_hbm, sem)
    keep.start()
    cuts = tiles_of(nx)
    magnetic = open_magnetic(basis_ref, table_ref, sz_ref, h_ref, packed_ref)

    @pl.loop(early_planes(nz), nz - 1)
    def _(z):
        for b in range(vectors):
            magnetic(b, z, False)

    lanes = lax.broadcasted_iota(jnp.int32, (nz, ny), 1)
    open_plane = lax.broadcasted_iota(jnp.int32, (nz, ny), 0) < nz - 1
    packed_ref[...] = packed_ref[...] + yadd_ref[...]
    corner = packed_ref[:, nx - 1, :]
    for b in range(vectors):
        for part in range(2):
            row = packed_row(0, part, b, vectors)
            more = xadd_ref[part, b, 1]
            corner = corner + jnp.where(lanes == row, pltpu.roll(more, (row + 1) % ny, 1), 0.0)
            more = more + lane_to_last(yadd_ref[:, nx - 1, :], 0, part, b, vectors)
            hxf_ref[part, b, 0] = h_ref[part, b, 1, :, nx - 1, :] + jnp.where(open_plane, xadd_ref[part, b, 0], 0.0)
            hxf_ref[part, b, 1] = h_ref[part, b, 2, :, nx - 1, :] + jnp.where(open_plane, more, 0.0)
    packed_ref[:, nx - 1, :] = corner
    acc_ref[...] = jnp.zeros(acc_ref.shape, jnp.float32)
    before_ref[...] = jnp.zeros(before_ref.shape, jnp.float32)

    @pl.loop(0, nz - 1)
    def _(z):
        for b in range(vectors):
            before = [
                tuple(tuple(before_ref[part, b, slot, cut] for part in range(2)) for slot in range(2)) for cut in cuts
            ]
            sums = [(acc_ref[b, a], acc_ref[b, vectors + a]) for a in range(vectors)]
            before, sums = plane_step(
                b, z, before, sums, ritz_rows(splat_ref, vectors), basis_ref, eps_ref, table_ref, sz_ref, h_ref, left_ref, (xadd_ref, yadd_ref)
            )
            for part in range(2):
                for a in range(vectors):
                    acc_ref[b, part * vectors + a] = sums[a][part]
                for t, cut in enumerate(cuts):
                    for slot in range(2):
                        before_ref[part, b, slot, cut] = before[t][slot][part]

    keep.wait()


def close_last_plane(sz_ref, zf_ref, packed_in, h_ref, hxf_ref, hyf_ref):
    _, vectors, _, nz, nx, ny = h_ref.shape
    parts = range(2)
    last = nz - 1
    lanes = lax.broadcasted_iota(jnp.int32, (SUB, ny), 1)
    shz = tuple(sz_ref[2 + part, last:] * has_neighbour(0, 1) for part in parts)
    packed = [packed_in[last, cut] for cut in tiles_of(nx)]
    for b in range(vectors):
        for t, cut in enumerate(tiles_of(nx)):
            ex, ey = (tuple(zf_ref[part, b, slot, cut] for part in parts) for slot in range(2))
            more = (tuple(-value for value in cmul(shz, ey)), cmul(shz, ex))
            for part in parts:
                for comp in range(2):
                    h_ref[part, b, comp, last, cut] = h_ref[part, b, comp, last, cut] + more[comp][part]
                row = packed_row(1, part, b, vectors)
                edge = pltpu.roll(more[0][part], (row + 1) % ny, 1)
                packed[t] = packed[t] + jnp.where(lanes == row, edge, 0.0)
                if cut.stop == nx:
                    hxf_ref[part, b, 0, last:] = hxf_ref[part, b, 0, last:] + more[1][part][SUB - 1:]
    inner = packed_in[:last].reshape(last * nx, ny)
    hyf_ref[...] = jnp.concatenate([inner] + packed, axis=0).T[:hyf_ref.shape[0]]


def outer_kernel(
    splat_ref, basis_ref, eps_ref, table_ref, sz_ref, h_in, zf_ref, xf_ref, yt_ref, hxf_in, packed_in,
    left_in, acc_ref, before_ref, left_ref, gram_ref, h_ref, hxf_ref, hyf_ref,
):
    del left_in, h_in, hxf_in
    close_last_plane(sz_ref, zf_ref, packed_in, h_ref, hxf_ref, hyf_ref)
    _, vectors, _, nz, nx, ny = basis_ref.shape
    parts = range(2)
    cuts = tiles_of(nx)
    under = end_value(splat_ref, "under")
    sez = tuple(sz_ref[part, 0:1] * has_neighbour(0, -1) for part in parts)
    sx_next = end_value(splat_ref, "next_x")
    sy_next = end_value(splat_ref, "next_y", nz * nx)
    both = 2 * vectors
    ends = [
        cmul(sy_next, (yt_ref[slot * both:slot * both + vectors], yt_ref[slot * both + vectors:(slot + 1) * both]))
        for slot in range(2)
    ]
    columns = lax.broadcasted_iota(jnp.int32, (both, ny), 1)
    gram = jnp.zeros((both, ny), jnp.float32)
    for b in range(vectors):

        def tile_of(ref, slot, cut, b=b):
            return tuple(ref[part, b, slot, cut] for part in parts)

        before = [tuple(tile_of(before_ref, slot, cut) for slot in range(2)) for cut in cuts]
        sums = [(acc_ref[b, a], acc_ref[b, vectors + a]) for a in range(vectors)]
        _, sums = plane_step(
            b, nz - 1, before, sums, ritz_rows(splat_ref, vectors), basis_ref, eps_ref, table_ref, sz_ref, h_ref, left_ref
        )
        for cut in cuts:
            ex, ey = (field_of(basis_ref, b, comp, 0, cut) for comp in range(2))
            hx = sub(tile_of(zf_ref, 0, cut), cmul(under, ey))
            hy = add(tile_of(zf_ref, 1, cut), cmul(under, ex))
            more = (cmul(sez, hy), cmul(sez, hx))
            for part in parts:
                left_ref[part, b, 0, 0, cut] = left_ref[part, b, 0, 0, cut] + more[0][part]
                left_ref[part, b, 1, 0, cut] = left_ref[part, b, 1, 0, cut] - more[1][part]
            for a in range(vectors):
                ex, ey = (field_of(basis_ref, a, comp, 0, cut) for comp in range(2))
                sums[a] = add(sums[a], sub(cmul(ex, more[0]), cmul(ey, more[1])))
        h_y = tuple(hxf_ref[part, b, 0] for part in parts)
        h_z = tuple(hxf_ref[part, b, 1] for part in parts)
        for a in range(vectors):
            over = cmul(tuple(xf_ref[part, a, 0] for part in parts), h_z)
            over = sub(over, cmul(tuple(xf_ref[part, a, 1] for part in parts), h_y))
            over = cmul(sx_next, over)
            for row in range(0, nz, SUB):
                sums[a] = add(sums[a], tuple(part[row:row + SUB] for part in over))
        flat = jnp.concatenate(
            [jnp.sum(sums[a][part], axis=0, keepdims=True) for part in parts for a in range(vectors)], axis=0
        )
        over = None
        for slot in range(2):
            h = tuple(hyf_ref[packed_row(slot, part, b, vectors)][None] for part in parts)
            term = cmul(ends[slot], h)
            over = term if over is None else sub(term, over)
        side = jnp.concatenate(over, axis=0)
        total = jnp.sum(flat, axis=1, keepdims=True) + jnp.sum(side, axis=1, keepdims=True)
        gram = jnp.where(columns == b, total, gram)
    everywhere = 3.0 * nz * nx * ny
    for axis in AXES:
        everywhere = everywhere * lax.axis_size(axis)
    gram = gram * (1.0 / everywhere)
    row = tree_sum([gram[0:1]] + [pltpu.roll(gram[row:row + 1], row * vectors, 1) for row in range(1, both)])
    block = jnp.concatenate([row, jnp.zeros((gram_ref.shape[1] - 1, ny), jnp.float32)], axis=0)
    for device in range(gram_ref.shape[0]):
        gram_ref[device] = block


def gather_kernel(rows_ref, gram_ref):
    vectors = gram_ref.shape[1]
    total = tree_sum([rows_ref[device] for device in range(rows_ref.shape[0])])[0:1]
    count = total.shape[1]
    for part in range(2):
        for a in range(vectors):
            row = (part * vectors + a) * vectors
            turned = pltpu.roll(total, count - row, 1) if row else total
            gram_ref[part, a:a + 1] = turned[:, :vectors]


def rim_y_kernel(splat_ref, left_in, hyf_ref, left_ref, residual_hbm, yadd_ref, sems):
    del left_in
    _, vectors, _, nz, nx, ny = left_ref.shape
    parts = range(2)
    both = 2 * vectors
    sey = end_value(splat_ref, "first_y", nz * nx)
    added = []
    for slot in range(2):
        first = slot * both
        value = cmul(sey, (hyf_ref[first:first + vectors], hyf_ref[first + vectors:first + both]))
        added += [part if slot else -part for part in value]
    rest = jnp.zeros((ny - 2 * both, nz * nx), jnp.float32)
    yadd_ref[...] = jnp.concatenate(added + [rest], axis=0).T.reshape(nz, nx, ny)
    lanes = lax.broadcasted_iota(jnp.int32, (SUB, ny), 1)

    def kept(z):
        blocks = [(slice(None), slice(None), 0, z)]
        blocks += [(slice(None), slice(None), comp, z, slice(SUB, nx)) for comp in (1, 2)]
        return [
            pltpu.make_async_copy(left_ref.at[block], residual_hbm.at[block], sems.at[place, z])
            for place, block in enumerate(blocks)
        ]

    @pl.loop(0, nz)
    def _(z):
        for cut in tiles_of(nx):
            column = yadd_ref[z, cut]
            for b in range(vectors):
                for part in parts:
                    for slot, comp in enumerate((0, 2)):
                        row = packed_row(slot, part, b, vectors)
                        value = pltpu.roll(column, ny - row, 1) if row else column
                        value = jnp.where(lanes == 0, value, 0.0)
                        left_ref[part, b, comp, z, cut] = left_ref[part, b, comp, z, cut] + value
        for copy in kept(z):
            copy.start()

    @pl.loop(0, nz)
    def _(z):
        for copy in kept(z):
            copy.wait()


def rim_x_kernel(splat_ref, left_in, residual_in, hxf_ref, left_ref, residual_hbm, xadd_ref, sems):
    del left_in, residual_in
    _, vectors, _, nz, nx, ny = left_ref.shape
    parts = range(2)
    sex = end_value(splat_ref, "first_x")
    for b in range(vectors):
        for slot in range(2):
            value = cmul(sex, tuple(hxf_ref[part, b, slot] for part in parts))
            for part in parts:
                xadd_ref[part, b, slot] = value[part] if slot else -value[part]
    rows = lax.broadcasted_iota(jnp.int32, (SUB, ny), 0)
    first = slice(0, SUB)
    copies = []
    for z in range(nz):
        for b in range(vectors):
            for part in parts:
                for slot, comp in ((1, 1), (0, 2)):
                    value = jnp.where(rows == 0, xadd_ref[part, b, slot, z:z + 1], 0.0)
                    left_ref[part, b, comp, z, first] = left_ref[part, b, comp, z, first] + value
        block = (slice(None), slice(None), slice(1, 3), z, first)
        copies.append(pltpu.make_async_copy(left_ref.at[block], residual_hbm.at[block], sems.at[z]))
        copies[-1].start()
    for copy in copies:
        copy.wait()


def body(fields, material, pml_width, eps_real, eps_loss, coeffs, ritz):
    _, vectors, _, nz, nx, ny = fields.shape
    f32 = lambda *shape: jax.ShapeDtypeStruct(shape, jnp.float32)
    scratch = lambda *shape: pltpu.VMEM(shape, jnp.float32)
    params = pltpu.CompilerParams(vmem_limit_bytes=40 * 1024 * 1024)
    whole = f32(*fields.shape)
    zf_shape = (2, vectors, 2, nx, ny)
    xf_shape = (2, vectors, 2, nz, ny)
    yf_shape = (4 * vectors, nz * nx)
    near, xf, yf = pl.pallas_call(
        face_kernel,
        out_shape=(whole, f32(*xf_shape), f32(*yf_shape)),
        in_specs=[HBM],
        out_specs=(VMEM,) * 3,
        scratch_shapes=[pltpu.SemaphoreType.DMA((2, 3, vectors))],
        compiler_params=params,
        name="take_faces",
    )(pltpu.with_memory_space_constraint(fields, pltpu.HBM))
    xf = passed_round(xf, "gx", -1)
    yf = passed_round(yf, "gy", -1)
    cells = fields.size // 6 // vectors

    def cost(flops, passes):
        return pl.CostEstimate(flops=flops * cells, bytes_accessed=passes * 4 * fields.size, transcendentals=0)

    planes = f32(nz, nx, ny)
    face = f32(*xf_shape)
    basis, eps, h, packed, table, sz, splats = pl.pallas_call(
        prepare_kernel,
        out_shape=(whole, f32(2, nz, nx, ny), whole, planes, f32(8, nx, ny), f32(4, nz, ny), f32(splat_count(vectors), ny)),
        in_specs=[VMEM] * 7,
        out_specs=(VMEM,) * 7,
        compiler_params=params,
        cost_estimate=cost(800, 4),
        name="prepare",
    )(pml_width[None], eps_real[None], eps_loss[None], coeffs, ritz, near, material)
    h, xf, yt, xadd, yadd, zf = pl.pallas_call(
        slab_kernel,
        out_shape=(whole, face, f32(*yf_shape), face, planes, f32(*zf_shape)),
        in_specs=[VMEM] * 5,
        out_specs=(VMEM,) * 6,
        input_output_aliases={2: 0},
        compiler_params=params,
        name="slab_face",
    )(splats, basis, h, xf, yf)
    zf = passed_round(zf, "gz", 1)
    h, packed, left, acc, before, hxf, basis_new = pl.pallas_call(
        inner_kernel,
        out_shape=(whole, planes, whole, f32(vectors, 2 * vectors, SUB, ny), f32(*zf_shape), face, whole),
        in_specs=[VMEM] * 9,
        out_specs=(VMEM,) * 6 + (HBM,),
        scratch_shapes=[pltpu.SemaphoreType.DMA],
        input_output_aliases={5: 0, 6: 1},
        compiler_params=params,
        cost_estimate=cost(800, 2),
        name="apply_inner",
    )(splats, basis, eps, table, sz, h, packed, xadd, yadd)
    devices = lax.axis_size("gx") * lax.axis_size("gy") * lax.axis_size("gz")
    left, gram, _, hxf, hyf = pl.pallas_call(
        outer_kernel,
        out_shape=(whole, f32(devices, 4, ny), whole, face, f32(*yf_shape)),
        in_specs=[VMEM] * 14,
        out_specs=(VMEM,) * 5,
        input_output_aliases={11: 0, 5: 2, 9: 3},
        compiler_params=params,
        cost_estimate=cost(300, 1),
        name="apply_outer",
    )(splats, basis, eps, table, sz, h, zf, xf, yt, hxf, packed, left, acc, before)
    gram, hxf, hyf = lax.optimization_barrier((gram, hxf, hyf))
    rows = lax.all_to_all(gram, ("gx", "gy", "gz"), 0, 0)
    from_x = passed_round(hxf, "gx", 1)
    from_y = passed_round(hyf, "gy", 1)
    free = pl.CostEstimate(flops=0, bytes_accessed=0, transcendentals=0)
    left, residual = pl.pallas_call(
        rim_y_kernel,
        out_shape=(whole, whole),
        in_specs=[VMEM] * 3,
        out_specs=(VMEM, HBM),
        scratch_shapes=[scratch(nz, nx, ny), pltpu.SemaphoreType.DMA((3, nz))],
        input_output_aliases={1: 0},
        compiler_params=params,
        cost_estimate=free,
        name="add_y_rims",
    )(splats, left, from_y)
    _, residual = pl.pallas_call(
        rim_x_kernel,
        out_shape=(whole, whole),
        in_specs=[VMEM, VMEM, HBM, VMEM],
        out_specs=(VMEM, HBM),
        scratch_shapes=[scratch(*xf_shape), pltpu.SemaphoreType.DMA((nz,))],
        input_output_aliases={1: 0, 2: 1},
        compiler_params=params,
        cost_estimate=free,
        name="add_x_rims",
    )(splats, left, residual, from_x)
    rows, residual = lax.optimization_barrier((rows, residual))
    gram = pl.pallas_call(
        gather_kernel,
        out_shape=f32(2, vectors, vectors),
        in_specs=[VMEM],
        out_specs=VMEM,
        compiler_params=params,
        name="sum_rows",
    )(rows)
    return basis_new, residual, gram


def solution(mesh):
    in_specs = (P(None, None, None, "gz", "gx", "gy"), P("gz", "gx", "gy"), P(), P(), P(), P(), P())
    out_specs = (P(None, None, None, "gz", "gx", "gy"), P(None, None, None, "gz", "gx", "gy"), P())
    return jax.shard_map(body, mesh=mesh, in_specs=in_specs, out_specs=out_specs, check_vma=False)
```
